32 devices in a mesh: dp: 8 (over y, x, core), head: 4 (over z).
Axes of the slice: x: 2, y: 2, z: 4, core: 2. Of those that a mesh axis runs over, the one named last changes fastest.
Arguments:
- patch_observations: bfloat16 [4096, 32], P(('dp', 'head')), may hold values from -6 to 6
- sequence_labels: int32 [32, 128], P(('dp', 'head')), may hold values from 0 to 41, never falling along the last dimension, each value on 1 to 64 neighbouring positions
- leading_filler_count: int32 [32, 42], P(('dp', 'head')), may hold values from 0 to 32
- intake_latent_matrix: bfloat16 [64, 1280], replicated, may hold values from -0.75 to 0.75
- intake_latent_offset: float32 [1280], replicated, may hold values from -3 to 3
- intake_emit_matrix: bfloat16 [1280, 1280], replicated, may hold values from -0.15625 to 0.15625
- intake_emit_offset: float32 [1280], replicated, may hold values from -2 to 2
- intake_shortcut_matrix: bfloat16 [64, 1280], replicated, may hold values from -0.75 to 0.75
- attention_entry_matrices: bfloat16 [2, 1280, 3840], P(None, ('dp', 'head')), may hold values from -0.15625 to 0.15625
- attention_merge_matrix: bfloat16 [2, 1280, 1280], P(None, ('dp', 'head')), may hold values from -0.3125 to 0.3125
- feedforward_widen_matrix: bfloat16 [2, 1280, 1280], P(None, ('dp', 'head')), may hold values from -0.15625 to 0.15625
- feedforward_shrink_matrix: bfloat16 [2, 1280, 1280], P(None, ('dp', 'head')), may hold values from -0.15625 to 0.15625
- layer_scale_factors: bfloat16 [2, 2, 1280], P(None, None, ('dp', 'head')), may hold values from 0.5 to 1.5
- readout_latent_matrix: bfloat16 [1280, 1280], P(None, 'head'), may hold values from -0.15625 to 0.15625
- readout_latent_offset: float32 [1280], P('head'), may hold values from -3 to 3
- readout_emit_matrix: bfloat16 [1280, 1280], P(None, 'head'), may hold values from -0.15625 to 0.15625
- readout_emit_offset: float32 [1280], P('head'), may hold values from -2 to 2
- readout_shortcut_matrix: bfloat16 [1280, 1280], P(None, 'head'), may hold values from -0.15625 to 0.15625
- loss_sensitivity: bfloat16 [4096, 1280], P('dp', 'head'), may hold values from -6 to 6
Outputs:
- token_predictions: bfloat16 [4096, 1280], P('dp', 'head')
- values_grad: float32 [4096, 32], P(('dp', 'head'))
- entry_inner_grad: float32 [64, 1280], replicated
- entry_inner_bias_grad: float32 [1280], replicated
- entry_outer_grad: float32 [1280, 1280], replicated
- entry_outer_bias_grad: float32 [1280], replicated
- entry_skip_grad: float32 [64, 1280], replicated
- qkv_weight_grad: float32 [2, 1280, 3840], P(None, ('dp', 'head'))
- out_weight_grad: float32 [2, 1280, 1280], P(None, ('dp', 'head'))
- up_weight_grad: float32 [2, 1280, 1280], P(None, ('dp', 'head'))
- down_weight_grad: float32 [2, 1280, 1280], P(None, ('dp', 'head'))
- norm_gains_grad: float32 [2, 2, 1280], P(None, None, ('dp', 'head'))
- head_inner_grad: float32 [1280, 1280], P(None, 'head')
- head_inner_bias_grad: float32 [1280], P('head')
- head_outer_grad: float32 [1280, 1280], P(None, 'head')
- head_outer_bias_grad: float32 [1280], P('head')
- head_skip_grad: float32 [1280, 1280], P(None, 'head')
The draws below stay inside these ranges and needn't reach their ends.
Inputs may be any that keep to these rules, and one draw needn't show every extreme that they name: `sequence_labels`: each row lists the series numbers of one device's 128 tokens in order, rising by one from series to series and starting at 0; each series has 1 to 64 tokens and one series of every device has exactly 64.
All inputs are finite; a program needn't handle non-finite values.
Results may differ from the reference program's by a relative error of at most 0.023.
Values may be sent and summed in bfloat16 or wider, within the bound.
No kernel may reach another device: no remote copies, remote signals or barrier semaphores. Data moves between devices by JAX's collectives and lax.ppermute only.
A program may use at most 192 MiB of HBM per device.

```python
import math
from functools import partial
import jax
import jax.numpy as jnp
import numpy as np
from jax import lax

MODEL_WIDTH = 1280
HEADS = 16
HEAD_DIM = 80
FF = 1280
PATCH = 32
LAYERS = 2
MAX_PATCHES = 64
TOK_DEV = 128
SERIES_DEV = 42
SHARDS = 32
TOKENS = 4096
FUTURE_LENGTH = 1280


def set_ends(array, key, low, high):
    longest = array.shape.index(max(array.shape))
    spots = []
    for shift in (0, 1):
        where = [jax.random.randint(jax.random.fold_in(key, axis), (), 0, length) for axis, length in enumerate(array.shape)]
        where[longest] = (where[longest] + shift) % array.shape[longest]
        spots.append(tuple(where))
    return array.at[spots[0]].set(low).at[spots[1]].set(high)


def block_levels(own_key, extent, split, least, largest):
    def one(dim, blocks):
        heights = jax.random.uniform(jax.random.fold_in(jax.random.fold_in(own_key, 6), dim), (blocks,), jnp.float32, least / len(split), largest / len(split))
        return jnp.repeat(jnp.exp(heights), extent[dim] // blocks).reshape((-1,) + (1,) * (len(extent) - dim - 1))

    level = one(*split[0])
    for cut in split[1:]:
        level = level * one(*cut)
    return level


def split_up(number_of, total, most, slope):
    loads = [(1 << 20) // math.isqrt(grade ** slope) + 1 for grade in range(2, number_of + 1)]
    spare, given = total - most - (number_of - 1), [1] * (number_of - 1)
    while spare > 0:
        movable = [i for i in range(number_of - 1) if given[i] < most]
        pool, budget = sum([loads[i] for i in movable]), spare
        for i in movable:
            more = min(most - given[i], max(1, budget * loads[i] // pool), spare)
            given[i] = given[i] + more
            spare = spare - more
    return np.array([most] + given)


def uneven_parts(own_key, number_of, total, most, lean):
    if number_of == 2:
        one = jax.random.randint(own_key, (), max(1, total - most), min(most, total - 1) + 1)
        return jnp.stack([one, total - one])
    sizes = jnp.asarray(split_up(number_of, total, most, lean), jnp.int32)
    couples = (number_of - 1) // 2
    giver, receiver = sizes[1:1 + 2 * couples:2], sizes[2:2 + 2 * couples:2]
    margin = jnp.minimum(giver - 1, most - receiver)
    passed = jax.random.randint(jax.random.fold_in(own_key, 1), (couples,), 0, 1 << 20) % (margin + 1)
    sizes = sizes.at[1:1 + 2 * couples:2].set(giver - passed).at[2:2 + 2 * couples:2].set(receiver + passed)
    return sizes[jax.random.permutation(jax.random.fold_in(own_key, 2), number_of)]


def gaussian(own_key, shape, deviation, bound, shards=(), kind=jnp.bfloat16):
    values = deviation * jax.random.normal(own_key, shape, jnp.float32)
    if shards:
        values = values * block_levels(own_key, shape, shards, -0.22, 0.18)
    return jnp.clip(values, -bound, bound).astype(kind)


def setup_inputs(seed: int = 0) -> dict:
    key_list = jax.random.split(jax.random.key(seed), 20)
    patch_observations = gaussian(key_list[0], (TOKENS, PATCH), 1.0, 6.0, ((0, 32),))
    sequence_labels = jax.vmap(lambda own: jnp.searchsorted(jnp.cumsum(uneven_parts(own, SERIES_DEV, TOK_DEV, MAX_PATCHES, 2)), jnp.arange(TOK_DEV), side="right"))(jax.random.split(key_list[1], SHARDS)).reshape((SHARDS, TOK_DEV)).astype(jnp.int32)
    leading_filler_count = set_ends(jax.random.randint(key_list[2], (SHARDS, SERIES_DEV), 0, PATCH + 1), jax.random.fold_in(key_list[2], 1), 0, PATCH).astype(jnp.int32)
    intake_latent_matrix = gaussian(key_list[3], (2 * PATCH, MODEL_WIDTH), (2 * PATCH) ** -0.5, 0.75)
    intake_latent_offset = gaussian(key_list[4], (MODEL_WIDTH,), 0.5, 3.0, (), jnp.float32)
    intake_emit_matrix = gaussian(key_list[5], (MODEL_WIDTH, MODEL_WIDTH), MODEL_WIDTH ** -0.5, 0.15625)
    intake_emit_offset = gaussian(key_list[6], (MODEL_WIDTH,), 0.3, 2.0, (), jnp.float32)
    intake_shortcut_matrix = gaussian(key_list[7], (2 * PATCH, MODEL_WIDTH), (2 * PATCH) ** -0.5, 0.75)
    attention_entry_matrices = gaussian(key_list[8], (LAYERS, MODEL_WIDTH, 3 * MODEL_WIDTH), MODEL_WIDTH ** -0.5, 0.15625, ((1, 32),))
    attention_merge_matrix = gaussian(key_list[9], (LAYERS, MODEL_WIDTH, MODEL_WIDTH), (MODEL_WIDTH // 4) ** -0.5, 0.3125, ((1, 32),))
    feedforward_widen_matrix = gaussian(key_list[10], (LAYERS, MODEL_WIDTH, FF), MODEL_WIDTH ** -0.5, 0.15625, ((1, 32),))
    feedforward_shrink_matrix = gaussian(key_list[11], (LAYERS, FF, MODEL_WIDTH), FF ** -0.5, 0.15625, ((1, 32),))
    layer_scale_factors = jnp.clip(1.0 + 0.1 * jax.random.normal(key_list[12], (LAYERS, 2, MODEL_WIDTH), jnp.float32), 0.5, 1.5).astype(jnp.bfloat16)
    readout_latent_matrix = gaussian(key_list[13], (MODEL_WIDTH, MODEL_WIDTH), MODEL_WIDTH ** -0.5, 0.15625, ((1, 4),))
    readout_latent_offset = gaussian(key_list[14], (MODEL_WIDTH,), 0.5, 3.0, ((0, 4),), jnp.float32)
    readout_emit_matrix = gaussian(key_list[15], (MODEL_WIDTH, FUTURE_LENGTH), MODEL_WIDTH ** -0.5, 0.15625, ((1, 4),))
    readout_emit_offset = gaussian(key_list[16], (FUTURE_LENGTH,), 0.3, 2.0, ((0, 4),), jnp.float32)
    readout_shortcut_matrix = gaussian(key_list[17], (MODEL_WIDTH, FUTURE_LENGTH), MODEL_WIDTH ** -0.5, 0.15625, ((1, 4),))
    loss_sensitivity = gaussian(key_list[18], (TOKENS, FUTURE_LENGTH), 1.0, 6.0, ((0, 8), (1, 4)))
    return dict(patch_observations=patch_observations, sequence_labels=sequence_labels, leading_filler_count=leading_filler_count, intake_latent_matrix=intake_latent_matrix, intake_latent_offset=intake_latent_offset, intake_emit_matrix=intake_emit_matrix, intake_emit_offset=intake_emit_offset, intake_shortcut_matrix=intake_shortcut_matrix, attention_entry_matrices=attention_entry_matrices, attention_merge_matrix=attention_merge_matrix, feedforward_widen_matrix=feedforward_widen_matrix, feedforward_shrink_matrix=feedforward_shrink_matrix, layer_scale_factors=layer_scale_factors, readout_latent_matrix=readout_latent_matrix, readout_latent_offset=readout_latent_offset, readout_emit_matrix=readout_emit_matrix, readout_emit_offset=readout_emit_offset, readout_shortcut_matrix=readout_shortcut_matrix, loss_sensitivity=loss_sensitivity)


EPS = 1e-06
ROPE_BASE = 10000.0

@jax.custom_vjp
def low(v):
    return lax.optimization_barrier(v.astype(jnp.bfloat16)).astype(jnp.float32)

@jax.custom_vjp
def low_back(v):
    return v

def low_keep(v):
    return (low(v), None)

def low_pass(kept, grad):
    return (grad,)

def back_keep(v):
    return (v, None)

def back_low(kept, grad):
    return (low(grad),)
low.defvjp(low_keep, low_pass)
low_back.defvjp(back_keep, back_low)

def exact_dot(left, right):
    return jnp.dot(left, right, precision=lax.Precision.HIGHEST)

def layout_rows(series_row, pad_row, patch_len):
    count = series_row.shape[0]
    order = jnp.arange(count, dtype=jnp.int32)
    same_series = series_row[:, None] == series_row[None, :]
    earlier = order[None, :] < order[:, None]
    position = lax.optimization_barrier(jnp.sum(jnp.logical_and(same_series, earlier).astype(jnp.int32), axis=1))
    numbers = jnp.arange(pad_row.shape[0], dtype=jnp.int32)
    series_pad = lax.optimization_barrier(jnp.sum(jnp.where(series_row[:, None] == numbers[None, :], pad_row[None, :], 0), axis=1))
    pad_count = jnp.where(position == 0, series_pad, 0)
    padded = pad_count == patch_len
    diagonal = order[:, None] == order[None, :]
    reach = jnp.logical_or(jnp.logical_and(earlier, jnp.logical_not(padded)[None, :]), diagonal)
    allowed = jnp.logical_and(same_series, reach)
    keep_rows = jnp.where(padded, 0.0, 1.0).astype(jnp.float32)
    return (position, pad_count, allowed, keep_rows)

def rotary_tables(position, head_dim):
    half = head_dim // 2
    steps = jnp.arange(half, dtype=jnp.float32) / half
    inverse = jnp.exp(-math.log(ROPE_BASE) * steps)
    angles = position.astype(jnp.float32)[:, None] * inverse[None, :]
    return (jnp.cos(angles)[:, None, :], jnp.sin(angles)[:, None, :])

def rotate(heads_rows, cosine, sine):
    half = heads_rows.shape[-1] // 2
    first = heads_rows[..., :half]
    second = heads_rows[..., half:]
    return jnp.concatenate([first * cosine - second * sine, second * cosine + first * sine], axis=-1)

def norm_apply(resid, gain):
    return resid * lax.rsqrt(lax.optimization_barrier(jnp.mean(resid * resid, axis=-1, keepdims=True)) + EPS) * gain

def attend_block(block):
    query_rows, key_rows, value_rows, allowed = block
    scale = 1.0 / math.sqrt(query_rows.shape[-1])
    scores = low_back(jnp.einsum('qhd,khd->hqk', query_rows, key_rows, precision=lax.Precision.HIGHEST) * scale)
    scores = jnp.where(allowed[None], scores, -1e+30)
    peak = lax.optimization_barrier(jnp.max(scores, axis=-1, keepdims=True))
    weights = jnp.exp(scores - peak)
    probs = low(weights / lax.optimization_barrier(jnp.sum(weights, axis=-1, keepdims=True)))
    return jnp.einsum('hqk,khd->qhd', probs, value_rows, precision=lax.Precision.HIGHEST)

def layer_apply(resid, qkv_full, out_full, up_full, down_full, gain_pair, cosine, sine, allowed):
    rows = resid.shape[0]
    blocks = allowed.shape[0]
    width = qkv_full.shape[0]
    normed = low(norm_apply(resid, gain_pair[0]))
    projected = low_back(exact_dot(normed, qkv_full))
    query_rows = low(rotate(projected[:, :width].reshape(rows, HEADS, HEAD_DIM), cosine, sine))
    key_rows = low(rotate(projected[:, width:2 * width].reshape(rows, HEADS, HEAD_DIM), cosine, sine))
    value_rows = low(projected[:, 2 * width:].reshape(rows, HEADS, HEAD_DIM))
    block_shape = (blocks, rows // blocks, HEADS, HEAD_DIM)
    mixed = lax.map(jax.checkpoint(attend_block), (query_rows.reshape(block_shape), key_rows.reshape(block_shape), value_rows.reshape(block_shape), allowed))
    mixed = low(low_back(mixed.reshape(rows, width)))
    middle = resid + low_back(exact_dot(mixed, out_full))
    normed_second = low(norm_apply(middle, gain_pair[1]))
    hidden_pre = low_back(exact_dot(normed_second, up_full))
    hidden_act = low(jax.nn.gelu(hidden_pre, approximate=True))
    return middle + low_back(exact_dot(hidden_act, down_full))

def reference(patch_observations, sequence_labels, leading_filler_count, intake_latent_matrix, intake_latent_offset, intake_emit_matrix, intake_emit_offset, intake_shortcut_matrix, attention_entry_matrices, attention_merge_matrix, feedforward_widen_matrix, feedforward_shrink_matrix, layer_scale_factors, readout_latent_matrix, readout_latent_offset, readout_emit_matrix, readout_emit_offset, readout_shortcut_matrix, loss_sensitivity):
    patch_len = patch_observations.shape[1]
    position, pad_count, allowed, keep_rows = jax.vmap(partial(layout_rows, patch_len=patch_len))(sequence_labels, leading_filler_count)
    cosine, sine = rotary_tables(position.reshape(-1), HEAD_DIM)
    columns = jnp.arange(patch_len, dtype=jnp.int32)
    pad_mask = jnp.where(columns[None, :] < pad_count.reshape(-1)[:, None], 1.0, 0.0).astype(jnp.float32)
    feature_retain_flags = keep_rows.reshape(-1)[:, None]

    def evaluate_network(values_in, inner_in, inner_bias_in, outer_in, outer_bias_in, skip_in, qkv_in, out_in, up_in, down_in, gains_in, head_inner_in, head_inner_bias_in, head_outer_in, head_outer_bias_in, head_skip_in):
        features = jnp.concatenate([values_in * (1.0 - pad_mask), pad_mask], axis=1)
        entry_pre = low_back(exact_dot(features, inner_in) + inner_bias_in)
        entry_hidden = low(jax.nn.silu(entry_pre))
        resid = low_back(exact_dot(entry_hidden, outer_in) + outer_bias_in + exact_dot(features, skip_in))
        for layer_index in range(qkv_in.shape[0]):
            resid = layer_apply(resid, qkv_in[layer_index], out_in[layer_index], up_in[layer_index], down_in[layer_index], gains_in[layer_index], cosine, sine, allowed)
        top = low(resid)
        head_pre = low_back(exact_dot(top, head_inner_in) + head_inner_bias_in)
        head_hidden = low(jax.nn.silu(head_pre))
        return (exact_dot(head_hidden, head_outer_in) + head_outer_bias_in + exact_dot(top, head_skip_in)) * feature_retain_flags
    network_arguments = (patch_observations, intake_latent_matrix, intake_latent_offset, intake_emit_matrix, intake_emit_offset, intake_shortcut_matrix, attention_entry_matrices, attention_merge_matrix, feedforward_widen_matrix, feedforward_shrink_matrix, layer_scale_factors, readout_latent_matrix, readout_latent_offset, readout_emit_matrix, readout_emit_offset, readout_shortcut_matrix)
    real_number_array = tuple((item.astype(jnp.float32) for item in network_arguments))
    estimated_future, reverse_chain_rule = jax.vjp(evaluate_network, *real_number_array)
    derivative_bundle = reverse_chain_rule(loss_sensitivity.astype(jnp.float32))
    return (estimated_future.astype(jnp.bfloat16), derivative_bundle[0], derivative_bundle[1], derivative_bundle[2], derivative_bundle[3], derivative_bundle[4], derivative_bundle[5], derivative_bundle[6], derivative_bundle[7], derivative_bundle[8], derivative_bundle[9], derivative_bundle[10], derivative_bundle[11], derivative_bundle[12], derivative_bundle[13], derivative_bundle[14], derivative_bundle[15])
```

```python
from functools import partial
import math

import jax
import jax.numpy as jnp
from jax import lax
from jax.experimental import pallas as pl
from jax.experimental.pallas import tpu as pltpu
from jax.sharding import PartitionSpec as P

MODEL_WIDTH = 1280
HEADS = 16
HEAD_DIM = 80


EPS = 1e-06
ROPE_BASE = 10000.0


def layout_rows(series_row, pad_row, patch_len):
    count = series_row.shape[0]
    order = jnp.arange(count, dtype=jnp.int32)
    same_series = series_row[:, None] == series_row[None, :]
    earlier = order[None, :] < order[:, None]
    position = jnp.sum(jnp.logical_and(same_series, earlier).astype(jnp.int32), axis=1)
    numbers = jnp.arange(pad_row.shape[0], dtype=jnp.int32)
    series_pad = jnp.sum(
        jnp.where(series_row[:, None] == numbers[None, :], pad_row[None, :], 0), axis=1
    )
    pad_count = jnp.where(position == 0, series_pad, 0)
    padded = pad_count == patch_len
    diagonal = order[:, None] == order[None, :]
    reach = jnp.logical_or(jnp.logical_and(earlier, jnp.logical_not(padded)[None, :]), diagonal)
    allowed = jnp.logical_and(same_series, reach)
    keep_rows = jnp.where(padded, 0.0, 1.0).astype(jnp.float32)
    return (position, pad_count, allowed, keep_rows)


def rotary_tables(position, head_dim):
    half = head_dim // 2
    steps = jnp.arange(half, dtype=jnp.float32) / half
    inverse = jnp.exp(-math.log(ROPE_BASE) * steps)
    angles = position.astype(jnp.float32)[:, None] * inverse[None, :]
    return (jnp.cos(angles)[:, None, :], jnp.sin(angles)[:, None, :])


def rotate(heads_rows, cosine, sine):
    half = heads_rows.shape[-1] // 2
    first = heads_rows[..., :half]
    second = heads_rows[..., half:]
    return jnp.concatenate(
        [first * cosine - second * sine, second * cosine + first * sine], axis=-1
    )


def unrotate(grad_rows, cosine, sine):
    half = grad_rows.shape[-1] // 2
    first = grad_rows[..., :half]
    second = grad_rows[..., half:]
    return jnp.concatenate(
        [first * cosine + second * sine, second * cosine - first * sine], axis=-1
    )


def norm_apply(resid, gain):
    return resid * lax.rsqrt(jnp.mean(resid * resid, axis=-1, keepdims=True) + EPS) * gain


def dyadic_accumulation(left, right):
    return lax.dot_general(
        left, right, (((0,), (0,)), ((), ())), preferred_element_type=jnp.float32
    )


def reverse_matmul_answer(grad_rows, weight):
    return lax.dot_general(
        grad_rows, weight, (((1,), (1,)), ((), ())), preferred_element_type=jnp.float32
    )


def masked_scores(query_rows, key_rows, allowed):
    scale = 1.0 / math.sqrt(query_rows.shape[-1])
    scores = (
        jnp.einsum("qhd,khd->hqk", query_rows, key_rows, preferred_element_type=jnp.float32) * scale
    )
    return jnp.where(allowed[None], scores, -1e30)


def attend_forward(query_rows, key_rows, value_rows, allowed):
    scores = masked_scores(query_rows, key_rows, allowed)
    peak = jnp.max(scores, axis=-1, keepdims=True)
    weights = jnp.exp(scores - peak)
    total = jnp.sum(weights, axis=-1, keepdims=True)
    probs = (weights / total).astype(jnp.bfloat16)
    mixed = jnp.einsum("hqk,khd->qhd", probs, value_rows, preferred_element_type=jnp.float32)
    return (mixed, peak + jnp.log(total))


def attend_backward(query_rows, key_rows, value_rows, allowed, log_total, grad_mixed):
    scale = 1.0 / math.sqrt(query_rows.shape[-1])
    scores = masked_scores(query_rows, key_rows, allowed)
    probs = jnp.where(allowed[None], jnp.exp(scores - log_total), 0.0)
    grad_probs = jnp.einsum(
        "qhd,khd->hqk", grad_mixed, value_rows, preferred_element_type=jnp.float32
    )
    grad_values = jnp.einsum(
        "hqk,qhd->khd", probs.astype(jnp.bfloat16), grad_mixed, preferred_element_type=jnp.float32
    )
    center = jnp.sum(grad_probs * probs, axis=-1, keepdims=True)
    grad_scores = (probs * (grad_probs - center)).astype(jnp.bfloat16)
    grad_query = (
        jnp.einsum("hqk,khd->qhd", grad_scores, key_rows, preferred_element_type=jnp.float32)
        * scale
    )
    grad_keys = (
        jnp.einsum("hqk,qhd->khd", grad_scores, query_rows, preferred_element_type=jnp.float32)
        * scale
    )
    return (grad_query, grad_keys, grad_values)


def swap(v, bit):
    size = lax.axis_size("dp")
    return lax.ppermute(v, "dp", [(i, i ^ (1 << bit)) for i in range(size)])


def outer_groups():
    size = lax.axis_size("dp")
    return [[j + 8 * o for o in range(size // 8)] for j in range(8)]


def place_kernel(plan, piece_count, out_count, me_ref, *refs):
    pieces = refs[:piece_count]
    outs = refs[piece_count : piece_count + out_count]
    sems = refs[piece_count + out_count]
    copies = []
    for n, (piece, out, rel, src, dst, width) in enumerate(plan):
        block = me_ref[0] ^ rel
        copies.append(
            pltpu.make_async_copy(
                pieces[piece].at[:, :, pl.ds(src, width)],
                outs[out].at[:, block, :, pl.ds(dst, width)],
                sems.at[n],
            )
        )
    for copy in copies:
        copy.start()
    for copy in copies:
        copy.wait()


def place(me, pieces, widths):
    plan = []
    arrays = []
    for rel, array, runs in pieces:
        for src, out, dst, width in runs:
            plan.append((len(arrays), out, rel, src, dst, width))
        arrays.append(array)
    outer, rows, _ = arrays[0].shape
    outs = pl.pallas_call(
        partial(place_kernel, plan, len(arrays), len(widths)),
        out_shape=[jax.ShapeDtypeStruct((outer, 8, rows, w), arrays[0].dtype) for w in widths],
        in_specs=[pl.BlockSpec(memory_space=pltpu.SMEM)]
        + [pl.BlockSpec(memory_space=pl.ANY)] * len(arrays),
        out_specs=[pl.BlockSpec(memory_space=pl.ANY)] * len(widths),
        scratch_shapes=[pltpu.SemaphoreType.DMA((len(plan),))],
        cost_estimate=pl.CostEstimate(
            flops=0, bytes_accessed=2 * 8 * arrays[0].size * 2, transcendentals=0
        ),
    )(me, *arrays)
    return [o.reshape(outer * 8 * rows, o.shape[-1]) for o in outs]


def runs_of(first, width, edges):
    runs = []
    for out, (lo, hi) in enumerate(zip(edges[:-1], edges[1:])):
        a, b = max(first, lo), min(first + width, hi)
        if a < b:
            runs.append((a - first, out, a - lo, b - a))
    return runs


def gather_rows(me, own, widths):
    held = lax.all_gather(own, "head", axis=0, tiled=True)[None]
    if lax.axis_size("dp") > 8:
        held = lax.all_gather(
            held, "dp", axis=0, tiled=True, axis_index_groups=outer_groups()
        )
    columns = own.shape[1]
    half = columns // 256 * 128
    from_x = swap(held, 1)
    from_y = swap(held, 2)
    far_left = swap(from_y[:, :, :half], 1)
    far_right = swap(from_x[:, :, half:], 2)
    edges = [0]
    for w in widths:
        edges.append(edges[-1] + w)
    pieces = []
    for rel, array, first in (
        (0, held, 0),
        (2, from_x, 0),
        (4, from_y, 0),
        (6, far_left, 0),
        (6, far_right, half),
    ):
        runs = runs_of(first, array.shape[-1], edges)
        pieces.append((rel, array, runs))
        pieces.append((rel | 1, swap(array, 0), runs))
    return place(me, pieces, widths)


def pair_rows(me, left, right):
    rows, width = left.shape
    outer = lax.axis_size("dp") // 8
    view = left.reshape(rows, outer, 4, 2, width // (8 * outer))
    core = me & 1
    mine = lax.dynamic_index_in_dim(view, core, 3, keepdims=False)
    other = lax.dynamic_index_in_dim(view, 1 - core, 3, keepdims=False)
    left_pair = jnp.concatenate([mine, swap(other, 0)], axis=0)
    right_pair = jnp.concatenate([right, swap(right, 0)], axis=0)
    return left_pair, right_pair


def low_sum(*parts):
    total = parts[0].astype(jnp.float32)
    for part in parts[1:]:
        total = total + part.astype(jnp.float32)
    return total.astype(jnp.bfloat16)


def sum_rows(blocks):
    outer = lax.axis_size("dp") // 8
    group = lax.axis_size("head")
    far = blocks(6)
    half = far.shape[-1] // 256 * 128
    far_x = swap(far[..., :half], 1)
    far_y = swap(far[..., half:], 2)
    at_x = blocks(2)
    at_y = blocks(4)
    x_left = swap(at_x[..., :half], 1)
    y_right = swap(at_y[..., half:], 2)
    y_left = swap(low_sum(at_y[..., :half], far_x), 2)
    x_right = swap(low_sum(at_x[..., half:], far_y), 1)
    own = blocks(0)
    sums = []
    for total in (
        low_sum(own[..., :half], x_left, y_left),
        low_sum(own[..., half:], y_right, x_right),
    ):
        rows = total.shape[-2]
        lead = total.shape[:-2]
        if outer > 1:
            total = lax.psum_scatter(
                total.reshape(*lead, outer, rows // outer, -1),
                "dp",
                scatter_dimension=len(lead),
                tiled=True,
                axis_index_groups=outer_groups(),
            )
        total = total.reshape(*lead, group, rows // (outer * group), -1)
        spread = lax.all_to_all(
            total, "head", split_axis=len(lead), concat_axis=len(lead), tiled=True
        )
        sums.append(jnp.sum(spread.astype(jnp.float32), axis=len(lead)))
    return jnp.concatenate(sums, axis=-1)


def weight_sums(me, pairs):
    lefts = jnp.stack([pair[0] for pair in pairs])
    rights = jnp.stack([pair[1] for pair in pairs])
    chip = me >> 1

    def blocks(rel):
        picked = lax.dynamic_index_in_dim(lefts, chip ^ (rel >> 1), 3, keepdims=False)
        picked = picked.reshape(lefts.shape[0], lefts.shape[1], -1)
        return jnp.einsum("wtr,wtc->wrc", picked, rights,
                          preferred_element_type=jnp.float32).astype(jnp.bfloat16)

    return sum_rows(blocks)

EXTRA_ROWS = 8


def sum_everywhere(me, main, extra):
    group = lax.axis_size("head")
    outer = lax.axis_size("dp") // 8
    devices = 8 * outer * group
    columns = main.shape[1]
    count = extra.shape[0]
    own = main.shape[0] // devices
    extra = jnp.pad(extra, ((0, EXTRA_ROWS * devices - count), (0, 0)))
    rows = jnp.concatenate(
        [main.reshape(devices, own, columns), extra.reshape(devices, EXTRA_ROWS, columns)], axis=1
    ).astype(jnp.bfloat16)
    view = rows.reshape(outer, 4, 2, group * (own + EXTRA_ROWS), columns)
    core = me & 1
    other = lax.dynamic_index_in_dim(view, 1 - core, 2, keepdims=False)
    pair = low_sum(lax.dynamic_index_in_dim(view, core, 2, keepdims=False), swap(other, 0))
    chip = me >> 1

    def blocks(rel):
        picked = lax.dynamic_index_in_dim(pair, chip ^ (rel >> 1), 1, keepdims=False)
        return picked.reshape(-1, columns)

    summed = sum_rows(blocks).astype(jnp.bfloat16)
    (whole,) = gather_rows(me.reshape(1), summed, [columns])
    whole = whole.reshape(devices, own + EXTRA_ROWS, columns).astype(jnp.float32)
    return (
        whole[:, :own].reshape(devices * own, columns),
        whole[:, own:].reshape(-1, columns)[:count],
    )


def layer_forward(resid, weights, cosine, sine, allowed):
    qkv_full, out_full, up_full, down_full, gain_pair = weights
    gains = gain_pair.astype(jnp.float32)
    rows = resid.shape[0]
    normed_first = norm_apply(resid, gains[0]).astype(jnp.bfloat16)
    projected = jnp.dot(normed_first, qkv_full, preferred_element_type=jnp.float32)
    query_rows = rotate(
        projected[:, :MODEL_WIDTH].reshape(rows, HEADS, HEAD_DIM), cosine, sine
    ).astype(jnp.bfloat16)
    key_rows = rotate(
        projected[:, MODEL_WIDTH : 2 * MODEL_WIDTH].reshape(rows, HEADS, HEAD_DIM), cosine, sine
    ).astype(jnp.bfloat16)
    value_rows = projected[:, 2 * MODEL_WIDTH :].reshape(rows, HEADS, HEAD_DIM).astype(jnp.bfloat16)

    mixed, log_total = attend_forward(query_rows, key_rows, value_rows, allowed)
    mixed_low = mixed.reshape(rows, MODEL_WIDTH).astype(jnp.bfloat16)
    middle = resid + jnp.dot(mixed_low, out_full, preferred_element_type=jnp.float32)
    normed_second = norm_apply(middle, gains[1]).astype(jnp.bfloat16)
    hidden_pre = jnp.dot(normed_second, up_full, preferred_element_type=jnp.float32)
    hidden_act = jax.nn.gelu(hidden_pre, approximate=True).astype(jnp.bfloat16)
    result = middle + jnp.dot(hidden_act, down_full, preferred_element_type=jnp.float32)
    saved = (
        resid,
        normed_first,
        query_rows,
        key_rows,
        value_rows,
        log_total,
        mixed_low,
        middle,
        normed_second,
        hidden_pre,
    )
    return (result, saved)


def layer_backward(saved, weights, cosine, sine, allowed, grad_result):
    (
        resid,
        normed_first,
        query_rows,
        key_rows,
        value_rows,
        log_total,
        mixed_low,
        middle,
        normed_second,
        hidden_pre,
    ) = saved
    qkv_full, out_full, up_full, down_full, gain_pair = weights
    gains = gain_pair.astype(jnp.float32)
    rows = resid.shape[0]
    grad_branch = grad_result.astype(jnp.bfloat16)
    hidden_act, gelu_pull = jax.vjp(partial(jax.nn.gelu, approximate=True), hidden_pre)
    hidden_low = hidden_act.astype(jnp.bfloat16)
    grad_act = reverse_matmul_answer(grad_branch, down_full)
    grad_pre = gelu_pull(grad_act)[0].astype(jnp.bfloat16)
    grad_normed_second = reverse_matmul_answer(grad_pre, up_full)
    unused_second, second_pull = jax.vjp(norm_apply, middle, gains[1])
    grad_middle_norm, grad_gain_second = second_pull(grad_normed_second)
    grad_middle = grad_result + grad_middle_norm
    grad_attn = grad_middle.astype(jnp.bfloat16)
    grad_mixed = (
        reverse_matmul_answer(grad_attn, out_full)
        .astype(jnp.bfloat16)
        .reshape(rows, HEADS, HEAD_DIM)
    )

    grad_query, grad_keys, grad_values = attend_backward(
        query_rows, key_rows, value_rows, allowed, log_total, grad_mixed
    )
    grad_query = unrotate(grad_query, cosine, sine).reshape(rows, MODEL_WIDTH)
    grad_keys = unrotate(grad_keys, cosine, sine).reshape(rows, MODEL_WIDTH)
    grad_values = grad_values.reshape(rows, MODEL_WIDTH)
    grad_projected = jnp.concatenate([grad_query, grad_keys, grad_values], axis=1).astype(
        jnp.bfloat16
    )
    grad_normed_first = reverse_matmul_answer(grad_projected, qkv_full)
    unused_first, first_pull = jax.vjp(norm_apply, resid, gains[0])
    grad_resid_norm, grad_gain_first = first_pull(grad_normed_first)
    grad_resid = grad_middle + grad_resid_norm
    left_rows = (normed_first, mixed_low, normed_second, hidden_low)
    right_rows = (grad_projected, grad_attn, grad_pre, grad_branch)
    return (grad_resid, left_rows, right_rows, (grad_gain_first, grad_gain_second))


def body(
    patch_observations,
    sequence_labels,
    leading_filler_count,
    intake_latent_matrix,
    intake_latent_offset,
    intake_emit_matrix,
    intake_emit_offset,
    intake_shortcut_matrix,
    attention_entry_matrices,
    attention_merge_matrix,
    feedforward_widen_matrix,
    feedforward_shrink_matrix,
    layer_scale_factors,
    readout_latent_matrix,
    readout_latent_offset,
    readout_emit_matrix,
    readout_emit_offset,
    readout_shortcut_matrix,
    loss_sensitivity,
):
    patch_len = patch_observations.shape[1]
    position, pad_count, allowed, keep_rows = layout_rows(
        sequence_labels[0], leading_filler_count[0], patch_len
    )
    cosine, sine = rotary_tables(position, HEAD_DIM)
    columns = jnp.arange(patch_len, dtype=jnp.int32)
    pad_mask = columns[None, :] < pad_count[:, None]
    features = jnp.concatenate(
        [
            jnp.where(pad_mask, jnp.zeros_like(patch_observations), patch_observations),
            pad_mask.astype(jnp.bfloat16),
        ],
        axis=1,
    )
    entry_pre = (
        jnp.dot(features, intake_latent_matrix, preferred_element_type=jnp.float32)
        + intake_latent_offset
    )
    entry_hidden = jax.nn.silu(entry_pre).astype(jnp.bfloat16)
    resid = (
        jnp.dot(entry_hidden, intake_emit_matrix, preferred_element_type=jnp.float32)
        + intake_emit_offset
        + jnp.dot(features, intake_shortcut_matrix, preferred_element_type=jnp.float32)
    )
    layer_count = attention_entry_matrices.shape[0]
    me = lax.axis_index("dp").astype(jnp.int32)
    places = me.reshape(1)
    own_count = layer_scale_factors.shape[2]
    gain_columns = layer_scale_factors.reshape(2 * layer_count, own_count).T
    gain_columns = jnp.pad(gain_columns, ((0, 0), (0, 128 - 2 * layer_count)))
    layer_weights = []
    for layer_index in range(layer_count):
        entry_own = attention_entry_matrices[layer_index]
        widths = [3 * MODEL_WIDTH]
        if layer_index == 0:
            entry_own = jnp.concatenate([entry_own, gain_columns], axis=1)
            widths.append(128)
        entry_all = gather_rows(places, entry_own, widths)
        if layer_index == 0:
            gain_rows = entry_all[1][:, : 2 * layer_count].T.reshape(layer_count, 2, -1)
        rest_all = gather_rows(
            places,
            jnp.concatenate(
                [
                    attention_merge_matrix[layer_index],
                    feedforward_widen_matrix[layer_index],
                    feedforward_shrink_matrix[layer_index],
                ],
                axis=1,
            ),
            [MODEL_WIDTH] * 3,
        )
        layer_weights.append((entry_all[0], *rest_all, gain_rows[layer_index]))
    saved_states = []
    for layer_index in range(layer_count):
        resid, saved = layer_forward(resid, layer_weights[layer_index], cosine, sine, allowed)
        saved_states.append(saved)
    final_layer_vectors, keep_all = (
        lax.all_gather(resid.astype(jnp.bfloat16), "head", axis=0, tiled=True),
        lax.all_gather(keep_rows.astype(jnp.bfloat16), "head", axis=0, tiled=True),
    )
    feature_retain_flags = keep_all.astype(jnp.float32)[:, None]
    head_pre = (
        jnp.dot(final_layer_vectors, readout_latent_matrix, preferred_element_type=jnp.float32)
        + readout_latent_offset
    )
    hidden_cols = jax.nn.silu(head_pre).astype(jnp.bfloat16)
    latent_token_vectors = lax.all_gather(hidden_cols, "head", axis=1, tiled=True)
    estimated_future = (
        jnp.dot(latent_token_vectors, readout_emit_matrix, preferred_element_type=jnp.float32)
        + readout_emit_offset
        + jnp.dot(final_layer_vectors, readout_shortcut_matrix, preferred_element_type=jnp.float32)
    ) * feature_retain_flags
    token_predictions = estimated_future.astype(jnp.bfloat16)
    prediction_derivative = (loss_sensitivity.astype(jnp.float32) * feature_retain_flags).astype(
        jnp.bfloat16
    )
    readout_emit_matrix_deriv = dyadic_accumulation(latent_token_vectors, prediction_derivative)
    readout_emit_offset_deriv = jnp.sum(prediction_derivative.astype(jnp.float32), axis=0)
    readout_shortcut_deriv = dyadic_accumulation(final_layer_vectors, prediction_derivative)
    grad_hidden = lax.psum_scatter(
        reverse_matmul_answer(prediction_derivative, readout_emit_matrix).astype(jnp.bfloat16),
        "head",
        scatter_dimension=1,
        tiled=True,
    ).astype(jnp.float32)
    unused_head, head_pull = jax.vjp(jax.nn.silu, head_pre)
    head_preactivation_gradient = head_pull(grad_hidden)[0].astype(jnp.bfloat16)
    grad_head_inner = dyadic_accumulation(final_layer_vectors, head_preactivation_gradient)
    grad_head_inner_bias = jnp.sum(head_preactivation_gradient.astype(jnp.float32), axis=0)
    top_gradient = reverse_matmul_answer(
        head_preactivation_gradient, readout_latent_matrix
    ) + reverse_matmul_answer(prediction_derivative, readout_shortcut_matrix)
    grad_resid = lax.psum_scatter(
        top_gradient.astype(jnp.bfloat16), "head", scatter_dimension=0, tiled=True
    ).astype(jnp.float32)
    head_sums = (
        lax.psum(grad_head_inner.astype(jnp.bfloat16), "dp").astype(jnp.float32),
        lax.psum(grad_head_inner_bias.astype(jnp.bfloat16), "dp").astype(jnp.float32),
        lax.psum(readout_emit_matrix_deriv.astype(jnp.bfloat16), "dp").astype(jnp.float32),
        lax.psum(readout_emit_offset_deriv.astype(jnp.bfloat16), "dp").astype(jnp.float32),
        lax.psum(readout_shortcut_deriv.astype(jnp.bfloat16), "dp").astype(jnp.float32),
    )
    layer_sums = [None] * layer_count
    gain_sums = [None] * layer_count
    for layer_index in reversed(range(layer_count)):
        grad_resid, left_rows, right_rows, gain_sums[layer_index] = layer_backward(
            saved_states[layer_index], layer_weights[layer_index], cosine, sine, allowed, grad_resid
        )
        pairs = [
            pair_rows(me, left, right) for left, right in zip(left_rows, right_rows, strict=True)
        ]
        rest = weight_sums(me, pairs[1:])
        layer_sums[layer_index] = (weight_sums(me, pairs[:1])[0], rest[0], rest[1], rest[2])
    grad_entry = grad_resid.astype(jnp.bfloat16)
    grad_entry_outer = dyadic_accumulation(entry_hidden, grad_entry)
    grad_entry_outer_bias = jnp.sum(grad_entry.astype(jnp.float32), axis=0)
    grad_entry_skip = dyadic_accumulation(features, grad_entry)
    unused_entry, entry_pull = jax.vjp(jax.nn.silu, entry_pre)
    grad_entry_pre = entry_pull(reverse_matmul_answer(grad_entry, intake_emit_matrix))[0].astype(
        jnp.bfloat16
    )
    grad_entry_inner = dyadic_accumulation(features, grad_entry_pre)
    grad_entry_inner_bias = jnp.sum(grad_entry_pre.astype(jnp.float32), axis=0)
    grad_features = reverse_matmul_answer(
        grad_entry_pre, intake_latent_matrix
    ) + reverse_matmul_answer(grad_entry, intake_shortcut_matrix)
    values_grad = jnp.where(pad_mask, 0.0, grad_features[:, :patch_len])
    extra_rows = jnp.concatenate(
        [
            grad_entry_inner,
            grad_entry_skip,
            grad_entry_inner_bias[None],
            grad_entry_outer_bias[None],
        ]
        + [row[None] for pair in gain_sums for row in pair],
        axis=0,
    )
    entry_main, entry_extra = sum_everywhere(me, grad_entry_outer, extra_rows)
    inner_rows = 2 * patch_len
    entry_sums = (
        entry_extra[:inner_rows],
        entry_extra[2 * inner_rows],
        entry_main,
        entry_extra[2 * inner_rows + 1],
        entry_extra[inner_rows : 2 * inner_rows],
    )
    gain_all = entry_extra[2 * inner_rows + 2 : 2 * inner_rows + 2 + 2 * layer_count]
    own_place = (me * lax.axis_size("head") + lax.axis_index("head")) * own_count
    gains_grad = lax.dynamic_slice_in_dim(gain_all, own_place, own_count, 1).reshape(
        layer_count, 2, own_count
    )
    qkv_grad = jnp.stack([layer_sums[member][0] for member in range(layer_count)])
    out_grad = jnp.stack([layer_sums[member][1] for member in range(layer_count)])
    up_grad = jnp.stack([layer_sums[member][2] for member in range(layer_count)])
    down_grad = jnp.stack([layer_sums[member][3] for member in range(layer_count)])
    return (
        token_predictions,
        values_grad,
        entry_sums[0],
        entry_sums[1],
        entry_sums[2],
        entry_sums[3],
        entry_sums[4],
        qkv_grad,
        out_grad,
        up_grad,
        down_grad,
        gains_grad,
        head_sums[0],
        head_sums[1],
        head_sums[2],
        head_sums[3],
        head_sums[4],
    )


def solution(mesh):
    return jax.shard_map(
        body,
        mesh=mesh,
        in_specs=(
            P(("dp", "head"), None),
            P(("dp", "head"), None),
            P(("dp", "head"), None),
            P(),
            P(),
            P(),
            P(),
            P(),
            P(None, ("dp", "head"), None),
            P(None, ("dp", "head"), None),
            P(None, ("dp", "head"), None),
            P(None, ("dp", "head"), None),
            P(None, None, ("dp", "head")),
            P(None, "head"),
            P("head"),
            P(None, "head"),
            P("head"),
            P(None, "head"),
            P("dp", "head"),
        ),
        out_specs=(
            P("dp", "head"),
            P(("dp", "head"), None),
            P(),
            P(),
            P(),
            P(),
            P(),
            P(None, ("dp", "head"), None),
            P(None, ("dp", "head"), None),
            P(None, ("dp", "head"), None),
            P(None, ("dp", "head"), None),
            P(None, None, ("dp", "head")),
            P(None, "head"),
            P("head"),
            P(None, "head"),
            P("head"),
            P(None, "head"),
        ),
        check_vma=False,
    )
```

```python
from functools import partial
import math

import jax
import jax.numpy as jnp
from jax import lax
from jax.experimental import pallas as pl
from jax.experimental.pallas import tpu as pltpu
from jax.sharding import PartitionSpec as P

MODEL_WIDTH = 1280
HEADS = 16
HEAD_DIM = 80


EPS = 1e-06
ROPE_BASE = 10000.0


def layout_rows(series_row, pad_row, patch_len):
    count = series_row.shape[0]
    order = jnp.arange(count, dtype=jnp.int32)
    same_series = series_row[:, None] == series_row[None, :]
    earlier = order[None, :] < order[:, None]
    position = jnp.sum(jnp.logical_and(same_series, earlier).astype(jnp.int32), axis=1)
    numbers = jnp.arange(pad_row.shape[0], dtype=jnp.int32)
    series_pad = jnp.sum(
        jnp.where(series_row[:, None] == numbers[None, :], pad_row[None, :], 0), axis=1
    )
    pad_count = jnp.where(position == 0, series_pad, 0)
    padded = pad_count == patch_len
    diagonal = order[:, None] == order[None, :]
    reach = jnp.logical_or(jnp.logical_and(earlier, jnp.logical_not(padded)[None, :]), diagonal)
    allowed = jnp.logical_and(same_series, reach)
    keep_rows = jnp.where(padded, 0.0, 1.0).astype(jnp.float32)
    return (position, pad_count, allowed, keep_rows)


def rotary_tables(position, head_dim):
    half = head_dim // 2
    steps = jnp.arange(half, dtype=jnp.float32) / half
    inverse = jnp.exp(-math.log(ROPE_BASE) * steps)
    angles = position.astype(jnp.float32)[:, None] * inverse[None, :]
    return (jnp.cos(angles)[:, None, :], jnp.sin(angles)[:, None, :])


def rotate(heads_rows, cosine, sine):
    half = heads_rows.shape[-1] // 2
    first = heads_rows[..., :half]
    second = heads_rows[..., half:]
    return jnp.concatenate(
        [first * cosine - second * sine, second * cosine + first * sine], axis=-1
    )


def unrotate(grad_rows, cosine, sine):
    half = grad_rows.shape[-1] // 2
    first = grad_rows[..., :half]
    second = grad_rows[..., half:]
    return jnp.concatenate(
        [first * cosine + second * sine, second * cosine - first * sine], axis=-1
    )


def norm_apply(resid, gain):
    return resid * lax.rsqrt(jnp.mean(resid * resid, axis=-1, keepdims=True) + EPS) * gain


def dyadic_accumulation(left, right):
    return lax.dot_general(
        left, right, (((0,), (0,)), ((), ())), preferred_element_type=jnp.float32
    )


def reverse_matmul_answer(grad_rows, weight):
    return lax.dot_general(
        grad_rows, weight, (((1,), (1,)), ((), ())), preferred_element_type=jnp.float32
    )


def masked_scores(query_rows, key_rows, allowed):
    scale = 1.0 / math.sqrt(query_rows.shape[-1])
    scores = (
        jnp.einsum("qhd,khd->hqk", query_rows, key_rows, preferred_element_type=jnp.float32) * scale
    )
    return jnp.where(allowed[None], scores, -1e30)


def attend_forward(query_rows, key_rows, value_rows, allowed):
    scores = masked_scores(query_rows, key_rows, allowed)
    peak = jnp.max(scores, axis=-1, keepdims=True)
    weights = jnp.exp(scores - peak)
    total = jnp.sum(weights, axis=-1, keepdims=True)
    probs = (weights / total).astype(jnp.bfloat16)
    mixed = jnp.einsum("hqk,khd->qhd", probs, value_rows, preferred_element_type=jnp.float32)
    return (mixed, peak + jnp.log(total))


def attend_backward(query_rows, key_rows, value_rows, allowed, log_total, grad_mixed):
    scale = 1.0 / math.sqrt(query_rows.shape[-1])
    scores = masked_scores(query_rows, key_rows, allowed)
    probs = jnp.where(allowed[None], jnp.exp(scores - log_total), 0.0)
    grad_probs = jnp.einsum(
        "qhd,khd->hqk", grad_mixed, value_rows, preferred_element_type=jnp.float32
    )
    grad_values = jnp.einsum(
        "hqk,qhd->khd", probs.astype(jnp.bfloat16), grad_mixed, preferred_element_type=jnp.float32
    )
    center = jnp.sum(grad_probs * probs, axis=-1, keepdims=True)
    grad_scores = (probs * (grad_probs - center)).astype(jnp.bfloat16)
    grad_query = (
        jnp.einsum("hqk,khd->qhd", grad_scores, key_rows, preferred_element_type=jnp.float32)
        * scale
    )
    grad_keys = (
        jnp.einsum("hqk,qhd->khd", grad_scores, query_rows, preferred_element_type=jnp.float32)
        * scale
    )
    return (grad_query, grad_keys, grad_values)


def after(value, *earlier):
    return lax.optimization_barrier((value, *earlier))[0]


def swap(v, bit):
    size = lax.axis_size("dp")
    return lax.ppermute(v, "dp", [(i, i ^ (1 << bit)) for i in range(size)])


def outer_groups():
    size = lax.axis_size("dp")
    return [[j + 8 * o for o in range(size // 8)] for j in range(8)]


def place_kernel(plan, piece_count, out_count, me_ref, *refs):
    pieces = refs[:piece_count]
    outs = refs[piece_count : piece_count + out_count]
    held = refs[piece_count + out_count : piece_count + 2 * out_count]
    in_sems, out_sems = refs[piece_count + 2 * out_count :]
    inward, outward = [], []
    for n, (piece, rel, row, out, column) in enumerate(plan):
        source = pieces[piece]
        width = held[out].shape[-1]
        if width != source.shape[-1]:
            source = source.at[:, :, pl.ds(column, width)]
        spot = (slice(None), me_ref[0] ^ rel, pl.ds(row, source.shape[1]), slice(None))
        inward.append(pltpu.make_async_copy(source, held[out].at[spot], in_sems.at[n]))
        outward.append(
            pltpu.make_async_copy(held[out].at[spot], outs[out].at[spot], out_sems.at[n])
        )
    for copy in inward:
        copy.start()
    for copy, onward in zip(inward, outward):
        copy.wait()
        onward.start()
    for onward in outward:
        onward.wait()


def place(me, pieces, widths):
    plan = []
    for n, (rel, row, _) in enumerate(pieces):
        column = 0
        for out, width in enumerate(widths):
            plan.append((n, rel, row, out, column))
            column += width
    arrays = [array for _, _, array in pieces]
    lead, rows, _ = arrays[0].shape
    kind = arrays[0].dtype
    total = sum(8 * lead * rows * -(-w // 128) * 128 for w in widths) * 2
    outs = pl.pallas_call(
        partial(place_kernel, plan, len(arrays), len(widths)),
        out_shape=[jax.ShapeDtypeStruct((lead, 8, rows, w), kind) for w in widths],
        in_specs=[pl.BlockSpec(memory_space=pltpu.SMEM)]
        + [pl.BlockSpec(memory_space=pl.ANY)] * len(arrays),
        out_specs=[pl.BlockSpec(memory_space=pl.ANY)] * len(widths),
        scratch_shapes=[pltpu.VMEM((lead, 8, rows, w), kind) for w in widths]
        + [pltpu.SemaphoreType.DMA((len(plan),))] * 2,
        compiler_params=pltpu.CompilerParams(vmem_limit_bytes=total + (4 << 20)),
        cost_estimate=pl.CostEstimate(flops=0, bytes_accessed=2 * total, transcendentals=0),
    )(me, *arrays)
    outer = lax.axis_size("dp") // 8
    return [o.reshape(-1, outer * 8 * rows, o.shape[-1]) for o in outs]


def row_half(rows):
    return rows // 32 * 16 if rows >= 32 else rows // 2


def spread_rows(held, gate):
    half = row_half(held.shape[1])
    if gate is not None:
        held = after(held, *gate)
    from_x = swap(held, 1)
    from_y = swap(held, 2)
    far_top = swap(from_y[:, :half], 1)
    far_rest = swap(from_x[:, half:], 2)
    pieces = []
    for rel, row, array in (
        (0, 0, held),
        (2, 0, from_x),
        (4, 0, from_y),
        (6, 0, far_top),
        (6, half, far_rest),
    ):
        pieces.append((rel, row, array))
        pieces.append((rel | 1, row, swap(array, 0)))
    return pieces, (from_x, from_y)


def gather_head(own):
    held = lax.all_gather(own, "head", axis=0, tiled=True)[None]
    if lax.axis_size("dp") > 8:
        held = lax.all_gather(
            held, "dp", axis=0, tiled=True, axis_index_groups=outer_groups()
        )
    return held


def pair_rows(me, left, right):
    rows, width = left.shape
    outer = lax.axis_size("dp") // 8
    view = left.reshape(rows, outer, 4, 2, width // (8 * outer))
    core = me & 1
    mine = lax.dynamic_index_in_dim(view, core, 3, keepdims=False)
    other = lax.dynamic_index_in_dim(view, 1 - core, 3, keepdims=False)
    left_pair = jnp.concatenate([mine, swap(other, 0)], axis=0)
    right_pair = jnp.concatenate([right, swap(right, 0)], axis=0)
    return left_pair, right_pair


def low_sum(*parts):
    total = parts[0].astype(jnp.float32)
    for part in parts[1:]:
        total = total + part.astype(jnp.float32)
    return total.astype(jnp.bfloat16)


def sum_chips(blocks):
    far_one, far_two = blocks(6)
    far_one, far_two = swap(far_one, 1), swap(far_two, 2)
    x_one, x_two = blocks(2)
    y_one, y_two = blocks(4)
    x_one, y_two = swap(x_one, 1), swap(y_two, 2)
    y_one = swap(low_sum(y_one, far_one), 2)
    x_two = swap(low_sum(x_two, far_two), 1)
    own_one, own_two = blocks(0)
    return low_sum(own_one, x_one, y_one), low_sum(own_two, y_two, x_two)


def sum_group(total):
    outer = lax.axis_size("dp") // 8
    group = lax.axis_size("head")
    lead = total.shape[:-2]
    rows, columns = total.shape[-2:]
    if outer > 1:
        total = lax.psum_scatter(
            total.reshape(*lead, outer, rows // outer, columns),
            "dp",
            scatter_dimension=len(lead),
            tiled=True,
            axis_index_groups=outer_groups(),
        )
    total = total.reshape(*lead, rows // outer, columns)
    return lax.psum_scatter(total, "head", scatter_dimension=len(lead), tiled=True)


def weight_blocks(me, pairs):
    lefts = jnp.stack([pair[0] for pair in pairs])
    rights = jnp.stack([pair[1] for pair in pairs])
    chip = me >> 1
    half = rights.shape[-1] // 2

    def blocks(rel):
        picked = lax.dynamic_index_in_dim(lefts, chip ^ (rel >> 1), 3, keepdims=False)
        picked = picked.reshape(lefts.shape[0], lefts.shape[1], -1)
        return tuple(
            jnp.einsum(
                "wtr,wtc->wrc", picked, part, preferred_element_type=jnp.float32
            ).astype(jnp.bfloat16)
            for part in (rights[..., :half], rights[..., half:])
        )

    return blocks


def weight_sums(me, pairs):
    one, two = sum_chips(weight_blocks(me, pairs))
    return sum_group(jnp.concatenate([one, two], axis=-1)).astype(jnp.float32)


def column_sums(me, pairs):
    group = lax.axis_size("head")
    outer = lax.axis_size("dp") // 8
    totals = []
    for part in sum_chips(weight_blocks(me, pairs)):
        count, rows, columns = part.shape
        part = part.reshape(count, rows, group // 2, 2 * columns // group)
        totals.append(jnp.moveaxis(part, 2, 0))
    total = jnp.concatenate(totals, axis=0)
    summed = lax.psum_scatter(total, "head", scatter_dimension=0, tiled=True)[0]
    count, rows, columns = summed.shape
    held = summed.reshape(count * outer, rows // outer, columns)
    pieces, _ = spread_rows(held, None)
    (whole,) = place(me.reshape(1), pieces, [columns])
    return whole.astype(jnp.float32)


EXTRA_ROWS = 8


def sum_everywhere(me, main, extra):
    group = lax.axis_size("head")
    outer = lax.axis_size("dp") // 8
    devices = 8 * outer * group
    columns = main.shape[1]
    count = extra.shape[0]
    own = main.shape[0] // devices
    extra = jnp.pad(extra, ((0, EXTRA_ROWS * devices - count), (0, 0)))
    rows = jnp.concatenate(
        [main.reshape(devices, own, columns), extra.reshape(devices, EXTRA_ROWS, columns)], axis=1
    ).astype(jnp.bfloat16)
    view = rows.reshape(outer, 4, 2, group * (own + EXTRA_ROWS), columns)
    core = me & 1
    other = lax.dynamic_index_in_dim(view, 1 - core, 2, keepdims=False)
    pair = low_sum(lax.dynamic_index_in_dim(view, core, 2, keepdims=False), swap(other, 0))
    chip = me >> 1

    def blocks(rel):
        picked = lax.dynamic_index_in_dim(pair, chip ^ (rel >> 1), 1, keepdims=False)
        picked = picked.reshape(-1, columns)
        return picked[:, : columns // 2], picked[:, columns // 2 :]

    one, two = sum_chips(blocks)
    summed = sum_group(jnp.concatenate([one, two], axis=-1))
    pieces, _ = spread_rows(gather_head(summed), None)
    (whole,) = place(me.reshape(1), pieces, [columns])
    whole = whole.reshape(devices, own + EXTRA_ROWS, columns).astype(jnp.float32)
    return (
        whole[:, :own].reshape(devices * own, columns),
        whole[:, own:].reshape(-1, columns)[:count],
    )


def layer_forward(resid, weights, cosine, sine, allowed):
    qkv_full, out_full, up_full, down_full, gain_pair = weights
    gains = gain_pair.astype(jnp.float32)
    rows = resid.shape[0]
    normed_first = norm_apply(resid, gains[0]).astype(jnp.bfloat16)
    projected = jnp.dot(normed_first, qkv_full, preferred_element_type=jnp.float32)
    query_rows = rotate(
        projected[:, :MODEL_WIDTH].reshape(rows, HEADS, HEAD_DIM), cosine, sine
    ).astype(jnp.bfloat16)
    key_rows = rotate(
        projected[:, MODEL_WIDTH : 2 * MODEL_WIDTH].reshape(rows, HEADS, HEAD_DIM), cosine, sine
    ).astype(jnp.bfloat16)
    value_rows = projected[:, 2 * MODEL_WIDTH :].reshape(rows, HEADS, HEAD_DIM).astype(jnp.bfloat16)

    mixed, log_total = attend_forward(query_rows, key_rows, value_rows, allowed)
    mixed_low = mixed.reshape(rows, MODEL_WIDTH).astype(jnp.bfloat16)
    middle = resid + jnp.dot(mixed_low, out_full, preferred_element_type=jnp.float32)
    normed_second = norm_apply(middle, gains[1]).astype(jnp.bfloat16)
    hidden_pre = jnp.dot(normed_second, up_full, preferred_element_type=jnp.float32)
    hidden_act = jax.nn.gelu(hidden_pre, approximate=True).astype(jnp.bfloat16)
    result = middle + jnp.dot(hidden_act, down_full, preferred_element_type=jnp.float32)
    saved = (
        resid,
        normed_first,
        query_rows,
        key_rows,
        value_rows,
        log_total,
        mixed_low,
        middle,
        normed_second,
        hidden_pre,
    )
    return (result, saved)


def layer_backward(saved, weights, cosine, sine, allowed, grad_result):
    (
        resid,
        normed_first,
        query_rows,
        key_rows,
        value_rows,
        log_total,
        mixed_low,
        middle,
        normed_second,
        hidden_pre,
    ) = saved
    qkv_full, out_full, up_full, down_full, gain_pair = weights
    gains = gain_pair.astype(jnp.float32)
    rows = resid.shape[0]
    grad_branch = grad_result.astype(jnp.bfloat16)
    hidden_act, gelu_pull = jax.vjp(partial(jax.nn.gelu, approximate=True), hidden_pre)
    hidden_low = hidden_act.astype(jnp.bfloat16)
    grad_act = reverse_matmul_answer(grad_branch, down_full)
    grad_pre = gelu_pull(grad_act)[0].astype(jnp.bfloat16)
    grad_normed_second = reverse_matmul_answer(grad_pre, up_full)
    unused_second, second_pull = jax.vjp(norm_apply, middle, gains[1])
    grad_middle_norm, grad_gain_second = second_pull(grad_normed_second)
    grad_middle = grad_result + grad_middle_norm
    grad_attn = grad_middle.astype(jnp.bfloat16)
    grad_mixed = (
        reverse_matmul_answer(grad_attn, out_full)
        .astype(jnp.bfloat16)
        .reshape(rows, HEADS, HEAD_DIM)
    )

    grad_query, grad_keys, grad_values = attend_backward(
        query_rows, key_rows, value_rows, allowed, log_total, grad_mixed
    )
    grad_query = unrotate(grad_query, cosine, sine).reshape(rows, MODEL_WIDTH)
    grad_keys = unrotate(grad_keys, cosine, sine).reshape(rows, MODEL_WIDTH)
    grad_values = grad_values.reshape(rows, MODEL_WIDTH)
    grad_projected = jnp.concatenate([grad_query, grad_keys, grad_values], axis=1).astype(
        jnp.bfloat16
    )
    grad_normed_first = reverse_matmul_answer(grad_projected, qkv_full)
    unused_first, first_pull = jax.vjp(norm_apply, resid, gains[0])
    grad_resid_norm, grad_gain_first = first_pull(grad_normed_first)
    grad_resid = grad_middle + grad_resid_norm
    left_rows = (normed_first, mixed_low, normed_second, hidden_low)
    right_rows = (grad_projected, grad_attn, grad_pre, grad_branch)
    return (grad_resid, left_rows, right_rows, (grad_gain_first, grad_gain_second))


def body(
    patch_observations,
    sequence_labels,
    leading_filler_count,
    intake_latent_matrix,
    intake_latent_offset,
    intake_emit_matrix,
    intake_emit_offset,
    intake_shortcut_matrix,
    attention_entry_matrices,
    attention_merge_matrix,
    feedforward_widen_matrix,
    feedforward_shrink_matrix,
    layer_scale_factors,
    readout_latent_matrix,
    readout_latent_offset,
    readout_emit_matrix,
    readout_emit_offset,
    readout_shortcut_matrix,
    loss_sensitivity,
):
    patch_len = patch_observations.shape[1]
    position, pad_count, allowed, keep_rows = layout_rows(
        sequence_labels[0], leading_filler_count[0], patch_len
    )
    cosine, sine = rotary_tables(position, HEAD_DIM)
    columns = jnp.arange(patch_len, dtype=jnp.int32)
    pad_mask = columns[None, :] < pad_count[:, None]
    features = jnp.concatenate(
        [
            jnp.where(pad_mask, jnp.zeros_like(patch_observations), patch_observations),
            pad_mask.astype(jnp.bfloat16),
        ],
        axis=1,
    )
    entry_pre = (
        jnp.dot(features, intake_latent_matrix, preferred_element_type=jnp.float32)
        + intake_latent_offset
    )
    entry_hidden = jax.nn.silu(entry_pre).astype(jnp.bfloat16)
    resid = (
        jnp.dot(entry_hidden, intake_emit_matrix, preferred_element_type=jnp.float32)
        + intake_emit_offset
        + jnp.dot(features, intake_shortcut_matrix, preferred_element_type=jnp.float32)
    )
    layer_count = attention_entry_matrices.shape[0]
    group = lax.axis_size("head")
    group_place = lax.axis_index("head")
    outer = lax.axis_size("dp") // 8
    me = lax.axis_index("dp").astype(jnp.int32)
    places = me.reshape(1)
    own_count = layer_scale_factors.shape[2]
    rows = patch_observations.shape[0]

    group_width = readout_latent_offset.shape[0]
    offsets = jnp.stack([readout_latent_offset, readout_emit_offset])
    coarse = lax.reduce_precision(offsets, 8, 7)
    offset_rows = jnp.concatenate([coarse, offsets - coarse], axis=0).astype(jnp.bfloat16)
    offset_rows = jnp.pad(offset_rows, ((0, 12), (0, 0)))
    sent = jnp.concatenate(
        [
            loss_sensitivity.reshape(group, rows, group_width),
            jnp.broadcast_to(offset_rows[None], (group, 16, group_width)),
        ],
        axis=1,
    )
    met = lax.all_to_all(sent, "head", split_axis=0, concat_axis=0, tiled=True)
    sensitivity = met[:, :rows]
    head_offsets = met[:, rows : rows + 4].astype(jnp.float32)
    latent_offsets = head_offsets[:, 0] + head_offsets[:, 2]
    emit_offsets = head_offsets[:, 1] + head_offsets[:, 3]

    gain_columns = layer_scale_factors.reshape(2 * layer_count, own_count).T
    gain_columns = jnp.pad(gain_columns, ((0, 0), (0, 128 - 2 * layer_count)))
    chunks = []
    for layer_index in range(layer_count):
        entry_own = attention_entry_matrices[layer_index]
        widths = [3 * MODEL_WIDTH]
        if layer_index == 0:
            entry_own = jnp.concatenate([entry_own, gain_columns], axis=1)
            widths.append(128)
        chunks.append((entry_own, widths))
        rest_own = jnp.concatenate(
            [
                attention_merge_matrix[layer_index],
                feedforward_widen_matrix[layer_index],
                feedforward_shrink_matrix[layer_index],
            ],
            axis=1,
        )
        chunks.append((rest_own, [MODEL_WIDTH] * 3))
    held_chunks = []
    for own, widths in chunks:
        if held_chunks:
            own = after(own, held_chunks[-1])
        held_chunks.append(gather_head(own))
    head_own = jnp.concatenate(
        [
            lax.dynamic_index_in_dim(
                matrix.reshape(outer, 8, -1, group_width), me % 8, 1, keepdims=False
            )
            for matrix in (readout_latent_matrix, readout_shortcut_matrix, readout_emit_matrix)
        ],
        axis=2,
    )
    head_held = lax.all_gather(after(head_own, held_chunks[-1]), "head", axis=0, tiled=True)
    gate = None
    whole_chunks = []
    for held, widths in [
        *zip(held_chunks, [widths for _, widths in chunks], strict=True),
        (head_held, [3 * group_width]),
    ]:
        pieces, gate = spread_rows(held, gate)
        whole_chunks.append(place(places, pieces, widths))
    gain_rows = whole_chunks[0][1][0, :, : 2 * layer_count].T.reshape(layer_count, 2, -1)
    layer_weights = [
        (
            whole_chunks[2 * member][0][0],
            *(part[0] for part in whole_chunks[2 * member + 1]),
            gain_rows[member],
        )
        for member in range(layer_count)
    ]
    head_whole = whole_chunks[-1][0]

    saved_states = []
    for layer_index in range(layer_count):
        resid, saved = layer_forward(resid, layer_weights[layer_index], cosine, sine, allowed)
        saved_states.append(saved)

    top = resid.astype(jnp.bfloat16)
    keep_column = keep_rows[:, None]
    two = 2 * group_width
    inner_parts = [
        jnp.dot(top, head_whole[part][:, :two], preferred_element_type=jnp.float32)
        for part in range(group)
    ]
    head_pre = jnp.concatenate(
        [inner_parts[part][:, :group_width] + latent_offsets[part] for part in range(group)],
        axis=1,
    )
    head_hidden = jax.nn.silu(head_pre).astype(jnp.bfloat16)
    forecast = jnp.stack(
        [
            (
                jnp.dot(
                    head_hidden, head_whole[part][:, two:], preferred_element_type=jnp.float32
                )
                + emit_offsets[part]
                + inner_parts[part][:, group_width:]
            )
            * keep_column
            for part in range(group)
        ]
    ).astype(jnp.bfloat16)
    token_predictions = lax.all_to_all(
        forecast, "head", split_axis=0, concat_axis=0, tiled=True
    ).reshape(group * rows, group_width)
    grad_forecast = (sensitivity.astype(jnp.float32) * keep_column).astype(jnp.bfloat16)
    grad_hidden = sum(
        reverse_matmul_answer(grad_forecast[part], head_whole[part][:, two:])
        for part in range(group)
    )
    unused_head, head_pull = jax.vjp(jax.nn.silu, head_pre)
    grad_head_pre = head_pull(grad_hidden)[0].astype(jnp.bfloat16)
    grad_resid = sum(
        reverse_matmul_answer(
            jnp.concatenate(
                [
                    grad_head_pre[:, part * group_width : (part + 1) * group_width],
                    grad_forecast[part],
                ],
                axis=1,
            ),
            head_whole[part][:, :two],
        )
        for part in range(group)
    )
    grad_forecast_rows = jnp.concatenate([grad_forecast[part] for part in range(group)], axis=1)
    head_bias_rows = (
        jnp.sum(grad_head_pre.astype(jnp.float32), axis=0),
        jnp.sum(grad_forecast_rows.astype(jnp.float32), axis=0),
    )
    pair_top = pair_rows(me, top, grad_head_pre)
    pair_hidden = pair_rows(me, head_hidden, grad_forecast_rows)
    head_sums = column_sums(me, [pair_top, (pair_top[0], pair_hidden[1]), pair_hidden])

    layer_sums = [None] * layer_count
    gain_sums = [None] * layer_count
    for layer_index in reversed(range(layer_count)):
        grad_resid, left_rows, right_rows, gain_sums[layer_index] = layer_backward(
            saved_states[layer_index], layer_weights[layer_index], cosine, sine, allowed, grad_resid
        )
        pairs = [
            pair_rows(me, left, right) for left, right in zip(left_rows, right_rows, strict=True)
        ]
        rest = weight_sums(me, pairs[1:])
        layer_sums[layer_index] = (weight_sums(me, pairs[:1])[0], rest[0], rest[1], rest[2])
    grad_entry = grad_resid.astype(jnp.bfloat16)
    grad_entry_outer = dyadic_accumulation(entry_hidden, grad_entry)
    grad_entry_outer_bias = jnp.sum(grad_entry.astype(jnp.float32), axis=0)
    grad_entry_skip = dyadic_accumulation(features, grad_entry)
    unused_entry, entry_pull = jax.vjp(jax.nn.silu, entry_pre)
    grad_entry_pre = entry_pull(reverse_matmul_answer(grad_entry, intake_emit_matrix))[0].astype(
        jnp.bfloat16
    )
    grad_entry_inner = dyadic_accumulation(features, grad_entry_pre)
    grad_entry_inner_bias = jnp.sum(grad_entry_pre.astype(jnp.float32), axis=0)
    grad_features = reverse_matmul_answer(
        grad_entry_pre, intake_latent_matrix
    ) + reverse_matmul_answer(grad_entry, intake_shortcut_matrix)
    values_grad = jnp.where(pad_mask, 0.0, grad_features[:, :patch_len])
    extra_rows = jnp.concatenate(
        [
            grad_entry_inner,
            grad_entry_skip,
            grad_entry_inner_bias[None],
            grad_entry_outer_bias[None],
        ]
        + [row[None] for row in head_bias_rows]
        + [row[None] for pair in gain_sums for row in pair],
        axis=0,
    )
    entry_main, entry_extra = sum_everywhere(me, grad_entry_outer, extra_rows)
    inner_rows = 2 * patch_len
    last = 2 * inner_rows
    entry_sums = (
        entry_extra[:inner_rows],
        entry_extra[last],
        entry_main,
        entry_extra[last + 1],
        entry_extra[inner_rows:last],
    )
    head_bias_sums = lax.dynamic_slice_in_dim(
        entry_extra[last + 2 : last + 4], group_place * group_width, group_width, 1
    )
    own_place = (me * group + group_place) * own_count
    gains_grad = lax.dynamic_slice_in_dim(
        entry_extra[last + 4 : last + 4 + 2 * layer_count], own_place, own_count, 1
    ).reshape(layer_count, 2, own_count)
    qkv_grad = jnp.stack([layer_sums[member][0] for member in range(layer_count)])
    out_grad = jnp.stack([layer_sums[member][1] for member in range(layer_count)])
    up_grad = jnp.stack([layer_sums[member][2] for member in range(layer_count)])
    down_grad = jnp.stack([layer_sums[member][3] for member in range(layer_count)])
    return (
        token_predictions,
        values_grad,
        entry_sums[0],
        entry_sums[1],
        entry_sums[2],
        entry_sums[3],
        entry_sums[4],
        qkv_grad,
        out_grad,
        up_grad,
        down_grad,
        gains_grad,
        head_sums[0],
        head_bias_sums[0],
        head_sums[2],
        head_bias_sums[1],
        head_sums[1],
    )


def solution(mesh):
    return jax.shard_map(
        body,
        mesh=mesh,
        in_specs=(
            P(("dp", "head"), None),
            P(("dp", "head"), None),
            P(("dp", "head"), None),
            P(),
            P(),
            P(),
            P(),
            P(),
            P(None, ("dp", "head"), None),
            P(None, ("dp", "head"), None),
            P(None, ("dp", "head"), None),
            P(None, ("dp", "head"), None),
            P(None, None, ("dp", "head")),
            P(None, "head"),
            P("head"),
            P(None, "head"),
            P("head"),
            P(None, "head"),
            P("dp", "head"),
        ),
        out_specs=(
            P("dp", "head"),
            P(("dp", "head"), None),
            P(),
            P(),
            P(),
            P(),
            P(),
            P(None, ("dp", "head"), None),
            P(None, ("dp", "head"), None),
            P(None, ("dp", "head"), None),
            P(None, ("dp", "head"), None),
            P(None, None, ("dp", "head")),
            P(None, "head"),
            P("head"),
            P(None, "head"),
            P("head"),
            P(None, "head"),
        ),
        check_vma=False,
    )
```

```python
from functools import partial
import math

import jax
import jax.numpy as jnp
from jax import lax
from jax.experimental import pallas as pl
from jax.experimental.pallas import tpu as pltpu
from jax.sharding import PartitionSpec as P

MODEL_WIDTH = 1280
HEADS = 16
HEAD_DIM = 80


EPS = 1e-06
ROPE_BASE = 10000.0


def layout_rows(series_row, pad_row, patch_len):
    count = series_row.shape[0]
    order = jnp.arange(count, dtype=jnp.int32)
    same_series = series_row[:, None] == series_row[None, :]
    earlier = order[None, :] < order[:, None]
    position = jnp.sum(jnp.logical_and(same_series, earlier).astype(jnp.int32), axis=1)
    numbers = jnp.arange(pad_row.shape[0], dtype=jnp.int32)
    series_pad = jnp.sum(
        jnp.where(series_row[:, None] == numbers[None, :], pad_row[None, :], 0), axis=1
    )
    pad_count = jnp.where(position == 0, series_pad, 0)
    padded = pad_count == patch_len
    diagonal = order[:, None] == order[None, :]
    reach = jnp.logical_or(jnp.logical_and(earlier, jnp.logical_not(padded)[None, :]), diagonal)
    allowed = jnp.logical_and(same_series, reach)
    keep_rows = jnp.where(padded, 0.0, 1.0).astype(jnp.float32)
    return (position, pad_count, allowed, keep_rows)


def rotary_tables(position, head_dim):
    half = head_dim // 2
    steps = jnp.arange(half, dtype=jnp.float32) / half
    inverse = jnp.exp(-math.log(ROPE_BASE) * steps)
    angles = position.astype(jnp.float32)[:, None] * inverse[None, :]
    return (jnp.cos(angles)[:, None, :], jnp.sin(angles)[:, None, :])


def rotate(heads_rows, cosine, sine):
    half = heads_rows.shape[-1] // 2
    first = heads_rows[..., :half]
    second = heads_rows[..., half:]
    return jnp.concatenate(
        [first * cosine - second * sine, second * cosine + first * sine], axis=-1
    )


def unrotate(grad_rows, cosine, sine):
    half = grad_rows.shape[-1] // 2
    first = grad_rows[..., :half]
    second = grad_rows[..., half:]
    return jnp.concatenate(
        [first * cosine + second * sine, second * cosine - first * sine], axis=-1
    )


def norm_apply(resid, gain):
    return resid * lax.rsqrt(jnp.mean(resid * resid, axis=-1, keepdims=True) + EPS) * gain


def dyadic_accumulation(left, right):
    return lax.dot_general(
        left, right, (((0,), (0,)), ((), ())), preferred_element_type=jnp.float32
    )


def reverse_matmul_answer(grad_rows, weight):
    return lax.dot_general(
        grad_rows, weight, (((1,), (1,)), ((), ())), preferred_element_type=jnp.float32
    )


def masked_scores(query_rows, key_rows, allowed):
    scale = 1.0 / math.sqrt(query_rows.shape[-1])
    scores = (
        jnp.einsum("qhd,khd->hqk", query_rows, key_rows, preferred_element_type=jnp.float32) * scale
    )
    return jnp.where(allowed[None], scores, -1e30)


def attend_forward(query_rows, key_rows, value_rows, allowed):
    scores = masked_scores(query_rows, key_rows, allowed)
    peak = jnp.max(scores, axis=-1, keepdims=True)
    weights = jnp.exp(scores - peak)
    total = jnp.sum(weights, axis=-1, keepdims=True)
    probs = (weights / total).astype(jnp.bfloat16)
    mixed = jnp.einsum("hqk,khd->qhd", probs, value_rows, preferred_element_type=jnp.float32)
    return (mixed, peak + jnp.log(total))


def attend_backward(query_rows, key_rows, value_rows, allowed, log_total, grad_mixed):
    scale = 1.0 / math.sqrt(query_rows.shape[-1])
    scores = masked_scores(query_rows, key_rows, allowed)
    probs = jnp.where(allowed[None], jnp.exp(scores - log_total), 0.0)
    grad_probs = jnp.einsum(
        "qhd,khd->hqk", grad_mixed, value_rows, preferred_element_type=jnp.float32
    )
    grad_values = jnp.einsum(
        "hqk,qhd->khd", probs.astype(jnp.bfloat16), grad_mixed, preferred_element_type=jnp.float32
    )
    center = jnp.sum(grad_probs * probs, axis=-1, keepdims=True)
    grad_scores = (probs * (grad_probs - center)).astype(jnp.bfloat16)
    grad_query = (
        jnp.einsum("hqk,khd->qhd", grad_scores, key_rows, preferred_element_type=jnp.float32)
        * scale
    )
    grad_keys = (
        jnp.einsum("hqk,qhd->khd", grad_scores, query_rows, preferred_element_type=jnp.float32)
        * scale
    )
    return (grad_query, grad_keys, grad_values)


def after(value, *earlier):
    return lax.optimization_barrier((value, *earlier))[0]


def swap(v, bit):
    size = lax.axis_size("dp")
    return lax.ppermute(v, "dp", [(i, i ^ (1 << bit)) for i in range(size)])


def outer_groups():
    size = lax.axis_size("dp")
    return [[j + 8 * o for o in range(size // 8)] for j in range(8)]


def place_kernel(plan, piece_count, out_count, me_ref, *refs):
    pieces = refs[:piece_count]
    outs = refs[piece_count : piece_count + out_count]
    held = refs[piece_count + out_count : piece_count + 2 * out_count]
    in_sems, out_sems = refs[piece_count + 2 * out_count :]
    inward, outward = [], []
    for n, (piece, rel, row, out, column) in enumerate(plan):
        source = pieces[piece]
        width = held[out].shape[-1]
        if width != source.shape[-1]:
            source = source.at[:, :, pl.ds(column, width)]
        spot = (slice(None), me_ref[0] ^ rel, pl.ds(row, source.shape[1]), slice(None))
        inward.append(pltpu.make_async_copy(source, held[out].at[spot], in_sems.at[n]))
        outward.append(
            pltpu.make_async_copy(held[out].at[spot], outs[out].at[spot], out_sems.at[n])
        )
    for copy in inward:
        copy.start()
    for copy, onward in zip(inward, outward):
        copy.wait()
        onward.start()
    for onward in outward:
        onward.wait()


def place(me, pieces, widths):
    plan = []
    for n, (rel, row, _) in enumerate(pieces):
        column = 0
        for out, width in enumerate(widths):
            plan.append((n, rel, row, out, column))
            column += width
    arrays = [array for _, _, array in pieces]
    lead, rows, _ = arrays[0].shape
    kind = arrays[0].dtype
    total = sum(8 * lead * rows * -(-w // 128) * 128 for w in widths) * 2
    outs = pl.pallas_call(
        partial(place_kernel, plan, len(arrays), len(widths)),
        out_shape=[jax.ShapeDtypeStruct((lead, 8, rows, w), kind) for w in widths],
        in_specs=[pl.BlockSpec(memory_space=pltpu.SMEM)]
        + [pl.BlockSpec(memory_space=pl.ANY)] * len(arrays),
        out_specs=[pl.BlockSpec(memory_space=pl.ANY)] * len(widths),
        scratch_shapes=[pltpu.VMEM((lead, 8, rows, w), kind) for w in widths]
        + [pltpu.SemaphoreType.DMA((len(plan),))] * 2,
        compiler_params=pltpu.CompilerParams(vmem_limit_bytes=total + (4 << 20)),
        cost_estimate=pl.CostEstimate(flops=0, bytes_accessed=2 * total, transcendentals=0),
    )(me, *arrays)
    outer = lax.axis_size("dp") // 8
    return [o.reshape(-1, outer * 8 * rows, o.shape[-1]) for o in outs]


def row_half(rows):
    return rows // 32 * 16 if rows >= 32 else rows // 2


def spread_rows(held, before, beside):
    half = row_half(held.shape[1])
    if before is not None:
        held = after(held, *before)
    from_x = swap(held, 1)
    from_y = swap(held, 2)
    onward_x, onward_y = from_y[:, :half], from_x[:, half:]
    if beside is not None:
        onward_x, onward_y, _ = lax.optimization_barrier((onward_x, onward_y, beside))
    far_top = swap(onward_x, 1)
    far_rest = swap(onward_y, 2)
    pieces = []
    for rel, row, array in (
        (0, 0, held),
        (2, 0, from_x),
        (4, 0, from_y),
        (6, 0, far_top),
        (6, half, far_rest),
    ):
        pieces.append((rel, row, array))
        pieces.append((rel | 1, row, swap(array, 0)))
    return pieces, (from_x, from_y)


def gather_head(own):
    held = lax.all_gather(own, "head", axis=0, tiled=True)[None]
    if lax.axis_size("dp") > 8:
        held = lax.all_gather(
            held, "dp", axis=0, tiled=True, axis_index_groups=outer_groups()
        )
    return held


def pair_rows(me, left, right):
    rows, width = left.shape
    outer = lax.axis_size("dp") // 8
    view = left.reshape(rows, outer, 4, 2, width // (8 * outer))
    core = me & 1
    mine = lax.dynamic_index_in_dim(view, core, 3, keepdims=False)
    other = lax.dynamic_index_in_dim(view, 1 - core, 3, keepdims=False)
    left_pair = jnp.concatenate([mine, swap(other, 0)], axis=0)
    right_pair = jnp.concatenate([right, swap(right, 0)], axis=0)
    return left_pair, right_pair


def low_sum(*parts):
    total = parts[0].astype(jnp.float32)
    for part in parts[1:]:
        total = total + part.astype(jnp.float32)
    return total.astype(jnp.bfloat16)


def sum_chips(blocks):
    far_one, far_two = blocks(6)
    far_one, far_two = swap(far_one, 1), swap(far_two, 2)
    x_one, x_two = blocks(2)
    y_one, y_two = blocks(4)
    x_one, y_two = swap(x_one, 1), swap(y_two, 2)
    y_one = swap(low_sum(y_one, far_one), 2)
    x_two = swap(low_sum(x_two, far_two), 1)
    own_one, own_two = blocks(0)
    totals = (low_sum(own_one, x_one, y_one), low_sum(own_two, y_two, x_two))
    return totals, (far_one, far_two), (y_one, x_two)


def sum_group(total):
    outer = lax.axis_size("dp") // 8
    group = lax.axis_size("head")
    lead = total.shape[:-2]
    rows, columns = total.shape[-2:]
    if outer > 1:
        total = lax.psum_scatter(
            total.reshape(*lead, outer, rows // outer, columns),
            "dp",
            scatter_dimension=len(lead),
            tiled=True,
            axis_index_groups=outer_groups(),
        )
    total = total.reshape(*lead, rows // outer, columns)
    return lax.psum_scatter(total, "head", scatter_dimension=len(lead), tiled=True)


def weight_blocks(me, pairs):
    lefts = jnp.stack([pair[0] for pair in pairs])
    rights = jnp.stack([pair[1] for pair in pairs])
    chip = me >> 1
    half = rights.shape[-1] // 2

    def blocks(rel):
        picked = lax.dynamic_index_in_dim(lefts, chip ^ (rel >> 1), 3, keepdims=False)
        picked = picked.reshape(lefts.shape[0], lefts.shape[1], -1)
        return tuple(
            jnp.einsum(
                "wtr,wtc->wrc", picked, part, preferred_element_type=jnp.float32
            ).astype(jnp.bfloat16)
            for part in (rights[..., :half], rights[..., half:])
        )

    return blocks


def weight_sums(me, pairs):
    (one, two), first, last = sum_chips(weight_blocks(me, pairs))
    total = sum_group(jnp.concatenate([one, two], axis=-1)).astype(jnp.float32)
    return total, first, last


def column_sums(me, pairs):
    group = lax.axis_size("head")
    outer = lax.axis_size("dp") // 8
    totals = []
    parts, first, last = sum_chips(weight_blocks(me, pairs))
    for part in parts:
        count, rows, columns = part.shape
        part = part.reshape(count, rows, group // 2, 2 * columns // group)
        totals.append(jnp.moveaxis(part, 2, 0))
    total = jnp.concatenate(totals, axis=0)
    summed = lax.psum_scatter(total, "head", scatter_dimension=0, tiled=True)[0]
    count, rows, columns = summed.shape
    held = summed.reshape(count * outer, rows // outer, columns)
    pieces, _ = spread_rows(held, None, None)
    (whole,) = place(me.reshape(1), pieces, [columns])
    return whole.astype(jnp.float32), first, last


EXTRA_ROWS = 8


def sum_everywhere(me, main, extra):
    group = lax.axis_size("head")
    outer = lax.axis_size("dp") // 8
    devices = 8 * outer * group
    columns = main.shape[1]
    count = extra.shape[0]
    own = main.shape[0] // devices
    extra = jnp.pad(extra, ((0, EXTRA_ROWS * devices - count), (0, 0)))
    rows = jnp.concatenate(
        [main.reshape(devices, own, columns), extra.reshape(devices, EXTRA_ROWS, columns)], axis=1
    ).astype(jnp.bfloat16)
    view = rows.reshape(outer, 4, 2, group * (own + EXTRA_ROWS), columns)
    core = me & 1
    other = lax.dynamic_index_in_dim(view, 1 - core, 2, keepdims=False)
    pair = low_sum(lax.dynamic_index_in_dim(view, core, 2, keepdims=False), swap(other, 0))
    chip = me >> 1

    def blocks(rel):
        picked = lax.dynamic_index_in_dim(pair, chip ^ (rel >> 1), 1, keepdims=False)
        picked = picked.reshape(-1, columns)
        return picked[:, : columns // 2], picked[:, columns // 2 :]

    (one, two), _, _ = sum_chips(blocks)
    summed = sum_group(jnp.concatenate([one, two], axis=-1))
    pieces, _ = spread_rows(gather_head(summed), None, None)
    (whole,) = place(me.reshape(1), pieces, [columns])
    whole = whole.reshape(devices, own + EXTRA_ROWS, columns).astype(jnp.float32)
    return (
        whole[:, :own].reshape(devices * own, columns),
        whole[:, own:].reshape(-1, columns)[:count],
    )


def layer_forward(resid, weights, cosine, sine, allowed):
    qkv_full, out_full, up_full, down_full, gain_pair = weights
    gains = gain_pair.astype(jnp.float32)
    rows = resid.shape[0]
    normed_first = norm_apply(resid, gains[0]).astype(jnp.bfloat16)
    projected = jnp.dot(normed_first, qkv_full, preferred_element_type=jnp.float32)
    query_rows = rotate(
        projected[:, :MODEL_WIDTH].reshape(rows, HEADS, HEAD_DIM), cosine, sine
    ).astype(jnp.bfloat16)
    key_rows = rotate(
        projected[:, MODEL_WIDTH : 2 * MODEL_WIDTH].reshape(rows, HEADS, HEAD_DIM), cosine, sine
    ).astype(jnp.bfloat16)
    value_rows = projected[:, 2 * MODEL_WIDTH :].reshape(rows, HEADS, HEAD_DIM).astype(jnp.bfloat16)

    mixed, log_total = attend_forward(query_rows, key_rows, value_rows, allowed)
    mixed_low = mixed.reshape(rows, MODEL_WIDTH).astype(jnp.bfloat16)
    middle = resid + jnp.dot(mixed_low, out_full, preferred_element_type=jnp.float32)
    normed_second = norm_apply(middle, gains[1]).astype(jnp.bfloat16)
    hidden_pre = jnp.dot(normed_second, up_full, preferred_element_type=jnp.float32)
    hidden_act = jax.nn.gelu(hidden_pre, approximate=True).astype(jnp.bfloat16)
    result = middle + jnp.dot(hidden_act, down_full, preferred_element_type=jnp.float32)
    saved = (
        resid,
        normed_first,
        query_rows,
        key_rows,
        value_rows,
        log_total,
        mixed_low,
        middle,
        normed_second,
        hidden_pre,
    )
    return (result, saved)


def rest_backward(saved, weights, grad_result):
    mixed_low, middle, normed_second, hidden_pre = saved[6:]
    _, out_full, up_full, down_full, gain_pair = weights
    gains = gain_pair.astype(jnp.float32)
    grad_branch = grad_result.astype(jnp.bfloat16)
    hidden_act, gelu_pull = jax.vjp(partial(jax.nn.gelu, approximate=True), hidden_pre)
    hidden_low = hidden_act.astype(jnp.bfloat16)
    grad_act = reverse_matmul_answer(grad_branch, down_full)
    grad_pre = gelu_pull(grad_act)[0].astype(jnp.bfloat16)
    grad_normed_second = reverse_matmul_answer(grad_pre, up_full)
    unused_second, second_pull = jax.vjp(norm_apply, middle, gains[1])
    grad_middle_norm, grad_gain_second = second_pull(grad_normed_second)
    grad_middle = grad_result + grad_middle_norm
    grad_attn = grad_middle.astype(jnp.bfloat16)
    grad_mixed = reverse_matmul_answer(grad_attn, out_full).astype(jnp.bfloat16)
    left_rows = (mixed_low, normed_second, hidden_low)
    right_rows = (grad_attn, grad_pre, grad_branch)
    return (grad_middle, grad_mixed, left_rows, right_rows, grad_gain_second)


def entry_backward(saved, weights, cosine, sine, allowed, grad_middle, grad_mixed):
    resid, normed_first, query_rows, key_rows, value_rows, log_total = saved[:6]
    qkv_full = weights[0]
    gains = weights[4].astype(jnp.float32)
    rows = resid.shape[0]
    grad_query, grad_keys, grad_values = attend_backward(
        query_rows,
        key_rows,
        value_rows,
        allowed,
        log_total,
        grad_mixed.reshape(rows, HEADS, HEAD_DIM),
    )
    grad_query = unrotate(grad_query, cosine, sine).reshape(rows, MODEL_WIDTH)
    grad_keys = unrotate(grad_keys, cosine, sine).reshape(rows, MODEL_WIDTH)
    grad_values = grad_values.reshape(rows, MODEL_WIDTH)
    grad_projected = jnp.concatenate([grad_query, grad_keys, grad_values], axis=1).astype(
        jnp.bfloat16
    )
    grad_normed_first = reverse_matmul_answer(grad_projected, qkv_full)
    unused_first, first_pull = jax.vjp(norm_apply, resid, gains[0])
    grad_resid_norm, grad_gain_first = first_pull(grad_normed_first)
    return (grad_middle + grad_resid_norm, normed_first, grad_projected, grad_gain_first)


def body(
    patch_observations,
    sequence_labels,
    leading_filler_count,
    intake_latent_matrix,
    intake_latent_offset,
    intake_emit_matrix,
    intake_emit_offset,
    intake_shortcut_matrix,
    attention_entry_matrices,
    attention_merge_matrix,
    feedforward_widen_matrix,
    feedforward_shrink_matrix,
    layer_scale_factors,
    readout_latent_matrix,
    readout_latent_offset,
    readout_emit_matrix,
    readout_emit_offset,
    readout_shortcut_matrix,
    loss_sensitivity,
):
    patch_len = patch_observations.shape[1]
    position, pad_count, allowed, keep_rows = layout_rows(
        sequence_labels[0], leading_filler_count[0], patch_len
    )
    cosine, sine = rotary_tables(position, HEAD_DIM)
    columns = jnp.arange(patch_len, dtype=jnp.int32)
    pad_mask = columns[None, :] < pad_count[:, None]
    features = jnp.concatenate(
        [
            jnp.where(pad_mask, jnp.zeros_like(patch_observations), patch_observations),
            pad_mask.astype(jnp.bfloat16),
        ],
        axis=1,
    )
    entry_pre = (
        jnp.dot(features, intake_latent_matrix, preferred_element_type=jnp.float32)
        + intake_latent_offset
    )
    entry_hidden = jax.nn.silu(entry_pre).astype(jnp.bfloat16)
    resid = (
        jnp.dot(entry_hidden, intake_emit_matrix, preferred_element_type=jnp.float32)
        + intake_emit_offset
        + jnp.dot(features, intake_shortcut_matrix, preferred_element_type=jnp.float32)
    )
    layer_count = attention_entry_matrices.shape[0]
    group = lax.axis_size("head")
    group_place = lax.axis_index("head")
    outer = lax.axis_size("dp") // 8
    me = lax.axis_index("dp").astype(jnp.int32)
    places = me.reshape(1)
    own_count = layer_scale_factors.shape[2]
    rows = patch_observations.shape[0]

    group_width = readout_latent_offset.shape[0]
    offsets = jnp.stack([readout_latent_offset, readout_emit_offset])
    coarse = lax.reduce_precision(offsets, 8, 7)
    offset_rows = jnp.concatenate([coarse, offsets - coarse], axis=0).astype(jnp.bfloat16)
    offset_rows = jnp.pad(offset_rows, ((0, 12), (0, 0)))
    sent = jnp.concatenate(
        [
            loss_sensitivity.reshape(group, rows, group_width),
            jnp.broadcast_to(offset_rows[None], (group, 16, group_width)),
        ],
        axis=1,
    )
    met = lax.all_to_all(sent, "head", split_axis=0, concat_axis=0, tiled=True)
    sensitivity = met[:, :rows]
    head_offsets = met[:, rows : rows + 4].astype(jnp.float32)
    latent_offsets = head_offsets[:, 0] + head_offsets[:, 2]
    emit_offsets = head_offsets[:, 1] + head_offsets[:, 3]

    gain_columns = layer_scale_factors.reshape(2 * layer_count, own_count).T
    gain_columns = jnp.pad(gain_columns, ((0, 0), (0, 128 - 2 * layer_count)))
    chunks = []
    for layer_index in range(layer_count):
        entry_own = attention_entry_matrices[layer_index]
        widths = [3 * MODEL_WIDTH]
        if layer_index == 0:
            entry_own = jnp.concatenate([entry_own, gain_columns], axis=1)
            widths.append(128)
        chunks.append((entry_own, widths))
        rest_own = jnp.concatenate(
            [
                attention_merge_matrix[layer_index],
                feedforward_widen_matrix[layer_index],
                feedforward_shrink_matrix[layer_index],
            ],
            axis=1,
        )
        chunks.append((rest_own, [MODEL_WIDTH] * 3))
    held_chunks = []
    for own, widths in chunks:
        if held_chunks:
            own = after(own, held_chunks[-1])
        held_chunks.append(gather_head(own))
    head_own = jnp.concatenate(
        [
            lax.dynamic_index_in_dim(
                matrix.reshape(outer, 8, -1, group_width), me % 8, 1, keepdims=False
            )
            for matrix in (readout_latent_matrix, readout_shortcut_matrix, readout_emit_matrix)
        ],
        axis=2,
    )
    head_held = lax.all_gather(after(head_own, held_chunks[-1]), "head", axis=0, tiled=True)
    held_chunks.append(head_held)
    chunk_widths = [widths for _, widths in chunks] + [[3 * group_width]]
    before = None
    whole_chunks = []
    for held, beside, widths in zip(
        held_chunks, [*held_chunks[1:], None], chunk_widths, strict=True
    ):
        pieces, before = spread_rows(held, before, beside)
        whole_chunks.append(place(places, pieces, widths))
    gain_rows = whole_chunks[0][1][0, :, : 2 * layer_count].T.reshape(layer_count, 2, -1)
    layer_weights = [
        (
            whole_chunks[2 * member][0][0],
            *(part[0] for part in whole_chunks[2 * member + 1]),
            gain_rows[member],
        )
        for member in range(layer_count)
    ]
    head_whole = whole_chunks[-1][0]

    saved_states = []
    for layer_index in range(layer_count):
        resid, saved = layer_forward(resid, layer_weights[layer_index], cosine, sine, allowed)
        saved_states.append(saved)

    top = resid.astype(jnp.bfloat16)
    keep_column = keep_rows[:, None]
    two = 2 * group_width
    inner_parts = [
        jnp.dot(top, head_whole[part][:, :two], preferred_element_type=jnp.float32)
        for part in range(group)
    ]
    head_pre = jnp.concatenate(
        [inner_parts[part][:, :group_width] + latent_offsets[part] for part in range(group)],
        axis=1,
    )
    head_hidden = jax.nn.silu(head_pre).astype(jnp.bfloat16)
    forecast = jnp.stack(
        [
            (
                jnp.dot(
                    head_hidden, head_whole[part][:, two:], preferred_element_type=jnp.float32
                )
                + emit_offsets[part]
                + inner_parts[part][:, group_width:]
            )
            * keep_column
            for part in range(group)
        ]
    ).astype(jnp.bfloat16)
    token_predictions = lax.all_to_all(
        forecast, "head", split_axis=0, concat_axis=0, tiled=True
    ).reshape(group * rows, group_width)
    grad_forecast = (sensitivity.astype(jnp.float32) * keep_column).astype(jnp.bfloat16)
    grad_hidden = sum(
        reverse_matmul_answer(grad_forecast[part], head_whole[part][:, two:])
        for part in range(group)
    )
    unused_head, head_pull = jax.vjp(jax.nn.silu, head_pre)
    grad_head_pre = head_pull(grad_hidden)[0].astype(jnp.bfloat16)
    grad_resid = sum(
        reverse_matmul_answer(
            jnp.concatenate(
                [
                    grad_head_pre[:, part * group_width : (part + 1) * group_width],
                    grad_forecast[part],
                ],
                axis=1,
            ),
            head_whole[part][:, :two],
        )
        for part in range(group)
    )
    grad_forecast_rows = jnp.concatenate([grad_forecast[part] for part in range(group)], axis=1)
    head_bias_rows = (
        jnp.sum(grad_head_pre.astype(jnp.float32), axis=0),
        jnp.sum(grad_forecast_rows.astype(jnp.float32), axis=0),
    )
    pair_top = pair_rows(me, top, grad_head_pre)
    pair_hidden = pair_rows(me, head_hidden, grad_forecast_rows)
    head_sums, first, last = column_sums(
        me, [pair_top, (pair_top[0], pair_hidden[1]), pair_hidden]
    )

    ahead = [(), first]
    lasts = [last]
    layer_sums = [None] * layer_count
    gain_sums = [None] * layer_count
    for layer_index in reversed(range(layer_count)):
        saved, weights = saved_states[layer_index], layer_weights[layer_index]
        grad_resid = after(grad_resid, *ahead[-2])
        grad_middle, grad_mixed, left_rows, right_rows, gain_second = rest_backward(
            saved, weights, grad_resid
        )
        pairs = [
            pair_rows(me, left, right) for left, right in zip(left_rows, right_rows, strict=True)
        ]
        rest, first, last = weight_sums(me, pairs)
        ahead.append((*lasts[-1], *first))
        lasts.append(last)
        grad_mixed = after(grad_mixed, *ahead[-2])
        grad_resid, left, right, gain_first = entry_backward(
            saved, weights, cosine, sine, allowed, grad_middle, grad_mixed
        )
        entry, first, last = weight_sums(me, [pair_rows(me, left, right)])
        ahead.append((*lasts[-1], *first))
        lasts.append(last)
        layer_sums[layer_index] = (entry[0], rest[0], rest[1], rest[2])
        gain_sums[layer_index] = (gain_first, gain_second)
    grad_resid = after(grad_resid, *ahead[-2])
    grad_entry = grad_resid.astype(jnp.bfloat16)
    grad_entry_outer = dyadic_accumulation(entry_hidden, grad_entry)
    grad_entry_outer_bias = jnp.sum(grad_entry.astype(jnp.float32), axis=0)
    grad_entry_skip = dyadic_accumulation(features, grad_entry)
    unused_entry, entry_pull = jax.vjp(jax.nn.silu, entry_pre)
    grad_entry_pre = entry_pull(reverse_matmul_answer(grad_entry, intake_emit_matrix))[0].astype(
        jnp.bfloat16
    )
    grad_entry_inner = dyadic_accumulation(features, grad_entry_pre)
    grad_entry_inner_bias = jnp.sum(grad_entry_pre.astype(jnp.float32), axis=0)
    grad_features = reverse_matmul_answer(
        grad_entry_pre, intake_latent_matrix
    ) + reverse_matmul_answer(grad_entry, intake_shortcut_matrix)
    values_grad = jnp.where(pad_mask, 0.0, grad_features[:, :patch_len])
    extra_rows = jnp.concatenate(
        [
            grad_entry_inner,
            grad_entry_skip,
            grad_entry_inner_bias[None],
            grad_entry_outer_bias[None],
        ]
        + [row[None] for row in head_bias_rows]
        + [row[None] for pair in gain_sums for row in pair],
        axis=0,
    )
    entry_main, entry_extra = sum_everywhere(me, grad_entry_outer, extra_rows)
    inner_rows = 2 * patch_len
    last = 2 * inner_rows
    entry_sums = (
        entry_extra[:inner_rows],
        entry_extra[last],
        entry_main,
        entry_extra[last + 1],
        entry_extra[inner_rows:last],
    )
    head_bias_sums = lax.dynamic_slice_in_dim(
        entry_extra[last + 2 : last + 4], group_place * group_width, group_width, 1
    )
    own_place = (me * group + group_place) * own_count
    gains_grad = lax.dynamic_slice_in_dim(
        entry_extra[last + 4 : last + 4 + 2 * layer_count], own_place, own_count, 1
    ).reshape(layer_count, 2, own_count)
    qkv_grad = jnp.stack([layer_sums[member][0] for member in range(layer_count)])
    out_grad = jnp.stack([layer_sums[member][1] for member in range(layer_count)])
    up_grad = jnp.stack([layer_sums[member][2] for member in range(layer_count)])
    down_grad = jnp.stack([layer_sums[member][3] for member in range(layer_count)])
    return (
        token_predictions,
        values_grad,
        entry_sums[0],
        entry_sums[1],
        entry_sums[2],
        entry_sums[3],
        entry_sums[4],
        qkv_grad,
        out_grad,
        up_grad,
        down_grad,
        gains_grad,
        head_sums[0],
        head_bias_sums[0],
        head_sums[2],
        head_bias_sums[1],
        head_sums[1],
    )


def solution(mesh):
    return jax.shard_map(
        body,
        mesh=mesh,
        in_specs=(
            P(("dp", "head"), None),
            P(("dp", "head"), None),
            P(("dp", "head"), None),
            P(),
            P(),
            P(),
            P(),
            P(),
            P(None, ("dp", "head"), None),
            P(None, ("dp", "head"), None),
            P(None, ("dp", "head"), None),
            P(None, ("dp", "head"), None),
            P(None, None, ("dp", "head")),
            P(None, "head"),
            P("head"),
            P(None, "head"),
            P("head"),
            P(None, "head"),
            P("dp", "head"),
        ),
        out_specs=(
            P("dp", "head"),
            P(("dp", "head"), None),
            P(),
            P(),
            P(),
            P(),
            P(),
            P(None, ("dp", "head"), None),
            P(None, ("dp", "head"), None),
            P(None, ("dp", "head"), None),
            P(None, ("dp", "head"), None),
            P(None, None, ("dp", "head")),
            P(None, "head"),
            P("head"),
            P(None, "head"),
            P("head"),
            P(None, "head"),
        ),
        check_vma=False,
    )
```

```python
from functools import partial
import math

import jax
import jax.numpy as jnp
from jax import lax
from jax.experimental import pallas as pl
from jax.experimental.pallas import tpu as pltpu
from jax.sharding import PartitionSpec as P

MODEL_WIDTH = 1280
HEADS = 16
HEAD_DIM = 80


EPS = 1e-06
ROPE_BASE = 10000.0


def layout_rows(series_row, pad_row, patch_len):
    count = series_row.shape[0]
    order = jnp.arange(count, dtype=jnp.int32)
    same_series = series_row[:, None] == series_row[None, :]
    earlier = order[None, :] < order[:, None]
    position = jnp.sum(jnp.logical_and(same_series, earlier).astype(jnp.int32), axis=1)
    numbers = jnp.arange(pad_row.shape[0], dtype=jnp.int32)
    series_pad = jnp.sum(
        jnp.where(series_row[:, None] == numbers[None, :], pad_row[None, :], 0), axis=1
    )
    pad_count = jnp.where(position == 0, series_pad, 0)
    padded = pad_count == patch_len
    diagonal = order[:, None] == order[None, :]
    reach = jnp.logical_or(jnp.logical_and(earlier, jnp.logical_not(padded)[None, :]), diagonal)
    allowed = jnp.logical_and(same_series, reach)
    keep_rows = jnp.where(padded, 0.0, 1.0).astype(jnp.float32)
    return (position, pad_count, allowed, keep_rows)


def rotary_tables(position, head_dim):
    half = head_dim // 2
    steps = jnp.arange(half, dtype=jnp.float32) / half
    inverse = jnp.exp(-math.log(ROPE_BASE) * steps)
    angles = position.astype(jnp.float32)[:, None] * inverse[None, :]
    return (jnp.cos(angles)[:, None, :], jnp.sin(angles)[:, None, :])


def rotate(heads_rows, cosine, sine):
    half = heads_rows.shape[-1] // 2
    first = heads_rows[..., :half]
    second = heads_rows[..., half:]
    return jnp.concatenate(
        [first * cosine - second * sine, second * cosine + first * sine], axis=-1
    )


def unrotate(grad_rows, cosine, sine):
    half = grad_rows.shape[-1] // 2
    first = grad_rows[..., :half]
    second = grad_rows[..., half:]
    return jnp.concatenate(
        [first * cosine + second * sine, second * cosine - first * sine], axis=-1
    )


def norm_apply(resid, gain):
    return resid * lax.rsqrt(jnp.mean(resid * resid, axis=-1, keepdims=True) + EPS) * gain


def dyadic_accumulation(left, right):
    return lax.dot_general(
        left, right, (((0,), (0,)), ((), ())), preferred_element_type=jnp.float32
    )


def reverse_matmul_answer(grad_rows, weight):
    return lax.dot_general(
        grad_rows, weight, (((1,), (1,)), ((), ())), preferred_element_type=jnp.float32
    )


def masked_scores(query_rows, key_rows, allowed):
    scale = 1.0 / math.sqrt(query_rows.shape[-1])
    scores = (
        jnp.einsum("qhd,khd->hqk", query_rows, key_rows, preferred_element_type=jnp.float32) * scale
    )
    return jnp.where(allowed[None], scores, -1e30)


def attend_forward(query_rows, key_rows, value_rows, allowed):
    scores = masked_scores(query_rows, key_rows, allowed)
    peak = jnp.max(scores, axis=-1, keepdims=True)
    weights = jnp.exp(scores - peak)
    total = jnp.sum(weights, axis=-1, keepdims=True)
    probs = (weights / total).astype(jnp.bfloat16)
    mixed = jnp.einsum("hqk,khd->qhd", probs, value_rows, preferred_element_type=jnp.float32)
    return (mixed, peak + jnp.log(total))


def attend_backward(query_rows, key_rows, value_rows, allowed, log_total, grad_mixed):
    scale = 1.0 / math.sqrt(query_rows.shape[-1])
    scores = masked_scores(query_rows, key_rows, allowed)
    probs = jnp.where(allowed[None], jnp.exp(scores - log_total), 0.0)
    grad_probs = jnp.einsum(
        "qhd,khd->hqk", grad_mixed, value_rows, preferred_element_type=jnp.float32
    )
    grad_values = jnp.einsum(
        "hqk,qhd->khd", probs.astype(jnp.bfloat16), grad_mixed, preferred_element_type=jnp.float32
    )
    center = jnp.sum(grad_probs * probs, axis=-1, keepdims=True)
    grad_scores = (probs * (grad_probs - center)).astype(jnp.bfloat16)
    grad_query = (
        jnp.einsum("hqk,khd->qhd", grad_scores, key_rows, preferred_element_type=jnp.float32)
        * scale
    )
    grad_keys = (
        jnp.einsum("hqk,qhd->khd", grad_scores, query_rows, preferred_element_type=jnp.float32)
        * scale
    )
    return (grad_query, grad_keys, grad_values)


def after(value, *earlier):
    return lax.optimization_barrier((value, *earlier))[0]


def swap(v, bit):
    size = lax.axis_size("dp")
    return lax.ppermute(v, "dp", [(i, i ^ (1 << bit)) for i in range(size)])


def outer_groups():
    size = lax.axis_size("dp")
    return [[j + 8 * o for o in range(size // 8)] for j in range(8)]


def place_kernel(plan, piece_count, out_count, me_ref, *refs):
    pieces = refs[:piece_count]
    outs = refs[piece_count : piece_count + out_count]
    held = refs[piece_count + out_count : piece_count + 2 * out_count]
    in_sems, out_sems = refs[piece_count + 2 * out_count :]
    inward, outward = [], []
    for n, (piece, rel, row, out, column) in enumerate(plan):
        source = pieces[piece]
        width = held[out].shape[-1]
        if width != source.shape[-1]:
            source = source.at[:, :, pl.ds(column, width)]
        spot = (slice(None), me_ref[0] ^ rel, pl.ds(row, source.shape[1]), slice(None))
        inward.append(pltpu.make_async_copy(source, held[out].at[spot], in_sems.at[n]))
        outward.append(
            pltpu.make_async_copy(held[out].at[spot], outs[out].at[spot], out_sems.at[n])
        )
    for copy in inward:
        copy.start()
    for copy, onward in zip(inward, outward):
        copy.wait()
        onward.start()
    for onward in outward:
        onward.wait()


def place(me, pieces, widths):
    plan = []
    for n, (rel, row, _) in enumerate(pieces):
        column = 0
        for out, width in enumerate(widths):
            plan.append((n, rel, row, out, column))
            column += width
    arrays = [array for _, _, array in pieces]
    lead, rows, _ = arrays[0].shape
    kind = arrays[0].dtype
    total = sum(8 * lead * rows * -(-w // 128) * 128 for w in widths) * 2
    outs = pl.pallas_call(
        partial(place_kernel, plan, len(arrays), len(widths)),
        out_shape=[jax.ShapeDtypeStruct((lead, 8, rows, w), kind) for w in widths],
        in_specs=[pl.BlockSpec(memory_space=pltpu.SMEM)]
        + [pl.BlockSpec(memory_space=pl.ANY)] * len(arrays),
        out_specs=[pl.BlockSpec(memory_space=pl.ANY)] * len(widths),
        scratch_shapes=[pltpu.VMEM((lead, 8, rows, w), kind) for w in widths]
        + [pltpu.SemaphoreType.DMA((len(plan),))] * 2,
        compiler_params=pltpu.CompilerParams(vmem_limit_bytes=total + (4 << 20)),
        cost_estimate=pl.CostEstimate(flops=0, bytes_accessed=2 * total, transcendentals=0),
    )(me, *arrays)
    outer = lax.axis_size("dp") // 8
    return [o.reshape(-1, outer * 8 * rows, o.shape[-1]) for o in outs]


def row_half(rows):
    return rows // 32 * 16 if rows >= 32 else rows // 2


def second_step(held, from_x, from_y):
    half = row_half(held.shape[1])
    return from_y[:, :half], from_x[:, half:]


def all_pieces(held, from_x, from_y, far_top, far_rest):
    half = far_top.shape[1]
    pieces = []
    for rel, row, array in (
        (0, 0, held),
        (2, 0, from_x),
        (4, 0, from_y),
        (6, 0, far_top),
        (6, half, far_rest),
    ):
        pieces.append((rel, row, array))
        pieces.append((rel | 1, row, swap(array, 0)))
    return pieces


def spread_rows(held):
    from_x, from_y = swap(held, 1), swap(held, 2)
    onward_x, onward_y = second_step(held, from_x, from_y)
    return all_pieces(held, from_x, from_y, swap(onward_x, 1), swap(onward_y, 2))


def gather_head(own):
    held = lax.all_gather(own, "head", axis=0, tiled=True)[None]
    if lax.axis_size("dp") > 8:
        held = lax.all_gather(
            held, "dp", axis=0, tiled=True, axis_index_groups=outer_groups()
        )
    return held


def product_kernel(count, me_ref, *refs):
    lefts, rights, met_lefts, met_rights = (refs[n * count : (n + 1) * count] for n in range(4))
    to_x, to_y, later, own = refs[4 * count :]
    core = me_ref[0] & 1
    chip = me_ref[0] >> 1
    width = own.shape[-1]
    half = width // 2
    for n in range(count):
        for rel in range(4):
            place = chip ^ rel
            near = lefts[n][place * 2 + core]
            met = met_lefts[n][place]
            for part in range(2):
                columns = slice(part * half, (part + 1) * half)
                total = dyadic_accumulation(near, rights[n][:, columns])
                total += dyadic_accumulation(met, met_rights[n][:, columns])
                total = total.astype(own.dtype)
                if rel == 0:
                    own[n, :, columns] = total
                elif rel == 1 and part == 0:
                    to_x[1, n] = total
                elif rel == 1:
                    later[1, n] = total
                elif rel == 2 and part == 0:
                    later[0, n] = total
                elif rel == 2:
                    to_y[1, n] = total
                elif part == 0:
                    to_x[0, n] = total
                else:
                    to_y[0, n] = total


def pair_products(me, pairs):
    outer = lax.axis_size("dp") // 8
    core = me & 1
    lefts, rights, met_lefts, met_rights = [], [], [], []
    known = {}
    for left, right in pairs:
        if id(left) not in known:
            rows, width = left.shape
            blocks = left.reshape(rows, outer, 8, width // (8 * outer))
            blocks = jnp.moveaxis(blocks, 2, 0).reshape(8, rows, width // 8)
            other = lax.dynamic_index_in_dim(
                blocks.reshape(4, 2, rows, width // 8), 1 - core, 1, keepdims=False
            )
            known[id(left)] = (blocks, swap(other, 0))
        if id(right) not in known:
            known[id(right)] = (right, swap(right, 0))
        lefts.append(known[id(left)][0])
        met_lefts.append(known[id(left)][1])
        rights.append(known[id(right)][0])
        met_rights.append(known[id(right)][1])
    count = len(pairs)
    block, width = lefts[0].shape[2], rights[0].shape[1]
    low = jnp.bfloat16
    return pl.pallas_call(
        partial(product_kernel, count),
        out_shape=[
            jax.ShapeDtypeStruct((2, count, block, width // 2), low),
            jax.ShapeDtypeStruct((2, count, block, width // 2), low),
            jax.ShapeDtypeStruct((2, count, block, width // 2), low),
            jax.ShapeDtypeStruct((count, block, width), low),
        ],
        in_specs=[pl.BlockSpec(memory_space=pltpu.SMEM)]
        + [pl.BlockSpec(memory_space=pltpu.VMEM)] * (4 * count),
        out_specs=[pl.BlockSpec(memory_space=pltpu.VMEM)] * 4,
        compiler_params=pltpu.CompilerParams(vmem_limit_bytes=40 << 20),
        cost_estimate=pl.CostEstimate(
            flops=2 * 256 * 4 * block * width * count,
            bytes_accessed=2 * count * (4 * block * width + 256 * width + 256 * 4 * block),
            transcendentals=0,
        ),
    )(me.reshape(1), *lefts, *rights, *met_lefts, *met_rights)


def low_sum(*parts):
    total = parts[0].astype(jnp.float32)
    for part in parts[1:]:
        total = total + part.astype(jnp.float32)
    return total.astype(jnp.bfloat16)


def sum_chips(to_x, to_y, later, own):
    to_x, to_y = swap(to_x, 1), swap(to_y, 2)
    last_y = swap(low_sum(later[0], to_x[0]), 2)
    last_x = swap(low_sum(later[1], to_y[0]), 1)
    half = own.shape[-1] // 2
    total = jnp.concatenate(
        [
            low_sum(own[..., :half], to_x[1], last_y),
            low_sum(own[..., half:], to_y[1], last_x),
        ],
        axis=-1,
    )
    return total, (to_x, to_y), (last_y, last_x)


def sum_group(total):
    outer = lax.axis_size("dp") // 8
    group = lax.axis_size("head")
    lead = total.shape[:-2]
    rows, columns = total.shape[-2:]
    if outer > 1:
        total = lax.psum_scatter(
            total.reshape(*lead, outer, rows // outer, columns),
            "dp",
            scatter_dimension=len(lead),
            tiled=True,
            axis_index_groups=outer_groups(),
        )
    total = total.reshape(*lead, rows // outer, columns)
    return lax.psum_scatter(total, "head", scatter_dimension=len(lead), tiled=True)


def weight_sums(me, pairs):
    total, first, last = sum_chips(*pair_products(me, pairs))
    return sum_group(total).astype(jnp.float32), first, last


def column_sums(me, pairs):
    group = lax.axis_size("head")
    outer = lax.axis_size("dp") // 8
    total, first, last = sum_chips(*pair_products(me, pairs))
    count, rows, columns = total.shape
    total = jnp.moveaxis(total.reshape(count, rows, group, columns // group), 2, 0)
    summed = lax.psum_scatter(total, "head", scatter_dimension=0, tiled=True)[0]
    held = summed.reshape(count * outer, rows // outer, columns // group)
    (whole,) = place(me.reshape(1), spread_rows(held), [columns // group])
    return whole.astype(jnp.float32), first, last


EXTRA_ROWS = 8


def sum_everywhere(me, main, extra):
    group = lax.axis_size("head")
    outer = lax.axis_size("dp") // 8
    devices = 8 * outer * group
    columns = main.shape[1]
    count = extra.shape[0]
    own = main.shape[0] // devices
    extra = jnp.pad(extra, ((0, EXTRA_ROWS * devices - count), (0, 0)))
    rows = jnp.concatenate(
        [main.reshape(devices, own, columns), extra.reshape(devices, EXTRA_ROWS, columns)], axis=1
    ).astype(jnp.bfloat16)
    view = rows.reshape(outer, 4, 2, group * (own + EXTRA_ROWS), columns)
    core = me & 1
    other = lax.dynamic_index_in_dim(view, 1 - core, 2, keepdims=False)
    pair = low_sum(lax.dynamic_index_in_dim(view, core, 2, keepdims=False), swap(other, 0))
    chip = me >> 1
    half = columns // 2

    def picked(rel):
        return lax.dynamic_index_in_dim(pair, chip ^ rel, 1, keepdims=False).reshape(-1, columns)

    own_rows, at_x, at_y, far = (picked(rel) for rel in range(4))
    total, _, _ = sum_chips(
        jnp.stack([far[:, :half], at_x[:, :half]]),
        jnp.stack([far[:, half:], at_y[:, half:]]),
        (at_y[:, :half], at_x[:, half:]),
        own_rows,
    )
    pieces = spread_rows(gather_head(sum_group(total)))
    (whole,) = place(me.reshape(1), pieces, [columns])
    whole = whole.reshape(devices, own + EXTRA_ROWS, columns).astype(jnp.float32)
    return (
        whole[:, :own].reshape(devices * own, columns),
        whole[:, own:].reshape(-1, columns)[:count],
    )


def entry_forward(resid, qkv_full, gain_pair, cosine, sine, allowed):
    gains = gain_pair.astype(jnp.float32)
    rows = resid.shape[0]
    normed_first = norm_apply(resid, gains[0]).astype(jnp.bfloat16)
    projected = jnp.dot(normed_first, qkv_full, preferred_element_type=jnp.float32)
    query_rows = rotate(
        projected[:, :MODEL_WIDTH].reshape(rows, HEADS, HEAD_DIM), cosine, sine
    ).astype(jnp.bfloat16)
    key_rows = rotate(
        projected[:, MODEL_WIDTH : 2 * MODEL_WIDTH].reshape(rows, HEADS, HEAD_DIM), cosine, sine
    ).astype(jnp.bfloat16)
    value_rows = projected[:, 2 * MODEL_WIDTH :].reshape(rows, HEADS, HEAD_DIM).astype(jnp.bfloat16)

    mixed, log_total = attend_forward(query_rows, key_rows, value_rows, allowed)
    mixed_low = mixed.reshape(rows, MODEL_WIDTH).astype(jnp.bfloat16)
    return (resid, normed_first, query_rows, key_rows, value_rows, log_total, mixed_low)


def rest_forward(saved, out_full, up_full, down_full, gain_pair):
    gains = gain_pair.astype(jnp.float32)
    resid, mixed_low = saved[0], saved[6]
    middle = resid + jnp.dot(mixed_low, out_full, preferred_element_type=jnp.float32)
    normed_second = norm_apply(middle, gains[1]).astype(jnp.bfloat16)
    hidden_pre = jnp.dot(normed_second, up_full, preferred_element_type=jnp.float32)
    hidden_act = jax.nn.gelu(hidden_pre, approximate=True).astype(jnp.bfloat16)
    result = middle + jnp.dot(hidden_act, down_full, preferred_element_type=jnp.float32)
    return (result, (*saved, middle, normed_second, hidden_pre))


def rest_backward(saved, weights, grad_result):
    mixed_low, middle, normed_second, hidden_pre = saved[6:]
    _, out_full, up_full, down_full, gain_pair = weights
    gains = gain_pair.astype(jnp.float32)
    grad_branch = grad_result.astype(jnp.bfloat16)
    hidden_act, gelu_pull = jax.vjp(partial(jax.nn.gelu, approximate=True), hidden_pre)
    hidden_low = hidden_act.astype(jnp.bfloat16)
    grad_act = reverse_matmul_answer(grad_branch, down_full)
    grad_pre = gelu_pull(grad_act)[0].astype(jnp.bfloat16)
    grad_normed_second = reverse_matmul_answer(grad_pre, up_full)
    unused_second, second_pull = jax.vjp(norm_apply, middle, gains[1])
    grad_middle_norm, grad_gain_second = second_pull(grad_normed_second)
    grad_middle = grad_result + grad_middle_norm
    grad_attn = grad_middle.astype(jnp.bfloat16)
    grad_mixed = reverse_matmul_answer(grad_attn, out_full).astype(jnp.bfloat16)
    left_rows = (mixed_low, normed_second, hidden_low)
    right_rows = (grad_attn, grad_pre, grad_branch)
    return (grad_middle, grad_mixed, left_rows, right_rows, grad_gain_second)


def entry_backward(saved, weights, cosine, sine, allowed, grad_middle, grad_mixed):
    resid, normed_first, query_rows, key_rows, value_rows, log_total = saved[:6]
    qkv_full = weights[0]
    gains = weights[4].astype(jnp.float32)
    rows = resid.shape[0]
    grad_query, grad_keys, grad_values = attend_backward(
        query_rows,
        key_rows,
        value_rows,
        allowed,
        log_total,
        grad_mixed.reshape(rows, HEADS, HEAD_DIM),
    )
    grad_query = unrotate(grad_query, cosine, sine).reshape(rows, MODEL_WIDTH)
    grad_keys = unrotate(grad_keys, cosine, sine).reshape(rows, MODEL_WIDTH)
    grad_values = grad_values.reshape(rows, MODEL_WIDTH)
    grad_projected = jnp.concatenate([grad_query, grad_keys, grad_values], axis=1).astype(
        jnp.bfloat16
    )
    grad_normed_first = reverse_matmul_answer(grad_projected, qkv_full)
    unused_first, first_pull = jax.vjp(norm_apply, resid, gains[0])
    grad_resid_norm, grad_gain_first = first_pull(grad_normed_first)
    return (grad_middle + grad_resid_norm, normed_first, grad_projected, grad_gain_first)


def body(
    patch_observations,
    sequence_labels,
    leading_filler_count,
    intake_latent_matrix,
    intake_latent_offset,
    intake_emit_matrix,
    intake_emit_offset,
    intake_shortcut_matrix,
    attention_entry_matrices,
    attention_merge_matrix,
    feedforward_widen_matrix,
    feedforward_shrink_matrix,
    layer_scale_factors,
    readout_latent_matrix,
    readout_latent_offset,
    readout_emit_matrix,
    readout_emit_offset,
    readout_shortcut_matrix,
    loss_sensitivity,
):
    patch_len = patch_observations.shape[1]
    position, pad_count, allowed, keep_rows = layout_rows(
        sequence_labels[0], leading_filler_count[0], patch_len
    )
    cosine, sine = rotary_tables(position, HEAD_DIM)
    columns = jnp.arange(patch_len, dtype=jnp.int32)
    pad_mask = columns[None, :] < pad_count[:, None]
    features = jnp.concatenate(
        [
            jnp.where(pad_mask, jnp.zeros_like(patch_observations), patch_observations),
            pad_mask.astype(jnp.bfloat16),
        ],
        axis=1,
    )
    entry_pre = (
        jnp.dot(features, intake_latent_matrix, preferred_element_type=jnp.float32)
        + intake_latent_offset
    )
    entry_hidden = jax.nn.silu(entry_pre).astype(jnp.bfloat16)
    resid = (
        jnp.dot(entry_hidden, intake_emit_matrix, preferred_element_type=jnp.float32)
        + intake_emit_offset
        + jnp.dot(features, intake_shortcut_matrix, preferred_element_type=jnp.float32)
    )
    layer_count = attention_entry_matrices.shape[0]
    group = lax.axis_size("head")
    group_place = lax.axis_index("head")
    outer = lax.axis_size("dp") // 8
    me = lax.axis_index("dp").astype(jnp.int32)
    places = me.reshape(1)
    own_count = layer_scale_factors.shape[2]
    rows = patch_observations.shape[0]

    group_width = readout_latent_offset.shape[0]
    offsets = jnp.stack([readout_latent_offset, readout_emit_offset])
    coarse = lax.reduce_precision(offsets, 8, 7)
    offset_rows = jnp.concatenate([coarse, offsets - coarse], axis=0).astype(jnp.bfloat16)
    offset_rows = jnp.pad(offset_rows, ((0, 12), (0, 0)))
    sent = jnp.concatenate(
        [
            loss_sensitivity.reshape(group, rows, group_width),
            jnp.broadcast_to(offset_rows[None], (group, 16, group_width)),
        ],
        axis=1,
    )
    gain_columns = layer_scale_factors.reshape(2 * layer_count, own_count).T
    gain_columns = jnp.pad(gain_columns, ((0, 0), (0, 128 - 2 * layer_count)))
    chunks = []
    for layer_index in range(layer_count):
        entry_own = attention_entry_matrices[layer_index]
        widths = [3 * MODEL_WIDTH]
        if layer_index == 0:
            entry_own = jnp.concatenate([entry_own, gain_columns], axis=1)
            widths.append(128)
        chunks.append((entry_own, widths))
        rest_own = jnp.concatenate(
            [
                attention_merge_matrix[layer_index],
                feedforward_widen_matrix[layer_index],
                feedforward_shrink_matrix[layer_index],
            ],
            axis=1,
        )
        chunks.append((rest_own, [MODEL_WIDTH] * 3))
    head_own = jnp.concatenate(
        [
            lax.dynamic_index_in_dim(
                matrix.reshape(outer, 8, -1, group_width), me % 8, 1, keepdims=False
            )
            for matrix in (readout_latent_matrix, readout_shortcut_matrix, readout_emit_matrix)
        ],
        axis=2,
    )
    chunks.append((head_own, [3 * group_width]))
    count = len(chunks)

    def gather_chunk(number, own):
        if number < count - 1:
            return gather_head(own)
        return lax.all_gather(own, "head", axis=0, tiled=True)

    helds = [gather_chunk(0, chunks[0][0])]
    firsts, fars, wholes = [], [], []
    onward = ()
    met = lax.all_to_all(after(sent, helds[0]), "head", split_axis=0, concat_axis=0, tiled=True)
    saved_states = []
    layer_weights = []
    gain_rows = None
    for number in range(count + 1):
        step = []
        if number < count:
            if number + 1 < count:
                helds.append(gather_chunk(number + 1, chunks[number + 1][0]))
                step.append(helds[-1])
            step += [swap(helds[number], 1), swap(helds[number], 2)]
            if number == 0:
                step.append(resid)
        if number > 0:
            step += [swap(onward[0], 1), swap(onward[1], 2)]
        if number > 1:
            chunk = number - 2
            layer_index = chunk // 2
            pieces = all_pieces(helds[chunk], *firsts[chunk], *fars[chunk])
            wholes.append(place(places, pieces, chunks[chunk][1]))
            if chunk == 0:
                gain_rows = wholes[0][1][0, :, : 2 * layer_count].T
                gain_rows = gain_rows.reshape(layer_count, 2, -1)
            if chunk % 2 == 0:
                saved = entry_forward(
                    resid, wholes[chunk][0][0], gain_rows[layer_index], cosine, sine, allowed
                )
                step.append(saved[6])
            else:
                rest_weights = [part[0] for part in wholes[chunk]]
                layer_weights.append((wholes[chunk - 1][0][0], *rest_weights, gain_rows[layer_index]))
                saved = (*saved[:6], mixed_low)
                resid, saved = rest_forward(saved, *rest_weights, gain_rows[layer_index])
                saved_states.append(saved)
                step.append(resid)
        waiting = [own for own, _ in chunks[number + 2 :]]
        values = lax.optimization_barrier((*step, *waiting))
        step = list(values[: len(step)])
        for member, own in enumerate(values[len(step) :]):
            chunks[number + 2 + member] = (own, chunks[number + 2 + member][1])
        if number < count:
            if number + 1 < count:
                helds[number + 1] = step.pop(0)
            firsts.append((step.pop(0), step.pop(0)))
            if number == 0:
                resid = step.pop(0)
        if number > 0:
            fars.append((step.pop(0), step.pop(0)))
        if number > 1:
            if (number - 2) % 2 == 0:
                mixed_low = step.pop(0)
            else:
                resid = step.pop(0)
        if number < count:
            onward = second_step(helds[number], *firsts[number])
    head_whole = place(
        places, all_pieces(helds[-1], *firsts[-1], *fars[-1]), chunks[-1][1]
    )[0]

    sensitivity = met[:, :rows]
    head_offsets = met[:, rows : rows + 4].astype(jnp.float32)
    latent_offsets = head_offsets[:, 0] + head_offsets[:, 2]
    emit_offsets = head_offsets[:, 1] + head_offsets[:, 3]

    top = resid.astype(jnp.bfloat16)
    keep_column = keep_rows[:, None]
    two = 2 * group_width
    inner_parts = [
        jnp.dot(top, head_whole[part][:, :two], preferred_element_type=jnp.float32)
        for part in range(group)
    ]
    head_pre = jnp.concatenate(
        [inner_parts[part][:, :group_width] + latent_offsets[part] for part in range(group)],
        axis=1,
    )
    head_hidden = jax.nn.silu(head_pre).astype(jnp.bfloat16)
    forecast = jnp.stack(
        [
            (
                jnp.dot(
                    head_hidden, head_whole[part][:, two:], preferred_element_type=jnp.float32
                )
                + emit_offsets[part]
                + inner_parts[part][:, group_width:]
            )
            * keep_column
            for part in range(group)
        ]
    ).astype(jnp.bfloat16)
    token_predictions = lax.all_to_all(
        forecast, "head", split_axis=0, concat_axis=0, tiled=True
    ).reshape(group * rows, group_width)
    grad_forecast = (sensitivity.astype(jnp.float32) * keep_column).astype(jnp.bfloat16)
    grad_hidden = sum(
        reverse_matmul_answer(grad_forecast[part], head_whole[part][:, two:])
        for part in range(group)
    )
    unused_head, head_pull = jax.vjp(jax.nn.silu, head_pre)
    grad_head_pre = head_pull(grad_hidden)[0].astype(jnp.bfloat16)
    grad_resid = sum(
        reverse_matmul_answer(
            jnp.concatenate(
                [
                    grad_head_pre[:, part * group_width : (part + 1) * group_width],
                    grad_forecast[part],
                ],
                axis=1,
            ),
            head_whole[part][:, :two],
        )
        for part in range(group)
    )
    grad_forecast_rows = jnp.concatenate([grad_forecast[part] for part in range(group)], axis=1)
    head_bias_rows = (
        jnp.sum(grad_head_pre.astype(jnp.float32), axis=0),
        jnp.sum(grad_forecast_rows.astype(jnp.float32), axis=0),
    )
    head_sums, first, last = column_sums(
        me,
        [
            (top, grad_head_pre),
            (top, grad_forecast_rows),
            (head_hidden, grad_forecast_rows),
        ],
    )

    ahead = [(), first]
    lasts = [last]
    layer_sums = [None] * layer_count
    gain_sums = [None] * layer_count
    for layer_index in reversed(range(layer_count)):
        saved, weights = saved_states[layer_index], layer_weights[layer_index]
        grad_resid = after(grad_resid, *ahead[-2])
        grad_middle, grad_mixed, left_rows, right_rows, gain_second = rest_backward(
            saved, weights, grad_resid
        )
        pairs = list(zip(left_rows, right_rows, strict=True))
        rest, first, last = weight_sums(me, pairs)
        ahead.append((*lasts[-1], *first))
        lasts.append(last)
        grad_mixed = after(grad_mixed, *ahead[-2])
        grad_resid, left, right, gain_first = entry_backward(
            saved, weights, cosine, sine, allowed, grad_middle, grad_mixed
        )
        entry, first, last = weight_sums(me, [(left, right)])
        ahead.append((*lasts[-1], *first))
        lasts.append(last)
        layer_sums[layer_index] = (entry[0], rest[0], rest[1], rest[2])
        gain_sums[layer_index] = (gain_first, gain_second)
    grad_resid = after(grad_resid, *ahead[-2])
    grad_entry = grad_resid.astype(jnp.bfloat16)
    grad_entry_outer = dyadic_accumulation(entry_hidden, grad_entry)
    grad_entry_outer_bias = jnp.sum(grad_entry.astype(jnp.float32), axis=0)
    grad_entry_skip = dyadic_accumulation(features, grad_entry)
    unused_entry, entry_pull = jax.vjp(jax.nn.silu, entry_pre)
    grad_entry_pre = entry_pull(reverse_matmul_answer(grad_entry, intake_emit_matrix))[0].astype(
        jnp.bfloat16
    )
    grad_entry_inner = dyadic_accumulation(features, grad_entry_pre)
    grad_entry_inner_bias = jnp.sum(grad_entry_pre.astype(jnp.float32), axis=0)
    grad_features = reverse_matmul_answer(
        grad_entry_pre, intake_latent_matrix
    ) + reverse_matmul_answer(grad_entry, intake_shortcut_matrix)
    values_grad = jnp.where(pad_mask, 0.0, grad_features[:, :patch_len])
    extra_rows = jnp.concatenate(
        [
            grad_entry_inner,
            grad_entry_skip,
            grad_entry_inner_bias[None],
            grad_entry_outer_bias[None],
        ]
        + [row[None] for row in head_bias_rows]
        + [row[None] for pair in gain_sums for row in pair],
        axis=0,
    )
    entry_main, entry_extra = sum_everywhere(me, grad_entry_outer, extra_rows)
    inner_rows = 2 * patch_len
    last = 2 * inner_rows
    entry_sums = (
        entry_extra[:inner_rows],
        entry_extra[last],
        entry_main,
        entry_extra[last + 1],
        entry_extra[inner_rows:last],
    )
    head_bias_sums = lax.dynamic_slice_in_dim(
        entry_extra[last + 2 : last + 4], group_place * group_width, group_width, 1
    )
    own_place = (me * group + group_place) * own_count
    gains_grad = lax.dynamic_slice_in_dim(
        entry_extra[last + 4 : last + 4 + 2 * layer_count], own_place, own_count, 1
    ).reshape(layer_count, 2, own_count)
    qkv_grad = jnp.stack([layer_sums[member][0] for member in range(layer_count)])
    out_grad = jnp.stack([layer_sums[member][1] for member in range(layer_count)])
    up_grad = jnp.stack([layer_sums[member][2] for member in range(layer_count)])
    down_grad = jnp.stack([layer_sums[member][3] for member in range(layer_count)])
    return (
        token_predictions,
        values_grad,
        entry_sums[0],
        entry_sums[1],
        entry_sums[2],
        entry_sums[3],
        entry_sums[4],
        qkv_grad,
        out_grad,
        up_grad,
        down_grad,
        gains_grad,
        head_sums[0],
        head_bias_sums[0],
        head_sums[2],
        head_bias_sums[1],
        head_sums[1],
    )


def solution(mesh):
    return jax.shard_map(
        body,
        mesh=mesh,
        in_specs=(
            P(("dp", "head"), None),
            P(("dp", "head"), None),
            P(("dp", "head"), None),
            P(),
            P(),
            P(),
            P(),
            P(),
            P(None, ("dp", "head"), None),
            P(None, ("dp", "head"), None),
            P(None, ("dp", "head"), None),
            P(None, ("dp", "head"), None),
            P(None, None, ("dp", "head")),
            P(None, "head"),
            P("head"),
            P(None, "head"),
            P("head"),
            P(None, "head"),
            P("dp", "head"),
        ),
        out_specs=(
            P("dp", "head"),
            P(("dp", "head"), None),
            P(),
            P(),
            P(),
            P(),
            P(),
            P(None, ("dp", "head"), None),
            P(None, ("dp", "head"), None),
            P(None, ("dp", "head"), None),
            P(None, ("dp", "head"), None),
            P(None, None, ("dp", "head")),
            P(None, "head"),
            P("head"),
            P(None, "head"),
            P("head"),
            P(None, "head"),
        ),
        check_vma=False,
    )
```

```python
from functools import partial
import math

import jax
import jax.numpy as jnp
from jax import lax
from jax.experimental import pallas as pl
from jax.experimental.pallas import tpu as pltpu
from jax.sharding import PartitionSpec as P

MODEL_WIDTH = 1280
HEADS = 16
HEAD_DIM = 80


EPS = 1e-06
ROPE_BASE = 10000.0


def layout_rows(series_row, pad_row, patch_len):
    count = series_row.shape[0]
    order = jnp.arange(count, dtype=jnp.int32)
    same_series = series_row[:, None] == series_row[None, :]
    earlier = order[None, :] < order[:, None]
    position = jnp.sum(jnp.logical_and(same_series, earlier).astype(jnp.int32), axis=1)
    numbers = jnp.arange(pad_row.shape[0], dtype=jnp.int32)
    series_pad = jnp.sum(
        jnp.where(series_row[:, None] == numbers[None, :], pad_row[None, :], 0), axis=1
    )
    pad_count = jnp.where(position == 0, series_pad, 0)
    padded = pad_count == patch_len
    diagonal = order[:, None] == order[None, :]
    reach = jnp.logical_or(jnp.logical_and(earlier, jnp.logical_not(padded)[None, :]), diagonal)
    allowed = jnp.logical_and(same_series, reach)
    keep_rows = jnp.where(padded, 0.0, 1.0).astype(jnp.float32)
    return (position, pad_count, allowed, keep_rows)


def rotary_tables(position, head_dim):
    half = head_dim // 2
    steps = jnp.arange(half, dtype=jnp.float32) / half
    inverse = jnp.exp(-math.log(ROPE_BASE) * steps)
    angles = position.astype(jnp.float32)[:, None] * inverse[None, :]
    return (jnp.cos(angles)[:, None, :], jnp.sin(angles)[:, None, :])


def rotate(heads_rows, cosine, sine):
    half = heads_rows.shape[-1] // 2
    first = heads_rows[..., :half]
    second = heads_rows[..., half:]
    return jnp.concatenate(
        [first * cosine - second * sine, second * cosine + first * sine], axis=-1
    )


def unrotate(grad_rows, cosine, sine):
    half = grad_rows.shape[-1] // 2
    first = grad_rows[..., :half]
    second = grad_rows[..., half:]
    return jnp.concatenate(
        [first * cosine + second * sine, second * cosine - first * sine], axis=-1
    )


def norm_apply(resid, gain):
    return resid * lax.rsqrt(jnp.mean(resid * resid, axis=-1, keepdims=True) + EPS) * gain


def dyadic_accumulation(left, right):
    return lax.dot_general(
        left, right, (((0,), (0,)), ((), ())), preferred_element_type=jnp.float32
    )


def reverse_matmul_answer(grad_rows, weight):
    return lax.dot_general(
        grad_rows, weight, (((1,), (1,)), ((), ())), preferred_element_type=jnp.float32
    )


def masked_scores(query_rows, key_rows, allowed):
    scale = 1.0 / math.sqrt(query_rows.shape[-1])
    scores = (
        jnp.einsum("qhd,khd->hqk", query_rows, key_rows, preferred_element_type=jnp.float32) * scale
    )
    return jnp.where(allowed[None], scores, -1e30)


def attend_forward(query_rows, key_rows, value_rows, allowed):
    scores = masked_scores(query_rows, key_rows, allowed)
    peak = jnp.max(scores, axis=-1, keepdims=True)
    weights = jnp.exp(scores - peak)
    total = jnp.sum(weights, axis=-1, keepdims=True)
    probs = (weights / total).astype(jnp.bfloat16)
    mixed = jnp.einsum("hqk,khd->qhd", probs, value_rows, preferred_element_type=jnp.float32)
    return (mixed, peak + jnp.log(total))


def attend_backward(query_rows, key_rows, value_rows, allowed, log_total, grad_mixed):
    scale = 1.0 / math.sqrt(query_rows.shape[-1])
    scores = masked_scores(query_rows, key_rows, allowed)
    probs = jnp.where(allowed[None], jnp.exp(scores - log_total), 0.0)
    grad_probs = jnp.einsum(
        "qhd,khd->hqk", grad_mixed, value_rows, preferred_element_type=jnp.float32
    )
    grad_values = jnp.einsum(
        "hqk,qhd->khd", probs.astype(jnp.bfloat16), grad_mixed, preferred_element_type=jnp.float32
    )
    center = jnp.sum(grad_probs * probs, axis=-1, keepdims=True)
    grad_scores = (probs * (grad_probs - center)).astype(jnp.bfloat16)
    grad_query = (
        jnp.einsum("hqk,khd->qhd", grad_scores, key_rows, preferred_element_type=jnp.float32)
        * scale
    )
    grad_keys = (
        jnp.einsum("hqk,qhd->khd", grad_scores, query_rows, preferred_element_type=jnp.float32)
        * scale
    )
    return (grad_query, grad_keys, grad_values)


def after(value, *earlier):
    return lax.optimization_barrier((value, *earlier))[0]


def swap(v, bit):
    size = lax.axis_size("dp")
    return lax.ppermute(v, "dp", [(i, i ^ (1 << bit)) for i in range(size)])


def outer_groups():
    size = lax.axis_size("dp")
    return [[j + 8 * o for o in range(size // 8)] for j in range(8)]


def place_kernel(plan, piece_count, out_count, me_ref, *refs):
    pieces = refs[:piece_count]
    outs = refs[piece_count : piece_count + out_count]
    held = refs[piece_count + out_count : piece_count + 2 * out_count]
    in_sems, out_sems = refs[piece_count + 2 * out_count :]
    inward, outward = [], []
    for n, (piece, rel, row, out, column) in enumerate(plan):
        source = pieces[piece]
        width = held[out].shape[-1]
        if width != source.shape[-1]:
            source = source.at[:, :, pl.ds(column, width)]
        spot = (slice(None), me_ref[0] ^ rel, pl.ds(row, source.shape[1]), slice(None))
        inward.append(pltpu.make_async_copy(source, held[out].at[spot], in_sems.at[n]))
        outward.append(
            pltpu.make_async_copy(held[out].at[spot], outs[out].at[spot], out_sems.at[n])
        )
    for copy in inward:
        copy.start()
    for copy, onward in zip(inward, outward):
        copy.wait()
        onward.start()
    for onward in outward:
        onward.wait()


def place(me, pieces, widths, first=0):
    plan = []
    for n, (rel, row, _) in enumerate(pieces):
        column = first
        for out, width in enumerate(widths):
            plan.append((n, rel, row, out, column))
            column += width
    arrays = [array for _, _, array in pieces]
    lead, rows, _ = arrays[0].shape
    kind = arrays[0].dtype
    total = sum(8 * lead * rows * -(-w // 128) * 128 for w in widths) * 2
    outs = pl.pallas_call(
        partial(place_kernel, plan, len(arrays), len(widths)),
        out_shape=[jax.ShapeDtypeStruct((lead, 8, rows, w), kind) for w in widths],
        in_specs=[pl.BlockSpec(memory_space=pltpu.SMEM)]
        + [pl.BlockSpec(memory_space=pl.ANY)] * len(arrays),
        out_specs=[pl.BlockSpec(memory_space=pl.ANY)] * len(widths),
        scratch_shapes=[pltpu.VMEM((lead, 8, rows, w), kind) for w in widths]
        + [pltpu.SemaphoreType.DMA((len(plan),))] * 2,
        compiler_params=pltpu.CompilerParams(vmem_limit_bytes=total + (4 << 20)),
        cost_estimate=pl.CostEstimate(flops=0, bytes_accessed=2 * total, transcendentals=0),
    )(me, *arrays)
    outer = lax.axis_size("dp") // 8
    return [o.reshape(-1, outer * 8 * rows, o.shape[-1]) for o in outs]


def row_half(rows):
    return rows // 32 * 16 if rows >= 32 else rows // 2


def second_step(held, from_x, from_y):
    half = row_half(held.shape[1])
    return from_y[:, :half], from_x[:, half:]


def all_pieces(near, far, near_met, far_met):
    half = far[0].shape[1]
    places = ((0, 0), (2, 0), (4, 0), (6, 0), (6, half))
    pieces = []
    for (rel, row), array, met in zip(places, (*near, *far), (*near_met, *far_met), strict=True):
        pieces += [(rel, row, array), (rel | 1, row, met)]
    return pieces


def spread_rows(held):
    near = (held, swap(held, 1), swap(held, 2))
    onward_x, onward_y = second_step(*near)
    far = (swap(onward_x, 1), swap(onward_y, 2))
    return all_pieces(near, far, [swap(part, 0) for part in near], [swap(part, 0) for part in far])


def gather_head(own):
    held = lax.all_gather(own, "head", axis=0, tiled=True)[None]
    if lax.axis_size("dp") > 8:
        held = lax.all_gather(
            held, "dp", axis=0, tiled=True, axis_index_groups=outer_groups()
        )
    return held


def pick(rows, place, width):
    picked = rows[:, :width]
    for n in range(1, rows.shape[1] // width):
        picked = jnp.where(place == n, rows[:, n * width : (n + 1) * width], picked)
    return picked


def product_kernel(count, outer, me_ref, *refs):
    lefts, rights, met_lefts, met_rights = (refs[n * count : (n + 1) * count] for n in range(4))
    to_x, to_y, later, own = refs[4 * count :]
    rows, width = own.shape[1] // outer, own.shape[-1]
    half = width // 2
    for n in range(count):
        left, met = lefts[n][...], met_lefts[n][...]
        for rel in range(4):
            place = me_ref[0] ^ (2 * rel)
            for part in range(outer):
                near_left = pick(left[:, part * 8 * rows : (part + 1) * 8 * rows], place, rows)
                met_left = pick(met[:, part * 8 * rows : (part + 1) * 8 * rows], place, rows)
                span = slice(part * rows, (part + 1) * rows)
                for side in range(2):
                    columns = slice(side * half, (side + 1) * half)
                    total = dyadic_accumulation(near_left, rights[n][:, columns])
                    total += dyadic_accumulation(met_left, met_rights[n][:, columns])
                    total = total.astype(own.dtype)
                    if rel == 0:
                        own[n, span, columns] = total
                    elif rel == 1 and side == 0:
                        to_x[1, n, span] = total
                    elif rel == 1:
                        later[1, n, span] = total
                    elif rel == 2 and side == 0:
                        later[0, n, span] = total
                    elif rel == 2:
                        to_y[1, n, span] = total
                    elif side == 0:
                        to_x[0, n, span] = total
                    else:
                        to_y[0, n, span] = total


def pair_products(me, pairs):
    outer = lax.axis_size("dp") // 8
    met = {}
    for pair in pairs:
        for rows in pair:
            if id(rows) not in met:
                met[id(rows)] = swap(rows, 0)
    lefts = [left for left, _ in pairs]
    rights = [right for _, right in pairs]
    count = len(pairs)
    block, width = lefts[0].shape[1] // 8, rights[0].shape[1]
    low = jnp.bfloat16
    return pl.pallas_call(
        partial(product_kernel, count, outer),
        out_shape=[
            jax.ShapeDtypeStruct((2, count, block, width // 2), low),
            jax.ShapeDtypeStruct((2, count, block, width // 2), low),
            jax.ShapeDtypeStruct((2, count, block, width // 2), low),
            jax.ShapeDtypeStruct((count, block, width), low),
        ],
        in_specs=[pl.BlockSpec(memory_space=pltpu.SMEM)]
        + [pl.BlockSpec(memory_space=pltpu.VMEM)] * (4 * count),
        out_specs=[pl.BlockSpec(memory_space=pltpu.VMEM)] * 4,
        compiler_params=pltpu.CompilerParams(vmem_limit_bytes=40 << 20),
        cost_estimate=pl.CostEstimate(
            flops=2 * 256 * 4 * block * width * count,
            bytes_accessed=2 * count * (4 * block * width + 256 * width + 256 * 4 * block),
            transcendentals=0,
        ),
    )(
        (me & 7).reshape(1),
        *lefts,
        *rights,
        *[met[id(left)] for left in lefts],
        *[met[id(right)] for right in rights],
    )


def low_sum(*parts):
    total = parts[0].astype(jnp.float32)
    for part in parts[1:]:
        total = total + part.astype(jnp.float32)
    return total.astype(jnp.bfloat16)


def sum_chips(to_x, to_y, later, own):
    to_x, to_y = swap(to_x, 1), swap(to_y, 2)
    last_y = swap(low_sum(later[0], to_x[0]), 2)
    last_x = swap(low_sum(later[1], to_y[0]), 1)
    half = own.shape[-1] // 2
    total = jnp.concatenate(
        [
            low_sum(own[..., :half], to_x[1], last_y),
            low_sum(own[..., half:], to_y[1], last_x),
        ],
        axis=-1,
    )
    return total, (to_x, to_y), (last_y, last_x)


def sum_group(total):
    outer = lax.axis_size("dp") // 8
    group = lax.axis_size("head")
    lead = total.shape[:-2]
    rows, columns = total.shape[-2:]
    if outer > 1:
        total = lax.psum_scatter(
            total.reshape(*lead, outer, rows // outer, columns),
            "dp",
            scatter_dimension=len(lead),
            tiled=True,
            axis_index_groups=outer_groups(),
        )
    total = total.reshape(*lead, rows // outer, columns)
    return lax.psum_scatter(total, "head", scatter_dimension=len(lead), tiled=True)


def weight_sums(me, pairs):
    total, first, last = sum_chips(*pair_products(me, pairs))
    return sum_group(total).astype(jnp.float32), first, last


def column_sums(me, pairs):
    group = lax.axis_size("head")
    outer = lax.axis_size("dp") // 8
    total, first, last = sum_chips(*pair_products(me, pairs))
    count, rows, columns = total.shape
    total = jnp.moveaxis(total.reshape(count, rows, group, columns // group), 2, 0)
    summed = lax.psum_scatter(total, "head", scatter_dimension=0, tiled=True)[0]
    held = summed.reshape(count * outer, rows // outer, columns // group)
    (whole,) = place((me & 7).reshape(1), spread_rows(held), [columns // group])
    return whole.astype(jnp.float32), first, last


EXTRA_ROWS = 8


def sum_everywhere(me, main, extra):
    group = lax.axis_size("head")
    outer = lax.axis_size("dp") // 8
    devices = 8 * outer * group
    columns = main.shape[1]
    count = extra.shape[0]
    own = main.shape[0] // devices
    extra = jnp.pad(extra, ((0, EXTRA_ROWS * devices - count), (0, 0)))
    rows = jnp.concatenate(
        [main.reshape(devices, own, columns), extra.reshape(devices, EXTRA_ROWS, columns)], axis=1
    ).astype(jnp.bfloat16)
    view = rows.reshape(outer, 4, 2, group * (own + EXTRA_ROWS), columns)
    core = me & 1
    other = lax.dynamic_index_in_dim(view, 1 - core, 2, keepdims=False)
    pair = low_sum(lax.dynamic_index_in_dim(view, core, 2, keepdims=False), swap(other, 0))
    chip = me >> 1
    half = columns // 2

    def picked(rel):
        return lax.dynamic_index_in_dim(pair, chip ^ rel, 1, keepdims=False).reshape(-1, columns)

    own_rows, at_x, at_y, far = (picked(rel) for rel in range(4))
    total, _, _ = sum_chips(
        jnp.stack([far[:, :half], at_x[:, :half]]),
        jnp.stack([far[:, half:], at_y[:, half:]]),
        (at_y[:, :half], at_x[:, half:]),
        own_rows,
    )
    pieces = spread_rows(gather_head(sum_group(total)))
    (whole,) = place((me & 7).reshape(1), pieces, [columns])
    whole = whole.reshape(devices, own + EXTRA_ROWS, columns).astype(jnp.float32)
    return (
        whole[:, :own].reshape(devices * own, columns),
        whole[:, own:].reshape(-1, columns)[:count],
    )


def fetch(plan, me, pieces, whole, sems):
    groups = []
    for group in range(whole.shape[1] // MODEL_WIDTH):
        columns = pl.ds(group * MODEL_WIDTH, MODEL_WIDTH)
        copies = []
        for n, (rel, row, rows) in enumerate(plan):
            first = pl.multiple_of((me ^ rel) * (whole.shape[0] // 8) + row, 16)
            copies.append(
                pltpu.make_async_copy(
                    pieces[n].at[0, :, columns],
                    whole.at[pl.ds(first, rows), columns],
                    sems.at[group * len(plan) + n],
                )
            )
        for copy in copies:
            copy.start()
        groups.append(copies)
    return groups


def arrive(copies):
    for copy in copies:
        copy.wait()


def rows_times(left, whole, first, out, tile):
    def step(n, _):
        at = pl.multiple_of(n * tile, 128)
        out[:, pl.ds(at, tile)] = jnp.dot(
            left, whole[:, pl.ds(first + at, tile)], preferred_element_type=jnp.float32
        )
        return 0

    lax.fori_loop(0, out.shape[1] // tile, step, 0)


def rows_times_turned(left, whole, first, width, out, tile):
    def step(n, _):
        at = pl.multiple_of(n * tile, 128)
        part = reverse_matmul_answer(whole[pl.ds(at, tile), pl.ds(first, width)], left)
        out[:, pl.ds(at, tile)] = part.T
        return 0

    lax.fori_loop(0, out.shape[1] // tile, step, 0)


def inverse_norm(rows):
    return lax.rsqrt(jnp.mean(rows * rows, axis=-1, keepdims=True) + EPS)


def other_half(rows):
    half = HEAD_DIM // 2
    lane = lax.broadcasted_iota(jnp.int32, rows.shape, 1) % HEAD_DIM
    ahead = pltpu.roll(rows, rows.shape[1] - half, 1)
    behind = pltpu.roll(rows, half, 1)
    return jnp.where(lane < half, ahead, behind)


def head_window(head, width):
    first = head * HEAD_DIM // 128 * 128
    last = min(-(-(head + 1) * HEAD_DIM // 128) * 128, width)
    start = head * HEAD_DIM - first
    lane = lax.broadcasted_iota(jnp.int32, (1, last - first), 1)
    return slice(first, last), jnp.logical_and(lane >= start, lane < start + HEAD_DIM)


def entry_forward_kernel(plan, me_ref, resid_ref, gain_ref, cosine_ref, sine_ref, allowed_ref, *refs):
    pieces = refs[: len(plan)]
    normed_ref, query_ref, key_ref, value_ref, total_ref, mixed_ref = refs[len(plan) : len(plan) + 6]
    whole, wide, sems = refs[len(plan) + 6 :]
    groups = fetch(plan, me_ref[0], pieces, whole, sems)
    resid = resid_ref[...]
    normed = (resid * inverse_norm(resid) * gain_ref[...]).astype(jnp.bfloat16)
    normed_ref[...] = normed
    for group, out in enumerate((query_ref, key_ref, value_ref)):
        arrive(groups[group])
        rows_times(normed, whole, group * MODEL_WIDTH, wide, 256)
        rows = wide[...]
        if group < 2:
            rows = rows * cosine_ref[...] + other_half(rows) * sine_ref[...]
        out[...] = rows.astype(jnp.bfloat16)
    scale = 1.0 / math.sqrt(HEAD_DIM)
    allowed = allowed_ref[...] > 0.0
    wide[...] = jnp.zeros_like(wide)
    totals = jnp.zeros(total_ref.shape, jnp.float32)
    head_lane = lax.broadcasted_iota(jnp.int32, total_ref.shape, 1)
    for head in range(HEADS):
        window, inside = head_window(head, MODEL_WIDTH)
        query = jnp.where(inside, query_ref[:, window], 0)
        scores = reverse_matmul_answer(query, key_ref[:, window]) * scale
        scores = jnp.where(allowed, scores, -1e30)
        peak = jnp.max(scores, axis=-1, keepdims=True)
        weights = jnp.exp(scores - peak)
        total = jnp.sum(weights, axis=-1, keepdims=True)
        probs = (weights / total).astype(jnp.bfloat16)
        mixed = jnp.dot(probs, value_ref[:, window], preferred_element_type=jnp.float32)
        wide[:, window] += jnp.where(inside, mixed, 0.0)
        totals = jnp.where(head_lane == head, peak + jnp.log(total), totals)
    total_ref[...] = totals
    mixed_ref[...] = wide[...].astype(jnp.bfloat16)


def gelu_parts(x):
    root = math.sqrt(2.0 / math.pi)
    bend = jnp.tanh(root * (x + 0.044715 * (x * x * x)))
    slope = 0.5 * (1.0 + bend) + 0.5 * x * (1.0 - bend * bend) * root * (
        1.0 + 3.0 * 0.044715 * (x * x)
    )
    return 0.5 * x * (1.0 + bend), slope


def rest_forward_kernel(plan, me_ref, resid_ref, mixed_ref, gain_ref, *refs):
    pieces = refs[: len(plan)]
    result_ref, middle_ref, normed_ref, pre_ref = refs[len(plan) : len(plan) + 4]
    whole, sems = refs[len(plan) + 4 :]
    groups = fetch(plan, me_ref[0], pieces, whole, sems)
    arrive(groups[0])
    rows_times(mixed_ref[...], whole, 0, middle_ref, 256)
    middle = resid_ref[...] + middle_ref[...]
    middle_ref[...] = middle
    normed = (middle * inverse_norm(middle) * gain_ref[...]).astype(jnp.bfloat16)
    normed_ref[...] = normed
    arrive(groups[1])
    rows_times(normed, whole, MODEL_WIDTH, pre_ref, 256)
    act = gelu_parts(pre_ref[...])[0].astype(jnp.bfloat16)
    arrive(groups[2])
    rows_times(act, whole, 2 * MODEL_WIDTH, result_ref, 256)
    result_ref[...] += middle_ref[...]


def norm_back(rows, gain, grad):
    inverse = inverse_norm(rows)
    scaled = grad * gain
    mean = jnp.mean(rows * scaled, axis=-1, keepdims=True)
    sent = inverse * scaled - rows * (inverse * inverse * inverse * mean)
    return sent, jnp.sum(grad * rows * inverse, axis=0, keepdims=True)


def rest_backward_kernel(plan, me_ref, grad_ref, middle_ref, pre_ref, gain_ref, *refs):
    pieces = refs[: len(plan)]
    outs = refs[len(plan) : len(plan) + 7]
    grad_middle_ref, mixed_ref, attn_ref, grad_pre_ref, branch_ref, act_ref, gain_grad_ref = outs
    whole, wide, sems = refs[len(plan) + 7 :]
    groups = fetch(plan, me_ref[0], pieces, whole, sems)
    grad = grad_ref[...]
    branch = grad.astype(jnp.bfloat16)
    branch_ref[...] = branch
    arrive(groups[2])
    rows_times_turned(branch, whole, 2 * MODEL_WIDTH, MODEL_WIDTH, wide, 256)
    act, slope = gelu_parts(pre_ref[...])
    act_ref[...] = act.astype(jnp.bfloat16)
    grad_pre = (wide[...] * slope).astype(jnp.bfloat16)
    grad_pre_ref[...] = grad_pre
    arrive(groups[1])
    rows_times_turned(grad_pre, whole, MODEL_WIDTH, MODEL_WIDTH, wide, 256)
    sent, gain_grad_ref[...] = norm_back(middle_ref[...], gain_ref[...], wide[...])
    grad_middle = grad + sent
    grad_middle_ref[...] = grad_middle
    attn = grad_middle.astype(jnp.bfloat16)
    attn_ref[...] = attn
    arrive(groups[0])
    rows_times_turned(attn, whole, 0, MODEL_WIDTH, wide, 256)
    mixed_ref[...] = wide[...].astype(jnp.bfloat16)


def entry_backward_kernel(
    plan,
    me_ref,
    grad_middle_ref,
    grad_mixed_ref,
    resid_ref,
    query_ref,
    key_ref,
    value_ref,
    total_ref,
    gain_ref,
    cosine_ref,
    sine_ref,
    allowed_ref,
    *refs,
):
    pieces = refs[: len(plan)]
    grad_resid_ref, projected_ref, gain_grad_ref = refs[len(plan) : len(plan) + 3]
    whole, grad_query, grad_key, grad_value, sems = refs[len(plan) + 3 :]
    groups = fetch(plan, me_ref[0], pieces, whole, sems)
    scale = 1.0 / math.sqrt(HEAD_DIM)
    allowed = allowed_ref[...] > 0.0
    totals = total_ref[...]
    grad_query[...] = jnp.zeros_like(grad_query)
    grad_key[...] = jnp.zeros_like(grad_key)
    grad_value[...] = jnp.zeros_like(grad_value)
    for head in range(HEADS):
        window, inside = head_window(head, MODEL_WIDTH)
        query = jnp.where(inside, query_ref[:, window], 0)
        keys = key_ref[:, window]
        grad_mixed = jnp.where(inside, grad_mixed_ref[:, window], 0)
        scores = reverse_matmul_answer(query, keys) * scale
        probs = jnp.where(allowed, jnp.exp(scores - totals[:, head : head + 1]), 0.0)
        grad_probs = reverse_matmul_answer(grad_mixed, value_ref[:, window])
        grad_value[:, window] += dyadic_accumulation(probs.astype(jnp.bfloat16), grad_mixed)
        center = jnp.sum(grad_probs * probs, axis=-1, keepdims=True)
        grad_scores = (probs * (grad_probs - center)).astype(jnp.bfloat16)
        along = jnp.dot(grad_scores, keys, preferred_element_type=jnp.float32)
        grad_query[:, window] += jnp.where(inside, along * scale, 0.0)
        grad_key[:, window] += dyadic_accumulation(grad_scores, query) * scale
    for group, part in enumerate((grad_query, grad_key, grad_value)):
        rows = part[...]
        if group < 2:
            rows = rows * cosine_ref[...] - other_half(rows) * sine_ref[...]
        projected_ref[:, group * MODEL_WIDTH : (group + 1) * MODEL_WIDTH] = rows.astype(jnp.bfloat16)
    for copies in groups:
        arrive(copies)
    rows_times_turned(projected_ref[...], whole, 0, 3 * MODEL_WIDTH, grad_query, 256)
    sent, gain_grad_ref[...] = norm_back(resid_ref[...], gain_ref[...], grad_query[...])
    grad_resid_ref[...] = grad_middle_ref[...] + sent


def whole_call(kernel, me, pieces, inputs, outs, wides, flops):
    rows = inputs[0].shape[0]
    plan = [(rel, row, array.shape[1]) for rel, row, array in pieces]
    blocks = 8 * pieces[0][2].shape[1]
    columns = 3 * MODEL_WIDTH
    vmem = pl.BlockSpec(memory_space=pltpu.VMEM)
    return pl.pallas_call(
        partial(kernel, plan),
        out_shape=[jax.ShapeDtypeStruct(shape, kind) for shape, kind in outs],
        in_specs=[pl.BlockSpec(memory_space=pltpu.SMEM)]
        + [vmem] * len(inputs)
        + [pl.BlockSpec(memory_space=pl.ANY)] * len(pieces),
        out_specs=[vmem] * len(outs),
        scratch_shapes=[pltpu.VMEM((blocks, columns), jnp.bfloat16)]
        + [pltpu.VMEM((rows, MODEL_WIDTH), jnp.float32)] * wides
        + [pltpu.SemaphoreType.DMA((3 * len(pieces),))],
        compiler_params=pltpu.CompilerParams(vmem_limit_bytes=44 << 20),
        cost_estimate=pl.CostEstimate(
            flops=flops, bytes_accessed=2 * blocks * columns, transcendentals=0
        ),
    )(me, *inputs, *[array for _, _, array in pieces])


def in_kernel(pieces):
    lead, rows, _ = pieces[0][2].shape
    return lead == 1 and rows % 32 == 0


LOW, FULL = jnp.bfloat16, jnp.float32


class Layer:
    def __init__(self, places, entry_pieces, gains, tables, allowed):
        self.places, self.entry_pieces, self.gains = places, entry_pieces, gains
        self.tables, self.allowed = tables, allowed
        self.fetched = in_kernel(entry_pieces)
        if not self.fetched:
            self.entry_whole = place(places, entry_pieces, [3 * MODEL_WIDTH])[0][0]

    def add_rest(self, rest_pieces):
        self.rest_pieces = rest_pieces
        if not self.fetched:
            self.rest_whole = [part[0] for part in place(self.places, rest_pieces, [MODEL_WIDTH] * 3)]

    def shapes(self, *kinds):
        rows = self.allowed.shape[0]
        return [((rows, width), kind) for width, kind in kinds]

    def entry_forward(self, resid):
        if not self.fetched:
            self.saved = entry_forward(
                resid, self.entry_whole, self.gains, *self.tables[:2], self.allowed
            )
            return self.saved[6]
        wide = (MODEL_WIDTH, LOW)
        self.resid = resid
        outs = whole_call(
            entry_forward_kernel,
            self.places,
            self.entry_pieces,
            (resid, self.gains[:1].astype(FULL), *self.tables[2:], self.allowed.astype(FULL)),
            self.shapes(wide, wide, wide, wide, (128, FULL), wide),
            1,
            2 * resid.shape[0] * 3 * MODEL_WIDTH * MODEL_WIDTH,
        )
        self.normed_first, self.heads = outs[0], outs[1:5]
        return outs[5]

    def rest_forward(self, mixed):
        if not self.fetched:
            result, self.saved = rest_forward(
                (*self.saved[:6], mixed), *self.rest_whole, self.gains
            )
            return result
        self.mixed = mixed
        result, self.middle, self.normed_second, self.hidden_pre = whole_call(
            rest_forward_kernel,
            self.places,
            self.rest_pieces,
            (self.resid, mixed, self.gains[1:].astype(FULL)),
            self.shapes(
                (MODEL_WIDTH, FULL), (MODEL_WIDTH, FULL), (MODEL_WIDTH, LOW), (MODEL_WIDTH, FULL)
            ),
            0,
            2 * mixed.shape[0] * 3 * MODEL_WIDTH * MODEL_WIDTH,
        )
        return result

    def rest_backward(self, grad):
        if not self.fetched:
            weights = (self.entry_whole, *self.rest_whole, self.gains)
            return rest_backward(self.saved, weights, grad)
        wide = (MODEL_WIDTH, LOW)
        grad_middle, grad_mixed, grad_attn, grad_pre, branch, act, gain_grad = whole_call(
            rest_backward_kernel,
            self.places,
            self.rest_pieces,
            (grad, self.middle, self.hidden_pre, self.gains[1:].astype(FULL)),
            self.shapes((MODEL_WIDTH, FULL), wide, wide, wide, wide, wide)
            + [((1, MODEL_WIDTH), FULL)],
            1,
            2 * grad.shape[0] * 3 * MODEL_WIDTH * MODEL_WIDTH,
        )
        lefts = (self.mixed, self.normed_second, act)
        return grad_middle, grad_mixed, lefts, (grad_attn, grad_pre, branch), gain_grad[0]

    def entry_backward(self, grad_middle, grad_mixed):
        if not self.fetched:
            weights = (self.entry_whole, *self.rest_whole, self.gains)
            return entry_backward(
                self.saved, weights, *self.tables[:2], self.allowed, grad_middle, grad_mixed
            )
        grad_resid, projected, gain_grad = whole_call(
            entry_backward_kernel,
            self.places,
            self.entry_pieces,
            (
                grad_middle,
                grad_mixed,
                self.resid,
                *self.heads,
                self.gains[:1].astype(FULL),
                *self.tables[2:],
                self.allowed.astype(FULL),
            ),
            self.shapes((MODEL_WIDTH, FULL), (3 * MODEL_WIDTH, LOW)) + [((1, MODEL_WIDTH), FULL)],
            3,
            2 * grad_middle.shape[0] * 3 * MODEL_WIDTH * MODEL_WIDTH,
        )
        return grad_resid, self.normed_first, projected, gain_grad[0]


def entry_forward(resid, qkv_full, gain_pair, cosine, sine, allowed):
    gains = gain_pair.astype(jnp.float32)
    rows = resid.shape[0]
    normed_first = norm_apply(resid, gains[0]).astype(jnp.bfloat16)
    projected = jnp.dot(normed_first, qkv_full, preferred_element_type=jnp.float32)
    query_rows = rotate(
        projected[:, :MODEL_WIDTH].reshape(rows, HEADS, HEAD_DIM), cosine, sine
    ).astype(jnp.bfloat16)
    key_rows = rotate(
        projected[:, MODEL_WIDTH : 2 * MODEL_WIDTH].reshape(rows, HEADS, HEAD_DIM), cosine, sine
    ).astype(jnp.bfloat16)
    value_rows = projected[:, 2 * MODEL_WIDTH :].reshape(rows, HEADS, HEAD_DIM).astype(jnp.bfloat16)

    mixed, log_total = attend_forward(query_rows, key_rows, value_rows, allowed)
    mixed_low = mixed.reshape(rows, MODEL_WIDTH).astype(jnp.bfloat16)
    return (resid, normed_first, query_rows, key_rows, value_rows, log_total, mixed_low)


def rest_forward(saved, out_full, up_full, down_full, gain_pair):
    gains = gain_pair.astype(jnp.float32)
    resid, mixed_low = saved[0], saved[6]
    middle = resid + jnp.dot(mixed_low, out_full, preferred_element_type=jnp.float32)
    normed_second = norm_apply(middle, gains[1]).astype(jnp.bfloat16)
    hidden_pre = jnp.dot(normed_second, up_full, preferred_element_type=jnp.float32)
    hidden_act = jax.nn.gelu(hidden_pre, approximate=True).astype(jnp.bfloat16)
    result = middle + jnp.dot(hidden_act, down_full, preferred_element_type=jnp.float32)
    return (result, (*saved, middle, normed_second, hidden_pre))


def rest_backward(saved, weights, grad_result):
    mixed_low, middle, normed_second, hidden_pre = saved[6:]
    _, out_full, up_full, down_full, gain_pair = weights
    gains = gain_pair.astype(jnp.float32)
    grad_branch = grad_result.astype(jnp.bfloat16)
    hidden_act, gelu_pull = jax.vjp(partial(jax.nn.gelu, approximate=True), hidden_pre)
    hidden_low = hidden_act.astype(jnp.bfloat16)
    grad_act = reverse_matmul_answer(grad_branch, down_full)
    grad_pre = gelu_pull(grad_act)[0].astype(jnp.bfloat16)
    grad_normed_second = reverse_matmul_answer(grad_pre, up_full)
    unused_second, second_pull = jax.vjp(norm_apply, middle, gains[1])
    grad_middle_norm, grad_gain_second = second_pull(grad_normed_second)
    grad_middle = grad_result + grad_middle_norm
    grad_attn = grad_middle.astype(jnp.bfloat16)
    grad_mixed = reverse_matmul_answer(grad_attn, out_full).astype(jnp.bfloat16)
    left_rows = (mixed_low, normed_second, hidden_low)
    right_rows = (grad_attn, grad_pre, grad_branch)
    return (grad_middle, grad_mixed, left_rows, right_rows, grad_gain_second)


def entry_backward(saved, weights, cosine, sine, allowed, grad_middle, grad_mixed):
    resid, normed_first, query_rows, key_rows, value_rows, log_total = saved[:6]
    qkv_full = weights[0]
    gains = weights[4].astype(jnp.float32)
    rows = resid.shape[0]
    grad_query, grad_keys, grad_values = attend_backward(
        query_rows,
        key_rows,
        value_rows,
        allowed,
        log_total,
        grad_mixed.reshape(rows, HEADS, HEAD_DIM),
    )
    grad_query = unrotate(grad_query, cosine, sine).reshape(rows, MODEL_WIDTH)
    grad_keys = unrotate(grad_keys, cosine, sine).reshape(rows, MODEL_WIDTH)
    grad_values = grad_values.reshape(rows, MODEL_WIDTH)
    grad_projected = jnp.concatenate([grad_query, grad_keys, grad_values], axis=1).astype(
        jnp.bfloat16
    )
    grad_normed_first = reverse_matmul_answer(grad_projected, qkv_full)
    unused_first, first_pull = jax.vjp(norm_apply, resid, gains[0])
    grad_resid_norm, grad_gain_first = first_pull(grad_normed_first)
    return (grad_middle + grad_resid_norm, normed_first, grad_projected, grad_gain_first)


def body(
    patch_observations,
    sequence_labels,
    leading_filler_count,
    intake_latent_matrix,
    intake_latent_offset,
    intake_emit_matrix,
    intake_emit_offset,
    intake_shortcut_matrix,
    attention_entry_matrices,
    attention_merge_matrix,
    feedforward_widen_matrix,
    feedforward_shrink_matrix,
    layer_scale_factors,
    readout_latent_matrix,
    readout_latent_offset,
    readout_emit_matrix,
    readout_emit_offset,
    readout_shortcut_matrix,
    loss_sensitivity,
):
    patch_len = patch_observations.shape[1]
    position, pad_count, allowed, keep_rows = layout_rows(
        sequence_labels[0], leading_filler_count[0], patch_len
    )
    cosine, sine = rotary_tables(position, HEAD_DIM)
    columns = jnp.arange(patch_len, dtype=jnp.int32)
    pad_mask = columns[None, :] < pad_count[:, None]
    features = jnp.concatenate(
        [
            jnp.where(pad_mask, jnp.zeros_like(patch_observations), patch_observations),
            pad_mask.astype(jnp.bfloat16),
        ],
        axis=1,
    )
    entry_pre = (
        jnp.dot(features, intake_latent_matrix, preferred_element_type=jnp.float32)
        + intake_latent_offset
    )
    entry_hidden = jax.nn.silu(entry_pre).astype(jnp.bfloat16)
    resid = (
        jnp.dot(entry_hidden, intake_emit_matrix, preferred_element_type=jnp.float32)
        + intake_emit_offset
        + jnp.dot(features, intake_shortcut_matrix, preferred_element_type=jnp.float32)
    )
    layer_count = attention_entry_matrices.shape[0]
    group = lax.axis_size("head")
    group_place = lax.axis_index("head")
    outer = lax.axis_size("dp") // 8
    me = lax.axis_index("dp").astype(jnp.int32)
    places = (me & 7).reshape(1)
    own_count = layer_scale_factors.shape[2]
    rows = patch_observations.shape[0]

    group_width = readout_latent_offset.shape[0]
    offsets = jnp.stack([readout_latent_offset, readout_emit_offset])
    coarse = lax.reduce_precision(offsets, 8, 7)
    offset_rows = jnp.concatenate([coarse, offsets - coarse], axis=0).astype(jnp.bfloat16)
    offset_rows = jnp.pad(offset_rows, ((0, 12), (0, 0)))
    sent = jnp.concatenate(
        [
            loss_sensitivity.reshape(group, rows, group_width),
            jnp.broadcast_to(offset_rows[None], (group, 16, group_width)),
        ],
        axis=1,
    )
    gain_columns = layer_scale_factors.reshape(2 * layer_count, own_count).T
    gain_columns = jnp.pad(gain_columns, ((0, 0), (0, 128 - 2 * layer_count)))
    chunks = []
    for layer_index in range(layer_count):
        entry_own = attention_entry_matrices[layer_index]
        if layer_index == 0:
            entry_own = jnp.concatenate([entry_own, gain_columns], axis=1)
        chunks.append(entry_own)
        rest_own = jnp.concatenate(
            [
                attention_merge_matrix[layer_index],
                feedforward_widen_matrix[layer_index],
                feedforward_shrink_matrix[layer_index],
            ],
            axis=1,
        )
        chunks.append(rest_own)
    head_own = jnp.concatenate(
        [
            lax.dynamic_index_in_dim(
                matrix.reshape(outer, 8, -1, group_width), me % 8, 1, keepdims=False
            )
            for matrix in (readout_latent_matrix, readout_shortcut_matrix, readout_emit_matrix)
        ],
        axis=2,
    )
    chunks.append(head_own)
    count = len(chunks)

    def gather_chunk(number, own):
        if number < count - 1:
            return gather_head(own)
        return lax.all_gather(own, "head", axis=0, tiled=True)

    held = gather_chunk(0, chunks[0])
    met = lax.all_to_all(after(sent, held), "head", split_axis=0, concat_axis=0, tiled=True)
    cosine_wide = jnp.tile(jnp.concatenate([cosine[:, 0], cosine[:, 0]], axis=1), (1, HEADS))
    sine_wide = jnp.tile(jnp.concatenate([-sine[:, 0], sine[:, 0]], axis=1), (1, HEADS))
    tables = (cosine, sine, cosine_wide, sine_wide)
    nears, fars, near_mets = [], [], []
    layers = []
    onward = None
    for number in range(count + 1):
        step = {}
        if number < count:
            step["x"], step["y"] = swap(held, 1), swap(held, 2)
        if number + 1 < count:
            step["next"] = gather_chunk(number + 1, chunks[number + 1])
        if number == 0:
            step["resid"] = resid
        else:
            step["far"] = (swap(onward[0], 1), swap(onward[1], 2))
            near_mets.append([swap(part, 0) for part in after(nears[number - 1], onward)])
        if number > 1:
            chunk = number - 2
            far_met = [swap(part, 0) for part in after(fars[chunk], onward)]
            pieces = all_pieces(nears[chunk], fars[chunk], near_mets[chunk], far_met)
            if chunk == 0:
                gain_rows = place(places, pieces, [128], 3 * MODEL_WIDTH)[0][0]
                gain_rows = gain_rows[:, : 2 * layer_count].T.reshape(layer_count, 2, -1)
            if chunk % 2 == 0:
                layers.append(Layer(places, pieces, gain_rows[chunk // 2], tables, allowed))
                step["mixed"] = layers[-1].entry_forward(resid)
            else:
                layers[-1].add_rest(pieces)
                step["resid"] = layers[-1].rest_forward(mixed)
        step["own"] = chunks[number + 2 :]
        step = lax.optimization_barrier(step)
        chunks[number + 2 :] = step["own"]
        if number < count:
            nears.append((held, step["x"], step["y"]))
            onward = second_step(*nears[-1])
        held = step.get("next")
        if number > 0:
            fars.append(step["far"])
        resid = step.get("resid", resid)
        mixed = step.get("mixed")
    head_far_met = [swap(part, 0) for part in fars[-1]]
    head_pieces = all_pieces(nears[-1], fars[-1], near_mets[-1], head_far_met)
    head_whole = place(places, head_pieces, [3 * group_width])[0]

    sensitivity = met[:, :rows]
    head_offsets = met[:, rows : rows + 4].astype(jnp.float32)
    latent_offsets = head_offsets[:, 0] + head_offsets[:, 2]
    emit_offsets = head_offsets[:, 1] + head_offsets[:, 3]

    top = resid.astype(jnp.bfloat16)
    keep_column = keep_rows[:, None]
    two = 2 * group_width
    inner_parts = [
        jnp.dot(top, head_whole[part][:, :two], preferred_element_type=jnp.float32)
        for part in range(group)
    ]
    head_pre = jnp.concatenate(
        [inner_parts[part][:, :group_width] + latent_offsets[part] for part in range(group)],
        axis=1,
    )
    head_hidden = jax.nn.silu(head_pre).astype(jnp.bfloat16)
    forecast = jnp.stack(
        [
            (
                jnp.dot(
                    head_hidden, head_whole[part][:, two:], preferred_element_type=jnp.float32
                )
                + emit_offsets[part]
                + inner_parts[part][:, group_width:]
            )
            * keep_column
            for part in range(group)
        ]
    ).astype(jnp.bfloat16)
    token_predictions = lax.all_to_all(
        forecast, "head", split_axis=0, concat_axis=0, tiled=True
    ).reshape(group * rows, group_width)
    grad_forecast = (sensitivity.astype(jnp.float32) * keep_column).astype(jnp.bfloat16)
    grad_hidden = sum(
        reverse_matmul_answer(grad_forecast[part], head_whole[part][:, two:])
        for part in range(group)
    )
    unused_head, head_pull = jax.vjp(jax.nn.silu, head_pre)
    grad_head_pre = head_pull(grad_hidden)[0].astype(jnp.bfloat16)
    grad_resid = sum(
        reverse_matmul_answer(
            jnp.concatenate(
                [
                    grad_head_pre[:, part * group_width : (part + 1) * group_width],
                    grad_forecast[part],
                ],
                axis=1,
            ),
            head_whole[part][:, :two],
        )
        for part in range(group)
    )
    grad_forecast_rows = jnp.concatenate([grad_forecast[part] for part in range(group)], axis=1)
    head_bias_rows = (
        jnp.sum(grad_head_pre.astype(jnp.float32), axis=0),
        jnp.sum(grad_forecast_rows.astype(jnp.float32), axis=0),
    )
    head_sums, first, last = column_sums(
        me,
        [
            (top, grad_head_pre),
            (top, grad_forecast_rows),
            (head_hidden, grad_forecast_rows),
        ],
    )

    ahead = [(), first]
    lasts = [last]
    layer_sums = [None] * layer_count
    gain_sums = [None] * layer_count
    for layer_index in reversed(range(layer_count)):
        layer = layers[layer_index]
        grad_resid = after(grad_resid, *ahead[-2])
        grad_middle, grad_mixed, left_rows, right_rows, gain_second = layer.rest_backward(grad_resid)
        pairs = list(zip(left_rows, right_rows, strict=True))
        rest, first, last = weight_sums(me, pairs)
        ahead.append((*lasts[-1], *first))
        lasts.append(last)
        grad_mixed = after(grad_mixed, *ahead[-2])
        grad_resid, left, right, gain_first = layer.entry_backward(grad_middle, grad_mixed)
        entry, first, last = weight_sums(me, [(left, right)])
        ahead.append((*lasts[-1], *first))
        lasts.append(last)
        layer_sums[layer_index] = (entry[0], rest[0], rest[1], rest[2])
        gain_sums[layer_index] = (gain_first, gain_second)
    grad_resid = after(grad_resid, *ahead[-2])
    grad_entry = grad_resid.astype(jnp.bfloat16)
    grad_entry_outer = dyadic_accumulation(entry_hidden, grad_entry)
    grad_entry_outer_bias = jnp.sum(grad_entry.astype(jnp.float32), axis=0)
    grad_entry_skip = dyadic_accumulation(features, grad_entry)
    unused_entry, entry_pull = jax.vjp(jax.nn.silu, entry_pre)
    grad_entry_pre = entry_pull(reverse_matmul_answer(grad_entry, intake_emit_matrix))[0].astype(
        jnp.bfloat16
    )
    grad_entry_inner = dyadic_accumulation(features, grad_entry_pre)
    grad_entry_inner_bias = jnp.sum(grad_entry_pre.astype(jnp.float32), axis=0)
    grad_features = reverse_matmul_answer(
        grad_entry_pre, intake_latent_matrix
    ) + reverse_matmul_answer(grad_entry, intake_shortcut_matrix)
    values_grad = jnp.where(pad_mask, 0.0, grad_features[:, :patch_len])
    extra_rows = jnp.concatenate(
        [
            grad_entry_inner,
            grad_entry_skip,
            grad_entry_inner_bias[None],
            grad_entry_outer_bias[None],
        ]
        + [row[None] for row in head_bias_rows]
        + [row[None] for pair in gain_sums for row in pair],
        axis=0,
    )
    entry_main, entry_extra = sum_everywhere(me, grad_entry_outer, extra_rows)
    inner_rows = 2 * patch_len
    last = 2 * inner_rows
    entry_sums = (
        entry_extra[:inner_rows],
        entry_extra[last],
        entry_main,
        entry_extra[last + 1],
        entry_extra[inner_rows:last],
    )
    head_bias_sums = lax.dynamic_slice_in_dim(
        entry_extra[last + 2 : last + 4], group_place * group_width, group_width, 1
    )
    own_place = (me * group + group_place) * own_count
    gains_grad = lax.dynamic_slice_in_dim(
        entry_extra[last + 4 : last + 4 + 2 * layer_count], own_place, own_count, 1
    ).reshape(layer_count, 2, own_count)
    qkv_grad = jnp.stack([layer_sums[member][0] for member in range(layer_count)])
    out_grad = jnp.stack([layer_sums[member][1] for member in range(layer_count)])
    up_grad = jnp.stack([layer_sums[member][2] for member in range(layer_count)])
    down_grad = jnp.stack([layer_sums[member][3] for member in range(layer_count)])
    return (
        token_predictions,
        values_grad,
        entry_sums[0],
        entry_sums[1],
        entry_sums[2],
        entry_sums[3],
        entry_sums[4],
        qkv_grad,
        out_grad,
        up_grad,
        down_grad,
        gains_grad,
        head_sums[0],
        head_bias_sums[0],
        head_sums[2],
        head_bias_sums[1],
        head_sums[1],
    )


def solution(mesh):
    return jax.shard_map(
        body,
        mesh=mesh,
        in_specs=(
            P(("dp", "head"), None),
            P(("dp", "head"), None),
            P(("dp", "head"), None),
            P(),
            P(),
            P(),
            P(),
            P(),
            P(None, ("dp", "head"), None),
            P(None, ("dp", "head"), None),
            P(None, ("dp", "head"), None),
            P(None, ("dp", "head"), None),
            P(None, None, ("dp", "head")),
            P(None, "head"),
            P("head"),
            P(None, "head"),
            P("head"),
            P(None, "head"),
            P("dp", "head"),
        ),
        out_specs=(
            P("dp", "head"),
            P(("dp", "head"), None),
            P(),
            P(),
            P(),
            P(),
            P(),
            P(None, ("dp", "head"), None),
            P(None, ("dp", "head"), None),
            P(None, ("dp", "head"), None),
            P(None, ("dp", "head"), None),
            P(None, None, ("dp", "head")),
            P(None, "head"),
            P("head"),
            P(None, "head"),
            P("head"),
            P(None, "head"),
        ),
        check_vma=False,
    )
```

```python
from functools import partial
import math

import jax
import jax.numpy as jnp
from jax import lax
from jax.experimental import pallas as pl
from jax.experimental.pallas import tpu as pltpu
from jax.sharding import PartitionSpec as P

MODEL_WIDTH = 1280
HEADS = 16
HEAD_DIM = 80


EPS = 1e-06
ROPE_BASE = 10000.0


def layout_rows(series_row, pad_row, patch_len):
    count = series_row.shape[0]
    order = jnp.arange(count, dtype=jnp.int32)
    same_series = series_row[:, None] == series_row[None, :]
    earlier = order[None, :] < order[:, None]
    position = jnp.sum(jnp.logical_and(same_series, earlier).astype(jnp.int32), axis=1)
    numbers = jnp.arange(pad_row.shape[0], dtype=jnp.int32)
    series_pad = jnp.sum(
        jnp.where(series_row[:, None] == numbers[None, :], pad_row[None, :], 0), axis=1
    )
    pad_count = jnp.where(position == 0, series_pad, 0)
    padded = pad_count == patch_len
    diagonal = order[:, None] == order[None, :]
    reach = jnp.logical_or(jnp.logical_and(earlier, jnp.logical_not(padded)[None, :]), diagonal)
    allowed = jnp.logical_and(same_series, reach)
    keep_rows = jnp.where(padded, 0.0, 1.0).astype(jnp.float32)
    return (position, pad_count, allowed, keep_rows)


def rotary_tables(position, head_dim):
    half = head_dim // 2
    steps = jnp.arange(half, dtype=jnp.float32) / half
    inverse = jnp.exp(-math.log(ROPE_BASE) * steps)
    angles = position.astype(jnp.float32)[:, None] * inverse[None, :]
    return (jnp.cos(angles)[:, None, :], jnp.sin(angles)[:, None, :])


def rotate(heads_rows, cosine, sine):
    half = heads_rows.shape[-1] // 2
    first = heads_rows[..., :half]
    second = heads_rows[..., half:]
    return jnp.concatenate(
        [first * cosine - second * sine, second * cosine + first * sine], axis=-1
    )


def unrotate(grad_rows, cosine, sine):
    half = grad_rows.shape[-1] // 2
    first = grad_rows[..., :half]
    second = grad_rows[..., half:]
    return jnp.concatenate(
        [first * cosine + second * sine, second * cosine - first * sine], axis=-1
    )


def norm_apply(resid, gain):
    return resid * lax.rsqrt(jnp.mean(resid * resid, axis=-1, keepdims=True) + EPS) * gain


def dyadic_accumulation(left, right):
    return lax.dot_general(
        left, right, (((0,), (0,)), ((), ())), preferred_element_type=jnp.float32
    )


def reverse_matmul_answer(grad_rows, weight):
    return lax.dot_general(
        grad_rows, weight, (((1,), (1,)), ((), ())), preferred_element_type=jnp.float32
    )


def masked_scores(query_rows, key_rows, allowed):
    scale = 1.0 / math.sqrt(query_rows.shape[-1])
    scores = (
        jnp.einsum("qhd,khd->hqk", query_rows, key_rows, preferred_element_type=jnp.float32) * scale
    )
    return jnp.where(allowed[None], scores, -1e30)


def attend_forward(query_rows, key_rows, value_rows, allowed):
    scores = masked_scores(query_rows, key_rows, allowed)
    peak = jnp.max(scores, axis=-1, keepdims=True)
    weights = jnp.exp(scores - peak)
    total = jnp.sum(weights, axis=-1, keepdims=True)
    probs = (weights / total).astype(jnp.bfloat16)
    mixed = jnp.einsum("hqk,khd->qhd", probs, value_rows, preferred_element_type=jnp.float32)
    return (mixed, peak + jnp.log(total))


def attend_backward(query_rows, key_rows, value_rows, allowed, log_total, grad_mixed):
    scale = 1.0 / math.sqrt(query_rows.shape[-1])
    scores = masked_scores(query_rows, key_rows, allowed)
    probs = jnp.where(allowed[None], jnp.exp(scores - log_total), 0.0)
    grad_probs = jnp.einsum(
        "qhd,khd->hqk", grad_mixed, value_rows, preferred_element_type=jnp.float32
    )
    grad_values = jnp.einsum(
        "hqk,qhd->khd", probs.astype(jnp.bfloat16), grad_mixed, preferred_element_type=jnp.float32
    )
    center = jnp.sum(grad_probs * probs, axis=-1, keepdims=True)
    grad_scores = (probs * (grad_probs - center)).astype(jnp.bfloat16)
    grad_query = (
        jnp.einsum("hqk,khd->qhd", grad_scores, key_rows, preferred_element_type=jnp.float32)
        * scale
    )
    grad_keys = (
        jnp.einsum("hqk,qhd->khd", grad_scores, query_rows, preferred_element_type=jnp.float32)
        * scale
    )
    return (grad_query, grad_keys, grad_values)


def after(value, *earlier):
    return lax.optimization_barrier((value, *earlier))[0]


def swap(v, bit):
    size = lax.axis_size("dp")
    return lax.ppermute(v, "dp", [(i, i ^ (1 << bit)) for i in range(size)])


def swap_in_turn(parts, bit, *earlier):
    met = []
    for part in parts:
        met.append(swap(after(part, *earlier), bit))
        earlier = (met[-1],)
    return met


def outer_groups():
    size = lax.axis_size("dp")
    return [[j + 8 * o for o in range(size // 8)] for j in range(8)]


def place_kernel(plan, piece_count, out_count, me_ref, *refs):
    pieces = refs[:piece_count]
    outs = refs[piece_count : piece_count + out_count]
    held = refs[piece_count + out_count : piece_count + 2 * out_count]
    in_sems, out_sems = refs[piece_count + 2 * out_count :]
    inward, outward = [], []
    for n, (piece, rel, row, out, column) in enumerate(plan):
        source = pieces[piece]
        width = held[out].shape[-1]
        if width != source.shape[-1]:
            source = source.at[:, :, pl.ds(column, width)]
        spot = (slice(None), me_ref[0] ^ rel, pl.ds(row, source.shape[1]), slice(None))
        inward.append(pltpu.make_async_copy(source, held[out].at[spot], in_sems.at[n]))
        outward.append(
            pltpu.make_async_copy(held[out].at[spot], outs[out].at[spot], out_sems.at[n])
        )
    for copy in inward:
        copy.start()
    for copy, onward in zip(inward, outward):
        copy.wait()
        onward.start()
    for onward in outward:
        onward.wait()


def place(me, pieces, widths, first=0):
    plan = []
    for n, (rel, row, _) in enumerate(pieces):
        column = first
        for out, width in enumerate(widths):
            plan.append((n, rel, row, out, column))
            column += width
    arrays = [array for _, _, array in pieces]
    lead, rows, _ = arrays[0].shape
    kind = arrays[0].dtype
    total = sum(8 * lead * rows * -(-w // 128) * 128 for w in widths) * 2
    outs = pl.pallas_call(
        partial(place_kernel, plan, len(arrays), len(widths)),
        out_shape=[jax.ShapeDtypeStruct((lead, 8, rows, w), kind) for w in widths],
        in_specs=[pl.BlockSpec(memory_space=pltpu.SMEM)]
        + [pl.BlockSpec(memory_space=pl.ANY)] * len(arrays),
        out_specs=[pl.BlockSpec(memory_space=pl.ANY)] * len(widths),
        scratch_shapes=[pltpu.VMEM((lead, 8, rows, w), kind) for w in widths]
        + [pltpu.SemaphoreType.DMA((len(plan),))] * 2,
        compiler_params=pltpu.CompilerParams(vmem_limit_bytes=total + (4 << 20)),
        cost_estimate=pl.CostEstimate(flops=0, bytes_accessed=2 * total, transcendentals=0),
    )(me, *arrays)
    outer = lax.axis_size("dp") // 8
    return [o.reshape(-1, outer * 8 * rows, o.shape[-1]) for o in outs]


def row_half(rows):
    return rows // 32 * 16 if rows >= 32 else rows // 2


def second_step(held, from_x, from_y):
    half = row_half(held.shape[1])
    return from_y[:, :half], from_x[:, half:]


def all_pieces(near, far, near_met, far_met):
    half = far[0].shape[1]
    places = ((0, 0), (2, 0), (4, 0), (6, 0), (6, half))
    pieces = []
    for (rel, row), array, met in zip(places, (*near, *far), (*near_met, *far_met), strict=True):
        pieces += [(rel, row, array), (rel | 1, row, met)]
    return pieces


def spread_rows(held):
    near = (held, swap(held, 1), swap(held, 2))
    onward_x, onward_y = second_step(*near)
    far = (swap(onward_x, 1), swap(onward_y, 2))
    return all_pieces(near, far, [swap(part, 0) for part in near], [swap(part, 0) for part in far])


def gather_head(own):
    held = lax.all_gather(own, "head", axis=0, tiled=True)[None]
    if lax.axis_size("dp") > 8:
        held = lax.all_gather(
            held, "dp", axis=0, tiled=True, axis_index_groups=outer_groups()
        )
    return held


def pick(rows, place, width):
    picked = rows[:, :width]
    for n in range(1, rows.shape[1] // width):
        picked = jnp.where(place == n, rows[:, n * width : (n + 1) * width], picked)
    return picked


def product_kernel(count, outer, me_ref, *refs):
    lefts, rights, met_lefts, met_rights = (refs[n * count : (n + 1) * count] for n in range(4))
    to_x, to_y, later, own = refs[4 * count :]
    rows, width = own.shape[1] // outer, own.shape[-1]
    half = width // 2
    for n in range(count):
        left, met = lefts[n][...], met_lefts[n][...]
        for rel in range(4):
            place = me_ref[0] ^ (2 * rel)
            for part in range(outer):
                near_left = pick(left[:, part * 8 * rows : (part + 1) * 8 * rows], place, rows)
                met_left = pick(met[:, part * 8 * rows : (part + 1) * 8 * rows], place, rows)
                span = slice(part * rows, (part + 1) * rows)
                for side in range(2):
                    columns = slice(side * half, (side + 1) * half)
                    total = dyadic_accumulation(near_left, rights[n][:, columns])
                    total += dyadic_accumulation(met_left, met_rights[n][:, columns])
                    total = total.astype(own.dtype)
                    if rel == 0:
                        own[n, span, columns] = total
                    elif rel == 1 and side == 0:
                        to_x[1, n, span] = total
                    elif rel == 1:
                        later[1, n, span] = total
                    elif rel == 2 and side == 0:
                        later[0, n, span] = total
                    elif rel == 2:
                        to_y[1, n, span] = total
                    elif side == 0:
                        to_x[0, n, span] = total
                    else:
                        to_y[0, n, span] = total


def pair_products(me, pairs):
    outer = lax.axis_size("dp") // 8
    met = {}
    earlier = ()
    for rows in [left for left, _ in pairs] + [right for _, right in pairs]:
        if id(rows) not in met:
            met[id(rows)] = swap(after(rows, *earlier), 0)
            earlier = (met[id(rows)],)
    lefts = [left for left, _ in pairs]
    rights = [right for _, right in pairs]
    count = len(pairs)
    block, width = lefts[0].shape[1] // 8, rights[0].shape[1]
    low = jnp.bfloat16
    return pl.pallas_call(
        partial(product_kernel, count, outer),
        out_shape=[
            jax.ShapeDtypeStruct((2, count, block, width // 2), low),
            jax.ShapeDtypeStruct((2, count, block, width // 2), low),
            jax.ShapeDtypeStruct((2, count, block, width // 2), low),
            jax.ShapeDtypeStruct((count, block, width), low),
        ],
        in_specs=[pl.BlockSpec(memory_space=pltpu.SMEM)]
        + [pl.BlockSpec(memory_space=pltpu.VMEM)] * (4 * count),
        out_specs=[pl.BlockSpec(memory_space=pltpu.VMEM)] * 4,
        compiler_params=pltpu.CompilerParams(vmem_limit_bytes=40 << 20),
        cost_estimate=pl.CostEstimate(
            flops=2 * 256 * 4 * block * width * count,
            bytes_accessed=2 * count * (4 * block * width + 256 * width + 256 * 4 * block),
            transcendentals=0,
        ),
    )(
        (me & 7).reshape(1),
        *lefts,
        *rights,
        *[met[id(left)] for left in lefts],
        *[met[id(right)] for right in rights],
    )


def low_sum(*parts):
    total = parts[0].astype(jnp.float32)
    for part in parts[1:]:
        total = total + part.astype(jnp.float32)
    return total.astype(jnp.bfloat16)


class RowSums:
    def __init__(self, to_x, to_y, later, own):
        self.sent, self.later, self.own = (to_x, to_y), later, own

    def first(self):
        return swap(self.sent[0], 1), swap(self.sent[1], 2)

    def last(self):
        return (
            swap(low_sum(self.later[0], self.met[0][0]), 2),
            swap(low_sum(self.later[1], self.met[1][0]), 1),
        )

    def total(self):
        half = self.own.shape[-1] // 2
        return jnp.concatenate(
            [
                low_sum(self.own[..., :half], self.met[0][1], self.last_met[0]),
                low_sum(self.own[..., half:], self.met[1][1], self.last_met[1]),
            ],
            axis=-1,
        )


def sum_group(total):
    outer = lax.axis_size("dp") // 8
    group = lax.axis_size("head")
    lead = total.shape[:-2]
    rows, columns = total.shape[-2:]
    if outer > 1:
        total = lax.psum_scatter(
            total.reshape(*lead, outer, rows // outer, columns),
            "dp",
            scatter_dimension=len(lead),
            tiled=True,
            axis_index_groups=outer_groups(),
        )
    total = total.reshape(*lead, rows // outer, columns)
    return lax.psum_scatter(total, "head", scatter_dimension=len(lead), tiled=True)


def sum_columns(total):
    group = lax.axis_size("head")
    count, rows, columns = total.shape
    total = jnp.moveaxis(total.reshape(count, rows, group, columns // group), 2, 0)
    return lax.psum_scatter(total, "head", scatter_dimension=0, tiled=True)[0]


def gather_blocks(me, summed):
    outer = lax.axis_size("dp") // 8
    count, rows, columns = summed.shape
    held = summed.reshape(count * outer, rows // outer, columns)
    return place((me & 7).reshape(1), spread_rows(held), [columns])[0]


EXTRA_ROWS = 8


def entry_products(me, main, extra):
    group = lax.axis_size("head")
    outer = lax.axis_size("dp") // 8
    devices = 8 * outer * group
    columns = main.shape[1]
    own = main.shape[0] // devices
    extra = jnp.pad(extra, ((0, EXTRA_ROWS * devices - extra.shape[0]), (0, 0)))
    rows = jnp.concatenate(
        [main.reshape(devices, own, columns), extra.reshape(devices, EXTRA_ROWS, columns)], axis=1
    ).astype(jnp.bfloat16)
    view = rows.reshape(outer, 4, 2, group * (own + EXTRA_ROWS), columns)
    core = me & 1
    other = lax.dynamic_index_in_dim(view, 1 - core, 2, keepdims=False)
    pair = low_sum(lax.dynamic_index_in_dim(view, core, 2, keepdims=False), swap(other, 0))
    chip = (me & 7) >> 1
    half = columns // 2

    def picked(rel):
        return lax.dynamic_index_in_dim(pair, chip ^ rel, 1, keepdims=False).reshape(-1, columns)

    own_rows, at_x, at_y, far = (picked(rel) for rel in range(4))
    return RowSums(
        jnp.stack([far[:, :half], at_x[:, :half]]),
        jnp.stack([far[:, half:], at_y[:, half:]]),
        (at_y[:, :half], at_x[:, half:]),
        own_rows,
    )


def entry_everywhere(me, summed, own, count):
    columns = summed.shape[1]
    (whole,) = place((me & 7).reshape(1), spread_rows(gather_head(summed)), [columns])
    whole = whole.reshape(-1, own + EXTRA_ROWS, columns).astype(jnp.float32)
    return whole[:, :own].reshape(-1, columns), whole[:, own:].reshape(-1, columns)[:count]


def fetch(plan, me, pieces, whole, sems):
    groups = []
    for group in range(whole.shape[1] // MODEL_WIDTH):
        columns = pl.ds(group * MODEL_WIDTH, MODEL_WIDTH)
        copies = []
        for n, (rel, row, rows) in enumerate(plan):
            first = pl.multiple_of((me ^ rel) * (whole.shape[0] // 8) + row, 16)
            copies.append(
                pltpu.make_async_copy(
                    pieces[n].at[0, :, columns],
                    whole.at[pl.ds(first, rows), columns],
                    sems.at[group * len(plan) + n],
                )
            )
        for copy in copies:
            copy.start()
        groups.append(copies)
    return groups


def arrive(copies):
    for copy in copies:
        copy.wait()


def rows_times(left, whole, first, out, tile):
    def step(n, _):
        at = pl.multiple_of(n * tile, 128)
        out[:, pl.ds(at, tile)] = jnp.dot(
            left, whole[:, pl.ds(first + at, tile)], preferred_element_type=jnp.float32
        )
        return 0

    lax.fori_loop(0, out.shape[1] // tile, step, 0)


def rows_times_turned(left, whole, first, width, out, tile):
    def step(n, _):
        at = pl.multiple_of(n * tile, 128)
        part = reverse_matmul_answer(whole[pl.ds(at, tile), pl.ds(first, width)], left)
        out[:, pl.ds(at, tile)] = part.T
        return 0

    lax.fori_loop(0, out.shape[1] // tile, step, 0)


def inverse_norm(rows):
    return lax.rsqrt(jnp.mean(rows * rows, axis=-1, keepdims=True) + EPS)


def other_half(rows):
    half = HEAD_DIM // 2
    lane = lax.broadcasted_iota(jnp.int32, rows.shape, 1) % HEAD_DIM
    ahead = pltpu.roll(rows, rows.shape[1] - half, 1)
    behind = pltpu.roll(rows, half, 1)
    return jnp.where(lane < half, ahead, behind)


def head_window(head, width):
    first = head * HEAD_DIM // 128 * 128
    last = min(-(-(head + 1) * HEAD_DIM // 128) * 128, width)
    start = head * HEAD_DIM - first
    lane = lax.broadcasted_iota(jnp.int32, (1, last - first), 1)
    return slice(first, last), jnp.logical_and(lane >= start, lane < start + HEAD_DIM)


def entry_forward_kernel(plan, me_ref, resid_ref, gain_ref, cosine_ref, sine_ref, allowed_ref, *refs):
    pieces = refs[: len(plan)]
    normed_ref, query_ref, key_ref, value_ref, total_ref, mixed_ref = refs[len(plan) : len(plan) + 6]
    whole, wide, sems = refs[len(plan) + 6 :]
    groups = fetch(plan, me_ref[0], pieces, whole, sems)
    resid = resid_ref[...]
    normed = (resid * inverse_norm(resid) * gain_ref[...]).astype(jnp.bfloat16)
    normed_ref[...] = normed
    for group, out in enumerate((query_ref, key_ref, value_ref)):
        arrive(groups[group])
        rows_times(normed, whole, group * MODEL_WIDTH, wide, 256)
        rows = wide[...]
        if group < 2:
            rows = rows * cosine_ref[...] + other_half(rows) * sine_ref[...]
        out[...] = rows.astype(jnp.bfloat16)
    scale = 1.0 / math.sqrt(HEAD_DIM)
    allowed = allowed_ref[...] > 0.0
    wide[...] = jnp.zeros_like(wide)
    totals = jnp.zeros(total_ref.shape, jnp.float32)
    head_lane = lax.broadcasted_iota(jnp.int32, total_ref.shape, 1)
    for head in range(HEADS):
        window, inside = head_window(head, MODEL_WIDTH)
        query = jnp.where(inside, query_ref[:, window], 0)
        scores = reverse_matmul_answer(query, key_ref[:, window]) * scale
        scores = jnp.where(allowed, scores, -1e30)
        peak = jnp.max(scores, axis=-1, keepdims=True)
        weights = jnp.exp(scores - peak)
        total = jnp.sum(weights, axis=-1, keepdims=True)
        probs = (weights / total).astype(jnp.bfloat16)
        mixed = jnp.dot(probs, value_ref[:, window], preferred_element_type=jnp.float32)
        wide[:, window] += jnp.where(inside, mixed, 0.0)
        totals = jnp.where(head_lane == head, peak + jnp.log(total), totals)
    total_ref[...] = totals
    mixed_ref[...] = wide[...].astype(jnp.bfloat16)


def gelu_parts(x):
    root = math.sqrt(2.0 / math.pi)
    bend = jnp.tanh(root * (x + 0.044715 * (x * x * x)))
    slope = 0.5 * (1.0 + bend) + 0.5 * x * (1.0 - bend * bend) * root * (
        1.0 + 3.0 * 0.044715 * (x * x)
    )
    return 0.5 * x * (1.0 + bend), slope


def rest_forward_kernel(plan, me_ref, resid_ref, mixed_ref, gain_ref, *refs):
    pieces = refs[: len(plan)]
    result_ref, middle_ref, normed_ref, pre_ref = refs[len(plan) : len(plan) + 4]
    whole, sems = refs[len(plan) + 4 :]
    groups = fetch(plan, me_ref[0], pieces, whole, sems)
    arrive(groups[0])
    rows_times(mixed_ref[...], whole, 0, middle_ref, 256)
    middle = resid_ref[...] + middle_ref[...]
    middle_ref[...] = middle
    normed = (middle * inverse_norm(middle) * gain_ref[...]).astype(jnp.bfloat16)
    normed_ref[...] = normed
    arrive(groups[1])
    rows_times(normed, whole, MODEL_WIDTH, pre_ref, 256)
    act = gelu_parts(pre_ref[...])[0].astype(jnp.bfloat16)
    arrive(groups[2])
    rows_times(act, whole, 2 * MODEL_WIDTH, result_ref, 256)
    result_ref[...] += middle_ref[...]


def norm_back(rows, gain, grad):
    inverse = inverse_norm(rows)
    scaled = grad * gain
    mean = jnp.mean(rows * scaled, axis=-1, keepdims=True)
    sent = inverse * scaled - rows * (inverse * inverse * inverse * mean)
    return sent, jnp.sum(grad * rows * inverse, axis=0, keepdims=True)


def rest_backward_kernel(plan, me_ref, grad_ref, middle_ref, pre_ref, gain_ref, *refs):
    pieces = refs[: len(plan)]
    outs = refs[len(plan) : len(plan) + 7]
    grad_middle_ref, mixed_ref, attn_ref, grad_pre_ref, branch_ref, act_ref, gain_grad_ref = outs
    whole, wide, sems = refs[len(plan) + 7 :]
    groups = fetch(plan, me_ref[0], pieces, whole, sems)
    grad = grad_ref[...]
    branch = grad.astype(jnp.bfloat16)
    branch_ref[...] = branch
    arrive(groups[2])
    rows_times_turned(branch, whole, 2 * MODEL_WIDTH, MODEL_WIDTH, wide, 256)
    act, slope = gelu_parts(pre_ref[...])
    act_ref[...] = act.astype(jnp.bfloat16)
    grad_pre = (wide[...] * slope).astype(jnp.bfloat16)
    grad_pre_ref[...] = grad_pre
    arrive(groups[1])
    rows_times_turned(grad_pre, whole, MODEL_WIDTH, MODEL_WIDTH, wide, 256)
    sent, gain_grad_ref[...] = norm_back(middle_ref[...], gain_ref[...], wide[...])
    grad_middle = grad + sent
    grad_middle_ref[...] = grad_middle
    attn = grad_middle.astype(jnp.bfloat16)
    attn_ref[...] = attn
    arrive(groups[0])
    rows_times_turned(attn, whole, 0, MODEL_WIDTH, wide, 256)
    mixed_ref[...] = wide[...].astype(jnp.bfloat16)


def entry_backward_kernel(
    plan,
    me_ref,
    grad_middle_ref,
    grad_mixed_ref,
    resid_ref,
    query_ref,
    key_ref,
    value_ref,
    total_ref,
    gain_ref,
    cosine_ref,
    sine_ref,
    allowed_ref,
    *refs,
):
    pieces = refs[: len(plan)]
    grad_resid_ref, projected_ref, gain_grad_ref = refs[len(plan) : len(plan) + 3]
    whole, grad_query, grad_key, grad_value, sems = refs[len(plan) + 3 :]
    groups = fetch(plan, me_ref[0], pieces, whole, sems)
    scale = 1.0 / math.sqrt(HEAD_DIM)
    allowed = allowed_ref[...] > 0.0
    totals = total_ref[...]
    grad_query[...] = jnp.zeros_like(grad_query)
    grad_key[...] = jnp.zeros_like(grad_key)
    grad_value[...] = jnp.zeros_like(grad_value)
    for head in range(HEADS):
        window, inside = head_window(head, MODEL_WIDTH)
        query = jnp.where(inside, query_ref[:, window], 0)
        keys = key_ref[:, window]
        grad_mixed = jnp.where(inside, grad_mixed_ref[:, window], 0)
        scores = reverse_matmul_answer(query, keys) * scale
        probs = jnp.where(allowed, jnp.exp(scores - totals[:, head : head + 1]), 0.0)
        grad_probs = reverse_matmul_answer(grad_mixed, value_ref[:, window])
        grad_value[:, window] += dyadic_accumulation(probs.astype(jnp.bfloat16), grad_mixed)
        center = jnp.sum(grad_probs * probs, axis=-1, keepdims=True)
        grad_scores = (probs * (grad_probs - center)).astype(jnp.bfloat16)
        along = jnp.dot(grad_scores, keys, preferred_element_type=jnp.float32)
        grad_query[:, window] += jnp.where(inside, along * scale, 0.0)
        grad_key[:, window] += dyadic_accumulation(grad_scores, query) * scale
    for group, part in enumerate((grad_query, grad_key, grad_value)):
        rows = part[...]
        if group < 2:
            rows = rows * cosine_ref[...] - other_half(rows) * sine_ref[...]
        projected_ref[:, group * MODEL_WIDTH : (group + 1) * MODEL_WIDTH] = rows.astype(jnp.bfloat16)
    for copies in groups:
        arrive(copies)
    rows_times_turned(projected_ref[...], whole, 0, 3 * MODEL_WIDTH, grad_query, 256)
    sent, gain_grad_ref[...] = norm_back(resid_ref[...], gain_ref[...], grad_query[...])
    grad_resid_ref[...] = grad_middle_ref[...] + sent


def whole_call(kernel, me, pieces, inputs, outs, wides, flops):
    rows = inputs[0].shape[0]
    plan = [(rel, row, array.shape[1]) for rel, row, array in pieces]
    blocks = 8 * pieces[0][2].shape[1]
    columns = 3 * MODEL_WIDTH
    vmem = pl.BlockSpec(memory_space=pltpu.VMEM)
    return pl.pallas_call(
        partial(kernel, plan),
        out_shape=[jax.ShapeDtypeStruct(shape, kind) for shape, kind in outs],
        in_specs=[pl.BlockSpec(memory_space=pltpu.SMEM)]
        + [vmem] * len(inputs)
        + [pl.BlockSpec(memory_space=pl.ANY)] * len(pieces),
        out_specs=[vmem] * len(outs),
        scratch_shapes=[pltpu.VMEM((blocks, columns), jnp.bfloat16)]
        + [pltpu.VMEM((rows, MODEL_WIDTH), jnp.float32)] * wides
        + [pltpu.SemaphoreType.DMA((3 * len(pieces),))],
        compiler_params=pltpu.CompilerParams(vmem_limit_bytes=44 << 20),
        cost_estimate=pl.CostEstimate(
            flops=flops, bytes_accessed=2 * blocks * columns, transcendentals=0
        ),
    )(me, *inputs, *[array for _, _, array in pieces])


def in_kernel(pieces):
    lead, rows, _ = pieces[0][2].shape
    return lead == 1 and rows % 32 == 0


LOW, FULL = jnp.bfloat16, jnp.float32


class Layer:
    def __init__(self, places, entry_pieces, gains, tables, allowed):
        self.places, self.entry_pieces, self.gains = places, entry_pieces, gains
        self.tables, self.allowed = tables, allowed
        self.fetched = in_kernel(entry_pieces)
        if not self.fetched:
            self.entry_whole = place(places, entry_pieces, [3 * MODEL_WIDTH])[0][0]

    def add_rest(self, rest_pieces):
        self.rest_pieces = rest_pieces
        if not self.fetched:
            self.rest_whole = [part[0] for part in place(self.places, rest_pieces, [MODEL_WIDTH] * 3)]

    def shapes(self, *kinds):
        rows = self.allowed.shape[0]
        return [((rows, width), kind) for width, kind in kinds]

    def entry_forward(self, resid):
        if not self.fetched:
            self.saved = entry_forward(
                resid, self.entry_whole, self.gains, *self.tables[:2], self.allowed
            )
            return self.saved[6]
        wide = (MODEL_WIDTH, LOW)
        self.resid = resid
        outs = whole_call(
            entry_forward_kernel,
            self.places,
            self.entry_pieces,
            (resid, self.gains[:1].astype(FULL), *self.tables[2:], self.allowed.astype(FULL)),
            self.shapes(wide, wide, wide, wide, (128, FULL), wide),
            1,
            2 * resid.shape[0] * 3 * MODEL_WIDTH * MODEL_WIDTH,
        )
        self.normed_first, self.heads = outs[0], outs[1:5]
        return outs[5]

    def rest_forward(self, mixed):
        if not self.fetched:
            result, self.saved = rest_forward(
                (*self.saved[:6], mixed), *self.rest_whole, self.gains
            )
            return result
        self.mixed = mixed
        result, self.middle, self.normed_second, self.hidden_pre = whole_call(
            rest_forward_kernel,
            self.places,
            self.rest_pieces,
            (self.resid, mixed, self.gains[1:].astype(FULL)),
            self.shapes(
                (MODEL_WIDTH, FULL), (MODEL_WIDTH, FULL), (MODEL_WIDTH, LOW), (MODEL_WIDTH, FULL)
            ),
            0,
            2 * mixed.shape[0] * 3 * MODEL_WIDTH * MODEL_WIDTH,
        )
        return result

    def rest_backward(self, grad):
        if not self.fetched:
            weights = (self.entry_whole, *self.rest_whole, self.gains)
            return rest_backward(self.saved, weights, grad)
        wide = (MODEL_WIDTH, LOW)
        grad_middle, grad_mixed, grad_attn, grad_pre, branch, act, gain_grad = whole_call(
            rest_backward_kernel,
            self.places,
            self.rest_pieces,
            (grad, self.middle, self.hidden_pre, self.gains[1:].astype(FULL)),
            self.shapes((MODEL_WIDTH, FULL), wide, wide, wide, wide, wide)
            + [((1, MODEL_WIDTH), FULL)],
            1,
            2 * grad.shape[0] * 3 * MODEL_WIDTH * MODEL_WIDTH,
        )
        lefts = (self.mixed, self.normed_second, act)
        return grad_middle, grad_mixed, lefts, (grad_attn, grad_pre, branch), gain_grad[0]

    def entry_backward(self, grad_middle, grad_mixed):
        if not self.fetched:
            weights = (self.entry_whole, *self.rest_whole, self.gains)
            return entry_backward(
                self.saved, weights, *self.tables[:2], self.allowed, grad_middle, grad_mixed
            )
        grad_resid, projected, gain_grad = whole_call(
            entry_backward_kernel,
            self.places,
            self.entry_pieces,
            (
                grad_middle,
                grad_mixed,
                self.resid,
                *self.heads,
                self.gains[:1].astype(FULL),
                *self.tables[2:],
                self.allowed.astype(FULL),
            ),
            self.shapes((MODEL_WIDTH, FULL), (3 * MODEL_WIDTH, LOW)) + [((1, MODEL_WIDTH), FULL)],
            3,
            2 * grad_middle.shape[0] * 3 * MODEL_WIDTH * MODEL_WIDTH,
        )
        return grad_resid, self.normed_first, projected, gain_grad[0]


def entry_forward(resid, qkv_full, gain_pair, cosine, sine, allowed):
    gains = gain_pair.astype(jnp.float32)
    rows = resid.shape[0]
    normed_first = norm_apply(resid, gains[0]).astype(jnp.bfloat16)
    projected = jnp.dot(normed_first, qkv_full, preferred_element_type=jnp.float32)
    query_rows = rotate(
        projected[:, :MODEL_WIDTH].reshape(rows, HEADS, HEAD_DIM), cosine, sine
    ).astype(jnp.bfloat16)
    key_rows = rotate(
        projected[:, MODEL_WIDTH : 2 * MODEL_WIDTH].reshape(rows, HEADS, HEAD_DIM), cosine, sine
    ).astype(jnp.bfloat16)
    value_rows = projected[:, 2 * MODEL_WIDTH :].reshape(rows, HEADS, HEAD_DIM).astype(jnp.bfloat16)

    mixed, log_total = attend_forward(query_rows, key_rows, value_rows, allowed)
    mixed_low = mixed.reshape(rows, MODEL_WIDTH).astype(jnp.bfloat16)
    return (resid, normed_first, query_rows, key_rows, value_rows, log_total, mixed_low)


def rest_forward(saved, out_full, up_full, down_full, gain_pair):
    gains = gain_pair.astype(jnp.float32)
    resid, mixed_low = saved[0], saved[6]
    middle = resid + jnp.dot(mixed_low, out_full, preferred_element_type=jnp.float32)
    normed_second = norm_apply(middle, gains[1]).astype(jnp.bfloat16)
    hidden_pre = jnp.dot(normed_second, up_full, preferred_element_type=jnp.float32)
    hidden_act = jax.nn.gelu(hidden_pre, approximate=True).astype(jnp.bfloat16)
    result = middle + jnp.dot(hidden_act, down_full, preferred_element_type=jnp.float32)
    return (result, (*saved, middle, normed_second, hidden_pre))


def rest_backward(saved, weights, grad_result):
    mixed_low, middle, normed_second, hidden_pre = saved[6:]
    _, out_full, up_full, down_full, gain_pair = weights
    gains = gain_pair.astype(jnp.float32)
    grad_branch = grad_result.astype(jnp.bfloat16)
    hidden_act, gelu_pull = jax.vjp(partial(jax.nn.gelu, approximate=True), hidden_pre)
    hidden_low = hidden_act.astype(jnp.bfloat16)
    grad_act = reverse_matmul_answer(grad_branch, down_full)
    grad_pre = gelu_pull(grad_act)[0].astype(jnp.bfloat16)
    grad_normed_second = reverse_matmul_answer(grad_pre, up_full)
    unused_second, second_pull = jax.vjp(norm_apply, middle, gains[1])
    grad_middle_norm, grad_gain_second = second_pull(grad_normed_second)
    grad_middle = grad_result + grad_middle_norm
    grad_attn = grad_middle.astype(jnp.bfloat16)
    grad_mixed = reverse_matmul_answer(grad_attn, out_full).astype(jnp.bfloat16)
    left_rows = (mixed_low, normed_second, hidden_low)
    right_rows = (grad_attn, grad_pre, grad_branch)
    return (grad_middle, grad_mixed, left_rows, right_rows, grad_gain_second)


def entry_backward(saved, weights, cosine, sine, allowed, grad_middle, grad_mixed):
    resid, normed_first, query_rows, key_rows, value_rows, log_total = saved[:6]
    qkv_full = weights[0]
    gains = weights[4].astype(jnp.float32)
    rows = resid.shape[0]
    grad_query, grad_keys, grad_values = attend_backward(
        query_rows,
        key_rows,
        value_rows,
        allowed,
        log_total,
        grad_mixed.reshape(rows, HEADS, HEAD_DIM),
    )
    grad_query = unrotate(grad_query, cosine, sine).reshape(rows, MODEL_WIDTH)
    grad_keys = unrotate(grad_keys, cosine, sine).reshape(rows, MODEL_WIDTH)
    grad_values = grad_values.reshape(rows, MODEL_WIDTH)
    grad_projected = jnp.concatenate([grad_query, grad_keys, grad_values], axis=1).astype(
        jnp.bfloat16
    )
    grad_normed_first = reverse_matmul_answer(grad_projected, qkv_full)
    unused_first, first_pull = jax.vjp(norm_apply, resid, gains[0])
    grad_resid_norm, grad_gain_first = first_pull(grad_normed_first)
    return (grad_middle + grad_resid_norm, normed_first, grad_projected, grad_gain_first)


def body(
    patch_observations,
    sequence_labels,
    leading_filler_count,
    intake_latent_matrix,
    intake_latent_offset,
    intake_emit_matrix,
    intake_emit_offset,
    intake_shortcut_matrix,
    attention_entry_matrices,
    attention_merge_matrix,
    feedforward_widen_matrix,
    feedforward_shrink_matrix,
    layer_scale_factors,
    readout_latent_matrix,
    readout_latent_offset,
    readout_emit_matrix,
    readout_emit_offset,
    readout_shortcut_matrix,
    loss_sensitivity,
):
    patch_len = patch_observations.shape[1]
    position, pad_count, allowed, keep_rows = layout_rows(
        sequence_labels[0], leading_filler_count[0], patch_len
    )
    cosine, sine = rotary_tables(position, HEAD_DIM)
    columns = jnp.arange(patch_len, dtype=jnp.int32)
    pad_mask = columns[None, :] < pad_count[:, None]
    features = jnp.concatenate(
        [
            jnp.where(pad_mask, jnp.zeros_like(patch_observations), patch_observations),
            pad_mask.astype(jnp.bfloat16),
        ],
        axis=1,
    )
    entry_pre = (
        jnp.dot(features, intake_latent_matrix, preferred_element_type=jnp.float32)
        + intake_latent_offset
    )
    entry_hidden = jax.nn.silu(entry_pre).astype(jnp.bfloat16)
    resid = (
        jnp.dot(entry_hidden, intake_emit_matrix, preferred_element_type=jnp.float32)
        + intake_emit_offset
        + jnp.dot(features, intake_shortcut_matrix, preferred_element_type=jnp.float32)
    )
    layer_count = attention_entry_matrices.shape[0]
    group = lax.axis_size("head")
    group_place = lax.axis_index("head")
    outer = lax.axis_size("dp") // 8
    me = lax.axis_index("dp").astype(jnp.int32)
    places = (me & 7).reshape(1)
    own_count = layer_scale_factors.shape[2]
    rows = patch_observations.shape[0]

    group_width = readout_latent_offset.shape[0]
    offsets = jnp.stack([readout_latent_offset, readout_emit_offset])
    coarse = lax.reduce_precision(offsets, 8, 7)
    offset_rows = jnp.concatenate([coarse, offsets - coarse], axis=0).astype(jnp.bfloat16)
    offset_rows = jnp.pad(offset_rows, ((0, 12), (0, 0)))
    sent = jnp.concatenate(
        [
            loss_sensitivity.reshape(group, rows, group_width),
            jnp.broadcast_to(offset_rows[None], (group, 16, group_width)),
        ],
        axis=1,
    )
    gain_columns = layer_scale_factors.reshape(2 * layer_count, own_count).T
    gain_columns = jnp.pad(gain_columns, ((0, 0), (0, 128 - 2 * layer_count)))
    chunks = []
    for layer_index in range(layer_count):
        entry_own = attention_entry_matrices[layer_index]
        if layer_index == 0:
            entry_own = jnp.concatenate([entry_own, gain_columns], axis=1)
        chunks.append(entry_own)
        rest_own = jnp.concatenate(
            [
                attention_merge_matrix[layer_index],
                feedforward_widen_matrix[layer_index],
                feedforward_shrink_matrix[layer_index],
            ],
            axis=1,
        )
        chunks.append(rest_own)
    head_own = jnp.concatenate(
        [
            lax.dynamic_index_in_dim(
                matrix.reshape(outer, 8, -1, group_width), me % 8, 1, keepdims=False
            )
            for matrix in (readout_latent_matrix, readout_shortcut_matrix, readout_emit_matrix)
        ],
        axis=2,
    )
    chunks.append(head_own)
    count = len(chunks)

    def gather_chunk(number, own):
        if number < count - 1:
            return gather_head(own)
        return lax.all_gather(own, "head", axis=0, tiled=True)

    held = gather_chunk(0, chunks[0])
    met = lax.all_to_all(after(sent, held), "head", split_axis=0, concat_axis=0, tiled=True)
    cosine_wide = jnp.tile(jnp.concatenate([cosine[:, 0], cosine[:, 0]], axis=1), (1, HEADS))
    sine_wide = jnp.tile(jnp.concatenate([-sine[:, 0], sine[:, 0]], axis=1), (1, HEADS))
    tables = (cosine, sine, cosine_wide, sine_wide)
    nears, fars, near_mets = [], [], []
    layers = []
    onward = None
    for number in range(count + 1):
        step = {}
        if number < count:
            step["x"], step["y"] = swap(held, 1), swap(held, 2)
        if number + 1 < count:
            step["next"] = gather_chunk(number + 1, chunks[number + 1])
        if number == 0:
            step["resid"] = resid
        else:
            step["far"] = (swap(onward[0], 1), swap(onward[1], 2))
            parts = [*(fars[number - 2] if number > 1 else ()), *nears[number - 1]]
            in_turn = swap_in_turn(parts, 0, onward)
            near_mets.append(in_turn[-3:])
        if number > 1:
            chunk = number - 2
            far_met = in_turn[:2]
            pieces = all_pieces(nears[chunk], fars[chunk], near_mets[chunk], far_met)
            if chunk == 0:
                gain_rows = place(places, pieces, [128], 3 * MODEL_WIDTH)[0][0]
                gain_rows = gain_rows[:, : 2 * layer_count].T.reshape(layer_count, 2, -1)
            if chunk % 2 == 0:
                layers.append(Layer(places, pieces, gain_rows[chunk // 2], tables, allowed))
                step["mixed"] = layers[-1].entry_forward(resid)
            else:
                layers[-1].add_rest(pieces)
                step["resid"] = layers[-1].rest_forward(mixed)
        step["own"] = chunks[number + 2 :]
        step = lax.optimization_barrier(step)
        chunks[number + 2 :] = step["own"]
        if number < count:
            nears.append((held, step["x"], step["y"]))
            onward = second_step(*nears[-1])
        held = step.get("next")
        if number > 0:
            fars.append(step["far"])
        resid = step.get("resid", resid)
        mixed = step.get("mixed")
    head_far_met = [swap(part, 0) for part in fars[-1]]
    head_pieces = all_pieces(nears[-1], fars[-1], near_mets[-1], head_far_met)
    head_whole = place(places, head_pieces, [3 * group_width])[0]

    sensitivity = met[:, :rows]
    head_offsets = met[:, rows : rows + 4].astype(jnp.float32)
    latent_offsets = head_offsets[:, 0] + head_offsets[:, 2]
    emit_offsets = head_offsets[:, 1] + head_offsets[:, 3]

    top = resid.astype(jnp.bfloat16)
    keep_column = keep_rows[:, None]
    two = 2 * group_width
    inner_parts = [
        jnp.dot(top, head_whole[part][:, :two], preferred_element_type=jnp.float32)
        for part in range(group)
    ]
    head_pre = jnp.concatenate(
        [inner_parts[part][:, :group_width] + latent_offsets[part] for part in range(group)],
        axis=1,
    )
    head_hidden = jax.nn.silu(head_pre).astype(jnp.bfloat16)
    forecast = jnp.stack(
        [
            (
                jnp.dot(
                    head_hidden, head_whole[part][:, two:], preferred_element_type=jnp.float32
                )
                + emit_offsets[part]
                + inner_parts[part][:, group_width:]
            )
            * keep_column
            for part in range(group)
        ]
    ).astype(jnp.bfloat16)
    token_predictions = lax.all_to_all(
        forecast, "head", split_axis=0, concat_axis=0, tiled=True
    ).reshape(group * rows, group_width)
    grad_forecast = (sensitivity.astype(jnp.float32) * keep_column).astype(jnp.bfloat16)
    grad_hidden = sum(
        reverse_matmul_answer(grad_forecast[part], head_whole[part][:, two:])
        for part in range(group)
    )
    unused_head, head_pull = jax.vjp(jax.nn.silu, head_pre)
    grad_head_pre = head_pull(grad_hidden)[0].astype(jnp.bfloat16)
    grad_resid = sum(
        reverse_matmul_answer(
            jnp.concatenate(
                [
                    grad_head_pre[:, part * group_width : (part + 1) * group_width],
                    grad_forecast[part],
                ],
                axis=1,
            ),
            head_whole[part][:, :two],
        )
        for part in range(group)
    )
    grad_forecast_rows = jnp.concatenate([grad_forecast[part] for part in range(group)], axis=1)
    head_bias_rows = (
        jnp.sum(grad_head_pre.astype(jnp.float32), axis=0),
        jnp.sum(grad_forecast_rows.astype(jnp.float32), axis=0),
    )
    head_products = RowSums(
        *pair_products(
            me,
            [
                (top, grad_head_pre),
                (top, grad_forecast_rows),
                (head_hidden, grad_forecast_rows),
            ],
        )
    )
    gain_sums = [[None, None] for _ in range(layer_count)]

    def rest_stage(layer_index, carry):
        outs = layers[layer_index].rest_backward(carry["grad"])
        carry = {"middle": outs[0], "mixed": outs[1]}
        gain_sums[layer_index][1] = outs[4]
        return carry, RowSums(*pair_products(me, list(zip(outs[2], outs[3], strict=True))))

    def entry_stage(layer_index, carry):
        outs = layers[layer_index].entry_backward(carry["middle"], carry["mixed"])
        gain_sums[layer_index][0] = outs[3]
        return {"grad": outs[0]}, RowSums(*pair_products(me, [(outs[1], outs[2])]))

    def input_stage(carry):
        grad_entry = carry["grad"].astype(jnp.bfloat16)
        grad_entry_outer = dyadic_accumulation(entry_hidden, grad_entry)
        grad_entry_outer_bias = jnp.sum(grad_entry.astype(jnp.float32), axis=0)
        grad_entry_skip = dyadic_accumulation(features, grad_entry)
        unused_entry, entry_pull = jax.vjp(jax.nn.silu, entry_pre)
        grad_entry_pre = entry_pull(reverse_matmul_answer(grad_entry, intake_emit_matrix))[0].astype(
            jnp.bfloat16
        )
        grad_entry_inner = dyadic_accumulation(features, grad_entry_pre)
        grad_entry_inner_bias = jnp.sum(grad_entry_pre.astype(jnp.float32), axis=0)
        grad_features = reverse_matmul_answer(
            grad_entry_pre, intake_latent_matrix
        ) + reverse_matmul_answer(grad_entry, intake_shortcut_matrix)
        values_grad = jnp.where(pad_mask, 0.0, grad_features[:, :patch_len])
        extra_rows = jnp.concatenate(
            [
                grad_entry_inner,
                grad_entry_skip,
                grad_entry_inner_bias[None],
                grad_entry_outer_bias[None],
            ]
            + [row[None] for row in head_bias_rows]
            + [row[None] for pair in gain_sums for row in pair],
            axis=0,
        )
        return values_grad, extra_rows.shape[0], entry_products(me, grad_entry_outer, extra_rows)

    carry = {"grad": grad_resid}
    sums = [[head_products]]
    stages = []
    for layer_index in reversed(range(layer_count)):
        stages += [(rest_stage, layer_index), (entry_stage, layer_index)]
    finished = []
    stage_count = len(stages)
    for number in range(stage_count + 3):
        step = {"carry": carry}
        if number <= stage_count:
            step["first"] = [chunk.first() for chunk in sums[number]]
        if 1 <= number <= stage_count + 1:
            step["last"] = [chunk.last() for chunk in sums[number - 1]]
        if number >= 2:
            step["total"] = [chunk.total() for chunk in sums[number - 2][::-1]]
            step["total"] = [
                sum_columns(total) if number == 2 else sum_group(total) for total in step["total"]
            ][::-1]
        if number < stage_count:
            stage, layer_index = stages[number]
            step["carry"], products = stage(layer_index, carry)
            sums.append([products])
            if number == stage_count - 1:
                values_grad, extra_count, entry_sum = input_stage(step["carry"])
                sums[-1].append(entry_sum)
            step["next"] = [(chunk.sent, chunk.later, chunk.own) for chunk in sums[-1]]
        step = lax.optimization_barrier(step)
        carry = step["carry"]
        if number <= stage_count:
            for chunk, met in zip(sums[number], step["first"], strict=True):
                chunk.met = met
        if 1 <= number <= stage_count + 1:
            for chunk, met in zip(sums[number - 1], step["last"], strict=True):
                chunk.last_met = met
        if number >= 2:
            finished.append(step["total"])
        if number < stage_count:
            for chunk, parts in zip(sums[-1], step["next"], strict=True):
                chunk.sent, chunk.later, chunk.own = parts
    head_sums = gather_blocks(me, finished[0][0]).astype(jnp.float32)
    layer_sums = [None] * layer_count
    for member, layer_index in enumerate(reversed(range(layer_count))):
        rest = finished[1 + 2 * member][0].astype(jnp.float32)
        entry = finished[2 + 2 * member][0].astype(jnp.float32)
        layer_sums[layer_index] = (entry[0], rest[0], rest[1], rest[2])
    entry_main, entry_extra = entry_everywhere(
        me, finished[-1][1], own_count, extra_count
    )
    inner_rows = 2 * patch_len
    last = 2 * inner_rows
    entry_sums = (
        entry_extra[:inner_rows],
        entry_extra[last],
        entry_main,
        entry_extra[last + 1],
        entry_extra[inner_rows:last],
    )
    head_bias_sums = lax.dynamic_slice_in_dim(
        entry_extra[last + 2 : last + 4], group_place * group_width, group_width, 1
    )
    own_place = (me * group + group_place) * own_count
    gains_grad = lax.dynamic_slice_in_dim(
        entry_extra[last + 4 : last + 4 + 2 * layer_count], own_place, own_count, 1
    ).reshape(layer_count, 2, own_count)
    qkv_grad = jnp.stack([layer_sums[member][0] for member in range(layer_count)])
    out_grad = jnp.stack([layer_sums[member][1] for member in range(layer_count)])
    up_grad = jnp.stack([layer_sums[member][2] for member in range(layer_count)])
    down_grad = jnp.stack([layer_sums[member][3] for member in range(layer_count)])
    return (
        token_predictions,
        values_grad,
        entry_sums[0],
        entry_sums[1],
        entry_sums[2],
        entry_sums[3],
        entry_sums[4],
        qkv_grad,
        out_grad,
        up_grad,
        down_grad,
        gains_grad,
        head_sums[0],
        head_bias_sums[0],
        head_sums[2],
        head_bias_sums[1],
        head_sums[1],
    )


def solution(mesh):
    return jax.shard_map(
        body,
        mesh=mesh,
        in_specs=(
            P(("dp", "head"), None),
            P(("dp", "head"), None),
            P(("dp", "head"), None),
            P(),
            P(),
            P(),
            P(),
            P(),
            P(None, ("dp", "head"), None),
            P(None, ("dp", "head"), None),
            P(None, ("dp", "head"), None),
            P(None, ("dp", "head"), None),
            P(None, None, ("dp", "head")),
            P(None, "head"),
            P("head"),
            P(None, "head"),
            P("head"),
            P(None, "head"),
            P("dp", "head"),
        ),
        out_specs=(
            P("dp", "head"),
            P(("dp", "head"), None),
            P(),
            P(),
            P(),
            P(),
            P(),
            P(None, ("dp", "head"), None),
            P(None, ("dp", "head"), None),
            P(None, ("dp", "head"), None),
            P(None, ("dp", "head"), None),
            P(None, None, ("dp", "head")),
            P(None, "head"),
            P("head"),
            P(None, "head"),
            P("head"),
            P(None, "head"),
        ),
        check_vma=False,
    )
```

```python
from functools import partial
import math

import jax
import jax.numpy as jnp
from jax import lax
from jax.experimental import pallas as pl
from jax.experimental.pallas import tpu as pltpu
from jax.sharding import PartitionSpec as P

MODEL_WIDTH = 1280
HEADS = 16
HEAD_DIM = 80


EPS = 1e-06
SMALL_COST = pl.CostEstimate(flops=1, bytes_accessed=1, transcendentals=0)
ROPE_BASE = 10000.0


def layout_rows(series_row, pad_row, patch_len):
    count = series_row.shape[0]
    order = jnp.arange(count, dtype=jnp.int32)
    same_series = series_row[:, None] == series_row[None, :]
    earlier = order[None, :] < order[:, None]
    position = jnp.sum(jnp.logical_and(same_series, earlier).astype(jnp.int32), axis=1)
    numbers = jnp.arange(pad_row.shape[0], dtype=jnp.int32)
    series_pad = jnp.sum(
        jnp.where(series_row[:, None] == numbers[None, :], pad_row[None, :], 0), axis=1
    )
    pad_count = jnp.where(position == 0, series_pad, 0)
    padded = pad_count == patch_len
    diagonal = order[:, None] == order[None, :]
    reach = jnp.logical_or(jnp.logical_and(earlier, jnp.logical_not(padded)[None, :]), diagonal)
    allowed = jnp.logical_and(same_series, reach)
    keep_rows = jnp.where(padded, 0.0, 1.0).astype(jnp.float32)
    return (position, pad_count, allowed, keep_rows)


def rotary_tables(position, head_dim):
    half = head_dim // 2
    steps = jnp.arange(half, dtype=jnp.float32) / half
    inverse = jnp.exp(-math.log(ROPE_BASE) * steps)
    angles = position.astype(jnp.float32)[:, None] * inverse[None, :]
    return (jnp.cos(angles)[:, None, :], jnp.sin(angles)[:, None, :])


def rotate(heads_rows, cosine, sine):
    half = heads_rows.shape[-1] // 2
    first = heads_rows[..., :half]
    second = heads_rows[..., half:]
    return jnp.concatenate(
        [first * cosine - second * sine, second * cosine + first * sine], axis=-1
    )


def unrotate(grad_rows, cosine, sine):
    half = grad_rows.shape[-1] // 2
    first = grad_rows[..., :half]
    second = grad_rows[..., half:]
    return jnp.concatenate(
        [first * cosine + second * sine, second * cosine - first * sine], axis=-1
    )


def norm_apply(resid, gain):
    return resid * lax.rsqrt(jnp.mean(resid * resid, axis=-1, keepdims=True) + EPS) * gain


def dyadic_accumulation(left, right):
    return lax.dot_general(
        left, right, (((0,), (0,)), ((), ())), preferred_element_type=jnp.float32
    )


def reverse_matmul_answer(grad_rows, weight):
    return lax.dot_general(
        grad_rows, weight, (((1,), (1,)), ((), ())), preferred_element_type=jnp.float32
    )


def masked_scores(query_rows, key_rows, allowed):
    scale = 1.0 / math.sqrt(query_rows.shape[-1])
    scores = (
        jnp.einsum("qhd,khd->hqk", query_rows, key_rows, preferred_element_type=jnp.float32) * scale
    )
    return jnp.where(allowed[None], scores, -1e30)


def attend_forward(query_rows, key_rows, value_rows, allowed):
    scores = masked_scores(query_rows, key_rows, allowed)
    peak = jnp.max(scores, axis=-1, keepdims=True)
    weights = jnp.exp(scores - peak)
    total = jnp.sum(weights, axis=-1, keepdims=True)
    probs = (weights / total).astype(jnp.bfloat16)
    mixed = jnp.einsum("hqk,khd->qhd", probs, value_rows, preferred_element_type=jnp.float32)
    return (mixed, peak + jnp.log(total))


def attend_backward(query_rows, key_rows, value_rows, allowed, log_total, grad_mixed):
    scale = 1.0 / math.sqrt(query_rows.shape[-1])
    scores = masked_scores(query_rows, key_rows, allowed)
    probs = jnp.where(allowed[None], jnp.exp(scores - log_total), 0.0)
    grad_probs = jnp.einsum(
        "qhd,khd->hqk", grad_mixed, value_rows, preferred_element_type=jnp.float32
    )
    grad_values = jnp.einsum(
        "hqk,qhd->khd", probs.astype(jnp.bfloat16), grad_mixed, preferred_element_type=jnp.float32
    )
    center = jnp.sum(grad_probs * probs, axis=-1, keepdims=True)
    grad_scores = (probs * (grad_probs - center)).astype(jnp.bfloat16)
    grad_query = (
        jnp.einsum("hqk,khd->qhd", grad_scores, key_rows, preferred_element_type=jnp.float32)
        * scale
    )
    grad_keys = (
        jnp.einsum("hqk,qhd->khd", grad_scores, query_rows, preferred_element_type=jnp.float32)
        * scale
    )
    return (grad_query, grad_keys, grad_values)


def after(value, *earlier):
    return lax.optimization_barrier((value, *earlier))[0]


def swap(v, bit):
    size = lax.axis_size("dp")
    return lax.ppermute(v, "dp", [(i, i ^ (1 << bit)) for i in range(size)])


def swap_in_turn(parts, bit, *earlier):
    met = []
    for part in parts:
        met.append(swap(after(part, *earlier), bit))
        earlier = (met[-1],)
    return met


def outer_groups():
    size = lax.axis_size("dp")
    return [[j + 8 * o for o in range(size // 8)] for j in range(8)]


def place_kernel(plan, piece_count, out_count, me_ref, *refs):
    pieces = refs[:piece_count]
    outs = refs[piece_count : piece_count + out_count]
    held = refs[piece_count + out_count : piece_count + 2 * out_count]
    in_sems, out_sems = refs[piece_count + 2 * out_count :]
    inward, outward = [], []
    for n, (piece, rel, row, out, column) in enumerate(plan):
        source = pieces[piece]
        width = held[out].shape[-1]
        if width != source.shape[-1]:
            source = source.at[:, :, pl.ds(column, width)]
        spot = (slice(None), me_ref[0] ^ rel, pl.ds(row, source.shape[1]), slice(None))
        inward.append(pltpu.make_async_copy(source, held[out].at[spot], in_sems.at[n]))
        outward.append(
            pltpu.make_async_copy(held[out].at[spot], outs[out].at[spot], out_sems.at[n])
        )
    for copy in inward:
        copy.start()
    for copy, onward in zip(inward, outward):
        copy.wait()
        onward.start()
    for onward in outward:
        onward.wait()


def place(me, pieces, widths, first=0):
    plan = []
    for n, (rel, row, _) in enumerate(pieces):
        column = first
        for out, width in enumerate(widths):
            plan.append((n, rel, row, out, column))
            column += width
    arrays = [array for _, _, array in pieces]
    lead, rows, _ = arrays[0].shape
    kind = arrays[0].dtype
    total = sum(8 * lead * rows * -(-w // 128) * 128 for w in widths) * 2
    outs = pl.pallas_call(
        partial(place_kernel, plan, len(arrays), len(widths)),
        out_shape=[jax.ShapeDtypeStruct((lead, 8, rows, w), kind) for w in widths],
        in_specs=[pl.BlockSpec(memory_space=pltpu.SMEM)]
        + [pl.BlockSpec(memory_space=pl.ANY)] * len(arrays),
        out_specs=[pl.BlockSpec(memory_space=pl.ANY)] * len(widths),
        scratch_shapes=[pltpu.VMEM((lead, 8, rows, w), kind) for w in widths]
        + [pltpu.SemaphoreType.DMA((len(plan),))] * 2,
        compiler_params=pltpu.CompilerParams(vmem_limit_bytes=total + (4 << 20)),
        cost_estimate=SMALL_COST,
    )(me, *arrays)
    outer = lax.axis_size("dp") // 8
    return [o.reshape(-1, outer * 8 * rows, o.shape[-1]) for o in outs]


def row_half(rows):
    return rows // 32 * 16 if rows >= 32 else rows // 2


def second_step(held, from_x, from_y):
    half = row_half(held.shape[1])
    return from_y[:, :half], from_x[:, half:]


def all_pieces(near, far, near_met, far_met):
    half = far[0].shape[1]
    places = ((0, 0), (2, 0), (4, 0), (6, 0), (6, half))
    pieces = []
    for (rel, row), array, met in zip(places, (*near, *far), (*near_met, *far_met), strict=True):
        pieces += [(rel, row, array), (rel | 1, row, met)]
    return pieces


def spread_rows(held):
    near = (held, swap(held, 1), swap(held, 2))
    onward_x, onward_y = second_step(*near)
    far = (swap(onward_x, 1), swap(onward_y, 2))
    return all_pieces(near, far, [swap(part, 0) for part in near], [swap(part, 0) for part in far])


def gather_head(own):
    held = lax.all_gather(own, "head", axis=0, tiled=True)[None]
    if lax.axis_size("dp") > 8:
        held = lax.all_gather(
            held, "dp", axis=0, tiled=True, axis_index_groups=outer_groups()
        )
    return held


def pick(rows, place, width):
    picked = rows[:, :width]
    for n in range(1, rows.shape[1] // width):
        picked = jnp.where(place == n, rows[:, n * width : (n + 1) * width], picked)
    return picked


def product_kernel(count, outer, me_ref, *refs):
    lefts, rights, met_lefts, met_rights = (refs[n * count : (n + 1) * count] for n in range(4))
    to_x, to_y, later, own, right_pair = refs[4 * count :]
    rows, width = own.shape[1] // outer, own.shape[-1]
    tokens = lefts[0].shape[0]
    half = width // 2
    for n in range(count):
        left, met = lefts[n][...], met_lefts[n][...]
        right_pair[:tokens] = rights[n][...]
        right_pair[tokens:] = met_rights[n][...]
        for rel in range(4):
            place = me_ref[0] ^ (2 * rel)
            for part in range(outer):
                block = slice(part * 8 * rows, (part + 1) * 8 * rows)
                left_pair = jnp.concatenate(
                    [pick(left[:, block], place, rows), pick(met[:, block], place, rows)], axis=0
                )
                total = dyadic_accumulation(left_pair, right_pair[...]).astype(own.dtype)
                one, two = total[:, :half], total[:, half:]
                span = slice(part * rows, (part + 1) * rows)
                if rel == 0:
                    own[n, span] = total
                elif rel == 1:
                    to_x[1, n, span] = one
                    later[1, n, span] = two
                elif rel == 2:
                    later[0, n, span] = one
                    to_y[1, n, span] = two
                else:
                    to_x[0, n, span] = one
                    to_y[0, n, span] = two


def pair_products(me, pairs):
    outer = lax.axis_size("dp") // 8
    met = {}
    earlier = ()
    for rows in [left for left, _ in pairs] + [right for _, right in pairs]:
        if id(rows) not in met:
            met[id(rows)] = swap(after(rows, *earlier), 0)
            earlier = (met[id(rows)],)
    lefts = [left for left, _ in pairs]
    rights = [right for _, right in pairs]
    count = len(pairs)
    block, width = lefts[0].shape[1] // 8, rights[0].shape[1]
    low = jnp.bfloat16
    return pl.pallas_call(
        partial(product_kernel, count, outer),
        out_shape=[
            jax.ShapeDtypeStruct((2, count, block, width // 2), low),
            jax.ShapeDtypeStruct((2, count, block, width // 2), low),
            jax.ShapeDtypeStruct((2, count, block, width // 2), low),
            jax.ShapeDtypeStruct((count, block, width), low),
        ],
        in_specs=[pl.BlockSpec(memory_space=pltpu.SMEM)]
        + [pl.BlockSpec(memory_space=pltpu.VMEM)] * (4 * count),
        out_specs=[pl.BlockSpec(memory_space=pltpu.VMEM)] * 4,
        scratch_shapes=[pltpu.VMEM((2 * lefts[0].shape[0], width), low)],
        compiler_params=pltpu.CompilerParams(vmem_limit_bytes=44 << 20),
        cost_estimate=SMALL_COST,
    )(
        (me & 7).reshape(1),
        *lefts,
        *rights,
        *[met[id(left)] for left in lefts],
        *[met[id(right)] for right in rights],
    )


def low_sum(*parts):
    total = parts[0].astype(jnp.float32)
    for part in parts[1:]:
        total = total + part.astype(jnp.float32)
    return total.astype(jnp.bfloat16)


class RowSums:
    def __init__(self, to_x, to_y, later, own):
        self.sent, self.later, self.own = (to_x, to_y), later, own

    def first(self):
        return swap(self.sent[0], 1), swap(self.sent[1], 2)

    def last(self):
        return (
            swap(low_sum(self.later[0], self.met[0][0]), 2),
            swap(low_sum(self.later[1], self.met[1][0]), 1),
        )

    def total(self):
        half = self.own.shape[-1] // 2
        return jnp.concatenate(
            [
                low_sum(self.own[..., :half], self.met[0][1], self.last_met[0]),
                low_sum(self.own[..., half:], self.met[1][1], self.last_met[1]),
            ],
            axis=-1,
        )


def sum_group(total):
    outer = lax.axis_size("dp") // 8
    group = lax.axis_size("head")
    lead = total.shape[:-2]
    rows, columns = total.shape[-2:]
    if outer > 1:
        total = lax.psum_scatter(
            total.reshape(*lead, outer, rows // outer, columns),
            "dp",
            scatter_dimension=len(lead),
            tiled=True,
            axis_index_groups=outer_groups(),
        )
    total = total.reshape(*lead, rows // outer, columns)
    return lax.psum_scatter(total, "head", scatter_dimension=len(lead), tiled=True)


def sum_group_at_once(total):
    outer = lax.axis_size("dp") // 8
    group = lax.axis_size("head")
    if outer > 1:
        return sum_group(total).astype(jnp.float32)
    lead = total.shape[:-2]
    rows, columns = total.shape[-2:]
    total = total.reshape(*lead, group, rows // group, columns)
    axis = len(lead)
    met = lax.all_to_all(total, "head", split_axis=axis, concat_axis=axis, tiled=True)
    return jnp.sum(met.astype(jnp.float32), axis=axis)


def sum_columns(total):
    group = lax.axis_size("head")
    count, rows, columns = total.shape
    total = jnp.moveaxis(total.reshape(count, rows, group, columns // group), 2, 0)
    return lax.psum_scatter(total, "head", scatter_dimension=0, tiled=True)[0]


def gather_blocks(me, summed):
    outer = lax.axis_size("dp") // 8
    count, rows, columns = summed.shape
    held = summed.reshape(count * outer, rows // outer, columns)
    return place((me & 7).reshape(1), spread_rows(held), [columns])[0]


EXTRA_ROWS = 8


def entry_products(me, main, extra):
    group = lax.axis_size("head")
    outer = lax.axis_size("dp") // 8
    devices = 8 * outer * group
    columns = main.shape[1]
    own = main.shape[0] // devices
    extra = jnp.pad(extra, ((0, EXTRA_ROWS * devices - extra.shape[0]), (0, 0)))
    rows = jnp.concatenate(
        [main.reshape(devices, own, columns), extra.reshape(devices, EXTRA_ROWS, columns)], axis=1
    ).astype(jnp.bfloat16)
    view = rows.reshape(outer, 4, 2, group * (own + EXTRA_ROWS), columns)
    core = me & 1
    other = lax.dynamic_index_in_dim(view, 1 - core, 2, keepdims=False)
    pair = low_sum(lax.dynamic_index_in_dim(view, core, 2, keepdims=False), swap(other, 0))
    chip = (me & 7) >> 1
    half = columns // 2

    def picked(rel):
        return lax.dynamic_index_in_dim(pair, chip ^ rel, 1, keepdims=False).reshape(-1, columns)

    own_rows, at_x, at_y, far = (picked(rel) for rel in range(4))
    return RowSums(
        jnp.stack([far[:, :half], at_x[:, :half]]),
        jnp.stack([far[:, half:], at_y[:, half:]]),
        (at_y[:, :half], at_x[:, half:]),
        own_rows,
    )


def entry_kernel(plan, own, me_ref, *refs):
    pieces = refs[: len(plan)]
    main_ref, extra_ref, held, sems = refs[len(plan) :]
    copies = []
    for n, (rel, row, rows) in enumerate(plan):
        spot = held.at[me_ref[0] ^ rel, pl.ds(row, rows)]
        copies.append(pltpu.make_async_copy(pieces[n].at[0], spot, sems.at[n]))
    for copy in copies:
        copy.start()
    for copy in copies:
        copy.wait()
    span = own + EXTRA_ROWS
    group = held.shape[1] // span
    for block in range(8):
        rows = held[block].astype(jnp.float32)
        for member in range(group):
            main_ref[block * group + member] = rows[member * span : member * span + own]
            extra_ref[block * group + member] = rows[member * span + own : (member + 1) * span]


def entry_everywhere(me, total, own, count):
    columns = total.shape[1]
    outer = lax.axis_size("dp") // 8
    if outer > 1:
        held = gather_head(sum_group(total))
    else:
        held = lax.psum(total, "head")[None]
    pieces = spread_rows(held)
    places = (me & 7).reshape(1)
    span = own + EXTRA_ROWS
    if held.shape[0] > 1 or own % 8 or not in_kernel(pieces):
        (whole,) = place(places, pieces, [columns])
        whole = whole.reshape(-1, span, columns).astype(jnp.float32)
        return whole[:, :own].reshape(-1, columns), whole[:, own:].reshape(-1, columns)[:count]
    rows = held.shape[1]
    blocks = 8 * rows // span
    plan = [(rel, row, array.shape[1]) for rel, row, array in pieces]
    vmem = pl.BlockSpec(memory_space=pltpu.VMEM)
    main, extra = pl.pallas_call(
        partial(entry_kernel, plan, own),
        out_shape=[
            jax.ShapeDtypeStruct((blocks, own, columns), jnp.float32),
            jax.ShapeDtypeStruct((blocks, EXTRA_ROWS, columns), jnp.float32),
        ],
        in_specs=[pl.BlockSpec(memory_space=pltpu.SMEM)]
        + [pl.BlockSpec(memory_space=pl.ANY)] * len(pieces),
        out_specs=[vmem, vmem],
        scratch_shapes=[
            pltpu.VMEM((8, rows, columns), held.dtype),
            pltpu.SemaphoreType.DMA((len(pieces),)),
        ],
        compiler_params=pltpu.CompilerParams(vmem_limit_bytes=44 << 20),
        cost_estimate=SMALL_COST,
    )(places, *[array for _, _, array in pieces])
    return main.reshape(-1, columns), extra.reshape(-1, columns)[:count]


def fetch(plan, me, pieces, whole, sems):
    groups = []
    for group in range(whole.shape[1] // MODEL_WIDTH):
        columns = pl.ds(group * MODEL_WIDTH, MODEL_WIDTH)
        copies = []
        for n, (rel, row, rows) in enumerate(plan):
            first = pl.multiple_of((me ^ rel) * (whole.shape[0] // 8) + row, 16)
            copies.append(
                pltpu.make_async_copy(
                    pieces[n].at[0, :, columns],
                    whole.at[pl.ds(first, rows), columns],
                    sems.at[group * len(plan) + n],
                )
            )
        for copy in copies:
            copy.start()
        groups.append(copies)
    return groups


def arrive(copies):
    for copy in copies:
        copy.wait()


def rows_times(left, whole, first, out, tile):
    def step(n, _):
        at = pl.multiple_of(n * tile, 128)
        out[:, pl.ds(at, tile)] = jnp.dot(
            left, whole[:, pl.ds(first + at, tile)], preferred_element_type=jnp.float32
        )
        return 0

    lax.fori_loop(0, out.shape[1] // tile, step, 0)


def rows_times_turned(left, whole, first, width, out, tile):
    def step(n, _):
        at = pl.multiple_of(n * tile, 128)
        part = reverse_matmul_answer(whole[pl.ds(at, tile), pl.ds(first, width)], left)
        out[:, pl.ds(at, tile)] = part.T
        return 0

    lax.fori_loop(0, out.shape[1] // tile, step, 0)


def inverse_norm(rows):
    return lax.rsqrt(jnp.mean(rows * rows, axis=-1, keepdims=True) + EPS)


def other_half(rows):
    half = HEAD_DIM // 2
    lane = lax.broadcasted_iota(jnp.int32, rows.shape, 1) % HEAD_DIM
    ahead = pltpu.roll(rows, rows.shape[1] - half, 1)
    behind = pltpu.roll(rows, half, 1)
    return jnp.where(lane < half, ahead, behind)


def head_window(head, width):
    first = head * HEAD_DIM // 128 * 128
    last = min(-(-(head + 1) * HEAD_DIM // 128) * 128, width)
    start = head * HEAD_DIM - first
    lane = lax.broadcasted_iota(jnp.int32, (1, last - first), 1)
    return slice(first, last), jnp.logical_and(lane >= start, lane < start + HEAD_DIM)


def entry_forward_kernel(plan, me_ref, resid_ref, gain_ref, cosine_ref, sine_ref, allowed_ref, *refs):
    pieces = refs[: len(plan)]
    normed_ref, query_ref, key_ref, value_ref, total_ref, mixed_ref = refs[len(plan) : len(plan) + 6]
    whole, wide, sems = refs[len(plan) + 6 :]
    groups = fetch(plan, me_ref[0], pieces, whole, sems)
    resid = resid_ref[...]
    normed = (resid * inverse_norm(resid) * gain_ref[...]).astype(jnp.bfloat16)
    normed_ref[...] = normed
    for group, out in enumerate((query_ref, key_ref, value_ref)):
        arrive(groups[group])
        rows_times(normed, whole, group * MODEL_WIDTH, wide, 256)
        rows = wide[...]
        if group < 2:
            rows = rows * cosine_ref[...] + other_half(rows) * sine_ref[...]
        out[...] = rows.astype(jnp.bfloat16)
    scale = 1.0 / math.sqrt(HEAD_DIM)
    allowed = allowed_ref[...] > 0.0
    wide[...] = jnp.zeros_like(wide)
    totals = jnp.zeros(total_ref.shape, jnp.float32)
    head_lane = lax.broadcasted_iota(jnp.int32, total_ref.shape, 1)
    for head in range(HEADS):
        window, inside = head_window(head, MODEL_WIDTH)
        query = jnp.where(inside, query_ref[:, window], 0)
        scores = reverse_matmul_answer(query, key_ref[:, window]) * scale
        scores = jnp.where(allowed, scores, -1e30)
        peak = jnp.max(scores, axis=-1, keepdims=True)
        weights = jnp.exp(scores - peak)
        total = jnp.sum(weights, axis=-1, keepdims=True)
        probs = (weights / total).astype(jnp.bfloat16)
        mixed = jnp.dot(probs, value_ref[:, window], preferred_element_type=jnp.float32)
        wide[:, window] += jnp.where(inside, mixed, 0.0)
        totals = jnp.where(head_lane == head, peak + jnp.log(total), totals)
    total_ref[...] = totals
    mixed_ref[...] = wide[...].astype(jnp.bfloat16)


def gelu_parts(x):
    root = math.sqrt(2.0 / math.pi)
    bend = jnp.tanh(root * (x + 0.044715 * (x * x * x)))
    slope = 0.5 * (1.0 + bend) + 0.5 * x * (1.0 - bend * bend) * root * (
        1.0 + 3.0 * 0.044715 * (x * x)
    )
    return 0.5 * x * (1.0 + bend), slope


def rest_forward_kernel(plan, me_ref, resid_ref, mixed_ref, gain_ref, *refs):
    pieces = refs[: len(plan)]
    result_ref, middle_ref, normed_ref, pre_ref = refs[len(plan) : len(plan) + 4]
    whole, sems = refs[len(plan) + 4 :]
    groups = fetch(plan, me_ref[0], pieces, whole, sems)
    arrive(groups[0])
    rows_times(mixed_ref[...], whole, 0, middle_ref, 256)
    middle = resid_ref[...] + middle_ref[...]
    middle_ref[...] = middle
    normed = (middle * inverse_norm(middle) * gain_ref[...]).astype(jnp.bfloat16)
    normed_ref[...] = normed
    arrive(groups[1])
    rows_times(normed, whole, MODEL_WIDTH, pre_ref, 256)
    act = gelu_parts(pre_ref[...])[0].astype(jnp.bfloat16)
    arrive(groups[2])
    rows_times(act, whole, 2 * MODEL_WIDTH, result_ref, 256)
    result_ref[...] += middle_ref[...]


def norm_back(rows, gain, grad):
    inverse = inverse_norm(rows)
    scaled = grad * gain
    mean = jnp.mean(rows * scaled, axis=-1, keepdims=True)
    sent = inverse * scaled - rows * (inverse * inverse * inverse * mean)
    return sent, jnp.sum(grad * rows * inverse, axis=0, keepdims=True)


def rest_backward_kernel(plan, me_ref, grad_ref, middle_ref, pre_ref, gain_ref, *refs):
    pieces = refs[: len(plan)]
    outs = refs[len(plan) : len(plan) + 7]
    grad_middle_ref, mixed_ref, attn_ref, grad_pre_ref, branch_ref, act_ref, gain_grad_ref = outs
    whole, wide, sems = refs[len(plan) + 7 :]
    groups = fetch(plan, me_ref[0], pieces, whole, sems)
    grad = grad_ref[...]
    branch = grad.astype(jnp.bfloat16)
    branch_ref[...] = branch
    arrive(groups[2])
    rows_times_turned(branch, whole, 2 * MODEL_WIDTH, MODEL_WIDTH, wide, 256)
    act, slope = gelu_parts(pre_ref[...])
    act_ref[...] = act.astype(jnp.bfloat16)
    grad_pre = (wide[...] * slope).astype(jnp.bfloat16)
    grad_pre_ref[...] = grad_pre
    arrive(groups[1])
    rows_times_turned(grad_pre, whole, MODEL_WIDTH, MODEL_WIDTH, wide, 256)
    sent, gain_grad_ref[...] = norm_back(middle_ref[...], gain_ref[...], wide[...])
    grad_middle = grad + sent
    grad_middle_ref[...] = grad_middle
    attn = grad_middle.astype(jnp.bfloat16)
    attn_ref[...] = attn
    arrive(groups[0])
    rows_times_turned(attn, whole, 0, MODEL_WIDTH, wide, 256)
    mixed_ref[...] = wide[...].astype(jnp.bfloat16)


def entry_backward_kernel(
    plan,
    me_ref,
    grad_middle_ref,
    grad_mixed_ref,
    resid_ref,
    query_ref,
    key_ref,
    value_ref,
    total_ref,
    gain_ref,
    cosine_ref,
    sine_ref,
    allowed_ref,
    *refs,
):
    pieces = refs[: len(plan)]
    grad_resid_ref, projected_ref, gain_grad_ref = refs[len(plan) : len(plan) + 3]
    whole, grad_query, grad_key, grad_value, sems = refs[len(plan) + 3 :]
    groups = fetch(plan, me_ref[0], pieces, whole, sems)
    scale = 1.0 / math.sqrt(HEAD_DIM)
    allowed = allowed_ref[...] > 0.0
    totals = total_ref[...]
    grad_query[...] = jnp.zeros_like(grad_query)
    grad_key[...] = jnp.zeros_like(grad_key)
    grad_value[...] = jnp.zeros_like(grad_value)
    for head in range(HEADS):
        window, inside = head_window(head, MODEL_WIDTH)
        query = jnp.where(inside, query_ref[:, window], 0)
        keys = key_ref[:, window]
        grad_mixed = jnp.where(inside, grad_mixed_ref[:, window], 0)
        scores = reverse_matmul_answer(query, keys) * scale
        probs = jnp.where(allowed, jnp.exp(scores - totals[:, head : head + 1]), 0.0)
        grad_probs = reverse_matmul_answer(grad_mixed, value_ref[:, window])
        grad_value[:, window] += dyadic_accumulation(probs.astype(jnp.bfloat16), grad_mixed)
        center = jnp.sum(grad_probs * probs, axis=-1, keepdims=True)
        grad_scores = (probs * (grad_probs - center)).astype(jnp.bfloat16)
        along = jnp.dot(grad_scores, keys, preferred_element_type=jnp.float32)
        grad_query[:, window] += jnp.where(inside, along * scale, 0.0)
        grad_key[:, window] += dyadic_accumulation(grad_scores, query) * scale
    for group, part in enumerate((grad_query, grad_key, grad_value)):
        rows = part[...]
        if group < 2:
            rows = rows * cosine_ref[...] - other_half(rows) * sine_ref[...]
        projected_ref[:, group * MODEL_WIDTH : (group + 1) * MODEL_WIDTH] = rows.astype(jnp.bfloat16)
    for copies in groups:
        arrive(copies)
    rows_times_turned(projected_ref[...], whole, 0, 3 * MODEL_WIDTH, grad_query, 256)
    sent, gain_grad_ref[...] = norm_back(resid_ref[...], gain_ref[...], grad_query[...])
    grad_resid_ref[...] = grad_middle_ref[...] + sent


def whole_call(kernel, me, pieces, inputs, outs, wides):
    rows = inputs[0].shape[0]
    plan = [(rel, row, array.shape[1]) for rel, row, array in pieces]
    blocks = 8 * pieces[0][2].shape[1]
    columns = 3 * MODEL_WIDTH
    vmem = pl.BlockSpec(memory_space=pltpu.VMEM)
    return pl.pallas_call(
        partial(kernel, plan),
        out_shape=[jax.ShapeDtypeStruct(shape, kind) for shape, kind in outs],
        in_specs=[pl.BlockSpec(memory_space=pltpu.SMEM)]
        + [vmem] * len(inputs)
        + [pl.BlockSpec(memory_space=pl.ANY)] * len(pieces),
        out_specs=[vmem] * len(outs),
        scratch_shapes=[pltpu.VMEM((blocks, columns), jnp.bfloat16)]
        + [pltpu.VMEM((rows, MODEL_WIDTH), jnp.float32)] * wides
        + [pltpu.SemaphoreType.DMA((3 * len(pieces),))],
        compiler_params=pltpu.CompilerParams(vmem_limit_bytes=44 << 20),
        cost_estimate=SMALL_COST,
    )(me, *inputs, *[array for _, _, array in pieces])


def in_kernel(pieces):
    lead, rows, _ = pieces[0][2].shape
    return lead == 1 and rows % 32 == 0


LOW, FULL = jnp.bfloat16, jnp.float32


class Layer:
    def __init__(self, places, entry_pieces, gains, tables, allowed):
        self.places, self.entry_pieces, self.gains = places, entry_pieces, gains
        self.tables, self.allowed = tables, allowed
        self.fetched = in_kernel(entry_pieces)
        if not self.fetched:
            self.entry_whole = place(places, entry_pieces, [3 * MODEL_WIDTH])[0][0]

    def add_rest(self, rest_pieces):
        self.rest_pieces = rest_pieces
        if not self.fetched:
            self.rest_whole = [part[0] for part in place(self.places, rest_pieces, [MODEL_WIDTH] * 3)]

    def shapes(self, *kinds):
        rows = self.allowed.shape[0]
        return [((rows, width), kind) for width, kind in kinds]

    def entry_forward(self, resid):
        if not self.fetched:
            self.saved = entry_forward(
                resid, self.entry_whole, self.gains, *self.tables[:2], self.allowed
            )
            return self.saved[6]
        wide = (MODEL_WIDTH, LOW)
        self.resid = resid
        outs = whole_call(
            entry_forward_kernel,
            self.places,
            self.entry_pieces,
            (resid, self.gains[:1].astype(FULL), *self.tables[2:], self.allowed.astype(FULL)),
            self.shapes(wide, wide, wide, wide, (128, FULL), wide),
            1,
        )
        self.normed_first, self.heads = outs[0], outs[1:5]
        return outs[5]

    def rest_forward(self, mixed):
        if not self.fetched:
            result, self.saved = rest_forward(
                (*self.saved[:6], mixed), *self.rest_whole, self.gains
            )
            return result
        self.mixed = mixed
        result, self.middle, self.normed_second, self.hidden_pre = whole_call(
            rest_forward_kernel,
            self.places,
            self.rest_pieces,
            (self.resid, mixed, self.gains[1:].astype(FULL)),
            self.shapes(
                (MODEL_WIDTH, FULL), (MODEL_WIDTH, FULL), (MODEL_WIDTH, LOW), (MODEL_WIDTH, FULL)
            ),
            0,
        )
        return result

    def rest_backward(self, grad):
        if not self.fetched:
            weights = (self.entry_whole, *self.rest_whole, self.gains)
            return rest_backward(self.saved, weights, grad)
        wide = (MODEL_WIDTH, LOW)
        grad_middle, grad_mixed, grad_attn, grad_pre, branch, act, gain_grad = whole_call(
            rest_backward_kernel,
            self.places,
            self.rest_pieces,
            (grad, self.middle, self.hidden_pre, self.gains[1:].astype(FULL)),
            self.shapes((MODEL_WIDTH, FULL), wide, wide, wide, wide, wide)
            + [((1, MODEL_WIDTH), FULL)],
            1,
        )
        lefts = (self.mixed, self.normed_second, act)
        return grad_middle, grad_mixed, lefts, (grad_attn, grad_pre, branch), gain_grad[0]

    def entry_backward(self, grad_middle, grad_mixed):
        if not self.fetched:
            weights = (self.entry_whole, *self.rest_whole, self.gains)
            return entry_backward(
                self.saved, weights, *self.tables[:2], self.allowed, grad_middle, grad_mixed
            )
        grad_resid, projected, gain_grad = whole_call(
            entry_backward_kernel,
            self.places,
            self.entry_pieces,
            (
                grad_middle,
                grad_mixed,
                self.resid,
                *self.heads,
                self.gains[:1].astype(FULL),
                *self.tables[2:],
                self.allowed.astype(FULL),
            ),
            self.shapes((MODEL_WIDTH, FULL), (3 * MODEL_WIDTH, LOW)) + [((1, MODEL_WIDTH), FULL)],
            3,
        )
        return grad_resid, self.normed_first, projected, gain_grad[0]


def entry_forward(resid, qkv_full, gain_pair, cosine, sine, allowed):
    gains = gain_pair.astype(jnp.float32)
    rows = resid.shape[0]
    normed_first = norm_apply(resid, gains[0]).astype(jnp.bfloat16)
    projected = jnp.dot(normed_first, qkv_full, preferred_element_type=jnp.float32)
    query_rows = rotate(
        projected[:, :MODEL_WIDTH].reshape(rows, HEADS, HEAD_DIM), cosine, sine
    ).astype(jnp.bfloat16)
    key_rows = rotate(
        projected[:, MODEL_WIDTH : 2 * MODEL_WIDTH].reshape(rows, HEADS, HEAD_DIM), cosine, sine
    ).astype(jnp.bfloat16)
    value_rows = projected[:, 2 * MODEL_WIDTH :].reshape(rows, HEADS, HEAD_DIM).astype(jnp.bfloat16)

    mixed, log_total = attend_forward(query_rows, key_rows, value_rows, allowed)
    mixed_low = mixed.reshape(rows, MODEL_WIDTH).astype(jnp.bfloat16)
    return (resid, normed_first, query_rows, key_rows, value_rows, log_total, mixed_low)


def rest_forward(saved, out_full, up_full, down_full, gain_pair):
    gains = gain_pair.astype(jnp.float32)
    resid, mixed_low = saved[0], saved[6]
    middle = resid + jnp.dot(mixed_low, out_full, preferred_element_type=jnp.float32)
    normed_second = norm_apply(middle, gains[1]).astype(jnp.bfloat16)
    hidden_pre = jnp.dot(normed_second, up_full, preferred_element_type=jnp.float32)
    hidden_act = jax.nn.gelu(hidden_pre, approximate=True).astype(jnp.bfloat16)
    result = middle + jnp.dot(hidden_act, down_full, preferred_element_type=jnp.float32)
    return (result, (*saved, middle, normed_second, hidden_pre))


def rest_backward(saved, weights, grad_result):
    mixed_low, middle, normed_second, hidden_pre = saved[6:]
    _, out_full, up_full, down_full, gain_pair = weights
    gains = gain_pair.astype(jnp.float32)
    grad_branch = grad_result.astype(jnp.bfloat16)
    hidden_act, gelu_pull = jax.vjp(partial(jax.nn.gelu, approximate=True), hidden_pre)
    hidden_low = hidden_act.astype(jnp.bfloat16)
    grad_act = reverse_matmul_answer(grad_branch, down_full)
    grad_pre = gelu_pull(grad_act)[0].astype(jnp.bfloat16)
    grad_normed_second = reverse_matmul_answer(grad_pre, up_full)
    unused_second, second_pull = jax.vjp(norm_apply, middle, gains[1])
    grad_middle_norm, grad_gain_second = second_pull(grad_normed_second)
    grad_middle = grad_result + grad_middle_norm
    grad_attn = grad_middle.astype(jnp.bfloat16)
    grad_mixed = reverse_matmul_answer(grad_attn, out_full).astype(jnp.bfloat16)
    left_rows = (mixed_low, normed_second, hidden_low)
    right_rows = (grad_attn, grad_pre, grad_branch)
    return (grad_middle, grad_mixed, left_rows, right_rows, grad_gain_second)


def entry_backward(saved, weights, cosine, sine, allowed, grad_middle, grad_mixed):
    resid, normed_first, query_rows, key_rows, value_rows, log_total = saved[:6]
    qkv_full = weights[0]
    gains = weights[4].astype(jnp.float32)
    rows = resid.shape[0]
    grad_query, grad_keys, grad_values = attend_backward(
        query_rows,
        key_rows,
        value_rows,
        allowed,
        log_total,
        grad_mixed.reshape(rows, HEADS, HEAD_DIM),
    )
    grad_query = unrotate(grad_query, cosine, sine).reshape(rows, MODEL_WIDTH)
    grad_keys = unrotate(grad_keys, cosine, sine).reshape(rows, MODEL_WIDTH)
    grad_values = grad_values.reshape(rows, MODEL_WIDTH)
    grad_projected = jnp.concatenate([grad_query, grad_keys, grad_values], axis=1).astype(
        jnp.bfloat16
    )
    grad_normed_first = reverse_matmul_answer(grad_projected, qkv_full)
    unused_first, first_pull = jax.vjp(norm_apply, resid, gains[0])
    grad_resid_norm, grad_gain_first = first_pull(grad_normed_first)
    return (grad_middle + grad_resid_norm, normed_first, grad_projected, grad_gain_first)


def body(
    patch_observations,
    sequence_labels,
    leading_filler_count,
    intake_latent_matrix,
    intake_latent_offset,
    intake_emit_matrix,
    intake_emit_offset,
    intake_shortcut_matrix,
    attention_entry_matrices,
    attention_merge_matrix,
    feedforward_widen_matrix,
    feedforward_shrink_matrix,
    layer_scale_factors,
    readout_latent_matrix,
    readout_latent_offset,
    readout_emit_matrix,
    readout_emit_offset,
    readout_shortcut_matrix,
    loss_sensitivity,
):
    patch_len = patch_observations.shape[1]
    position, pad_count, allowed, keep_rows = layout_rows(
        sequence_labels[0], leading_filler_count[0], patch_len
    )
    cosine, sine = rotary_tables(position, HEAD_DIM)
    columns = jnp.arange(patch_len, dtype=jnp.int32)
    pad_mask = columns[None, :] < pad_count[:, None]
    features = jnp.concatenate(
        [
            jnp.where(pad_mask, jnp.zeros_like(patch_observations), patch_observations),
            pad_mask.astype(jnp.bfloat16),
        ],
        axis=1,
    )
    entry_pre = (
        jnp.dot(features, intake_latent_matrix, preferred_element_type=jnp.float32)
        + intake_latent_offset
    )
    entry_hidden = jax.nn.silu(entry_pre).astype(jnp.bfloat16)
    resid = (
        jnp.dot(entry_hidden, intake_emit_matrix, preferred_element_type=jnp.float32)
        + intake_emit_offset
        + jnp.dot(features, intake_shortcut_matrix, preferred_element_type=jnp.float32)
    )
    layer_count = attention_entry_matrices.shape[0]
    group = lax.axis_size("head")
    group_place = lax.axis_index("head")
    outer = lax.axis_size("dp") // 8
    me = lax.axis_index("dp").astype(jnp.int32)
    places = (me & 7).reshape(1)
    own_count = layer_scale_factors.shape[2]
    rows = patch_observations.shape[0]

    group_width = readout_latent_offset.shape[0]
    offsets = jnp.stack([readout_latent_offset, readout_emit_offset])
    coarse = lax.reduce_precision(offsets, 8, 7)
    offset_rows = jnp.concatenate([coarse, offsets - coarse], axis=0).astype(jnp.bfloat16)
    offset_rows = jnp.pad(offset_rows, ((0, 12), (0, 0)))
    sent = jnp.concatenate(
        [
            loss_sensitivity.reshape(group, rows, group_width),
            jnp.broadcast_to(offset_rows[None], (group, 16, group_width)),
        ],
        axis=1,
    )
    gain_columns = layer_scale_factors.reshape(2 * layer_count, own_count).T
    gain_columns = jnp.pad(gain_columns, ((0, 0), (0, 128 - 2 * layer_count)))
    chunks = []
    for layer_index in range(layer_count):
        entry_own = attention_entry_matrices[layer_index]
        if layer_index == 0:
            entry_own = jnp.concatenate([entry_own, gain_columns], axis=1)
        chunks.append(entry_own)
        rest_own = jnp.concatenate(
            [
                attention_merge_matrix[layer_index],
                feedforward_widen_matrix[layer_index],
                feedforward_shrink_matrix[layer_index],
            ],
            axis=1,
        )
        chunks.append(rest_own)
    head_own = jnp.concatenate(
        [
            lax.dynamic_index_in_dim(
                matrix.reshape(outer, 8, -1, group_width), me % 8, 1, keepdims=False
            )
            for matrix in (readout_latent_matrix, readout_shortcut_matrix, readout_emit_matrix)
        ],
        axis=2,
    )
    chunks.append(head_own)
    count = len(chunks)

    def gather_chunk(number, own):
        if number < count - 1:
            return gather_head(own)
        return lax.all_gather(own, "head", axis=0, tiled=True)

    held = gather_chunk(0, chunks[0])
    met = lax.all_to_all(after(sent, held), "head", split_axis=0, concat_axis=0, tiled=True)
    cosine_wide = jnp.tile(jnp.concatenate([cosine[:, 0], cosine[:, 0]], axis=1), (1, HEADS))
    sine_wide = jnp.tile(jnp.concatenate([-sine[:, 0], sine[:, 0]], axis=1), (1, HEADS))
    tables = (cosine, sine, cosine_wide, sine_wide)
    nears, fars, near_mets = [], [], []
    layers = []
    onward = None
    for number in range(count + 1):
        step = {}
        if number < count:
            step["x"], step["y"] = swap(held, 1), swap(held, 2)
        if number + 1 < count:
            step["next"] = gather_chunk(number + 1, chunks[number + 1])
        if number == 0:
            step["resid"] = resid
        else:
            step["far"] = (swap(onward[0], 1), swap(onward[1], 2))
            parts = [*(fars[number - 2] if number > 1 else ()), *nears[number - 1]]
            in_turn = swap_in_turn(parts, 0, onward)
            near_mets.append(in_turn[-3:])
        if number > 1:
            chunk = number - 2
            far_met = in_turn[:2]
            pieces = all_pieces(nears[chunk], fars[chunk], near_mets[chunk], far_met)
            if chunk == 0:
                gain_rows = place(places, pieces, [128], 3 * MODEL_WIDTH)[0][0]
                gain_rows = gain_rows[:, : 2 * layer_count].T.reshape(layer_count, 2, -1)
            if chunk % 2 == 0:
                layers.append(Layer(places, pieces, gain_rows[chunk // 2], tables, allowed))
                step["mixed"] = layers[-1].entry_forward(resid)
            else:
                layers[-1].add_rest(pieces)
                step["resid"] = layers[-1].rest_forward(mixed)
        step["own"] = chunks[number + 2 :]
        step = lax.optimization_barrier(step)
        chunks[number + 2 :] = step["own"]
        if number < count:
            nears.append((held, step["x"], step["y"]))
            onward = second_step(*nears[-1])
        held = step.get("next")
        if number > 0:
            fars.append(step["far"])
        resid = step.get("resid", resid)
        mixed = step.get("mixed")
    head_far_met = [swap(part, 0) for part in fars[-1]]
    head_pieces = all_pieces(nears[-1], fars[-1], near_mets[-1], head_far_met)
    head_whole = place(places, head_pieces, [3 * group_width])[0]

    sensitivity = met[:, :rows]
    head_offsets = met[:, rows : rows + 4].astype(jnp.float32)
    latent_offsets = head_offsets[:, 0] + head_offsets[:, 2]
    emit_offsets = head_offsets[:, 1] + head_offsets[:, 3]

    top = resid.astype(jnp.bfloat16)
    keep_column = keep_rows[:, None]
    two = 2 * group_width
    inner_parts = [
        jnp.dot(top, head_whole[part][:, :two], preferred_element_type=jnp.float32)
        for part in range(group)
    ]
    head_pre = jnp.concatenate(
        [inner_parts[part][:, :group_width] + latent_offsets[part] for part in range(group)],
        axis=1,
    )
    head_hidden = jax.nn.silu(head_pre).astype(jnp.bfloat16)
    forecast = jnp.stack(
        [
            (
                jnp.dot(
                    head_hidden, head_whole[part][:, two:], preferred_element_type=jnp.float32
                )
                + emit_offsets[part]
                + inner_parts[part][:, group_width:]
            )
            * keep_column
            for part in range(group)
        ]
    ).astype(jnp.bfloat16)
    token_predictions = lax.all_to_all(
        forecast, "head", split_axis=0, concat_axis=0, tiled=True
    ).reshape(group * rows, group_width)
    grad_forecast = (sensitivity.astype(jnp.float32) * keep_column).astype(jnp.bfloat16)
    grad_hidden = sum(
        reverse_matmul_answer(grad_forecast[part], head_whole[part][:, two:])
        for part in range(group)
    )
    unused_head, head_pull = jax.vjp(jax.nn.silu, head_pre)
    grad_head_pre = head_pull(grad_hidden)[0].astype(jnp.bfloat16)
    grad_resid = sum(
        reverse_matmul_answer(
            jnp.concatenate(
                [
                    grad_head_pre[:, part * group_width : (part + 1) * group_width],
                    grad_forecast[part],
                ],
                axis=1,
            ),
            head_whole[part][:, :two],
        )
        for part in range(group)
    )
    grad_forecast_rows = jnp.concatenate([grad_forecast[part] for part in range(group)], axis=1)
    head_bias_rows = (
        jnp.sum(grad_head_pre.astype(jnp.float32), axis=0),
        jnp.sum(grad_forecast_rows.astype(jnp.float32), axis=0),
    )
    head_products = RowSums(
        *pair_products(
            me,
            [
                (top, grad_head_pre),
                (top, grad_forecast_rows),
                (head_hidden, grad_forecast_rows),
            ],
        )
    )
    gain_sums = [[None, None] for _ in range(layer_count)]

    def rest_stage(layer_index, carry):
        outs = layers[layer_index].rest_backward(carry["grad"])
        carry = {"middle": outs[0], "mixed": outs[1]}
        gain_sums[layer_index][1] = outs[4]
        return carry, RowSums(*pair_products(me, list(zip(outs[2], outs[3], strict=True))))

    def entry_stage(layer_index, carry):
        outs = layers[layer_index].entry_backward(carry["middle"], carry["mixed"])
        gain_sums[layer_index][0] = outs[3]
        return {"grad": outs[0]}, RowSums(*pair_products(me, [(outs[1], outs[2])]))

    def input_stage(carry):
        grad_entry = carry["grad"].astype(jnp.bfloat16)
        grad_entry_outer = dyadic_accumulation(entry_hidden, grad_entry)
        grad_entry_outer_bias = jnp.sum(grad_entry.astype(jnp.float32), axis=0)
        grad_entry_skip = dyadic_accumulation(features, grad_entry)
        unused_entry, entry_pull = jax.vjp(jax.nn.silu, entry_pre)
        grad_entry_pre = entry_pull(reverse_matmul_answer(grad_entry, intake_emit_matrix))[0].astype(
            jnp.bfloat16
        )
        grad_entry_inner = dyadic_accumulation(features, grad_entry_pre)
        grad_entry_inner_bias = jnp.sum(grad_entry_pre.astype(jnp.float32), axis=0)
        grad_features = reverse_matmul_answer(
            grad_entry_pre, intake_latent_matrix
        ) + reverse_matmul_answer(grad_entry, intake_shortcut_matrix)
        values_grad = jnp.where(pad_mask, 0.0, grad_features[:, :patch_len])
        extra_rows = jnp.concatenate(
            [
                grad_entry_inner,
                grad_entry_skip,
                grad_entry_inner_bias[None],
                grad_entry_outer_bias[None],
            ]
            + [row[None] for row in head_bias_rows]
            + [row[None] for pair in gain_sums for row in pair],
            axis=0,
        )
        return values_grad, extra_rows.shape[0], entry_products(me, grad_entry_outer, extra_rows)

    parts = (head_products.sent, head_products.later, head_products.own)
    grad_resid, parts = lax.optimization_barrier((grad_resid, parts))
    head_products.sent, head_products.later, head_products.own = parts
    carry = {"grad": grad_resid}
    sums = [[head_products]]
    stages = []
    for layer_index in reversed(range(layer_count)):
        stages += [(rest_stage, layer_index), (entry_stage, layer_index)]
    finished = []
    stage_count = len(stages)
    for number in range(stage_count + 1):
        step = {"carry": carry}
        step["first"] = [chunk.first() for chunk in sums[number]]
        if number >= 1:
            step["last"] = [chunk.last() for chunk in sums[number - 1]]
        if number >= 2:
            total = sums[number - 2][0].total()
            step["total"] = sum_columns(total) if number == 2 else sum_group(total)
        if number < stage_count:
            stage, layer_index = stages[number]
            step["carry"], products = stage(layer_index, carry)
            sums.append([products])
            if number == stage_count - 1:
                values_grad, extra_count, entry_sum = input_stage(step["carry"])
                sums[-1].append(entry_sum)
            step["next"] = [(chunk.sent, chunk.later, chunk.own) for chunk in sums[-1]]
        step = lax.optimization_barrier(step)
        carry = step["carry"]
        for chunk, met in zip(sums[number], step["first"], strict=True):
            chunk.met = met
        if number >= 1:
            for chunk, met in zip(sums[number - 1], step["last"], strict=True):
                chunk.last_met = met
        if number >= 2:
            finished.append(step["total"])
        if number < stage_count:
            for chunk, parts in zip(sums[-1], step["next"], strict=True):
                chunk.sent, chunk.later, chunk.own = parts
    entry_chunk = sums[-1][1]
    entry_chunk.last_met = entry_chunk.last()
    sums[-1][0].last_met = sums[-1][0].last()
    finished.append(sum_group_at_once(sums[-2][0].total()))
    finished.append(sum_group_at_once(sums[-1][0].total()))
    head_sums = gather_blocks(me, finished[0]).astype(jnp.float32)
    layer_sums = [None] * layer_count
    for member, layer_index in enumerate(reversed(range(layer_count))):
        rest = finished[1 + 2 * member].astype(jnp.float32)
        entry = finished[2 + 2 * member].astype(jnp.float32)
        layer_sums[layer_index] = (entry[0], rest[0], rest[1], rest[2])
    entry_main, entry_extra = entry_everywhere(me, entry_chunk.total(), own_count, extra_count)
    inner_rows = 2 * patch_len
    last = 2 * inner_rows
    entry_sums = (
        entry_extra[:inner_rows],
        entry_extra[last],
        entry_main,
        entry_extra[last + 1],
        entry_extra[inner_rows:last],
    )
    head_bias_sums = lax.dynamic_slice_in_dim(
        entry_extra[last + 2 : last + 4], group_place * group_width, group_width, 1
    )
    own_place = (me * group + group_place) * own_count
    gains_grad = lax.dynamic_slice_in_dim(
        entry_extra[last + 4 : last + 4 + 2 * layer_count], own_place, own_count, 1
    ).reshape(layer_count, 2, own_count)
    qkv_grad = jnp.stack([layer_sums[member][0] for member in range(layer_count)])
    out_grad = jnp.stack([layer_sums[member][1] for member in range(layer_count)])
    up_grad = jnp.stack([layer_sums[member][2] for member in range(layer_count)])
    down_grad = jnp.stack([layer_sums[member][3] for member in range(layer_count)])
    return (
        token_predictions,
        values_grad,
        entry_sums[0],
        entry_sums[1],
        entry_sums[2],
        entry_sums[3],
        entry_sums[4],
        qkv_grad,
        out_grad,
        up_grad,
        down_grad,
        gains_grad,
        head_sums[0],
        head_bias_sums[0],
        head_sums[2],
        head_bias_sums[1],
        head_sums[1],
    )


def solution(mesh):
    return jax.shard_map(
        body,
        mesh=mesh,
        in_specs=(
            P(("dp", "head"), None),
            P(("dp", "head"), None),
            P(("dp", "head"), None),
            P(),
            P(),
            P(),
            P(),
            P(),
            P(None, ("dp", "head"), None),
            P(None, ("dp", "head"), None),
            P(None, ("dp", "head"), None),
            P(None, ("dp", "head"), None),
            P(None, None, ("dp", "head")),
            P(None, "head"),
            P("head"),
            P(None, "head"),
            P("head"),
            P(None, "head"),
            P("dp", "head"),
        ),
        out_specs=(
            P("dp", "head"),
            P(("dp", "head"), None),
            P(),
            P(),
            P(),
            P(),
            P(),
            P(None, ("dp", "head"), None),
            P(None, ("dp", "head"), None),
            P(None, ("dp", "head"), None),
            P(None, ("dp", "head"), None),
            P(None, None, ("dp", "head")),
            P(None, "head"),
            P("head"),
            P(None, "head"),
            P("head"),
            P(None, "head"),
        ),
        check_vma=False,
    )
```

```python
from functools import partial
import math

import jax
import jax.numpy as jnp
from jax import lax
from jax.experimental import pallas as pl
from jax.experimental.pallas import tpu as pltpu
from jax.sharding import PartitionSpec as P

MODEL_WIDTH = 1280
HEADS = 16
HEAD_DIM = 80


EPS = 1e-06
SMALL_COST = pl.CostEstimate(flops=1, bytes_accessed=1, transcendentals=0)
ROPE_BASE = 10000.0


def layout_rows(series_row, pad_row, patch_len):
    count = series_row.shape[0]
    order = jnp.arange(count, dtype=jnp.int32)
    same_series = series_row[:, None] == series_row[None, :]
    earlier = order[None, :] < order[:, None]
    position = jnp.sum(jnp.logical_and(same_series, earlier).astype(jnp.int32), axis=1)
    numbers = jnp.arange(pad_row.shape[0], dtype=jnp.int32)
    series_pad = jnp.sum(
        jnp.where(series_row[:, None] == numbers[None, :], pad_row[None, :], 0), axis=1
    )
    pad_count = jnp.where(position == 0, series_pad, 0)
    padded = pad_count == patch_len
    diagonal = order[:, None] == order[None, :]
    reach = jnp.logical_or(jnp.logical_and(earlier, jnp.logical_not(padded)[None, :]), diagonal)
    allowed = jnp.logical_and(same_series, reach)
    keep_rows = jnp.where(padded, 0.0, 1.0).astype(jnp.float32)
    return (position, pad_count, allowed, keep_rows)


def rotary_tables(position, head_dim):
    half = head_dim // 2
    steps = jnp.arange(half, dtype=jnp.float32) / half
    inverse = jnp.exp(-math.log(ROPE_BASE) * steps)
    angles = position.astype(jnp.float32)[:, None] * inverse[None, :]
    return (jnp.cos(angles)[:, None, :], jnp.sin(angles)[:, None, :])


def rotate(heads_rows, cosine, sine):
    half = heads_rows.shape[-1] // 2
    first = heads_rows[..., :half]
    second = heads_rows[..., half:]
    return jnp.concatenate(
        [first * cosine - second * sine, second * cosine + first * sine], axis=-1
    )


def unrotate(grad_rows, cosine, sine):
    half = grad_rows.shape[-1] // 2
    first = grad_rows[..., :half]
    second = grad_rows[..., half:]
    return jnp.concatenate(
        [first * cosine + second * sine, second * cosine - first * sine], axis=-1
    )


def norm_apply(resid, gain):
    return resid * lax.rsqrt(jnp.mean(resid * resid, axis=-1, keepdims=True) + EPS) * gain


def dyadic_accumulation(left, right):
    return lax.dot_general(
        left, right, (((0,), (0,)), ((), ())), preferred_element_type=jnp.float32
    )


def reverse_matmul_answer(grad_rows, weight):
    return lax.dot_general(
        grad_rows, weight, (((1,), (1,)), ((), ())), preferred_element_type=jnp.float32
    )


def masked_scores(query_rows, key_rows, allowed):
    scale = 1.0 / math.sqrt(query_rows.shape[-1])
    scores = (
        jnp.einsum("qhd,khd->hqk", query_rows, key_rows, preferred_element_type=jnp.float32) * scale
    )
    return jnp.where(allowed[None], scores, -1e30)


def attend_forward(query_rows, key_rows, value_rows, allowed):
    scores = masked_scores(query_rows, key_rows, allowed)
    peak = jnp.max(scores, axis=-1, keepdims=True)
    weights = jnp.exp(scores - peak)
    total = jnp.sum(weights, axis=-1, keepdims=True)
    probs = (weights / total).astype(jnp.bfloat16)
    mixed = jnp.einsum("hqk,khd->qhd", probs, value_rows, preferred_element_type=jnp.float32)
    return (mixed, peak + jnp.log(total))


def attend_backward(query_rows, key_rows, value_rows, allowed, log_total, grad_mixed):
    scale = 1.0 / math.sqrt(query_rows.shape[-1])
    scores = masked_scores(query_rows, key_rows, allowed)
    probs = jnp.where(allowed[None], jnp.exp(scores - log_total), 0.0)
    grad_probs = jnp.einsum(
        "qhd,khd->hqk", grad_mixed, value_rows, preferred_element_type=jnp.float32
    )
    grad_values = jnp.einsum(
        "hqk,qhd->khd", probs.astype(jnp.bfloat16), grad_mixed, preferred_element_type=jnp.float32
    )
    center = jnp.sum(grad_probs * probs, axis=-1, keepdims=True)
    grad_scores = (probs * (grad_probs - center)).astype(jnp.bfloat16)
    grad_query = (
        jnp.einsum("hqk,khd->qhd", grad_scores, key_rows, preferred_element_type=jnp.float32)
        * scale
    )
    grad_keys = (
        jnp.einsum("hqk,qhd->khd", grad_scores, query_rows, preferred_element_type=jnp.float32)
        * scale
    )
    return (grad_query, grad_keys, grad_values)


def after(value, *earlier):
    return lax.optimization_barrier((value, *earlier))[0]


def swap(v, bit):
    size = lax.axis_size("dp")
    return lax.ppermute(v, "dp", [(i, i ^ (1 << bit)) for i in range(size)])


def outer_groups():
    size = lax.axis_size("dp")
    return [[j + 8 * o for o in range(size // 8)] for j in range(8)]


def place_kernel(plan, piece_count, out_count, me_ref, *refs):
    pieces = refs[:piece_count]
    outs = refs[piece_count : piece_count + out_count]
    held = refs[piece_count + out_count : piece_count + 2 * out_count]
    in_sems, out_sems = refs[piece_count + 2 * out_count :]
    inward, outward = [], []
    for n, (piece, rel, row, out, column) in enumerate(plan):
        source = pieces[piece]
        width = held[out].shape[-1]
        if width != source.shape[-1]:
            source = source.at[:, :, pl.ds(column, width)]
        spot = (slice(None), me_ref[0] ^ rel, pl.ds(row, source.shape[1]), slice(None))
        inward.append(pltpu.make_async_copy(source, held[out].at[spot], in_sems.at[n]))
        outward.append(
            pltpu.make_async_copy(held[out].at[spot], outs[out].at[spot], out_sems.at[n])
        )
    for copy in inward:
        copy.start()
    for copy, onward in zip(inward, outward):
        copy.wait()
        onward.start()
    for onward in outward:
        onward.wait()


def place(me, pieces, widths, first=0):
    plan = []
    for n, (rel, row, _) in enumerate(pieces):
        column = first
        for out, width in enumerate(widths):
            plan.append((n, rel, row, out, column))
            column += width
    arrays = [array for _, _, array in pieces]
    lead, rows, _ = arrays[0].shape
    kind = arrays[0].dtype
    total = sum(8 * lead * rows * -(-w // 128) * 128 for w in widths) * 2
    outs = pl.pallas_call(
        partial(place_kernel, plan, len(arrays), len(widths)),
        out_shape=[jax.ShapeDtypeStruct((lead, 8, rows, w), kind) for w in widths],
        in_specs=[pl.BlockSpec(memory_space=pltpu.SMEM)]
        + [pl.BlockSpec(memory_space=pl.ANY)] * len(arrays),
        out_specs=[pl.BlockSpec(memory_space=pl.ANY)] * len(widths),
        scratch_shapes=[pltpu.VMEM((lead, 8, rows, w), kind) for w in widths]
        + [pltpu.SemaphoreType.DMA((len(plan),))] * 2,
        compiler_params=pltpu.CompilerParams(vmem_limit_bytes=total + (4 << 20)),
        cost_estimate=SMALL_COST,
    )(me, *arrays)
    outer = lax.axis_size("dp") // 8
    return [o.reshape(-1, outer * 8 * rows, o.shape[-1]) for o in outs]


def row_half(rows):
    return rows // 32 * 16 if rows >= 32 else rows // 2


def second_step(held, from_x, from_y):
    half = row_half(held.shape[1])
    return from_y[:, :half], from_x[:, half:]


def all_pieces(near, far, near_met, far_met):
    half = far[0].shape[1]
    places = ((0, 0), (2, 0), (4, 0), (6, 0), (6, half))
    pieces = []
    for (rel, row), array, met in zip(places, (*near, *far), (*near_met, *far_met), strict=True):
        pieces += [(rel, row, array), (rel | 1, row, met)]
    return pieces


def spread_rows(held):
    near = (held, swap(held, 1), swap(held, 2))
    onward_x, onward_y = second_step(*near)
    far = (swap(onward_x, 1), swap(onward_y, 2))
    return all_pieces(near, far, [swap(part, 0) for part in near], [swap(part, 0) for part in far])


def gather_head(own):
    held = lax.all_gather(own, "head", axis=0, tiled=True)[None]
    if lax.axis_size("dp") > 8:
        held = lax.all_gather(
            held, "dp", axis=0, tiled=True, axis_index_groups=outer_groups()
        )
    return held


def pick(rows, place, width):
    picked = rows[:, :width]
    for n in range(1, rows.shape[1] // width):
        picked = jnp.where(place == n, rows[:, n * width : (n + 1) * width], picked)
    return picked


def product_kernel(count, outer, me_ref, *refs):
    lefts, rights, met_lefts, met_rights = (refs[n * count : (n + 1) * count] for n in range(4))
    to_x, to_y, later, own, right_pair = refs[4 * count :]
    rows, width = own.shape[1] // outer, own.shape[-1]
    tokens = lefts[0].shape[0]
    half = width // 2
    for n in range(count):
        left, met = lefts[n][...], met_lefts[n][...]
        right_pair[:tokens] = rights[n][...]
        right_pair[tokens:] = met_rights[n][...]
        for rel in range(4):
            place = me_ref[0] ^ (2 * rel)
            for part in range(outer):
                block = slice(part * 8 * rows, (part + 1) * 8 * rows)
                left_pair = jnp.concatenate(
                    [pick(left[:, block], place, rows), pick(met[:, block], place, rows)], axis=0
                )
                total = dyadic_accumulation(left_pair, right_pair[...]).astype(own.dtype)
                one, two = total[:, :half], total[:, half:]
                span = slice(part * rows, (part + 1) * rows)
                if rel == 0:
                    own[n, span] = total
                elif rel == 1:
                    to_x[1, n, span] = one
                    later[1, n, span] = two
                elif rel == 2:
                    later[0, n, span] = one
                    to_y[1, n, span] = two
                else:
                    to_x[0, n, span] = one
                    to_y[0, n, span] = two


def pair_products(me, pairs):
    outer = lax.axis_size("dp") // 8
    met = {}
    for pair in pairs:
        for rows in pair:
            if id(rows) not in met:
                met[id(rows)] = swap(rows, 0)
    lefts = [left for left, _ in pairs]
    rights = [right for _, right in pairs]
    count = len(pairs)
    block, width = lefts[0].shape[1] // 8, rights[0].shape[1]
    low = jnp.bfloat16
    return pl.pallas_call(
        partial(product_kernel, count, outer),
        out_shape=[
            jax.ShapeDtypeStruct((2, count, block, width // 2), low),
            jax.ShapeDtypeStruct((2, count, block, width // 2), low),
            jax.ShapeDtypeStruct((2, count, block, width // 2), low),
            jax.ShapeDtypeStruct((count, block, width), low),
        ],
        in_specs=[pl.BlockSpec(memory_space=pltpu.SMEM)]
        + [pl.BlockSpec(memory_space=pltpu.VMEM)] * (4 * count),
        out_specs=[pl.BlockSpec(memory_space=pltpu.VMEM)] * 4,
        scratch_shapes=[pltpu.VMEM((2 * lefts[0].shape[0], width), low)],
        compiler_params=pltpu.CompilerParams(vmem_limit_bytes=44 << 20),
        cost_estimate=SMALL_COST,
    )(
        (me & 7).reshape(1),
        *lefts,
        *rights,
        *[met[id(left)] for left in lefts],
        *[met[id(right)] for right in rights],
    )


def low_sum(*parts):
    total = parts[0].astype(jnp.float32)
    for part in parts[1:]:
        total = total + part.astype(jnp.float32)
    return total.astype(jnp.bfloat16)


class RowSums:
    def __init__(self, to_x, to_y, later, own):
        self.sent, self.later, self.own = (to_x, to_y), later, own

    def first(self):
        return swap(self.sent[0], 1), swap(self.sent[1], 2)

    def last(self):
        return (
            swap(low_sum(self.later[0], self.met[0][0]), 2),
            swap(low_sum(self.later[1], self.met[1][0]), 1),
        )

    def total(self):
        half = self.own.shape[-1] // 2
        return jnp.concatenate(
            [
                low_sum(self.own[..., :half], self.met[0][1], self.last_met[0]),
                low_sum(self.own[..., half:], self.met[1][1], self.last_met[1]),
            ],
            axis=-1,
        )


def sum_group(total):
    outer = lax.axis_size("dp") // 8
    group = lax.axis_size("head")
    lead = total.shape[:-2]
    rows, columns = total.shape[-2:]
    if outer > 1:
        total = lax.psum_scatter(
            total.reshape(*lead, outer, rows // outer, columns),
            "dp",
            scatter_dimension=len(lead),
            tiled=True,
            axis_index_groups=outer_groups(),
        )
    total = total.reshape(*lead, rows // outer, columns)
    return lax.psum_scatter(total, "head", scatter_dimension=len(lead), tiled=True)


def sum_group_at_once(total):
    outer = lax.axis_size("dp") // 8
    group = lax.axis_size("head")
    if outer > 1:
        return sum_group(total).astype(jnp.float32)
    lead = total.shape[:-2]
    rows, columns = total.shape[-2:]
    total = total.reshape(*lead, group, rows // group, columns)
    axis = len(lead)
    met = lax.all_to_all(total, "head", split_axis=axis, concat_axis=axis, tiled=True)
    return jnp.sum(met.astype(jnp.float32), axis=axis)


def sum_columns(total):
    group = lax.axis_size("head")
    count, rows, columns = total.shape
    total = jnp.moveaxis(total.reshape(count, rows, group, columns // group), 2, 0)
    return lax.psum_scatter(total, "head", scatter_dimension=0, tiled=True)[0]


def gather_blocks(me, summed):
    outer = lax.axis_size("dp") // 8
    count, rows, columns = summed.shape
    held = summed.reshape(count * outer, rows // outer, columns)
    return place((me & 7).reshape(1), spread_rows(held), [columns])[0]


EXTRA_ROWS = 8


def entry_products(me, main, extra):
    group = lax.axis_size("head")
    outer = lax.axis_size("dp") // 8
    devices = 8 * outer * group
    columns = main.shape[1]
    own = main.shape[0] // devices
    extra = jnp.pad(extra, ((0, EXTRA_ROWS * devices - extra.shape[0]), (0, 0)))
    rows = jnp.concatenate(
        [main.reshape(devices, own, columns), extra.reshape(devices, EXTRA_ROWS, columns)], axis=1
    ).astype(jnp.bfloat16)
    view = rows.reshape(outer, 4, 2, group * (own + EXTRA_ROWS), columns)
    core = me & 1
    other = lax.dynamic_index_in_dim(view, 1 - core, 2, keepdims=False)
    pair = low_sum(lax.dynamic_index_in_dim(view, core, 2, keepdims=False), swap(other, 0))
    chip = (me & 7) >> 1
    half = columns // 2

    def picked(rel):
        return lax.dynamic_index_in_dim(pair, chip ^ rel, 1, keepdims=False).reshape(-1, columns)

    own_rows, at_x, at_y, far = (picked(rel) for rel in range(4))
    return RowSums(
        jnp.stack([far[:, :half], at_x[:, :half]]),
        jnp.stack([far[:, half:], at_y[:, half:]]),
        (at_y[:, :half], at_x[:, half:]),
        own_rows,
    )


def entry_kernel(plan, own, me_ref, *refs):
    pieces = refs[: len(plan)]
    main_ref, extra_ref, held, sems = refs[len(plan) :]
    copies = []
    for n, (rel, row, rows) in enumerate(plan):
        spot = held.at[me_ref[0] ^ rel, pl.ds(row, rows)]
        copies.append(pltpu.make_async_copy(pieces[n].at[0], spot, sems.at[n]))
    for copy in copies:
        copy.start()
    for copy in copies:
        copy.wait()
    span = own + EXTRA_ROWS
    group = held.shape[1] // span
    for block in range(8):
        rows = held[block].astype(jnp.float32)
        for member in range(group):
            main_ref[block * group + member] = rows[member * span : member * span + own]
            extra_ref[block * group + member] = rows[member * span + own : (member + 1) * span]


def entry_everywhere(me, total, own, count):
    columns = total.shape[1]
    outer = lax.axis_size("dp") // 8
    if outer > 1:
        held = gather_head(sum_group(total))
    else:
        held = lax.psum(total, "head")[None]
    pieces = spread_rows(held)
    places = (me & 7).reshape(1)
    span = own + EXTRA_ROWS
    if held.shape[0] > 1 or own % 8 or not in_kernel(pieces):
        (whole,) = place(places, pieces, [columns])
        whole = whole.reshape(-1, span, columns).astype(jnp.float32)
        return whole[:, :own].reshape(-1, columns), whole[:, own:].reshape(-1, columns)[:count]
    rows = held.shape[1]
    blocks = 8 * rows // span
    plan = [(rel, row, array.shape[1]) for rel, row, array in pieces]
    vmem = pl.BlockSpec(memory_space=pltpu.VMEM)
    main, extra = pl.pallas_call(
        partial(entry_kernel, plan, own),
        out_shape=[
            jax.ShapeDtypeStruct((blocks, own, columns), jnp.float32),
            jax.ShapeDtypeStruct((blocks, EXTRA_ROWS, columns), jnp.float32),
        ],
        in_specs=[pl.BlockSpec(memory_space=pltpu.SMEM)]
        + [pl.BlockSpec(memory_space=pl.ANY)] * len(pieces),
        out_specs=[vmem, vmem],
        scratch_shapes=[
            pltpu.VMEM((8, rows, columns), held.dtype),
            pltpu.SemaphoreType.DMA((len(pieces),)),
        ],
        compiler_params=pltpu.CompilerParams(vmem_limit_bytes=44 << 20),
        cost_estimate=SMALL_COST,
    )(places, *[array for _, _, array in pieces])
    return main.reshape(-1, columns), extra.reshape(-1, columns)[:count]


def fetch(plan, me, pieces, whole, sems):
    groups = []
    for group in range(whole.shape[1] // MODEL_WIDTH):
        columns = pl.ds(group * MODEL_WIDTH, MODEL_WIDTH)
        copies = []
        for n, (rel, row, rows) in enumerate(plan):
            first = pl.multiple_of((me ^ rel) * (whole.shape[0] // 8) + row, 16)
            copies.append(
                pltpu.make_async_copy(
                    pieces[n].at[0, :, columns],
                    whole.at[pl.ds(first, rows), columns],
                    sems.at[group * len(plan) + n],
                )
            )
        for copy in copies:
            copy.start()
        groups.append(copies)
    return groups


def arrive(copies):
    for copy in copies:
        copy.wait()


def rows_times(left, whole, first, out, tile):
    def step(n, _):
        at = pl.multiple_of(n * tile, 128)
        out[:, pl.ds(at, tile)] = jnp.dot(
            left, whole[:, pl.ds(first + at, tile)], preferred_element_type=jnp.float32
        )
        return 0

    lax.fori_loop(0, out.shape[1] // tile, step, 0)


def rows_times_turned(left, whole, first, width, out, tile):
    def step(n, _):
        at = pl.multiple_of(n * tile, 128)
        part = reverse_matmul_answer(whole[pl.ds(at, tile), pl.ds(first, width)], left)
        out[:, pl.ds(at, tile)] = part.T
        return 0

    lax.fori_loop(0, out.shape[1] // tile, step, 0)


def inverse_norm(rows):
    return lax.rsqrt(jnp.mean(rows * rows, axis=-1, keepdims=True) + EPS)


def other_half(rows):
    half = HEAD_DIM // 2
    lane = lax.broadcasted_iota(jnp.int32, rows.shape, 1) % HEAD_DIM
    ahead = pltpu.roll(rows, rows.shape[1] - half, 1)
    behind = pltpu.roll(rows, half, 1)
    return jnp.where(lane < half, ahead, behind)


def head_window(head, width):
    first = head * HEAD_DIM // 128 * 128
    last = min(-(-(head + 1) * HEAD_DIM // 128) * 128, width)
    start = head * HEAD_DIM - first
    lane = lax.broadcasted_iota(jnp.int32, (1, last - first), 1)
    return slice(first, last), jnp.logical_and(lane >= start, lane < start + HEAD_DIM)


def entry_forward_kernel(plan, me_ref, resid_ref, gain_ref, cosine_ref, sine_ref, allowed_ref, *refs):
    pieces = refs[: len(plan)]
    normed_ref, query_ref, key_ref, value_ref, total_ref, mixed_ref = refs[len(plan) : len(plan) + 6]
    whole, wide, sems = refs[len(plan) + 6 :]
    groups = fetch(plan, me_ref[0], pieces, whole, sems)
    resid = resid_ref[...]
    normed = (resid * inverse_norm(resid) * gain_ref[...]).astype(jnp.bfloat16)
    normed_ref[...] = normed
    for group, out in enumerate((query_ref, key_ref, value_ref)):
        arrive(groups[group])
        rows_times(normed, whole, group * MODEL_WIDTH, wide, 256)
        rows = wide[...]
        if group < 2:
            rows = rows * cosine_ref[...] + other_half(rows) * sine_ref[...]
        out[...] = rows.astype(jnp.bfloat16)
    scale = 1.0 / math.sqrt(HEAD_DIM)
    allowed = allowed_ref[...] > 0.0
    wide[...] = jnp.zeros_like(wide)
    totals = jnp.zeros(total_ref.shape, jnp.float32)
    head_lane = lax.broadcasted_iota(jnp.int32, total_ref.shape, 1)
    for head in range(HEADS):
        window, inside = head_window(head, MODEL_WIDTH)
        query = jnp.where(inside, query_ref[:, window], 0)
        scores = reverse_matmul_answer(query, key_ref[:, window]) * scale
        scores = jnp.where(allowed, scores, -1e30)
        peak = jnp.max(scores, axis=-1, keepdims=True)
        weights = jnp.exp(scores - peak)
        total = jnp.sum(weights, axis=-1, keepdims=True)
        probs = (weights / total).astype(jnp.bfloat16)
        mixed = jnp.dot(probs, value_ref[:, window], preferred_element_type=jnp.float32)
        wide[:, window] += jnp.where(inside, mixed, 0.0)
        totals = jnp.where(head_lane == head, peak + jnp.log(total), totals)
    total_ref[...] = totals
    mixed_ref[...] = wide[...].astype(jnp.bfloat16)


def gelu_parts(x):
    root = math.sqrt(2.0 / math.pi)
    bend = jnp.tanh(root * (x + 0.044715 * (x * x * x)))
    slope = 0.5 * (1.0 + bend) + 0.5 * x * (1.0 - bend * bend) * root * (
        1.0 + 3.0 * 0.044715 * (x * x)
    )
    return 0.5 * x * (1.0 + bend), slope


def rest_forward_kernel(plan, me_ref, resid_ref, mixed_ref, gain_ref, *refs):
    pieces = refs[: len(plan)]
    result_ref, middle_ref, normed_ref, pre_ref = refs[len(plan) : len(plan) + 4]
    whole, sems = refs[len(plan) + 4 :]
    groups = fetch(plan, me_ref[0], pieces, whole, sems)
    arrive(groups[0])
    rows_times(mixed_ref[...], whole, 0, middle_ref, 256)
    middle = resid_ref[...] + middle_ref[...]
    middle_ref[...] = middle
    normed = (middle * inverse_norm(middle) * gain_ref[...]).astype(jnp.bfloat16)
    normed_ref[...] = normed
    arrive(groups[1])
    rows_times(normed, whole, MODEL_WIDTH, pre_ref, 256)
    act = gelu_parts(pre_ref[...])[0].astype(jnp.bfloat16)
    arrive(groups[2])
    rows_times(act, whole, 2 * MODEL_WIDTH, result_ref, 256)
    result_ref[...] += middle_ref[...]


def norm_back(rows, gain, grad):
    inverse = inverse_norm(rows)
    scaled = grad * gain
    mean = jnp.mean(rows * scaled, axis=-1, keepdims=True)
    sent = inverse * scaled - rows * (inverse * inverse * inverse * mean)
    return sent, jnp.sum(grad * rows * inverse, axis=0, keepdims=True)


def rest_backward_kernel(plan, me_ref, grad_ref, middle_ref, pre_ref, gain_ref, *refs):
    pieces = refs[: len(plan)]
    outs = refs[len(plan) : len(plan) + 7]
    grad_middle_ref, mixed_ref, attn_ref, grad_pre_ref, branch_ref, act_ref, gain_grad_ref = outs
    whole, wide, sems = refs[len(plan) + 7 :]
    groups = fetch(plan, me_ref[0], pieces, whole, sems)
    grad = grad_ref[...]
    branch = grad.astype(jnp.bfloat16)
    branch_ref[...] = branch
    arrive(groups[2])
    rows_times_turned(branch, whole, 2 * MODEL_WIDTH, MODEL_WIDTH, wide, 256)
    act, slope = gelu_parts(pre_ref[...])
    act_ref[...] = act.astype(jnp.bfloat16)
    grad_pre = (wide[...] * slope).astype(jnp.bfloat16)
    grad_pre_ref[...] = grad_pre
    arrive(groups[1])
    rows_times_turned(grad_pre, whole, MODEL_WIDTH, MODEL_WIDTH, wide, 256)
    sent, gain_grad_ref[...] = norm_back(middle_ref[...], gain_ref[...], wide[...])
    grad_middle = grad + sent
    grad_middle_ref[...] = grad_middle
    attn = grad_middle.astype(jnp.bfloat16)
    attn_ref[...] = attn
    arrive(groups[0])
    rows_times_turned(attn, whole, 0, MODEL_WIDTH, wide, 256)
    mixed_ref[...] = wide[...].astype(jnp.bfloat16)


def entry_backward_kernel(
    plan,
    me_ref,
    grad_middle_ref,
    grad_mixed_ref,
    resid_ref,
    query_ref,
    key_ref,
    value_ref,
    total_ref,
    gain_ref,
    cosine_ref,
    sine_ref,
    allowed_ref,
    *refs,
):
    pieces = refs[: len(plan)]
    grad_resid_ref, projected_ref, gain_grad_ref = refs[len(plan) : len(plan) + 3]
    whole, grad_query, grad_key, grad_value, sems = refs[len(plan) + 3 :]
    groups = fetch(plan, me_ref[0], pieces, whole, sems)
    scale = 1.0 / math.sqrt(HEAD_DIM)
    allowed = allowed_ref[...] > 0.0
    totals = total_ref[...]
    grad_query[...] = jnp.zeros_like(grad_query)
    grad_key[...] = jnp.zeros_like(grad_key)
    grad_value[...] = jnp.zeros_like(grad_value)
    for head in range(HEADS):
        window, inside = head_window(head, MODEL_WIDTH)
        query = jnp.where(inside, query_ref[:, window], 0)
        keys = key_ref[:, window]
        grad_mixed = jnp.where(inside, grad_mixed_ref[:, window], 0)
        scores = reverse_matmul_answer(query, keys) * scale
        probs = jnp.where(allowed, jnp.exp(scores - totals[:, head : head + 1]), 0.0)
        grad_probs = reverse_matmul_answer(grad_mixed, value_ref[:, window])
        grad_value[:, window] += dyadic_accumulation(probs.astype(jnp.bfloat16), grad_mixed)
        center = jnp.sum(grad_probs * probs, axis=-1, keepdims=True)
        grad_scores = (probs * (grad_probs - center)).astype(jnp.bfloat16)
        along = jnp.dot(grad_scores, keys, preferred_element_type=jnp.float32)
        grad_query[:, window] += jnp.where(inside, along * scale, 0.0)
        grad_key[:, window] += dyadic_accumulation(grad_scores, query) * scale
    for group, part in enumerate((grad_query, grad_key, grad_value)):
        rows = part[...]
        if group < 2:
            rows = rows * cosine_ref[...] - other_half(rows) * sine_ref[...]
        projected_ref[:, group * MODEL_WIDTH : (group + 1) * MODEL_WIDTH] = rows.astype(jnp.bfloat16)
    for copies in groups:
        arrive(copies)
    rows_times_turned(projected_ref[...], whole, 0, 3 * MODEL_WIDTH, grad_query, 256)
    sent, gain_grad_ref[...] = norm_back(resid_ref[...], gain_ref[...], grad_query[...])
    grad_resid_ref[...] = grad_middle_ref[...] + sent


def whole_call(kernel, me, pieces, inputs, outs, wides):
    rows = inputs[0].shape[0]
    plan = [(rel, row, array.shape[1]) for rel, row, array in pieces]
    blocks = 8 * pieces[0][2].shape[1]
    columns = 3 * MODEL_WIDTH
    vmem = pl.BlockSpec(memory_space=pltpu.VMEM)
    return pl.pallas_call(
        partial(kernel, plan),
        out_shape=[jax.ShapeDtypeStruct(shape, kind) for shape, kind in outs],
        in_specs=[pl.BlockSpec(memory_space=pltpu.SMEM)]
        + [vmem] * len(inputs)
        + [pl.BlockSpec(memory_space=pl.ANY)] * len(pieces),
        out_specs=[vmem] * len(outs),
        scratch_shapes=[pltpu.VMEM((blocks, columns), jnp.bfloat16)]
        + [pltpu.VMEM((rows, MODEL_WIDTH), jnp.float32)] * wides
        + [pltpu.SemaphoreType.DMA((3 * len(pieces),))],
        compiler_params=pltpu.CompilerParams(vmem_limit_bytes=44 << 20),
        cost_estimate=SMALL_COST,
    )(me, *inputs, *[array for _, _, array in pieces])


def in_kernel(pieces):
    lead, rows, _ = pieces[0][2].shape
    return lead == 1 and rows % 32 == 0


LOW, FULL = jnp.bfloat16, jnp.float32


class Layer:
    def __init__(self, places, entry_pieces, gains, tables, allowed):
        self.places, self.entry_pieces, self.gains = places, entry_pieces, gains
        self.tables, self.allowed = tables, allowed
        self.fetched = in_kernel(entry_pieces)
        if not self.fetched:
            self.entry_whole = place(places, entry_pieces, [3 * MODEL_WIDTH])[0][0]

    def add_rest(self, rest_pieces):
        self.rest_pieces = rest_pieces
        if not self.fetched:
            self.rest_whole = [part[0] for part in place(self.places, rest_pieces, [MODEL_WIDTH] * 3)]

    def shapes(self, *kinds):
        rows = self.allowed.shape[0]
        return [((rows, width), kind) for width, kind in kinds]

    def entry_forward(self, resid):
        if not self.fetched:
            self.saved = entry_forward(
                resid, self.entry_whole, self.gains, *self.tables[:2], self.allowed
            )
            return self.saved[6]
        wide = (MODEL_WIDTH, LOW)
        self.resid = resid
        outs = whole_call(
            entry_forward_kernel,
            self.places,
            self.entry_pieces,
            (resid, self.gains[:1].astype(FULL), *self.tables[2:], self.allowed.astype(FULL)),
            self.shapes(wide, wide, wide, wide, (128, FULL), wide),
            1,
        )
        self.normed_first, self.heads = outs[0], outs[1:5]
        return outs[5]

    def rest_forward(self, mixed):
        if not self.fetched:
            result, self.saved = rest_forward(
                (*self.saved[:6], mixed), *self.rest_whole, self.gains
            )
            return result
        self.mixed = mixed
        result, self.middle, self.normed_second, self.hidden_pre = whole_call(
            rest_forward_kernel,
            self.places,
            self.rest_pieces,
            (self.resid, mixed, self.gains[1:].astype(FULL)),
            self.shapes(
                (MODEL_WIDTH, FULL), (MODEL_WIDTH, FULL), (MODEL_WIDTH, LOW), (MODEL_WIDTH, FULL)
            ),
            0,
        )
        return result

    def rest_backward(self, grad):
        if not self.fetched:
            weights = (self.entry_whole, *self.rest_whole, self.gains)
            return rest_backward(self.saved, weights, grad)
        wide = (MODEL_WIDTH, LOW)
        grad_middle, grad_mixed, grad_attn, grad_pre, branch, act, gain_grad = whole_call(
            rest_backward_kernel,
            self.places,
            self.rest_pieces,
            (grad, self.middle, self.hidden_pre, self.gains[1:].astype(FULL)),
            self.shapes((MODEL_WIDTH, FULL), wide, wide, wide, wide, wide)
            + [((1, MODEL_WIDTH), FULL)],
            1,
        )
        lefts = (self.mixed, self.normed_second, act)
        return grad_middle, grad_mixed, lefts, (grad_attn, grad_pre, branch), gain_grad[0]

    def entry_backward(self, grad_middle, grad_mixed):
        if not self.fetched:
            weights = (self.entry_whole, *self.rest_whole, self.gains)
            return entry_backward(
                self.saved, weights, *self.tables[:2], self.allowed, grad_middle, grad_mixed
            )
        grad_resid, projected, gain_grad = whole_call(
            entry_backward_kernel,
            self.places,
            self.entry_pieces,
            (
                grad_middle,
                grad_mixed,
                self.resid,
                *self.heads,
                self.gains[:1].astype(FULL),
                *self.tables[2:],
                self.allowed.astype(FULL),
            ),
            self.shapes((MODEL_WIDTH, FULL), (3 * MODEL_WIDTH, LOW)) + [((1, MODEL_WIDTH), FULL)],
            3,
        )
        return grad_resid, self.normed_first, projected, gain_grad[0]


def entry_forward(resid, qkv_full, gain_pair, cosine, sine, allowed):
    gains = gain_pair.astype(jnp.float32)
    rows = resid.shape[0]
    normed_first = norm_apply(resid, gains[0]).astype(jnp.bfloat16)
    projected = jnp.dot(normed_first, qkv_full, preferred_element_type=jnp.float32)
    query_rows = rotate(
        projected[:, :MODEL_WIDTH].reshape(rows, HEADS, HEAD_DIM), cosine, sine
    ).astype(jnp.bfloat16)
    key_rows = rotate(
        projected[:, MODEL_WIDTH : 2 * MODEL_WIDTH].reshape(rows, HEADS, HEAD_DIM), cosine, sine
    ).astype(jnp.bfloat16)
    value_rows = projected[:, 2 * MODEL_WIDTH :].reshape(rows, HEADS, HEAD_DIM).astype(jnp.bfloat16)

    mixed, log_total = attend_forward(query_rows, key_rows, value_rows, allowed)
    mixed_low = mixed.reshape(rows, MODEL_WIDTH).astype(jnp.bfloat16)
    return (resid, normed_first, query_rows, key_rows, value_rows, log_total, mixed_low)


def rest_forward(saved, out_full, up_full, down_full, gain_pair):
    gains = gain_pair.astype(jnp.float32)
    resid, mixed_low = saved[0], saved[6]
    middle = resid + jnp.dot(mixed_low, out_full, preferred_element_type=jnp.float32)
    normed_second = norm_apply(middle, gains[1]).astype(jnp.bfloat16)
    hidden_pre = jnp.dot(normed_second, up_full, preferred_element_type=jnp.float32)
    hidden_act = jax.nn.gelu(hidden_pre, approximate=True).astype(jnp.bfloat16)
    result = middle + jnp.dot(hidden_act, down_full, preferred_element_type=jnp.float32)
    return (result, (*saved, middle, normed_second, hidden_pre))


def rest_backward(saved, weights, grad_result):
    mixed_low, middle, normed_second, hidden_pre = saved[6:]
    _, out_full, up_full, down_full, gain_pair = weights
    gains = gain_pair.astype(jnp.float32)
    grad_branch = grad_result.astype(jnp.bfloat16)
    hidden_act, gelu_pull = jax.vjp(partial(jax.nn.gelu, approximate=True), hidden_pre)
    hidden_low = hidden_act.astype(jnp.bfloat16)
    grad_act = reverse_matmul_answer(grad_branch, down_full)
    grad_pre = gelu_pull(grad_act)[0].astype(jnp.bfloat16)
    grad_normed_second = reverse_matmul_answer(grad_pre, up_full)
    unused_second, second_pull = jax.vjp(norm_apply, middle, gains[1])
    grad_middle_norm, grad_gain_second = second_pull(grad_normed_second)
    grad_middle = grad_result + grad_middle_norm
    grad_attn = grad_middle.astype(jnp.bfloat16)
    grad_mixed = reverse_matmul_answer(grad_attn, out_full).astype(jnp.bfloat16)
    left_rows = (mixed_low, normed_second, hidden_low)
    right_rows = (grad_attn, grad_pre, grad_branch)
    return (grad_middle, grad_mixed, left_rows, right_rows, grad_gain_second)


def entry_backward(saved, weights, cosine, sine, allowed, grad_middle, grad_mixed):
    resid, normed_first, query_rows, key_rows, value_rows, log_total = saved[:6]
    qkv_full = weights[0]
    gains = weights[4].astype(jnp.float32)
    rows = resid.shape[0]
    grad_query, grad_keys, grad_values = attend_backward(
        query_rows,
        key_rows,
        value_rows,
        allowed,
        log_total,
        grad_mixed.reshape(rows, HEADS, HEAD_DIM),
    )
    grad_query = unrotate(grad_query, cosine, sine).reshape(rows, MODEL_WIDTH)
    grad_keys = unrotate(grad_keys, cosine, sine).reshape(rows, MODEL_WIDTH)
    grad_values = grad_values.reshape(rows, MODEL_WIDTH)
    grad_projected = jnp.concatenate([grad_query, grad_keys, grad_values], axis=1).astype(
        jnp.bfloat16
    )
    grad_normed_first = reverse_matmul_answer(grad_projected, qkv_full)
    unused_first, first_pull = jax.vjp(norm_apply, resid, gains[0])
    grad_resid_norm, grad_gain_first = first_pull(grad_normed_first)
    return (grad_middle + grad_resid_norm, normed_first, grad_projected, grad_gain_first)


def body(
    patch_observations,
    sequence_labels,
    leading_filler_count,
    intake_latent_matrix,
    intake_latent_offset,
    intake_emit_matrix,
    intake_emit_offset,
    intake_shortcut_matrix,
    attention_entry_matrices,
    attention_merge_matrix,
    feedforward_widen_matrix,
    feedforward_shrink_matrix,
    layer_scale_factors,
    readout_latent_matrix,
    readout_latent_offset,
    readout_emit_matrix,
    readout_emit_offset,
    readout_shortcut_matrix,
    loss_sensitivity,
):
    patch_len = patch_observations.shape[1]
    position, pad_count, allowed, keep_rows = layout_rows(
        sequence_labels[0], leading_filler_count[0], patch_len
    )
    cosine, sine = rotary_tables(position, HEAD_DIM)
    columns = jnp.arange(patch_len, dtype=jnp.int32)
    pad_mask = columns[None, :] < pad_count[:, None]
    features = jnp.concatenate(
        [
            jnp.where(pad_mask, jnp.zeros_like(patch_observations), patch_observations),
            pad_mask.astype(jnp.bfloat16),
        ],
        axis=1,
    )
    entry_pre = (
        jnp.dot(features, intake_latent_matrix, preferred_element_type=jnp.float32)
        + intake_latent_offset
    )
    entry_hidden = jax.nn.silu(entry_pre).astype(jnp.bfloat16)
    resid = (
        jnp.dot(entry_hidden, intake_emit_matrix, preferred_element_type=jnp.float32)
        + intake_emit_offset
        + jnp.dot(features, intake_shortcut_matrix, preferred_element_type=jnp.float32)
    )
    layer_count = attention_entry_matrices.shape[0]
    group = lax.axis_size("head")
    group_place = lax.axis_index("head")
    outer = lax.axis_size("dp") // 8
    me = lax.axis_index("dp").astype(jnp.int32)
    places = (me & 7).reshape(1)
    own_count = layer_scale_factors.shape[2]
    rows = patch_observations.shape[0]

    group_width = readout_latent_offset.shape[0]
    offsets = jnp.stack([readout_latent_offset, readout_emit_offset])
    coarse = lax.reduce_precision(offsets, 8, 7)
    offset_rows = jnp.concatenate([coarse, offsets - coarse], axis=0).astype(jnp.bfloat16)
    offset_rows = jnp.pad(offset_rows, ((0, 12), (0, 0)))
    sent = jnp.concatenate(
        [
            loss_sensitivity.reshape(group, rows, group_width),
            jnp.broadcast_to(offset_rows[None], (group, 16, group_width)),
        ],
        axis=1,
    )
    gain_columns = layer_scale_factors.reshape(2 * layer_count, own_count).T
    gain_columns = jnp.pad(gain_columns, ((0, 0), (0, 128 - 2 * layer_count)))
    chunks = []
    for layer_index in range(layer_count):
        entry_own = attention_entry_matrices[layer_index]
        if layer_index == 0:
            entry_own = jnp.concatenate([entry_own, gain_columns], axis=1)
        chunks.append(entry_own)
        rest_own = jnp.concatenate(
            [
                attention_merge_matrix[layer_index],
                feedforward_widen_matrix[layer_index],
                feedforward_shrink_matrix[layer_index],
            ],
            axis=1,
        )
        chunks.append(rest_own)
    head_own = jnp.concatenate(
        [
            lax.dynamic_index_in_dim(
                matrix.reshape(outer, 8, -1, group_width), me % 8, 1, keepdims=False
            )
            for matrix in (readout_latent_matrix, readout_shortcut_matrix, readout_emit_matrix)
        ],
        axis=2,
    )
    chunks.append(head_own)
    count = len(chunks)

    def gather_chunk(number, own):
        if number < count - 1:
            return gather_head(own)
        return lax.all_gather(own, "head", axis=0, tiled=True)

    held = gather_chunk(0, chunks[0])
    cosine_wide = jnp.tile(jnp.concatenate([cosine[:, 0], cosine[:, 0]], axis=1), (1, HEADS))
    sine_wide = jnp.tile(jnp.concatenate([-sine[:, 0], sine[:, 0]], axis=1), (1, HEADS))
    tables = (cosine, sine, cosine_wide, sine_wide)
    nears, fars, near_mets = [], [], []
    layers = []
    onward = None
    for number in range(count + 1):
        step = {}
        if number < count:
            step["x"], step["y"] = swap(held, 1), swap(held, 2)
        if number + 1 < count:
            step["next"] = gather_chunk(number + 1, chunks[number + 1])
        if number == 0:
            step["resid"] = resid
            step["met"] = lax.all_to_all(
                after(sent, held), "head", split_axis=0, concat_axis=0, tiled=True
            )
        else:
            step["far"] = (swap(onward[0], 1), swap(onward[1], 2))
            near_mets.append([swap(part, 0) for part in after(nears[number - 1], onward)])
        if number > 1:
            chunk = number - 2
            far_met = [swap(part, 0) for part in after(fars[chunk], onward)]
            pieces = all_pieces(nears[chunk], fars[chunk], near_mets[chunk], far_met)
            if chunk == 0:
                gain_rows = place(places, pieces, [128], 3 * MODEL_WIDTH)[0][0]
                gain_rows = gain_rows[:, : 2 * layer_count].T.reshape(layer_count, 2, -1)
            if chunk % 2 == 0:
                layers.append(Layer(places, pieces, gain_rows[chunk // 2], tables, allowed))
                step["mixed"] = layers[-1].entry_forward(resid)
            else:
                layers[-1].add_rest(pieces)
                step["resid"] = layers[-1].rest_forward(mixed)
        step["own"] = chunks[number + 2 :]
        step = lax.optimization_barrier(step)
        chunks[number + 2 :] = step["own"]
        if number < count:
            nears.append((held, step["x"], step["y"]))
            onward = second_step(*nears[-1])
        held = step.get("next")
        if number > 0:
            fars.append(step["far"])
        resid = step.get("resid", resid)
        mixed = step.get("mixed")
        met = step.get("met") if number == 0 else met
    head_far_met = [swap(part, 0) for part in fars[-1]]
    head_pieces = all_pieces(nears[-1], fars[-1], near_mets[-1], head_far_met)
    head_whole = place(places, head_pieces, [3 * group_width])[0]

    sensitivity = met[:, :rows]
    head_offsets = met[:, rows : rows + 4].astype(jnp.float32)
    latent_offsets = head_offsets[:, 0] + head_offsets[:, 2]
    emit_offsets = head_offsets[:, 1] + head_offsets[:, 3]

    top = resid.astype(jnp.bfloat16)
    keep_column = keep_rows[:, None]
    two = 2 * group_width
    inner_parts = [
        jnp.dot(top, head_whole[part][:, :two], preferred_element_type=jnp.float32)
        for part in range(group)
    ]
    head_pre = jnp.concatenate(
        [inner_parts[part][:, :group_width] + latent_offsets[part] for part in range(group)],
        axis=1,
    )
    head_hidden = jax.nn.silu(head_pre).astype(jnp.bfloat16)
    forecast = jnp.stack(
        [
            (
                jnp.dot(
                    head_hidden, head_whole[part][:, two:], preferred_element_type=jnp.float32
                )
                + emit_offsets[part]
                + inner_parts[part][:, group_width:]
            )
            * keep_column
            for part in range(group)
        ]
    ).astype(jnp.bfloat16)
    token_predictions = lax.all_to_all(
        forecast, "head", split_axis=0, concat_axis=0, tiled=True
    ).reshape(group * rows, group_width)
    grad_forecast = (sensitivity.astype(jnp.float32) * keep_column).astype(jnp.bfloat16)
    grad_hidden = sum(
        reverse_matmul_answer(grad_forecast[part], head_whole[part][:, two:])
        for part in range(group)
    )
    unused_head, head_pull = jax.vjp(jax.nn.silu, head_pre)
    grad_head_pre = head_pull(grad_hidden)[0].astype(jnp.bfloat16)
    grad_resid = sum(
        reverse_matmul_answer(
            jnp.concatenate(
                [
                    grad_head_pre[:, part * group_width : (part + 1) * group_width],
                    grad_forecast[part],
                ],
                axis=1,
            ),
            head_whole[part][:, :two],
        )
        for part in range(group)
    )
    grad_forecast_rows = jnp.concatenate([grad_forecast[part] for part in range(group)], axis=1)
    head_bias_rows = (
        jnp.sum(grad_head_pre.astype(jnp.float32), axis=0),
        jnp.sum(grad_forecast_rows.astype(jnp.float32), axis=0),
    )
    head_products = RowSums(
        *pair_products(
            me,
            [
                (top, grad_head_pre),
                (top, grad_forecast_rows),
                (head_hidden, grad_forecast_rows),
            ],
        )
    )
    gain_sums = [[None, None] for _ in range(layer_count)]

    def rest_stage(layer_index, carry):
        outs = layers[layer_index].rest_backward(carry["grad"])
        carry = {"middle": outs[0], "mixed": outs[1]}
        gain_sums[layer_index][1] = outs[4]
        return carry, RowSums(*pair_products(me, list(zip(outs[2], outs[3], strict=True))))

    def entry_stage(layer_index, carry):
        outs = layers[layer_index].entry_backward(carry["middle"], carry["mixed"])
        gain_sums[layer_index][0] = outs[3]
        return {"grad": outs[0]}, RowSums(*pair_products(me, [(outs[1], outs[2])]))

    def input_stage(carry):
        grad_entry = carry["grad"].astype(jnp.bfloat16)
        grad_entry_outer = dyadic_accumulation(entry_hidden, grad_entry)
        grad_entry_outer_bias = jnp.sum(grad_entry.astype(jnp.float32), axis=0)
        grad_entry_skip = dyadic_accumulation(features, grad_entry)
        unused_entry, entry_pull = jax.vjp(jax.nn.silu, entry_pre)
        grad_entry_pre = entry_pull(reverse_matmul_answer(grad_entry, intake_emit_matrix))[0].astype(
            jnp.bfloat16
        )
        grad_entry_inner = dyadic_accumulation(features, grad_entry_pre)
        grad_entry_inner_bias = jnp.sum(grad_entry_pre.astype(jnp.float32), axis=0)
        grad_features = reverse_matmul_answer(
            grad_entry_pre, intake_latent_matrix
        ) + reverse_matmul_answer(grad_entry, intake_shortcut_matrix)
        values_grad = jnp.where(pad_mask, 0.0, grad_features[:, :patch_len])
        extra_rows = jnp.concatenate(
            [
                grad_entry_inner,
                grad_entry_skip,
                grad_entry_inner_bias[None],
                grad_entry_outer_bias[None],
            ]
            + [row[None] for row in head_bias_rows]
            + [row[None] for pair in gain_sums for row in pair],
            axis=0,
        )
        return values_grad, extra_rows.shape[0], entry_products(me, grad_entry_outer, extra_rows)

    chunks = [head_products]
    grad_resid, head_products.sent = lax.optimization_barrier((grad_resid, head_products.sent))
    carry = {"grad": grad_resid}
    stages = []
    for layer_index in reversed(range(layer_count)):
        stages += [(rest_stage, layer_index), (entry_stage, layer_index)]
    finished = {}

    def waits(number):
        earlier = []
        if number >= 1:
            earlier.append(chunks[number - 1].met)
        if number >= 2:
            earlier.append(chunks[number - 2].last_met)
        if number >= 3:
            earlier.append(finished[number - 3])
        return earlier

    def under_way(number):
        chunks[number].met = chunks[number].first()
        chunks[number].last_met = chunks[number].last()
        total = chunks[number].total()
        if number == 0:
            finished[number] = sum_columns(total)
        elif number < 2:
            finished[number] = sum_group(total)
        else:
            finished[number] = sum_group_at_once(total)

    under_way(0)
    for number, (stage, layer_index) in enumerate(stages):
        carry = after(carry, *waits(number))
        carry, products = stage(layer_index, carry)
        chunks.append(products)
        under_way(number + 1)
    carry = after(carry, *waits(len(stages)), chunks[-1].sent)
    values_grad, extra_count, entry_chunk = input_stage(carry)
    entry_chunk.met = entry_chunk.first()
    entry_chunk.last_met = entry_chunk.last()
    head_sums = gather_blocks(me, finished[0]).astype(jnp.float32)
    layer_sums = [None] * layer_count
    for member, layer_index in enumerate(reversed(range(layer_count))):
        rest = finished[1 + 2 * member].astype(jnp.float32)
        entry = finished[2 + 2 * member].astype(jnp.float32)
        layer_sums[layer_index] = (entry[0], rest[0], rest[1], rest[2])
    entry_main, entry_extra = entry_everywhere(me, entry_chunk.total(), own_count, extra_count)
    inner_rows = 2 * patch_len
    last = 2 * inner_rows
    entry_sums = (
        entry_extra[:inner_rows],
        entry_extra[last],
        entry_main,
        entry_extra[last + 1],
        entry_extra[inner_rows:last],
    )
    head_bias_sums = lax.dynamic_slice_in_dim(
        entry_extra[last + 2 : last + 4], group_place * group_width, group_width, 1
    )
    own_place = (me * group + group_place) * own_count
    gains_grad = lax.dynamic_slice_in_dim(
        entry_extra[last + 4 : last + 4 + 2 * layer_count], own_place, own_count, 1
    ).reshape(layer_count, 2, own_count)
    qkv_grad = jnp.stack([layer_sums[member][0] for member in range(layer_count)])
    out_grad = jnp.stack([layer_sums[member][1] for member in range(layer_count)])
    up_grad = jnp.stack([layer_sums[member][2] for member in range(layer_count)])
    down_grad = jnp.stack([layer_sums[member][3] for member in range(layer_count)])
    return (
        token_predictions,
        values_grad,
        entry_sums[0],
        entry_sums[1],
        entry_sums[2],
        entry_sums[3],
        entry_sums[4],
        qkv_grad,
        out_grad,
        up_grad,
        down_grad,
        gains_grad,
        head_sums[0],
        head_bias_sums[0],
        head_sums[2],
        head_bias_sums[1],
        head_sums[1],
    )


def solution(mesh):
    return jax.shard_map(
        body,
        mesh=mesh,
        in_specs=(
            P(("dp", "head"), None),
            P(("dp", "head"), None),
            P(("dp", "head"), None),
            P(),
            P(),
            P(),
            P(),
            P(),
            P(None, ("dp", "head"), None),
            P(None, ("dp", "head"), None),
            P(None, ("dp", "head"), None),
            P(None, ("dp", "head"), None),
            P(None, None, ("dp", "head")),
            P(None, "head"),
            P("head"),
            P(None, "head"),
            P("head"),
            P(None, "head"),
            P("dp", "head"),
        ),
        out_specs=(
            P("dp", "head"),
            P(("dp", "head"), None),
            P(),
            P(),
            P(),
            P(),
            P(),
            P(None, ("dp", "head"), None),
            P(None, ("dp", "head"), None),
            P(None, ("dp", "head"), None),
            P(None, ("dp", "head"), None),
            P(None, None, ("dp", "head")),
            P(None, "head"),
            P("head"),
            P(None, "head"),
            P("head"),
            P(None, "head"),
        ),
        check_vma=False,
    )
```

```python
from functools import partial
import math

import jax
import jax.numpy as jnp
from jax import lax
from jax.experimental import pallas as pl
from jax.experimental.pallas import tpu as pltpu
from jax.sharding import PartitionSpec as P

MODEL_WIDTH = 1280
HEADS = 16
HEAD_DIM = 80


EPS = 1e-06
SMALL_COST = pl.CostEstimate(flops=1, bytes_accessed=1, transcendentals=0)
ROPE_BASE = 10000.0


def layout_rows(series_row, pad_row, patch_len):
    count = series_row.shape[0]
    order = jnp.arange(count, dtype=jnp.int32)
    same_series = series_row[:, None] == series_row[None, :]
    earlier = order[None, :] < order[:, None]
    position = jnp.sum(jnp.logical_and(same_series, earlier).astype(jnp.int32), axis=1)
    numbers = jnp.arange(pad_row.shape[0], dtype=jnp.int32)
    series_pad = jnp.sum(
        jnp.where(series_row[:, None] == numbers[None, :], pad_row[None, :], 0), axis=1
    )
    pad_count = jnp.where(position == 0, series_pad, 0)
    padded = pad_count == patch_len
    diagonal = order[:, None] == order[None, :]
    reach = jnp.logical_or(jnp.logical_and(earlier, jnp.logical_not(padded)[None, :]), diagonal)
    allowed = jnp.logical_and(same_series, reach)
    keep_rows = jnp.where(padded, 0.0, 1.0).astype(jnp.float32)
    return (position, pad_count, allowed, keep_rows)


def rotary_tables(position, head_dim):
    half = head_dim // 2
    steps = jnp.arange(half, dtype=jnp.float32) / half
    inverse = jnp.exp(-math.log(ROPE_BASE) * steps)
    angles = position.astype(jnp.float32)[:, None] * inverse[None, :]
    return (jnp.cos(angles)[:, None, :], jnp.sin(angles)[:, None, :])


def rotate(heads_rows, cosine, sine):
    half = heads_rows.shape[-1] // 2
    first = heads_rows[..., :half]
    second = heads_rows[..., half:]
    return jnp.concatenate(
        [first * cosine - second * sine, second * cosine + first * sine], axis=-1
    )


def unrotate(grad_rows, cosine, sine):
    half = grad_rows.shape[-1] // 2
    first = grad_rows[..., :half]
    second = grad_rows[..., half:]
    return jnp.concatenate(
        [first * cosine + second * sine, second * cosine - first * sine], axis=-1
    )


def norm_apply(resid, gain):
    return resid * lax.rsqrt(jnp.mean(resid * resid, axis=-1, keepdims=True) + EPS) * gain


def dyadic_accumulation(left, right):
    return lax.dot_general(
        left, right, (((0,), (0,)), ((), ())), preferred_element_type=jnp.float32
    )


def reverse_matmul_answer(grad_rows, weight):
    return lax.dot_general(
        grad_rows, weight, (((1,), (1,)), ((), ())), preferred_element_type=jnp.float32
    )


def masked_scores(query_rows, key_rows, allowed):
    scale = 1.0 / math.sqrt(query_rows.shape[-1])
    scores = (
        jnp.einsum("qhd,khd->hqk", query_rows, key_rows, preferred_element_type=jnp.float32) * scale
    )
    return jnp.where(allowed[None], scores, -1e30)


def attend_forward(query_rows, key_rows, value_rows, allowed):
    scores = masked_scores(query_rows, key_rows, allowed)
    peak = jnp.max(scores, axis=-1, keepdims=True)
    weights = jnp.exp(scores - peak)
    total = jnp.sum(weights, axis=-1, keepdims=True)
    probs = (weights / total).astype(jnp.bfloat16)
    mixed = jnp.einsum("hqk,khd->qhd", probs, value_rows, preferred_element_type=jnp.float32)
    return (mixed, peak + jnp.log(total))


def attend_backward(query_rows, key_rows, value_rows, allowed, log_total, grad_mixed):
    scale = 1.0 / math.sqrt(query_rows.shape[-1])
    scores = masked_scores(query_rows, key_rows, allowed)
    probs = jnp.where(allowed[None], jnp.exp(scores - log_total), 0.0)
    grad_probs = jnp.einsum(
        "qhd,khd->hqk", grad_mixed, value_rows, preferred_element_type=jnp.float32
    )
    grad_values = jnp.einsum(
        "hqk,qhd->khd", probs.astype(jnp.bfloat16), grad_mixed, preferred_element_type=jnp.float32
    )
    center = jnp.sum(grad_probs * probs, axis=-1, keepdims=True)
    grad_scores = (probs * (grad_probs - center)).astype(jnp.bfloat16)
    grad_query = (
        jnp.einsum("hqk,khd->qhd", grad_scores, key_rows, preferred_element_type=jnp.float32)
        * scale
    )
    grad_keys = (
        jnp.einsum("hqk,qhd->khd", grad_scores, query_rows, preferred_element_type=jnp.float32)
        * scale
    )
    return (grad_query, grad_keys, grad_values)


def after(value, *earlier):
    return lax.optimization_barrier((value, *earlier))[0]


def swap(v, bit):
    size = lax.axis_size("dp")
    return lax.ppermute(v, "dp", [(i, i ^ (1 << bit)) for i in range(size)])


def outer_groups():
    size = lax.axis_size("dp")
    return [[j + 8 * o for o in range(size // 8)] for j in range(8)]


def place_kernel(plan, piece_count, out_count, me_ref, *refs):
    pieces = refs[:piece_count]
    outs = refs[piece_count : piece_count + out_count]
    held = refs[piece_count + out_count : piece_count + 2 * out_count]
    in_sems, out_sems = refs[piece_count + 2 * out_count :]
    inward, outward = [], []
    for n, (piece, rel, row, out, column) in enumerate(plan):
        source = pieces[piece]
        width = held[out].shape[-1]
        if width != source.shape[-1]:
            source = source.at[:, :, pl.ds(column, width)]
        spot = (slice(None), me_ref[0] ^ rel, pl.ds(row, source.shape[1]), slice(None))
        inward.append(pltpu.make_async_copy(source, held[out].at[spot], in_sems.at[n]))
        outward.append(
            pltpu.make_async_copy(held[out].at[spot], outs[out].at[spot], out_sems.at[n])
        )
    for copy in inward:
        copy.start()
    for copy, onward in zip(inward, outward):
        copy.wait()
        onward.start()
    for onward in outward:
        onward.wait()


def place(me, pieces, widths, first=0):
    plan = []
    for n, (rel, row, _) in enumerate(pieces):
        column = first
        for out, width in enumerate(widths):
            plan.append((n, rel, row, out, column))
            column += width
    arrays = [array for _, _, array in pieces]
    lead, rows, _ = arrays[0].shape
    kind = arrays[0].dtype
    total = sum(8 * lead * rows * -(-w // 128) * 128 for w in widths) * 2
    outs = pl.pallas_call(
        partial(place_kernel, plan, len(arrays), len(widths)),
        out_shape=[jax.ShapeDtypeStruct((lead, 8, rows, w), kind) for w in widths],
        in_specs=[pl.BlockSpec(memory_space=pltpu.SMEM)]
        + [pl.BlockSpec(memory_space=pl.ANY)] * len(arrays),
        out_specs=[pl.BlockSpec(memory_space=pl.ANY)] * len(widths),
        scratch_shapes=[pltpu.VMEM((lead, 8, rows, w), kind) for w in widths]
        + [pltpu.SemaphoreType.DMA((len(plan),))] * 2,
        compiler_params=pltpu.CompilerParams(vmem_limit_bytes=total + (4 << 20)),
        cost_estimate=SMALL_COST,
    )(me, *arrays)
    outer = lax.axis_size("dp") // 8
    return [o.reshape(-1, outer * 8 * rows, o.shape[-1]) for o in outs]


def row_half(rows):
    return rows // 32 * 16 if rows >= 32 else rows // 2


def second_step(held, from_x, from_y):
    half = row_half(held.shape[1])
    return from_y[:, :half], from_x[:, half:]


def all_pieces(near, far, near_met, far_met):
    half = far[0].shape[1]
    places = ((0, 0), (2, 0), (4, 0), (6, 0), (6, half))
    pieces = []
    for (rel, row), array, met in zip(places, (*near, *far), (*near_met, *far_met), strict=True):
        pieces += [(rel, row, array), (rel | 1, row, met)]
    return pieces


def spread_rows(held):
    near = (held, swap(held, 1), swap(held, 2))
    onward_x, onward_y = second_step(*near)
    far = (swap(onward_x, 1), swap(onward_y, 2))
    return all_pieces(near, far, [swap(part, 0) for part in near], [swap(part, 0) for part in far])


def gather_head(own):
    held = lax.all_gather(own, "head", axis=0, tiled=True)[None]
    if lax.axis_size("dp") > 8:
        held = lax.all_gather(
            held, "dp", axis=0, tiled=True, axis_index_groups=outer_groups()
        )
    return held


def product_kernel(count, outer, me_ref, *refs):
    lefts, rights, met_lefts, met_rights = (refs[n * count : (n + 1) * count] for n in range(4))
    to_x, to_y, later, own, right_pair = refs[4 * count :]
    rows, width = own.shape[1] // outer, own.shape[-1]
    tokens = lefts[0].shape[0]
    half = width // 2
    tile = half if half <= 640 else 640
    odd = me_ref[0] & 1 == 1
    chip = me_ref[0] >> 1

    def store(rel, n, span, side, columns, total):
        if rel == 0:
            own[n, span, slice(side * half + columns.start, side * half + columns.stop)] = total
        elif rel == 1 and side == 0:
            to_x[1, n, span, columns] = total
        elif rel == 1:
            later[1, n, span, columns] = total
        elif rel == 2 and side == 0:
            later[0, n, span, columns] = total
        elif rel == 2:
            to_y[1, n, span, columns] = total
        elif side == 0:
            to_x[0, n, span, columns] = total
        else:
            to_y[0, n, span, columns] = total

    for n in range(count):
        right_pair[:tokens] = rights[n][...]
        right_pair[tokens:] = met_rights[n][...]
        for part in range(outer):
            span = slice(part * rows, (part + 1) * rows)
            for place in range(4):
                first = (part * 8 + 2 * place) * rows
                near, far = slice(first, first + rows), slice(first + rows, first + 2 * rows)
                left_pair = jnp.concatenate(
                    [
                        jnp.where(odd, side[n][:, far], side[n][:, near]).astype(jnp.float32)
                        for side in (lefts, met_lefts)
                    ],
                    axis=0,
                )
                turned = left_pair.T.astype(own.dtype)
                for side in range(2):
                    for at in range(0, half, tile):
                        total = jnp.dot(
                            turned,
                            right_pair[:, side * half + at : side * half + at + tile],
                            preferred_element_type=jnp.float32,
                        ).astype(own.dtype)
                        for rel in range(4):
                            pl.when(chip ^ place == rel)(
                                partial(store, rel, n, span, side, slice(at, at + tile), total)
                            )


def exchange(pairs):
    met = {}
    for pair in pairs:
        for rows in pair:
            if id(rows) not in met:
                met[id(rows)] = swap(rows, 0)
    return [(left, right, met[id(left)], met[id(right)]) for left, right in pairs]


def pair_products(me, both):
    outer = lax.axis_size("dp") // 8
    count = len(both)
    left, right = both[0][:2]
    block, width = left.shape[1] // 8, right.shape[1]
    low = jnp.bfloat16
    return pl.pallas_call(
        partial(product_kernel, count, outer),
        out_shape=[
            jax.ShapeDtypeStruct((2, count, block, width // 2), low),
            jax.ShapeDtypeStruct((2, count, block, width // 2), low),
            jax.ShapeDtypeStruct((2, count, block, width // 2), low),
            jax.ShapeDtypeStruct((count, block, width), low),
        ],
        in_specs=[pl.BlockSpec(memory_space=pltpu.SMEM)]
        + [pl.BlockSpec(memory_space=pltpu.VMEM)] * (4 * count),
        out_specs=[pl.BlockSpec(memory_space=pltpu.VMEM)] * 4,
        scratch_shapes=[pltpu.VMEM((2 * left.shape[0], width), low)],
        compiler_params=pltpu.CompilerParams(vmem_limit_bytes=44 << 20),
        cost_estimate=SMALL_COST,
    )((me & 7).reshape(1), *[part for parts in zip(*both, strict=True) for part in parts])


def low_sum(*parts):
    total = parts[0].astype(jnp.float32)
    for part in parts[1:]:
        total = total + part.astype(jnp.float32)
    return total.astype(jnp.bfloat16)


class RowSums:
    def __init__(self, to_x, to_y, later, own):
        self.sent, self.later, self.own = (to_x, to_y), later, own

    def first(self):
        return swap(self.sent[0], 1), swap(self.sent[1], 2)

    def last(self):
        return (
            swap(low_sum(self.later[0], self.met[0][0]), 2),
            swap(low_sum(self.later[1], self.met[1][0]), 1),
        )

    def total(self):
        half = self.own.shape[-1] // 2
        return jnp.concatenate(
            [
                low_sum(self.own[..., :half], self.met[0][1], self.last_met[0]),
                low_sum(self.own[..., half:], self.met[1][1], self.last_met[1]),
            ],
            axis=-1,
        )


def sum_group(total):
    outer = lax.axis_size("dp") // 8
    group = lax.axis_size("head")
    lead = total.shape[:-2]
    rows, columns = total.shape[-2:]
    if outer > 1:
        total = lax.psum_scatter(
            total.reshape(*lead, outer, rows // outer, columns),
            "dp",
            scatter_dimension=len(lead),
            tiled=True,
            axis_index_groups=outer_groups(),
        )
    total = total.reshape(*lead, rows // outer, columns)
    return lax.psum_scatter(total, "head", scatter_dimension=len(lead), tiled=True)


def sum_group_at_once(total):
    outer = lax.axis_size("dp") // 8
    group = lax.axis_size("head")
    if outer > 1:
        return sum_group(total).astype(jnp.float32)
    lead = total.shape[:-2]
    rows, columns = total.shape[-2:]
    total = total.reshape(*lead, group, rows // group, columns)
    axis = len(lead)
    met = lax.all_to_all(total, "head", split_axis=axis, concat_axis=axis, tiled=True)
    return jnp.sum(met.astype(jnp.float32), axis=axis)


def sum_columns(total):
    group = lax.axis_size("head")
    if lax.axis_size("dp") > 8:
        total = lax.psum(total, "dp", axis_index_groups=outer_groups())
    count, rows, columns = total.shape
    total = jnp.moveaxis(total.reshape(count, rows, group, columns // group), 2, 0)
    return lax.psum_scatter(total, "head", scatter_dimension=0, tiled=True)[0]


def gather_blocks(me, summed):
    outer = lax.axis_size("dp") // 8
    count, rows, columns = summed.shape
    if outer == 1:
        whole = lax.all_gather(summed, "dp", axis=0)
        return jnp.moveaxis(whole, 0, 1).reshape(count, 8 * rows, columns)
    held = summed.reshape(count * outer, rows // outer, columns)
    return place((me & 7).reshape(1), spread_rows(held), [columns])[0]


EXTRA_ROWS = 8


def entry_products(me, main, extra):
    group = lax.axis_size("head")
    outer = lax.axis_size("dp") // 8
    devices = 8 * outer * group
    columns = main.shape[1]
    own = main.shape[0] // devices
    extra = jnp.pad(extra, ((0, EXTRA_ROWS * devices - extra.shape[0]), (0, 0)))
    rows = jnp.concatenate(
        [main.reshape(devices, own, columns), extra.reshape(devices, EXTRA_ROWS, columns)], axis=1
    ).astype(jnp.bfloat16)
    view = rows.reshape(outer, 4, 2, group * (own + EXTRA_ROWS), columns)
    core = me & 1
    other = lax.dynamic_index_in_dim(view, 1 - core, 2, keepdims=False)
    pair = low_sum(lax.dynamic_index_in_dim(view, core, 2, keepdims=False), swap(other, 0))
    chip = (me & 7) >> 1
    half = columns // 2

    def picked(rel):
        return lax.dynamic_index_in_dim(pair, chip ^ rel, 1, keepdims=False).reshape(-1, columns)

    own_rows, at_x, at_y, far = (picked(rel) for rel in range(4))
    return RowSums(
        jnp.stack([far[:, :half], at_x[:, :half]]),
        jnp.stack([far[:, half:], at_y[:, half:]]),
        (at_y[:, :half], at_x[:, half:]),
        own_rows,
    )


def entry_kernel(plan, own, me_ref, *refs):
    pieces = refs[: len(plan)]
    main_ref, extra_ref, held, sems = refs[len(plan) :]
    copies = []
    for n, (rel, row, rows) in enumerate(plan):
        spot = held.at[me_ref[0] ^ rel, pl.ds(row, rows)]
        copies.append(pltpu.make_async_copy(pieces[n].at[0], spot, sems.at[n]))
    for copy in copies:
        copy.start()
    for copy in copies:
        copy.wait()
    span = own + EXTRA_ROWS
    group = held.shape[1] // span
    for block in range(8):
        rows = held[block].astype(jnp.float32)
        for member in range(group):
            main_ref[block * group + member] = rows[member * span : member * span + own]
            extra_ref[block * group + member] = rows[member * span + own : (member + 1) * span]


def entry_everywhere(me, total, own, count):
    columns = total.shape[1]
    held = gather_head(sum_group_at_once(total).astype(total.dtype))
    pieces = spread_rows(held)
    places = (me & 7).reshape(1)
    span = own + EXTRA_ROWS
    if held.shape[0] > 1 or own % 8 or not in_kernel(pieces):
        (whole,) = place(places, pieces, [columns])
        whole = whole.reshape(-1, span, columns).astype(jnp.float32)
        return whole[:, :own].reshape(-1, columns), whole[:, own:].reshape(-1, columns)[:count]
    rows = held.shape[1]
    blocks = 8 * rows // span
    plan = [(rel, row, array.shape[1]) for rel, row, array in pieces]
    vmem = pl.BlockSpec(memory_space=pltpu.VMEM)
    main, extra = pl.pallas_call(
        partial(entry_kernel, plan, own),
        out_shape=[
            jax.ShapeDtypeStruct((blocks, own, columns), jnp.float32),
            jax.ShapeDtypeStruct((blocks, EXTRA_ROWS, columns), jnp.float32),
        ],
        in_specs=[pl.BlockSpec(memory_space=pltpu.SMEM)]
        + [pl.BlockSpec(memory_space=pl.ANY)] * len(pieces),
        out_specs=[vmem, vmem],
        scratch_shapes=[
            pltpu.VMEM((8, rows, columns), held.dtype),
            pltpu.SemaphoreType.DMA((len(pieces),)),
        ],
        compiler_params=pltpu.CompilerParams(vmem_limit_bytes=44 << 20),
        cost_estimate=SMALL_COST,
    )(places, *[array for _, _, array in pieces])
    return main.reshape(-1, columns), extra.reshape(-1, columns)[:count]


def fetch(plan, me, pieces, whole, sems):
    groups = []
    for group in range(whole.shape[1] // MODEL_WIDTH):
        columns = pl.ds(group * MODEL_WIDTH, MODEL_WIDTH)
        copies = []
        for n, (rel, row, rows) in enumerate(plan):
            first = pl.multiple_of((me ^ rel) * (whole.shape[0] // 8) + row, 16)
            copies.append(
                pltpu.make_async_copy(
                    pieces[n].at[0, :, columns],
                    whole.at[pl.ds(first, rows), columns],
                    sems.at[group * len(plan) + n],
                )
            )
        for copy in copies:
            copy.start()
        groups.append(copies)
    return groups


def arrive(copies):
    for copy in copies:
        copy.wait()


def rows_times(left, whole, first, out, tile):
    def step(n, _):
        at = pl.multiple_of(n * tile, 128)
        out[:, pl.ds(at, tile)] = jnp.dot(
            left, whole[:, pl.ds(first + at, tile)], preferred_element_type=jnp.float32
        )
        return 0

    lax.fori_loop(0, out.shape[1] // tile, step, 0)


def rows_times_turned(left, whole, first, width, out, tile):
    def step(n, _):
        at = pl.multiple_of(n * tile, 128)
        part = reverse_matmul_answer(whole[pl.ds(at, tile), pl.ds(first, width)], left)
        out[:, pl.ds(at, tile)] = part.T
        return 0

    lax.fori_loop(0, out.shape[1] // tile, step, 0)


def inverse_norm(rows):
    return lax.rsqrt(jnp.mean(rows * rows, axis=-1, keepdims=True) + EPS)


def other_half(rows):
    half = HEAD_DIM // 2
    lane = lax.broadcasted_iota(jnp.int32, rows.shape, 1) % HEAD_DIM
    ahead = pltpu.roll(rows, rows.shape[1] - half, 1)
    behind = pltpu.roll(rows, half, 1)
    return jnp.where(lane < half, ahead, behind)


def head_window(head, width):
    first = head * HEAD_DIM // 128 * 128
    last = min(-(-(head + 1) * HEAD_DIM // 128) * 128, width)
    start = head * HEAD_DIM - first
    lane = lax.broadcasted_iota(jnp.int32, (1, last - first), 1)
    return slice(first, last), jnp.logical_and(lane >= start, lane < start + HEAD_DIM)


def entry_forward_kernel(plan, me_ref, resid_ref, gain_ref, cosine_ref, sine_ref, allowed_ref, *refs):
    pieces = refs[: len(plan)]
    normed_ref, query_ref, key_ref, value_ref, total_ref, mixed_ref = refs[len(plan) : len(plan) + 6]
    whole, wide, sems = refs[len(plan) + 6 :]
    groups = fetch(plan, me_ref[0], pieces, whole, sems)
    resid = resid_ref[...]
    normed = (resid * inverse_norm(resid) * gain_ref[...]).astype(jnp.bfloat16)
    normed_ref[...] = normed
    for group, out in enumerate((query_ref, key_ref, value_ref)):
        arrive(groups[group])
        rows_times(normed, whole, group * MODEL_WIDTH, wide, 256)
        rows = wide[...]
        if group < 2:
            rows = rows * cosine_ref[...] + other_half(rows) * sine_ref[...]
        out[...] = rows.astype(jnp.bfloat16)
    scale = 1.0 / math.sqrt(HEAD_DIM)
    allowed = allowed_ref[...] > 0.0
    wide[...] = jnp.zeros_like(wide)
    totals = jnp.zeros(total_ref.shape, jnp.float32)
    head_lane = lax.broadcasted_iota(jnp.int32, total_ref.shape, 1)
    for head in range(HEADS):
        window, inside = head_window(head, MODEL_WIDTH)
        query = jnp.where(inside, query_ref[:, window], 0)
        scores = reverse_matmul_answer(query, key_ref[:, window]) * scale
        scores = jnp.where(allowed, scores, -1e30)
        peak = jnp.max(scores, axis=-1, keepdims=True)
        weights = jnp.exp(scores - peak)
        total = jnp.sum(weights, axis=-1, keepdims=True)
        probs = (weights / total).astype(jnp.bfloat16)
        mixed = jnp.dot(probs, value_ref[:, window], preferred_element_type=jnp.float32)
        wide[:, window] += jnp.where(inside, mixed, 0.0)
        totals = jnp.where(head_lane == head, peak + jnp.log(total), totals)
    total_ref[...] = totals
    mixed_ref[...] = wide[...].astype(jnp.bfloat16)


def gelu_parts(x):
    root = math.sqrt(2.0 / math.pi)
    bend = jnp.tanh(root * (x + 0.044715 * (x * x * x)))
    slope = 0.5 * (1.0 + bend) + 0.5 * x * (1.0 - bend * bend) * root * (
        1.0 + 3.0 * 0.044715 * (x * x)
    )
    return 0.5 * x * (1.0 + bend), slope


def rest_forward_kernel(plan, me_ref, resid_ref, mixed_ref, gain_ref, *refs):
    pieces = refs[: len(plan)]
    result_ref, middle_ref, normed_ref, pre_ref = refs[len(plan) : len(plan) + 4]
    whole, sems = refs[len(plan) + 4 :]
    groups = fetch(plan, me_ref[0], pieces, whole, sems)
    arrive(groups[0])
    rows_times(mixed_ref[...], whole, 0, middle_ref, 256)
    middle = resid_ref[...] + middle_ref[...]
    middle_ref[...] = middle
    normed = (middle * inverse_norm(middle) * gain_ref[...]).astype(jnp.bfloat16)
    normed_ref[...] = normed
    arrive(groups[1])
    rows_times(normed, whole, MODEL_WIDTH, pre_ref, 256)
    act = gelu_parts(pre_ref[...])[0].astype(jnp.bfloat16)
    arrive(groups[2])
    rows_times(act, whole, 2 * MODEL_WIDTH, result_ref, 256)
    result_ref[...] += middle_ref[...]


def norm_back(rows, gain, grad):
    inverse = inverse_norm(rows)
    scaled = grad * gain
    mean = jnp.mean(rows * scaled, axis=-1, keepdims=True)
    sent = inverse * scaled - rows * (inverse * inverse * inverse * mean)
    return sent, jnp.sum(grad * rows * inverse, axis=0, keepdims=True)


def rest_backward_kernel(plan, me_ref, grad_ref, middle_ref, pre_ref, gain_ref, *refs):
    pieces = refs[: len(plan)]
    outs = refs[len(plan) : len(plan) + 7]
    grad_middle_ref, mixed_ref, attn_ref, grad_pre_ref, branch_ref, act_ref, gain_grad_ref = outs
    whole, wide, sems = refs[len(plan) + 7 :]
    groups = fetch(plan, me_ref[0], pieces, whole, sems)
    grad = grad_ref[...]
    branch = grad.astype(jnp.bfloat16)
    branch_ref[...] = branch
    arrive(groups[2])
    rows_times_turned(branch, whole, 2 * MODEL_WIDTH, MODEL_WIDTH, wide, 256)
    act, slope = gelu_parts(pre_ref[...])
    act_ref[...] = act.astype(jnp.bfloat16)
    grad_pre = (wide[...] * slope).astype(jnp.bfloat16)
    grad_pre_ref[...] = grad_pre
    arrive(groups[1])
    rows_times_turned(grad_pre, whole, MODEL_WIDTH, MODEL_WIDTH, wide, 256)
    sent, gain_grad_ref[...] = norm_back(middle_ref[...], gain_ref[...], wide[...])
    grad_middle = grad + sent
    grad_middle_ref[...] = grad_middle
    attn = grad_middle.astype(jnp.bfloat16)
    attn_ref[...] = attn
    arrive(groups[0])
    rows_times_turned(attn, whole, 0, MODEL_WIDTH, wide, 256)
    mixed_ref[...] = wide[...].astype(jnp.bfloat16)


def entry_backward_kernel(
    plan,
    me_ref,
    grad_middle_ref,
    grad_mixed_ref,
    resid_ref,
    query_ref,
    key_ref,
    value_ref,
    total_ref,
    gain_ref,
    cosine_ref,
    sine_ref,
    allowed_ref,
    *refs,
):
    pieces = refs[: len(plan)]
    grad_resid_ref, projected_ref, gain_grad_ref = refs[len(plan) : len(plan) + 3]
    whole, grad_query, grad_key, grad_value, sems = refs[len(plan) + 3 :]
    groups = fetch(plan, me_ref[0], pieces, whole, sems)
    scale = 1.0 / math.sqrt(HEAD_DIM)
    allowed = allowed_ref[...] > 0.0
    totals = total_ref[...]
    grad_query[...] = jnp.zeros_like(grad_query)
    grad_key[...] = jnp.zeros_like(grad_key)
    grad_value[...] = jnp.zeros_like(grad_value)
    for head in range(HEADS):
        window, inside = head_window(head, MODEL_WIDTH)
        query = jnp.where(inside, query_ref[:, window], 0)
        keys = key_ref[:, window]
        grad_mixed = jnp.where(inside, grad_mixed_ref[:, window], 0)
        scores = reverse_matmul_answer(query, keys) * scale
        probs = jnp.where(allowed, jnp.exp(scores - totals[:, head : head + 1]), 0.0)
        grad_probs = reverse_matmul_answer(grad_mixed, value_ref[:, window])
        grad_value[:, window] += dyadic_accumulation(probs.astype(jnp.bfloat16), grad_mixed)
        center = jnp.sum(grad_probs * probs, axis=-1, keepdims=True)
        grad_scores = (probs * (grad_probs - center)).astype(jnp.bfloat16)
        along = jnp.dot(grad_scores, keys, preferred_element_type=jnp.float32)
        grad_query[:, window] += jnp.where(inside, along * scale, 0.0)
        grad_key[:, window] += dyadic_accumulation(grad_scores, query) * scale
    for group, part in enumerate((grad_query, grad_key, grad_value)):
        rows = part[...]
        if group < 2:
            rows = rows * cosine_ref[...] - other_half(rows) * sine_ref[...]
        projected_ref[:, group * MODEL_WIDTH : (group + 1) * MODEL_WIDTH] = rows.astype(jnp.bfloat16)
    for copies in groups:
        arrive(copies)
    rows_times_turned(projected_ref[...], whole, 0, 3 * MODEL_WIDTH, grad_query, 256)
    sent, gain_grad_ref[...] = norm_back(resid_ref[...], gain_ref[...], grad_query[...])
    grad_resid_ref[...] = grad_middle_ref[...] + sent


def whole_call(kernel, me, pieces, inputs, outs, wides):
    rows = inputs[0].shape[0]
    plan = [(rel, row, array.shape[1]) for rel, row, array in pieces]
    blocks = 8 * pieces[0][2].shape[1]
    columns = 3 * MODEL_WIDTH
    vmem = pl.BlockSpec(memory_space=pltpu.VMEM)
    return pl.pallas_call(
        partial(kernel, plan),
        out_shape=[jax.ShapeDtypeStruct(shape, kind) for shape, kind in outs],
        in_specs=[pl.BlockSpec(memory_space=pltpu.SMEM)]
        + [vmem] * len(inputs)
        + [pl.BlockSpec(memory_space=pl.ANY)] * len(pieces),
        out_specs=[vmem] * len(outs),
        scratch_shapes=[pltpu.VMEM((blocks, columns), jnp.bfloat16)]
        + [pltpu.VMEM((rows, MODEL_WIDTH), jnp.float32)] * wides
        + [pltpu.SemaphoreType.DMA((3 * len(pieces),))],
        compiler_params=pltpu.CompilerParams(vmem_limit_bytes=44 << 20),
        cost_estimate=SMALL_COST,
    )(me, *inputs, *[array for _, _, array in pieces])


def in_kernel(pieces):
    lead, rows, _ = pieces[0][2].shape
    return lead == 1 and rows % 32 == 0


LOW, FULL = jnp.bfloat16, jnp.float32


class Layer:
    def __init__(self, places, entry_pieces, gains, tables, allowed):
        self.places, self.entry_pieces, self.gains = places, entry_pieces, gains
        self.tables, self.allowed = tables, allowed
        self.fetched = in_kernel(entry_pieces)
        if not self.fetched:
            self.entry_whole = place(places, entry_pieces, [3 * MODEL_WIDTH])[0][0]

    def add_rest(self, rest_pieces):
        self.rest_pieces = rest_pieces
        if not self.fetched:
            self.rest_whole = [part[0] for part in place(self.places, rest_pieces, [MODEL_WIDTH] * 3)]

    def shapes(self, *kinds):
        rows = self.allowed.shape[0]
        return [((rows, width), kind) for width, kind in kinds]

    def entry_forward(self, resid):
        if not self.fetched:
            self.saved = entry_forward(
                resid, self.entry_whole, self.gains, *self.tables[:2], self.allowed
            )
            return self.saved[6]
        wide = (MODEL_WIDTH, LOW)
        self.resid = resid
        outs = whole_call(
            entry_forward_kernel,
            self.places,
            self.entry_pieces,
            (resid, self.gains[:1].astype(FULL), *self.tables[2:], self.allowed.astype(FULL)),
            self.shapes(wide, wide, wide, wide, (128, FULL), wide),
            1,
        )
        self.normed_first, self.heads = outs[0], outs[1:5]
        return outs[5]

    def rest_forward(self, mixed):
        if not self.fetched:
            result, self.saved = rest_forward(
                (*self.saved[:6], mixed), *self.rest_whole, self.gains
            )
            return result
        self.mixed = mixed
        result, self.middle, self.normed_second, self.hidden_pre = whole_call(
            rest_forward_kernel,
            self.places,
            self.rest_pieces,
            (self.resid, mixed, self.gains[1:].astype(FULL)),
            self.shapes(
                (MODEL_WIDTH, FULL), (MODEL_WIDTH, FULL), (MODEL_WIDTH, LOW), (MODEL_WIDTH, FULL)
            ),
            0,
        )
        return result

    def rest_backward(self, grad):
        if not self.fetched:
            weights = (self.entry_whole, *self.rest_whole, self.gains)
            return rest_backward(self.saved, weights, grad)
        wide = (MODEL_WIDTH, LOW)
        grad_middle, grad_mixed, grad_attn, grad_pre, branch, act, gain_grad = whole_call(
            rest_backward_kernel,
            self.places,
            self.rest_pieces,
            (grad, self.middle, self.hidden_pre, self.gains[1:].astype(FULL)),
            self.shapes((MODEL_WIDTH, FULL), wide, wide, wide, wide, wide)
            + [((1, MODEL_WIDTH), FULL)],
            1,
        )
        lefts = (self.mixed, self.normed_second, act)
        return grad_middle, grad_mixed, lefts, (grad_attn, grad_pre, branch), gain_grad[0]

    def entry_backward(self, grad_middle, grad_mixed):
        if not self.fetched:
            weights = (self.entry_whole, *self.rest_whole, self.gains)
            return entry_backward(
                self.saved, weights, *self.tables[:2], self.allowed, grad_middle, grad_mixed
            )
        grad_resid, projected, gain_grad = whole_call(
            entry_backward_kernel,
            self.places,
            self.entry_pieces,
            (
                grad_middle,
                grad_mixed,
                self.resid,
                *self.heads,
                self.gains[:1].astype(FULL),
                *self.tables[2:],
                self.allowed.astype(FULL),
            ),
            self.shapes((MODEL_WIDTH, FULL), (3 * MODEL_WIDTH, LOW)) + [((1, MODEL_WIDTH), FULL)],
            3,
        )
        return grad_resid, self.normed_first, projected, gain_grad[0]


def entry_forward(resid, qkv_full, gain_pair, cosine, sine, allowed):
    gains = gain_pair.astype(jnp.float32)
    rows = resid.shape[0]
    normed_first = norm_apply(resid, gains[0]).astype(jnp.bfloat16)
    projected = jnp.dot(normed_first, qkv_full, preferred_element_type=jnp.float32)
    query_rows = rotate(
        projected[:, :MODEL_WIDTH].reshape(rows, HEADS, HEAD_DIM), cosine, sine
    ).astype(jnp.bfloat16)
    key_rows = rotate(
        projected[:, MODEL_WIDTH : 2 * MODEL_WIDTH].reshape(rows, HEADS, HEAD_DIM), cosine, sine
    ).astype(jnp.bfloat16)
    value_rows = projected[:, 2 * MODEL_WIDTH :].reshape(rows, HEADS, HEAD_DIM).astype(jnp.bfloat16)

    mixed, log_total = attend_forward(query_rows, key_rows, value_rows, allowed)
    mixed_low = mixed.reshape(rows, MODEL_WIDTH).astype(jnp.bfloat16)
    return (resid, normed_first, query_rows, key_rows, value_rows, log_total, mixed_low)


def rest_forward(saved, out_full, up_full, down_full, gain_pair):
    gains = gain_pair.astype(jnp.float32)
    resid, mixed_low = saved[0], saved[6]
    middle = resid + jnp.dot(mixed_low, out_full, preferred_element_type=jnp.float32)
    normed_second = norm_apply(middle, gains[1]).astype(jnp.bfloat16)
    hidden_pre = jnp.dot(normed_second, up_full, preferred_element_type=jnp.float32)
    hidden_act = jax.nn.gelu(hidden_pre, approximate=True).astype(jnp.bfloat16)
    result = middle + jnp.dot(hidden_act, down_full, preferred_element_type=jnp.float32)
    return (result, (*saved, middle, normed_second, hidden_pre))


def rest_backward(saved, weights, grad_result):
    mixed_low, middle, normed_second, hidden_pre = saved[6:]
    _, out_full, up_full, down_full, gain_pair = weights
    gains = gain_pair.astype(jnp.float32)
    grad_branch = grad_result.astype(jnp.bfloat16)
    hidden_act, gelu_pull = jax.vjp(partial(jax.nn.gelu, approximate=True), hidden_pre)
    hidden_low = hidden_act.astype(jnp.bfloat16)
    grad_act = reverse_matmul_answer(grad_branch, down_full)
    grad_pre = gelu_pull(grad_act)[0].astype(jnp.bfloat16)
    grad_normed_second = reverse_matmul_answer(grad_pre, up_full)
    unused_second, second_pull = jax.vjp(norm_apply, middle, gains[1])
    grad_middle_norm, grad_gain_second = second_pull(grad_normed_second)
    grad_middle = grad_result + grad_middle_norm
    grad_attn = grad_middle.astype(jnp.bfloat16)
    grad_mixed = reverse_matmul_answer(grad_attn, out_full).astype(jnp.bfloat16)
    left_rows = (mixed_low, normed_second, hidden_low)
    right_rows = (grad_attn, grad_pre, grad_branch)
    return (grad_middle, grad_mixed, left_rows, right_rows, grad_gain_second)


def entry_backward(saved, weights, cosine, sine, allowed, grad_middle, grad_mixed):
    resid, normed_first, query_rows, key_rows, value_rows, log_total = saved[:6]
    qkv_full = weights[0]
    gains = weights[4].astype(jnp.float32)
    rows = resid.shape[0]
    grad_query, grad_keys, grad_values = attend_backward(
        query_rows,
        key_rows,
        value_rows,
        allowed,
        log_total,
        grad_mixed.reshape(rows, HEADS, HEAD_DIM),
    )
    grad_query = unrotate(grad_query, cosine, sine).reshape(rows, MODEL_WIDTH)
    grad_keys = unrotate(grad_keys, cosine, sine).reshape(rows, MODEL_WIDTH)
    grad_values = grad_values.reshape(rows, MODEL_WIDTH)
    grad_projected = jnp.concatenate([grad_query, grad_keys, grad_values], axis=1).astype(
        jnp.bfloat16
    )
    grad_normed_first = reverse_matmul_answer(grad_projected, qkv_full)
    unused_first, first_pull = jax.vjp(norm_apply, resid, gains[0])
    grad_resid_norm, grad_gain_first = first_pull(grad_normed_first)
    return (grad_middle + grad_resid_norm, normed_first, grad_projected, grad_gain_first)


def body(
    patch_observations,
    sequence_labels,
    leading_filler_count,
    intake_latent_matrix,
    intake_latent_offset,
    intake_emit_matrix,
    intake_emit_offset,
    intake_shortcut_matrix,
    attention_entry_matrices,
    attention_merge_matrix,
    feedforward_widen_matrix,
    feedforward_shrink_matrix,
    layer_scale_factors,
    readout_latent_matrix,
    readout_latent_offset,
    readout_emit_matrix,
    readout_emit_offset,
    readout_shortcut_matrix,
    loss_sensitivity,
):
    patch_len = patch_observations.shape[1]
    position, pad_count, allowed, keep_rows = layout_rows(
        sequence_labels[0], leading_filler_count[0], patch_len
    )
    cosine, sine = rotary_tables(position, HEAD_DIM)
    columns = jnp.arange(patch_len, dtype=jnp.int32)
    pad_mask = columns[None, :] < pad_count[:, None]
    features = jnp.concatenate(
        [
            jnp.where(pad_mask, jnp.zeros_like(patch_observations), patch_observations),
            pad_mask.astype(jnp.bfloat16),
        ],
        axis=1,
    )
    entry_pre = (
        jnp.dot(features, intake_latent_matrix, preferred_element_type=jnp.float32)
        + intake_latent_offset
    )
    entry_hidden = jax.nn.silu(entry_pre).astype(jnp.bfloat16)
    resid = (
        jnp.dot(entry_hidden, intake_emit_matrix, preferred_element_type=jnp.float32)
        + intake_emit_offset
        + jnp.dot(features, intake_shortcut_matrix, preferred_element_type=jnp.float32)
    )
    layer_count = attention_entry_matrices.shape[0]
    group = lax.axis_size("head")
    group_place = lax.axis_index("head")
    outer = lax.axis_size("dp") // 8
    me = lax.axis_index("dp").astype(jnp.int32)
    places = (me & 7).reshape(1)
    own_count = layer_scale_factors.shape[2]
    rows = patch_observations.shape[0]

    group_width = readout_latent_offset.shape[0]
    offsets = jnp.stack([readout_latent_offset, readout_emit_offset])
    coarse = lax.reduce_precision(offsets, 8, 7)
    offset_rows = jnp.concatenate([coarse, offsets - coarse], axis=0).astype(jnp.bfloat16)
    offset_rows = jnp.pad(offset_rows, ((0, 12), (0, 0)))
    sent = jnp.concatenate(
        [
            loss_sensitivity.reshape(group, rows, group_width),
            jnp.broadcast_to(offset_rows[None], (group, 16, group_width)),
        ],
        axis=1,
    )
    gain_columns = layer_scale_factors.reshape(2 * layer_count, own_count).T
    gain_columns = jnp.pad(gain_columns, ((0, 0), (0, 128 - 2 * layer_count)))
    chunks = []
    for layer_index in range(layer_count):
        entry_own = attention_entry_matrices[layer_index]
        if layer_index == 0:
            entry_own = jnp.concatenate([entry_own, gain_columns], axis=1)
        chunks.append(entry_own)
        rest_own = jnp.concatenate(
            [
                attention_merge_matrix[layer_index],
                feedforward_widen_matrix[layer_index],
                feedforward_shrink_matrix[layer_index],
            ],
            axis=1,
        )
        chunks.append(rest_own)
    head_own = jnp.concatenate(
        [
            lax.dynamic_index_in_dim(
                matrix.reshape(outer, 8, -1, group_width), me % 8, 1, keepdims=False
            )
            for matrix in (readout_latent_matrix, readout_shortcut_matrix, readout_emit_matrix)
        ],
        axis=2,
    )
    chunks.append(head_own)
    count = len(chunks)

    def gather_chunk(number, own):
        if number < count - 1:
            return gather_head(own)
        return lax.all_gather(own, "head", axis=0, tiled=True)

    held = gather_chunk(0, chunks[0])
    cosine_wide = jnp.tile(jnp.concatenate([cosine[:, 0], cosine[:, 0]], axis=1), (1, HEADS))
    sine_wide = jnp.tile(jnp.concatenate([-sine[:, 0], sine[:, 0]], axis=1), (1, HEADS))
    tables = (cosine, sine, cosine_wide, sine_wide)
    nears, fars, near_mets = [], [], []
    layers = []
    onward = None
    for number in range(count + 1):
        step = {}
        if number < count:
            step["x"], step["y"] = swap(held, 1), swap(held, 2)
        if number + 1 < count:
            step["next"] = gather_chunk(number + 1, chunks[number + 1])
        if number == 0:
            step["resid"] = resid
            step["met"] = lax.all_to_all(
                after(sent, held), "head", split_axis=0, concat_axis=0, tiled=True
            )
        else:
            step["far"] = (swap(onward[0], 1), swap(onward[1], 2))
            near_mets.append([swap(part, 0) for part in after(nears[number - 1], onward)])
        if number > 1:
            chunk = number - 2
            far_met = [swap(part, 0) for part in after(fars[chunk], onward)]
            pieces = all_pieces(nears[chunk], fars[chunk], near_mets[chunk], far_met)
            if chunk == 0:
                gain_rows = place(places, pieces, [128], 3 * MODEL_WIDTH)[0][0]
                gain_rows = gain_rows[:, : 2 * layer_count].T.reshape(layer_count, 2, -1)
            if chunk % 2 == 0:
                layers.append(Layer(places, pieces, gain_rows[chunk // 2], tables, allowed))
                step["mixed"] = layers[-1].entry_forward(resid)
            else:
                layers[-1].add_rest(pieces)
                step["resid"] = layers[-1].rest_forward(mixed)
        step["own"] = chunks[number + 2 :]
        step = lax.optimization_barrier(step)
        chunks[number + 2 :] = step["own"]
        if number < count:
            nears.append((held, step["x"], step["y"]))
            onward = second_step(*nears[-1])
        held = step.get("next")
        if number > 0:
            fars.append(step["far"])
        resid = step.get("resid", resid)
        mixed = step.get("mixed")
        met = step.get("met") if number == 0 else met
    head_far_met = [swap(part, 0) for part in fars[-1]]
    head_pieces = all_pieces(nears[-1], fars[-1], near_mets[-1], head_far_met)
    head_whole = place(places, head_pieces, [3 * group_width])[0]

    sensitivity = met[:, :rows]
    head_offsets = met[:, rows : rows + 4].astype(jnp.float32)
    latent_offsets = head_offsets[:, 0] + head_offsets[:, 2]
    emit_offsets = head_offsets[:, 1] + head_offsets[:, 3]

    top = resid.astype(jnp.bfloat16)
    keep_column = keep_rows[:, None]
    two = 2 * group_width
    inner_parts = [
        jnp.dot(top, head_whole[part][:, :two], preferred_element_type=jnp.float32)
        for part in range(group)
    ]
    head_pre = jnp.concatenate(
        [inner_parts[part][:, :group_width] + latent_offsets[part] for part in range(group)],
        axis=1,
    )
    head_hidden = jax.nn.silu(head_pre).astype(jnp.bfloat16)
    forecast = jnp.stack(
        [
            (
                jnp.dot(
                    head_hidden, head_whole[part][:, two:], preferred_element_type=jnp.float32
                )
                + emit_offsets[part]
                + inner_parts[part][:, group_width:]
            )
            * keep_column
            for part in range(group)
        ]
    ).astype(jnp.bfloat16)
    token_predictions = lax.all_to_all(
        forecast, "head", split_axis=0, concat_axis=0, tiled=True
    ).reshape(group * rows, group_width)
    grad_forecast = (sensitivity.astype(jnp.float32) * keep_column).astype(jnp.bfloat16)
    grad_hidden = sum(
        reverse_matmul_answer(grad_forecast[part], head_whole[part][:, two:])
        for part in range(group)
    )
    unused_head, head_pull = jax.vjp(jax.nn.silu, head_pre)
    grad_head_pre = head_pull(grad_hidden)[0].astype(jnp.bfloat16)
    grad_resid = sum(
        reverse_matmul_answer(
            jnp.concatenate(
                [
                    grad_head_pre[:, part * group_width : (part + 1) * group_width],
                    grad_forecast[part],
                ],
                axis=1,
            ),
            head_whole[part][:, :two],
        )
        for part in range(group)
    )
    grad_forecast_rows = jnp.concatenate([grad_forecast[part] for part in range(group)], axis=1)
    head_bias_rows = (
        jnp.sum(grad_head_pre.astype(jnp.float32), axis=0),
        jnp.sum(grad_forecast_rows.astype(jnp.float32), axis=0),
    )
    head_both = exchange(
        [
            (top, grad_head_pre),
            (top, grad_forecast_rows),
            (head_hidden, grad_forecast_rows),
        ]
    )
    gain_sums = [[None, None] for _ in range(layer_count)]

    def rest_stage(layer_index, carry):
        outs = layers[layer_index].rest_backward(carry["grad"])
        gain_sums[layer_index][1] = outs[4]
        both = exchange(list(zip(outs[2], outs[3], strict=True)))
        return {"middle": outs[0], "mixed": outs[1]}, both

    def entry_stage(layer_index, carry):
        outs = layers[layer_index].entry_backward(carry["middle"], carry["mixed"])
        gain_sums[layer_index][0] = outs[3]
        return {"grad": outs[0]}, exchange([(outs[1], outs[2])])

    def input_stage(carry):
        grad_entry = carry["grad"].astype(jnp.bfloat16)
        grad_entry_outer = dyadic_accumulation(entry_hidden, grad_entry)
        grad_entry_outer_bias = jnp.sum(grad_entry.astype(jnp.float32), axis=0)
        grad_entry_skip = dyadic_accumulation(features, grad_entry)
        unused_entry, entry_pull = jax.vjp(jax.nn.silu, entry_pre)
        grad_entry_pre = entry_pull(reverse_matmul_answer(grad_entry, intake_emit_matrix))[0].astype(
            jnp.bfloat16
        )
        grad_entry_inner = dyadic_accumulation(features, grad_entry_pre)
        grad_entry_inner_bias = jnp.sum(grad_entry_pre.astype(jnp.float32), axis=0)
        grad_features = reverse_matmul_answer(
            grad_entry_pre, intake_latent_matrix
        ) + reverse_matmul_answer(grad_entry, intake_shortcut_matrix)
        values_grad = jnp.where(pad_mask, 0.0, grad_features[:, :patch_len])
        extra_rows = jnp.concatenate(
            [
                grad_entry_inner,
                grad_entry_skip,
                grad_entry_inner_bias[None],
                grad_entry_outer_bias[None],
            ]
            + [row[None] for row in head_bias_rows]
            + [row[None] for pair in gain_sums for row in pair],
            axis=0,
        )
        return values_grad, extra_rows.shape[0], entry_products(me, grad_entry_outer, extra_rows)

    stages = []
    for layer_index in reversed(range(layer_count)):
        stages += [(rest_stage, layer_index), (entry_stage, layer_index)]
    stage_count = len(stages)
    carry = {"grad": grad_resid}
    boths = {0: head_both}
    sums = {0: RowSums(*pair_products(me, head_both))}
    totals, finished = {}, {}
    entry_chunk = None
    done = 0

    def close(**step):
        step["sent"] = {n: (sums[n].sent, sums[n].later, sums[n].own) for n in sums}
        step["boths"] = boths
        step["carry"] = carry
        step = lax.optimization_barrier(step)
        for n, parts in step.pop("sent").items():
            sums[n].sent, sums[n].later, sums[n].own = parts
        return step

    step = close()
    for number in range(stage_count + 1):
        carry, boths = step["carry"], step["boths"]
        parts = {"first": sums[number].first()}
        if number >= 1:
            totals[number - 1] = sums.pop(number - 1).total()
            if number == 1:
                finished[0] = sum_columns(totals[0])
            else:
                finished[number - 1] = sum_group(totals[number - 1])
        if number >= 2:
            parts["finished"] = finished[number - 2]
        until = {stage_count - 2: stage_count}.get(number, number + 1)
        while done < min(until, stage_count):
            stage, layer_index = stages[done]
            carry, boths[done + 1] = stage(layer_index, carry)
            done += 1
        if number == stage_count - 1:
            values_grad, extra_count, entry_chunk = input_stage(carry)
            parts["entry"] = (entry_chunk.sent, entry_chunk.later, entry_chunk.own)
        if number == stage_count:
            parts["entry"] = entry_chunk.last()
        step = close(**parts)
        sums[number].met = step["first"]
        if number >= 2:
            finished[number - 2] = step["finished"]
        carry, boths = step["carry"], step["boths"]
        parts = {"last": sums[number].last()}
        if number == stage_count - 1:
            entry_chunk.sent, entry_chunk.later, entry_chunk.own = step["entry"]
            parts["entry"] = entry_chunk.first()
        if number == stage_count:
            entry_chunk.last_met = step["entry"]
            entry_total = entry_chunk.total()
        if number < stage_count:
            sums[number + 1] = RowSums(*pair_products(me, boths.pop(number + 1)))
            step = close(**parts)
        else:
            step = parts
        sums[number].last_met = step["last"]
        if number == stage_count - 1:
            entry_chunk.met = step["entry"]
    finished[stage_count] = sum_group_at_once(sums[stage_count].total())
    head_sums = gather_blocks(me, finished[0]).astype(jnp.float32)
    layer_sums = [None] * layer_count
    for member, layer_index in enumerate(reversed(range(layer_count))):
        rest = finished[1 + 2 * member].astype(jnp.float32)
        entry = finished[2 + 2 * member].astype(jnp.float32)
        layer_sums[layer_index] = (entry[0], rest[0], rest[1], rest[2])
    entry_main, entry_extra = entry_everywhere(me, entry_total, own_count, extra_count)
    inner_rows = 2 * patch_len
    last = 2 * inner_rows
    entry_sums = (
        entry_extra[:inner_rows],
        entry_extra[last],
        entry_main,
        entry_extra[last + 1],
        entry_extra[inner_rows:last],
    )
    head_bias_sums = lax.dynamic_slice_in_dim(
        entry_extra[last + 2 : last + 4], group_place * group_width, group_width, 1
    )
    own_place = (me * group + group_place) * own_count
    gains_grad = lax.dynamic_slice_in_dim(
        entry_extra[last + 4 : last + 4 + 2 * layer_count], own_place, own_count, 1
    ).reshape(layer_count, 2, own_count)
    qkv_grad = jnp.stack([layer_sums[member][0] for member in range(layer_count)])
    out_grad = jnp.stack([layer_sums[member][1] for member in range(layer_count)])
    up_grad = jnp.stack([layer_sums[member][2] for member in range(layer_count)])
    down_grad = jnp.stack([layer_sums[member][3] for member in range(layer_count)])
    return (
        token_predictions,
        values_grad,
        entry_sums[0],
        entry_sums[1],
        entry_sums[2],
        entry_sums[3],
        entry_sums[4],
        qkv_grad,
        out_grad,
        up_grad,
        down_grad,
        gains_grad,
        head_sums[0],
        head_bias_sums[0],
        head_sums[2],
        head_bias_sums[1],
        head_sums[1],
    )


def solution(mesh):
    return jax.shard_map(
        body,
        mesh=mesh,
        in_specs=(
            P(("dp", "head"), None),
            P(("dp", "head"), None),
            P(("dp", "head"), None),
            P(),
            P(),
            P(),
            P(),
            P(),
            P(None, ("dp", "head"), None),
            P(None, ("dp", "head"), None),
            P(None, ("dp", "head"), None),
            P(None, ("dp", "head"), None),
            P(None, None, ("dp", "head")),
            P(None, "head"),
            P("head"),
            P(None, "head"),
            P("head"),
            P(None, "head"),
            P("dp", "head"),
        ),
        out_specs=(
            P("dp", "head"),
            P(("dp", "head"), None),
            P(),
            P(),
            P(),
            P(),
            P(),
            P(None, ("dp", "head"), None),
            P(None, ("dp", "head"), None),
            P(None, ("dp", "head"), None),
            P(None, ("dp", "head"), None),
            P(None, None, ("dp", "head")),
            P(None, "head"),
            P("head"),
            P(None, "head"),
            P("head"),
            P(None, "head"),
        ),
        check_vma=False,
    )
```

```python
from functools import partial
import math

import jax
import jax.numpy as jnp
from jax import lax
from jax.experimental import pallas as pl
from jax.experimental.pallas import tpu as pltpu
from jax.sharding import PartitionSpec as P

MODEL_WIDTH = 1280
HEADS = 16
HEAD_DIM = 80


EPS = 1e-06
SMALL_COST = pl.CostEstimate(flops=1, bytes_accessed=1, transcendentals=0)
ROPE_BASE = 10000.0


def layout_rows(series_row, pad_row, patch_len):
    count = series_row.shape[0]
    order = jnp.arange(count, dtype=jnp.int32)
    same_series = series_row[:, None] == series_row[None, :]
    earlier = order[None, :] < order[:, None]
    position = jnp.sum(jnp.logical_and(same_series, earlier).astype(jnp.int32), axis=1)
    numbers = jnp.arange(pad_row.shape[0], dtype=jnp.int32)
    series_pad = jnp.sum(
        jnp.where(series_row[:, None] == numbers[None, :], pad_row[None, :], 0), axis=1
    )
    pad_count = jnp.where(position == 0, series_pad, 0)
    padded = pad_count == patch_len
    diagonal = order[:, None] == order[None, :]
    reach = jnp.logical_or(jnp.logical_and(earlier, jnp.logical_not(padded)[None, :]), diagonal)
    allowed = jnp.logical_and(same_series, reach)
    keep_rows = jnp.where(padded, 0.0, 1.0).astype(jnp.float32)
    return (position, pad_count, allowed, keep_rows)


def rotary_tables(position, head_dim):
    half = head_dim // 2
    steps = jnp.arange(half, dtype=jnp.float32) / half
    inverse = jnp.exp(-math.log(ROPE_BASE) * steps)
    angles = position.astype(jnp.float32)[:, None] * inverse[None, :]
    return (jnp.cos(angles)[:, None, :], jnp.sin(angles)[:, None, :])


def rotate(heads_rows, cosine, sine):
    half = heads_rows.shape[-1] // 2
    first = heads_rows[..., :half]
    second = heads_rows[..., half:]
    return jnp.concatenate(
        [first * cosine - second * sine, second * cosine + first * sine], axis=-1
    )


def unrotate(grad_rows, cosine, sine):
    half = grad_rows.shape[-1] // 2
    first = grad_rows[..., :half]
    second = grad_rows[..., half:]
    return jnp.concatenate(
        [first * cosine + second * sine, second * cosine - first * sine], axis=-1
    )


def norm_apply(resid, gain):
    return resid * lax.rsqrt(jnp.mean(resid * resid, axis=-1, keepdims=True) + EPS) * gain


def dyadic_accumulation(left, right):
    return lax.dot_general(
        left, right, (((0,), (0,)), ((), ())), preferred_element_type=jnp.float32
    )


def reverse_matmul_answer(grad_rows, weight):
    return lax.dot_general(
        grad_rows, weight, (((1,), (1,)), ((), ())), preferred_element_type=jnp.float32
    )


def masked_scores(query_rows, key_rows, allowed):
    scale = 1.0 / math.sqrt(query_rows.shape[-1])
    scores = (
        jnp.einsum("qhd,khd->hqk", query_rows, key_rows, preferred_element_type=jnp.float32) * scale
    )
    return jnp.where(allowed[None], scores, -1e30)


def attend_forward(query_rows, key_rows, value_rows, allowed):
    scores = masked_scores(query_rows, key_rows, allowed)
    peak = jnp.max(scores, axis=-1, keepdims=True)
    weights = jnp.exp(scores - peak)
    total = jnp.sum(weights, axis=-1, keepdims=True)
    probs = (weights / total).astype(jnp.bfloat16)
    mixed = jnp.einsum("hqk,khd->qhd", probs, value_rows, preferred_element_type=jnp.float32)
    return (mixed, peak + jnp.log(total))


def attend_backward(query_rows, key_rows, value_rows, allowed, log_total, grad_mixed):
    scale = 1.0 / math.sqrt(query_rows.shape[-1])
    scores = masked_scores(query_rows, key_rows, allowed)
    probs = jnp.where(allowed[None], jnp.exp(scores - log_total), 0.0)
    grad_probs = jnp.einsum(
        "qhd,khd->hqk", grad_mixed, value_rows, preferred_element_type=jnp.float32
    )
    grad_values = jnp.einsum(
        "hqk,qhd->khd", probs.astype(jnp.bfloat16), grad_mixed, preferred_element_type=jnp.float32
    )
    center = jnp.sum(grad_probs * probs, axis=-1, keepdims=True)
    grad_scores = (probs * (grad_probs - center)).astype(jnp.bfloat16)
    grad_query = (
        jnp.einsum("hqk,khd->qhd", grad_scores, key_rows, preferred_element_type=jnp.float32)
        * scale
    )
    grad_keys = (
        jnp.einsum("hqk,qhd->khd", grad_scores, query_rows, preferred_element_type=jnp.float32)
        * scale
    )
    return (grad_query, grad_keys, grad_values)


def after(value, *earlier):
    return lax.optimization_barrier((value, *earlier))[0]


def swap(v, bit):
    size = lax.axis_size("dp")
    return lax.ppermute(v, "dp", [(i, i ^ (1 << bit)) for i in range(size)])


def outer_groups():
    size = lax.axis_size("dp")
    return [[j + 8 * o for o in range(size // 8)] for j in range(8)]


def place_kernel(plan, piece_count, out_count, me_ref, *refs):
    pieces = refs[:piece_count]
    outs = refs[piece_count : piece_count + out_count]
    held = refs[piece_count + out_count : piece_count + 2 * out_count]
    in_sems, out_sems = refs[piece_count + 2 * out_count :]
    inward, outward = [], []
    for n, (piece, rel, row, out, column) in enumerate(plan):
        source = pieces[piece]
        width = held[out].shape[-1]
        if width != source.shape[-1]:
            source = source.at[:, :, pl.ds(column, width)]
        spot = (slice(None), me_ref[0] ^ rel, pl.ds(row, source.shape[1]), slice(None))
        inward.append(pltpu.make_async_copy(source, held[out].at[spot], in_sems.at[n]))
        outward.append(
            pltpu.make_async_copy(held[out].at[spot], outs[out].at[spot], out_sems.at[n])
        )
    for copy in inward:
        copy.start()
    for copy, onward in zip(inward, outward):
        copy.wait()
        onward.start()
    for onward in outward:
        onward.wait()


def place(me, pieces, widths, first=0):
    plan = []
    for n, (rel, row, _) in enumerate(pieces):
        column = first
        for out, width in enumerate(widths):
            plan.append((n, rel, row, out, column))
            column += width
    arrays = [array for _, _, array in pieces]
    lead, rows, _ = arrays[0].shape
    kind = arrays[0].dtype
    total = sum(8 * lead * rows * -(-w // 128) * 128 for w in widths) * 2
    outs = pl.pallas_call(
        partial(place_kernel, plan, len(arrays), len(widths)),
        out_shape=[jax.ShapeDtypeStruct((lead, 8, rows, w), kind) for w in widths],
        in_specs=[pl.BlockSpec(memory_space=pltpu.SMEM)]
        + [pl.BlockSpec(memory_space=pl.ANY)] * len(arrays),
        out_specs=[pl.BlockSpec(memory_space=pl.ANY)] * len(widths),
        scratch_shapes=[pltpu.VMEM((lead, 8, rows, w), kind) for w in widths]
        + [pltpu.SemaphoreType.DMA((len(plan),))] * 2,
        compiler_params=pltpu.CompilerParams(vmem_limit_bytes=total + (4 << 20)),
        cost_estimate=SMALL_COST,
    )(me, *arrays)
    outer = lax.axis_size("dp") // 8
    return [o.reshape(-1, outer * 8 * rows, o.shape[-1]) for o in outs]


def row_half(rows):
    return rows // 32 * 16 if rows >= 32 else rows // 2


def second_step(held, from_x, from_y):
    half = row_half(held.shape[1])
    return from_y[:, :half], from_x[:, half:]


def all_pieces(near, far, near_met, far_met):
    half = far[0].shape[1]
    places = ((0, 0), (2, 0), (4, 0), (6, 0), (6, half))
    pieces = []
    for (rel, row), array, met in zip(places, (*near, *far), (*near_met, *far_met), strict=True):
        pieces += [(rel, row, array), (rel | 1, row, met)]
    return pieces


def spread_rows(held):
    near = (held, swap(held, 1), swap(held, 2))
    onward_x, onward_y = second_step(*near)
    far = (swap(onward_x, 1), swap(onward_y, 2))
    return all_pieces(near, far, [swap(part, 0) for part in near], [swap(part, 0) for part in far])


def gather_head(own):
    held = lax.all_gather(own, "head", axis=0, tiled=True)[None]
    if lax.axis_size("dp") > 8:
        held = lax.all_gather(
            held, "dp", axis=0, tiled=True, axis_index_groups=outer_groups()
        )
    return held


def product_kernel(count, outer, me_ref, *refs):
    lefts, rights, met_lefts, met_rights = (refs[n * count : (n + 1) * count] for n in range(4))
    to_x, to_y, later, own, right_pair, turned = refs[4 * count :]
    rows, width = own.shape[1] // outer, own.shape[-1]
    tokens = lefts[0].shape[0]
    half = width // 2
    tile = half if half <= 640 else 640
    odd = me_ref[0] & 1 == 1
    chip = me_ref[0] >> 1

    def store(rel, n, span, side, columns, total):
        if rel == 0:
            own[n, span, slice(side * half + columns.start, side * half + columns.stop)] = total
        elif rel == 1 and side == 0:
            to_x[1, n, span, columns] = total
        elif rel == 1:
            later[1, n, span, columns] = total
        elif rel == 2 and side == 0:
            later[0, n, span, columns] = total
        elif rel == 2:
            to_y[1, n, span, columns] = total
        elif side == 0:
            to_x[0, n, span, columns] = total
        else:
            to_y[0, n, span, columns] = total

    for n in range(count):
        right_pair[:tokens] = rights[n][...]
        right_pair[tokens:] = met_rights[n][...]
        for part in range(outer):
            span = slice(part * rows, (part + 1) * rows)
            for place in range(4):
                first = (part * 8 + 2 * place) * rows
                near, far = slice(first, first + rows), slice(first + rows, first + 2 * rows)
                left_pair = jnp.concatenate(
                    [
                        jnp.where(odd, side[n][:, far], side[n][:, near]).astype(jnp.float32)
                        for side in (lefts, met_lefts)
                    ],
                    axis=0,
                )
                turned[place] = left_pair.T.astype(own.dtype)
            every = turned[...].reshape(4 * rows, 2 * tokens)
            for side in range(2):
                for at in range(0, half, tile):
                    total = jnp.dot(
                        every,
                        right_pair[:, side * half + at : side * half + at + tile],
                        preferred_element_type=jnp.float32,
                    ).astype(own.dtype)
                    for place in range(4):
                        for rel in range(4):
                            pl.when(chip ^ place == rel)(
                                partial(
                                    store,
                                    rel,
                                    n,
                                    span,
                                    side,
                                    slice(at, at + tile),
                                    total[place * rows : (place + 1) * rows],
                                )
                            )


def exchange(pairs):
    met = {}
    for pair in pairs:
        for rows in pair:
            if id(rows) not in met:
                met[id(rows)] = swap(rows, 0)
    return [(left, right, met[id(left)], met[id(right)]) for left, right in pairs]


def pair_products(me, both):
    outer = lax.axis_size("dp") // 8
    count = len(both)
    left, right = both[0][:2]
    block, width = left.shape[1] // 8, right.shape[1]
    low = jnp.bfloat16
    return pl.pallas_call(
        partial(product_kernel, count, outer),
        out_shape=[
            jax.ShapeDtypeStruct((2, count, block, width // 2), low),
            jax.ShapeDtypeStruct((2, count, block, width // 2), low),
            jax.ShapeDtypeStruct((2, count, block, width // 2), low),
            jax.ShapeDtypeStruct((count, block, width), low),
        ],
        in_specs=[pl.BlockSpec(memory_space=pltpu.SMEM)]
        + [pl.BlockSpec(memory_space=pltpu.VMEM)] * (4 * count),
        out_specs=[pl.BlockSpec(memory_space=pltpu.VMEM)] * 4,
        scratch_shapes=[
            pltpu.VMEM((2 * left.shape[0], width), low),
            pltpu.VMEM((4, block // outer, 2 * left.shape[0]), low),
        ],
        compiler_params=pltpu.CompilerParams(vmem_limit_bytes=44 << 20),
        cost_estimate=SMALL_COST,
    )((me & 7).reshape(1), *[part for parts in zip(*both, strict=True) for part in parts])


def low_sum(*parts):
    total = parts[0].astype(jnp.float32)
    for part in parts[1:]:
        total = total + part.astype(jnp.float32)
    return total.astype(jnp.bfloat16)


class RowSums:
    def __init__(self, to_x, to_y, later, own):
        self.sent, self.later, self.own = (to_x, to_y), later, own

    def first(self):
        return swap(self.sent[0], 1), swap(self.sent[1], 2)

    def last(self):
        return (
            swap(low_sum(self.later[0], self.met[0][0]), 2),
            swap(low_sum(self.later[1], self.met[1][0]), 1),
        )

    def total(self):
        half = self.own.shape[-1] // 2
        return jnp.concatenate(
            [
                low_sum(self.own[..., :half], self.met[0][1], self.last_met[0]),
                low_sum(self.own[..., half:], self.met[1][1], self.last_met[1]),
            ],
            axis=-1,
        )


def sum_group(total):
    outer = lax.axis_size("dp") // 8
    group = lax.axis_size("head")
    lead = total.shape[:-2]
    rows, columns = total.shape[-2:]
    if outer > 1:
        total = lax.psum_scatter(
            total.reshape(*lead, outer, rows // outer, columns),
            "dp",
            scatter_dimension=len(lead),
            tiled=True,
            axis_index_groups=outer_groups(),
        )
    total = total.reshape(*lead, rows // outer, columns)
    return lax.psum_scatter(total, "head", scatter_dimension=len(lead), tiled=True)


def sum_group_at_once(total):
    outer = lax.axis_size("dp") // 8
    group = lax.axis_size("head")
    if outer > 1:
        return sum_group(total).astype(jnp.float32)
    lead = total.shape[:-2]
    rows, columns = total.shape[-2:]
    total = total.reshape(*lead, group, rows // group, columns)
    axis = len(lead)
    met = lax.all_to_all(total, "head", split_axis=axis, concat_axis=axis, tiled=True)
    return jnp.sum(met.astype(jnp.float32), axis=axis)


def sum_columns(total):
    group = lax.axis_size("head")
    if lax.axis_size("dp") > 8:
        total = lax.psum(total, "dp", axis_index_groups=outer_groups())
    count, rows, columns = total.shape
    total = jnp.moveaxis(total.reshape(count, rows, group, columns // group), 2, 0)
    return lax.psum_scatter(total, "head", scatter_dimension=0, tiled=True)[0]


def gather_blocks(me, summed):
    outer = lax.axis_size("dp") // 8
    count, rows, columns = summed.shape
    if outer == 1:
        whole = lax.all_gather(summed, "dp", axis=0)
        return [whole[:, n].reshape(8 * rows, columns) for n in range(count)]
    held = summed.reshape(count * outer, rows // outer, columns)
    return place((me & 7).reshape(1), spread_rows(held), [columns])[0]


EXTRA_ROWS = 8


def entry_products(me, main, extra):
    group = lax.axis_size("head")
    outer = lax.axis_size("dp") // 8
    devices = 8 * outer * group
    columns = main.shape[1]
    own = main.shape[0] // devices
    extra = jnp.pad(extra, ((0, EXTRA_ROWS * devices - extra.shape[0]), (0, 0)))
    rows = jnp.concatenate(
        [main.reshape(devices, own, columns), extra.reshape(devices, EXTRA_ROWS, columns)], axis=1
    ).astype(jnp.bfloat16)
    view = rows.reshape(outer, 4, 2, group * (own + EXTRA_ROWS), columns)
    core = me & 1
    other = lax.dynamic_index_in_dim(view, 1 - core, 2, keepdims=False)
    pair = low_sum(lax.dynamic_index_in_dim(view, core, 2, keepdims=False), swap(other, 0))
    chip = (me & 7) >> 1
    half = columns // 2

    def picked(rel):
        return lax.dynamic_index_in_dim(pair, chip ^ rel, 1, keepdims=False).reshape(-1, columns)

    own_rows, at_x, at_y, far = (picked(rel) for rel in range(4))
    return RowSums(
        jnp.stack([far[:, :half], at_x[:, :half]]),
        jnp.stack([far[:, half:], at_y[:, half:]]),
        (at_y[:, :half], at_x[:, half:]),
        own_rows,
    )


def input_back_kernel(
    grad_ref, pre_ref, emit_ref, latent_ref, shortcut_ref, low_ref, pre_low_ref, sent_ref, bias_ref, wide
):
    low = grad_ref[...].astype(jnp.bfloat16)
    low_ref[...] = low
    rows_times_turned(low, emit_ref, 0, emit_ref.shape[1], wide, 256)
    pre = pre_ref[...]
    gate = 1.0 / (1.0 + jnp.exp(-pre))
    pre_low = (wide[...] * (gate * (1.0 + pre * (1.0 - gate)))).astype(jnp.bfloat16)
    pre_low_ref[...] = pre_low
    sent_ref[...] = reverse_matmul_answer(pre_low, latent_ref[...]) + reverse_matmul_answer(
        low, shortcut_ref[...]
    )
    bias_ref[0:1] = jnp.sum(pre_low.astype(jnp.float32), axis=0, keepdims=True)
    bias_ref[1:2] = jnp.sum(low.astype(jnp.float32), axis=0, keepdims=True)


def input_products_kernel(group, me_ref, *refs):
    hidden, met_hidden, low, met_low, pre_low, met_pre_low, features, met_features = refs[:8]
    vectors, met_vectors, to_x, to_y, later, own = refs[8:14]
    turned, low_pair, extras, block = refs[14:]
    tokens = hidden.shape[0]
    columns = low.shape[1]
    half = columns // 2
    core, chip = me_ref[0] & 1, me_ref[0] >> 1
    turned[:, :tokens] = hidden[...].astype(jnp.float32).T.astype(jnp.bfloat16)
    turned[:, tokens:] = met_hidden[...].astype(jnp.float32).T.astype(jnp.bfloat16)
    low_pair[:tokens] = low[...]
    low_pair[tokens:] = met_low[...]
    wide = features.shape[1]
    extras[...] = jnp.zeros_like(extras)
    extras[:wide] = dyadic_accumulation(features[...], pre_low[...]) + dyadic_accumulation(
        met_features[...], met_pre_low[...]
    )
    extras[wide : 2 * wide] = dyadic_accumulation(features[...], low[...]) + dyadic_accumulation(
        met_features[...], met_low[...]
    )
    extras[2 * wide : 2 * wide + vectors.shape[0]] = vectors[...] + met_vectors[...]
    rows = hidden.shape[1] // 8
    each = rows // group
    span = each + EXTRA_ROWS

    def store(rel, total):
        if rel == 0:
            own[0] = total
        elif rel == 1:
            to_x[1, 0] = total[:, :half]
            later[1, 0] = total[:, half:]
        elif rel == 2:
            later[0, 0] = total[:, :half]
            to_y[1, 0] = total[:, half:]
        else:
            to_x[0, 0] = total[:, :half]
            to_y[0, 0] = total[:, half:]

    for place in range(4):
        number = 2 * place + core
        first = pl.multiple_of(number * rows, rows)
        outer = jnp.dot(
            turned[pl.ds(first, rows), :], low_pair[...], preferred_element_type=jnp.float32
        )
        first = pl.multiple_of(number * group * EXTRA_ROWS, group * EXTRA_ROWS)
        extra = extras[pl.ds(first, group * EXTRA_ROWS), :]
        for member in range(group):
            block[member * span : member * span + each] = outer[member * each : (member + 1) * each]
            block[member * span + each : (member + 1) * span] = extra[
                member * EXTRA_ROWS : (member + 1) * EXTRA_ROWS
            ]
        total = block[...].astype(own.dtype)
        for rel in range(4):
            pl.when(chip ^ place == rel)(partial(store, rel, total))


def input_back(grad, pre, emit, latent, shortcut):
    rows, columns = grad.shape
    vmem = pl.BlockSpec(memory_space=pltpu.VMEM)
    return pl.pallas_call(
        input_back_kernel,
        out_shape=[
            jax.ShapeDtypeStruct((rows, columns), LOW),
            jax.ShapeDtypeStruct((rows, columns), LOW),
            jax.ShapeDtypeStruct((rows, latent.shape[0]), FULL),
            jax.ShapeDtypeStruct((2, columns), FULL),
        ],
        in_specs=[vmem] * 5,
        out_specs=[vmem] * 4,
        scratch_shapes=[pltpu.VMEM((rows, columns), FULL)],
        compiler_params=pltpu.CompilerParams(vmem_limit_bytes=32 << 20),
        cost_estimate=SMALL_COST,
    )(grad, pre, emit, latent, shortcut)


def input_products(me, hidden, low, pre_low, features, vectors):
    group = lax.axis_size("head")
    tokens, columns = low.shape
    width = hidden.shape[1]
    block = width // 8 + group * EXTRA_ROWS
    operands = []
    for rows in (hidden, low, pre_low, features, vectors):
        operands += [rows, swap(rows, 0)]
    pair = jax.ShapeDtypeStruct((2, 1, block, columns // 2), LOW)
    return RowSums(
        *pl.pallas_call(
            partial(input_products_kernel, group),
            out_shape=[pair, pair, pair, jax.ShapeDtypeStruct((1, block, columns), LOW)],
            in_specs=[pl.BlockSpec(memory_space=pltpu.SMEM)]
            + [pl.BlockSpec(memory_space=pltpu.VMEM)] * len(operands),
            out_specs=[pl.BlockSpec(memory_space=pltpu.VMEM)] * 4,
            scratch_shapes=[
                pltpu.VMEM((width, 2 * tokens), LOW),
                pltpu.VMEM((2 * tokens, columns), LOW),
                pltpu.VMEM((8 * group * EXTRA_ROWS, columns), FULL),
                pltpu.VMEM((block, columns), FULL),
            ],
            compiler_params=pltpu.CompilerParams(vmem_limit_bytes=32 << 20),
            cost_estimate=SMALL_COST,
        )((me & 7).reshape(1), *operands)
    )


def entry_kernel(plan, own, me_ref, *refs):
    pieces = refs[: len(plan)]
    main_ref, extra_ref, held, sems = refs[len(plan) :]
    copies = []
    for n, (rel, row, rows) in enumerate(plan):
        spot = held.at[me_ref[0] ^ rel, pl.ds(row, rows)]
        copies.append(pltpu.make_async_copy(pieces[n].at[0], spot, sems.at[n]))
    for copy in copies:
        copy.start()
    for copy in copies:
        copy.wait()
    span = own + EXTRA_ROWS
    group = held.shape[1] // span
    for block in range(8):
        rows = held[block].astype(jnp.float32)
        for member in range(group):
            main_ref[block * group + member] = rows[member * span : member * span + own]
            extra_ref[block * group + member] = rows[member * span + own : (member + 1) * span]


def entry_everywhere(me, total, own, count):
    columns = total.shape[-1]
    total = total.reshape(-1, columns)
    summed = sum_group_at_once(total).astype(total.dtype)
    group = lax.axis_size("head")
    if lax.axis_size("dp") > 8:
        held = gather_head(summed)
    else:
        every = jnp.broadcast_to(summed[None], (group, *summed.shape))
        held = lax.all_to_all(every, "head", split_axis=0, concat_axis=0, tiled=True)
        held = held.reshape(1, -1, columns)
    pieces = spread_rows(held)
    places = (me & 7).reshape(1)
    span = own + EXTRA_ROWS
    if held.shape[0] > 1 or own % 8 or not in_kernel(pieces):
        (whole,) = place(places, pieces, [columns])
        whole = whole.reshape(-1, span, columns).astype(jnp.float32)
        return whole[:, :own].reshape(-1, columns), whole[:, own:].reshape(-1, columns)[:count], held
    rows = held.shape[1]
    blocks = 8 * rows // span
    plan = [(rel, row, array.shape[1]) for rel, row, array in pieces]
    vmem = pl.BlockSpec(memory_space=pltpu.VMEM)
    main, extra = pl.pallas_call(
        partial(entry_kernel, plan, own),
        out_shape=[
            jax.ShapeDtypeStruct((blocks, own, columns), jnp.float32),
            jax.ShapeDtypeStruct((blocks, EXTRA_ROWS, columns), jnp.float32),
        ],
        in_specs=[pl.BlockSpec(memory_space=pltpu.SMEM)]
        + [pl.BlockSpec(memory_space=pl.ANY)] * len(pieces),
        out_specs=[vmem, vmem],
        scratch_shapes=[
            pltpu.VMEM((8, rows, columns), held.dtype),
            pltpu.SemaphoreType.DMA((len(pieces),)),
        ],
        compiler_params=pltpu.CompilerParams(vmem_limit_bytes=44 << 20),
        cost_estimate=SMALL_COST,
    )(places, *[array for _, _, array in pieces])
    return main.reshape(-1, columns), extra.reshape(-1, columns)[:count], held


def fetch(plan, me, pieces, whole, sems):
    groups = []
    for group in range(whole.shape[1] // MODEL_WIDTH):
        columns = pl.ds(group * MODEL_WIDTH, MODEL_WIDTH)
        copies = []
        for n, (rel, row, rows) in enumerate(plan):
            first = pl.multiple_of((me ^ rel) * (whole.shape[0] // 8) + row, 16)
            copies.append(
                pltpu.make_async_copy(
                    pieces[n].at[0, :, columns],
                    whole.at[pl.ds(first, rows), columns],
                    sems.at[group * len(plan) + n],
                )
            )
        for copy in copies:
            copy.start()
        groups.append(copies)
    return groups


def arrive(copies):
    for copy in copies:
        copy.wait()


def rows_times(left, whole, first, out, tile):
    def step(n, _):
        at = pl.multiple_of(n * tile, 128)
        out[:, pl.ds(at, tile)] = jnp.dot(
            left, whole[:, pl.ds(first + at, tile)], preferred_element_type=jnp.float32
        )
        return 0

    lax.fori_loop(0, out.shape[1] // tile, step, 0)


def rows_times_turned(left, whole, first, width, out, tile):
    def step(n, _):
        at = pl.multiple_of(n * tile, 128)
        part = reverse_matmul_answer(whole[pl.ds(at, tile), pl.ds(first, width)], left)
        out[:, pl.ds(at, tile)] = part.T
        return 0

    lax.fori_loop(0, out.shape[1] // tile, step, 0)


def inverse_norm(rows):
    return lax.rsqrt(jnp.mean(rows * rows, axis=-1, keepdims=True) + EPS)


def other_half(rows):
    half = HEAD_DIM // 2
    lane = lax.broadcasted_iota(jnp.int32, rows.shape, 1) % HEAD_DIM
    ahead = pltpu.roll(rows, rows.shape[1] - half, 1)
    behind = pltpu.roll(rows, half, 1)
    return jnp.where(lane < half, ahead, behind)


def head_window(head, width):
    first = head * HEAD_DIM // 128 * 128
    last = min(-(-(head + 1) * HEAD_DIM // 128) * 128, width)
    start = head * HEAD_DIM - first
    lane = lax.broadcasted_iota(jnp.int32, (1, last - first), 1)
    return slice(first, last), jnp.logical_and(lane >= start, lane < start + HEAD_DIM)


def entry_forward_kernel(plan, me_ref, resid_ref, gain_ref, cosine_ref, sine_ref, allowed_ref, *refs):
    pieces = refs[: len(plan)]
    normed_ref, query_ref, key_ref, value_ref, total_ref, mixed_ref = refs[len(plan) : len(plan) + 6]
    whole, wide, sems = refs[len(plan) + 6 :]
    groups = fetch(plan, me_ref[0], pieces, whole, sems)
    resid = resid_ref[...]
    normed = (resid * inverse_norm(resid) * gain_ref[...]).astype(jnp.bfloat16)
    normed_ref[...] = normed
    for group, out in enumerate((query_ref, key_ref, value_ref)):
        arrive(groups[group])
        rows_times(normed, whole, group * MODEL_WIDTH, wide, 256)
        rows = wide[...]
        if group < 2:
            rows = rows * cosine_ref[...] + other_half(rows) * sine_ref[...]
        out[...] = rows.astype(jnp.bfloat16)
    scale = 1.0 / math.sqrt(HEAD_DIM)
    allowed = allowed_ref[...] > 0.0
    wide[...] = jnp.zeros_like(wide)
    totals = jnp.zeros(total_ref.shape, jnp.float32)
    head_lane = lax.broadcasted_iota(jnp.int32, total_ref.shape, 1)
    for head in range(HEADS):
        window, inside = head_window(head, MODEL_WIDTH)
        query = jnp.where(inside, query_ref[:, window], 0)
        scores = reverse_matmul_answer(query, key_ref[:, window]) * scale
        scores = jnp.where(allowed, scores, -1e30)
        peak = jnp.max(scores, axis=-1, keepdims=True)
        weights = jnp.exp(scores - peak)
        total = jnp.sum(weights, axis=-1, keepdims=True)
        probs = (weights / total).astype(jnp.bfloat16)
        mixed = jnp.dot(probs, value_ref[:, window], preferred_element_type=jnp.float32)
        wide[:, window] += jnp.where(inside, mixed, 0.0)
        totals = jnp.where(head_lane == head, peak + jnp.log(total), totals)
    total_ref[...] = totals
    mixed_ref[...] = wide[...].astype(jnp.bfloat16)


def gelu_parts(x):
    root = math.sqrt(2.0 / math.pi)
    bend = jnp.tanh(root * (x + 0.044715 * (x * x * x)))
    slope = 0.5 * (1.0 + bend) + 0.5 * x * (1.0 - bend * bend) * root * (
        1.0 + 3.0 * 0.044715 * (x * x)
    )
    return 0.5 * x * (1.0 + bend), slope


def rest_forward_kernel(plan, me_ref, resid_ref, mixed_ref, gain_ref, *refs):
    pieces = refs[: len(plan)]
    result_ref, middle_ref, normed_ref, pre_ref = refs[len(plan) : len(plan) + 4]
    whole, sems = refs[len(plan) + 4 :]
    groups = fetch(plan, me_ref[0], pieces, whole, sems)
    arrive(groups[0])
    rows_times(mixed_ref[...], whole, 0, middle_ref, 256)
    middle = resid_ref[...] + middle_ref[...]
    middle_ref[...] = middle
    normed = (middle * inverse_norm(middle) * gain_ref[...]).astype(jnp.bfloat16)
    normed_ref[...] = normed
    arrive(groups[1])
    rows_times(normed, whole, MODEL_WIDTH, pre_ref, 256)
    act = gelu_parts(pre_ref[...])[0].astype(jnp.bfloat16)
    arrive(groups[2])
    rows_times(act, whole, 2 * MODEL_WIDTH, result_ref, 256)
    result_ref[...] += middle_ref[...]


def norm_back(rows, gain, grad):
    inverse = inverse_norm(rows)
    scaled = grad * gain
    mean = jnp.mean(rows * scaled, axis=-1, keepdims=True)
    sent = inverse * scaled - rows * (inverse * inverse * inverse * mean)
    return sent, jnp.sum(grad * rows * inverse, axis=0, keepdims=True)


def rest_backward_kernel(plan, me_ref, grad_ref, middle_ref, pre_ref, gain_ref, *refs):
    pieces = refs[: len(plan)]
    outs = refs[len(plan) : len(plan) + 7]
    grad_middle_ref, mixed_ref, attn_ref, grad_pre_ref, branch_ref, act_ref, gain_grad_ref = outs
    whole, wide, sems = refs[len(plan) + 7 :]
    groups = fetch(plan, me_ref[0], pieces, whole, sems)
    grad = grad_ref[...]
    branch = grad.astype(jnp.bfloat16)
    branch_ref[...] = branch
    arrive(groups[2])
    rows_times_turned(branch, whole, 2 * MODEL_WIDTH, MODEL_WIDTH, wide, 256)
    act, slope = gelu_parts(pre_ref[...])
    act_ref[...] = act.astype(jnp.bfloat16)
    grad_pre = (wide[...] * slope).astype(jnp.bfloat16)
    grad_pre_ref[...] = grad_pre
    arrive(groups[1])
    rows_times_turned(grad_pre, whole, MODEL_WIDTH, MODEL_WIDTH, wide, 256)
    sent, gain_grad_ref[...] = norm_back(middle_ref[...], gain_ref[...], wide[...])
    grad_middle = grad + sent
    grad_middle_ref[...] = grad_middle
    attn = grad_middle.astype(jnp.bfloat16)
    attn_ref[...] = attn
    arrive(groups[0])
    rows_times_turned(attn, whole, 0, MODEL_WIDTH, wide, 256)
    mixed_ref[...] = wide[...].astype(jnp.bfloat16)


def entry_backward_kernel(
    plan,
    me_ref,
    grad_middle_ref,
    grad_mixed_ref,
    resid_ref,
    query_ref,
    key_ref,
    value_ref,
    total_ref,
    gain_ref,
    cosine_ref,
    sine_ref,
    allowed_ref,
    *refs,
):
    pieces = refs[: len(plan)]
    grad_resid_ref, projected_ref, gain_grad_ref = refs[len(plan) : len(plan) + 3]
    whole, grad_query, grad_key, grad_value, sems = refs[len(plan) + 3 :]
    groups = fetch(plan, me_ref[0], pieces, whole, sems)
    scale = 1.0 / math.sqrt(HEAD_DIM)
    allowed = allowed_ref[...] > 0.0
    totals = total_ref[...]
    grad_query[...] = jnp.zeros_like(grad_query)
    grad_key[...] = jnp.zeros_like(grad_key)
    grad_value[...] = jnp.zeros_like(grad_value)
    for head in range(HEADS):
        window, inside = head_window(head, MODEL_WIDTH)
        query = jnp.where(inside, query_ref[:, window], 0)
        keys = key_ref[:, window]
        grad_mixed = jnp.where(inside, grad_mixed_ref[:, window], 0)
        scores = reverse_matmul_answer(query, keys) * scale
        probs = jnp.where(allowed, jnp.exp(scores - totals[:, head : head + 1]), 0.0)
        grad_probs = reverse_matmul_answer(grad_mixed, value_ref[:, window])
        grad_value[:, window] += dyadic_accumulation(probs.astype(jnp.bfloat16), grad_mixed)
        center = jnp.sum(grad_probs * probs, axis=-1, keepdims=True)
        grad_scores = (probs * (grad_probs - center)).astype(jnp.bfloat16)
        along = jnp.dot(grad_scores, keys, preferred_element_type=jnp.float32)
        grad_query[:, window] += jnp.where(inside, along * scale, 0.0)
        grad_key[:, window] += dyadic_accumulation(grad_scores, query) * scale
    for group, part in enumerate((grad_query, grad_key, grad_value)):
        rows = part[...]
        if group < 2:
            rows = rows * cosine_ref[...] - other_half(rows) * sine_ref[...]
        projected_ref[:, group * MODEL_WIDTH : (group + 1) * MODEL_WIDTH] = rows.astype(jnp.bfloat16)
    for copies in groups:
        arrive(copies)
    rows_times_turned(projected_ref[...], whole, 0, 3 * MODEL_WIDTH, grad_query, 256)
    sent, gain_grad_ref[...] = norm_back(resid_ref[...], gain_ref[...], grad_query[...])
    grad_resid_ref[...] = grad_middle_ref[...] + sent


def whole_call(kernel, me, pieces, inputs, outs, wides):
    rows = inputs[0].shape[0]
    plan = [(rel, row, array.shape[1]) for rel, row, array in pieces]
    blocks = 8 * pieces[0][2].shape[1]
    columns = 3 * MODEL_WIDTH
    vmem = pl.BlockSpec(memory_space=pltpu.VMEM)
    return pl.pallas_call(
        partial(kernel, plan),
        out_shape=[jax.ShapeDtypeStruct(shape, kind) for shape, kind in outs],
        in_specs=[pl.BlockSpec(memory_space=pltpu.SMEM)]
        + [vmem] * len(inputs)
        + [pl.BlockSpec(memory_space=pl.ANY)] * len(pieces),
        out_specs=[vmem] * len(outs),
        scratch_shapes=[pltpu.VMEM((blocks, columns), jnp.bfloat16)]
        + [pltpu.VMEM((rows, MODEL_WIDTH), jnp.float32)] * wides
        + [pltpu.SemaphoreType.DMA((3 * len(pieces),))],
        compiler_params=pltpu.CompilerParams(vmem_limit_bytes=44 << 20),
        cost_estimate=SMALL_COST,
    )(me, *inputs, *[array for _, _, array in pieces])


def in_kernel(pieces):
    lead, rows, _ = pieces[0][2].shape
    return lead == 1 and rows % 32 == 0


LOW, FULL = jnp.bfloat16, jnp.float32


class Layer:
    def __init__(self, places, entry_pieces, gains, tables, allowed):
        self.places, self.entry_pieces, self.gains = places, entry_pieces, gains
        self.tables, self.allowed = tables, allowed
        self.fetched = in_kernel(entry_pieces)
        if not self.fetched:
            self.entry_whole = place(places, entry_pieces, [3 * MODEL_WIDTH])[0][0]

    def add_rest(self, rest_pieces):
        self.rest_pieces = rest_pieces
        if not self.fetched:
            self.rest_whole = [part[0] for part in place(self.places, rest_pieces, [MODEL_WIDTH] * 3)]

    def shapes(self, *kinds):
        rows = self.allowed.shape[0]
        return [((rows, width), kind) for width, kind in kinds]

    def entry_forward(self, resid):
        if not self.fetched:
            self.saved = entry_forward(
                resid, self.entry_whole, self.gains, *self.tables[:2], self.allowed
            )
            return self.saved[6]
        wide = (MODEL_WIDTH, LOW)
        self.resid = resid
        outs = whole_call(
            entry_forward_kernel,
            self.places,
            self.entry_pieces,
            (resid, self.gains[:1].astype(FULL), *self.tables[2:], self.allowed.astype(FULL)),
            self.shapes(wide, wide, wide, wide, (128, FULL), wide),
            1,
        )
        self.normed_first, self.heads = outs[0], outs[1:5]
        return outs[5]

    def rest_forward(self, mixed):
        if not self.fetched:
            result, self.saved = rest_forward(
                (*self.saved[:6], mixed), *self.rest_whole, self.gains
            )
            return result
        self.mixed = mixed
        result, self.middle, self.normed_second, self.hidden_pre = whole_call(
            rest_forward_kernel,
            self.places,
            self.rest_pieces,
            (self.resid, mixed, self.gains[1:].astype(FULL)),
            self.shapes(
                (MODEL_WIDTH, FULL), (MODEL_WIDTH, FULL), (MODEL_WIDTH, LOW), (MODEL_WIDTH, FULL)
            ),
            0,
        )
        return result

    def rest_backward(self, grad):
        if not self.fetched:
            weights = (self.entry_whole, *self.rest_whole, self.gains)
            return rest_backward(self.saved, weights, grad)
        wide = (MODEL_WIDTH, LOW)
        grad_middle, grad_mixed, grad_attn, grad_pre, branch, act, gain_grad = whole_call(
            rest_backward_kernel,
            self.places,
            self.rest_pieces,
            (grad, self.middle, self.hidden_pre, self.gains[1:].astype(FULL)),
            self.shapes((MODEL_WIDTH, FULL), wide, wide, wide, wide, wide)
            + [((1, MODEL_WIDTH), FULL)],
            1,
        )
        lefts = (self.mixed, self.normed_second, act)
        return grad_middle, grad_mixed, lefts, (grad_attn, grad_pre, branch), gain_grad[0]

    def entry_backward(self, grad_middle, grad_mixed):
        if not self.fetched:
            weights = (self.entry_whole, *self.rest_whole, self.gains)
            return entry_backward(
                self.saved, weights, *self.tables[:2], self.allowed, grad_middle, grad_mixed
            )
        grad_resid, projected, gain_grad = whole_call(
            entry_backward_kernel,
            self.places,
            self.entry_pieces,
            (
                grad_middle,
                grad_mixed,
                self.resid,
                *self.heads,
                self.gains[:1].astype(FULL),
                *self.tables[2:],
                self.allowed.astype(FULL),
            ),
            self.shapes((MODEL_WIDTH, FULL), (3 * MODEL_WIDTH, LOW)) + [((1, MODEL_WIDTH), FULL)],
            3,
        )
        return grad_resid, self.normed_first, projected, gain_grad[0]


def entry_forward(resid, qkv_full, gain_pair, cosine, sine, allowed):
    gains = gain_pair.astype(jnp.float32)
    rows = resid.shape[0]
    normed_first = norm_apply(resid, gains[0]).astype(jnp.bfloat16)
    projected = jnp.dot(normed_first, qkv_full, preferred_element_type=jnp.float32)
    query_rows = rotate(
        projected[:, :MODEL_WIDTH].reshape(rows, HEADS, HEAD_DIM), cosine, sine
    ).astype(jnp.bfloat16)
    key_rows = rotate(
        projected[:, MODEL_WIDTH : 2 * MODEL_WIDTH].reshape(rows, HEADS, HEAD_DIM), cosine, sine
    ).astype(jnp.bfloat16)
    value_rows = projected[:, 2 * MODEL_WIDTH :].reshape(rows, HEADS, HEAD_DIM).astype(jnp.bfloat16)

    mixed, log_total = attend_forward(query_rows, key_rows, value_rows, allowed)
    mixed_low = mixed.reshape(rows, MODEL_WIDTH).astype(jnp.bfloat16)
    return (resid, normed_first, query_rows, key_rows, value_rows, log_total, mixed_low)


def rest_forward(saved, out_full, up_full, down_full, gain_pair):
    gains = gain_pair.astype(jnp.float32)
    resid, mixed_low = saved[0], saved[6]
    middle = resid + jnp.dot(mixed_low, out_full, preferred_element_type=jnp.float32)
    normed_second = norm_apply(middle, gains[1]).astype(jnp.bfloat16)
    hidden_pre = jnp.dot(normed_second, up_full, preferred_element_type=jnp.float32)
    hidden_act = jax.nn.gelu(hidden_pre, approximate=True).astype(jnp.bfloat16)
    result = middle + jnp.dot(hidden_act, down_full, preferred_element_type=jnp.float32)
    return (result, (*saved, middle, normed_second, hidden_pre))


def rest_backward(saved, weights, grad_result):
    mixed_low, middle, normed_second, hidden_pre = saved[6:]
    _, out_full, up_full, down_full, gain_pair = weights
    gains = gain_pair.astype(jnp.float32)
    grad_branch = grad_result.astype(jnp.bfloat16)
    hidden_act, gelu_pull = jax.vjp(partial(jax.nn.gelu, approximate=True), hidden_pre)
    hidden_low = hidden_act.astype(jnp.bfloat16)
    grad_act = reverse_matmul_answer(grad_branch, down_full)
    grad_pre = gelu_pull(grad_act)[0].astype(jnp.bfloat16)
    grad_normed_second = reverse_matmul_answer(grad_pre, up_full)
    unused_second, second_pull = jax.vjp(norm_apply, middle, gains[1])
    grad_middle_norm, grad_gain_second = second_pull(grad_normed_second)
    grad_middle = grad_result + grad_middle_norm
    grad_attn = grad_middle.astype(jnp.bfloat16)
    grad_mixed = reverse_matmul_answer(grad_attn, out_full).astype(jnp.bfloat16)
    left_rows = (mixed_low, normed_second, hidden_low)
    right_rows = (grad_attn, grad_pre, grad_branch)
    return (grad_middle, grad_mixed, left_rows, right_rows, grad_gain_second)


def entry_backward(saved, weights, cosine, sine, allowed, grad_middle, grad_mixed):
    resid, normed_first, query_rows, key_rows, value_rows, log_total = saved[:6]
    qkv_full = weights[0]
    gains = weights[4].astype(jnp.float32)
    rows = resid.shape[0]
    grad_query, grad_keys, grad_values = attend_backward(
        query_rows,
        key_rows,
        value_rows,
        allowed,
        log_total,
        grad_mixed.reshape(rows, HEADS, HEAD_DIM),
    )
    grad_query = unrotate(grad_query, cosine, sine).reshape(rows, MODEL_WIDTH)
    grad_keys = unrotate(grad_keys, cosine, sine).reshape(rows, MODEL_WIDTH)
    grad_values = grad_values.reshape(rows, MODEL_WIDTH)
    grad_projected = jnp.concatenate([grad_query, grad_keys, grad_values], axis=1).astype(
        jnp.bfloat16
    )
    grad_normed_first = reverse_matmul_answer(grad_projected, qkv_full)
    unused_first, first_pull = jax.vjp(norm_apply, resid, gains[0])
    grad_resid_norm, grad_gain_first = first_pull(grad_normed_first)
    return (grad_middle + grad_resid_norm, normed_first, grad_projected, grad_gain_first)


def body(
    patch_observations,
    sequence_labels,
    leading_filler_count,
    intake_latent_matrix,
    intake_latent_offset,
    intake_emit_matrix,
    intake_emit_offset,
    intake_shortcut_matrix,
    attention_entry_matrices,
    attention_merge_matrix,
    feedforward_widen_matrix,
    feedforward_shrink_matrix,
    layer_scale_factors,
    readout_latent_matrix,
    readout_latent_offset,
    readout_emit_matrix,
    readout_emit_offset,
    readout_shortcut_matrix,
    loss_sensitivity,
):
    patch_len = patch_observations.shape[1]
    position, pad_count, allowed, keep_rows = layout_rows(
        sequence_labels[0], leading_filler_count[0], patch_len
    )
    cosine, sine = rotary_tables(position, HEAD_DIM)
    columns = jnp.arange(patch_len, dtype=jnp.int32)
    pad_mask = columns[None, :] < pad_count[:, None]
    features = jnp.concatenate(
        [
            jnp.where(pad_mask, jnp.zeros_like(patch_observations), patch_observations),
            pad_mask.astype(jnp.bfloat16),
        ],
        axis=1,
    )
    entry_pre = (
        jnp.dot(features, intake_latent_matrix, preferred_element_type=jnp.float32)
        + intake_latent_offset
    )
    entry_hidden = jax.nn.silu(entry_pre).astype(jnp.bfloat16)
    resid = (
        jnp.dot(entry_hidden, intake_emit_matrix, preferred_element_type=jnp.float32)
        + intake_emit_offset
        + jnp.dot(features, intake_shortcut_matrix, preferred_element_type=jnp.float32)
    )
    layer_count = attention_entry_matrices.shape[0]
    group = lax.axis_size("head")
    group_place = lax.axis_index("head")
    outer = lax.axis_size("dp") // 8
    me = lax.axis_index("dp").astype(jnp.int32)
    places = (me & 7).reshape(1)
    own_count = layer_scale_factors.shape[2]
    rows = patch_observations.shape[0]

    group_width = readout_latent_offset.shape[0]
    offsets = jnp.stack([readout_latent_offset, readout_emit_offset])
    coarse = lax.reduce_precision(offsets, 8, 7)
    offset_rows = jnp.concatenate([coarse, offsets - coarse], axis=0).astype(jnp.bfloat16)
    offset_rows = jnp.pad(offset_rows, ((0, 12), (0, 0)))
    sent = jnp.concatenate(
        [
            loss_sensitivity.reshape(group, rows, group_width),
            jnp.broadcast_to(offset_rows[None], (group, 16, group_width)),
        ],
        axis=1,
    )
    gain_columns = layer_scale_factors.reshape(2 * layer_count, own_count).T
    gain_columns = jnp.pad(gain_columns, ((0, 0), (0, 128 - 2 * layer_count)))
    chunks = []
    for layer_index in range(layer_count):
        entry_own = attention_entry_matrices[layer_index]
        if layer_index == 0:
            entry_own = jnp.concatenate([entry_own, gain_columns], axis=1)
        chunks.append(entry_own)
        rest_own = jnp.concatenate(
            [
                attention_merge_matrix[layer_index],
                feedforward_widen_matrix[layer_index],
                feedforward_shrink_matrix[layer_index],
            ],
            axis=1,
        )
        chunks.append(rest_own)
    head_own = jnp.concatenate(
        [
            lax.dynamic_index_in_dim(
                matrix.reshape(outer, 8, -1, group_width), me % 8, 1, keepdims=False
            )
            for matrix in (readout_latent_matrix, readout_shortcut_matrix, readout_emit_matrix)
        ],
        axis=2,
    )
    chunks.append(head_own)
    count = len(chunks)

    def gather_chunk(number, own):
        if number < count - 1:
            return gather_head(own)
        return lax.all_gather(own, "head", axis=0, tiled=True)

    held = gather_chunk(0, chunks[0])
    cosine_wide = jnp.tile(jnp.concatenate([cosine[:, 0], cosine[:, 0]], axis=1), (1, HEADS))
    sine_wide = jnp.tile(jnp.concatenate([-sine[:, 0], sine[:, 0]], axis=1), (1, HEADS))
    tables = (cosine, sine, cosine_wide, sine_wide)
    nears, fars, near_mets = [], [], []
    layers = []
    onward = None
    for number in range(count + 1):
        step = {}
        if number < count:
            step["x"], step["y"] = swap(held, 1), swap(held, 2)
        if number + 1 < count:
            step["next"] = gather_chunk(number + 1, chunks[number + 1])
        if number == 0:
            step["resid"] = resid
            step["met"] = lax.all_to_all(
                after(sent, held), "head", split_axis=0, concat_axis=0, tiled=True
            )
        else:
            step["far"] = (swap(onward[0], 1), swap(onward[1], 2))
            near_mets.append([swap(part, 0) for part in after(nears[number - 1], onward)])
        if number > 1:
            chunk = number - 2
            far_met = [swap(part, 0) for part in after(fars[chunk], onward)]
            pieces = all_pieces(nears[chunk], fars[chunk], near_mets[chunk], far_met)
            if chunk == 0:
                gain_rows = place(places, pieces, [128], 3 * MODEL_WIDTH)[0][0]
                gain_rows = gain_rows[:, : 2 * layer_count].T.reshape(layer_count, 2, -1)
            if chunk % 2 == 0:
                layers.append(Layer(places, pieces, gain_rows[chunk // 2], tables, allowed))
                step["mixed"] = layers[-1].entry_forward(resid)
            else:
                layers[-1].add_rest(pieces)
                step["resid"] = layers[-1].rest_forward(mixed)
        step["own"] = chunks[number + 2 :]
        step = lax.optimization_barrier(step)
        chunks[number + 2 :] = step["own"]
        if number < count:
            nears.append((held, step["x"], step["y"]))
            onward = second_step(*nears[-1])
        held = step.get("next")
        if number > 0:
            fars.append(step["far"])
        resid = step.get("resid", resid)
        mixed = step.get("mixed")
        met = step.get("met") if number == 0 else met
    head_far_met = [swap(part, 0) for part in fars[-1]]
    head_pieces = all_pieces(nears[-1], fars[-1], near_mets[-1], head_far_met)
    head_whole = place(places, head_pieces, [3 * group_width])[0]

    sensitivity = met[:, :rows]
    head_offsets = met[:, rows : rows + 4].astype(jnp.float32)
    latent_offsets = head_offsets[:, 0] + head_offsets[:, 2]
    emit_offsets = head_offsets[:, 1] + head_offsets[:, 3]

    top = resid.astype(jnp.bfloat16)
    keep_column = keep_rows[:, None]
    two = 2 * group_width
    inner_parts = [
        jnp.dot(top, head_whole[part][:, :two], preferred_element_type=jnp.float32)
        for part in range(group)
    ]
    head_pre = jnp.concatenate(
        [inner_parts[part][:, :group_width] + latent_offsets[part] for part in range(group)],
        axis=1,
    )
    head_hidden = jax.nn.silu(head_pre).astype(jnp.bfloat16)
    forecast = jnp.stack(
        [
            (
                jnp.dot(
                    head_hidden, head_whole[part][:, two:], preferred_element_type=jnp.float32
                )
                + emit_offsets[part]
                + inner_parts[part][:, group_width:]
            )
            * keep_column
            for part in range(group)
        ]
    ).astype(jnp.bfloat16)
    token_predictions = lax.all_to_all(
        forecast, "head", split_axis=0, concat_axis=0, tiled=True
    ).reshape(group * rows, group_width)
    grad_forecast = (sensitivity.astype(jnp.float32) * keep_column).astype(jnp.bfloat16)
    grad_hidden = sum(
        reverse_matmul_answer(grad_forecast[part], head_whole[part][:, two:])
        for part in range(group)
    )
    unused_head, head_pull = jax.vjp(jax.nn.silu, head_pre)
    grad_head_pre = head_pull(grad_hidden)[0].astype(jnp.bfloat16)
    grad_resid = sum(
        reverse_matmul_answer(
            jnp.concatenate(
                [
                    grad_head_pre[:, part * group_width : (part + 1) * group_width],
                    grad_forecast[part],
                ],
                axis=1,
            ),
            head_whole[part][:, :two],
        )
        for part in range(group)
    )
    grad_forecast_rows = jnp.concatenate([grad_forecast[part] for part in range(group)], axis=1)
    head_bias_rows = (
        jnp.sum(grad_head_pre.astype(jnp.float32), axis=0),
        jnp.sum(grad_forecast_rows.astype(jnp.float32), axis=0),
    )
    head_both = exchange(
        [
            (top, grad_head_pre),
            (top, grad_forecast_rows),
            (head_hidden, grad_forecast_rows),
        ]
    )
    gain_sums = [[None, None] for _ in range(layer_count)]

    def rest_stage(layer_index, carry):
        outs = layers[layer_index].rest_backward(carry["grad"])
        gain_sums[layer_index][1] = outs[4]
        both = exchange(list(zip(outs[2], outs[3], strict=True)))
        return {"middle": outs[0], "mixed": outs[1]}, both

    def entry_stage(layer_index, carry):
        outs = layers[layer_index].entry_backward(carry["middle"], carry["mixed"])
        gain_sums[layer_index][0] = outs[3]
        return {"grad": outs[0]}, exchange([(outs[1], outs[2])])

    def input_stage(carry):
        head_rows = [row[None] for row in head_bias_rows]
        gain_rows = [row[None] for pair in gain_sums for row in pair]
        if layers[0].fetched and 2 + len(head_rows) + len(gain_rows) == EXTRA_ROWS:
            low, pre_low, grad_features, bias_rows = input_back(
                carry["grad"],
                entry_pre,
                intake_emit_matrix,
                intake_latent_matrix,
                intake_shortcut_matrix,
            )
            values_grad = jnp.where(pad_mask, 0.0, grad_features[:, :patch_len])
            vectors = jnp.concatenate([bias_rows, *head_rows, *gain_rows], axis=0)
            products = input_products(me, entry_hidden, low, pre_low, features, vectors)
            return values_grad, 4 * patch_len + EXTRA_ROWS, products
        grad_entry = carry["grad"].astype(jnp.bfloat16)
        grad_entry_outer = dyadic_accumulation(entry_hidden, grad_entry)
        grad_entry_outer_bias = jnp.sum(grad_entry.astype(jnp.float32), axis=0)
        grad_entry_skip = dyadic_accumulation(features, grad_entry)
        unused_entry, entry_pull = jax.vjp(jax.nn.silu, entry_pre)
        grad_entry_pre = entry_pull(reverse_matmul_answer(grad_entry, intake_emit_matrix))[0].astype(
            jnp.bfloat16
        )
        grad_entry_inner = dyadic_accumulation(features, grad_entry_pre)
        grad_entry_inner_bias = jnp.sum(grad_entry_pre.astype(jnp.float32), axis=0)
        grad_features = reverse_matmul_answer(
            grad_entry_pre, intake_latent_matrix
        ) + reverse_matmul_answer(grad_entry, intake_shortcut_matrix)
        values_grad = jnp.where(pad_mask, 0.0, grad_features[:, :patch_len])
        extra_rows = jnp.concatenate(
            [
                grad_entry_inner,
                grad_entry_skip,
                grad_entry_inner_bias[None],
                grad_entry_outer_bias[None],
            ]
            + head_rows
            + [row[None] for pair in gain_sums for row in pair],
            axis=0,
        )
        return values_grad, extra_rows.shape[0], entry_products(me, grad_entry_outer, extra_rows)

    stages = []
    for layer_index in reversed(range(layer_count)):
        stages += [(rest_stage, layer_index), (entry_stage, layer_index)]
    stage_count = len(stages)
    carry = {"grad": grad_resid}
    boths = {0: head_both}
    sums = {0: RowSums(*pair_products(me, head_both))}
    totals, finished = {}, {}
    entry_chunk = None
    done = 0

    def close(**step):
        step["sent"] = {n: (sums[n].sent, sums[n].later, sums[n].own) for n in sums}
        step["boths"] = boths
        step["carry"] = carry
        step = lax.optimization_barrier(step)
        for n, parts in step.pop("sent").items():
            sums[n].sent, sums[n].later, sums[n].own = parts
        return step

    step = close()
    for number in range(stage_count + 1):
        carry, boths = step["carry"], step["boths"]
        parts = {"first": sums[number].first()}
        if number >= 1:
            totals[number - 1] = sums.pop(number - 1).total()
            if number == 1:
                finished[0] = sum_columns(totals[0])
            else:
                finished[number - 1] = sum_group(totals[number - 1])
        if number >= 2:
            parts["finished"] = finished[number - 2]
        until = {stage_count - 2: stage_count}.get(number, number + 1)
        while done < min(until, stage_count):
            stage, layer_index = stages[done]
            carry, boths[done + 1] = stage(layer_index, carry)
            done += 1
        if number == stage_count - 1:
            values_grad, extra_count, entry_chunk = input_stage(carry)
            parts["entry"] = (entry_chunk.sent, entry_chunk.later, entry_chunk.own)
        if number == stage_count:
            parts["entry"] = entry_chunk.last()
        step = close(**parts)
        sums[number].met = step["first"]
        if number >= 2:
            finished[number - 2] = step["finished"]
        carry, boths = step["carry"], step["boths"]
        parts = {"last": sums[number].last()}
        if number == stage_count - 1:
            entry_chunk.sent, entry_chunk.later, entry_chunk.own = step["entry"]
            parts["entry"] = entry_chunk.first()
        if number == stage_count:
            entry_chunk.last_met = step["entry"]
            entry_total = entry_chunk.total()
        if number < stage_count:
            sums[number + 1] = RowSums(*pair_products(me, boths.pop(number + 1)))
            step = close(**parts)
        else:
            step = parts
        sums[number].last_met = step["last"]
        if number == stage_count - 1:
            entry_chunk.met = step["entry"]
    finished[stage_count] = sum_group_at_once(sums[stage_count].total())
    entry_main, entry_extra, entry_held = entry_everywhere(
        me, entry_total, own_count, extra_count
    )
    head_rows = gather_blocks(me, finished[0])
    head_sums = [after(head_rows[n], entry_held).astype(jnp.float32) for n in range(3)]
    layer_sums = [None] * layer_count
    for member, layer_index in enumerate(reversed(range(layer_count))):
        rest = finished[1 + 2 * member].astype(jnp.float32)
        entry = finished[2 + 2 * member].astype(jnp.float32)
        layer_sums[layer_index] = (entry[0], rest[0], rest[1], rest[2])
    inner_rows = 2 * patch_len
    last = 2 * inner_rows
    entry_sums = (
        entry_extra[:inner_rows],
        entry_extra[last],
        entry_main,
        entry_extra[last + 1],
        entry_extra[inner_rows:last],
    )
    head_bias_sums = lax.dynamic_slice_in_dim(
        entry_extra[last + 2 : last + 4], group_place * group_width, group_width, 1
    )
    own_place = (me * group + group_place) * own_count
    gains_grad = lax.dynamic_slice_in_dim(
        entry_extra[last + 4 : last + 4 + 2 * layer_count], own_place, own_count, 1
    ).reshape(layer_count, 2, own_count)
    qkv_grad = jnp.stack([layer_sums[member][0] for member in range(layer_count)])
    out_grad = jnp.stack([layer_sums[member][1] for member in range(layer_count)])
    up_grad = jnp.stack([layer_sums[member][2] for member in range(layer_count)])
    down_grad = jnp.stack([layer_sums[member][3] for member in range(layer_count)])
    return (
        token_predictions,
        values_grad,
        entry_sums[0],
        entry_sums[1],
        entry_sums[2],
        entry_sums[3],
        entry_sums[4],
        qkv_grad,
        out_grad,
        up_grad,
        down_grad,
        gains_grad,
        head_sums[0],
        head_bias_sums[0],
        head_sums[2],
        head_bias_sums[1],
        head_sums[1],
    )


def solution(mesh):
    return jax.shard_map(
        body,
        mesh=mesh,
        in_specs=(
            P(("dp", "head"), None),
            P(("dp", "head"), None),
            P(("dp", "head"), None),
            P(),
            P(),
            P(),
            P(),
            P(),
            P(None, ("dp", "head"), None),
            P(None, ("dp", "head"), None),
            P(None, ("dp", "head"), None),
            P(None, ("dp", "head"), None),
            P(None, None, ("dp", "head")),
            P(None, "head"),
            P("head"),
            P(None, "head"),
            P("head"),
            P(None, "head"),
            P("dp", "head"),
        ),
        out_specs=(
            P("dp", "head"),
            P(("dp", "head"), None),
            P(),
            P(),
            P(),
            P(),
            P(),
            P(None, ("dp", "head"), None),
            P(None, ("dp", "head"), None),
            P(None, ("dp", "head"), None),
            P(None, ("dp", "head"), None),
            P(None, None, ("dp", "head")),
            P(None, "head"),
            P("head"),
            P(None, "head"),
            P("head"),
            P(None, "head"),
        ),
        check_vma=False,
    )
```

```python
from functools import partial
import math

import jax
import jax.numpy as jnp
from jax import lax
from jax.experimental import pallas as pl
from jax.experimental.pallas import tpu as pltpu
from jax.sharding import PartitionSpec as P

MODEL_WIDTH = 1280
HEADS = 16
HEAD_DIM = 80


EPS = 1e-06
SMALL_COST = pl.CostEstimate(flops=1, bytes_accessed=1, transcendentals=0)
ROPE_BASE = 10000.0


def layout_rows(series_row, pad_row, patch_len):
    count = series_row.shape[0]
    order = jnp.arange(count, dtype=jnp.int32)
    same_series = series_row[:, None] == series_row[None, :]
    earlier = order[None, :] < order[:, None]
    position = jnp.sum(jnp.logical_and(same_series, earlier).astype(jnp.int32), axis=1)
    numbers = jnp.arange(pad_row.shape[0], dtype=jnp.int32)
    series_pad = jnp.sum(
        jnp.where(series_row[:, None] == numbers[None, :], pad_row[None, :], 0), axis=1
    )
    pad_count = jnp.where(position == 0, series_pad, 0)
    padded = pad_count == patch_len
    diagonal = order[:, None] == order[None, :]
    reach = jnp.logical_or(jnp.logical_and(earlier, jnp.logical_not(padded)[None, :]), diagonal)
    allowed = jnp.logical_and(same_series, reach)
    keep_rows = jnp.where(padded, 0.0, 1.0).astype(jnp.float32)
    return (position, pad_count, allowed, keep_rows)


def rotary_tables(position, head_dim):
    half = head_dim // 2
    steps = jnp.arange(half, dtype=jnp.float32) / half
    inverse = jnp.exp(-math.log(ROPE_BASE) * steps)
    angles = position.astype(jnp.float32)[:, None] * inverse[None, :]
    return (jnp.cos(angles)[:, None, :], jnp.sin(angles)[:, None, :])


def rotate(heads_rows, cosine, sine):
    half = heads_rows.shape[-1] // 2
    first = heads_rows[..., :half]
    second = heads_rows[..., half:]
    return jnp.concatenate(
        [first * cosine - second * sine, second * cosine + first * sine], axis=-1
    )


def unrotate(grad_rows, cosine, sine):
    half = grad_rows.shape[-1] // 2
    first = grad_rows[..., :half]
    second = grad_rows[..., half:]
    return jnp.concatenate(
        [first * cosine + second * sine, second * cosine - first * sine], axis=-1
    )


def norm_apply(resid, gain):
    return resid * lax.rsqrt(jnp.mean(resid * resid, axis=-1, keepdims=True) + EPS) * gain


def dyadic_accumulation(left, right):
    return lax.dot_general(
        left, right, (((0,), (0,)), ((), ())), preferred_element_type=jnp.float32
    )


def reverse_matmul_answer(grad_rows, weight):
    return lax.dot_general(
        grad_rows, weight, (((1,), (1,)), ((), ())), preferred_element_type=jnp.float32
    )


def masked_scores(query_rows, key_rows, allowed):
    scale = 1.0 / math.sqrt(query_rows.shape[-1])
    scores = (
        jnp.einsum("qhd,khd->hqk", query_rows, key_rows, preferred_element_type=jnp.float32) * scale
    )
    return jnp.where(allowed[None], scores, -1e30)


def attend_forward(query_rows, key_rows, value_rows, allowed):
    scores = masked_scores(query_rows, key_rows, allowed)
    peak = jnp.max(scores, axis=-1, keepdims=True)
    weights = jnp.exp(scores - peak)
    total = jnp.sum(weights, axis=-1, keepdims=True)
    probs = (weights / total).astype(jnp.bfloat16)
    mixed = jnp.einsum("hqk,khd->qhd", probs, value_rows, preferred_element_type=jnp.float32)
    return (mixed, peak + jnp.log(total))


def attend_backward(query_rows, key_rows, value_rows, allowed, log_total, grad_mixed):
    scale = 1.0 / math.sqrt(query_rows.shape[-1])
    scores = masked_scores(query_rows, key_rows, allowed)
    probs = jnp.where(allowed[None], jnp.exp(scores - log_total), 0.0)
    grad_probs = jnp.einsum(
        "qhd,khd->hqk", grad_mixed, value_rows, preferred_element_type=jnp.float32
    )
    grad_values = jnp.einsum(
        "hqk,qhd->khd", probs.astype(jnp.bfloat16), grad_mixed, preferred_element_type=jnp.float32
    )
    center = jnp.sum(grad_probs * probs, axis=-1, keepdims=True)
    grad_scores = (probs * (grad_probs - center)).astype(jnp.bfloat16)
    grad_query = (
        jnp.einsum("hqk,khd->qhd", grad_scores, key_rows, preferred_element_type=jnp.float32)
        * scale
    )
    grad_keys = (
        jnp.einsum("hqk,qhd->khd", grad_scores, query_rows, preferred_element_type=jnp.float32)
        * scale
    )
    return (grad_query, grad_keys, grad_values)


def after(value, *earlier):
    return lax.optimization_barrier((value, *earlier))[0]


def swap(v, bit):
    size = lax.axis_size("dp")
    return lax.ppermute(v, "dp", [(i, i ^ (1 << bit)) for i in range(size)])


def outer_groups():
    size = lax.axis_size("dp")
    return [[j + 8 * o for o in range(size // 8)] for j in range(8)]


def place_kernel(plan, piece_count, out_count, me_ref, *refs):
    pieces = refs[:piece_count]
    outs = refs[piece_count : piece_count + out_count]
    held = refs[piece_count + out_count : piece_count + 2 * out_count]
    in_sems, out_sems = refs[piece_count + 2 * out_count :]
    inward, outward = [], []
    for n, (piece, rel, row, out, column) in enumerate(plan):
        source = pieces[piece]
        width = held[out].shape[-1]
        if width != source.shape[-1]:
            source = source.at[:, :, pl.ds(column, width)]
        spot = (slice(None), me_ref[0] ^ rel, pl.ds(row, source.shape[1]), slice(None))
        inward.append(pltpu.make_async_copy(source, held[out].at[spot], in_sems.at[n]))
        outward.append(
            pltpu.make_async_copy(held[out].at[spot], outs[out].at[spot], out_sems.at[n])
        )
    for copy in inward:
        copy.start()
    for copy, onward in zip(inward, outward):
        copy.wait()
        onward.start()
    for onward in outward:
        onward.wait()


def place(me, pieces, widths, first=0):
    plan = []
    for n, (rel, row, _) in enumerate(pieces):
        column = first
        for out, width in enumerate(widths):
            plan.append((n, rel, row, out, column))
            column += width
    arrays = [array for _, _, array in pieces]
    lead, rows, _ = arrays[0].shape
    kind = arrays[0].dtype
    total = sum(8 * lead * rows * -(-w // 128) * 128 for w in widths) * 2
    outs = pl.pallas_call(
        partial(place_kernel, plan, len(arrays), len(widths)),
        out_shape=[jax.ShapeDtypeStruct((lead, 8, rows, w), kind) for w in widths],
        in_specs=[pl.BlockSpec(memory_space=pltpu.SMEM)]
        + [pl.BlockSpec(memory_space=pl.ANY)] * len(arrays),
        out_specs=[pl.BlockSpec(memory_space=pl.ANY)] * len(widths),
        scratch_shapes=[pltpu.VMEM((lead, 8, rows, w), kind) for w in widths]
        + [pltpu.SemaphoreType.DMA((len(plan),))] * 2,
        compiler_params=pltpu.CompilerParams(vmem_limit_bytes=total + (4 << 20)),
        cost_estimate=SMALL_COST,
    )(me, *arrays)
    outer = lax.axis_size("dp") // 8
    return [o.reshape(-1, outer * 8 * rows, o.shape[-1]) for o in outs]


def row_half(rows):
    return rows // 32 * 16 if rows >= 32 else rows // 2


def second_step(held, from_x, from_y):
    half = row_half(held.shape[1])
    return from_y[:, :half], from_x[:, half:]


def all_pieces(near, far, near_met, far_met):
    half = far[0].shape[1]
    places = ((0, 0), (2, 0), (4, 0), (6, 0), (6, half))
    pieces = []
    for (rel, row), array, met in zip(places, (*near, *far), (*near_met, *far_met), strict=True):
        pieces += [(rel, row, array), (rel | 1, row, met)]
    return pieces


def spread_rows(held):
    near = (held, swap(held, 1), swap(held, 2))
    onward_x, onward_y = second_step(*near)
    far = (swap(onward_x, 1), swap(onward_y, 2))
    return all_pieces(near, far, [swap(part, 0) for part in near], [swap(part, 0) for part in far])


def gather_head(own):
    held = lax.all_gather(own, "head", axis=0, tiled=True)[None]
    if lax.axis_size("dp") > 8:
        held = lax.all_gather(
            held, "dp", axis=0, tiled=True, axis_index_groups=outer_groups()
        )
    return held


def product_kernel(count, outer, me_ref, *refs):
    lefts, rights, met_lefts, met_rights = (refs[n * count : (n + 1) * count] for n in range(4))
    to_x, to_y, later, own, right_pair, turned = refs[4 * count :]
    rows, width = own.shape[1] // outer, own.shape[-1]
    tokens = lefts[0].shape[0]
    half = width // 2
    tile = half if half <= 640 else 640
    odd = me_ref[0] & 1 == 1
    chip = me_ref[0] >> 1

    def store(rel, n, span, side, columns, total):
        if rel == 0:
            own[n, span, slice(side * half + columns.start, side * half + columns.stop)] = total
        elif rel == 1 and side == 0:
            to_x[1, n, span, columns] = total
        elif rel == 1:
            later[1, n, span, columns] = total
        elif rel == 2 and side == 0:
            later[0, n, span, columns] = total
        elif rel == 2:
            to_y[1, n, span, columns] = total
        elif side == 0:
            to_x[0, n, span, columns] = total
        else:
            to_y[0, n, span, columns] = total

    for n in range(count):
        right_pair[:tokens] = rights[n][...]
        right_pair[tokens:] = met_rights[n][...]
        for part in range(outer):
            span = slice(part * rows, (part + 1) * rows)
            for place in range(4):
                first = (part * 8 + 2 * place) * rows
                near, far = slice(first, first + rows), slice(first + rows, first + 2 * rows)
                left_pair = jnp.concatenate(
                    [
                        jnp.where(odd, side[n][:, far], side[n][:, near]).astype(jnp.float32)
                        for side in (lefts, met_lefts)
                    ],
                    axis=0,
                )
                turned[place] = left_pair.T.astype(own.dtype)
            every = turned[...].reshape(4 * rows, 2 * tokens)
            for side in range(2):
                for at in range(0, half, tile):
                    total = jnp.dot(
                        every,
                        right_pair[:, side * half + at : side * half + at + tile],
                        preferred_element_type=jnp.float32,
                    ).astype(own.dtype)
                    for place in range(4):
                        for rel in range(4):
                            pl.when(chip ^ place == rel)(
                                partial(
                                    store,
                                    rel,
                                    n,
                                    span,
                                    side,
                                    slice(at, at + tile),
                                    total[place * rows : (place + 1) * rows],
                                )
                            )


def exchange(pairs):
    met = {}
    for pair in pairs:
        for rows in pair:
            if id(rows) not in met:
                met[id(rows)] = swap(rows, 0)
    return [(left, right, met[id(left)], met[id(right)]) for left, right in pairs]


def pair_products(me, both):
    outer = lax.axis_size("dp") // 8
    count = len(both)
    left, right = both[0][:2]
    block, width = left.shape[1] // 8, right.shape[1]
    low = jnp.bfloat16
    return pl.pallas_call(
        partial(product_kernel, count, outer),
        out_shape=[
            jax.ShapeDtypeStruct((2, count, block, width // 2), low),
            jax.ShapeDtypeStruct((2, count, block, width // 2), low),
            jax.ShapeDtypeStruct((2, count, block, width // 2), low),
            jax.ShapeDtypeStruct((count, block, width), low),
        ],
        in_specs=[pl.BlockSpec(memory_space=pltpu.SMEM)]
        + [pl.BlockSpec(memory_space=pltpu.VMEM)] * (4 * count),
        out_specs=[pl.BlockSpec(memory_space=pltpu.VMEM)] * 4,
        scratch_shapes=[
            pltpu.VMEM((2 * left.shape[0], width), low),
            pltpu.VMEM((4, block // outer, 2 * left.shape[0]), low),
        ],
        compiler_params=pltpu.CompilerParams(vmem_limit_bytes=44 << 20),
        cost_estimate=SMALL_COST,
    )((me & 7).reshape(1), *[part for parts in zip(*both, strict=True) for part in parts])


def low_sum(*parts):
    total = parts[0].astype(jnp.float32)
    for part in parts[1:]:
        total = total + part.astype(jnp.float32)
    return total.astype(jnp.bfloat16)


class RowSums:
    def __init__(self, to_x, to_y, later, own):
        self.sent, self.later, self.own = (to_x, to_y), later, own

    def first(self):
        return swap(self.sent[0], 1), swap(self.sent[1], 2)

    def last(self):
        return (
            swap(low_sum(self.later[0], self.met[0][0]), 2),
            swap(low_sum(self.later[1], self.met[1][0]), 1),
        )

    def total(self):
        half = self.own.shape[-1] // 2
        return jnp.concatenate(
            [
                low_sum(self.own[..., :half], self.met[0][1], self.last_met[0]),
                low_sum(self.own[..., half:], self.met[1][1], self.last_met[1]),
            ],
            axis=-1,
        )


def sum_group(total):
    outer = lax.axis_size("dp") // 8
    group = lax.axis_size("head")
    lead = total.shape[:-2]
    rows, columns = total.shape[-2:]
    if outer > 1:
        total = lax.psum_scatter(
            total.reshape(*lead, outer, rows // outer, columns),
            "dp",
            scatter_dimension=len(lead),
            tiled=True,
            axis_index_groups=outer_groups(),
        )
    total = total.reshape(*lead, rows // outer, columns)
    return lax.psum_scatter(total, "head", scatter_dimension=len(lead), tiled=True)


def sum_group_at_once(total):
    outer = lax.axis_size("dp") // 8
    group = lax.axis_size("head")
    if outer > 1:
        return sum_group(total).astype(jnp.float32)
    lead = total.shape[:-2]
    rows, columns = total.shape[-2:]
    total = total.reshape(*lead, group, rows // group, columns)
    axis = len(lead)
    met = lax.all_to_all(total, "head", split_axis=axis, concat_axis=axis, tiled=True)
    return jnp.sum(met.astype(jnp.float32), axis=axis)


def sum_columns(total):
    group = lax.axis_size("head")
    if lax.axis_size("dp") > 8:
        total = lax.psum(total, "dp", axis_index_groups=outer_groups())
    count, rows, columns = total.shape
    total = jnp.moveaxis(total.reshape(count, rows, group, columns // group), 2, 0)
    return lax.psum_scatter(total, "head", scatter_dimension=0, tiled=True)[0]


def gather_blocks(me, summed):
    outer = lax.axis_size("dp") // 8
    count, rows, columns = summed.shape
    if outer == 1:
        whole = lax.all_gather(summed, "dp", axis=0)
        return [whole[:, n].reshape(8 * rows, columns) for n in range(count)]
    held = summed.reshape(count * outer, rows // outer, columns)
    return place((me & 7).reshape(1), spread_rows(held), [columns])[0]


EXTRA_ROWS = 8


def entry_products(me, main, extra):
    group = lax.axis_size("head")
    outer = lax.axis_size("dp") // 8
    devices = 8 * outer * group
    columns = main.shape[1]
    own = main.shape[0] // devices
    extra = jnp.pad(extra, ((0, EXTRA_ROWS * devices - extra.shape[0]), (0, 0)))
    rows = jnp.concatenate(
        [main.reshape(devices, own, columns), extra.reshape(devices, EXTRA_ROWS, columns)], axis=1
    ).astype(jnp.bfloat16)
    view = rows.reshape(outer, 4, 2, group * (own + EXTRA_ROWS), columns)
    core = me & 1
    other = lax.dynamic_index_in_dim(view, 1 - core, 2, keepdims=False)
    pair = low_sum(lax.dynamic_index_in_dim(view, core, 2, keepdims=False), swap(other, 0))
    chip = (me & 7) >> 1
    half = columns // 2

    def picked(rel):
        return lax.dynamic_index_in_dim(pair, chip ^ rel, 1, keepdims=False).reshape(-1, columns)

    own_rows, at_x, at_y, far = (picked(rel) for rel in range(4))
    return RowSums(
        jnp.stack([far[:, :half], at_x[:, :half]]),
        jnp.stack([far[:, half:], at_y[:, half:]]),
        (at_y[:, :half], at_x[:, half:]),
        own_rows,
    )


def input_back_kernel(
    grad_ref, pre_ref, emit_ref, latent_ref, shortcut_ref, low_ref, pre_low_ref, sent_ref, bias_ref, wide
):
    low = grad_ref[...].astype(jnp.bfloat16)
    low_ref[...] = low
    rows_times_turned(low, emit_ref, 0, emit_ref.shape[1], wide, 256)
    pre = pre_ref[...]
    gate = 1.0 / (1.0 + jnp.exp(-pre))
    pre_low = (wide[...] * (gate * (1.0 + pre * (1.0 - gate)))).astype(jnp.bfloat16)
    pre_low_ref[...] = pre_low
    sent_ref[...] = reverse_matmul_answer(pre_low, latent_ref[...]) + reverse_matmul_answer(
        low, shortcut_ref[...]
    )
    bias_ref[0:1] = jnp.sum(pre_low.astype(jnp.float32), axis=0, keepdims=True)
    bias_ref[1:2] = jnp.sum(low.astype(jnp.float32), axis=0, keepdims=True)


def input_products_kernel(group, me_ref, *refs):
    hidden, met_hidden, low, met_low, pre_low, met_pre_low, features, met_features = refs[:8]
    vectors, met_vectors, to_x, to_y, later, own = refs[8:14]
    turned, low_pair, extras, block = refs[14:]
    tokens = hidden.shape[0]
    columns = low.shape[1]
    half = columns // 2
    core, chip = me_ref[0] & 1, me_ref[0] >> 1
    turned[:, :tokens] = hidden[...].astype(jnp.float32).T.astype(jnp.bfloat16)
    turned[:, tokens:] = met_hidden[...].astype(jnp.float32).T.astype(jnp.bfloat16)
    low_pair[:tokens] = low[...]
    low_pair[tokens:] = met_low[...]
    wide = features.shape[1]
    extras[...] = jnp.zeros_like(extras)
    extras[:wide] = dyadic_accumulation(features[...], pre_low[...]) + dyadic_accumulation(
        met_features[...], met_pre_low[...]
    )
    extras[wide : 2 * wide] = dyadic_accumulation(features[...], low[...]) + dyadic_accumulation(
        met_features[...], met_low[...]
    )
    extras[2 * wide : 2 * wide + vectors.shape[0]] = vectors[...] + met_vectors[...]
    rows = hidden.shape[1] // 8
    each = rows // group
    span = each + EXTRA_ROWS

    def store(rel, total):
        if rel == 0:
            own[0] = total
        elif rel == 1:
            to_x[1, 0] = total[:, :half]
            later[1, 0] = total[:, half:]
        elif rel == 2:
            later[0, 0] = total[:, :half]
            to_y[1, 0] = total[:, half:]
        else:
            to_x[0, 0] = total[:, :half]
            to_y[0, 0] = total[:, half:]

    for place in range(4):
        number = 2 * place + core
        first = pl.multiple_of(number * rows, rows)
        outer = jnp.dot(
            turned[pl.ds(first, rows), :], low_pair[...], preferred_element_type=jnp.float32
        )
        first = pl.multiple_of(number * group * EXTRA_ROWS, group * EXTRA_ROWS)
        extra = extras[pl.ds(first, group * EXTRA_ROWS), :]
        for member in range(group):
            block[member * span : member * span + each] = outer[member * each : (member + 1) * each]
            block[member * span + each : (member + 1) * span] = extra[
                member * EXTRA_ROWS : (member + 1) * EXTRA_ROWS
            ]
        total = block[...].astype(own.dtype)
        for rel in range(4):
            pl.when(chip ^ place == rel)(partial(store, rel, total))


def input_back(grad, pre, emit, latent, shortcut):
    rows, columns = grad.shape
    vmem = pl.BlockSpec(memory_space=pltpu.VMEM)
    return pl.pallas_call(
        input_back_kernel,
        out_shape=[
            jax.ShapeDtypeStruct((rows, columns), LOW),
            jax.ShapeDtypeStruct((rows, columns), LOW),
            jax.ShapeDtypeStruct((rows, latent.shape[0]), FULL),
            jax.ShapeDtypeStruct((2, columns), FULL),
        ],
        in_specs=[vmem] * 5,
        out_specs=[vmem] * 4,
        scratch_shapes=[pltpu.VMEM((rows, columns), FULL)],
        compiler_params=pltpu.CompilerParams(vmem_limit_bytes=32 << 20),
        cost_estimate=SMALL_COST,
    )(grad, pre, emit, latent, shortcut)


def input_products(me, hidden, low, pre_low, features, vectors):
    group = lax.axis_size("head")
    tokens, columns = low.shape
    width = hidden.shape[1]
    block = width // 8 + group * EXTRA_ROWS
    operands = []
    for rows in (hidden, low, pre_low, features, vectors):
        operands += [rows, swap(rows, 0)]
    pair = jax.ShapeDtypeStruct((2, 1, block, columns // 2), LOW)
    return RowSums(
        *pl.pallas_call(
            partial(input_products_kernel, group),
            out_shape=[pair, pair, pair, jax.ShapeDtypeStruct((1, block, columns), LOW)],
            in_specs=[pl.BlockSpec(memory_space=pltpu.SMEM)]
            + [pl.BlockSpec(memory_space=pltpu.VMEM)] * len(operands),
            out_specs=[pl.BlockSpec(memory_space=pltpu.VMEM)] * 4,
            scratch_shapes=[
                pltpu.VMEM((width, 2 * tokens), LOW),
                pltpu.VMEM((2 * tokens, columns), LOW),
                pltpu.VMEM((8 * group * EXTRA_ROWS, columns), FULL),
                pltpu.VMEM((block, columns), FULL),
            ],
            compiler_params=pltpu.CompilerParams(vmem_limit_bytes=32 << 20),
            cost_estimate=SMALL_COST,
        )((me & 7).reshape(1), *operands)
    )


def entry_kernel(plan, own, me_ref, *refs):
    pieces = refs[: len(plan)]
    main_ref, extra_ref, held, sems = refs[len(plan) :]
    copies = []
    for n, (rel, row, rows) in enumerate(plan):
        spot = held.at[me_ref[0] ^ rel, pl.ds(row, rows)]
        copies.append(pltpu.make_async_copy(pieces[n].at[0], spot, sems.at[n]))
    for copy in copies:
        copy.start()
    for copy in copies:
        copy.wait()
    span = own + EXTRA_ROWS
    group = held.shape[1] // span
    for block in range(8):
        rows = held[block].astype(jnp.float32)
        for member in range(group):
            main_ref[block * group + member] = rows[member * span : member * span + own]
            extra_ref[block * group + member] = rows[member * span + own : (member + 1) * span]


def entry_sums_of_group(total):
    total = total.reshape(-1, total.shape[-1])
    return sum_group_at_once(total).astype(total.dtype)


def entry_everywhere(me, summed, own, count):
    columns = summed.shape[-1]
    group = lax.axis_size("head")
    if lax.axis_size("dp") > 8:
        held = gather_head(summed)
    else:
        every = jnp.broadcast_to(summed[None], (group, *summed.shape))
        held = lax.all_to_all(every, "head", split_axis=0, concat_axis=0, tiled=True)
        held = held.reshape(1, -1, columns)
    pieces = spread_rows(held)
    places = (me & 7).reshape(1)
    span = own + EXTRA_ROWS
    if held.shape[0] > 1 or own % 8 or not in_kernel(pieces):
        (whole,) = place(places, pieces, [columns])
        whole = whole.reshape(-1, span, columns).astype(jnp.float32)
        return whole[:, :own].reshape(-1, columns), whole[:, own:].reshape(-1, columns)[:count], held
    rows = held.shape[1]
    blocks = 8 * rows // span
    plan = [(rel, row, array.shape[1]) for rel, row, array in pieces]
    vmem = pl.BlockSpec(memory_space=pltpu.VMEM)
    main, extra = pl.pallas_call(
        partial(entry_kernel, plan, own),
        out_shape=[
            jax.ShapeDtypeStruct((blocks, own, columns), jnp.float32),
            jax.ShapeDtypeStruct((blocks, EXTRA_ROWS, columns), jnp.float32),
        ],
        in_specs=[pl.BlockSpec(memory_space=pltpu.SMEM)]
        + [pl.BlockSpec(memory_space=pl.ANY)] * len(pieces),
        out_specs=[vmem, vmem],
        scratch_shapes=[
            pltpu.VMEM((8, rows, columns), held.dtype),
            pltpu.SemaphoreType.DMA((len(pieces),)),
        ],
        compiler_params=pltpu.CompilerParams(vmem_limit_bytes=44 << 20),
        cost_estimate=SMALL_COST,
    )(places, *[array for _, _, array in pieces])
    return main.reshape(-1, columns), extra.reshape(-1, columns)[:count], held


def fetch(plan, me, pieces, whole, sems):
    groups = []
    for group in range(whole.shape[1] // MODEL_WIDTH):
        columns = pl.ds(group * MODEL_WIDTH, MODEL_WIDTH)
        copies = []
        for n, (rel, row, rows) in enumerate(plan):
            first = pl.multiple_of((me ^ rel) * (whole.shape[0] // 8) + row, 16)
            copies.append(
                pltpu.make_async_copy(
                    pieces[n].at[0, :, columns],
                    whole.at[pl.ds(first, rows), columns],
                    sems.at[group * len(plan) + n],
                )
            )
        for copy in copies:
            copy.start()
        groups.append(copies)
    return groups


def arrive(copies):
    for copy in copies:
        copy.wait()


def rows_times(left, whole, first, out, tile):
    def step(n, _):
        at = pl.multiple_of(n * tile, 128)
        out[:, pl.ds(at, tile)] = jnp.dot(
            left, whole[:, pl.ds(first + at, tile)], preferred_element_type=jnp.float32
        )
        return 0

    lax.fori_loop(0, out.shape[1] // tile, step, 0)


def rows_times_turned(left, whole, first, width, out, tile):
    def step(n, _):
        at = pl.multiple_of(n * tile, 128)
        part = reverse_matmul_answer(whole[pl.ds(at, tile), pl.ds(first, width)], left)
        out[:, pl.ds(at, tile)] = part.T
        return 0

    lax.fori_loop(0, out.shape[1] // tile, step, 0)


def inverse_norm(rows):
    return lax.rsqrt(jnp.mean(rows * rows, axis=-1, keepdims=True) + EPS)


def other_half(rows):
    half = HEAD_DIM // 2
    lane = lax.broadcasted_iota(jnp.int32, rows.shape, 1) % HEAD_DIM
    ahead = pltpu.roll(rows, rows.shape[1] - half, 1)
    behind = pltpu.roll(rows, half, 1)
    return jnp.where(lane < half, ahead, behind)


def head_window(head, width):
    first = head * HEAD_DIM // 128 * 128
    last = min(-(-(head + 1) * HEAD_DIM // 128) * 128, width)
    start = head * HEAD_DIM - first
    lane = lax.broadcasted_iota(jnp.int32, (1, last - first), 1)
    return slice(first, last), jnp.logical_and(lane >= start, lane < start + HEAD_DIM)


def entry_forward_kernel(plan, me_ref, resid_ref, gain_ref, cosine_ref, sine_ref, allowed_ref, *refs):
    pieces = refs[: len(plan)]
    normed_ref, query_ref, key_ref, value_ref, total_ref, mixed_ref = refs[len(plan) : len(plan) + 6]
    whole, wide, sems = refs[len(plan) + 6 :]
    groups = fetch(plan, me_ref[0], pieces, whole, sems)
    resid = resid_ref[...]
    normed = (resid * inverse_norm(resid) * gain_ref[...]).astype(jnp.bfloat16)
    normed_ref[...] = normed
    for group, out in enumerate((query_ref, key_ref, value_ref)):
        arrive(groups[group])
        rows_times(normed, whole, group * MODEL_WIDTH, wide, 256)
        rows = wide[...]
        if group < 2:
            rows = rows * cosine_ref[...] + other_half(rows) * sine_ref[...]
        out[...] = rows.astype(jnp.bfloat16)
    scale = 1.0 / math.sqrt(HEAD_DIM)
    allowed = allowed_ref[...] > 0.0
    wide[...] = jnp.zeros_like(wide)
    totals = jnp.zeros(total_ref.shape, jnp.float32)
    head_lane = lax.broadcasted_iota(jnp.int32, total_ref.shape, 1)
    for head in range(HEADS):
        window, inside = head_window(head, MODEL_WIDTH)
        query = jnp.where(inside, query_ref[:, window], 0)
        scores = reverse_matmul_answer(query, key_ref[:, window]) * scale
        scores = jnp.where(allowed, scores, -1e30)
        peak = jnp.max(scores, axis=-1, keepdims=True)
        weights = jnp.exp(scores - peak)
        total = jnp.sum(weights, axis=-1, keepdims=True)
        probs = (weights / total).astype(jnp.bfloat16)
        mixed = jnp.dot(probs, value_ref[:, window], preferred_element_type=jnp.float32)
        wide[:, window] += jnp.where(inside, mixed, 0.0)
        totals = jnp.where(head_lane == head, peak + jnp.log(total), totals)
    total_ref[...] = totals
    mixed_ref[...] = wide[...].astype(jnp.bfloat16)


def gelu_parts(x):
    root = math.sqrt(2.0 / math.pi)
    bend = jnp.tanh(root * (x + 0.044715 * (x * x * x)))
    slope = 0.5 * (1.0 + bend) + 0.5 * x * (1.0 - bend * bend) * root * (
        1.0 + 3.0 * 0.044715 * (x * x)
    )
    return 0.5 * x * (1.0 + bend), slope


def rest_forward_kernel(plan, me_ref, resid_ref, mixed_ref, gain_ref, *refs):
    pieces = refs[: len(plan)]
    result_ref, middle_ref, normed_ref, pre_ref = refs[len(plan) : len(plan) + 4]
    whole, sems = refs[len(plan) + 4 :]
    groups = fetch(plan, me_ref[0], pieces, whole, sems)
    arrive(groups[0])
    rows_times(mixed_ref[...], whole, 0, middle_ref, 256)
    middle = resid_ref[...] + middle_ref[...]
    middle_ref[...] = middle
    normed = (middle * inverse_norm(middle) * gain_ref[...]).astype(jnp.bfloat16)
    normed_ref[...] = normed
    arrive(groups[1])
    rows_times(normed, whole, MODEL_WIDTH, pre_ref, 256)
    act = gelu_parts(pre_ref[...])[0].astype(jnp.bfloat16)
    arrive(groups[2])
    rows_times(act, whole, 2 * MODEL_WIDTH, result_ref, 256)
    result_ref[...] += middle_ref[...]


def norm_back(rows, gain, grad):
    inverse = inverse_norm(rows)
    scaled = grad * gain
    mean = jnp.mean(rows * scaled, axis=-1, keepdims=True)
    sent = inverse * scaled - rows * (inverse * inverse * inverse * mean)
    return sent, jnp.sum(grad * rows * inverse, axis=0, keepdims=True)


def rest_backward_kernel(plan, me_ref, grad_ref, middle_ref, pre_ref, gain_ref, *refs):
    pieces = refs[: len(plan)]
    outs = refs[len(plan) : len(plan) + 7]
    grad_middle_ref, mixed_ref, attn_ref, grad_pre_ref, branch_ref, act_ref, gain_grad_ref = outs
    whole, wide, sems = refs[len(plan) + 7 :]
    groups = fetch(plan, me_ref[0], pieces, whole, sems)
    grad = grad_ref[...]
    branch = grad.astype(jnp.bfloat16)
    branch_ref[...] = branch
    arrive(groups[2])
    rows_times_turned(branch, whole, 2 * MODEL_WIDTH, MODEL_WIDTH, wide, 256)
    act, slope = gelu_parts(pre_ref[...])
    act_ref[...] = act.astype(jnp.bfloat16)
    grad_pre = (wide[...] * slope).astype(jnp.bfloat16)
    grad_pre_ref[...] = grad_pre
    arrive(groups[1])
    rows_times_turned(grad_pre, whole, MODEL_WIDTH, MODEL_WIDTH, wide, 256)
    sent, gain_grad_ref[...] = norm_back(middle_ref[...], gain_ref[...], wide[...])
    grad_middle = grad + sent
    grad_middle_ref[...] = grad_middle
    attn = grad_middle.astype(jnp.bfloat16)
    attn_ref[...] = attn
    arrive(groups[0])
    rows_times_turned(attn, whole, 0, MODEL_WIDTH, wide, 256)
    mixed_ref[...] = wide[...].astype(jnp.bfloat16)


def entry_backward_kernel(
    plan,
    me_ref,
    grad_middle_ref,
    grad_mixed_ref,
    resid_ref,
    query_ref,
    key_ref,
    value_ref,
    total_ref,
    gain_ref,
    cosine_ref,
    sine_ref,
    allowed_ref,
    *refs,
):
    pieces = refs[: len(plan)]
    grad_resid_ref, projected_ref, gain_grad_ref = refs[len(plan) : len(plan) + 3]
    whole, grad_query, grad_key, grad_value, sems = refs[len(plan) + 3 :]
    groups = fetch(plan, me_ref[0], pieces, whole, sems)
    scale = 1.0 / math.sqrt(HEAD_DIM)
    allowed = allowed_ref[...] > 0.0
    totals = total_ref[...]
    grad_query[...] = jnp.zeros_like(grad_query)
    grad_key[...] = jnp.zeros_like(grad_key)
    grad_value[...] = jnp.zeros_like(grad_value)
    for head in range(HEADS):
        window, inside = head_window(head, MODEL_WIDTH)
        query = jnp.where(inside, query_ref[:, window], 0)
        keys = key_ref[:, window]
        grad_mixed = jnp.where(inside, grad_mixed_ref[:, window], 0)
        scores = reverse_matmul_answer(query, keys) * scale
        probs = jnp.where(allowed, jnp.exp(scores - totals[:, head : head + 1]), 0.0)
        grad_probs = reverse_matmul_answer(grad_mixed, value_ref[:, window])
        grad_value[:, window] += dyadic_accumulation(probs.astype(jnp.bfloat16), grad_mixed)
        center = jnp.sum(grad_probs * probs, axis=-1, keepdims=True)
        grad_scores = (probs * (grad_probs - center)).astype(jnp.bfloat16)
        along = jnp.dot(grad_scores, keys, preferred_element_type=jnp.float32)
        grad_query[:, window] += jnp.where(inside, along * scale, 0.0)
        grad_key[:, window] += dyadic_accumulation(grad_scores, query) * scale
    for group, part in enumerate((grad_query, grad_key, grad_value)):
        rows = part[...]
        if group < 2:
            rows = rows * cosine_ref[...] - other_half(rows) * sine_ref[...]
        projected_ref[:, group * MODEL_WIDTH : (group + 1) * MODEL_WIDTH] = rows.astype(jnp.bfloat16)
    for copies in groups:
        arrive(copies)
    rows_times_turned(projected_ref[...], whole, 0, 3 * MODEL_WIDTH, grad_query, 256)
    sent, gain_grad_ref[...] = norm_back(resid_ref[...], gain_ref[...], grad_query[...])
    grad_resid_ref[...] = grad_middle_ref[...] + sent


def whole_call(kernel, me, pieces, inputs, outs, wides):
    rows = inputs[0].shape[0]
    plan = [(rel, row, array.shape[1]) for rel, row, array in pieces]
    blocks = 8 * pieces[0][2].shape[1]
    columns = 3 * MODEL_WIDTH
    vmem = pl.BlockSpec(memory_space=pltpu.VMEM)
    return pl.pallas_call(
        partial(kernel, plan),
        out_shape=[jax.ShapeDtypeStruct(shape, kind) for shape, kind in outs],
        in_specs=[pl.BlockSpec(memory_space=pltpu.SMEM)]
        + [vmem] * len(inputs)
        + [pl.BlockSpec(memory_space=pl.ANY)] * len(pieces),
        out_specs=[vmem] * len(outs),
        scratch_shapes=[pltpu.VMEM((blocks, columns), jnp.bfloat16)]
        + [pltpu.VMEM((rows, MODEL_WIDTH), jnp.float32)] * wides
        + [pltpu.SemaphoreType.DMA((3 * len(pieces),))],
        compiler_params=pltpu.CompilerParams(vmem_limit_bytes=44 << 20),
        cost_estimate=SMALL_COST,
    )(me, *inputs, *[array for _, _, array in pieces])


def in_kernel(pieces):
    lead, rows, _ = pieces[0][2].shape
    return lead == 1 and rows % 32 == 0


LOW, FULL = jnp.bfloat16, jnp.float32


class Layer:
    def __init__(self, places, entry_pieces, gains, tables, allowed):
        self.places, self.entry_pieces, self.gains = places, entry_pieces, gains
        self.tables, self.allowed = tables, allowed
        self.fetched = in_kernel(entry_pieces)
        if not self.fetched:
            self.entry_whole = place(places, entry_pieces, [3 * MODEL_WIDTH])[0][0]

    def add_rest(self, rest_pieces):
        self.rest_pieces = rest_pieces
        if not self.fetched:
            self.rest_whole = [part[0] for part in place(self.places, rest_pieces, [MODEL_WIDTH] * 3)]

    def shapes(self, *kinds):
        rows = self.allowed.shape[0]
        return [((rows, width), kind) for width, kind in kinds]

    def entry_forward(self, resid):
        if not self.fetched:
            self.saved = entry_forward(
                resid, self.entry_whole, self.gains, *self.tables[:2], self.allowed
            )
            return self.saved[6]
        wide = (MODEL_WIDTH, LOW)
        self.resid = resid
        outs = whole_call(
            entry_forward_kernel,
            self.places,
            self.entry_pieces,
            (resid, self.gains[:1].astype(FULL), *self.tables[2:], self.allowed.astype(FULL)),
            self.shapes(wide, wide, wide, wide, (128, FULL), wide),
            1,
        )
        self.normed_first, self.heads = outs[0], outs[1:5]
        return outs[5]

    def rest_forward(self, mixed):
        if not self.fetched:
            result, self.saved = rest_forward(
                (*self.saved[:6], mixed), *self.rest_whole, self.gains
            )
            return result
        self.mixed = mixed
        result, self.middle, self.normed_second, self.hidden_pre = whole_call(
            rest_forward_kernel,
            self.places,
            self.rest_pieces,
            (self.resid, mixed, self.gains[1:].astype(FULL)),
            self.shapes(
                (MODEL_WIDTH, FULL), (MODEL_WIDTH, FULL), (MODEL_WIDTH, LOW), (MODEL_WIDTH, FULL)
            ),
            0,
        )
        return result

    def rest_backward(self, grad):
        if not self.fetched:
            weights = (self.entry_whole, *self.rest_whole, self.gains)
            return rest_backward(self.saved, weights, grad)
        wide = (MODEL_WIDTH, LOW)
        grad_middle, grad_mixed, grad_attn, grad_pre, branch, act, gain_grad = whole_call(
            rest_backward_kernel,
            self.places,
            self.rest_pieces,
            (grad, self.middle, self.hidden_pre, self.gains[1:].astype(FULL)),
            self.shapes((MODEL_WIDTH, FULL), wide, wide, wide, wide, wide)
            + [((1, MODEL_WIDTH), FULL)],
            1,
        )
        lefts = (self.mixed, self.normed_second, act)
        return grad_middle, grad_mixed, lefts, (grad_attn, grad_pre, branch), gain_grad[0]

    def entry_backward(self, grad_middle, grad_mixed):
        if not self.fetched:
            weights = (self.entry_whole, *self.rest_whole, self.gains)
            return entry_backward(
                self.saved, weights, *self.tables[:2], self.allowed, grad_middle, grad_mixed
            )
        grad_resid, projected, gain_grad = whole_call(
            entry_backward_kernel,
            self.places,
            self.entry_pieces,
            (
                grad_middle,
                grad_mixed,
                self.resid,
                *self.heads,
                self.gains[:1].astype(FULL),
                *self.tables[2:],
                self.allowed.astype(FULL),
            ),
            self.shapes((MODEL_WIDTH, FULL), (3 * MODEL_WIDTH, LOW)) + [((1, MODEL_WIDTH), FULL)],
            3,
        )
        return grad_resid, self.normed_first, projected, gain_grad[0]


def entry_forward(resid, qkv_full, gain_pair, cosine, sine, allowed):
    gains = gain_pair.astype(jnp.float32)
    rows = resid.shape[0]
    normed_first = norm_apply(resid, gains[0]).astype(jnp.bfloat16)
    projected = jnp.dot(normed_first, qkv_full, preferred_element_type=jnp.float32)
    query_rows = rotate(
        projected[:, :MODEL_WIDTH].reshape(rows, HEADS, HEAD_DIM), cosine, sine
    ).astype(jnp.bfloat16)
    key_rows = rotate(
        projected[:, MODEL_WIDTH : 2 * MODEL_WIDTH].reshape(rows, HEADS, HEAD_DIM), cosine, sine
    ).astype(jnp.bfloat16)
    value_rows = projected[:, 2 * MODEL_WIDTH :].reshape(rows, HEADS, HEAD_DIM).astype(jnp.bfloat16)

    mixed, log_total = attend_forward(query_rows, key_rows, value_rows, allowed)
    mixed_low = mixed.reshape(rows, MODEL_WIDTH).astype(jnp.bfloat16)
    return (resid, normed_first, query_rows, key_rows, value_rows, log_total, mixed_low)


def rest_forward(saved, out_full, up_full, down_full, gain_pair):
    gains = gain_pair.astype(jnp.float32)
    resid, mixed_low = saved[0], saved[6]
    middle = resid + jnp.dot(mixed_low, out_full, preferred_element_type=jnp.float32)
    normed_second = norm_apply(middle, gains[1]).astype(jnp.bfloat16)
    hidden_pre = jnp.dot(normed_second, up_full, preferred_element_type=jnp.float32)
    hidden_act = jax.nn.gelu(hidden_pre, approximate=True).astype(jnp.bfloat16)
    result = middle + jnp.dot(hidden_act, down_full, preferred_element_type=jnp.float32)
    return (result, (*saved, middle, normed_second, hidden_pre))


def rest_backward(saved, weights, grad_result):
    mixed_low, middle, normed_second, hidden_pre = saved[6:]
    _, out_full, up_full, down_full, gain_pair = weights
    gains = gain_pair.astype(jnp.float32)
    grad_branch = grad_result.astype(jnp.bfloat16)
    hidden_act, gelu_pull = jax.vjp(partial(jax.nn.gelu, approximate=True), hidden_pre)
    hidden_low = hidden_act.astype(jnp.bfloat16)
    grad_act = reverse_matmul_answer(grad_branch, down_full)
    grad_pre = gelu_pull(grad_act)[0].astype(jnp.bfloat16)
    grad_normed_second = reverse_matmul_answer(grad_pre, up_full)
    unused_second, second_pull = jax.vjp(norm_apply, middle, gains[1])
    grad_middle_norm, grad_gain_second = second_pull(grad_normed_second)
    grad_middle = grad_result + grad_middle_norm
    grad_attn = grad_middle.astype(jnp.bfloat16)
    grad_mixed = reverse_matmul_answer(grad_attn, out_full).astype(jnp.bfloat16)
    left_rows = (mixed_low, normed_second, hidden_low)
    right_rows = (grad_attn, grad_pre, grad_branch)
    return (grad_middle, grad_mixed, left_rows, right_rows, grad_gain_second)


def entry_backward(saved, weights, cosine, sine, allowed, grad_middle, grad_mixed):
    resid, normed_first, query_rows, key_rows, value_rows, log_total = saved[:6]
    qkv_full = weights[0]
    gains = weights[4].astype(jnp.float32)
    rows = resid.shape[0]
    grad_query, grad_keys, grad_values = attend_backward(
        query_rows,
        key_rows,
        value_rows,
        allowed,
        log_total,
        grad_mixed.reshape(rows, HEADS, HEAD_DIM),
    )
    grad_query = unrotate(grad_query, cosine, sine).reshape(rows, MODEL_WIDTH)
    grad_keys = unrotate(grad_keys, cosine, sine).reshape(rows, MODEL_WIDTH)
    grad_values = grad_values.reshape(rows, MODEL_WIDTH)
    grad_projected = jnp.concatenate([grad_query, grad_keys, grad_values], axis=1).astype(
        jnp.bfloat16
    )
    grad_normed_first = reverse_matmul_answer(grad_projected, qkv_full)
    unused_first, first_pull = jax.vjp(norm_apply, resid, gains[0])
    grad_resid_norm, grad_gain_first = first_pull(grad_normed_first)
    return (grad_middle + grad_resid_norm, normed_first, grad_projected, grad_gain_first)


def body(
    patch_observations,
    sequence_labels,
    leading_filler_count,
    intake_latent_matrix,
    intake_latent_offset,
    intake_emit_matrix,
    intake_emit_offset,
    intake_shortcut_matrix,
    attention_entry_matrices,
    attention_merge_matrix,
    feedforward_widen_matrix,
    feedforward_shrink_matrix,
    layer_scale_factors,
    readout_latent_matrix,
    readout_latent_offset,
    readout_emit_matrix,
    readout_emit_offset,
    readout_shortcut_matrix,
    loss_sensitivity,
):
    patch_len = patch_observations.shape[1]
    position, pad_count, allowed, keep_rows = layout_rows(
        sequence_labels[0], leading_filler_count[0], patch_len
    )
    cosine, sine = rotary_tables(position, HEAD_DIM)
    columns = jnp.arange(patch_len, dtype=jnp.int32)
    pad_mask = columns[None, :] < pad_count[:, None]
    features = jnp.concatenate(
        [
            jnp.where(pad_mask, jnp.zeros_like(patch_observations), patch_observations),
            pad_mask.astype(jnp.bfloat16),
        ],
        axis=1,
    )
    entry_pre = (
        jnp.dot(features, intake_latent_matrix, preferred_element_type=jnp.float32)
        + intake_latent_offset
    )
    entry_hidden = jax.nn.silu(entry_pre).astype(jnp.bfloat16)
    resid = (
        jnp.dot(entry_hidden, intake_emit_matrix, preferred_element_type=jnp.float32)
        + intake_emit_offset
        + jnp.dot(features, intake_shortcut_matrix, preferred_element_type=jnp.float32)
    )
    layer_count = attention_entry_matrices.shape[0]
    group = lax.axis_size("head")
    group_place = lax.axis_index("head")
    outer = lax.axis_size("dp") // 8
    me = lax.axis_index("dp").astype(jnp.int32)
    places = (me & 7).reshape(1)
    own_count = layer_scale_factors.shape[2]
    rows = patch_observations.shape[0]

    group_width = readout_latent_offset.shape[0]
    offsets = jnp.stack([readout_latent_offset, readout_emit_offset])
    coarse = lax.reduce_precision(offsets, 8, 7)
    offset_rows = jnp.concatenate([coarse, offsets - coarse], axis=0).astype(jnp.bfloat16)
    offset_rows = jnp.pad(offset_rows, ((0, 12), (0, 0)))
    sent = jnp.concatenate(
        [
            loss_sensitivity.reshape(group, rows, group_width),
            jnp.broadcast_to(offset_rows[None], (group, 16, group_width)),
        ],
        axis=1,
    )
    gain_columns = layer_scale_factors.reshape(2 * layer_count, own_count).T
    gain_columns = jnp.pad(gain_columns, ((0, 0), (0, 128 - 2 * layer_count)))
    chunks = []
    for layer_index in range(layer_count):
        entry_own = attention_entry_matrices[layer_index]
        if layer_index == 0:
            entry_own = jnp.concatenate([entry_own, gain_columns], axis=1)
        chunks.append(entry_own)
        rest_own = jnp.concatenate(
            [
                attention_merge_matrix[layer_index],
                feedforward_widen_matrix[layer_index],
                feedforward_shrink_matrix[layer_index],
            ],
            axis=1,
        )
        chunks.append(rest_own)
    head_own = jnp.concatenate(
        [
            lax.dynamic_index_in_dim(
                matrix.reshape(outer, 8, -1, group_width), me % 8, 1, keepdims=False
            )
            for matrix in (readout_latent_matrix, readout_shortcut_matrix, readout_emit_matrix)
        ],
        axis=2,
    )
    chunks.append(head_own)
    count = len(chunks)

    def gather_chunk(number, own):
        if number < count - 1:
            return gather_head(own)
        return lax.all_gather(own, "head", axis=0, tiled=True)

    held = gather_chunk(0, chunks[0])
    cosine_wide = jnp.tile(jnp.concatenate([cosine[:, 0], cosine[:, 0]], axis=1), (1, HEADS))
    sine_wide = jnp.tile(jnp.concatenate([-sine[:, 0], sine[:, 0]], axis=1), (1, HEADS))
    tables = (cosine, sine, cosine_wide, sine_wide)
    nears, fars, near_mets = [], [], []
    layers = []
    onward = None
    for number in range(count + 1):
        step = {}
        if number < count:
            step["x"], step["y"] = swap(held, 1), swap(held, 2)
        if number + 1 < count:
            step["next"] = gather_chunk(number + 1, chunks[number + 1])
        if number == count - 1:
            step["met"] = lax.all_to_all(
                after(sent, held), "head", split_axis=0, concat_axis=0, tiled=True
            )
        if number == 0:
            step["resid"] = resid
        else:
            step["far"] = (swap(onward[0], 1), swap(onward[1], 2))
            turn = step["far"] if number < count else onward
            near_mets.append([swap(part, 0) for part in after(nears[number - 1], turn)])
        if number > 1:
            chunk = number - 2
            far_met = [swap(part, 0) for part in after(fars[chunk], turn)]
            pieces = all_pieces(nears[chunk], fars[chunk], near_mets[chunk], far_met)
            if chunk == 0:
                gain_rows = place(places, pieces, [128], 3 * MODEL_WIDTH)[0][0]
                gain_rows = gain_rows[:, : 2 * layer_count].T.reshape(layer_count, 2, -1)
            if chunk % 2 == 0:
                layers.append(Layer(places, pieces, gain_rows[chunk // 2], tables, allowed))
                step["mixed"] = layers[-1].entry_forward(resid)
            else:
                layers[-1].add_rest(pieces)
                step["resid"] = layers[-1].rest_forward(mixed)
        step["own"] = chunks[number + 2 :]
        step = lax.optimization_barrier(step)
        chunks[number + 2 :] = step["own"]
        if number < count:
            nears.append((held, step["x"], step["y"]))
            onward = second_step(*nears[-1])
        held = step.get("next")
        if number > 0:
            fars.append(step["far"])
        resid = step.get("resid", resid)
        mixed = step.get("mixed")
        if "met" in step:
            met = step["met"]
    head_far_met = [swap(part, 0) for part in fars[-1]]
    head_pieces = all_pieces(nears[-1], fars[-1], near_mets[-1], head_far_met)
    head_whole = place(places, head_pieces, [3 * group_width])[0]

    sensitivity = met[:, :rows]
    head_offsets = met[:, rows : rows + 4].astype(jnp.float32)
    latent_offsets = head_offsets[:, 0] + head_offsets[:, 2]
    emit_offsets = head_offsets[:, 1] + head_offsets[:, 3]

    top = resid.astype(jnp.bfloat16)
    keep_column = keep_rows[:, None]
    two = 2 * group_width
    inner_parts = [
        jnp.dot(top, head_whole[part][:, :two], preferred_element_type=jnp.float32)
        for part in range(group)
    ]
    head_pre = jnp.concatenate(
        [inner_parts[part][:, :group_width] + latent_offsets[part] for part in range(group)],
        axis=1,
    )
    head_hidden = jax.nn.silu(head_pre).astype(jnp.bfloat16)
    forecast = jnp.stack(
        [
            (
                jnp.dot(
                    head_hidden, head_whole[part][:, two:], preferred_element_type=jnp.float32
                )
                + emit_offsets[part]
                + inner_parts[part][:, group_width:]
            )
            * keep_column
            for part in range(group)
        ]
    ).astype(jnp.bfloat16)
    token_predictions = lax.all_to_all(
        forecast, "head", split_axis=0, concat_axis=0, tiled=True
    ).reshape(group * rows, group_width)
    grad_forecast = (sensitivity.astype(jnp.float32) * keep_column).astype(jnp.bfloat16)
    grad_hidden = sum(
        reverse_matmul_answer(grad_forecast[part], head_whole[part][:, two:])
        for part in range(group)
    )
    unused_head, head_pull = jax.vjp(jax.nn.silu, head_pre)
    grad_head_pre = head_pull(grad_hidden)[0].astype(jnp.bfloat16)
    grad_resid = sum(
        reverse_matmul_answer(
            jnp.concatenate(
                [
                    grad_head_pre[:, part * group_width : (part + 1) * group_width],
                    grad_forecast[part],
                ],
                axis=1,
            ),
            head_whole[part][:, :two],
        )
        for part in range(group)
    )
    grad_forecast_rows = jnp.concatenate([grad_forecast[part] for part in range(group)], axis=1)
    head_bias_rows = (
        jnp.sum(grad_head_pre.astype(jnp.float32), axis=0),
        jnp.sum(grad_forecast_rows.astype(jnp.float32), axis=0),
    )
    head_both = exchange(
        [
            (top, grad_head_pre),
            (top, grad_forecast_rows),
            (head_hidden, grad_forecast_rows),
        ]
    )
    gain_sums = [[None, None] for _ in range(layer_count)]

    def rest_stage(layer_index, carry):
        outs = layers[layer_index].rest_backward(carry["grad"])
        gain_sums[layer_index][1] = outs[4]
        both = exchange(list(zip(outs[2], outs[3], strict=True)))
        return {"middle": outs[0], "mixed": outs[1]}, both

    def entry_stage(layer_index, carry):
        outs = layers[layer_index].entry_backward(carry["middle"], carry["mixed"])
        gain_sums[layer_index][0] = outs[3]
        return {"grad": outs[0]}, exchange([(outs[1], outs[2])])

    def input_stage(carry):
        head_rows = [row[None] for row in head_bias_rows]
        gain_rows = [row[None] for pair in gain_sums for row in pair]
        if layers[0].fetched and 2 + len(head_rows) + len(gain_rows) == EXTRA_ROWS:
            low, pre_low, grad_features, bias_rows = input_back(
                carry["grad"],
                entry_pre,
                intake_emit_matrix,
                intake_latent_matrix,
                intake_shortcut_matrix,
            )
            values_grad = jnp.where(pad_mask, 0.0, grad_features[:, :patch_len])
            vectors = jnp.concatenate([bias_rows, *head_rows, *gain_rows], axis=0)
            products = input_products(me, entry_hidden, low, pre_low, features, vectors)
            return values_grad, 4 * patch_len + EXTRA_ROWS, products
        grad_entry = carry["grad"].astype(jnp.bfloat16)
        grad_entry_outer = dyadic_accumulation(entry_hidden, grad_entry)
        grad_entry_outer_bias = jnp.sum(grad_entry.astype(jnp.float32), axis=0)
        grad_entry_skip = dyadic_accumulation(features, grad_entry)
        unused_entry, entry_pull = jax.vjp(jax.nn.silu, entry_pre)
        grad_entry_pre = entry_pull(reverse_matmul_answer(grad_entry, intake_emit_matrix))[0].astype(
            jnp.bfloat16
        )
        grad_entry_inner = dyadic_accumulation(features, grad_entry_pre)
        grad_entry_inner_bias = jnp.sum(grad_entry_pre.astype(jnp.float32), axis=0)
        grad_features = reverse_matmul_answer(
            grad_entry_pre, intake_latent_matrix
        ) + reverse_matmul_answer(grad_entry, intake_shortcut_matrix)
        values_grad = jnp.where(pad_mask, 0.0, grad_features[:, :patch_len])
        extra_rows = jnp.concatenate(
            [
                grad_entry_inner,
                grad_entry_skip,
                grad_entry_inner_bias[None],
                grad_entry_outer_bias[None],
            ]
            + head_rows
            + [row[None] for pair in gain_sums for row in pair],
            axis=0,
        )
        return values_grad, extra_rows.shape[0], entry_products(me, grad_entry_outer, extra_rows)

    stages = []
    for layer_index in reversed(range(layer_count)):
        stages += [(rest_stage, layer_index), (entry_stage, layer_index)]
    stage_count = len(stages)
    carry = {"grad": grad_resid}
    boths = {0: head_both}
    sums = {0: RowSums(*pair_products(me, head_both))}
    totals, finished = {}, {}
    entry_chunk = None
    done = 0

    def close(**step):
        step["sent"] = {n: (sums[n].sent, sums[n].later, sums[n].own) for n in sums}
        step["boths"] = boths
        step["carry"] = carry
        step = lax.optimization_barrier(step)
        for n, parts in step.pop("sent").items():
            sums[n].sent, sums[n].later, sums[n].own = parts
        return step

    step = close()
    for number in range(stage_count + 1):
        carry, boths = step["carry"], step["boths"]
        parts = {"first": sums[number].first()}
        if number >= 1:
            totals[number - 1] = sums.pop(number - 1).total()
            if number == 1:
                finished[0] = sum_columns(totals[0])
            else:
                finished[number - 1] = sum_group(totals[number - 1])
        if number >= 2:
            parts["finished"] = finished[number - 2]
        until = {stage_count - 2: stage_count}.get(number, number + 1)
        while done < min(until, stage_count):
            stage, layer_index = stages[done]
            carry, boths[done + 1] = stage(layer_index, carry)
            done += 1
        if number == stage_count - 1:
            parts["entry"] = entry_chunk.first()
        if number == stage_count:
            entry_total = entry_chunk.total()
            parts["entry"] = entry_sums_of_group(entry_total)
        step = close(**parts)
        sums[number].met = step["first"]
        if number >= 2:
            finished[number - 2] = step["finished"]
        carry, boths = step["carry"], step["boths"]
        parts = {"last": sums[number].last()}
        if number == stage_count - 2:
            values_grad, extra_count, entry_chunk = input_stage(carry)
            parts["entry"] = (entry_chunk.sent, entry_chunk.later, entry_chunk.own)
        if number == stage_count - 1:
            entry_chunk.met = step["entry"]
            parts["entry"] = entry_chunk.last()
        if number == stage_count:
            entry_summed = step["entry"]
        if number < stage_count:
            sums[number + 1] = RowSums(*pair_products(me, boths.pop(number + 1)))
            step = close(**parts)
        else:
            step = parts
        sums[number].last_met = step["last"]
        if number == stage_count - 2:
            entry_chunk.sent, entry_chunk.later, entry_chunk.own = step["entry"]
        if number == stage_count - 1:
            entry_chunk.last_met = step["entry"]
    finished[stage_count] = sum_group_at_once(sums[stage_count].total())
    entry_main, entry_extra, entry_held = entry_everywhere(
        me, entry_summed, own_count, extra_count
    )
    head_rows = gather_blocks(me, finished[0])
    head_sums = [after(head_rows[n], entry_held).astype(jnp.float32) for n in range(3)]
    layer_sums = [None] * layer_count
    for member, layer_index in enumerate(reversed(range(layer_count))):
        rest = finished[1 + 2 * member].astype(jnp.float32)
        entry = finished[2 + 2 * member].astype(jnp.float32)
        layer_sums[layer_index] = (entry[0], rest[0], rest[1], rest[2])
    inner_rows = 2 * patch_len
    last = 2 * inner_rows
    entry_sums = (
        entry_extra[:inner_rows],
        entry_extra[last],
        entry_main,
        entry_extra[last + 1],
        entry_extra[inner_rows:last],
    )
    head_bias_sums = lax.dynamic_slice_in_dim(
        entry_extra[last + 2 : last + 4], group_place * group_width, group_width, 1
    )
    own_place = (me * group + group_place) * own_count
    gains_grad = lax.dynamic_slice_in_dim(
        entry_extra[last + 4 : last + 4 + 2 * layer_count], own_place, own_count, 1
    ).reshape(layer_count, 2, own_count)
    qkv_grad = jnp.stack([layer_sums[member][0] for member in range(layer_count)])
    out_grad = jnp.stack([layer_sums[member][1] for member in range(layer_count)])
    up_grad = jnp.stack([layer_sums[member][2] for member in range(layer_count)])
    down_grad = jnp.stack([layer_sums[member][3] for member in range(layer_count)])
    return (
        token_predictions,
        values_grad,
        entry_sums[0],
        entry_sums[1],
        entry_sums[2],
        entry_sums[3],
        entry_sums[4],
        qkv_grad,
        out_grad,
        up_grad,
        down_grad,
        gains_grad,
        head_sums[0],
        head_bias_sums[0],
        head_sums[2],
        head_bias_sums[1],
        head_sums[1],
    )


def solution(mesh):
    return jax.shard_map(
        body,
        mesh=mesh,
        in_specs=(
            P(("dp", "head"), None),
            P(("dp", "head"), None),
            P(("dp", "head"), None),
            P(),
            P(),
            P(),
            P(),
            P(),
            P(None, ("dp", "head"), None),
            P(None, ("dp", "head"), None),
            P(None, ("dp", "head"), None),
            P(None, ("dp", "head"), None),
            P(None, None, ("dp", "head")),
            P(None, "head"),
            P("head"),
            P(None, "head"),
            P("head"),
            P(None, "head"),
            P("dp", "head"),
        ),
        out_specs=(
            P("dp", "head"),
            P(("dp", "head"), None),
            P(),
            P(),
            P(),
            P(),
            P(),
            P(None, ("dp", "head"), None),
            P(None, ("dp", "head"), None),
            P(None, ("dp", "head"), None),
            P(None, ("dp", "head"), None),
            P(None, None, ("dp", "head")),
            P(None, "head"),
            P("head"),
            P(None, "head"),
            P("head"),
            P(None, "head"),
        ),
        check_vma=False,
    )
```

```python
from functools import partial
import math

import jax
import jax.numpy as jnp
from jax import lax
from jax.experimental import pallas as pl
from jax.experimental.pallas import tpu as pltpu
from jax.sharding import PartitionSpec as P

MODEL_WIDTH = 1280
HEADS = 16
HEAD_DIM = 80


EPS = 1e-06
SMALL_COST = pl.CostEstimate(flops=1, bytes_accessed=1, transcendentals=0)
ROPE_BASE = 10000.0


def layout_rows(series_row, pad_row, patch_len):
    count = series_row.shape[0]
    order = jnp.arange(count, dtype=jnp.int32)
    same_series = series_row[:, None] == series_row[None, :]
    earlier = order[None, :] < order[:, None]
    position = jnp.sum(jnp.logical_and(same_series, earlier).astype(jnp.int32), axis=1)
    numbers = jnp.arange(pad_row.shape[0], dtype=jnp.int32)
    series_pad = jnp.sum(
        jnp.where(series_row[:, None] == numbers[None, :], pad_row[None, :], 0), axis=1
    )
    pad_count = jnp.where(position == 0, series_pad, 0)
    padded = pad_count == patch_len
    diagonal = order[:, None] == order[None, :]
    reach = jnp.logical_or(jnp.logical_and(earlier, jnp.logical_not(padded)[None, :]), diagonal)
    allowed = jnp.logical_and(same_series, reach)
    keep_rows = jnp.where(padded, 0.0, 1.0).astype(jnp.float32)
    return (position, pad_count, allowed, keep_rows)


def rotary_tables(position, head_dim):
    half = head_dim // 2
    steps = jnp.arange(half, dtype=jnp.float32) / half
    inverse = jnp.exp(-math.log(ROPE_BASE) * steps)
    angles = position.astype(jnp.float32)[:, None] * inverse[None, :]
    return (jnp.cos(angles)[:, None, :], jnp.sin(angles)[:, None, :])


def rotate(heads_rows, cosine, sine):
    half = heads_rows.shape[-1] // 2
    first = heads_rows[..., :half]
    second = heads_rows[..., half:]
    return jnp.concatenate(
        [first * cosine - second * sine, second * cosine + first * sine], axis=-1
    )


def unrotate(grad_rows, cosine, sine):
    half = grad_rows.shape[-1] // 2
    first = grad_rows[..., :half]
    second = grad_rows[..., half:]
    return jnp.concatenate(
        [first * cosine + second * sine, second * cosine - first * sine], axis=-1
    )


def norm_apply(resid, gain):
    return resid * lax.rsqrt(jnp.mean(resid * resid, axis=-1, keepdims=True) + EPS) * gain


def dyadic_accumulation(left, right):
    return lax.dot_general(
        left, right, (((0,), (0,)), ((), ())), preferred_element_type=jnp.float32
    )


def reverse_matmul_answer(grad_rows, weight):
    return lax.dot_general(
        grad_rows, weight, (((1,), (1,)), ((), ())), preferred_element_type=jnp.float32
    )


def masked_scores(query_rows, key_rows, allowed):
    scale = 1.0 / math.sqrt(query_rows.shape[-1])
    scores = (
        jnp.einsum("qhd,khd->hqk", query_rows, key_rows, preferred_element_type=jnp.float32) * scale
    )
    return jnp.where(allowed[None], scores, -1e30)


def attend_forward(query_rows, key_rows, value_rows, allowed):
    scores = masked_scores(query_rows, key_rows, allowed)
    peak = jnp.max(scores, axis=-1, keepdims=True)
    weights = jnp.exp(scores - peak)
    total = jnp.sum(weights, axis=-1, keepdims=True)
    probs = (weights / total).astype(jnp.bfloat16)
    mixed = jnp.einsum("hqk,khd->qhd", probs, value_rows, preferred_element_type=jnp.float32)
    return (mixed, peak + jnp.log(total))


def attend_backward(query_rows, key_rows, value_rows, allowed, log_total, grad_mixed):
    scale = 1.0 / math.sqrt(query_rows.shape[-1])
    scores = masked_scores(query_rows, key_rows, allowed)
    probs = jnp.where(allowed[None], jnp.exp(scores - log_total), 0.0)
    grad_probs = jnp.einsum(
        "qhd,khd->hqk", grad_mixed, value_rows, preferred_element_type=jnp.float32
    )
    grad_values = jnp.einsum(
        "hqk,qhd->khd", probs.astype(jnp.bfloat16), grad_mixed, preferred_element_type=jnp.float32
    )
    center = jnp.sum(grad_probs * probs, axis=-1, keepdims=True)
    grad_scores = (probs * (grad_probs - center)).astype(jnp.bfloat16)
    grad_query = (
        jnp.einsum("hqk,khd->qhd", grad_scores, key_rows, preferred_element_type=jnp.float32)
        * scale
    )
    grad_keys = (
        jnp.einsum("hqk,qhd->khd", grad_scores, query_rows, preferred_element_type=jnp.float32)
        * scale
    )
    return (grad_query, grad_keys, grad_values)


def after(value, *earlier):
    return lax.optimization_barrier((value, *earlier))[0]


def swap(v, bit):
    size = lax.axis_size("dp")
    return lax.ppermute(v, "dp", [(i, i ^ (1 << bit)) for i in range(size)])


def outer_groups():
    size = lax.axis_size("dp")
    return [[j + 8 * o for o in range(size // 8)] for j in range(8)]


def place_kernel(plan, piece_count, out_count, me_ref, *refs):
    pieces = refs[:piece_count]
    outs = refs[piece_count : piece_count + out_count]
    held = refs[piece_count + out_count : piece_count + 2 * out_count]
    in_sems, out_sems = refs[piece_count + 2 * out_count :]
    inward, outward = [], []
    for n, (piece, rel, row, out, column) in enumerate(plan):
        source = pieces[piece]
        width = held[out].shape[-1]
        if width != source.shape[-1]:
            source = source.at[:, :, pl.ds(column, width)]
        spot = (slice(None), me_ref[0] ^ rel, pl.ds(row, source.shape[1]), slice(None))
        inward.append(pltpu.make_async_copy(source, held[out].at[spot], in_sems.at[n]))
        outward.append(
            pltpu.make_async_copy(held[out].at[spot], outs[out].at[spot], out_sems.at[n])
        )
    for copy in inward:
        copy.start()
    for copy, onward in zip(inward, outward):
        copy.wait()
        onward.start()
    for onward in outward:
        onward.wait()


def place(me, pieces, widths, first=0):
    plan = []
    for n, (rel, row, _) in enumerate(pieces):
        column = first
        for out, width in enumerate(widths):
            plan.append((n, rel, row, out, column))
            column += width
    arrays = [array for _, _, array in pieces]
    lead, rows, _ = arrays[0].shape
    kind = arrays[0].dtype
    total = sum(8 * lead * rows * -(-w // 128) * 128 for w in widths) * 2
    outs = pl.pallas_call(
        partial(place_kernel, plan, len(arrays), len(widths)),
        out_shape=[jax.ShapeDtypeStruct((lead, 8, rows, w), kind) for w in widths],
        in_specs=[pl.BlockSpec(memory_space=pltpu.SMEM)]
        + [pl.BlockSpec(memory_space=pl.ANY)] * len(arrays),
        out_specs=[pl.BlockSpec(memory_space=pl.ANY)] * len(widths),
        scratch_shapes=[pltpu.VMEM((lead, 8, rows, w), kind) for w in widths]
        + [pltpu.SemaphoreType.DMA((len(plan),))] * 2,
        compiler_params=pltpu.CompilerParams(vmem_limit_bytes=total + (4 << 20)),
        cost_estimate=SMALL_COST,
    )(me, *arrays)
    outer = lax.axis_size("dp") // 8
    return [o.reshape(-1, outer * 8 * rows, o.shape[-1]) for o in outs]


def row_half(rows):
    return rows // 32 * 16 if rows >= 32 else rows // 2


def second_step(held, from_x, from_y):
    half = row_half(held.shape[1])
    return from_y[:, :half], from_x[:, half:]


def all_pieces(near, far, near_met, far_met):
    half = far[0].shape[1]
    places = ((0, 0), (2, 0), (4, 0), (6, 0), (6, half))
    pieces = []
    for (rel, row), array, met in zip(places, (*near, *far), (*near_met, *far_met), strict=True):
        pieces += [(rel, row, array), (rel | 1, row, met)]
    return pieces


def spread_rows(held):
    near = (held, swap(held, 1), swap(held, 2))
    onward_x, onward_y = second_step(*near)
    far = (swap(onward_x, 1), swap(onward_y, 2))
    return all_pieces(near, far, [swap(part, 0) for part in near], [swap(part, 0) for part in far])


def gather_head(own):
    held = lax.all_gather(own, "head", axis=0, tiled=True)[None]
    if lax.axis_size("dp") > 8:
        held = lax.all_gather(
            held, "dp", axis=0, tiled=True, axis_index_groups=outer_groups()
        )
    return held


def product_kernel(count, outer, me_ref, *refs):
    lefts, rights, met_lefts, met_rights = (refs[n * count : (n + 1) * count] for n in range(4))
    to_x, to_y, later, own, right_pair, turned = refs[4 * count :]
    rows, width = own.shape[1] // outer, own.shape[-1]
    tokens = lefts[0].shape[0]
    half = width // 2
    tile = half if half <= 640 else 640
    odd = me_ref[0] & 1 == 1
    chip = me_ref[0] >> 1

    def store(rel, n, span, side, columns, total):
        if rel == 0:
            own[n, span, slice(side * half + columns.start, side * half + columns.stop)] = total
        elif rel == 1 and side == 0:
            to_x[1, n, span, columns] = total
        elif rel == 1:
            later[1, n, span, columns] = total
        elif rel == 2 and side == 0:
            later[0, n, span, columns] = total
        elif rel == 2:
            to_y[1, n, span, columns] = total
        elif side == 0:
            to_x[0, n, span, columns] = total
        else:
            to_y[0, n, span, columns] = total

    for n in range(count):
        right_pair[:tokens] = rights[n][...]
        right_pair[tokens:] = met_rights[n][...]
        for part in range(outer):
            span = slice(part * rows, (part + 1) * rows)
            for place in range(4):
                first = (part * 8 + 2 * place) * rows
                near, far = slice(first, first + rows), slice(first + rows, first + 2 * rows)
                left_pair = jnp.concatenate(
                    [
                        jnp.where(odd, side[n][:, far], side[n][:, near]).astype(jnp.float32)
                        for side in (lefts, met_lefts)
                    ],
                    axis=0,
                )
                turned[place] = left_pair.T.astype(own.dtype)
            every = turned[...].reshape(4 * rows, 2 * tokens)
            for side in range(2):
                for at in range(0, half, tile):
                    total = jnp.dot(
                        every,
                        right_pair[:, side * half + at : side * half + at + tile],
                        preferred_element_type=jnp.float32,
                    ).astype(own.dtype)
                    for place in range(4):
                        for rel in range(4):
                            pl.when(chip ^ place == rel)(
                                partial(
                                    store,
                                    rel,
                                    n,
                                    span,
                                    side,
                                    slice(at, at + tile),
                                    total[place * rows : (place + 1) * rows],
                                )
                            )


def exchange(pairs):
    met = {}
    for pair in pairs:
        for rows in pair:
            if id(rows) not in met:
                met[id(rows)] = swap(rows, 0)
    return [(left, right, met[id(left)], met[id(right)]) for left, right in pairs]


def pair_products(me, both):
    outer = lax.axis_size("dp") // 8
    count = len(both)
    left, right = both[0][:2]
    block, width = left.shape[1] // 8, right.shape[1]
    low = jnp.bfloat16
    return pl.pallas_call(
        partial(product_kernel, count, outer),
        out_shape=[
            jax.ShapeDtypeStruct((2, count, block, width // 2), low),
            jax.ShapeDtypeStruct((2, count, block, width // 2), low),
            jax.ShapeDtypeStruct((2, count, block, width // 2), low),
            jax.ShapeDtypeStruct((count, block, width), low),
        ],
        in_specs=[pl.BlockSpec(memory_space=pltpu.SMEM)]
        + [pl.BlockSpec(memory_space=pltpu.VMEM)] * (4 * count),
        out_specs=[pl.BlockSpec(memory_space=pltpu.VMEM)] * 4,
        scratch_shapes=[
            pltpu.VMEM((2 * left.shape[0], width), low),
            pltpu.VMEM((4, block // outer, 2 * left.shape[0]), low),
        ],
        compiler_params=pltpu.CompilerParams(vmem_limit_bytes=44 << 20),
        cost_estimate=SMALL_COST,
    )((me & 7).reshape(1), *[part for parts in zip(*both, strict=True) for part in parts])


def low_sum(*parts):
    total = parts[0].astype(jnp.float32)
    for part in parts[1:]:
        total = total + part.astype(jnp.float32)
    return total.astype(jnp.bfloat16)


class RowSums:
    def __init__(self, to_x, to_y, later, own):
        self.sent, self.later, self.own = (to_x, to_y), later, own

    def first(self):
        return swap(self.sent[0], 1), swap(self.sent[1], 2)

    def last(self):
        return (
            swap(low_sum(self.later[0], self.met[0][0]), 2),
            swap(low_sum(self.later[1], self.met[1][0]), 1),
        )

    def total(self):
        half = self.own.shape[-1] // 2
        return jnp.concatenate(
            [
                low_sum(self.own[..., :half], self.met[0][1], self.last_met[0]),
                low_sum(self.own[..., half:], self.met[1][1], self.last_met[1]),
            ],
            axis=-1,
        )


def sum_group(total):
    outer = lax.axis_size("dp") // 8
    group = lax.axis_size("head")
    lead = total.shape[:-2]
    rows, columns = total.shape[-2:]
    if outer > 1:
        total = lax.psum_scatter(
            total.reshape(*lead, outer, rows // outer, columns),
            "dp",
            scatter_dimension=len(lead),
            tiled=True,
            axis_index_groups=outer_groups(),
        )
    total = total.reshape(*lead, rows // outer, columns)
    return lax.psum_scatter(total, "head", scatter_dimension=len(lead), tiled=True)


def sum_group_at_once(total):
    outer = lax.axis_size("dp") // 8
    group = lax.axis_size("head")
    if outer > 1:
        return sum_group(total).astype(jnp.float32)
    lead = total.shape[:-2]
    rows, columns = total.shape[-2:]
    total = total.reshape(*lead, group, rows // group, columns)
    axis = len(lead)
    met = lax.all_to_all(total, "head", split_axis=axis, concat_axis=axis, tiled=True)
    return jnp.sum(met.astype(jnp.float32), axis=axis)


def sum_columns(total):
    group = lax.axis_size("head")
    if lax.axis_size("dp") > 8:
        total = lax.psum(total, "dp", axis_index_groups=outer_groups())
    count, rows, columns = total.shape
    total = jnp.moveaxis(total.reshape(count, rows, group, columns // group), 2, 0)
    return lax.psum_scatter(total, "head", scatter_dimension=0, tiled=True)[0]


def gather_blocks(me, summed):
    outer = lax.axis_size("dp") // 8
    count, rows, columns = summed.shape
    if outer == 1:
        whole = lax.all_gather(summed, "dp", axis=0)
        return [whole[:, n].reshape(8 * rows, columns) for n in range(count)]
    held = summed.reshape(count * outer, rows // outer, columns)
    return place((me & 7).reshape(1), spread_rows(held), [columns])[0]


EXTRA_ROWS = 8


def entry_products(me, main, extra):
    group = lax.axis_size("head")
    outer = lax.axis_size("dp") // 8
    devices = 8 * outer * group
    columns = main.shape[1]
    own = main.shape[0] // devices
    extra = jnp.pad(extra, ((0, EXTRA_ROWS * devices - extra.shape[0]), (0, 0)))
    rows = jnp.concatenate(
        [main.reshape(devices, own, columns), extra.reshape(devices, EXTRA_ROWS, columns)], axis=1
    ).astype(jnp.bfloat16)
    view = rows.reshape(outer, 4, 2, group * (own + EXTRA_ROWS), columns)
    core = me & 1
    other = lax.dynamic_index_in_dim(view, 1 - core, 2, keepdims=False)
    pair = low_sum(lax.dynamic_index_in_dim(view, core, 2, keepdims=False), swap(other, 0))
    chip = (me & 7) >> 1
    half = columns // 2

    def picked(rel):
        return lax.dynamic_index_in_dim(pair, chip ^ rel, 1, keepdims=False).reshape(-1, columns)

    own_rows, at_x, at_y, far = (picked(rel) for rel in range(4))
    return RowSums(
        jnp.stack([far[:, :half], at_x[:, :half]]),
        jnp.stack([far[:, half:], at_y[:, half:]]),
        (at_y[:, :half], at_x[:, half:]),
        own_rows,
    )


def silu_parts(x):
    gate = 1.0 / (1.0 + jnp.exp(-x))
    return x * gate, gate * (1.0 + x * (1.0 - gate))


def output_kernel(
    plan, me_ref, top_ref, keep_ref, latent_offset, emit_offset, sensitivity, *refs
):
    pieces = refs[: len(plan)]
    hidden_ref, forecast_ref, pre_low_ref, grad_ref, bias_ref = refs[len(plan) : len(plan) + 5]
    whole, pre, skips, sent, both, sems = refs[len(plan) + 5 :]
    group, width, _ = whole.shape
    each = sensitivity.shape[2]
    two = 2 * each
    rows = width // 8
    copies = []
    for n, (rel, row, count) in enumerate(plan):
        first = pl.multiple_of((me_ref[0] ^ rel) * rows + row, 16)
        spot = whole.at[:, pl.ds(first, count), :]
        copies.append(pltpu.make_async_copy(pieces[n], spot, sems.at[n]))
    for copy in copies:
        copy.start()
    for copy in copies:
        copy.wait()
    top = top_ref[...]
    keep = keep_ref[...]
    for part in range(group):
        rows_times(top, whole.at[part], 0, both, 128)
        pre[:, part * each : (part + 1) * each] = both[:, :each] + latent_offset[part : part + 1]
        skips[part] = both[:, each:two] + emit_offset[part : part + 1]
    hidden, slope = silu_parts(pre[...])
    hidden = hidden.astype(jnp.bfloat16)
    hidden_ref[...] = hidden
    for part in range(group):
        emitted = jnp.dot(hidden, whole[part, :, two:], preferred_element_type=jnp.float32)
        forecast_ref[part] = ((emitted + skips[part]) * keep).astype(jnp.bfloat16)

    def back_hidden(n, _):
        at = pl.multiple_of(n * 256, 256)
        total = reverse_matmul_answer(whole[0, pl.ds(at, 256), two:], sensitivity[0])
        for part in range(1, group):
            total += reverse_matmul_answer(whole[part, pl.ds(at, 256), two:], sensitivity[part])
        grad_ref[:, pl.ds(at, 256)] = total.T
        return 0

    lax.fori_loop(0, width // 256, back_hidden, 0)
    pre[...] = grad_ref[...] * slope
    pre_low_ref[...] = pre[...].astype(jnp.bfloat16)
    bias_ref[...] = jnp.sum(pre_low_ref[...].astype(jnp.float32), axis=0, keepdims=True)
    for part in range(group):
        both[:, :each] = pre[:, part * each : (part + 1) * each]
        both[:, each:] = sensitivity[part].astype(jnp.float32)
        sent[part] = both[...].astype(jnp.bfloat16)

    def back_top(n, _):
        at = pl.multiple_of(n * 256, 256)
        total = reverse_matmul_answer(whole[0, pl.ds(at, 256), :two], sent[0])
        for part in range(1, group):
            total += reverse_matmul_answer(whole[part, pl.ds(at, 256), :two], sent[part])
        grad_ref[:, pl.ds(at, 256)] = total.T
        return 0

    lax.fori_loop(0, width // 256, back_top, 0)


def output_block(me, pieces, top, keep, latent_offsets, emit_offsets, grad_forecast):
    plan = [(rel, row, array.shape[1]) for rel, row, array in pieces]
    group, rows, each = grad_forecast.shape
    width = top.shape[1]
    vmem = pl.BlockSpec(memory_space=pltpu.VMEM)
    return pl.pallas_call(
        partial(output_kernel, plan),
        out_shape=[
            jax.ShapeDtypeStruct((rows, width), LOW),
            jax.ShapeDtypeStruct((group, rows, each), LOW),
            jax.ShapeDtypeStruct((rows, width), LOW),
            jax.ShapeDtypeStruct((rows, width), FULL),
            jax.ShapeDtypeStruct((1, width), FULL),
        ],
        in_specs=[pl.BlockSpec(memory_space=pltpu.SMEM)]
        + [vmem] * 5
        + [pl.BlockSpec(memory_space=pl.ANY)] * len(pieces),
        out_specs=[vmem] * 5,
        scratch_shapes=[
            pltpu.VMEM((group, width, 3 * each), LOW),
            pltpu.VMEM((rows, width), FULL),
            pltpu.VMEM((group, rows, each), FULL),
            pltpu.VMEM((group, rows, 2 * each), LOW),
            pltpu.VMEM((rows, 2 * each), FULL),
            pltpu.SemaphoreType.DMA((len(pieces),)),
        ],
        compiler_params=pltpu.CompilerParams(vmem_limit_bytes=44 << 20),
        cost_estimate=SMALL_COST,
    )(
        me,
        top,
        keep,
        latent_offsets,
        emit_offsets,
        grad_forecast,
        *[array for _, _, array in pieces],
    )


def output_plain(head_whole, top, keep, latent_offsets, emit_offsets, grad_forecast):
    group, _, each = grad_forecast.shape
    two = 2 * each
    inner_parts = [
        jnp.dot(top, head_whole[part][:, :two], preferred_element_type=jnp.float32)
        for part in range(group)
    ]
    head_pre = jnp.concatenate(
        [inner_parts[part][:, :each] + latent_offsets[part] for part in range(group)], axis=1
    )
    hidden, slope = silu_parts(head_pre)
    hidden = hidden.astype(jnp.bfloat16)
    forecast = jnp.stack(
        [
            (
                jnp.dot(hidden, head_whole[part][:, two:], preferred_element_type=jnp.float32)
                + emit_offsets[part]
                + inner_parts[part][:, each:]
            )
            * keep
            for part in range(group)
        ]
    ).astype(jnp.bfloat16)
    grad_hidden = sum(
        reverse_matmul_answer(grad_forecast[part], head_whole[part][:, two:])
        for part in range(group)
    )
    pre_low = (grad_hidden * slope).astype(jnp.bfloat16)
    grad_top = sum(
        reverse_matmul_answer(
            jnp.concatenate(
                [pre_low[:, part * each : (part + 1) * each], grad_forecast[part]], axis=1
            ),
            head_whole[part][:, :two],
        )
        for part in range(group)
    )
    return hidden, forecast, pre_low, grad_top, jnp.sum(pre_low.astype(FULL), axis=0, keepdims=True)


def input_back_kernel(
    grad_ref, pre_ref, emit_ref, latent_ref, shortcut_ref, low_ref, pre_low_ref, sent_ref, bias_ref, wide
):
    low = grad_ref[...].astype(jnp.bfloat16)
    low_ref[...] = low
    rows_times_turned(low, emit_ref, 0, emit_ref.shape[1], wide, 256)
    pre = pre_ref[...]
    gate = 1.0 / (1.0 + jnp.exp(-pre))
    pre_low = (wide[...] * (gate * (1.0 + pre * (1.0 - gate)))).astype(jnp.bfloat16)
    pre_low_ref[...] = pre_low
    sent_ref[...] = reverse_matmul_answer(pre_low, latent_ref[...]) + reverse_matmul_answer(
        low, shortcut_ref[...]
    )
    bias_ref[0:1] = jnp.sum(pre_low.astype(jnp.float32), axis=0, keepdims=True)
    bias_ref[1:2] = jnp.sum(low.astype(jnp.float32), axis=0, keepdims=True)


def input_products_kernel(group, me_ref, *refs):
    hidden, met_hidden, low, met_low, pre_low, met_pre_low, features, met_features = refs[:8]
    vectors, met_vectors, to_x, to_y, later, own = refs[8:14]
    turned, low_pair, extras, block = refs[14:]
    tokens = hidden.shape[0]
    columns = low.shape[1]
    half = columns // 2
    core, chip = me_ref[0] & 1, me_ref[0] >> 1
    turned[:, :tokens] = hidden[...].astype(jnp.float32).T.astype(jnp.bfloat16)
    turned[:, tokens:] = met_hidden[...].astype(jnp.float32).T.astype(jnp.bfloat16)
    low_pair[:tokens] = low[...]
    low_pair[tokens:] = met_low[...]
    wide = features.shape[1]
    extras[...] = jnp.zeros_like(extras)
    extras[:wide] = dyadic_accumulation(features[...], pre_low[...]) + dyadic_accumulation(
        met_features[...], met_pre_low[...]
    )
    extras[wide : 2 * wide] = dyadic_accumulation(features[...], low[...]) + dyadic_accumulation(
        met_features[...], met_low[...]
    )
    extras[2 * wide : 2 * wide + vectors.shape[0]] = vectors[...] + met_vectors[...]
    rows = hidden.shape[1] // 8
    each = rows // group
    span = each + EXTRA_ROWS

    def store(rel, total):
        if rel == 0:
            own[0] = total
        elif rel == 1:
            to_x[1, 0] = total[:, :half]
            later[1, 0] = total[:, half:]
        elif rel == 2:
            later[0, 0] = total[:, :half]
            to_y[1, 0] = total[:, half:]
        else:
            to_x[0, 0] = total[:, :half]
            to_y[0, 0] = total[:, half:]

    for place in range(4):
        number = 2 * place + core
        first = pl.multiple_of(number * rows, rows)
        outer = jnp.dot(
            turned[pl.ds(first, rows), :], low_pair[...], preferred_element_type=jnp.float32
        )
        first = pl.multiple_of(number * group * EXTRA_ROWS, group * EXTRA_ROWS)
        extra = extras[pl.ds(first, group * EXTRA_ROWS), :]
        for member in range(group):
            block[member * span : member * span + each] = outer[member * each : (member + 1) * each]
            block[member * span + each : (member + 1) * span] = extra[
                member * EXTRA_ROWS : (member + 1) * EXTRA_ROWS
            ]
        total = block[...].astype(own.dtype)
        for rel in range(4):
            pl.when(chip ^ place == rel)(partial(store, rel, total))


def input_back(grad, pre, emit, latent, shortcut):
    rows, columns = grad.shape
    vmem = pl.BlockSpec(memory_space=pltpu.VMEM)
    return pl.pallas_call(
        input_back_kernel,
        out_shape=[
            jax.ShapeDtypeStruct((rows, columns), LOW),
            jax.ShapeDtypeStruct((rows, columns), LOW),
            jax.ShapeDtypeStruct((rows, latent.shape[0]), FULL),
            jax.ShapeDtypeStruct((2, columns), FULL),
        ],
        in_specs=[vmem] * 5,
        out_specs=[vmem] * 4,
        scratch_shapes=[pltpu.VMEM((rows, columns), FULL)],
        compiler_params=pltpu.CompilerParams(vmem_limit_bytes=32 << 20),
        cost_estimate=SMALL_COST,
    )(grad, pre, emit, latent, shortcut)


def input_products(me, hidden, low, pre_low, features, vectors):
    group = lax.axis_size("head")
    tokens, columns = low.shape
    width = hidden.shape[1]
    block = width // 8 + group * EXTRA_ROWS
    operands = []
    for rows in (hidden, low, pre_low, features, vectors):
        operands += [rows, swap(rows, 0)]
    pair = jax.ShapeDtypeStruct((2, 1, block, columns // 2), LOW)
    return RowSums(
        *pl.pallas_call(
            partial(input_products_kernel, group),
            out_shape=[pair, pair, pair, jax.ShapeDtypeStruct((1, block, columns), LOW)],
            in_specs=[pl.BlockSpec(memory_space=pltpu.SMEM)]
            + [pl.BlockSpec(memory_space=pltpu.VMEM)] * len(operands),
            out_specs=[pl.BlockSpec(memory_space=pltpu.VMEM)] * 4,
            scratch_shapes=[
                pltpu.VMEM((width, 2 * tokens), LOW),
                pltpu.VMEM((2 * tokens, columns), LOW),
                pltpu.VMEM((8 * group * EXTRA_ROWS, columns), FULL),
                pltpu.VMEM((block, columns), FULL),
            ],
            compiler_params=pltpu.CompilerParams(vmem_limit_bytes=32 << 20),
            cost_estimate=SMALL_COST,
        )((me & 7).reshape(1), *operands)
    )


def entry_kernel(plan, own, me_ref, *refs):
    pieces = refs[: len(plan)]
    main_ref, extra_ref, held, sems = refs[len(plan) :]
    copies = []
    for n, (rel, row, rows) in enumerate(plan):
        spot = held.at[me_ref[0] ^ rel, pl.ds(row, rows)]
        copies.append(pltpu.make_async_copy(pieces[n].at[0], spot, sems.at[n]))
    for copy in copies:
        copy.start()
    for copy in copies:
        copy.wait()
    span = own + EXTRA_ROWS
    group = held.shape[1] // span
    for block in range(8):
        rows = held[block].astype(jnp.float32)
        for member in range(group):
            main_ref[block * group + member] = rows[member * span : member * span + own]
            extra_ref[block * group + member] = rows[member * span + own : (member + 1) * span]


def entry_sums_of_group(total):
    total = total.reshape(-1, total.shape[-1])
    return sum_group_at_once(total).astype(total.dtype)


def entry_everywhere(me, summed, own, count):
    columns = summed.shape[-1]
    group = lax.axis_size("head")
    if lax.axis_size("dp") > 8:
        held = gather_head(summed)
    else:
        every = jnp.broadcast_to(summed[None], (group, *summed.shape))
        held = lax.all_to_all(every, "head", split_axis=0, concat_axis=0, tiled=True)
        held = held.reshape(1, -1, columns)
    pieces = spread_rows(held)
    places = (me & 7).reshape(1)
    span = own + EXTRA_ROWS
    if held.shape[0] > 1 or own % 8 or not in_kernel(pieces):
        (whole,) = place(places, pieces, [columns])
        whole = whole.reshape(-1, span, columns).astype(jnp.float32)
        return whole[:, :own].reshape(-1, columns), whole[:, own:].reshape(-1, columns)[:count], held
    rows = held.shape[1]
    blocks = 8 * rows // span
    plan = [(rel, row, array.shape[1]) for rel, row, array in pieces]
    vmem = pl.BlockSpec(memory_space=pltpu.VMEM)
    main, extra = pl.pallas_call(
        partial(entry_kernel, plan, own),
        out_shape=[
            jax.ShapeDtypeStruct((blocks, own, columns), jnp.float32),
            jax.ShapeDtypeStruct((blocks, EXTRA_ROWS, columns), jnp.float32),
        ],
        in_specs=[pl.BlockSpec(memory_space=pltpu.SMEM)]
        + [pl.BlockSpec(memory_space=pl.ANY)] * len(pieces),
        out_specs=[vmem, vmem],
        scratch_shapes=[
            pltpu.VMEM((8, rows, columns), held.dtype),
            pltpu.SemaphoreType.DMA((len(pieces),)),
        ],
        compiler_params=pltpu.CompilerParams(vmem_limit_bytes=44 << 20),
        cost_estimate=SMALL_COST,
    )(places, *[array for _, _, array in pieces])
    return main.reshape(-1, columns), extra.reshape(-1, columns)[:count], held


def fetch(plan, me, pieces, whole, sems):
    groups = []
    for group in range(whole.shape[1] // MODEL_WIDTH):
        columns = pl.ds(group * MODEL_WIDTH, MODEL_WIDTH)
        copies = []
        for n, (rel, row, rows) in enumerate(plan):
            first = pl.multiple_of((me ^ rel) * (whole.shape[0] // 8) + row, 16)
            copies.append(
                pltpu.make_async_copy(
                    pieces[n].at[0, :, columns],
                    whole.at[pl.ds(first, rows), columns],
                    sems.at[group * len(plan) + n],
                )
            )
        for copy in copies:
            copy.start()
        groups.append(copies)
    return groups


def arrive(copies):
    for copy in copies:
        copy.wait()


def rows_times(left, whole, first, out, tile):
    def step(n, _):
        at = pl.multiple_of(n * tile, 128)
        out[:, pl.ds(at, tile)] = jnp.dot(
            left, whole[:, pl.ds(first + at, tile)], preferred_element_type=jnp.float32
        )
        return 0

    lax.fori_loop(0, out.shape[1] // tile, step, 0)


def rows_times_turned(left, whole, first, width, out, tile):
    def step(n, _):
        at = pl.multiple_of(n * tile, 128)
        part = reverse_matmul_answer(whole[pl.ds(at, tile), pl.ds(first, width)], left)
        out[:, pl.ds(at, tile)] = part.T
        return 0

    lax.fori_loop(0, out.shape[1] // tile, step, 0)


def inverse_norm(rows):
    return lax.rsqrt(jnp.mean(rows * rows, axis=-1, keepdims=True) + EPS)


def other_half(rows):
    half = HEAD_DIM // 2
    lane = lax.broadcasted_iota(jnp.int32, rows.shape, 1) % HEAD_DIM
    ahead = pltpu.roll(rows, rows.shape[1] - half, 1)
    behind = pltpu.roll(rows, half, 1)
    return jnp.where(lane < half, ahead, behind)


def head_window(head, width):
    first = head * HEAD_DIM // 128 * 128
    last = min(-(-(head + 1) * HEAD_DIM // 128) * 128, width)
    start = head * HEAD_DIM - first
    lane = lax.broadcasted_iota(jnp.int32, (1, last - first), 1)
    return slice(first, last), jnp.logical_and(lane >= start, lane < start + HEAD_DIM)


def entry_forward_kernel(plan, me_ref, resid_ref, gain_ref, cosine_ref, sine_ref, allowed_ref, *refs):
    pieces = refs[: len(plan)]
    normed_ref, query_ref, key_ref, value_ref, total_ref, mixed_ref = refs[len(plan) : len(plan) + 6]
    whole, wide, sems = refs[len(plan) + 6 :]
    groups = fetch(plan, me_ref[0], pieces, whole, sems)
    resid = resid_ref[...]
    normed = (resid * inverse_norm(resid) * gain_ref[...]).astype(jnp.bfloat16)
    normed_ref[...] = normed
    for group, out in enumerate((query_ref, key_ref, value_ref)):
        arrive(groups[group])
        rows_times(normed, whole, group * MODEL_WIDTH, wide, 256)
        rows = wide[...]
        if group < 2:
            rows = rows * cosine_ref[...] + other_half(rows) * sine_ref[...]
        out[...] = rows.astype(jnp.bfloat16)
    scale = 1.0 / math.sqrt(HEAD_DIM)
    allowed = allowed_ref[...] > 0.0
    wide[...] = jnp.zeros_like(wide)
    totals = jnp.zeros(total_ref.shape, jnp.float32)
    head_lane = lax.broadcasted_iota(jnp.int32, total_ref.shape, 1)
    for head in range(HEADS):
        window, inside = head_window(head, MODEL_WIDTH)
        query = jnp.where(inside, query_ref[:, window], 0)
        scores = reverse_matmul_answer(query, key_ref[:, window]) * scale
        scores = jnp.where(allowed, scores, -1e30)
        peak = jnp.max(scores, axis=-1, keepdims=True)
        weights = jnp.exp(scores - peak)
        total = jnp.sum(weights, axis=-1, keepdims=True)
        probs = (weights / total).astype(jnp.bfloat16)
        mixed = jnp.dot(probs, value_ref[:, window], preferred_element_type=jnp.float32)
        wide[:, window] += jnp.where(inside, mixed, 0.0)
        totals = jnp.where(head_lane == head, peak + jnp.log(total), totals)
    total_ref[...] = totals
    mixed_ref[...] = wide[...].astype(jnp.bfloat16)


def gelu_parts(x):
    root = math.sqrt(2.0 / math.pi)
    bend = jnp.tanh(root * (x + 0.044715 * (x * x * x)))
    slope = 0.5 * (1.0 + bend) + 0.5 * x * (1.0 - bend * bend) * root * (
        1.0 + 3.0 * 0.044715 * (x * x)
    )
    return 0.5 * x * (1.0 + bend), slope


def rest_forward_kernel(plan, me_ref, resid_ref, mixed_ref, gain_ref, *refs):
    pieces = refs[: len(plan)]
    result_ref, middle_ref, normed_ref, pre_ref = refs[len(plan) : len(plan) + 4]
    whole, sems = refs[len(plan) + 4 :]
    groups = fetch(plan, me_ref[0], pieces, whole, sems)
    arrive(groups[0])
    rows_times(mixed_ref[...], whole, 0, middle_ref, 256)
    middle = resid_ref[...] + middle_ref[...]
    middle_ref[...] = middle
    normed = (middle * inverse_norm(middle) * gain_ref[...]).astype(jnp.bfloat16)
    normed_ref[...] = normed
    arrive(groups[1])
    rows_times(normed, whole, MODEL_WIDTH, pre_ref, 256)
    act = gelu_parts(pre_ref[...])[0].astype(jnp.bfloat16)
    arrive(groups[2])
    rows_times(act, whole, 2 * MODEL_WIDTH, result_ref, 256)
    result_ref[...] += middle_ref[...]


def norm_back(rows, gain, grad):
    inverse = inverse_norm(rows)
    scaled = grad * gain
    mean = jnp.mean(rows * scaled, axis=-1, keepdims=True)
    sent = inverse * scaled - rows * (inverse * inverse * inverse * mean)
    return sent, jnp.sum(grad * rows * inverse, axis=0, keepdims=True)


def rest_backward_kernel(plan, me_ref, grad_ref, middle_ref, pre_ref, gain_ref, *refs):
    pieces = refs[: len(plan)]
    outs = refs[len(plan) : len(plan) + 7]
    grad_middle_ref, mixed_ref, attn_ref, grad_pre_ref, branch_ref, act_ref, gain_grad_ref = outs
    whole, wide, sems = refs[len(plan) + 7 :]
    groups = fetch(plan, me_ref[0], pieces, whole, sems)
    grad = grad_ref[...]
    branch = grad.astype(jnp.bfloat16)
    branch_ref[...] = branch
    arrive(groups[2])
    rows_times_turned(branch, whole, 2 * MODEL_WIDTH, MODEL_WIDTH, wide, 256)
    act, slope = gelu_parts(pre_ref[...])
    act_ref[...] = act.astype(jnp.bfloat16)
    grad_pre = (wide[...] * slope).astype(jnp.bfloat16)
    grad_pre_ref[...] = grad_pre
    arrive(groups[1])
    rows_times_turned(grad_pre, whole, MODEL_WIDTH, MODEL_WIDTH, wide, 256)
    sent, gain_grad_ref[...] = norm_back(middle_ref[...], gain_ref[...], wide[...])
    grad_middle = grad + sent
    grad_middle_ref[...] = grad_middle
    attn = grad_middle.astype(jnp.bfloat16)
    attn_ref[...] = attn
    arrive(groups[0])
    rows_times_turned(attn, whole, 0, MODEL_WIDTH, wide, 256)
    mixed_ref[...] = wide[...].astype(jnp.bfloat16)


def entry_backward_kernel(
    plan,
    me_ref,
    grad_middle_ref,
    grad_mixed_ref,
    resid_ref,
    query_ref,
    key_ref,
    value_ref,
    total_ref,
    gain_ref,
    cosine_ref,
    sine_ref,
    allowed_ref,
    *refs,
):
    pieces = refs[: len(plan)]
    grad_resid_ref, projected_ref, gain_grad_ref = refs[len(plan) : len(plan) + 3]
    whole, grad_query, grad_key, grad_value, sems = refs[len(plan) + 3 :]
    groups = fetch(plan, me_ref[0], pieces, whole, sems)
    scale = 1.0 / math.sqrt(HEAD_DIM)
    allowed = allowed_ref[...] > 0.0
    totals = total_ref[...]
    grad_query[...] = jnp.zeros_like(grad_query)
    grad_key[...] = jnp.zeros_like(grad_key)
    grad_value[...] = jnp.zeros_like(grad_value)
    for head in range(HEADS):
        window, inside = head_window(head, MODEL_WIDTH)
        query = jnp.where(inside, query_ref[:, window], 0)
        keys = key_ref[:, window]
        grad_mixed = jnp.where(inside, grad_mixed_ref[:, window], 0)
        scores = reverse_matmul_answer(query, keys) * scale
        probs = jnp.where(allowed, jnp.exp(scores - totals[:, head : head + 1]), 0.0)
        grad_probs = reverse_matmul_answer(grad_mixed, value_ref[:, window])
        grad_value[:, window] += dyadic_accumulation(probs.astype(jnp.bfloat16), grad_mixed)
        center = jnp.sum(grad_probs * probs, axis=-1, keepdims=True)
        grad_scores = (probs * (grad_probs - center)).astype(jnp.bfloat16)
        along = jnp.dot(grad_scores, keys, preferred_element_type=jnp.float32)
        grad_query[:, window] += jnp.where(inside, along * scale, 0.0)
        grad_key[:, window] += dyadic_accumulation(grad_scores, query) * scale
    for group, part in enumerate((grad_query, grad_key, grad_value)):
        rows = part[...]
        if group < 2:
            rows = rows * cosine_ref[...] - other_half(rows) * sine_ref[...]
        projected_ref[:, group * MODEL_WIDTH : (group + 1) * MODEL_WIDTH] = rows.astype(jnp.bfloat16)
    for copies in groups:
        arrive(copies)
    rows_times_turned(projected_ref[...], whole, 0, 3 * MODEL_WIDTH, grad_query, 256)
    sent, gain_grad_ref[...] = norm_back(resid_ref[...], gain_ref[...], grad_query[...])
    grad_resid_ref[...] = grad_middle_ref[...] + sent


def whole_call(kernel, me, pieces, inputs, outs, wides):
    rows = inputs[0].shape[0]
    plan = [(rel, row, array.shape[1]) for rel, row, array in pieces]
    blocks = 8 * pieces[0][2].shape[1]
    columns = 3 * MODEL_WIDTH
    vmem = pl.BlockSpec(memory_space=pltpu.VMEM)
    return pl.pallas_call(
        partial(kernel, plan),
        out_shape=[jax.ShapeDtypeStruct(shape, kind) for shape, kind in outs],
        in_specs=[pl.BlockSpec(memory_space=pltpu.SMEM)]
        + [vmem] * len(inputs)
        + [pl.BlockSpec(memory_space=pl.ANY)] * len(pieces),
        out_specs=[vmem] * len(outs),
        scratch_shapes=[pltpu.VMEM((blocks, columns), jnp.bfloat16)]
        + [pltpu.VMEM((rows, MODEL_WIDTH), jnp.float32)] * wides
        + [pltpu.SemaphoreType.DMA((3 * len(pieces),))],
        compiler_params=pltpu.CompilerParams(vmem_limit_bytes=44 << 20),
        cost_estimate=SMALL_COST,
    )(me, *inputs, *[array for _, _, array in pieces])


def in_kernel(pieces):
    lead, rows, _ = pieces[0][2].shape
    return lead == 1 and rows % 32 == 0


LOW, FULL = jnp.bfloat16, jnp.float32


class Layer:
    def __init__(self, places, entry_pieces, gains, tables, allowed):
        self.places, self.entry_pieces, self.gains = places, entry_pieces, gains
        self.tables, self.allowed = tables, allowed
        self.fetched = in_kernel(entry_pieces)
        if not self.fetched:
            self.entry_whole = place(places, entry_pieces, [3 * MODEL_WIDTH])[0][0]

    def add_rest(self, rest_pieces):
        self.rest_pieces = rest_pieces
        if not self.fetched:
            self.rest_whole = [part[0] for part in place(self.places, rest_pieces, [MODEL_WIDTH] * 3)]

    def shapes(self, *kinds):
        rows = self.allowed.shape[0]
        return [((rows, width), kind) for width, kind in kinds]

    def entry_forward(self, resid):
        if not self.fetched:
            self.saved = entry_forward(
                resid, self.entry_whole, self.gains, *self.tables[:2], self.allowed
            )
            return self.saved[6]
        wide = (MODEL_WIDTH, LOW)
        self.resid = resid
        outs = whole_call(
            entry_forward_kernel,
            self.places,
            self.entry_pieces,
            (resid, self.gains[:1].astype(FULL), *self.tables[2:], self.allowed.astype(FULL)),
            self.shapes(wide, wide, wide, wide, (128, FULL), wide),
            1,
        )
        self.normed_first, self.heads = outs[0], outs[1:5]
        return outs[5]

    def rest_forward(self, mixed):
        if not self.fetched:
            result, self.saved = rest_forward(
                (*self.saved[:6], mixed), *self.rest_whole, self.gains
            )
            return result
        self.mixed = mixed
        result, self.middle, self.normed_second, self.hidden_pre = whole_call(
            rest_forward_kernel,
            self.places,
            self.rest_pieces,
            (self.resid, mixed, self.gains[1:].astype(FULL)),
            self.shapes(
                (MODEL_WIDTH, FULL), (MODEL_WIDTH, FULL), (MODEL_WIDTH, LOW), (MODEL_WIDTH, FULL)
            ),
            0,
        )
        return result

    def rest_backward(self, grad):
        if not self.fetched:
            weights = (self.entry_whole, *self.rest_whole, self.gains)
            return rest_backward(self.saved, weights, grad)
        wide = (MODEL_WIDTH, LOW)
        grad_middle, grad_mixed, grad_attn, grad_pre, branch, act, gain_grad = whole_call(
            rest_backward_kernel,
            self.places,
            self.rest_pieces,
            (grad, self.middle, self.hidden_pre, self.gains[1:].astype(FULL)),
            self.shapes((MODEL_WIDTH, FULL), wide, wide, wide, wide, wide)
            + [((1, MODEL_WIDTH), FULL)],
            1,
        )
        lefts = (self.mixed, self.normed_second, act)
        return grad_middle, grad_mixed, lefts, (grad_attn, grad_pre, branch), gain_grad[0]

    def entry_backward(self, grad_middle, grad_mixed):
        if not self.fetched:
            weights = (self.entry_whole, *self.rest_whole, self.gains)
            return entry_backward(
                self.saved, weights, *self.tables[:2], self.allowed, grad_middle, grad_mixed
            )
        grad_resid, projected, gain_grad = whole_call(
            entry_backward_kernel,
            self.places,
            self.entry_pieces,
            (
                grad_middle,
                grad_mixed,
                self.resid,
                *self.heads,
                self.gains[:1].astype(FULL),
                *self.tables[2:],
                self.allowed.astype(FULL),
            ),
            self.shapes((MODEL_WIDTH, FULL), (3 * MODEL_WIDTH, LOW)) + [((1, MODEL_WIDTH), FULL)],
            3,
        )
        return grad_resid, self.normed_first, projected, gain_grad[0]


def entry_forward(resid, qkv_full, gain_pair, cosine, sine, allowed):
    gains = gain_pair.astype(jnp.float32)
    rows = resid.shape[0]
    normed_first = norm_apply(resid, gains[0]).astype(jnp.bfloat16)
    projected = jnp.dot(normed_first, qkv_full, preferred_element_type=jnp.float32)
    query_rows = rotate(
        projected[:, :MODEL_WIDTH].reshape(rows, HEADS, HEAD_DIM), cosine, sine
    ).astype(jnp.bfloat16)
    key_rows = rotate(
        projected[:, MODEL_WIDTH : 2 * MODEL_WIDTH].reshape(rows, HEADS, HEAD_DIM), cosine, sine
    ).astype(jnp.bfloat16)
    value_rows = projected[:, 2 * MODEL_WIDTH :].reshape(rows, HEADS, HEAD_DIM).astype(jnp.bfloat16)

    mixed, log_total = attend_forward(query_rows, key_rows, value_rows, allowed)
    mixed_low = mixed.reshape(rows, MODEL_WIDTH).astype(jnp.bfloat16)
    return (resid, normed_first, query_rows, key_rows, value_rows, log_total, mixed_low)


def rest_forward(saved, out_full, up_full, down_full, gain_pair):
    gains = gain_pair.astype(jnp.float32)
    resid, mixed_low = saved[0], saved[6]
    middle = resid + jnp.dot(mixed_low, out_full, preferred_element_type=jnp.float32)
    normed_second = norm_apply(middle, gains[1]).astype(jnp.bfloat16)
    hidden_pre = jnp.dot(normed_second, up_full, preferred_element_type=jnp.float32)
    hidden_act = jax.nn.gelu(hidden_pre, approximate=True).astype(jnp.bfloat16)
    result = middle + jnp.dot(hidden_act, down_full, preferred_element_type=jnp.float32)
    return (result, (*saved, middle, normed_second, hidden_pre))


def rest_backward(saved, weights, grad_result):
    mixed_low, middle, normed_second, hidden_pre = saved[6:]
    _, out_full, up_full, down_full, gain_pair = weights
    gains = gain_pair.astype(jnp.float32)
    grad_branch = grad_result.astype(jnp.bfloat16)
    hidden_act, gelu_pull = jax.vjp(partial(jax.nn.gelu, approximate=True), hidden_pre)
    hidden_low = hidden_act.astype(jnp.bfloat16)
    grad_act = reverse_matmul_answer(grad_branch, down_full)
    grad_pre = gelu_pull(grad_act)[0].astype(jnp.bfloat16)
    grad_normed_second = reverse_matmul_answer(grad_pre, up_full)
    unused_second, second_pull = jax.vjp(norm_apply, middle, gains[1])
    grad_middle_norm, grad_gain_second = second_pull(grad_normed_second)
    grad_middle = grad_result + grad_middle_norm
    grad_attn = grad_middle.astype(jnp.bfloat16)
    grad_mixed = reverse_matmul_answer(grad_attn, out_full).astype(jnp.bfloat16)
    left_rows = (mixed_low, normed_second, hidden_low)
    right_rows = (grad_attn, grad_pre, grad_branch)
    return (grad_middle, grad_mixed, left_rows, right_rows, grad_gain_second)


def entry_backward(saved, weights, cosine, sine, allowed, grad_middle, grad_mixed):
    resid, normed_first, query_rows, key_rows, value_rows, log_total = saved[:6]
    qkv_full = weights[0]
    gains = weights[4].astype(jnp.float32)
    rows = resid.shape[0]
    grad_query, grad_keys, grad_values = attend_backward(
        query_rows,
        key_rows,
        value_rows,
        allowed,
        log_total,
        grad_mixed.reshape(rows, HEADS, HEAD_DIM),
    )
    grad_query = unrotate(grad_query, cosine, sine).reshape(rows, MODEL_WIDTH)
    grad_keys = unrotate(grad_keys, cosine, sine).reshape(rows, MODEL_WIDTH)
    grad_values = grad_values.reshape(rows, MODEL_WIDTH)
    grad_projected = jnp.concatenate([grad_query, grad_keys, grad_values], axis=1).astype(
        jnp.bfloat16
    )
    grad_normed_first = reverse_matmul_answer(grad_projected, qkv_full)
    unused_first, first_pull = jax.vjp(norm_apply, resid, gains[0])
    grad_resid_norm, grad_gain_first = first_pull(grad_normed_first)
    return (grad_middle + grad_resid_norm, normed_first, grad_projected, grad_gain_first)


def body(
    patch_observations,
    sequence_labels,
    leading_filler_count,
    intake_latent_matrix,
    intake_latent_offset,
    intake_emit_matrix,
    intake_emit_offset,
    intake_shortcut_matrix,
    attention_entry_matrices,
    attention_merge_matrix,
    feedforward_widen_matrix,
    feedforward_shrink_matrix,
    layer_scale_factors,
    readout_latent_matrix,
    readout_latent_offset,
    readout_emit_matrix,
    readout_emit_offset,
    readout_shortcut_matrix,
    loss_sensitivity,
):
    patch_len = patch_observations.shape[1]
    position, pad_count, allowed, keep_rows = layout_rows(
        sequence_labels[0], leading_filler_count[0], patch_len
    )
    cosine, sine = rotary_tables(position, HEAD_DIM)
    columns = jnp.arange(patch_len, dtype=jnp.int32)
    pad_mask = columns[None, :] < pad_count[:, None]
    features = jnp.concatenate(
        [
            jnp.where(pad_mask, jnp.zeros_like(patch_observations), patch_observations),
            pad_mask.astype(jnp.bfloat16),
        ],
        axis=1,
    )
    entry_pre = (
        jnp.dot(features, intake_latent_matrix, preferred_element_type=jnp.float32)
        + intake_latent_offset
    )
    entry_hidden = jax.nn.silu(entry_pre).astype(jnp.bfloat16)
    resid = (
        jnp.dot(entry_hidden, intake_emit_matrix, preferred_element_type=jnp.float32)
        + intake_emit_offset
        + jnp.dot(features, intake_shortcut_matrix, preferred_element_type=jnp.float32)
    )
    layer_count = attention_entry_matrices.shape[0]
    group = lax.axis_size("head")
    group_place = lax.axis_index("head")
    outer = lax.axis_size("dp") // 8
    me = lax.axis_index("dp").astype(jnp.int32)
    places = (me & 7).reshape(1)
    own_count = layer_scale_factors.shape[2]
    rows = patch_observations.shape[0]

    group_width = readout_latent_offset.shape[0]
    offsets = jnp.stack([readout_latent_offset, readout_emit_offset])
    coarse = lax.reduce_precision(offsets, 8, 7)
    offset_rows = jnp.concatenate([coarse, offsets - coarse], axis=0).astype(jnp.bfloat16)
    offset_rows = jnp.pad(offset_rows, ((0, 12), (0, 0)))
    sent = jnp.concatenate(
        [
            loss_sensitivity.reshape(group, rows, group_width),
            jnp.broadcast_to(offset_rows[None], (group, 16, group_width)),
        ],
        axis=1,
    )
    gain_columns = layer_scale_factors.reshape(2 * layer_count, own_count).T
    gain_columns = jnp.pad(gain_columns, ((0, 0), (0, 128 - 2 * layer_count)))
    chunks = []
    for layer_index in range(layer_count):
        entry_own = attention_entry_matrices[layer_index]
        if layer_index == 0:
            entry_own = jnp.concatenate([entry_own, gain_columns], axis=1)
        chunks.append(entry_own)
        rest_own = jnp.concatenate(
            [
                attention_merge_matrix[layer_index],
                feedforward_widen_matrix[layer_index],
                feedforward_shrink_matrix[layer_index],
            ],
            axis=1,
        )
        chunks.append(rest_own)
    head_own = jnp.concatenate(
        [
            lax.dynamic_index_in_dim(
                matrix.reshape(outer, 8, -1, group_width), me % 8, 1, keepdims=False
            )
            for matrix in (readout_latent_matrix, readout_shortcut_matrix, readout_emit_matrix)
        ],
        axis=2,
    )
    chunks.append(head_own)
    count = len(chunks)

    def gather_chunk(number, own):
        if number < count - 1:
            return gather_head(own)
        return lax.all_gather(own, "head", axis=0, tiled=True)

    held = gather_chunk(0, chunks[0])
    cosine_wide = jnp.tile(jnp.concatenate([cosine[:, 0], cosine[:, 0]], axis=1), (1, HEADS))
    sine_wide = jnp.tile(jnp.concatenate([-sine[:, 0], sine[:, 0]], axis=1), (1, HEADS))
    tables = (cosine, sine, cosine_wide, sine_wide)
    nears, fars, near_mets = [], [], []
    layers = []
    onward = None
    for number in range(count + 1):
        step = {}
        if number < count:
            step["x"], step["y"] = swap(held, 1), swap(held, 2)
        if number + 1 < count:
            step["next"] = gather_chunk(number + 1, chunks[number + 1])
        if number == count - 1:
            step["met"] = lax.all_to_all(
                after(sent, held), "head", split_axis=0, concat_axis=0, tiled=True
            )
        if number == 0:
            step["resid"] = resid
        else:
            step["far"] = (swap(onward[0], 1), swap(onward[1], 2))
            near_mets.append([swap(part, 0) for part in after(nears[number - 1], onward)])
        if number > 1:
            chunk = number - 2
            far_met = [swap(part, 0) for part in after(fars[chunk], onward)]
            pieces = all_pieces(nears[chunk], fars[chunk], near_mets[chunk], far_met)
            if chunk == 0:
                gain_rows = place(places, pieces, [128], 3 * MODEL_WIDTH)[0][0]
                gain_rows = gain_rows[:, : 2 * layer_count].T.reshape(layer_count, 2, -1)
            if chunk % 2 == 0:
                layers.append(Layer(places, pieces, gain_rows[chunk // 2], tables, allowed))
                step["mixed"] = layers[-1].entry_forward(resid)
            else:
                layers[-1].add_rest(pieces)
                step["resid"] = layers[-1].rest_forward(mixed)
        step["own"] = chunks[number + 2 :]
        step = lax.optimization_barrier(step)
        chunks[number + 2 :] = step["own"]
        if number < count:
            nears.append((held, step["x"], step["y"]))
            onward = second_step(*nears[-1])
        held = step.get("next")
        if number > 0:
            fars.append(step["far"])
        resid = step.get("resid", resid)
        mixed = step.get("mixed")
        if "met" in step:
            met = step["met"]
    head_far_met = [swap(part, 0) for part in fars[-1]]
    head_pieces = all_pieces(nears[-1], fars[-1], near_mets[-1], head_far_met)
    sensitivity = met[:, :rows]
    head_offsets = met[:, rows : rows + 4].astype(jnp.float32)
    latent_offsets = head_offsets[:, 0] + head_offsets[:, 2]
    emit_offsets = head_offsets[:, 1] + head_offsets[:, 3]

    top = resid.astype(jnp.bfloat16)
    keep_column = keep_rows[:, None]
    grad_forecast = (sensitivity.astype(jnp.float32) * keep_column).astype(jnp.bfloat16)
    grad_forecast_rows = jnp.concatenate([grad_forecast[part] for part in range(group)], axis=1)
    head_inputs = (top, keep_column, latent_offsets, emit_offsets, grad_forecast)
    if layers[0].fetched:
        outs = output_block(places, head_pieces, *head_inputs)
    else:
        head_whole = place(places, head_pieces, [3 * group_width])[0]
        outs = output_plain(head_whole, *head_inputs)
    head_hidden, forecast, grad_head_pre, grad_resid, pre_sums = outs
    token_predictions = lax.all_to_all(
        forecast, "head", split_axis=0, concat_axis=0, tiled=True
    ).reshape(group * rows, group_width)
    head_bias_rows = (pre_sums[0], jnp.sum(grad_forecast_rows.astype(jnp.float32), axis=0))
    head_both = exchange(
        [
            (top, grad_head_pre),
            (top, grad_forecast_rows),
            (head_hidden, grad_forecast_rows),
        ]
    )
    gain_sums = [[None, None] for _ in range(layer_count)]

    def rest_stage(layer_index, carry):
        outs = layers[layer_index].rest_backward(carry["grad"])
        gain_sums[layer_index][1] = outs[4]
        both = exchange(list(zip(outs[2], outs[3], strict=True)))
        return {"middle": outs[0], "mixed": outs[1]}, both

    def entry_stage(layer_index, carry):
        outs = layers[layer_index].entry_backward(carry["middle"], carry["mixed"])
        gain_sums[layer_index][0] = outs[3]
        return {"grad": outs[0]}, exchange([(outs[1], outs[2])])

    def input_stage(carry):
        head_rows = [row[None] for row in head_bias_rows]
        gain_rows = [row[None] for pair in gain_sums for row in pair]
        if layers[0].fetched and 2 + len(head_rows) + len(gain_rows) == EXTRA_ROWS:
            low, pre_low, grad_features, bias_rows = input_back(
                carry["grad"],
                entry_pre,
                intake_emit_matrix,
                intake_latent_matrix,
                intake_shortcut_matrix,
            )
            values_grad = jnp.where(pad_mask, 0.0, grad_features[:, :patch_len])
            vectors = jnp.concatenate([bias_rows, *head_rows, *gain_rows], axis=0)
            products = input_products(me, entry_hidden, low, pre_low, features, vectors)
            return values_grad, 4 * patch_len + EXTRA_ROWS, products
        grad_entry = carry["grad"].astype(jnp.bfloat16)
        grad_entry_outer = dyadic_accumulation(entry_hidden, grad_entry)
        grad_entry_outer_bias = jnp.sum(grad_entry.astype(jnp.float32), axis=0)
        grad_entry_skip = dyadic_accumulation(features, grad_entry)
        unused_entry, entry_pull = jax.vjp(jax.nn.silu, entry_pre)
        grad_entry_pre = entry_pull(reverse_matmul_answer(grad_entry, intake_emit_matrix))[0].astype(
            jnp.bfloat16
        )
        grad_entry_inner = dyadic_accumulation(features, grad_entry_pre)
        grad_entry_inner_bias = jnp.sum(grad_entry_pre.astype(jnp.float32), axis=0)
        grad_features = reverse_matmul_answer(
            grad_entry_pre, intake_latent_matrix
        ) + reverse_matmul_answer(grad_entry, intake_shortcut_matrix)
        values_grad = jnp.where(pad_mask, 0.0, grad_features[:, :patch_len])
        extra_rows = jnp.concatenate(
            [
                grad_entry_inner,
                grad_entry_skip,
                grad_entry_inner_bias[None],
                grad_entry_outer_bias[None],
            ]
            + head_rows
            + [row[None] for pair in gain_sums for row in pair],
            axis=0,
        )
        return values_grad, extra_rows.shape[0], entry_products(me, grad_entry_outer, extra_rows)

    stages = []
    for layer_index in reversed(range(layer_count)):
        stages += [(rest_stage, layer_index), (entry_stage, layer_index)]
    stage_count = len(stages)
    carry = {"grad": grad_resid}
    boths = {0: head_both}
    sums = {0: RowSums(*pair_products(me, head_both))}
    totals, finished = {}, {}
    entry_chunk = None
    done = 0

    def close(**step):
        step["sent"] = {n: (sums[n].sent, sums[n].later, sums[n].own) for n in sums}
        step["boths"] = boths
        step["carry"] = carry
        step = lax.optimization_barrier(step)
        for n, parts in step.pop("sent").items():
            sums[n].sent, sums[n].later, sums[n].own = parts
        return step

    step = close()
    for number in range(stage_count + 1):
        carry, boths = step["carry"], step["boths"]
        parts = {"first": sums[number].first()}
        if number >= 1:
            totals[number - 1] = sums.pop(number - 1).total()
            if number == 1:
                finished[0] = sum_columns(totals[0])
            else:
                finished[number - 1] = sum_group(totals[number - 1])
        if number >= 2:
            parts["finished"] = finished[number - 2]
        until = {stage_count - 2: stage_count}.get(number, number + 1)
        while done < min(until, stage_count):
            stage, layer_index = stages[done]
            carry, boths[done + 1] = stage(layer_index, carry)
            done += 1
        if number == stage_count - 1:
            parts["entry"] = entry_chunk.first()
        if number == stage_count:
            entry_summed = entry_sums_of_group(entry_chunk.total())
        step = close(**parts)
        sums[number].met = step["first"]
        if number >= 2:
            finished[number - 2] = step["finished"]
        carry, boths = step["carry"], step["boths"]
        parts = {"last": sums[number].last()}
        if number == stage_count - 2:
            values_grad, extra_count, entry_chunk = input_stage(carry)
            parts["entry"] = (entry_chunk.sent, entry_chunk.later, entry_chunk.own)
        if number == stage_count - 1:
            entry_chunk.met = step["entry"]
            parts["entry"] = entry_chunk.last()
        if number < stage_count:
            sums[number + 1] = RowSums(*pair_products(me, boths.pop(number + 1)))
            step = close(**parts)
        else:
            step = parts
        sums[number].last_met = step["last"]
        if number == stage_count - 2:
            entry_chunk.sent, entry_chunk.later, entry_chunk.own = step["entry"]
        if number == stage_count - 1:
            entry_chunk.last_met = step["entry"]
    finished[stage_count] = sum_group_at_once(sums[stage_count].total())
    entry_main, entry_extra, entry_held = entry_everywhere(
        me, entry_summed, own_count, extra_count
    )
    head_rows = gather_blocks(me, finished[0])
    head_sums = [after(head_rows[n], entry_held).astype(jnp.float32) for n in range(3)]
    layer_sums = [None] * layer_count
    for member, layer_index in enumerate(reversed(range(layer_count))):
        rest = finished[1 + 2 * member].astype(jnp.float32)
        entry = finished[2 + 2 * member].astype(jnp.float32)
        layer_sums[layer_index] = (entry[0], rest[0], rest[1], rest[2])
    inner_rows = 2 * patch_len
    last = 2 * inner_rows
    entry_sums = (
        entry_extra[:inner_rows],
        entry_extra[last],
        entry_main,
        entry_extra[last + 1],
        entry_extra[inner_rows:last],
    )
    head_bias_sums = lax.dynamic_slice_in_dim(
        entry_extra[last + 2 : last + 4], group_place * group_width, group_width, 1
    )
    own_place = (me * group + group_place) * own_count
    gains_grad = lax.dynamic_slice_in_dim(
        entry_extra[last + 4 : last + 4 + 2 * layer_count], own_place, own_count, 1
    ).reshape(layer_count, 2, own_count)
    qkv_grad = jnp.stack([layer_sums[member][0] for member in range(layer_count)])
    out_grad = jnp.stack([layer_sums[member][1] for member in range(layer_count)])
    up_grad = jnp.stack([layer_sums[member][2] for member in range(layer_count)])
    down_grad = jnp.stack([layer_sums[member][3] for member in range(layer_count)])
    return (
        token_predictions,
        values_grad,
        entry_sums[0],
        entry_sums[1],
        entry_sums[2],
        entry_sums[3],
        entry_sums[4],
        qkv_grad,
        out_grad,
        up_grad,
        down_grad,
        gains_grad,
        head_sums[0],
        head_bias_sums[0],
        head_sums[2],
        head_bias_sums[1],
        head_sums[1],
    )


def solution(mesh):
    return jax.shard_map(
        body,
        mesh=mesh,
        in_specs=(
            P(("dp", "head"), None),
            P(("dp", "head"), None),
            P(("dp", "head"), None),
            P(),
            P(),
            P(),
            P(),
            P(),
            P(None, ("dp", "head"), None),
            P(None, ("dp", "head"), None),
            P(None, ("dp", "head"), None),
            P(None, ("dp", "head"), None),
            P(None, None, ("dp", "head")),
            P(None, "head"),
            P("head"),
            P(None, "head"),
            P("head"),
            P(None, "head"),
            P("dp", "head"),
        ),
        out_specs=(
            P("dp", "head"),
            P(("dp", "head"), None),
            P(),
            P(),
            P(),
            P(),
            P(),
            P(None, ("dp", "head"), None),
            P(None, ("dp", "head"), None),
            P(None, ("dp", "head"), None),
            P(None, ("dp", "head"), None),
            P(None, None, ("dp", "head")),
            P(None, "head"),
            P("head"),
            P(None, "head"),
            P("head"),
            P(None, "head"),
        ),
        check_vma=False,
    )
```

```python
from functools import partial
import math

import jax
import jax.numpy as jnp
from jax import lax
from jax.experimental import pallas as pl
from jax.experimental.pallas import tpu as pltpu
from jax.sharding import PartitionSpec as P

MODEL_WIDTH = 1280
HEADS = 16
HEAD_DIM = 80


EPS = 1e-06
SMALL_COST = pl.CostEstimate(flops=1, bytes_accessed=1, transcendentals=0)
ROPE_BASE = 10000.0


def layout_rows(series_row, pad_row, patch_len):
    count = series_row.shape[0]
    order = jnp.arange(count, dtype=jnp.int32)
    same_series = series_row[:, None] == series_row[None, :]
    earlier = order[None, :] < order[:, None]
    position = jnp.sum(jnp.logical_and(same_series, earlier).astype(jnp.int32), axis=1)
    numbers = jnp.arange(pad_row.shape[0], dtype=jnp.int32)
    series_pad = jnp.sum(
        jnp.where(series_row[:, None] == numbers[None, :], pad_row[None, :], 0), axis=1
    )
    pad_count = jnp.where(position == 0, series_pad, 0)
    padded = pad_count == patch_len
    diagonal = order[:, None] == order[None, :]
    reach = jnp.logical_or(jnp.logical_and(earlier, jnp.logical_not(padded)[None, :]), diagonal)
    allowed = jnp.logical_and(same_series, reach)
    keep_rows = jnp.where(padded, 0.0, 1.0).astype(jnp.float32)
    return (position, pad_count, allowed, keep_rows)


def rotary_tables(position, head_dim):
    half = head_dim // 2
    steps = jnp.arange(half, dtype=jnp.float32) / half
    inverse = jnp.exp(-math.log(ROPE_BASE) * steps)
    angles = position.astype(jnp.float32)[:, None] * inverse[None, :]
    return (jnp.cos(angles)[:, None, :], jnp.sin(angles)[:, None, :])


def rotate(heads_rows, cosine, sine):
    half = heads_rows.shape[-1] // 2
    first = heads_rows[..., :half]
    second = heads_rows[..., half:]
    return jnp.concatenate(
        [first * cosine - second * sine, second * cosine + first * sine], axis=-1
    )


def unrotate(grad_rows, cosine, sine):
    half = grad_rows.shape[-1] // 2
    first = grad_rows[..., :half]
    second = grad_rows[..., half:]
    return jnp.concatenate(
        [first * cosine + second * sine, second * cosine - first * sine], axis=-1
    )


def norm_apply(resid, gain):
    return resid * lax.rsqrt(jnp.mean(resid * resid, axis=-1, keepdims=True) + EPS) * gain


def dyadic_accumulation(left, right):
    return lax.dot_general(
        left, right, (((0,), (0,)), ((), ())), preferred_element_type=jnp.float32
    )


def reverse_matmul_answer(grad_rows, weight):
    return lax.dot_general(
        grad_rows, weight, (((1,), (1,)), ((), ())), preferred_element_type=jnp.float32
    )


def masked_scores(query_rows, key_rows, allowed):
    scale = 1.0 / math.sqrt(query_rows.shape[-1])
    scores = (
        jnp.einsum("qhd,khd->hqk", query_rows, key_rows, preferred_element_type=jnp.float32) * scale
    )
    return jnp.where(allowed[None], scores, -1e30)


def attend_forward(query_rows, key_rows, value_rows, allowed):
    scores = masked_scores(query_rows, key_rows, allowed)
    peak = jnp.max(scores, axis=-1, keepdims=True)
    weights = jnp.exp(scores - peak)
    total = jnp.sum(weights, axis=-1, keepdims=True)
    probs = (weights / total).astype(jnp.bfloat16)
    mixed = jnp.einsum("hqk,khd->qhd", probs, value_rows, preferred_element_type=jnp.float32)
    return (mixed, peak + jnp.log(total))


def attend_backward(query_rows, key_rows, value_rows, allowed, log_total, grad_mixed):
    scale = 1.0 / math.sqrt(query_rows.shape[-1])
    scores = masked_scores(query_rows, key_rows, allowed)
    probs = jnp.where(allowed[None], jnp.exp(scores - log_total), 0.0)
    grad_probs = jnp.einsum(
        "qhd,khd->hqk", grad_mixed, value_rows, preferred_element_type=jnp.float32
    )
    grad_values = jnp.einsum(
        "hqk,qhd->khd", probs.astype(jnp.bfloat16), grad_mixed, preferred_element_type=jnp.float32
    )
    center = jnp.sum(grad_probs * probs, axis=-1, keepdims=True)
    grad_scores = (probs * (grad_probs - center)).astype(jnp.bfloat16)
    grad_query = (
        jnp.einsum("hqk,khd->qhd", grad_scores, key_rows, preferred_element_type=jnp.float32)
        * scale
    )
    grad_keys = (
        jnp.einsum("hqk,qhd->khd", grad_scores, query_rows, preferred_element_type=jnp.float32)
        * scale
    )
    return (grad_query, grad_keys, grad_values)


def after(value, *earlier):
    return lax.optimization_barrier((value, *earlier))[0]


def swap(v, bit):
    size = lax.axis_size("dp")
    return lax.ppermute(v, "dp", [(i, i ^ (1 << bit)) for i in range(size)])


def outer_groups():
    size = lax.axis_size("dp")
    return [[j + 8 * o for o in range(size // 8)] for j in range(8)]


def place_kernel(plan, piece_count, out_count, me_ref, *refs):
    pieces = refs[:piece_count]
    outs = refs[piece_count : piece_count + out_count]
    held = refs[piece_count + out_count : piece_count + 2 * out_count]
    in_sems, out_sems = refs[piece_count + 2 * out_count :]
    inward, outward = [], []
    for n, (piece, rel, row, out, column) in enumerate(plan):
        source = pieces[piece]
        width = held[out].shape[-1]
        if width != source.shape[-1]:
            source = source.at[:, :, pl.ds(column, width)]
        spot = (slice(None), me_ref[0] ^ rel, pl.ds(row, source.shape[1]), slice(None))
        inward.append(pltpu.make_async_copy(source, held[out].at[spot], in_sems.at[n]))
        outward.append(
            pltpu.make_async_copy(held[out].at[spot], outs[out].at[spot], out_sems.at[n])
        )
    for copy in inward:
        copy.start()
    for copy, onward in zip(inward, outward):
        copy.wait()
        onward.start()
    for onward in outward:
        onward.wait()


def place(me, pieces, widths, first=0):
    plan = []
    for n, (rel, row, _) in enumerate(pieces):
        column = first
        for out, width in enumerate(widths):
            plan.append((n, rel, row, out, column))
            column += width
    arrays = [array for _, _, array in pieces]
    lead, rows, _ = arrays[0].shape
    kind = arrays[0].dtype
    total = sum(8 * lead * rows * -(-w // 128) * 128 for w in widths) * 2
    outs = pl.pallas_call(
        partial(place_kernel, plan, len(arrays), len(widths)),
        out_shape=[jax.ShapeDtypeStruct((lead, 8, rows, w), kind) for w in widths],
        in_specs=[pl.BlockSpec(memory_space=pltpu.SMEM)]
        + [pl.BlockSpec(memory_space=pl.ANY)] * len(arrays),
        out_specs=[pl.BlockSpec(memory_space=pl.ANY)] * len(widths),
        scratch_shapes=[pltpu.VMEM((lead, 8, rows, w), kind) for w in widths]
        + [pltpu.SemaphoreType.DMA((len(plan),))] * 2,
        compiler_params=pltpu.CompilerParams(vmem_limit_bytes=total + (4 << 20)),
        cost_estimate=SMALL_COST,
    )(me, *arrays)
    outer = lax.axis_size("dp") // 8
    return [o.reshape(-1, outer * 8 * rows, o.shape[-1]) for o in outs]


def row_half(rows):
    return rows // 32 * 16 if rows >= 32 else rows // 2


def second_step(held, from_x, from_y):
    half = row_half(held.shape[1])
    return from_y[:, :half], from_x[:, half:]


def all_pieces(near, far, near_met, far_met):
    half = far[0].shape[1]
    places = ((0, 0), (2, 0), (4, 0), (6, 0), (6, half))
    pieces = []
    for (rel, row), array, met in zip(places, (*near, *far), (*near_met, *far_met), strict=True):
        pieces += [(rel, row, array), (rel | 1, row, met)]
    return pieces


def spread_rows(held):
    near = (held, swap(held, 1), swap(held, 2))
    onward_x, onward_y = second_step(*near)
    far = (swap(onward_x, 1), swap(onward_y, 2))
    return all_pieces(near, far, [swap(part, 0) for part in near], [swap(part, 0) for part in far])


def gather_head(own):
    held = lax.all_gather(own, "head", axis=0, tiled=True)[None]
    if lax.axis_size("dp") > 8:
        held = lax.all_gather(
            held, "dp", axis=0, tiled=True, axis_index_groups=outer_groups()
        )
    return held


def product_kernel(count, outer, me_ref, *refs):
    lefts, rights, met_lefts, met_rights = (refs[n * count : (n + 1) * count] for n in range(4))
    to_x, to_y, later, own, right_pair, turned = refs[4 * count :]
    rows, width = own.shape[1] // outer, own.shape[-1]
    tokens = lefts[0].shape[0]
    half = width // 2
    tile = half if half <= 640 else 640
    odd = me_ref[0] & 1 == 1
    chip = me_ref[0] >> 1

    def store(rel, n, span, side, columns, total):
        if rel == 0:
            own[n, span, slice(side * half + columns.start, side * half + columns.stop)] = total
        elif rel == 1 and side == 0:
            to_x[1, n, span, columns] = total
        elif rel == 1:
            later[1, n, span, columns] = total
        elif rel == 2 and side == 0:
            later[0, n, span, columns] = total
        elif rel == 2:
            to_y[1, n, span, columns] = total
        elif side == 0:
            to_x[0, n, span, columns] = total
        else:
            to_y[0, n, span, columns] = total

    for n in range(count):
        right_pair[:tokens] = rights[n][...]
        right_pair[tokens:] = met_rights[n][...]
        for part in range(outer):
            span = slice(part * rows, (part + 1) * rows)
            for place in range(4):
                first = (part * 8 + 2 * place) * rows
                near, far = slice(first, first + rows), slice(first + rows, first + 2 * rows)
                left_pair = jnp.concatenate(
                    [
                        jnp.where(odd, side[n][:, far], side[n][:, near]).astype(jnp.float32)
                        for side in (lefts, met_lefts)
                    ],
                    axis=0,
                )
                turned[place] = left_pair.T.astype(own.dtype)
            every = turned[...].reshape(4 * rows, 2 * tokens)
            for side in range(2):
                for at in range(0, half, tile):
                    total = jnp.dot(
                        every,
                        right_pair[:, side * half + at : side * half + at + tile],
                        preferred_element_type=jnp.float32,
                    ).astype(own.dtype)
                    for place in range(4):
                        for rel in range(4):
                            pl.when(chip ^ place == rel)(
                                partial(
                                    store,
                                    rel,
                                    n,
                                    span,
                                    side,
                                    slice(at, at + tile),
                                    total[place * rows : (place + 1) * rows],
                                )
                            )


def exchange(pairs):
    met = {}
    for pair in pairs:
        for rows in pair:
            if id(rows) not in met:
                met[id(rows)] = swap(rows, 0)
    return [(left, right, met[id(left)], met[id(right)]) for left, right in pairs]


def pair_products(me, both):
    outer = lax.axis_size("dp") // 8
    count = len(both)
    left, right = both[0][:2]
    block, width = left.shape[1] // 8, right.shape[1]
    low = jnp.bfloat16
    return pl.pallas_call(
        partial(product_kernel, count, outer),
        out_shape=[
            jax.ShapeDtypeStruct((2, count, block, width // 2), low),
            jax.ShapeDtypeStruct((2, count, block, width // 2), low),
            jax.ShapeDtypeStruct((2, count, block, width // 2), low),
            jax.ShapeDtypeStruct((count, block, width), low),
        ],
        in_specs=[pl.BlockSpec(memory_space=pltpu.SMEM)]
        + [pl.BlockSpec(memory_space=pltpu.VMEM)] * (4 * count),
        out_specs=[pl.BlockSpec(memory_space=pltpu.VMEM)] * 4,
        scratch_shapes=[
            pltpu.VMEM((2 * left.shape[0], width), low),
            pltpu.VMEM((4, block // outer, 2 * left.shape[0]), low),
        ],
        compiler_params=pltpu.CompilerParams(vmem_limit_bytes=44 << 20),
        cost_estimate=SMALL_COST,
    )((me & 7).reshape(1), *[part for parts in zip(*both, strict=True) for part in parts])


def low_sum(*parts):
    total = parts[0].astype(jnp.float32)
    for part in parts[1:]:
        total = total + part.astype(jnp.float32)
    return total.astype(jnp.bfloat16)


class RowSums:
    def __init__(self, to_x, to_y, later, own):
        self.sent, self.later, self.own = (to_x, to_y), later, own

    def first(self):
        return swap(self.sent[0], 1), swap(self.sent[1], 2)

    def last(self):
        return (
            swap(low_sum(self.later[0], self.met[0][0]), 2),
            swap(low_sum(self.later[1], self.met[1][0]), 1),
        )

    def total(self):
        half = self.own.shape[-1] // 2
        return jnp.concatenate(
            [
                low_sum(self.own[..., :half], self.met[0][1], self.last_met[0]),
                low_sum(self.own[..., half:], self.met[1][1], self.last_met[1]),
            ],
            axis=-1,
        )


def sum_group(total):
    outer = lax.axis_size("dp") // 8
    group = lax.axis_size("head")
    lead = total.shape[:-2]
    rows, columns = total.shape[-2:]
    if outer > 1:
        total = lax.psum_scatter(
            total.reshape(*lead, outer, rows // outer, columns),
            "dp",
            scatter_dimension=len(lead),
            tiled=True,
            axis_index_groups=outer_groups(),
        )
    total = total.reshape(*lead, rows // outer, columns)
    return lax.psum_scatter(total, "head", scatter_dimension=len(lead), tiled=True)


def sum_group_at_once(total):
    outer = lax.axis_size("dp") // 8
    group = lax.axis_size("head")
    if outer > 1:
        return sum_group(total).astype(jnp.float32)
    lead = total.shape[:-2]
    rows, columns = total.shape[-2:]
    total = total.reshape(*lead, group, rows // group, columns)
    axis = len(lead)
    met = lax.all_to_all(total, "head", split_axis=axis, concat_axis=axis, tiled=True)
    return jnp.sum(met.astype(jnp.float32), axis=axis)


def sum_columns(total):
    group = lax.axis_size("head")
    if lax.axis_size("dp") > 8:
        total = lax.psum(total, "dp", axis_index_groups=outer_groups())
    count, rows, columns = total.shape
    total = jnp.moveaxis(total.reshape(count, rows, group, columns // group), 2, 0)
    return lax.psum_scatter(total, "head", scatter_dimension=0, tiled=True)[0]


def gather_blocks(me, summed):
    outer = lax.axis_size("dp") // 8
    count, rows, columns = summed.shape
    if outer == 1:
        whole = lax.all_gather(summed, "dp", axis=0)
        return [whole[:, n].reshape(8 * rows, columns) for n in range(count)]
    held = summed.reshape(count * outer, rows // outer, columns)
    return place((me & 7).reshape(1), spread_rows(held), [columns])[0]


EXTRA_ROWS = 8


def entry_products(me, main, extra):
    group = lax.axis_size("head")
    outer = lax.axis_size("dp") // 8
    devices = 8 * outer * group
    columns = main.shape[1]
    own = main.shape[0] // devices
    extra = jnp.pad(extra, ((0, EXTRA_ROWS * devices - extra.shape[0]), (0, 0)))
    rows = jnp.concatenate(
        [main.reshape(devices, own, columns), extra.reshape(devices, EXTRA_ROWS, columns)], axis=1
    ).astype(jnp.bfloat16)
    view = rows.reshape(outer, 4, 2, group * (own + EXTRA_ROWS), columns)
    core = me & 1
    other = lax.dynamic_index_in_dim(view, 1 - core, 2, keepdims=False)
    pair = low_sum(lax.dynamic_index_in_dim(view, core, 2, keepdims=False), swap(other, 0))
    chip = (me & 7) >> 1
    half = columns // 2

    def picked(rel):
        return lax.dynamic_index_in_dim(pair, chip ^ rel, 1, keepdims=False).reshape(-1, columns)

    own_rows, at_x, at_y, far = (picked(rel) for rel in range(4))
    return RowSums(
        jnp.stack([far[:, :half], at_x[:, :half]]),
        jnp.stack([far[:, half:], at_y[:, half:]]),
        (at_y[:, :half], at_x[:, half:]),
        own_rows,
    )


def silu_parts(x):
    gate = 1.0 / (1.0 + jnp.exp(-x))
    return x * gate, gate * (1.0 + x * (1.0 - gate))


def output_kernel(
    plan, me_ref, top_ref, keep_ref, latent_offset, emit_offset, sensitivity, *refs
):
    pieces = refs[: len(plan)]
    hidden_ref, forecast_ref, pre_low_ref, grad_ref, bias_ref = refs[len(plan) : len(plan) + 5]
    whole, pre, skips, sent, both, sems = refs[len(plan) + 5 :]
    group, width, _ = whole.shape
    each = sensitivity.shape[2]
    two = 2 * each
    rows = width // 8
    copies = []
    for n, (rel, row, count) in enumerate(plan):
        first = pl.multiple_of((me_ref[0] ^ rel) * rows + row, 16)
        spot = whole.at[:, pl.ds(first, count), :]
        copies.append(pltpu.make_async_copy(pieces[n], spot, sems.at[n]))
    for copy in copies:
        copy.start()
    for copy in copies:
        copy.wait()
    top = top_ref[...]
    keep = keep_ref[...]
    for part in range(group):
        rows_times(top, whole.at[part], 0, both, 128)
        pre[:, part * each : (part + 1) * each] = both[:, :each] + latent_offset[part : part + 1]
        skips[part] = both[:, each:two] + emit_offset[part : part + 1]
    hidden, slope = silu_parts(pre[...])
    hidden = hidden.astype(jnp.bfloat16)
    hidden_ref[...] = hidden
    for part in range(group):
        emitted = jnp.dot(hidden, whole[part, :, two:], preferred_element_type=jnp.float32)
        forecast_ref[part] = ((emitted + skips[part]) * keep).astype(jnp.bfloat16)

    def back_hidden(n, _):
        at = pl.multiple_of(n * 256, 256)
        total = reverse_matmul_answer(whole[0, pl.ds(at, 256), two:], sensitivity[0])
        for part in range(1, group):
            total += reverse_matmul_answer(whole[part, pl.ds(at, 256), two:], sensitivity[part])
        grad_ref[:, pl.ds(at, 256)] = total.T
        return 0

    lax.fori_loop(0, width // 256, back_hidden, 0)
    pre[...] = grad_ref[...] * slope
    pre_low_ref[...] = pre[...].astype(jnp.bfloat16)
    bias_ref[...] = jnp.sum(pre_low_ref[...].astype(jnp.float32), axis=0, keepdims=True)
    for part in range(group):
        both[:, :each] = pre[:, part * each : (part + 1) * each]
        both[:, each:] = sensitivity[part].astype(jnp.float32)
        sent[part] = both[...].astype(jnp.bfloat16)

    def back_top(n, _):
        at = pl.multiple_of(n * 256, 256)
        total = reverse_matmul_answer(whole[0, pl.ds(at, 256), :two], sent[0])
        for part in range(1, group):
            total += reverse_matmul_answer(whole[part, pl.ds(at, 256), :two], sent[part])
        grad_ref[:, pl.ds(at, 256)] = total.T
        return 0

    lax.fori_loop(0, width // 256, back_top, 0)


def output_block(me, pieces, top, keep, latent_offsets, emit_offsets, grad_forecast):
    plan = [(rel, row, array.shape[1]) for rel, row, array in pieces]
    group, rows, each = grad_forecast.shape
    width = top.shape[1]
    vmem = pl.BlockSpec(memory_space=pltpu.VMEM)
    return pl.pallas_call(
        partial(output_kernel, plan),
        out_shape=[
            jax.ShapeDtypeStruct((rows, width), LOW),
            jax.ShapeDtypeStruct((group, rows, each), LOW),
            jax.ShapeDtypeStruct((rows, width), LOW),
            jax.ShapeDtypeStruct((rows, width), FULL),
            jax.ShapeDtypeStruct((1, width), FULL),
        ],
        in_specs=[pl.BlockSpec(memory_space=pltpu.SMEM)]
        + [vmem] * 5
        + [pl.BlockSpec(memory_space=pl.ANY)] * len(pieces),
        out_specs=[vmem] * 5,
        scratch_shapes=[
            pltpu.VMEM((group, width, 3 * each), LOW),
            pltpu.VMEM((rows, width), FULL),
            pltpu.VMEM((group, rows, each), FULL),
            pltpu.VMEM((group, rows, 2 * each), LOW),
            pltpu.VMEM((rows, 2 * each), FULL),
            pltpu.SemaphoreType.DMA((len(pieces),)),
        ],
        compiler_params=pltpu.CompilerParams(vmem_limit_bytes=44 << 20),
        cost_estimate=SMALL_COST,
    )(
        me,
        top,
        keep,
        latent_offsets,
        emit_offsets,
        grad_forecast,
        *[array for _, _, array in pieces],
    )


def output_plain(head_whole, top, keep, latent_offsets, emit_offsets, grad_forecast):
    group, _, each = grad_forecast.shape
    two = 2 * each
    inner_parts = [
        jnp.dot(top, head_whole[part][:, :two], preferred_element_type=jnp.float32)
        for part in range(group)
    ]
    head_pre = jnp.concatenate(
        [inner_parts[part][:, :each] + latent_offsets[part] for part in range(group)], axis=1
    )
    hidden, slope = silu_parts(head_pre)
    hidden = hidden.astype(jnp.bfloat16)
    forecast = jnp.stack(
        [
            (
                jnp.dot(hidden, head_whole[part][:, two:], preferred_element_type=jnp.float32)
                + emit_offsets[part]
                + inner_parts[part][:, each:]
            )
            * keep
            for part in range(group)
        ]
    ).astype(jnp.bfloat16)
    grad_hidden = sum(
        reverse_matmul_answer(grad_forecast[part], head_whole[part][:, two:])
        for part in range(group)
    )
    pre_low = (grad_hidden * slope).astype(jnp.bfloat16)
    grad_top = sum(
        reverse_matmul_answer(
            jnp.concatenate(
                [pre_low[:, part * each : (part + 1) * each], grad_forecast[part]], axis=1
            ),
            head_whole[part][:, :two],
        )
        for part in range(group)
    )
    return hidden, forecast, pre_low, grad_top, jnp.sum(pre_low.astype(FULL), axis=0, keepdims=True)


def input_back_kernel(
    grad_ref, pre_ref, emit_ref, latent_ref, shortcut_ref, low_ref, pre_low_ref, sent_ref, bias_ref, wide
):
    low = grad_ref[...].astype(jnp.bfloat16)
    low_ref[...] = low
    rows_times_turned(low, emit_ref, 0, emit_ref.shape[1], wide, 256)
    pre = pre_ref[...]
    gate = 1.0 / (1.0 + jnp.exp(-pre))
    pre_low = (wide[...] * (gate * (1.0 + pre * (1.0 - gate)))).astype(jnp.bfloat16)
    pre_low_ref[...] = pre_low
    sent_ref[...] = reverse_matmul_answer(pre_low, latent_ref[...]) + reverse_matmul_answer(
        low, shortcut_ref[...]
    )
    bias_ref[0:1] = jnp.sum(pre_low.astype(jnp.float32), axis=0, keepdims=True)
    bias_ref[1:2] = jnp.sum(low.astype(jnp.float32), axis=0, keepdims=True)


def input_products_kernel(group, me_ref, *refs):
    hidden, met_hidden, low, met_low, pre_low, met_pre_low, features, met_features = refs[:8]
    vectors, met_vectors, to_x, to_y, later, own = refs[8:14]
    turned, low_pair, extras, block = refs[14:]
    tokens = hidden.shape[0]
    columns = low.shape[1]
    half = columns // 2
    core, chip = me_ref[0] & 1, me_ref[0] >> 1
    turned[:, :tokens] = hidden[...].astype(jnp.float32).T.astype(jnp.bfloat16)
    turned[:, tokens:] = met_hidden[...].astype(jnp.float32).T.astype(jnp.bfloat16)
    low_pair[:tokens] = low[...]
    low_pair[tokens:] = met_low[...]
    wide = features.shape[1]
    extras[...] = jnp.zeros_like(extras)
    extras[:wide] = dyadic_accumulation(features[...], pre_low[...]) + dyadic_accumulation(
        met_features[...], met_pre_low[...]
    )
    extras[wide : 2 * wide] = dyadic_accumulation(features[...], low[...]) + dyadic_accumulation(
        met_features[...], met_low[...]
    )
    extras[2 * wide : 2 * wide + vectors.shape[0]] = vectors[...] + met_vectors[...]
    rows = hidden.shape[1] // 8
    each = rows // group
    span = each + EXTRA_ROWS

    def store(rel, total):
        if rel == 0:
            own[0] = total
        elif rel == 1:
            to_x[1, 0] = total[:, :half]
            later[1, 0] = total[:, half:]
        elif rel == 2:
            later[0, 0] = total[:, :half]
            to_y[1, 0] = total[:, half:]
        else:
            to_x[0, 0] = total[:, :half]
            to_y[0, 0] = total[:, half:]

    for place in range(4):
        number = 2 * place + core
        first = pl.multiple_of(number * rows, rows)
        outer = jnp.dot(
            turned[pl.ds(first, rows), :], low_pair[...], preferred_element_type=jnp.float32
        )
        first = pl.multiple_of(number * group * EXTRA_ROWS, group * EXTRA_ROWS)
        extra = extras[pl.ds(first, group * EXTRA_ROWS), :]
        for member in range(group):
            block[member * span : member * span + each] = outer[member * each : (member + 1) * each]
            block[member * span + each : (member + 1) * span] = extra[
                member * EXTRA_ROWS : (member + 1) * EXTRA_ROWS
            ]
        total = block[...].astype(own.dtype)
        for rel in range(4):
            pl.when(chip ^ place == rel)(partial(store, rel, total))


def input_back(grad, pre, emit, latent, shortcut):
    rows, columns = grad.shape
    vmem = pl.BlockSpec(memory_space=pltpu.VMEM)
    return pl.pallas_call(
        input_back_kernel,
        out_shape=[
            jax.ShapeDtypeStruct((rows, columns), LOW),
            jax.ShapeDtypeStruct((rows, columns), LOW),
            jax.ShapeDtypeStruct((rows, latent.shape[0]), FULL),
            jax.ShapeDtypeStruct((2, columns), FULL),
        ],
        in_specs=[vmem] * 5,
        out_specs=[vmem] * 4,
        scratch_shapes=[pltpu.VMEM((rows, columns), FULL)],
        compiler_params=pltpu.CompilerParams(vmem_limit_bytes=32 << 20),
        cost_estimate=SMALL_COST,
    )(grad, pre, emit, latent, shortcut)


def input_products(me, operands):
    group = lax.axis_size("head")
    tokens, columns = operands[2].shape
    width = operands[0].shape[1]
    block = width // 8 + group * EXTRA_ROWS
    pair = jax.ShapeDtypeStruct((2, 1, block, columns // 2), LOW)
    return RowSums(
        *pl.pallas_call(
            partial(input_products_kernel, group),
            out_shape=[pair, pair, pair, jax.ShapeDtypeStruct((1, block, columns), LOW)],
            in_specs=[pl.BlockSpec(memory_space=pltpu.SMEM)]
            + [pl.BlockSpec(memory_space=pltpu.VMEM)] * len(operands),
            out_specs=[pl.BlockSpec(memory_space=pltpu.VMEM)] * 4,
            scratch_shapes=[
                pltpu.VMEM((width, 2 * tokens), LOW),
                pltpu.VMEM((2 * tokens, columns), LOW),
                pltpu.VMEM((8 * group * EXTRA_ROWS, columns), FULL),
                pltpu.VMEM((block, columns), FULL),
            ],
            compiler_params=pltpu.CompilerParams(vmem_limit_bytes=32 << 20),
            cost_estimate=SMALL_COST,
        )((me & 7).reshape(1), *operands)
    )


def entry_kernel(plan, own, me_ref, *refs):
    pieces = refs[: len(plan)]
    main_ref, extra_ref, held, sems = refs[len(plan) :]
    copies = []
    for n, (rel, row, rows) in enumerate(plan):
        spot = held.at[me_ref[0] ^ rel, pl.ds(row, rows)]
        copies.append(pltpu.make_async_copy(pieces[n].at[0], spot, sems.at[n]))
    for copy in copies:
        copy.start()
    for copy in copies:
        copy.wait()
    span = own + EXTRA_ROWS
    group = held.shape[1] // span
    for block in range(8):
        rows = held[block].astype(jnp.float32)
        for member in range(group):
            main_ref[block * group + member] = rows[member * span : member * span + own]
            extra_ref[block * group + member] = rows[member * span + own : (member + 1) * span]


def entry_sums_of_group(total):
    total = total.reshape(-1, total.shape[-1])
    return sum_group_at_once(total).astype(total.dtype)


def entry_everywhere(me, summed, own, count):
    columns = summed.shape[-1]
    group = lax.axis_size("head")
    if lax.axis_size("dp") > 8:
        held = gather_head(summed)
    else:
        every = jnp.broadcast_to(summed[None], (group, *summed.shape))
        held = lax.all_to_all(every, "head", split_axis=0, concat_axis=0, tiled=True)
        held = held.reshape(1, -1, columns)
    pieces = spread_rows(held)
    places = (me & 7).reshape(1)
    span = own + EXTRA_ROWS
    if held.shape[0] > 1 or own % 8 or not in_kernel(pieces):
        (whole,) = place(places, pieces, [columns])
        whole = whole.reshape(-1, span, columns).astype(jnp.float32)
        return whole[:, :own].reshape(-1, columns), whole[:, own:].reshape(-1, columns)[:count], held
    rows = held.shape[1]
    blocks = 8 * rows // span
    plan = [(rel, row, array.shape[1]) for rel, row, array in pieces]
    vmem = pl.BlockSpec(memory_space=pltpu.VMEM)
    main, extra = pl.pallas_call(
        partial(entry_kernel, plan, own),
        out_shape=[
            jax.ShapeDtypeStruct((blocks, own, columns), jnp.float32),
            jax.ShapeDtypeStruct((blocks, EXTRA_ROWS, columns), jnp.float32),
        ],
        in_specs=[pl.BlockSpec(memory_space=pltpu.SMEM)]
        + [pl.BlockSpec(memory_space=pl.ANY)] * len(pieces),
        out_specs=[vmem, vmem],
        scratch_shapes=[
            pltpu.VMEM((8, rows, columns), held.dtype),
            pltpu.SemaphoreType.DMA((len(pieces),)),
        ],
        compiler_params=pltpu.CompilerParams(vmem_limit_bytes=44 << 20),
        cost_estimate=SMALL_COST,
    )(places, *[array for _, _, array in pieces])
    return main.reshape(-1, columns), extra.reshape(-1, columns)[:count], held


def fetch(plan, me, pieces, whole, sems):
    groups = []
    for group in range(whole.shape[1] // MODEL_WIDTH):
        columns = pl.ds(group * MODEL_WIDTH, MODEL_WIDTH)
        copies = []
        for n, (rel, row, rows) in enumerate(plan):
            first = pl.multiple_of((me ^ rel) * (whole.shape[0] // 8) + row, 16)
            copies.append(
                pltpu.make_async_copy(
                    pieces[n].at[0, :, columns],
                    whole.at[pl.ds(first, rows), columns],
                    sems.at[group * len(plan) + n],
                )
            )
        for copy in copies:
            copy.start()
        groups.append(copies)
    return groups


def arrive(copies):
    for copy in copies:
        copy.wait()


def rows_times(left, whole, first, out, tile):
    def step(n, _):
        at = pl.multiple_of(n * tile, 128)
        out[:, pl.ds(at, tile)] = jnp.dot(
            left, whole[:, pl.ds(first + at, tile)], preferred_element_type=jnp.float32
        )
        return 0

    lax.fori_loop(0, out.shape[1] // tile, step, 0)


def rows_times_turned(left, whole, first, width, out, tile):
    def step(n, _):
        at = pl.multiple_of(n * tile, 128)
        part = reverse_matmul_answer(whole[pl.ds(at, tile), pl.ds(first, width)], left)
        out[:, pl.ds(at, tile)] = part.T
        return 0

    lax.fori_loop(0, out.shape[1] // tile, step, 0)


def inverse_norm(rows):
    return lax.rsqrt(jnp.mean(rows * rows, axis=-1, keepdims=True) + EPS)


def other_half(rows):
    half = HEAD_DIM // 2
    lane = lax.broadcasted_iota(jnp.int32, rows.shape, 1) % HEAD_DIM
    ahead = pltpu.roll(rows, rows.shape[1] - half, 1)
    behind = pltpu.roll(rows, half, 1)
    return jnp.where(lane < half, ahead, behind)


def head_window(head, width):
    first = head * HEAD_DIM // 128 * 128
    last = min(-(-(head + 1) * HEAD_DIM // 128) * 128, width)
    start = head * HEAD_DIM - first
    lane = lax.broadcasted_iota(jnp.int32, (1, last - first), 1)
    return slice(first, last), jnp.logical_and(lane >= start, lane < start + HEAD_DIM)


def entry_forward_kernel(plan, me_ref, resid_ref, gain_ref, cosine_ref, sine_ref, allowed_ref, *refs):
    pieces = refs[: len(plan)]
    normed_ref, query_ref, key_ref, value_ref, total_ref, mixed_ref = refs[len(plan) : len(plan) + 6]
    whole, wide, sems = refs[len(plan) + 6 :]
    groups = fetch(plan, me_ref[0], pieces, whole, sems)
    resid = resid_ref[...]
    normed = (resid * inverse_norm(resid) * gain_ref[...]).astype(jnp.bfloat16)
    normed_ref[...] = normed
    for group, out in enumerate((query_ref, key_ref, value_ref)):
        arrive(groups[group])
        rows_times(normed, whole, group * MODEL_WIDTH, wide, 256)
        rows = wide[...]
        if group < 2:
            rows = rows * cosine_ref[...] + other_half(rows) * sine_ref[...]
        out[...] = rows.astype(jnp.bfloat16)
    scale = 1.0 / math.sqrt(HEAD_DIM)
    allowed = allowed_ref[...] > 0.0
    wide[...] = jnp.zeros_like(wide)
    totals = jnp.zeros(total_ref.shape, jnp.float32)
    head_lane = lax.broadcasted_iota(jnp.int32, total_ref.shape, 1)
    for head in range(HEADS):
        window, inside = head_window(head, MODEL_WIDTH)
        query = jnp.where(inside, query_ref[:, window], 0)
        scores = reverse_matmul_answer(query, key_ref[:, window]) * scale
        scores = jnp.where(allowed, scores, -1e30)
        peak = jnp.max(scores, axis=-1, keepdims=True)
        weights = jnp.exp(scores - peak)
        total = jnp.sum(weights, axis=-1, keepdims=True)
        probs = (weights / total).astype(jnp.bfloat16)
        mixed = jnp.dot(probs, value_ref[:, window], preferred_element_type=jnp.float32)
        wide[:, window] += jnp.where(inside, mixed, 0.0)
        totals = jnp.where(head_lane == head, peak + jnp.log(total), totals)
    total_ref[...] = totals
    mixed_ref[...] = wide[...].astype(jnp.bfloat16)


def gelu_parts(x):
    root = math.sqrt(2.0 / math.pi)
    bend = jnp.tanh(root * (x + 0.044715 * (x * x * x)))
    slope = 0.5 * (1.0 + bend) + 0.5 * x * (1.0 - bend * bend) * root * (
        1.0 + 3.0 * 0.044715 * (x * x)
    )
    return 0.5 * x * (1.0 + bend), slope


def rest_forward_kernel(plan, me_ref, resid_ref, mixed_ref, gain_ref, *refs):
    pieces = refs[: len(plan)]
    result_ref, middle_ref, normed_ref, pre_ref = refs[len(plan) : len(plan) + 4]
    whole, sems = refs[len(plan) + 4 :]
    groups = fetch(plan, me_ref[0], pieces, whole, sems)
    arrive(groups[0])
    rows_times(mixed_ref[...], whole, 0, middle_ref, 256)
    middle = resid_ref[...] + middle_ref[...]
    middle_ref[...] = middle
    normed = (middle * inverse_norm(middle) * gain_ref[...]).astype(jnp.bfloat16)
    normed_ref[...] = normed
    arrive(groups[1])
    rows_times(normed, whole, MODEL_WIDTH, pre_ref, 256)
    act = gelu_parts(pre_ref[...])[0].astype(jnp.bfloat16)
    arrive(groups[2])
    rows_times(act, whole, 2 * MODEL_WIDTH, result_ref, 256)
    result_ref[...] += middle_ref[...]


def norm_back(rows, gain, grad):
    inverse = inverse_norm(rows)
    scaled = grad * gain
    mean = jnp.mean(rows * scaled, axis=-1, keepdims=True)
    sent = inverse * scaled - rows * (inverse * inverse * inverse * mean)
    return sent, jnp.sum(grad * rows * inverse, axis=0, keepdims=True)


def rest_backward_kernel(plan, me_ref, grad_ref, middle_ref, pre_ref, gain_ref, *refs):
    pieces = refs[: len(plan)]
    outs = refs[len(plan) : len(plan) + 7]
    grad_middle_ref, mixed_ref, attn_ref, grad_pre_ref, branch_ref, act_ref, gain_grad_ref = outs
    whole, wide, sems = refs[len(plan) + 7 :]
    groups = fetch(plan, me_ref[0], pieces, whole, sems)
    grad = grad_ref[...]
    branch = grad.astype(jnp.bfloat16)
    branch_ref[...] = branch
    arrive(groups[2])
    rows_times_turned(branch, whole, 2 * MODEL_WIDTH, MODEL_WIDTH, wide, 256)
    act, slope = gelu_parts(pre_ref[...])
    act_ref[...] = act.astype(jnp.bfloat16)
    grad_pre = (wide[...] * slope).astype(jnp.bfloat16)
    grad_pre_ref[...] = grad_pre
    arrive(groups[1])
    rows_times_turned(grad_pre, whole, MODEL_WIDTH, MODEL_WIDTH, wide, 256)
    sent, gain_grad_ref[...] = norm_back(middle_ref[...], gain_ref[...], wide[...])
    grad_middle = grad + sent
    grad_middle_ref[...] = grad_middle
    attn = grad_middle.astype(jnp.bfloat16)
    attn_ref[...] = attn
    arrive(groups[0])
    rows_times_turned(attn, whole, 0, MODEL_WIDTH, wide, 256)
    mixed_ref[...] = wide[...].astype(jnp.bfloat16)


def entry_backward_kernel(
    plan,
    me_ref,
    grad_middle_ref,
    grad_mixed_ref,
    resid_ref,
    query_ref,
    key_ref,
    value_ref,
    total_ref,
    gain_ref,
    cosine_ref,
    sine_ref,
    allowed_ref,
    *refs,
):
    pieces = refs[: len(plan)]
    grad_resid_ref, projected_ref, gain_grad_ref = refs[len(plan) : len(plan) + 3]
    whole, grad_query, grad_key, grad_value, sems = refs[len(plan) + 3 :]
    groups = fetch(plan, me_ref[0], pieces, whole, sems)
    scale = 1.0 / math.sqrt(HEAD_DIM)
    allowed = allowed_ref[...] > 0.0
    totals = total_ref[...]
    grad_query[...] = jnp.zeros_like(grad_query)
    grad_key[...] = jnp.zeros_like(grad_key)
    grad_value[...] = jnp.zeros_like(grad_value)
    for head in range(HEADS):
        window, inside = head_window(head, MODEL_WIDTH)
        query = jnp.where(inside, query_ref[:, window], 0)
        keys = key_ref[:, window]
        grad_mixed = jnp.where(inside, grad_mixed_ref[:, window], 0)
        scores = reverse_matmul_answer(query, keys) * scale
        probs = jnp.where(allowed, jnp.exp(scores - totals[:, head : head + 1]), 0.0)
        grad_probs = reverse_matmul_answer(grad_mixed, value_ref[:, window])
        grad_value[:, window] += dyadic_accumulation(probs.astype(jnp.bfloat16), grad_mixed)
        center = jnp.sum(grad_probs * probs, axis=-1, keepdims=True)
        grad_scores = (probs * (grad_probs - center)).astype(jnp.bfloat16)
        along = jnp.dot(grad_scores, keys, preferred_element_type=jnp.float32)
        grad_query[:, window] += jnp.where(inside, along * scale, 0.0)
        grad_key[:, window] += dyadic_accumulation(grad_scores, query) * scale
    for group, part in enumerate((grad_query, grad_key, grad_value)):
        rows = part[...]
        if group < 2:
            rows = rows * cosine_ref[...] - other_half(rows) * sine_ref[...]
        projected_ref[:, group * MODEL_WIDTH : (group + 1) * MODEL_WIDTH] = rows.astype(jnp.bfloat16)
    for copies in groups:
        arrive(copies)
    rows_times_turned(projected_ref[...], whole, 0, 3 * MODEL_WIDTH, grad_query, 256)
    sent, gain_grad_ref[...] = norm_back(resid_ref[...], gain_ref[...], grad_query[...])
    grad_resid_ref[...] = grad_middle_ref[...] + sent


def whole_call(kernel, me, pieces, inputs, outs, wides):
    rows = inputs[0].shape[0]
    plan = [(rel, row, array.shape[1]) for rel, row, array in pieces]
    blocks = 8 * pieces[0][2].shape[1]
    columns = 3 * MODEL_WIDTH
    vmem = pl.BlockSpec(memory_space=pltpu.VMEM)
    return pl.pallas_call(
        partial(kernel, plan),
        out_shape=[jax.ShapeDtypeStruct(shape, kind) for shape, kind in outs],
        in_specs=[pl.BlockSpec(memory_space=pltpu.SMEM)]
        + [vmem] * len(inputs)
        + [pl.BlockSpec(memory_space=pl.ANY)] * len(pieces),
        out_specs=[vmem] * len(outs),
        scratch_shapes=[pltpu.VMEM((blocks, columns), jnp.bfloat16)]
        + [pltpu.VMEM((rows, MODEL_WIDTH), jnp.float32)] * wides
        + [pltpu.SemaphoreType.DMA((3 * len(pieces),))],
        compiler_params=pltpu.CompilerParams(vmem_limit_bytes=44 << 20),
        cost_estimate=SMALL_COST,
    )(me, *inputs, *[array for _, _, array in pieces])


def in_kernel(pieces):
    lead, rows, _ = pieces[0][2].shape
    return lead == 1 and rows % 32 == 0


LOW, FULL = jnp.bfloat16, jnp.float32


class Layer:
    def __init__(self, places, entry_pieces, gains, tables, allowed):
        self.places, self.entry_pieces, self.gains = places, entry_pieces, gains
        self.tables, self.allowed = tables, allowed
        self.fetched = in_kernel(entry_pieces)
        if not self.fetched:
            self.entry_whole = place(places, entry_pieces, [3 * MODEL_WIDTH])[0][0]

    def add_rest(self, rest_pieces):
        self.rest_pieces = rest_pieces
        if not self.fetched:
            self.rest_whole = [part[0] for part in place(self.places, rest_pieces, [MODEL_WIDTH] * 3)]

    def shapes(self, *kinds):
        rows = self.allowed.shape[0]
        return [((rows, width), kind) for width, kind in kinds]

    def entry_forward(self, resid):
        if not self.fetched:
            self.saved = entry_forward(
                resid, self.entry_whole, self.gains, *self.tables[:2], self.allowed
            )
            return self.saved[6]
        wide = (MODEL_WIDTH, LOW)
        self.resid = resid
        outs = whole_call(
            entry_forward_kernel,
            self.places,
            self.entry_pieces,
            (resid, self.gains[:1].astype(FULL), *self.tables[2:], self.allowed.astype(FULL)),
            self.shapes(wide, wide, wide, wide, (128, FULL), wide),
            1,
        )
        self.normed_first, self.heads = outs[0], outs[1:5]
        return outs[5]

    def rest_forward(self, mixed):
        if not self.fetched:
            result, self.saved = rest_forward(
                (*self.saved[:6], mixed), *self.rest_whole, self.gains
            )
            return result
        self.mixed = mixed
        result, self.middle, self.normed_second, self.hidden_pre = whole_call(
            rest_forward_kernel,
            self.places,
            self.rest_pieces,
            (self.resid, mixed, self.gains[1:].astype(FULL)),
            self.shapes(
                (MODEL_WIDTH, FULL), (MODEL_WIDTH, FULL), (MODEL_WIDTH, LOW), (MODEL_WIDTH, FULL)
            ),
            0,
        )
        return result

    def rest_backward(self, grad):
        if not self.fetched:
            weights = (self.entry_whole, *self.rest_whole, self.gains)
            return rest_backward(self.saved, weights, grad)
        wide = (MODEL_WIDTH, LOW)
        grad_middle, grad_mixed, grad_attn, grad_pre, branch, act, gain_grad = whole_call(
            rest_backward_kernel,
            self.places,
            self.rest_pieces,
            (grad, self.middle, self.hidden_pre, self.gains[1:].astype(FULL)),
            self.shapes((MODEL_WIDTH, FULL), wide, wide, wide, wide, wide)
            + [((1, MODEL_WIDTH), FULL)],
            1,
        )
        lefts = (self.mixed, self.normed_second, act)
        return grad_middle, grad_mixed, lefts, (grad_attn, grad_pre, branch), gain_grad[0]

    def entry_backward(self, grad_middle, grad_mixed):
        if not self.fetched:
            weights = (self.entry_whole, *self.rest_whole, self.gains)
            return entry_backward(
                self.saved, weights, *self.tables[:2], self.allowed, grad_middle, grad_mixed
            )
        grad_resid, projected, gain_grad = whole_call(
            entry_backward_kernel,
            self.places,
            self.entry_pieces,
            (
                grad_middle,
                grad_mixed,
                self.resid,
                *self.heads,
                self.gains[:1].astype(FULL),
                *self.tables[2:],
                self.allowed.astype(FULL),
            ),
            self.shapes((MODEL_WIDTH, FULL), (3 * MODEL_WIDTH, LOW)) + [((1, MODEL_WIDTH), FULL)],
            3,
        )
        return grad_resid, self.normed_first, projected, gain_grad[0]


def entry_forward(resid, qkv_full, gain_pair, cosine, sine, allowed):
    gains = gain_pair.astype(jnp.float32)
    rows = resid.shape[0]
    normed_first = norm_apply(resid, gains[0]).astype(jnp.bfloat16)
    projected = jnp.dot(normed_first, qkv_full, preferred_element_type=jnp.float32)
    query_rows = rotate(
        projected[:, :MODEL_WIDTH].reshape(rows, HEADS, HEAD_DIM), cosine, sine
    ).astype(jnp.bfloat16)
    key_rows = rotate(
        projected[:, MODEL_WIDTH : 2 * MODEL_WIDTH].reshape(rows, HEADS, HEAD_DIM), cosine, sine
    ).astype(jnp.bfloat16)
    value_rows = projected[:, 2 * MODEL_WIDTH :].reshape(rows, HEADS, HEAD_DIM).astype(jnp.bfloat16)

    mixed, log_total = attend_forward(query_rows, key_rows, value_rows, allowed)
    mixed_low = mixed.reshape(rows, MODEL_WIDTH).astype(jnp.bfloat16)
    return (resid, normed_first, query_rows, key_rows, value_rows, log_total, mixed_low)


def rest_forward(saved, out_full, up_full, down_full, gain_pair):
    gains = gain_pair.astype(jnp.float32)
    resid, mixed_low = saved[0], saved[6]
    middle = resid + jnp.dot(mixed_low, out_full, preferred_element_type=jnp.float32)
    normed_second = norm_apply(middle, gains[1]).astype(jnp.bfloat16)
    hidden_pre = jnp.dot(normed_second, up_full, preferred_element_type=jnp.float32)
    hidden_act = jax.nn.gelu(hidden_pre, approximate=True).astype(jnp.bfloat16)
    result = middle + jnp.dot(hidden_act, down_full, preferred_element_type=jnp.float32)
    return (result, (*saved, middle, normed_second, hidden_pre))


def rest_backward(saved, weights, grad_result):
    mixed_low, middle, normed_second, hidden_pre = saved[6:]
    _, out_full, up_full, down_full, gain_pair = weights
    gains = gain_pair.astype(jnp.float32)
    grad_branch = grad_result.astype(jnp.bfloat16)
    hidden_act, gelu_pull = jax.vjp(partial(jax.nn.gelu, approximate=True), hidden_pre)
    hidden_low = hidden_act.astype(jnp.bfloat16)
    grad_act = reverse_matmul_answer(grad_branch, down_full)
    grad_pre = gelu_pull(grad_act)[0].astype(jnp.bfloat16)
    grad_normed_second = reverse_matmul_answer(grad_pre, up_full)
    unused_second, second_pull = jax.vjp(norm_apply, middle, gains[1])
    grad_middle_norm, grad_gain_second = second_pull(grad_normed_second)
    grad_middle = grad_result + grad_middle_norm
    grad_attn = grad_middle.astype(jnp.bfloat16)
    grad_mixed = reverse_matmul_answer(grad_attn, out_full).astype(jnp.bfloat16)
    left_rows = (mixed_low, normed_second, hidden_low)
    right_rows = (grad_attn, grad_pre, grad_branch)
    return (grad_middle, grad_mixed, left_rows, right_rows, grad_gain_second)


def entry_backward(saved, weights, cosine, sine, allowed, grad_middle, grad_mixed):
    resid, normed_first, query_rows, key_rows, value_rows, log_total = saved[:6]
    qkv_full = weights[0]
    gains = weights[4].astype(jnp.float32)
    rows = resid.shape[0]
    grad_query, grad_keys, grad_values = attend_backward(
        query_rows,
        key_rows,
        value_rows,
        allowed,
        log_total,
        grad_mixed.reshape(rows, HEADS, HEAD_DIM),
    )
    grad_query = unrotate(grad_query, cosine, sine).reshape(rows, MODEL_WIDTH)
    grad_keys = unrotate(grad_keys, cosine, sine).reshape(rows, MODEL_WIDTH)
    grad_values = grad_values.reshape(rows, MODEL_WIDTH)
    grad_projected = jnp.concatenate([grad_query, grad_keys, grad_values], axis=1).astype(
        jnp.bfloat16
    )
    grad_normed_first = reverse_matmul_answer(grad_projected, qkv_full)
    unused_first, first_pull = jax.vjp(norm_apply, resid, gains[0])
    grad_resid_norm, grad_gain_first = first_pull(grad_normed_first)
    return (grad_middle + grad_resid_norm, normed_first, grad_projected, grad_gain_first)


def body(
    patch_observations,
    sequence_labels,
    leading_filler_count,
    intake_latent_matrix,
    intake_latent_offset,
    intake_emit_matrix,
    intake_emit_offset,
    intake_shortcut_matrix,
    attention_entry_matrices,
    attention_merge_matrix,
    feedforward_widen_matrix,
    feedforward_shrink_matrix,
    layer_scale_factors,
    readout_latent_matrix,
    readout_latent_offset,
    readout_emit_matrix,
    readout_emit_offset,
    readout_shortcut_matrix,
    loss_sensitivity,
):
    patch_len = patch_observations.shape[1]
    position, pad_count, allowed, keep_rows = layout_rows(
        sequence_labels[0], leading_filler_count[0], patch_len
    )
    cosine, sine = rotary_tables(position, HEAD_DIM)
    columns = jnp.arange(patch_len, dtype=jnp.int32)
    pad_mask = columns[None, :] < pad_count[:, None]
    features = jnp.concatenate(
        [
            jnp.where(pad_mask, jnp.zeros_like(patch_observations), patch_observations),
            pad_mask.astype(jnp.bfloat16),
        ],
        axis=1,
    )
    entry_pre = (
        jnp.dot(features, intake_latent_matrix, preferred_element_type=jnp.float32)
        + intake_latent_offset
    )
    entry_hidden = jax.nn.silu(entry_pre).astype(jnp.bfloat16)
    resid = (
        jnp.dot(entry_hidden, intake_emit_matrix, preferred_element_type=jnp.float32)
        + intake_emit_offset
        + jnp.dot(features, intake_shortcut_matrix, preferred_element_type=jnp.float32)
    )
    layer_count = attention_entry_matrices.shape[0]
    group = lax.axis_size("head")
    group_place = lax.axis_index("head")
    outer = lax.axis_size("dp") // 8
    me = lax.axis_index("dp").astype(jnp.int32)
    places = (me & 7).reshape(1)
    own_count = layer_scale_factors.shape[2]
    rows = patch_observations.shape[0]

    group_width = readout_latent_offset.shape[0]
    offsets = jnp.stack([readout_latent_offset, readout_emit_offset])
    coarse = lax.reduce_precision(offsets, 8, 7)
    offset_rows = jnp.concatenate([coarse, offsets - coarse], axis=0).astype(jnp.bfloat16)
    offset_rows = jnp.pad(offset_rows, ((0, 12), (0, 0)))
    sent = jnp.concatenate(
        [
            loss_sensitivity.reshape(group, rows, group_width),
            jnp.broadcast_to(offset_rows[None], (group, 16, group_width)),
        ],
        axis=1,
    )
    gain_columns = layer_scale_factors.reshape(2 * layer_count, own_count).T
    gain_columns = jnp.pad(gain_columns, ((0, 0), (0, 128 - 2 * layer_count)))
    chunks = []
    for layer_index in range(layer_count):
        entry_own = attention_entry_matrices[layer_index]
        if layer_index == 0:
            entry_own = jnp.concatenate([entry_own, gain_columns], axis=1)
        chunks.append(entry_own)
        rest_own = jnp.concatenate(
            [
                attention_merge_matrix[layer_index],
                feedforward_widen_matrix[layer_index],
                feedforward_shrink_matrix[layer_index],
            ],
            axis=1,
        )
        chunks.append(rest_own)
    head_own = jnp.concatenate(
        [
            lax.dynamic_index_in_dim(
                matrix.reshape(outer, 8, -1, group_width), me % 8, 1, keepdims=False
            )
            for matrix in (readout_latent_matrix, readout_shortcut_matrix, readout_emit_matrix)
        ],
        axis=2,
    )
    chunks.append(head_own)
    count = len(chunks)

    def gather_chunk(number, own):
        if number < count - 1:
            return gather_head(own)
        return lax.all_gather(own, "head", axis=0, tiled=True)

    held = gather_chunk(0, chunks[0])
    cosine_wide = jnp.tile(jnp.concatenate([cosine[:, 0], cosine[:, 0]], axis=1), (1, HEADS))
    sine_wide = jnp.tile(jnp.concatenate([-sine[:, 0], sine[:, 0]], axis=1), (1, HEADS))
    tables = (cosine, sine, cosine_wide, sine_wide)
    nears, fars, near_mets, far_mets = [], [], [], []
    layers = []
    onward = None
    for number in range(count + 1):
        step = {}
        if number < count:
            step["x"], step["y"] = swap(held, 1), swap(held, 2)
        if number + 1 < count:
            step["next"] = gather_chunk(number + 1, chunks[number + 1])
        if number == count - 1:
            step["met"] = lax.all_to_all(
                after(sent, held), "head", split_axis=0, concat_axis=0, tiled=True
            )
        if number == 0:
            step["resid"] = resid
        else:
            step["far"] = (swap(onward[0], 1), swap(onward[1], 2))
            step["far_met"] = [swap(part, 0) for part in step["far"]]
        turn = onward
        if number > 1:
            chunk = number - 2
            pieces = all_pieces(nears[chunk], fars[chunk], near_mets[chunk], far_mets[chunk])
            if chunk == 0:
                gain_rows = place(places, pieces, [128], 3 * MODEL_WIDTH)[0][0]
                gain_rows = gain_rows[:, : 2 * layer_count].T.reshape(layer_count, 2, -1)
            if chunk % 2 == 0:
                layers.append(Layer(places, pieces, gain_rows[chunk // 2], tables, allowed))
                step["mixed"] = layers[-1].entry_forward(resid)
            else:
                layers[-1].add_rest(pieces)
                step["resid"] = layers[-1].rest_forward(mixed)
            if number < count:
                turn = step.get("mixed", step.get("resid"))
        if number > 0:
            step["near_met"] = [swap(part, 0) for part in after(nears[number - 1], turn)]
        step["own"] = chunks[number + 2 :]
        step = lax.optimization_barrier(step)
        chunks[number + 2 :] = step["own"]
        if number < count:
            nears.append((held, step["x"], step["y"]))
            onward = second_step(*nears[-1])
        held = step.get("next")
        if number > 0:
            fars.append(step["far"])
            far_mets.append(step["far_met"])
            near_mets.append(step["near_met"])
        resid = step.get("resid", resid)
        mixed = step.get("mixed")
        if "met" in step:
            met = step["met"]
    head_pieces = all_pieces(nears[-1], fars[-1], near_mets[-1], far_mets[-1])
    sensitivity = met[:, :rows]
    head_offsets = met[:, rows : rows + 4].astype(jnp.float32)
    latent_offsets = head_offsets[:, 0] + head_offsets[:, 2]
    emit_offsets = head_offsets[:, 1] + head_offsets[:, 3]

    top = resid.astype(jnp.bfloat16)
    keep_column = keep_rows[:, None]
    grad_forecast = (sensitivity.astype(jnp.float32) * keep_column).astype(jnp.bfloat16)
    grad_forecast_rows = jnp.concatenate([grad_forecast[part] for part in range(group)], axis=1)
    head_inputs = (top, keep_column, latent_offsets, emit_offsets, grad_forecast)
    if layers[0].fetched:
        outs = output_block(places, head_pieces, *head_inputs)
    else:
        head_whole = place(places, head_pieces, [3 * group_width])[0]
        outs = output_plain(head_whole, *head_inputs)
    head_hidden, forecast, grad_head_pre, grad_resid, pre_sums = outs
    token_predictions = lax.all_to_all(
        forecast, "head", split_axis=0, concat_axis=0, tiled=True
    ).reshape(group * rows, group_width)
    head_bias_rows = (pre_sums[0], jnp.sum(grad_forecast_rows.astype(jnp.float32), axis=0))
    head_both = exchange(
        [
            (top, grad_head_pre),
            (top, grad_forecast_rows),
            (head_hidden, grad_forecast_rows),
        ]
    )
    gain_sums = [[None, None] for _ in range(layer_count)]

    def rest_stage(layer_index, carry):
        outs = layers[layer_index].rest_backward(carry["grad"])
        gain_sums[layer_index][1] = outs[4]
        both = exchange(list(zip(outs[2], outs[3], strict=True)))
        return {"middle": outs[0], "mixed": outs[1]}, both

    def entry_stage(layer_index, carry):
        outs = layers[layer_index].entry_backward(carry["middle"], carry["mixed"])
        gain_sums[layer_index][0] = outs[3]
        return {"grad": outs[0]}, exchange([(outs[1], outs[2])])

    def input_stage(carry):
        head_rows = [row[None] for row in head_bias_rows]
        gain_rows = [row[None] for pair in gain_sums for row in pair]
        if layers[0].fetched and 2 + len(head_rows) + len(gain_rows) == EXTRA_ROWS:
            low, pre_low, grad_features, bias_rows = input_back(
                carry["grad"],
                entry_pre,
                intake_emit_matrix,
                intake_latent_matrix,
                intake_shortcut_matrix,
            )
            values_grad = jnp.where(pad_mask, 0.0, grad_features[:, :patch_len])
            vectors = jnp.concatenate([bias_rows, *head_rows, *gain_rows], axis=0)
            operands = []
            for part in (entry_hidden, low, pre_low, features, vectors):
                operands += [part, swap(part, 0)]
            return values_grad, 4 * patch_len + EXTRA_ROWS, operands
        grad_entry = carry["grad"].astype(jnp.bfloat16)
        grad_entry_outer = dyadic_accumulation(entry_hidden, grad_entry)
        grad_entry_outer_bias = jnp.sum(grad_entry.astype(jnp.float32), axis=0)
        grad_entry_skip = dyadic_accumulation(features, grad_entry)
        unused_entry, entry_pull = jax.vjp(jax.nn.silu, entry_pre)
        grad_entry_pre = entry_pull(reverse_matmul_answer(grad_entry, intake_emit_matrix))[0].astype(
            jnp.bfloat16
        )
        grad_entry_inner = dyadic_accumulation(features, grad_entry_pre)
        grad_entry_inner_bias = jnp.sum(grad_entry_pre.astype(jnp.float32), axis=0)
        grad_features = reverse_matmul_answer(
            grad_entry_pre, intake_latent_matrix
        ) + reverse_matmul_answer(grad_entry, intake_shortcut_matrix)
        values_grad = jnp.where(pad_mask, 0.0, grad_features[:, :patch_len])
        extra_rows = jnp.concatenate(
            [
                grad_entry_inner,
                grad_entry_skip,
                grad_entry_inner_bias[None],
                grad_entry_outer_bias[None],
            ]
            + head_rows
            + [row[None] for pair in gain_sums for row in pair],
            axis=0,
        )
        plain = entry_products(me, grad_entry_outer, extra_rows)
        return values_grad, extra_rows.shape[0], (plain.sent, plain.later, plain.own)

    stages = []
    for layer_index in reversed(range(layer_count)):
        stages += [(rest_stage, layer_index), (entry_stage, layer_index)]
    stage_count = len(stages)
    carry = {"grad": grad_resid}
    boths = {0: head_both}
    sums = {0: RowSums(*pair_products(me, head_both))}
    totals, finished = {}, {}
    entry_chunk = None
    done = 0

    def close(**step):
        step["sent"] = {n: (sums[n].sent, sums[n].later, sums[n].own) for n in sums}
        step["boths"] = boths
        step["carry"] = carry
        step = lax.optimization_barrier(step)
        for n, parts in step.pop("sent").items():
            sums[n].sent, sums[n].later, sums[n].own = parts
        return step

    step = close()
    for number in range(stage_count + 1):
        carry, boths = step["carry"], step["boths"]
        parts = {"first": sums[number].first()}
        if number >= 1:
            totals[number - 1] = sums.pop(number - 1).total()
            if number == 1:
                finished[0] = sum_columns(totals[0])
            else:
                finished[number - 1] = sum_group(totals[number - 1])
        if number >= 2:
            parts["finished"] = finished[number - 2]
        until = {stage_count - 2: stage_count}.get(number, number + 1)
        while done < min(until, stage_count):
            stage, layer_index = stages[done]
            carry, boths[done + 1] = stage(layer_index, carry)
            done += 1
        if number == stage_count - 2:
            values_grad, extra_count, parts["entry"] = input_stage(carry)
        if number == stage_count - 1:
            entry_chunk.met = entry_chunk.first()
        if number == stage_count:
            entry_summed = entry_sums_of_group(entry_chunk.total())
        step = close(**parts)
        sums[number].met = step["first"]
        if number >= 2:
            finished[number - 2] = step["finished"]
        carry, boths = step["carry"], step["boths"]
        parts = {"last": sums[number].last()}
        if number == stage_count - 2:
            if layers[0].fetched:
                entry_chunk = input_products(me, step["entry"])
            else:
                (to_x, to_y), later, own = step["entry"]
                entry_chunk = RowSums(to_x, to_y, later, own)
            parts["entry"] = (entry_chunk.sent, entry_chunk.later, entry_chunk.own)
        if number == stage_count - 1:
            parts["entry"] = entry_chunk.last()
        if number < stage_count:
            sums[number + 1] = RowSums(*pair_products(me, boths.pop(number + 1)))
            step = close(**parts)
        else:
            step = parts
        sums[number].last_met = step["last"]
        if number == stage_count - 2:
            entry_chunk.sent, entry_chunk.later, entry_chunk.own = step["entry"]
        if number == stage_count - 1:
            entry_chunk.last_met = step["entry"]
    finished[stage_count] = sum_group_at_once(sums[stage_count].total())
    entry_main, entry_extra, entry_held = entry_everywhere(
        me, entry_summed, own_count, extra_count
    )
    head_rows = gather_blocks(me, finished[0])
    head_sums = [after(head_rows[n], entry_held).astype(jnp.float32) for n in range(3)]
    layer_sums = [None] * layer_count
    for member, layer_index in enumerate(reversed(range(layer_count))):
        rest = finished[1 + 2 * member].astype(jnp.float32)
        entry = finished[2 + 2 * member].astype(jnp.float32)
        layer_sums[layer_index] = (entry[0], rest[0], rest[1], rest[2])
    inner_rows = 2 * patch_len
    last = 2 * inner_rows
    entry_sums = (
        entry_extra[:inner_rows],
        entry_extra[last],
        entry_main,
        entry_extra[last + 1],
        entry_extra[inner_rows:last],
    )
    head_bias_sums = lax.dynamic_slice_in_dim(
        entry_extra[last + 2 : last + 4], group_place * group_width, group_width, 1
    )
    own_place = (me * group + group_place) * own_count
    gains_grad = lax.dynamic_slice_in_dim(
        entry_extra[last + 4 : last + 4 + 2 * layer_count], own_place, own_count, 1
    ).reshape(layer_count, 2, own_count)
    qkv_grad = jnp.stack([layer_sums[member][0] for member in range(layer_count)])
    out_grad = jnp.stack([layer_sums[member][1] for member in range(layer_count)])
    up_grad = jnp.stack([layer_sums[member][2] for member in range(layer_count)])
    down_grad = jnp.stack([layer_sums[member][3] for member in range(layer_count)])
    return (
        token_predictions,
        values_grad,
        entry_sums[0],
        entry_sums[1],
        entry_sums[2],
        entry_sums[3],
        entry_sums[4],
        qkv_grad,
        out_grad,
        up_grad,
        down_grad,
        gains_grad,
        head_sums[0],
        head_bias_sums[0],
        head_sums[2],
        head_bias_sums[1],
        head_sums[1],
    )


def solution(mesh):
    return jax.shard_map(
        body,
        mesh=mesh,
        in_specs=(
            P(("dp", "head"), None),
            P(("dp", "head"), None),
            P(("dp", "head"), None),
            P(),
            P(),
            P(),
            P(),
            P(),
            P(None, ("dp", "head"), None),
            P(None, ("dp", "head"), None),
            P(None, ("dp", "head"), None),
            P(None, ("dp", "head"), None),
            P(None, None, ("dp", "head")),
            P(None, "head"),
            P("head"),
            P(None, "head"),
            P("head"),
            P(None, "head"),
            P("dp", "head"),
        ),
        out_specs=(
            P("dp", "head"),
            P(("dp", "head"), None),
            P(),
            P(),
            P(),
            P(),
            P(),
            P(None, ("dp", "head"), None),
            P(None, ("dp", "head"), None),
            P(None, ("dp", "head"), None),
            P(None, ("dp", "head"), None),
            P(None, None, ("dp", "head")),
            P(None, "head"),
            P("head"),
            P(None, "head"),
            P("head"),
            P(None, "head"),
        ),
        check_vma=False,
    )
```

```python
from functools import partial
import math

import jax
import jax.numpy as jnp
from jax import lax
from jax.experimental import pallas as pl
from jax.experimental.pallas import tpu as pltpu
from jax.sharding import PartitionSpec as P

MODEL_WIDTH = 1280
HEADS = 16
HEAD_DIM = 80


EPS = 1e-06
SMALL_COST = pl.CostEstimate(flops=1, bytes_accessed=1, transcendentals=0)
ROPE_BASE = 10000.0


def layout_rows(series_row, pad_row, patch_len):
    count = series_row.shape[0]
    order = jnp.arange(count, dtype=jnp.int32)
    same_series = series_row[:, None] == series_row[None, :]
    earlier = order[None, :] < order[:, None]
    position = jnp.sum(jnp.logical_and(same_series, earlier).astype(jnp.int32), axis=1)
    numbers = jnp.arange(pad_row.shape[0], dtype=jnp.int32)
    series_pad = jnp.sum(
        jnp.where(series_row[:, None] == numbers[None, :], pad_row[None, :], 0), axis=1
    )
    pad_count = jnp.where(position == 0, series_pad, 0)
    padded = pad_count == patch_len
    diagonal = order[:, None] == order[None, :]
    reach = jnp.logical_or(jnp.logical_and(earlier, jnp.logical_not(padded)[None, :]), diagonal)
    allowed = jnp.logical_and(same_series, reach)
    keep_rows = jnp.where(padded, 0.0, 1.0).astype(jnp.float32)
    return (position, pad_count, allowed, keep_rows)


def rotary_tables(position, head_dim):
    half = head_dim // 2
    steps = jnp.arange(half, dtype=jnp.float32) / half
    inverse = jnp.exp(-math.log(ROPE_BASE) * steps)
    angles = position.astype(jnp.float32)[:, None] * inverse[None, :]
    return (jnp.cos(angles)[:, None, :], jnp.sin(angles)[:, None, :])


def rotate(heads_rows, cosine, sine):
    half = heads_rows.shape[-1] // 2
    first = heads_rows[..., :half]
    second = heads_rows[..., half:]
    return jnp.concatenate(
        [first * cosine - second * sine, second * cosine + first * sine], axis=-1
    )


def unrotate(grad_rows, cosine, sine):
    half = grad_rows.shape[-1] // 2
    first = grad_rows[..., :half]
    second = grad_rows[..., half:]
    return jnp.concatenate(
        [first * cosine + second * sine, second * cosine - first * sine], axis=-1
    )


def norm_apply(resid, gain):
    return resid * lax.rsqrt(jnp.mean(resid * resid, axis=-1, keepdims=True) + EPS) * gain


def dyadic_accumulation(left, right):
    return lax.dot_general(
        left, right, (((0,), (0,)), ((), ())), preferred_element_type=jnp.float32
    )


def reverse_matmul_answer(grad_rows, weight):
    return lax.dot_general(
        grad_rows, weight, (((1,), (1,)), ((), ())), preferred_element_type=jnp.float32
    )


def masked_scores(query_rows, key_rows, allowed):
    scale = 1.0 / math.sqrt(query_rows.shape[-1])
    scores = (
        jnp.einsum("qhd,khd->hqk", query_rows, key_rows, preferred_element_type=jnp.float32) * scale
    )
    return jnp.where(allowed[None], scores, -1e30)


def attend_forward(query_rows, key_rows, value_rows, allowed):
    scores = masked_scores(query_rows, key_rows, allowed)
    peak = jnp.max(scores, axis=-1, keepdims=True)
    weights = jnp.exp(scores - peak)
    total = jnp.sum(weights, axis=-1, keepdims=True)
    probs = (weights / total).astype(jnp.bfloat16)
    mixed = jnp.einsum("hqk,khd->qhd", probs, value_rows, preferred_element_type=jnp.float32)
    return (mixed, peak + jnp.log(total))


def attend_backward(query_rows, key_rows, value_rows, allowed, log_total, grad_mixed):
    scale = 1.0 / math.sqrt(query_rows.shape[-1])
    scores = masked_scores(query_rows, key_rows, allowed)
    probs = jnp.where(allowed[None], jnp.exp(scores - log_total), 0.0)
    grad_probs = jnp.einsum(
        "qhd,khd->hqk", grad_mixed, value_rows, preferred_element_type=jnp.float32
    )
    grad_values = jnp.einsum(
        "hqk,qhd->khd", probs.astype(jnp.bfloat16), grad_mixed, preferred_element_type=jnp.float32
    )
    center = jnp.sum(grad_probs * probs, axis=-1, keepdims=True)
    grad_scores = (probs * (grad_probs - center)).astype(jnp.bfloat16)
    grad_query = (
        jnp.einsum("hqk,khd->qhd", grad_scores, key_rows, preferred_element_type=jnp.float32)
        * scale
    )
    grad_keys = (
        jnp.einsum("hqk,qhd->khd", grad_scores, query_rows, preferred_element_type=jnp.float32)
        * scale
    )
    return (grad_query, grad_keys, grad_values)


def after(value, *earlier):
    return lax.optimization_barrier((value, *earlier))[0]


def swap(v, bit):
    size = lax.axis_size("dp")
    return lax.ppermute(v, "dp", [(i, i ^ (1 << bit)) for i in range(size)])


def outer_groups():
    size = lax.axis_size("dp")
    return [[j + 8 * o for o in range(size // 8)] for j in range(8)]


def place_kernel(plan, piece_count, out_count, me_ref, *refs):
    pieces = refs[:piece_count]
    outs = refs[piece_count : piece_count + out_count]
    held = refs[piece_count + out_count : piece_count + 2 * out_count]
    in_sems, out_sems = refs[piece_count + 2 * out_count :]
    inward, outward = [], []
    for n, (piece, rel, row, out, column) in enumerate(plan):
        source = pieces[piece]
        width = held[out].shape[-1]
        if width != source.shape[-1]:
            source = source.at[:, :, pl.ds(column, width)]
        spot = (slice(None), me_ref[0] ^ rel, pl.ds(row, source.shape[1]), slice(None))
        inward.append(pltpu.make_async_copy(source, held[out].at[spot], in_sems.at[n]))
        outward.append(
            pltpu.make_async_copy(held[out].at[spot], outs[out].at[spot], out_sems.at[n])
        )
    for copy in inward:
        copy.start()
    for copy, onward in zip(inward, outward):
        copy.wait()
        onward.start()
    for onward in outward:
        onward.wait()


def place(me, pieces, widths, first=0):
    plan = []
    for n, (rel, row, _) in enumerate(pieces):
        column = first
        for out, width in enumerate(widths):
            plan.append((n, rel, row, out, column))
            column += width
    arrays = [array for _, _, array in pieces]
    lead, rows, _ = arrays[0].shape
    kind = arrays[0].dtype
    total = sum(8 * lead * rows * -(-w // 128) * 128 for w in widths) * 2
    outs = pl.pallas_call(
        partial(place_kernel, plan, len(arrays), len(widths)),
        out_shape=[jax.ShapeDtypeStruct((lead, 8, rows, w), kind) for w in widths],
        in_specs=[pl.BlockSpec(memory_space=pltpu.SMEM)]
        + [pl.BlockSpec(memory_space=pl.ANY)] * len(arrays),
        out_specs=[pl.BlockSpec(memory_space=pl.ANY)] * len(widths),
        scratch_shapes=[pltpu.VMEM((lead, 8, rows, w), kind) for w in widths]
        + [pltpu.SemaphoreType.DMA((len(plan),))] * 2,
        compiler_params=pltpu.CompilerParams(vmem_limit_bytes=total + (4 << 20)),
        cost_estimate=SMALL_COST,
    )(me, *arrays)
    outer = lax.axis_size("dp") // 8
    return [o.reshape(-1, outer * 8 * rows, o.shape[-1]) for o in outs]


def row_half(rows):
    return rows // 32 * 16 if rows >= 32 else rows // 2


def second_step(held, from_x, from_y):
    half = row_half(held.shape[1])
    return from_y[:, :half], from_x[:, half:]


def all_pieces(near, far, near_met, far_met):
    half = far[0].shape[1]
    places = ((0, 0), (2, 0), (4, 0), (6, 0), (6, half))
    pieces = []
    for (rel, row), array, met in zip(places, (*near, *far), (*near_met, *far_met), strict=True):
        pieces += [(rel, row, array), (rel | 1, row, met)]
    return pieces


def spread_rows(held):
    near = (held, swap(held, 1), swap(held, 2))
    onward_x, onward_y = second_step(*near)
    far = (swap(onward_x, 1), swap(onward_y, 2))
    return all_pieces(near, far, [swap(part, 0) for part in near], [swap(part, 0) for part in far])


def gather_head(own):
    held = lax.all_gather(own, "head", axis=0, tiled=True)[None]
    if lax.axis_size("dp") > 8:
        held = lax.all_gather(
            held, "dp", axis=0, tiled=True, axis_index_groups=outer_groups()
        )
    return held


def product_kernel(count, outer, me_ref, *refs):
    lefts, rights, met_lefts, met_rights = (refs[n * count : (n + 1) * count] for n in range(4))
    to_x, to_y, later, own, right_pair, turned = refs[4 * count :]
    rows, width = own.shape[1] // outer, own.shape[-1]
    tokens = lefts[0].shape[0]
    half = width // 2
    tile = half if half <= 640 else 640
    odd = me_ref[0] & 1 == 1
    chip = me_ref[0] >> 1

    def store(rel, n, span, side, columns, total):
        if rel == 0:
            own[n, span, slice(side * half + columns.start, side * half + columns.stop)] = total
        elif rel == 1 and side == 0:
            to_x[1, n, span, columns] = total
        elif rel == 1:
            later[1, n, span, columns] = total
        elif rel == 2 and side == 0:
            later[0, n, span, columns] = total
        elif rel == 2:
            to_y[1, n, span, columns] = total
        elif side == 0:
            to_x[0, n, span, columns] = total
        else:
            to_y[0, n, span, columns] = total

    for n in range(count):
        right_pair[:tokens] = rights[n][...]
        right_pair[tokens:] = met_rights[n][...]
        for part in range(outer):
            span = slice(part * rows, (part + 1) * rows)
            for place in range(4):
                first = (part * 8 + 2 * place) * rows
                near, far = slice(first, first + rows), slice(first + rows, first + 2 * rows)
                left_pair = jnp.concatenate(
                    [
                        jnp.where(odd, side[n][:, far], side[n][:, near]).astype(jnp.float32)
                        for side in (lefts, met_lefts)
                    ],
                    axis=0,
                )
                turned[place] = left_pair.T.astype(own.dtype)
            every = turned[...].reshape(4 * rows, 2 * tokens)
            for side in range(2):
                for at in range(0, half, tile):
                    total = jnp.dot(
                        every,
                        right_pair[:, side * half + at : side * half + at + tile],
                        preferred_element_type=jnp.float32,
                    ).astype(own.dtype)
                    for place in range(4):
                        for rel in range(4):
                            pl.when(chip ^ place == rel)(
                                partial(
                                    store,
                                    rel,
                                    n,
                                    span,
                                    side,
                                    slice(at, at + tile),
                                    total[place * rows : (place + 1) * rows],
                                )
                            )


def exchange(pairs):
    met = {}
    for pair in pairs:
        for rows in pair:
            if id(rows) not in met:
                met[id(rows)] = swap(rows, 0)
    return [(left, right, met[id(left)], met[id(right)]) for left, right in pairs]


def pair_products(me, both):
    outer = lax.axis_size("dp") // 8
    count = len(both)
    left, right = both[0][:2]
    block, width = left.shape[1] // 8, right.shape[1]
    low = jnp.bfloat16
    return pl.pallas_call(
        partial(product_kernel, count, outer),
        out_shape=[
            jax.ShapeDtypeStruct((2, count, block, width // 2), low),
            jax.ShapeDtypeStruct((2, count, block, width // 2), low),
            jax.ShapeDtypeStruct((2, count, block, width // 2), low),
            jax.ShapeDtypeStruct((count, block, width), low),
        ],
        in_specs=[pl.BlockSpec(memory_space=pltpu.SMEM)]
        + [pl.BlockSpec(memory_space=pltpu.VMEM)] * (4 * count),
        out_specs=[pl.BlockSpec(memory_space=pltpu.VMEM)] * 4,
        scratch_shapes=[
            pltpu.VMEM((2 * left.shape[0], width), low),
            pltpu.VMEM((4, block // outer, 2 * left.shape[0]), low),
        ],
        compiler_params=pltpu.CompilerParams(vmem_limit_bytes=44 << 20),
        cost_estimate=SMALL_COST,
    )((me & 7).reshape(1), *[part for parts in zip(*both, strict=True) for part in parts])


def low_sum(*parts):
    total = parts[0].astype(jnp.float32)
    for part in parts[1:]:
        total = total + part.astype(jnp.float32)
    return total.astype(jnp.bfloat16)


class RowSums:
    def __init__(self, to_x, to_y, later, own):
        self.sent, self.later, self.own = (to_x, to_y), later, own

    def first(self):
        return swap(self.sent[0], 1), swap(self.sent[1], 2)

    def last(self):
        return (
            swap(low_sum(self.later[0], self.met[0][0]), 2),
            swap(low_sum(self.later[1], self.met[1][0]), 1),
        )

    def total(self):
        half = self.own.shape[-1] // 2
        return jnp.concatenate(
            [
                low_sum(self.own[..., :half], self.met[0][1], self.last_met[0]),
                low_sum(self.own[..., half:], self.met[1][1], self.last_met[1]),
            ],
            axis=-1,
        )


def sum_group(total):
    outer = lax.axis_size("dp") // 8
    group = lax.axis_size("head")
    lead = total.shape[:-2]
    rows, columns = total.shape[-2:]
    if outer > 1:
        total = lax.psum_scatter(
            total.reshape(*lead, outer, rows // outer, columns),
            "dp",
            scatter_dimension=len(lead),
            tiled=True,
            axis_index_groups=outer_groups(),
        )
    total = total.reshape(*lead, rows // outer, columns)
    return lax.psum_scatter(total, "head", scatter_dimension=len(lead), tiled=True)


def sum_group_at_once(total):
    outer = lax.axis_size("dp") // 8
    group = lax.axis_size("head")
    if outer > 1:
        return sum_group(total).astype(jnp.float32)
    lead = total.shape[:-2]
    rows, columns = total.shape[-2:]
    total = total.reshape(*lead, group, rows // group, columns)
    axis = len(lead)
    met = lax.all_to_all(total, "head", split_axis=axis, concat_axis=axis, tiled=True)
    return jnp.sum(met.astype(jnp.float32), axis=axis)


def sum_columns(total):
    group = lax.axis_size("head")
    if lax.axis_size("dp") > 8:
        total = lax.psum(total, "dp", axis_index_groups=outer_groups())
    count, rows, columns = total.shape
    total = jnp.moveaxis(total.reshape(count, rows, group, columns // group), 2, 0)
    return lax.psum_scatter(total, "head", scatter_dimension=0, tiled=True)[0]


def gather_blocks(me, summed):
    outer = lax.axis_size("dp") // 8
    count, rows, columns = summed.shape
    if outer == 1:
        whole = lax.all_gather(summed, "dp", axis=0)
        return [whole[:, n].reshape(8 * rows, columns) for n in range(count)]
    held = summed.reshape(count * outer, rows // outer, columns)
    return place((me & 7).reshape(1), spread_rows(held), [columns])[0]


EXTRA_ROWS = 8


def entry_products(me, main, extra):
    group = lax.axis_size("head")
    outer = lax.axis_size("dp") // 8
    devices = 8 * outer * group
    columns = main.shape[1]
    own = main.shape[0] // devices
    extra = jnp.pad(extra, ((0, EXTRA_ROWS * devices - extra.shape[0]), (0, 0)))
    rows = jnp.concatenate(
        [main.reshape(devices, own, columns), extra.reshape(devices, EXTRA_ROWS, columns)], axis=1
    ).astype(jnp.bfloat16)
    view = rows.reshape(outer, 4, 2, group * (own + EXTRA_ROWS), columns)
    core = me & 1
    other = lax.dynamic_index_in_dim(view, 1 - core, 2, keepdims=False)
    pair = low_sum(lax.dynamic_index_in_dim(view, core, 2, keepdims=False), swap(other, 0))
    chip = (me & 7) >> 1
    half = columns // 2

    def picked(rel):
        return lax.dynamic_index_in_dim(pair, chip ^ rel, 1, keepdims=False).reshape(-1, columns)

    own_rows, at_x, at_y, far = (picked(rel) for rel in range(4))
    return RowSums(
        jnp.stack([far[:, :half], at_x[:, :half]]),
        jnp.stack([far[:, half:], at_y[:, half:]]),
        (at_y[:, :half], at_x[:, half:]),
        own_rows,
    )


def silu_parts(x):
    gate = 1.0 / (1.0 + jnp.exp(-x))
    return x * gate, gate * (1.0 + x * (1.0 - gate))


def output_kernel(
    plan, me_ref, top_ref, keep_ref, latent_offset, emit_offset, sensitivity, *refs
):
    pieces = refs[: len(plan)]
    hidden_ref, forecast_ref, pre_low_ref, grad_ref, bias_ref = refs[len(plan) : len(plan) + 5]
    whole, pre, skips, sent, both, sems = refs[len(plan) + 5 :]
    group, width, _ = whole.shape
    each = sensitivity.shape[2]
    two = 2 * each
    rows = width // 8
    copies = []
    for part in range(group):
        copies.append([])
        for n, (rel, row, count) in enumerate(plan):
            first = pl.multiple_of((me_ref[0] ^ rel) * rows + row, 16)
            spot = whole.at[part, pl.ds(first, count), :]
            sem = sems.at[part * len(plan) + n]
            copies[part].append(pltpu.make_async_copy(pieces[n].at[part], spot, sem))
            copies[part][n].start()
    top = top_ref[...]
    keep = keep_ref[...]
    for part in range(group):
        arrive(copies[part])
        both[...] = jnp.dot(top, whole[part, :, :two], preferred_element_type=jnp.float32)
        pre[:, part * each : (part + 1) * each] = both[:, :each] + latent_offset[part : part + 1]
        skips[part] = both[:, each:two] + emit_offset[part : part + 1]
    hidden, slope = silu_parts(pre[...])
    hidden = hidden.astype(jnp.bfloat16)
    hidden_ref[...] = hidden
    for part in range(group):
        emitted = jnp.dot(hidden, whole[part, :, two:], preferred_element_type=jnp.float32)
        forecast_ref[part] = ((emitted + skips[part]) * keep).astype(jnp.bfloat16)

    def back_hidden(n, _):
        at = pl.multiple_of(n * 256, 256)
        total = reverse_matmul_answer(whole[0, pl.ds(at, 256), two:], sensitivity[0])
        for part in range(1, group):
            total += reverse_matmul_answer(whole[part, pl.ds(at, 256), two:], sensitivity[part])
        grad_ref[:, pl.ds(at, 256)] = total.T
        return 0

    lax.fori_loop(0, width // 256, back_hidden, 0)
    pre[...] = grad_ref[...] * slope
    pre_low_ref[...] = pre[...].astype(jnp.bfloat16)
    bias_ref[...] = jnp.sum(pre_low_ref[...].astype(jnp.float32), axis=0, keepdims=True)
    for part in range(group):
        both[:, :each] = pre[:, part * each : (part + 1) * each]
        both[:, each:] = sensitivity[part].astype(jnp.float32)
        sent[part] = both[...].astype(jnp.bfloat16)

    def back_top(n, _):
        at = pl.multiple_of(n * 256, 256)
        total = reverse_matmul_answer(whole[0, pl.ds(at, 256), :two], sent[0])
        for part in range(1, group):
            total += reverse_matmul_answer(whole[part, pl.ds(at, 256), :two], sent[part])
        grad_ref[:, pl.ds(at, 256)] = total.T
        return 0

    lax.fori_loop(0, width // 256, back_top, 0)


def output_block(me, pieces, top, keep, latent_offsets, emit_offsets, grad_forecast):
    plan = [(rel, row, array.shape[1]) for rel, row, array in pieces]
    group, rows, each = grad_forecast.shape
    width = top.shape[1]
    vmem = pl.BlockSpec(memory_space=pltpu.VMEM)
    return pl.pallas_call(
        partial(output_kernel, plan),
        out_shape=[
            jax.ShapeDtypeStruct((rows, width), LOW),
            jax.ShapeDtypeStruct((group, rows, each), LOW),
            jax.ShapeDtypeStruct((rows, width), LOW),
            jax.ShapeDtypeStruct((rows, width), FULL),
            jax.ShapeDtypeStruct((1, width), FULL),
        ],
        in_specs=[pl.BlockSpec(memory_space=pltpu.SMEM)]
        + [vmem] * 5
        + [pl.BlockSpec(memory_space=pl.ANY)] * len(pieces),
        out_specs=[vmem] * 5,
        scratch_shapes=[
            pltpu.VMEM((group, width, 3 * each), LOW),
            pltpu.VMEM((rows, width), FULL),
            pltpu.VMEM((group, rows, each), FULL),
            pltpu.VMEM((group, rows, 2 * each), LOW),
            pltpu.VMEM((rows, 2 * each), FULL),
            pltpu.SemaphoreType.DMA((group * len(pieces),)),
        ],
        compiler_params=pltpu.CompilerParams(vmem_limit_bytes=44 << 20),
        cost_estimate=SMALL_COST,
    )(
        me,
        top,
        keep,
        latent_offsets,
        emit_offsets,
        grad_forecast,
        *[array for _, _, array in pieces],
    )


def output_plain(head_whole, top, keep, latent_offsets, emit_offsets, grad_forecast):
    group, _, each = grad_forecast.shape
    two = 2 * each
    inner_parts = [
        jnp.dot(top, head_whole[part][:, :two], preferred_element_type=jnp.float32)
        for part in range(group)
    ]
    head_pre = jnp.concatenate(
        [inner_parts[part][:, :each] + latent_offsets[part] for part in range(group)], axis=1
    )
    hidden, slope = silu_parts(head_pre)
    hidden = hidden.astype(jnp.bfloat16)
    forecast = jnp.stack(
        [
            (
                jnp.dot(hidden, head_whole[part][:, two:], preferred_element_type=jnp.float32)
                + emit_offsets[part]
                + inner_parts[part][:, each:]
            )
            * keep
            for part in range(group)
        ]
    ).astype(jnp.bfloat16)
    grad_hidden = sum(
        reverse_matmul_answer(grad_forecast[part], head_whole[part][:, two:])
        for part in range(group)
    )
    pre_low = (grad_hidden * slope).astype(jnp.bfloat16)
    grad_top = sum(
        reverse_matmul_answer(
            jnp.concatenate(
                [pre_low[:, part * each : (part + 1) * each], grad_forecast[part]], axis=1
            ),
            head_whole[part][:, :two],
        )
        for part in range(group)
    )
    return hidden, forecast, pre_low, grad_top, jnp.sum(pre_low.astype(FULL), axis=0, keepdims=True)


def input_back_kernel(
    grad_ref, pre_ref, emit_ref, latent_ref, shortcut_ref, low_ref, pre_low_ref, sent_ref, bias_ref, wide
):
    low = grad_ref[...].astype(jnp.bfloat16)
    low_ref[...] = low
    rows_times_turned(low, emit_ref, 0, emit_ref.shape[1], wide, 256)
    pre = pre_ref[...]
    gate = 1.0 / (1.0 + jnp.exp(-pre))
    pre_low = (wide[...] * (gate * (1.0 + pre * (1.0 - gate)))).astype(jnp.bfloat16)
    pre_low_ref[...] = pre_low
    sent_ref[...] = reverse_matmul_answer(pre_low, latent_ref[...]) + reverse_matmul_answer(
        low, shortcut_ref[...]
    )
    bias_ref[0:1] = jnp.sum(pre_low.astype(jnp.float32), axis=0, keepdims=True)
    bias_ref[1:2] = jnp.sum(low.astype(jnp.float32), axis=0, keepdims=True)


def input_products_kernel(group, me_ref, *refs):
    hidden, met_hidden, low, met_low, pre_low, met_pre_low, features, met_features = refs[:8]
    vectors, met_vectors, to_x, to_y, later, own = refs[8:14]
    turned, low_pair, extras, block = refs[14:]
    tokens = hidden.shape[0]
    columns = low.shape[1]
    half = columns // 2
    core, chip = me_ref[0] & 1, me_ref[0] >> 1
    turned[:, :tokens] = hidden[...].astype(jnp.float32).T.astype(jnp.bfloat16)
    turned[:, tokens:] = met_hidden[...].astype(jnp.float32).T.astype(jnp.bfloat16)
    low_pair[:tokens] = low[...]
    low_pair[tokens:] = met_low[...]
    wide = features.shape[1]
    extras[...] = jnp.zeros_like(extras)
    extras[:wide] = dyadic_accumulation(features[...], pre_low[...]) + dyadic_accumulation(
        met_features[...], met_pre_low[...]
    )
    extras[wide : 2 * wide] = dyadic_accumulation(features[...], low[...]) + dyadic_accumulation(
        met_features[...], met_low[...]
    )
    extras[2 * wide : 2 * wide + vectors.shape[0]] = vectors[...] + met_vectors[...]
    rows = hidden.shape[1] // 8
    each = rows // group
    span = each + EXTRA_ROWS

    def store(rel, total):
        if rel == 0:
            own[0] = total
        elif rel == 1:
            to_x[1, 0] = total[:, :half]
            later[1, 0] = total[:, half:]
        elif rel == 2:
            later[0, 0] = total[:, :half]
            to_y[1, 0] = total[:, half:]
        else:
            to_x[0, 0] = total[:, :half]
            to_y[0, 0] = total[:, half:]

    for place in range(4):
        number = 2 * place + core
        first = pl.multiple_of(number * rows, rows)
        outer = jnp.dot(
            turned[pl.ds(first, rows), :], low_pair[...], preferred_element_type=jnp.float32
        )
        first = pl.multiple_of(number * group * EXTRA_ROWS, group * EXTRA_ROWS)
        extra = extras[pl.ds(first, group * EXTRA_ROWS), :]
        for member in range(group):
            block[member * span : member * span + each] = outer[member * each : (member + 1) * each]
            block[member * span + each : (member + 1) * span] = extra[
                member * EXTRA_ROWS : (member + 1) * EXTRA_ROWS
            ]
        total = block[...].astype(own.dtype)
        for rel in range(4):
            pl.when(chip ^ place == rel)(partial(store, rel, total))


def input_back(grad, pre, emit, latent, shortcut):
    rows, columns = grad.shape
    vmem = pl.BlockSpec(memory_space=pltpu.VMEM)
    return pl.pallas_call(
        input_back_kernel,
        out_shape=[
            jax.ShapeDtypeStruct((rows, columns), LOW),
            jax.ShapeDtypeStruct((rows, columns), LOW),
            jax.ShapeDtypeStruct((rows, latent.shape[0]), FULL),
            jax.ShapeDtypeStruct((2, columns), FULL),
        ],
        in_specs=[vmem] * 5,
        out_specs=[vmem] * 4,
        scratch_shapes=[pltpu.VMEM((rows, columns), FULL)],
        compiler_params=pltpu.CompilerParams(vmem_limit_bytes=32 << 20),
        cost_estimate=SMALL_COST,
    )(grad, pre, emit, latent, shortcut)


def input_products(me, operands):
    group = lax.axis_size("head")
    tokens, columns = operands[2].shape
    width = operands[0].shape[1]
    block = width // 8 + group * EXTRA_ROWS
    pair = jax.ShapeDtypeStruct((2, 1, block, columns // 2), LOW)
    return RowSums(
        *pl.pallas_call(
            partial(input_products_kernel, group),
            out_shape=[pair, pair, pair, jax.ShapeDtypeStruct((1, block, columns), LOW)],
            in_specs=[pl.BlockSpec(memory_space=pltpu.SMEM)]
            + [pl.BlockSpec(memory_space=pltpu.VMEM)] * len(operands),
            out_specs=[pl.BlockSpec(memory_space=pltpu.VMEM)] * 4,
            scratch_shapes=[
                pltpu.VMEM((width, 2 * tokens), LOW),
                pltpu.VMEM((2 * tokens, columns), LOW),
                pltpu.VMEM((8 * group * EXTRA_ROWS, columns), FULL),
                pltpu.VMEM((block, columns), FULL),
            ],
            compiler_params=pltpu.CompilerParams(vmem_limit_bytes=32 << 20),
            cost_estimate=SMALL_COST,
        )((me & 7).reshape(1), *operands)
    )


def entry_kernel(plan, own, me_ref, *refs):
    pieces = refs[: len(plan)]
    main_ref, extra_ref, held, sems = refs[len(plan) :]
    copies = []
    for n, (rel, row, rows) in enumerate(plan):
        spot = held.at[me_ref[0] ^ rel, pl.ds(row, rows)]
        copies.append(pltpu.make_async_copy(pieces[n].at[0], spot, sems.at[n]))
    for copy in copies:
        copy.start()
    for copy in copies:
        copy.wait()
    span = own + EXTRA_ROWS
    group = held.shape[1] // span
    for block in range(8):
        rows = held[block].astype(jnp.float32)
        for member in range(group):
            main_ref[block * group + member] = rows[member * span : member * span + own]
            extra_ref[block * group + member] = rows[member * span + own : (member + 1) * span]


def entry_sums_of_group(total):
    total = total.reshape(-1, total.shape[-1])
    return sum_group_at_once(total).astype(total.dtype)


def entry_everywhere(me, summed, own, count):
    columns = summed.shape[-1]
    group = lax.axis_size("head")
    if lax.axis_size("dp") > 8:
        held = gather_head(summed)
    else:
        every = jnp.broadcast_to(summed[None], (group, *summed.shape))
        held = lax.all_to_all(every, "head", split_axis=0, concat_axis=0, tiled=True)
        held = held.reshape(1, -1, columns)
    pieces = spread_rows(held)
    places = (me & 7).reshape(1)
    span = own + EXTRA_ROWS
    if held.shape[0] > 1 or own % 8 or not in_kernel(pieces):
        (whole,) = place(places, pieces, [columns])
        whole = whole.reshape(-1, span, columns).astype(jnp.float32)
        return whole[:, :own].reshape(-1, columns), whole[:, own:].reshape(-1, columns)[:count], held
    rows = held.shape[1]
    blocks = 8 * rows // span
    plan = [(rel, row, array.shape[1]) for rel, row, array in pieces]
    vmem = pl.BlockSpec(memory_space=pltpu.VMEM)
    main, extra = pl.pallas_call(
        partial(entry_kernel, plan, own),
        out_shape=[
            jax.ShapeDtypeStruct((blocks, own, columns), jnp.float32),
            jax.ShapeDtypeStruct((blocks, EXTRA_ROWS, columns), jnp.float32),
        ],
        in_specs=[pl.BlockSpec(memory_space=pltpu.SMEM)]
        + [pl.BlockSpec(memory_space=pl.ANY)] * len(pieces),
        out_specs=[vmem, vmem],
        scratch_shapes=[
            pltpu.VMEM((8, rows, columns), held.dtype),
            pltpu.SemaphoreType.DMA((len(pieces),)),
        ],
        compiler_params=pltpu.CompilerParams(vmem_limit_bytes=44 << 20),
        cost_estimate=SMALL_COST,
    )(places, *[array for _, _, array in pieces])
    return main.reshape(-1, columns), extra.reshape(-1, columns)[:count], held


def fetch(plan, me, pieces, whole, sems):
    groups = []
    for group in range(whole.shape[1] // MODEL_WIDTH):
        columns = pl.ds(group * MODEL_WIDTH, MODEL_WIDTH)
        copies = []
        for n, (rel, row, rows) in enumerate(plan):
            first = pl.multiple_of((me ^ rel) * (whole.shape[0] // 8) + row, 16)
            copies.append(
                pltpu.make_async_copy(
                    pieces[n].at[0, :, columns],
                    whole.at[pl.ds(first, rows), columns],
                    sems.at[group * len(plan) + n],
                )
            )
        for copy in copies:
            copy.start()
        groups.append(copies)
    return groups


def arrive(copies):
    for copy in copies:
        copy.wait()


def rows_times(left, whole, first, out, tile):
    def step(n, _):
        at = pl.multiple_of(n * tile, 128)
        out[:, pl.ds(at, tile)] = jnp.dot(
            left, whole[:, pl.ds(first + at, tile)], preferred_element_type=jnp.float32
        )
        return 0

    lax.fori_loop(0, out.shape[1] // tile, step, 0)


def rows_times_turned(left, whole, first, width, out, tile):
    def step(n, _):
        at = pl.multiple_of(n * tile, 128)
        part = reverse_matmul_answer(whole[pl.ds(at, tile), pl.ds(first, width)], left)
        out[:, pl.ds(at, tile)] = part.T
        return 0

    lax.fori_loop(0, out.shape[1] // tile, step, 0)


def inverse_norm(rows):
    return lax.rsqrt(jnp.mean(rows * rows, axis=-1, keepdims=True) + EPS)


def other_half(rows):
    half = HEAD_DIM // 2
    lane = lax.broadcasted_iota(jnp.int32, rows.shape, 1) % HEAD_DIM
    ahead = pltpu.roll(rows, rows.shape[1] - half, 1)
    behind = pltpu.roll(rows, half, 1)
    return jnp.where(lane < half, ahead, behind)


def head_window(head, width):
    first = head * HEAD_DIM // 128 * 128
    last = min(-(-(head + 1) * HEAD_DIM // 128) * 128, width)
    start = head * HEAD_DIM - first
    lane = lax.broadcasted_iota(jnp.int32, (1, last - first), 1)
    return slice(first, last), jnp.logical_and(lane >= start, lane < start + HEAD_DIM)


def entry_forward_kernel(plan, me_ref, resid_ref, gain_ref, cosine_ref, sine_ref, allowed_ref, *refs):
    pieces = refs[: len(plan)]
    normed_ref, query_ref, key_ref, value_ref, total_ref, mixed_ref = refs[len(plan) : len(plan) + 6]
    whole, wide, sems = refs[len(plan) + 6 :]
    groups = fetch(plan, me_ref[0], pieces, whole, sems)
    resid = resid_ref[...]
    normed = (resid * inverse_norm(resid) * gain_ref[...]).astype(jnp.bfloat16)
    normed_ref[...] = normed
    for group, out in enumerate((query_ref, key_ref, value_ref)):
        arrive(groups[group])
        rows_times(normed, whole, group * MODEL_WIDTH, wide, 256)
        rows = wide[...]
        if group < 2:
            rows = rows * cosine_ref[...] + other_half(rows) * sine_ref[...]
        out[...] = rows.astype(jnp.bfloat16)
    scale = 1.0 / math.sqrt(HEAD_DIM)
    allowed = allowed_ref[...] > 0.0
    wide[...] = jnp.zeros_like(wide)
    totals = jnp.zeros(total_ref.shape, jnp.float32)
    head_lane = lax.broadcasted_iota(jnp.int32, total_ref.shape, 1)
    for head in range(HEADS):
        window, inside = head_window(head, MODEL_WIDTH)
        query = jnp.where(inside, query_ref[:, window], 0)
        scores = reverse_matmul_answer(query, key_ref[:, window]) * scale
        scores = jnp.where(allowed, scores, -1e30)
        peak = jnp.max(scores, axis=-1, keepdims=True)
        weights = jnp.exp(scores - peak)
        total = jnp.sum(weights, axis=-1, keepdims=True)
        probs = (weights / total).astype(jnp.bfloat16)
        mixed = jnp.dot(probs, value_ref[:, window], preferred_element_type=jnp.float32)
        wide[:, window] += jnp.where(inside, mixed, 0.0)
        totals = jnp.where(head_lane == head, peak + jnp.log(total), totals)
    total_ref[...] = totals
    mixed_ref[...] = wide[...].astype(jnp.bfloat16)


def gelu_parts(x):
    root = math.sqrt(2.0 / math.pi)
    bend = jnp.tanh(root * (x + 0.044715 * (x * x * x)))
    slope = 0.5 * (1.0 + bend) + 0.5 * x * (1.0 - bend * bend) * root * (
        1.0 + 3.0 * 0.044715 * (x * x)
    )
    return 0.5 * x * (1.0 + bend), slope


def rest_forward_kernel(plan, me_ref, resid_ref, mixed_ref, gain_ref, *refs):
    pieces = refs[: len(plan)]
    result_ref, middle_ref, normed_ref, pre_ref = refs[len(plan) : len(plan) + 4]
    whole, sems = refs[len(plan) + 4 :]
    groups = fetch(plan, me_ref[0], pieces, whole, sems)
    arrive(groups[0])
    rows_times(mixed_ref[...], whole, 0, middle_ref, 256)
    middle = resid_ref[...] + middle_ref[...]
    middle_ref[...] = middle
    normed = (middle * inverse_norm(middle) * gain_ref[...]).astype(jnp.bfloat16)
    normed_ref[...] = normed
    arrive(groups[1])
    rows_times(normed, whole, MODEL_WIDTH, pre_ref, 256)
    act = gelu_parts(pre_ref[...])[0].astype(jnp.bfloat16)
    arrive(groups[2])
    rows_times(act, whole, 2 * MODEL_WIDTH, result_ref, 256)
    result_ref[...] += middle_ref[...]


def norm_back(rows, gain, grad):
    inverse = inverse_norm(rows)
    scaled = grad * gain
    mean = jnp.mean(rows * scaled, axis=-1, keepdims=True)
    sent = inverse * scaled - rows * (inverse * inverse * inverse * mean)
    return sent, jnp.sum(grad * rows * inverse, axis=0, keepdims=True)


def rest_backward_kernel(plan, me_ref, grad_ref, middle_ref, pre_ref, gain_ref, *refs):
    pieces = refs[: len(plan)]
    outs = refs[len(plan) : len(plan) + 7]
    grad_middle_ref, mixed_ref, attn_ref, grad_pre_ref, branch_ref, act_ref, gain_grad_ref = outs
    whole, wide, sems = refs[len(plan) + 7 :]
    groups = fetch(plan, me_ref[0], pieces, whole, sems)
    grad = grad_ref[...]
    branch = grad.astype(jnp.bfloat16)
    branch_ref[...] = branch
    arrive(groups[2])
    rows_times_turned(branch, whole, 2 * MODEL_WIDTH, MODEL_WIDTH, wide, 256)
    act, slope = gelu_parts(pre_ref[...])
    act_ref[...] = act.astype(jnp.bfloat16)
    grad_pre = (wide[...] * slope).astype(jnp.bfloat16)
    grad_pre_ref[...] = grad_pre
    arrive(groups[1])
    rows_times_turned(grad_pre, whole, MODEL_WIDTH, MODEL_WIDTH, wide, 256)
    sent, gain_grad_ref[...] = norm_back(middle_ref[...], gain_ref[...], wide[...])
    grad_middle = grad + sent
    grad_middle_ref[...] = grad_middle
    attn = grad_middle.astype(jnp.bfloat16)
    attn_ref[...] = attn
    arrive(groups[0])
    rows_times_turned(attn, whole, 0, MODEL_WIDTH, wide, 256)
    mixed_ref[...] = wide[...].astype(jnp.bfloat16)


def entry_backward_kernel(
    plan,
    me_ref,
    grad_middle_ref,
    grad_mixed_ref,
    resid_ref,
    query_ref,
    key_ref,
    value_ref,
    total_ref,
    gain_ref,
    cosine_ref,
    sine_ref,
    allowed_ref,
    *refs,
):
    pieces = refs[: len(plan)]
    grad_resid_ref, projected_ref, gain_grad_ref = refs[len(plan) : len(plan) + 3]
    whole, grad_query, grad_key, grad_value, sems = refs[len(plan) + 3 :]
    groups = fetch(plan, me_ref[0], pieces, whole, sems)
    scale = 1.0 / math.sqrt(HEAD_DIM)
    allowed = allowed_ref[...] > 0.0
    totals = total_ref[...]
    grad_query[...] = jnp.zeros_like(grad_query)
    grad_key[...] = jnp.zeros_like(grad_key)
    grad_value[...] = jnp.zeros_like(grad_value)
    for head in range(HEADS):
        window, inside = head_window(head, MODEL_WIDTH)
        query = jnp.where(inside, query_ref[:, window], 0)
        keys = key_ref[:, window]
        grad_mixed = jnp.where(inside, grad_mixed_ref[:, window], 0)
        scores = reverse_matmul_answer(query, keys) * scale
        probs = jnp.where(allowed, jnp.exp(scores - totals[:, head : head + 1]), 0.0)
        grad_probs = reverse_matmul_answer(grad_mixed, value_ref[:, window])
        grad_value[:, window] += dyadic_accumulation(probs.astype(jnp.bfloat16), grad_mixed)
        center = jnp.sum(grad_probs * probs, axis=-1, keepdims=True)
        grad_scores = (probs * (grad_probs - center)).astype(jnp.bfloat16)
        along = jnp.dot(grad_scores, keys, preferred_element_type=jnp.float32)
        grad_query[:, window] += jnp.where(inside, along * scale, 0.0)
        grad_key[:, window] += dyadic_accumulation(grad_scores, query) * scale
    for group, part in enumerate((grad_query, grad_key, grad_value)):
        rows = part[...]
        if group < 2:
            rows = rows * cosine_ref[...] - other_half(rows) * sine_ref[...]
        projected_ref[:, group * MODEL_WIDTH : (group + 1) * MODEL_WIDTH] = rows.astype(jnp.bfloat16)
    for copies in groups:
        arrive(copies)
    rows_times_turned(projected_ref[...], whole, 0, 3 * MODEL_WIDTH, grad_query, 256)
    sent, gain_grad_ref[...] = norm_back(resid_ref[...], gain_ref[...], grad_query[...])
    grad_resid_ref[...] = grad_middle_ref[...] + sent


def whole_call(kernel, me, pieces, inputs, outs, wides):
    rows = inputs[0].shape[0]
    plan = [(rel, row, array.shape[1]) for rel, row, array in pieces]
    blocks = 8 * pieces[0][2].shape[1]
    columns = 3 * MODEL_WIDTH
    vmem = pl.BlockSpec(memory_space=pltpu.VMEM)
    return pl.pallas_call(
        partial(kernel, plan),
        out_shape=[jax.ShapeDtypeStruct(shape, kind) for shape, kind in outs],
        in_specs=[pl.BlockSpec(memory_space=pltpu.SMEM)]
        + [vmem] * len(inputs)
        + [pl.BlockSpec(memory_space=pl.ANY)] * len(pieces),
        out_specs=[vmem] * len(outs),
        scratch_shapes=[pltpu.VMEM((blocks, columns), jnp.bfloat16)]
        + [pltpu.VMEM((rows, MODEL_WIDTH), jnp.float32)] * wides
        + [pltpu.SemaphoreType.DMA((3 * len(pieces),))],
        compiler_params=pltpu.CompilerParams(vmem_limit_bytes=44 << 20),
        cost_estimate=SMALL_COST,
    )(me, *inputs, *[array for _, _, array in pieces])


def in_kernel(pieces):
    lead, rows, _ = pieces[0][2].shape
    return lead == 1 and rows % 32 == 0


LOW, FULL = jnp.bfloat16, jnp.float32


class Layer:
    def __init__(self, places, entry_pieces, gains, tables, allowed):
        self.places, self.entry_pieces, self.gains = places, entry_pieces, gains
        self.tables, self.allowed = tables, allowed
        self.fetched = in_kernel(entry_pieces)
        if not self.fetched:
            self.entry_whole = place(places, entry_pieces, [3 * MODEL_WIDTH])[0][0]

    def add_rest(self, rest_pieces):
        self.rest_pieces = rest_pieces
        if not self.fetched:
            self.rest_whole = [part[0] for part in place(self.places, rest_pieces, [MODEL_WIDTH] * 3)]

    def shapes(self, *kinds):
        rows = self.allowed.shape[0]
        return [((rows, width), kind) for width, kind in kinds]

    def entry_forward(self, resid):
        if not self.fetched:
            self.saved = entry_forward(
                resid, self.entry_whole, self.gains, *self.tables[:2], self.allowed
            )
            return self.saved[6]
        wide = (MODEL_WIDTH, LOW)
        self.resid = resid
        outs = whole_call(
            entry_forward_kernel,
            self.places,
            self.entry_pieces,
            (resid, self.gains[:1].astype(FULL), *self.tables[2:], self.allowed.astype(FULL)),
            self.shapes(wide, wide, wide, wide, (128, FULL), wide),
            1,
        )
        self.normed_first, self.heads = outs[0], outs[1:5]
        return outs[5]

    def rest_forward(self, mixed):
        if not self.fetched:
            result, self.saved = rest_forward(
                (*self.saved[:6], mixed), *self.rest_whole, self.gains
            )
            return result
        self.mixed = mixed
        result, self.middle, self.normed_second, self.hidden_pre = whole_call(
            rest_forward_kernel,
            self.places,
            self.rest_pieces,
            (self.resid, mixed, self.gains[1:].astype(FULL)),
            self.shapes(
                (MODEL_WIDTH, FULL), (MODEL_WIDTH, FULL), (MODEL_WIDTH, LOW), (MODEL_WIDTH, FULL)
            ),
            0,
        )
        return result

    def rest_backward(self, grad):
        if not self.fetched:
            weights = (self.entry_whole, *self.rest_whole, self.gains)
            return rest_backward(self.saved, weights, grad)
        wide = (MODEL_WIDTH, LOW)
        grad_middle, grad_mixed, grad_attn, grad_pre, branch, act, gain_grad = whole_call(
            rest_backward_kernel,
            self.places,
            self.rest_pieces,
            (grad, self.middle, self.hidden_pre, self.gains[1:].astype(FULL)),
            self.shapes((MODEL_WIDTH, FULL), wide, wide, wide, wide, wide)
            + [((1, MODEL_WIDTH), FULL)],
            1,
        )
        lefts = (self.mixed, self.normed_second, act)
        return grad_middle, grad_mixed, lefts, (grad_attn, grad_pre, branch), gain_grad[0]

    def entry_backward(self, grad_middle, grad_mixed):
        if not self.fetched:
            weights = (self.entry_whole, *self.rest_whole, self.gains)
            return entry_backward(
                self.saved, weights, *self.tables[:2], self.allowed, grad_middle, grad_mixed
            )
        grad_resid, projected, gain_grad = whole_call(
            entry_backward_kernel,
            self.places,
            self.entry_pieces,
            (
                grad_middle,
                grad_mixed,
                self.resid,
                *self.heads,
                self.gains[:1].astype(FULL),
                *self.tables[2:],
                self.allowed.astype(FULL),
            ),
            self.shapes((MODEL_WIDTH, FULL), (3 * MODEL_WIDTH, LOW)) + [((1, MODEL_WIDTH), FULL)],
            3,
        )
        return grad_resid, self.normed_first, projected, gain_grad[0]


def entry_forward(resid, qkv_full, gain_pair, cosine, sine, allowed):
    gains = gain_pair.astype(jnp.float32)
    rows = resid.shape[0]
    normed_first = norm_apply(resid, gains[0]).astype(jnp.bfloat16)
    projected = jnp.dot(normed_first, qkv_full, preferred_element_type=jnp.float32)
    query_rows = rotate(
        projected[:, :MODEL_WIDTH].reshape(rows, HEADS, HEAD_DIM), cosine, sine
    ).astype(jnp.bfloat16)
    key_rows = rotate(
        projected[:, MODEL_WIDTH : 2 * MODEL_WIDTH].reshape(rows, HEADS, HEAD_DIM), cosine, sine
    ).astype(jnp.bfloat16)
    value_rows = projected[:, 2 * MODEL_WIDTH :].reshape(rows, HEADS, HEAD_DIM).astype(jnp.bfloat16)

    mixed, log_total = attend_forward(query_rows, key_rows, value_rows, allowed)
    mixed_low = mixed.reshape(rows, MODEL_WIDTH).astype(jnp.bfloat16)
    return (resid, normed_first, query_rows, key_rows, value_rows, log_total, mixed_low)


def rest_forward(saved, out_full, up_full, down_full, gain_pair):
    gains = gain_pair.astype(jnp.float32)
    resid, mixed_low = saved[0], saved[6]
    middle = resid + jnp.dot(mixed_low, out_full, preferred_element_type=jnp.float32)
    normed_second = norm_apply(middle, gains[1]).astype(jnp.bfloat16)
    hidden_pre = jnp.dot(normed_second, up_full, preferred_element_type=jnp.float32)
    hidden_act = jax.nn.gelu(hidden_pre, approximate=True).astype(jnp.bfloat16)
    result = middle + jnp.dot(hidden_act, down_full, preferred_element_type=jnp.float32)
    return (result, (*saved, middle, normed_second, hidden_pre))


def rest_backward(saved, weights, grad_result):
    mixed_low, middle, normed_second, hidden_pre = saved[6:]
    _, out_full, up_full, down_full, gain_pair = weights
    gains = gain_pair.astype(jnp.float32)
    grad_branch = grad_result.astype(jnp.bfloat16)
    hidden_act, gelu_pull = jax.vjp(partial(jax.nn.gelu, approximate=True), hidden_pre)
    hidden_low = hidden_act.astype(jnp.bfloat16)
    grad_act = reverse_matmul_answer(grad_branch, down_full)
    grad_pre = gelu_pull(grad_act)[0].astype(jnp.bfloat16)
    grad_normed_second = reverse_matmul_answer(grad_pre, up_full)
    unused_second, second_pull = jax.vjp(norm_apply, middle, gains[1])
    grad_middle_norm, grad_gain_second = second_pull(grad_normed_second)
    grad_middle = grad_result + grad_middle_norm
    grad_attn = grad_middle.astype(jnp.bfloat16)
    grad_mixed = reverse_matmul_answer(grad_attn, out_full).astype(jnp.bfloat16)
    left_rows = (mixed_low, normed_second, hidden_low)
    right_rows = (grad_attn, grad_pre, grad_branch)
    return (grad_middle, grad_mixed, left_rows, right_rows, grad_gain_second)


def entry_backward(saved, weights, cosine, sine, allowed, grad_middle, grad_mixed):
    resid, normed_first, query_rows, key_rows, value_rows, log_total = saved[:6]
    qkv_full = weights[0]
    gains = weights[4].astype(jnp.float32)
    rows = resid.shape[0]
    grad_query, grad_keys, grad_values = attend_backward(
        query_rows,
        key_rows,
        value_rows,
        allowed,
        log_total,
        grad_mixed.reshape(rows, HEADS, HEAD_DIM),
    )
    grad_query = unrotate(grad_query, cosine, sine).reshape(rows, MODEL_WIDTH)
    grad_keys = unrotate(grad_keys, cosine, sine).reshape(rows, MODEL_WIDTH)
    grad_values = grad_values.reshape(rows, MODEL_WIDTH)
    grad_projected = jnp.concatenate([grad_query, grad_keys, grad_values], axis=1).astype(
        jnp.bfloat16
    )
    grad_normed_first = reverse_matmul_answer(grad_projected, qkv_full)
    unused_first, first_pull = jax.vjp(norm_apply, resid, gains[0])
    grad_resid_norm, grad_gain_first = first_pull(grad_normed_first)
    return (grad_middle + grad_resid_norm, normed_first, grad_projected, grad_gain_first)


def body(
    patch_observations,
    sequence_labels,
    leading_filler_count,
    intake_latent_matrix,
    intake_latent_offset,
    intake_emit_matrix,
    intake_emit_offset,
    intake_shortcut_matrix,
    attention_entry_matrices,
    attention_merge_matrix,
    feedforward_widen_matrix,
    feedforward_shrink_matrix,
    layer_scale_factors,
    readout_latent_matrix,
    readout_latent_offset,
    readout_emit_matrix,
    readout_emit_offset,
    readout_shortcut_matrix,
    loss_sensitivity,
):
    patch_len = patch_observations.shape[1]
    position, pad_count, allowed, keep_rows = layout_rows(
        sequence_labels[0], leading_filler_count[0], patch_len
    )
    cosine, sine = rotary_tables(position, HEAD_DIM)
    columns = jnp.arange(patch_len, dtype=jnp.int32)
    pad_mask = columns[None, :] < pad_count[:, None]
    features = jnp.concatenate(
        [
            jnp.where(pad_mask, jnp.zeros_like(patch_observations), patch_observations),
            pad_mask.astype(jnp.bfloat16),
        ],
        axis=1,
    )
    entry_pre = (
        jnp.dot(features, intake_latent_matrix, preferred_element_type=jnp.float32)
        + intake_latent_offset
    )
    entry_hidden = jax.nn.silu(entry_pre).astype(jnp.bfloat16)
    resid = (
        jnp.dot(entry_hidden, intake_emit_matrix, preferred_element_type=jnp.float32)
        + intake_emit_offset
        + jnp.dot(features, intake_shortcut_matrix, preferred_element_type=jnp.float32)
    )
    layer_count = attention_entry_matrices.shape[0]
    group = lax.axis_size("head")
    group_place = lax.axis_index("head")
    outer = lax.axis_size("dp") // 8
    me = lax.axis_index("dp").astype(jnp.int32)
    places = (me & 7).reshape(1)
    own_count = layer_scale_factors.shape[2]
    rows = patch_observations.shape[0]

    group_width = readout_latent_offset.shape[0]
    offsets = jnp.stack([readout_latent_offset, readout_emit_offset])
    coarse = lax.reduce_precision(offsets, 8, 7)
    offset_rows = jnp.concatenate([coarse, offsets - coarse], axis=0).astype(jnp.bfloat16)
    offset_rows = jnp.pad(offset_rows, ((0, 12), (0, 0)))
    sent = jnp.concatenate(
        [
            loss_sensitivity.reshape(group, rows, group_width),
            jnp.broadcast_to(offset_rows[None], (group, 16, group_width)),
        ],
        axis=1,
    )
    gain_columns = layer_scale_factors.reshape(2 * layer_count, own_count).T
    gain_columns = jnp.pad(gain_columns, ((0, 0), (0, 128 - 2 * layer_count)))
    chunks = []
    for layer_index in range(layer_count):
        entry_own = attention_entry_matrices[layer_index]
        if layer_index == 0:
            entry_own = jnp.concatenate([entry_own, gain_columns], axis=1)
        chunks.append(entry_own)
        rest_own = jnp.concatenate(
            [
                attention_merge_matrix[layer_index],
                feedforward_widen_matrix[layer_index],
                feedforward_shrink_matrix[layer_index],
            ],
            axis=1,
        )
        chunks.append(rest_own)
    head_own = jnp.concatenate(
        [
            lax.dynamic_index_in_dim(
                matrix.reshape(outer, 8, -1, group_width), me % 8, 1, keepdims=False
            )
            for matrix in (readout_latent_matrix, readout_shortcut_matrix, readout_emit_matrix)
        ],
        axis=2,
    )
    chunks.append(head_own)
    count = len(chunks)

    def gather_chunk(number, own):
        if number < count - 1:
            return gather_head(own)
        return lax.all_gather(own, "head", axis=0, tiled=True)

    held = gather_chunk(0, chunks[0])
    cosine_wide = jnp.tile(jnp.concatenate([cosine[:, 0], cosine[:, 0]], axis=1), (1, HEADS))
    sine_wide = jnp.tile(jnp.concatenate([-sine[:, 0], sine[:, 0]], axis=1), (1, HEADS))
    tables = (cosine, sine, cosine_wide, sine_wide)
    nears, fars, near_mets = [], [], []
    layers = []
    onward = None
    for number in range(count + 1):
        step = {}
        if number < count:
            step["x"], step["y"] = swap(held, 1), swap(held, 2)
        if number + 1 < count:
            step["next"] = gather_chunk(number + 1, chunks[number + 1])
        if number == count - 1:
            step["met"] = lax.all_to_all(
                after(sent, held), "head", split_axis=0, concat_axis=0, tiled=True
            )
        if number == 0:
            step["resid"] = resid
        else:
            step["far"] = (swap(onward[0], 1), swap(onward[1], 2))
            near_mets.append([swap(part, 0) for part in after(nears[number - 1], onward)])
        if number > 1:
            chunk = number - 2
            far_met = [swap(part, 0) for part in after(fars[chunk], onward)]
            pieces = all_pieces(nears[chunk], fars[chunk], near_mets[chunk], far_met)
            if chunk == 0:
                gain_rows = place(places, pieces, [128], 3 * MODEL_WIDTH)[0][0]
                gain_rows = gain_rows[:, : 2 * layer_count].T.reshape(layer_count, 2, -1)
            if chunk % 2 == 0:
                layers.append(Layer(places, pieces, gain_rows[chunk // 2], tables, allowed))
                step["mixed"] = layers[-1].entry_forward(resid)
            else:
                layers[-1].add_rest(pieces)
                step["resid"] = layers[-1].rest_forward(mixed)
        step["own"] = chunks[number + 2 :]
        step = lax.optimization_barrier(step)
        chunks[number + 2 :] = step["own"]
        if number < count:
            nears.append((held, step["x"], step["y"]))
            onward = second_step(*nears[-1])
        held = step.get("next")
        if number > 0:
            fars.append(step["far"])
        resid = step.get("resid", resid)
        mixed = step.get("mixed")
        if "met" in step:
            met = step["met"]
    head_far_met = [swap(part, 0) for part in fars[-1]]
    head_pieces = all_pieces(nears[-1], fars[-1], near_mets[-1], head_far_met)
    sensitivity = met[:, :rows]
    head_offsets = met[:, rows : rows + 4].astype(jnp.float32)
    latent_offsets = head_offsets[:, 0] + head_offsets[:, 2]
    emit_offsets = head_offsets[:, 1] + head_offsets[:, 3]

    top = resid.astype(jnp.bfloat16)
    keep_column = keep_rows[:, None]
    grad_forecast = (sensitivity.astype(jnp.float32) * keep_column).astype(jnp.bfloat16)
    grad_forecast_rows = jnp.concatenate([grad_forecast[part] for part in range(group)], axis=1)
    head_inputs = (top, keep_column, latent_offsets, emit_offsets, grad_forecast)
    if layers[0].fetched:
        outs = output_block(places, head_pieces, *head_inputs)
    else:
        head_whole = place(places, head_pieces, [3 * group_width])[0]
        outs = output_plain(head_whole, *head_inputs)
    head_hidden, forecast, grad_head_pre, grad_resid, pre_sums = outs
    token_predictions = lax.all_to_all(
        forecast, "head", split_axis=0, concat_axis=0, tiled=True
    ).reshape(group * rows, group_width)
    head_bias_rows = (pre_sums[0], jnp.sum(grad_forecast_rows.astype(jnp.float32), axis=0))
    head_both = exchange(
        [
            (top, grad_head_pre),
            (top, grad_forecast_rows),
            (head_hidden, grad_forecast_rows),
        ]
    )
    gain_sums = [[None, None] for _ in range(layer_count)]

    def rest_stage(layer_index, carry):
        outs = layers[layer_index].rest_backward(carry["grad"])
        gain_sums[layer_index][1] = outs[4]
        both = exchange(list(zip(outs[2], outs[3], strict=True)))
        return {"middle": outs[0], "mixed": outs[1]}, both

    def entry_stage(layer_index, carry):
        outs = layers[layer_index].entry_backward(carry["middle"], carry["mixed"])
        gain_sums[layer_index][0] = outs[3]
        return {"grad": outs[0]}, exchange([(outs[1], outs[2])])

    def input_stage(carry):
        head_rows = [row[None] for row in head_bias_rows]
        gain_rows = [row[None] for pair in gain_sums for row in pair]
        if layers[0].fetched and 2 + len(head_rows) + len(gain_rows) == EXTRA_ROWS:
            low, pre_low, grad_features, bias_rows = input_back(
                carry["grad"],
                entry_pre,
                intake_emit_matrix,
                intake_latent_matrix,
                intake_shortcut_matrix,
            )
            values_grad = jnp.where(pad_mask, 0.0, grad_features[:, :patch_len])
            vectors = jnp.concatenate([bias_rows, *head_rows, *gain_rows], axis=0)
            operands = []
            for part in (entry_hidden, low, pre_low, features, vectors):
                operands += [part, swap(part, 0)]
            return values_grad, 4 * patch_len + EXTRA_ROWS, operands
        grad_entry = carry["grad"].astype(jnp.bfloat16)
        grad_entry_outer = dyadic_accumulation(entry_hidden, grad_entry)
        grad_entry_outer_bias = jnp.sum(grad_entry.astype(jnp.float32), axis=0)
        grad_entry_skip = dyadic_accumulation(features, grad_entry)
        unused_entry, entry_pull = jax.vjp(jax.nn.silu, entry_pre)
        grad_entry_pre = entry_pull(reverse_matmul_answer(grad_entry, intake_emit_matrix))[0].astype(
            jnp.bfloat16
        )
        grad_entry_inner = dyadic_accumulation(features, grad_entry_pre)
        grad_entry_inner_bias = jnp.sum(grad_entry_pre.astype(jnp.float32), axis=0)
        grad_features = reverse_matmul_answer(
            grad_entry_pre, intake_latent_matrix
        ) + reverse_matmul_answer(grad_entry, intake_shortcut_matrix)
        values_grad = jnp.where(pad_mask, 0.0, grad_features[:, :patch_len])
        extra_rows = jnp.concatenate(
            [
                grad_entry_inner,
                grad_entry_skip,
                grad_entry_inner_bias[None],
                grad_entry_outer_bias[None],
            ]
            + head_rows
            + [row[None] for pair in gain_sums for row in pair],
            axis=0,
        )
        plain = entry_products(me, grad_entry_outer, extra_rows)
        return values_grad, extra_rows.shape[0], (plain.sent, plain.later, plain.own)

    stages = []
    for layer_index in reversed(range(layer_count)):
        stages += [(rest_stage, layer_index), (entry_stage, layer_index)]
    stage_count = len(stages)
    carry = {"grad": grad_resid}
    boths = {0: head_both}
    sums = {0: RowSums(*pair_products(me, head_both))}
    totals, finished = {}, {}
    entry_chunk = None
    done = 0

    def close(**step):
        step["sent"] = {n: (sums[n].sent, sums[n].later, sums[n].own) for n in sums}
        step["boths"] = boths
        step["carry"] = carry
        step = lax.optimization_barrier(step)
        for n, parts in step.pop("sent").items():
            sums[n].sent, sums[n].later, sums[n].own = parts
        return step

    step = close()
    for number in range(stage_count + 1):
        carry, boths = step["carry"], step["boths"]
        parts = {"first": sums[number].first()}
        if number >= 1:
            totals[number - 1] = sums.pop(number - 1).total()
            if number == 1:
                finished[0] = sum_columns(totals[0])
            else:
                finished[number - 1] = sum_group(totals[number - 1])
        if number >= 2:
            parts["finished"] = finished[number - 2]
        until = number + 1 if number == 0 else number + 2
        while done < min(until, stage_count):
            stage, layer_index = stages[done]
            carry, boths[done + 1] = stage(layer_index, carry)
            done += 1
        if number == stage_count - 2:
            values_grad, extra_count, parts["entry"] = input_stage(carry)
        if number == stage_count - 1:
            entry_chunk.met = entry_chunk.first()
        if number == stage_count:
            entry_summed = entry_sums_of_group(entry_chunk.total())
        step = close(**parts)
        sums[number].met = step["first"]
        if number >= 2:
            finished[number - 2] = step["finished"]
        carry, boths = step["carry"], step["boths"]
        parts = {"last": sums[number].last()}
        if number == stage_count - 2:
            if layers[0].fetched:
                entry_chunk = input_products(me, step["entry"])
            else:
                (to_x, to_y), later, own = step["entry"]
                entry_chunk = RowSums(to_x, to_y, later, own)
            parts["entry"] = (entry_chunk.sent, entry_chunk.later, entry_chunk.own)
        if number == stage_count - 1:
            parts["entry"] = entry_chunk.last()
        if number < stage_count:
            sums[number + 1] = RowSums(*pair_products(me, boths.pop(number + 1)))
            step = close(**parts)
        else:
            step = parts
        sums[number].last_met = step["last"]
        if number == stage_count - 2:
            entry_chunk.sent, entry_chunk.later, entry_chunk.own = step["entry"]
        if number == stage_count - 1:
            entry_chunk.last_met = step["entry"]
    finished[stage_count] = sum_group_at_once(sums[stage_count].total())
    entry_main, entry_extra, entry_held = entry_everywhere(
        me, entry_summed, own_count, extra_count
    )
    head_rows = gather_blocks(me, finished[0])
    head_sums = [after(head_rows[n], entry_held).astype(jnp.float32) for n in range(3)]
    layer_sums = [None] * layer_count
    for member, layer_index in enumerate(reversed(range(layer_count))):
        rest = finished[1 + 2 * member].astype(jnp.float32)
        entry = finished[2 + 2 * member].astype(jnp.float32)
        layer_sums[layer_index] = (entry[0], rest[0], rest[1], rest[2])
    inner_rows = 2 * patch_len
    last = 2 * inner_rows
    entry_sums = (
        entry_extra[:inner_rows],
        entry_extra[last],
        entry_main,
        entry_extra[last + 1],
        entry_extra[inner_rows:last],
    )
    head_bias_sums = lax.dynamic_slice_in_dim(
        entry_extra[last + 2 : last + 4], group_place * group_width, group_width, 1
    )
    own_place = (me * group + group_place) * own_count
    gains_grad = lax.dynamic_slice_in_dim(
        entry_extra[last + 4 : last + 4 + 2 * layer_count], own_place, own_count, 1
    ).reshape(layer_count, 2, own_count)
    qkv_grad = jnp.stack([layer_sums[member][0] for member in range(layer_count)])
    out_grad = jnp.stack([layer_sums[member][1] for member in range(layer_count)])
    up_grad = jnp.stack([layer_sums[member][2] for member in range(layer_count)])
    down_grad = jnp.stack([layer_sums[member][3] for member in range(layer_count)])
    return (
        token_predictions,
        values_grad,
        entry_sums[0],
        entry_sums[1],
        entry_sums[2],
        entry_sums[3],
        entry_sums[4],
        qkv_grad,
        out_grad,
        up_grad,
        down_grad,
        gains_grad,
        head_sums[0],
        head_bias_sums[0],
        head_sums[2],
        head_bias_sums[1],
        head_sums[1],
    )


def solution(mesh):
    return jax.shard_map(
        body,
        mesh=mesh,
        in_specs=(
            P(("dp", "head"), None),
            P(("dp", "head"), None),
            P(("dp", "head"), None),
            P(),
            P(),
            P(),
            P(),
            P(),
            P(None, ("dp", "head"), None),
            P(None, ("dp", "head"), None),
            P(None, ("dp", "head"), None),
            P(None, ("dp", "head"), None),
            P(None, None, ("dp", "head")),
            P(None, "head"),
            P("head"),
            P(None, "head"),
            P("head"),
            P(None, "head"),
            P("dp", "head"),
        ),
        out_specs=(
            P("dp", "head"),
            P(("dp", "head"), None),
            P(),
            P(),
            P(),
            P(),
            P(),
            P(None, ("dp", "head"), None),
            P(None, ("dp", "head"), None),
            P(None, ("dp", "head"), None),
            P(None, ("dp", "head"), None),
            P(None, None, ("dp", "head")),
            P(None, "head"),
            P("head"),
            P(None, "head"),
            P("head"),
            P(None, "head"),
        ),
        check_vma=False,
    )
```

```python
from functools import partial
import math

import jax
import jax.numpy as jnp
from jax import lax
from jax.experimental import pallas as pl
from jax.experimental.pallas import tpu as pltpu
from jax.sharding import PartitionSpec as P

MODEL_WIDTH = 1280
HEADS = 16
HEAD_DIM = 80


EPS = 1e-06
SMALL_COST = pl.CostEstimate(flops=1, bytes_accessed=1, transcendentals=0)
ROPE_BASE = 10000.0


def layout_rows(series_row, pad_row, patch_len):
    count = series_row.shape[0]
    order = jnp.arange(count, dtype=jnp.int32)
    same_series = series_row[:, None] == series_row[None, :]
    earlier = order[None, :] < order[:, None]
    position = jnp.sum(jnp.logical_and(same_series, earlier).astype(jnp.int32), axis=1)
    numbers = jnp.arange(pad_row.shape[0], dtype=jnp.int32)
    series_pad = jnp.sum(
        jnp.where(series_row[:, None] == numbers[None, :], pad_row[None, :], 0), axis=1
    )
    pad_count = jnp.where(position == 0, series_pad, 0)
    padded = pad_count == patch_len
    diagonal = order[:, None] == order[None, :]
    reach = jnp.logical_or(jnp.logical_and(earlier, jnp.logical_not(padded)[None, :]), diagonal)
    allowed = jnp.logical_and(same_series, reach)
    keep_rows = jnp.where(padded, 0.0, 1.0).astype(jnp.float32)
    return (position, pad_count, allowed, keep_rows)


def rotary_tables(position, head_dim):
    half = head_dim // 2
    steps = jnp.arange(half, dtype=jnp.float32) / half
    inverse = jnp.exp(-math.log(ROPE_BASE) * steps)
    angles = position.astype(jnp.float32)[:, None] * inverse[None, :]
    return (jnp.cos(angles)[:, None, :], jnp.sin(angles)[:, None, :])


def rotate(heads_rows, cosine, sine):
    half = heads_rows.shape[-1] // 2
    first = heads_rows[..., :half]
    second = heads_rows[..., half:]
    return jnp.concatenate(
        [first * cosine - second * sine, second * cosine + first * sine], axis=-1
    )


def unrotate(grad_rows, cosine, sine):
    half = grad_rows.shape[-1] // 2
    first = grad_rows[..., :half]
    second = grad_rows[..., half:]
    return jnp.concatenate(
        [first * cosine + second * sine, second * cosine - first * sine], axis=-1
    )


def norm_apply(resid, gain):
    return resid * lax.rsqrt(jnp.mean(resid * resid, axis=-1, keepdims=True) + EPS) * gain


def dyadic_accumulation(left, right):
    return lax.dot_general(
        left, right, (((0,), (0,)), ((), ())), preferred_element_type=jnp.float32
    )


def reverse_matmul_answer(grad_rows, weight):
    return lax.dot_general(
        grad_rows, weight, (((1,), (1,)), ((), ())), preferred_element_type=jnp.float32
    )


def masked_scores(query_rows, key_rows, allowed):
    scale = 1.0 / math.sqrt(query_rows.shape[-1])
    scores = (
        jnp.einsum("qhd,khd->hqk", query_rows, key_rows, preferred_element_type=jnp.float32) * scale
    )
    return jnp.where(allowed[None], scores, -1e30)


def attend_forward(query_rows, key_rows, value_rows, allowed):
    scores = masked_scores(query_rows, key_rows, allowed)
    peak = jnp.max(scores, axis=-1, keepdims=True)
    weights = jnp.exp(scores - peak)
    total = jnp.sum(weights, axis=-1, keepdims=True)
    probs = (weights / total).astype(jnp.bfloat16)
    mixed = jnp.einsum("hqk,khd->qhd", probs, value_rows, preferred_element_type=jnp.float32)
    return (mixed, peak + jnp.log(total))


def attend_backward(query_rows, key_rows, value_rows, allowed, log_total, grad_mixed):
    scale = 1.0 / math.sqrt(query_rows.shape[-1])
    scores = masked_scores(query_rows, key_rows, allowed)
    probs = jnp.where(allowed[None], jnp.exp(scores - log_total), 0.0)
    grad_probs = jnp.einsum(
        "qhd,khd->hqk", grad_mixed, value_rows, preferred_element_type=jnp.float32
    )
    grad_values = jnp.einsum(
        "hqk,qhd->khd", probs.astype(jnp.bfloat16), grad_mixed, preferred_element_type=jnp.float32
    )
    center = jnp.sum(grad_probs * probs, axis=-1, keepdims=True)
    grad_scores = (probs * (grad_probs - center)).astype(jnp.bfloat16)
    grad_query = (
        jnp.einsum("hqk,khd->qhd", grad_scores, key_rows, preferred_element_type=jnp.float32)
        * scale
    )
    grad_keys = (
        jnp.einsum("hqk,qhd->khd", grad_scores, query_rows, preferred_element_type=jnp.float32)
        * scale
    )
    return (grad_query, grad_keys, grad_values)


def after(value, *earlier):
    return lax.optimization_barrier((value, *earlier))[0]


def swap(v, bit):
    size = lax.axis_size("dp")
    return lax.ppermute(v, "dp", [(i, i ^ (1 << bit)) for i in range(size)])


def outer_groups():
    size = lax.axis_size("dp")
    return [[j + 8 * o for o in range(size // 8)] for j in range(8)]


def place_kernel(plan, piece_count, out_count, me_ref, *refs):
    pieces = refs[:piece_count]
    outs = refs[piece_count : piece_count + out_count]
    held = refs[piece_count + out_count : piece_count + 2 * out_count]
    in_sems, out_sems = refs[piece_count + 2 * out_count :]
    inward, outward = [], []
    for n, (piece, rel, row, out, column) in enumerate(plan):
        source = pieces[piece]
        width = held[out].shape[-1]
        if width != source.shape[-1]:
            source = source.at[:, :, pl.ds(column, width)]
        spot = (slice(None), me_ref[0] ^ rel, pl.ds(row, source.shape[1]), slice(None))
        inward.append(pltpu.make_async_copy(source, held[out].at[spot], in_sems.at[n]))
        outward.append(
            pltpu.make_async_copy(held[out].at[spot], outs[out].at[spot], out_sems.at[n])
        )
    for copy in inward:
        copy.start()
    for copy, onward in zip(inward, outward):
        copy.wait()
        onward.start()
    for onward in outward:
        onward.wait()


def place(me, pieces, widths, first=0):
    plan = []
    for n, (rel, row, _) in enumerate(pieces):
        column = first
        for out, width in enumerate(widths):
            plan.append((n, rel, row, out, column))
            column += width
    arrays = [array for _, _, array in pieces]
    lead, rows, _ = arrays[0].shape
    kind = arrays[0].dtype
    total = sum(8 * lead * rows * -(-w // 128) * 128 for w in widths) * 2
    outs = pl.pallas_call(
        partial(place_kernel, plan, len(arrays), len(widths)),
        out_shape=[jax.ShapeDtypeStruct((lead, 8, rows, w), kind) for w in widths],
        in_specs=[pl.BlockSpec(memory_space=pltpu.SMEM)]
        + [pl.BlockSpec(memory_space=pl.ANY)] * len(arrays),
        out_specs=[pl.BlockSpec(memory_space=pl.ANY)] * len(widths),
        scratch_shapes=[pltpu.VMEM((lead, 8, rows, w), kind) for w in widths]
        + [pltpu.SemaphoreType.DMA((len(plan),))] * 2,
        compiler_params=pltpu.CompilerParams(vmem_limit_bytes=total + (4 << 20)),
        cost_estimate=SMALL_COST,
    )(me, *arrays)
    outer = lax.axis_size("dp") // 8
    return [o.reshape(-1, outer * 8 * rows, o.shape[-1]) for o in outs]


def row_half(rows):
    return rows // 32 * 16 if rows >= 32 else rows // 2


def second_step(held, from_x, from_y):
    half = row_half(held.shape[1])
    return from_y[:, :half], from_x[:, half:]


def all_pieces(near, far, near_met, far_met):
    half = far[0].shape[1]
    places = ((0, 0), (2, 0), (4, 0), (6, 0), (6, half))
    pieces = []
    for (rel, row), array, met in zip(places, (*near, *far), (*near_met, *far_met), strict=True):
        pieces += [(rel, row, array), (rel | 1, row, met)]
    return pieces


def spread_rows(held):
    near = (held, swap(held, 1), swap(held, 2))
    onward_x, onward_y = second_step(*near)
    far = (swap(onward_x, 1), swap(onward_y, 2))
    return all_pieces(near, far, [swap(part, 0) for part in near], [swap(part, 0) for part in far])


def gather_head(own):
    held = lax.all_gather(own, "head", axis=0, tiled=True)[None]
    if lax.axis_size("dp") > 8:
        held = lax.all_gather(
            held, "dp", axis=0, tiled=True, axis_index_groups=outer_groups()
        )
    return held


def product_kernel(count, outer, me_ref, *refs):
    lefts, rights, met_lefts, met_rights = (refs[n * count : (n + 1) * count] for n in range(4))
    to_x, to_y, later, own, right_pair, turned = refs[4 * count :]
    rows, width = own.shape[1] // outer, own.shape[-1]
    tokens = lefts[0].shape[0]
    half = width // 2
    tile = half if half <= 640 else 640
    odd = me_ref[0] & 1 == 1
    chip = me_ref[0] >> 1

    def store(rel, n, span, side, columns, total):
        if rel == 0:
            own[n, span, slice(side * half + columns.start, side * half + columns.stop)] = total
        elif rel == 1 and side == 0:
            to_x[1, n, span, columns] = total
        elif rel == 1:
            later[1, n, span, columns] = total
        elif rel == 2 and side == 0:
            later[0, n, span, columns] = total
        elif rel == 2:
            to_y[1, n, span, columns] = total
        elif side == 0:
            to_x[0, n, span, columns] = total
        else:
            to_y[0, n, span, columns] = total

    for n in range(count):
        right_pair[:tokens] = rights[n][...]
        right_pair[tokens:] = met_rights[n][...]
        for part in range(outer):
            span = slice(part * rows, (part + 1) * rows)
            for place in range(4):
                first = (part * 8 + 2 * place) * rows
                near, far = slice(first, first + rows), slice(first + rows, first + 2 * rows)
                left_pair = jnp.concatenate(
                    [
                        jnp.where(odd, side[n][:, far], side[n][:, near]).astype(jnp.float32)
                        for side in (lefts, met_lefts)
                    ],
                    axis=0,
                )
                turned[place] = left_pair.T.astype(own.dtype)
            every = turned[...].reshape(4 * rows, 2 * tokens)
            for side in range(2):
                for at in range(0, half, tile):
                    total = jnp.dot(
                        every,
                        right_pair[:, side * half + at : side * half + at + tile],
                        preferred_element_type=jnp.float32,
                    ).astype(own.dtype)
                    for place in range(4):
                        for rel in range(4):
                            pl.when(chip ^ place == rel)(
                                partial(
                                    store,
                                    rel,
                                    n,
                                    span,
                                    side,
                                    slice(at, at + tile),
                                    total[place * rows : (place + 1) * rows],
                                )
                            )


def exchange(pairs):
    met = {}
    for pair in pairs:
        for rows in pair:
            if id(rows) not in met:
                met[id(rows)] = swap(rows, 0)
    return [(left, right, met[id(left)], met[id(right)]) for left, right in pairs]


def pair_products(me, both):
    outer = lax.axis_size("dp") // 8
    count = len(both)
    left, right = both[0][:2]
    block, width = left.shape[1] // 8, right.shape[1]
    low = jnp.bfloat16
    return pl.pallas_call(
        partial(product_kernel, count, outer),
        out_shape=[
            jax.ShapeDtypeStruct((2, count, block, width // 2), low),
            jax.ShapeDtypeStruct((2, count, block, width // 2), low),
            jax.ShapeDtypeStruct((2, count, block, width // 2), low),
            jax.ShapeDtypeStruct((count, block, width), low),
        ],
        in_specs=[pl.BlockSpec(memory_space=pltpu.SMEM)]
        + [pl.BlockSpec(memory_space=pltpu.VMEM)] * (4 * count),
        out_specs=[pl.BlockSpec(memory_space=pltpu.VMEM)] * 4,
        scratch_shapes=[
            pltpu.VMEM((2 * left.shape[0], width), low),
            pltpu.VMEM((4, block // outer, 2 * left.shape[0]), low),
        ],
        compiler_params=pltpu.CompilerParams(vmem_limit_bytes=44 << 20),
        cost_estimate=SMALL_COST,
    )((me & 7).reshape(1), *[part for parts in zip(*both, strict=True) for part in parts])


def low_sum(*parts):
    total = parts[0].astype(jnp.float32)
    for part in parts[1:]:
        total = total + part.astype(jnp.float32)
    return total.astype(jnp.bfloat16)


class RowSums:
    def __init__(self, to_x, to_y, later, own):
        self.sent, self.later, self.own = (to_x, to_y), later, own

    def first(self):
        return swap(self.sent[0], 1), swap(self.sent[1], 2)

    def last(self):
        return (
            swap(low_sum(self.later[0], self.met[0][0]), 2),
            swap(low_sum(self.later[1], self.met[1][0]), 1),
        )

    def total(self):
        half = self.own.shape[-1] // 2
        return jnp.concatenate(
            [
                low_sum(self.own[..., :half], self.met[0][1], self.last_met[0]),
                low_sum(self.own[..., half:], self.met[1][1], self.last_met[1]),
            ],
            axis=-1,
        )


def sum_group(total):
    outer = lax.axis_size("dp") // 8
    group = lax.axis_size("head")
    lead = total.shape[:-2]
    rows, columns = total.shape[-2:]
    if outer > 1:
        total = lax.psum_scatter(
            total.reshape(*lead, outer, rows // outer, columns),
            "dp",
            scatter_dimension=len(lead),
            tiled=True,
            axis_index_groups=outer_groups(),
        )
    total = total.reshape(*lead, rows // outer, columns)
    return lax.psum_scatter(total, "head", scatter_dimension=len(lead), tiled=True)


def sum_group_at_once(total):
    outer = lax.axis_size("dp") // 8
    group = lax.axis_size("head")
    if outer > 1:
        return sum_group(total).astype(jnp.float32)
    lead = total.shape[:-2]
    rows, columns = total.shape[-2:]
    total = total.reshape(*lead, group, rows // group, columns)
    axis = len(lead)
    met = lax.all_to_all(total, "head", split_axis=axis, concat_axis=axis, tiled=True)
    return jnp.sum(met.astype(jnp.float32), axis=axis)


def sum_columns(total):
    group = lax.axis_size("head")
    if lax.axis_size("dp") > 8:
        total = lax.psum(total, "dp", axis_index_groups=outer_groups())
    count, rows, columns = total.shape
    total = jnp.moveaxis(total.reshape(count, rows, group, columns // group), 2, 0)
    return lax.psum_scatter(total, "head", scatter_dimension=0, tiled=True)[0]


def gather_blocks(me, summed):
    outer = lax.axis_size("dp") // 8
    count, rows, columns = summed.shape
    if outer == 1:
        whole = lax.all_gather(summed, "dp", axis=0)
        return [whole[:, n].reshape(8 * rows, columns) for n in range(count)]
    held = summed.reshape(count * outer, rows // outer, columns)
    return place((me & 7).reshape(1), spread_rows(held), [columns])[0]


EXTRA_ROWS = 8


def entry_products(me, main, extra):
    group = lax.axis_size("head")
    outer = lax.axis_size("dp") // 8
    devices = 8 * outer * group
    columns = main.shape[1]
    own = main.shape[0] // devices
    extra = jnp.pad(extra, ((0, EXTRA_ROWS * devices - extra.shape[0]), (0, 0)))
    rows = jnp.concatenate(
        [main.reshape(devices, own, columns), extra.reshape(devices, EXTRA_ROWS, columns)], axis=1
    ).astype(jnp.bfloat16)
    view = rows.reshape(outer, 4, 2, group * (own + EXTRA_ROWS), columns)
    core = me & 1
    other = lax.dynamic_index_in_dim(view, 1 - core, 2, keepdims=False)
    pair = low_sum(lax.dynamic_index_in_dim(view, core, 2, keepdims=False), swap(other, 0))
    chip = (me & 7) >> 1
    half = columns // 2

    def picked(rel):
        return lax.dynamic_index_in_dim(pair, chip ^ rel, 1, keepdims=False).reshape(-1, columns)

    own_rows, at_x, at_y, far = (picked(rel) for rel in range(4))
    return RowSums(
        jnp.stack([far[:, :half], at_x[:, :half]]),
        jnp.stack([far[:, half:], at_y[:, half:]]),
        (at_y[:, :half], at_x[:, half:]),
        own_rows,
    )


def silu_parts(x):
    gate = 1.0 / (1.0 + jnp.exp(-x))
    return x * gate, gate * (1.0 + x * (1.0 - gate))


def output_kernel(
    plan, me_ref, top_ref, keep_ref, latent_offset, emit_offset, sensitivity, *refs
):
    pieces = refs[: len(plan)]
    hidden_ref, forecast_ref, pre_low_ref, grad_ref, bias_ref = refs[len(plan) : len(plan) + 5]
    whole, pre, skips, sent, both, sems = refs[len(plan) + 5 :]
    group, width, _ = whole.shape
    each = sensitivity.shape[2]
    two = 2 * each
    rows = width // 8
    copies = []
    for part in range(group):
        copies.append([])
        for n, (rel, row, count) in enumerate(plan):
            first = pl.multiple_of((me_ref[0] ^ rel) * rows + row, 16)
            spot = whole.at[part, pl.ds(first, count), :]
            sem = sems.at[part * len(plan) + n]
            copies[part].append(pltpu.make_async_copy(pieces[n].at[part], spot, sem))
            copies[part][n].start()
    top = top_ref[...]
    keep = keep_ref[...]
    for part in range(group):
        arrive(copies[part])
        both[...] = jnp.dot(top, whole[part, :, :two], preferred_element_type=jnp.float32)
        pre[:, part * each : (part + 1) * each] = both[:, :each] + latent_offset[part : part + 1]
        skips[part] = both[:, each:two] + emit_offset[part : part + 1]
    hidden, slope = silu_parts(pre[...])
    hidden = hidden.astype(jnp.bfloat16)
    hidden_ref[...] = hidden
    for part in range(group):
        emitted = jnp.dot(hidden, whole[part, :, two:], preferred_element_type=jnp.float32)
        forecast_ref[part] = ((emitted + skips[part]) * keep).astype(jnp.bfloat16)

    def back_hidden(n, _):
        at = pl.multiple_of(n * 256, 256)
        total = reverse_matmul_answer(whole[0, pl.ds(at, 256), two:], sensitivity[0])
        for part in range(1, group):
            total += reverse_matmul_answer(whole[part, pl.ds(at, 256), two:], sensitivity[part])
        grad_ref[:, pl.ds(at, 256)] = total.T
        return 0

    lax.fori_loop(0, width // 256, back_hidden, 0)
    pre[...] = grad_ref[...] * slope
    pre_low_ref[...] = pre[...].astype(jnp.bfloat16)
    bias_ref[...] = jnp.sum(pre_low_ref[...].astype(jnp.float32), axis=0, keepdims=True)
    for part in range(group):
        both[:, :each] = pre[:, part * each : (part + 1) * each]
        both[:, each:] = sensitivity[part].astype(jnp.float32)
        sent[part] = both[...].astype(jnp.bfloat16)

    def back_top(n, _):
        at = pl.multiple_of(n * 256, 256)
        total = reverse_matmul_answer(whole[0, pl.ds(at, 256), :two], sent[0])
        for part in range(1, group):
            total += reverse_matmul_answer(whole[part, pl.ds(at, 256), :two], sent[part])
        grad_ref[:, pl.ds(at, 256)] = total.T
        return 0

    lax.fori_loop(0, width // 256, back_top, 0)


def output_block(me, pieces, top, keep, latent_offsets, emit_offsets, grad_forecast):
    plan = [(rel, row, array.shape[1]) for rel, row, array in pieces]
    group, rows, each = grad_forecast.shape
    width = top.shape[1]
    vmem = pl.BlockSpec(memory_space=pltpu.VMEM)
    return pl.pallas_call(
        partial(output_kernel, plan),
        out_shape=[
            jax.ShapeDtypeStruct((rows, width), LOW),
            jax.ShapeDtypeStruct((group, rows, each), LOW),
            jax.ShapeDtypeStruct((rows, width), LOW),
            jax.ShapeDtypeStruct((rows, width), FULL),
            jax.ShapeDtypeStruct((1, width), FULL),
        ],
        in_specs=[pl.BlockSpec(memory_space=pltpu.SMEM)]
        + [vmem] * 5
        + [pl.BlockSpec(memory_space=pl.ANY)] * len(pieces),
        out_specs=[vmem] * 5,
        scratch_shapes=[
            pltpu.VMEM((group, width, 3 * each), LOW),
            pltpu.VMEM((rows, width), FULL),
            pltpu.VMEM((group, rows, each), FULL),
            pltpu.VMEM((group, rows, 2 * each), LOW),
            pltpu.VMEM((rows, 2 * each), FULL),
            pltpu.SemaphoreType.DMA((group * len(pieces),)),
        ],
        compiler_params=pltpu.CompilerParams(vmem_limit_bytes=44 << 20),
        cost_estimate=SMALL_COST,
    )(
        me,
        top,
        keep,
        latent_offsets,
        emit_offsets,
        grad_forecast,
        *[array for _, _, array in pieces],
    )


def output_plain(head_whole, top, keep, latent_offsets, emit_offsets, grad_forecast):
    group, _, each = grad_forecast.shape
    two = 2 * each
    inner_parts = [
        jnp.dot(top, head_whole[part][:, :two], preferred_element_type=jnp.float32)
        for part in range(group)
    ]
    head_pre = jnp.concatenate(
        [inner_parts[part][:, :each] + latent_offsets[part] for part in range(group)], axis=1
    )
    hidden, slope = silu_parts(head_pre)
    hidden = hidden.astype(jnp.bfloat16)
    forecast = jnp.stack(
        [
            (
                jnp.dot(hidden, head_whole[part][:, two:], preferred_element_type=jnp.float32)
                + emit_offsets[part]
                + inner_parts[part][:, each:]
            )
            * keep
            for part in range(group)
        ]
    ).astype(jnp.bfloat16)
    grad_hidden = sum(
        reverse_matmul_answer(grad_forecast[part], head_whole[part][:, two:])
        for part in range(group)
    )
    pre_low = (grad_hidden * slope).astype(jnp.bfloat16)
    grad_top = sum(
        reverse_matmul_answer(
            jnp.concatenate(
                [pre_low[:, part * each : (part + 1) * each], grad_forecast[part]], axis=1
            ),
            head_whole[part][:, :two],
        )
        for part in range(group)
    )
    return hidden, forecast, pre_low, grad_top, jnp.sum(pre_low.astype(FULL), axis=0, keepdims=True)


def input_back_kernel(
    grad_ref, pre_ref, emit_ref, latent_ref, shortcut_ref, low_ref, pre_low_ref, sent_ref, bias_ref, wide
):
    low = grad_ref[...].astype(jnp.bfloat16)
    low_ref[...] = low
    rows_times_turned(low, emit_ref, 0, emit_ref.shape[1], wide, 256)
    pre = pre_ref[...]
    gate = 1.0 / (1.0 + jnp.exp(-pre))
    pre_low = (wide[...] * (gate * (1.0 + pre * (1.0 - gate)))).astype(jnp.bfloat16)
    pre_low_ref[...] = pre_low
    sent_ref[...] = reverse_matmul_answer(pre_low, latent_ref[...]) + reverse_matmul_answer(
        low, shortcut_ref[...]
    )
    bias_ref[0:1] = jnp.sum(pre_low.astype(jnp.float32), axis=0, keepdims=True)
    bias_ref[1:2] = jnp.sum(low.astype(jnp.float32), axis=0, keepdims=True)


def input_products_kernel(group, me_ref, *refs):
    hidden, met_hidden, low, met_low, pre_low, met_pre_low, features, met_features = refs[:8]
    vectors, met_vectors, to_x, to_y, later, own = refs[8:14]
    turned, low_pair, extras, block = refs[14:]
    tokens = hidden.shape[0]
    columns = low.shape[1]
    half = columns // 2
    core, chip = me_ref[0] & 1, me_ref[0] >> 1
    turned[:, :tokens] = hidden[...].astype(jnp.float32).T.astype(jnp.bfloat16)
    turned[:, tokens:] = met_hidden[...].astype(jnp.float32).T.astype(jnp.bfloat16)
    low_pair[:tokens] = low[...]
    low_pair[tokens:] = met_low[...]
    wide = features.shape[1]
    extras[...] = jnp.zeros_like(extras)
    extras[:wide] = dyadic_accumulation(features[...], pre_low[...]) + dyadic_accumulation(
        met_features[...], met_pre_low[...]
    )
    extras[wide : 2 * wide] = dyadic_accumulation(features[...], low[...]) + dyadic_accumulation(
        met_features[...], met_low[...]
    )
    extras[2 * wide : 2 * wide + vectors.shape[0]] = vectors[...] + met_vectors[...]
    rows = hidden.shape[1] // 8
    each = rows // group
    span = each + EXTRA_ROWS

    def store(rel, total):
        if rel == 0:
            own[0] = total
        elif rel == 1:
            to_x[1, 0] = total[:, :half]
            later[1, 0] = total[:, half:]
        elif rel == 2:
            later[0, 0] = total[:, :half]
            to_y[1, 0] = total[:, half:]
        else:
            to_x[0, 0] = total[:, :half]
            to_y[0, 0] = total[:, half:]

    for place in range(4):
        number = 2 * place + core
        first = pl.multiple_of(number * rows, rows)
        outer = jnp.dot(
            turned[pl.ds(first, rows), :], low_pair[...], preferred_element_type=jnp.float32
        )
        first = pl.multiple_of(number * group * EXTRA_ROWS, group * EXTRA_ROWS)
        extra = extras[pl.ds(first, group * EXTRA_ROWS), :]
        for member in range(group):
            block[member * span : member * span + each] = outer[member * each : (member + 1) * each]
            block[member * span + each : (member + 1) * span] = extra[
                member * EXTRA_ROWS : (member + 1) * EXTRA_ROWS
            ]
        total = block[...].astype(own.dtype)
        for rel in range(4):
            pl.when(chip ^ place == rel)(partial(store, rel, total))


def input_back(grad, pre, emit, latent, shortcut):
    rows, columns = grad.shape
    vmem = pl.BlockSpec(memory_space=pltpu.VMEM)
    return pl.pallas_call(
        input_back_kernel,
        out_shape=[
            jax.ShapeDtypeStruct((rows, columns), LOW),
            jax.ShapeDtypeStruct((rows, columns), LOW),
            jax.ShapeDtypeStruct((rows, latent.shape[0]), FULL),
            jax.ShapeDtypeStruct((2, columns), FULL),
        ],
        in_specs=[vmem] * 5,
        out_specs=[vmem] * 4,
        scratch_shapes=[pltpu.VMEM((rows, columns), FULL)],
        compiler_params=pltpu.CompilerParams(vmem_limit_bytes=32 << 20),
        cost_estimate=SMALL_COST,
    )(grad, pre, emit, latent, shortcut)


def input_products(me, operands):
    group = lax.axis_size("head")
    tokens, columns = operands[2].shape
    width = operands[0].shape[1]
    block = width // 8 + group * EXTRA_ROWS
    pair = jax.ShapeDtypeStruct((2, 1, block, columns // 2), LOW)
    return RowSums(
        *pl.pallas_call(
            partial(input_products_kernel, group),
            out_shape=[pair, pair, pair, jax.ShapeDtypeStruct((1, block, columns), LOW)],
            in_specs=[pl.BlockSpec(memory_space=pltpu.SMEM)]
            + [pl.BlockSpec(memory_space=pltpu.VMEM)] * len(operands),
            out_specs=[pl.BlockSpec(memory_space=pltpu.VMEM)] * 4,
            scratch_shapes=[
                pltpu.VMEM((width, 2 * tokens), LOW),
                pltpu.VMEM((2 * tokens, columns), LOW),
                pltpu.VMEM((8 * group * EXTRA_ROWS, columns), FULL),
                pltpu.VMEM((block, columns), FULL),
            ],
            compiler_params=pltpu.CompilerParams(vmem_limit_bytes=32 << 20),
            cost_estimate=SMALL_COST,
        )((me & 7).reshape(1), *operands)
    )


def entry_kernel(plan, own, me_ref, *refs):
    pieces = refs[: len(plan)]
    main_ref, extra_ref, held, sems = refs[len(plan) :]
    copies = []
    for n, (rel, row, rows) in enumerate(plan):
        spot = held.at[me_ref[0] ^ rel, pl.ds(row, rows)]
        copies.append(pltpu.make_async_copy(pieces[n].at[0], spot, sems.at[n]))
    for copy in copies:
        copy.start()
    for copy in copies:
        copy.wait()
    span = own + EXTRA_ROWS
    group = held.shape[1] // span
    for block in range(8):
        rows = held[block].astype(jnp.float32)
        for member in range(group):
            main_ref[block * group + member] = rows[member * span : member * span + own]
            extra_ref[block * group + member] = rows[member * span + own : (member + 1) * span]


def entry_sums_of_group(total):
    total = total.reshape(-1, total.shape[-1])
    return sum_group_at_once(total).astype(total.dtype)


def entry_everywhere(me, summed, own, count):
    columns = summed.shape[-1]
    group = lax.axis_size("head")
    if lax.axis_size("dp") > 8:
        held = gather_head(summed)
    else:
        every = jnp.broadcast_to(summed[None], (group, *summed.shape))
        held = lax.all_to_all(every, "head", split_axis=0, concat_axis=0, tiled=True)
        held = held.reshape(1, -1, columns)
    pieces = spread_rows(held)
    places = (me & 7).reshape(1)
    span = own + EXTRA_ROWS
    if held.shape[0] > 1 or own % 8 or not in_kernel(pieces):
        (whole,) = place(places, pieces, [columns])
        whole = whole.reshape(-1, span, columns).astype(jnp.float32)
        return whole[:, :own].reshape(-1, columns), whole[:, own:].reshape(-1, columns)[:count]
    rows = held.shape[1]
    blocks = 8 * rows // span
    plan = [(rel, row, array.shape[1]) for rel, row, array in pieces]
    vmem = pl.BlockSpec(memory_space=pltpu.VMEM)
    main, extra = pl.pallas_call(
        partial(entry_kernel, plan, own),
        out_shape=[
            jax.ShapeDtypeStruct((blocks, own, columns), jnp.float32),
            jax.ShapeDtypeStruct((blocks, EXTRA_ROWS, columns), jnp.float32),
        ],
        in_specs=[pl.BlockSpec(memory_space=pltpu.SMEM)]
        + [pl.BlockSpec(memory_space=pl.ANY)] * len(pieces),
        out_specs=[vmem, vmem],
        scratch_shapes=[
            pltpu.VMEM((8, rows, columns), held.dtype),
            pltpu.SemaphoreType.DMA((len(pieces),)),
        ],
        compiler_params=pltpu.CompilerParams(vmem_limit_bytes=44 << 20),
        cost_estimate=SMALL_COST,
    )(places, *[array for _, _, array in pieces])
    return main.reshape(-1, columns), extra.reshape(-1, columns)[:count]


def fetch(plan, me, pieces, whole, sems):
    groups = []
    for group in range(whole.shape[1] // MODEL_WIDTH):
        columns = pl.ds(group * MODEL_WIDTH, MODEL_WIDTH)
        copies = []
        for n, (rel, row, rows) in enumerate(plan):
            first = pl.multiple_of((me ^ rel) * (whole.shape[0] // 8) + row, 16)
            copies.append(
                pltpu.make_async_copy(
                    pieces[n].at[0, :, columns],
                    whole.at[pl.ds(first, rows), columns],
                    sems.at[group * len(plan) + n],
                )
            )
        for copy in copies:
            copy.start()
        groups.append(copies)
    return groups


def arrive(copies):
    for copy in copies:
        copy.wait()


def rows_times(left, whole, first, out, tile):
    def step(n, _):
        at = pl.multiple_of(n * tile, 128)
        out[:, pl.ds(at, tile)] = jnp.dot(
            left, whole[:, pl.ds(first + at, tile)], preferred_element_type=jnp.float32
        )
        return 0

    lax.fori_loop(0, out.shape[1] // tile, step, 0)


def rows_times_turned(left, whole, first, width, out, tile):
    def step(n, _):
        at = pl.multiple_of(n * tile, 128)
        part = reverse_matmul_answer(whole[pl.ds(at, tile), pl.ds(first, width)], left)
        out[:, pl.ds(at, tile)] = part.T
        return 0

    lax.fori_loop(0, out.shape[1] // tile, step, 0)


def inverse_norm(rows):
    return lax.rsqrt(jnp.mean(rows * rows, axis=-1, keepdims=True) + EPS)


def other_half(rows):
    half = HEAD_DIM // 2
    lane = lax.broadcasted_iota(jnp.int32, rows.shape, 1) % HEAD_DIM
    ahead = pltpu.roll(rows, rows.shape[1] - half, 1)
    behind = pltpu.roll(rows, half, 1)
    return jnp.where(lane < half, ahead, behind)


def head_window(head, width):
    first = head * HEAD_DIM // 128 * 128
    last = min(-(-(head + 1) * HEAD_DIM // 128) * 128, width)
    start = head * HEAD_DIM - first
    lane = lax.broadcasted_iota(jnp.int32, (1, last - first), 1)
    return slice(first, last), jnp.logical_and(lane >= start, lane < start + HEAD_DIM)


def entry_forward_kernel(plan, me_ref, resid_ref, gain_ref, cosine_ref, sine_ref, allowed_ref, *refs):
    pieces = refs[: len(plan)]
    normed_ref, query_ref, key_ref, value_ref, total_ref, mixed_ref = refs[len(plan) : len(plan) + 6]
    whole, wide, sems = refs[len(plan) + 6 :]
    groups = fetch(plan, me_ref[0], pieces, whole, sems)
    resid = resid_ref[...]
    normed = (resid * inverse_norm(resid) * gain_ref[...]).astype(jnp.bfloat16)
    normed_ref[...] = normed
    for group, out in enumerate((query_ref, key_ref, value_ref)):
        arrive(groups[group])
        rows_times(normed, whole, group * MODEL_WIDTH, wide, 256)
        rows = wide[...]
        if group < 2:
            rows = rows * cosine_ref[...] + other_half(rows) * sine_ref[...]
        out[...] = rows.astype(jnp.bfloat16)
    scale = 1.0 / math.sqrt(HEAD_DIM)
    allowed = allowed_ref[...] > 0.0
    wide[...] = jnp.zeros_like(wide)
    totals = jnp.zeros(total_ref.shape, jnp.float32)
    head_lane = lax.broadcasted_iota(jnp.int32, total_ref.shape, 1)
    for head in range(HEADS):
        window, inside = head_window(head, MODEL_WIDTH)
        query = jnp.where(inside, query_ref[:, window], 0)
        scores = reverse_matmul_answer(query, key_ref[:, window]) * scale
        scores = jnp.where(allowed, scores, -1e30)
        peak = jnp.max(scores, axis=-1, keepdims=True)
        weights = jnp.exp(scores - peak)
        total = jnp.sum(weights, axis=-1, keepdims=True)
        probs = (weights / total).astype(jnp.bfloat16)
        mixed = jnp.dot(probs, value_ref[:, window], preferred_element_type=jnp.float32)
        wide[:, window] += jnp.where(inside, mixed, 0.0)
        totals = jnp.where(head_lane == head, peak + jnp.log(total), totals)
    total_ref[...] = totals
    mixed_ref[...] = wide[...].astype(jnp.bfloat16)


def gelu_parts(x):
    root = math.sqrt(2.0 / math.pi)
    bend = jnp.tanh(root * (x + 0.044715 * (x * x * x)))
    slope = 0.5 * (1.0 + bend) + 0.5 * x * (1.0 - bend * bend) * root * (
        1.0 + 3.0 * 0.044715 * (x * x)
    )
    return 0.5 * x * (1.0 + bend), slope


def rest_forward_kernel(plan, me_ref, resid_ref, mixed_ref, gain_ref, *refs):
    pieces = refs[: len(plan)]
    result_ref, middle_ref, normed_ref, pre_ref = refs[len(plan) : len(plan) + 4]
    whole, sems = refs[len(plan) + 4 :]
    groups = fetch(plan, me_ref[0], pieces, whole, sems)
    arrive(groups[0])
    rows_times(mixed_ref[...], whole, 0, middle_ref, 256)
    middle = resid_ref[...] + middle_ref[...]
    middle_ref[...] = middle
    normed = (middle * inverse_norm(middle) * gain_ref[...]).astype(jnp.bfloat16)
    normed_ref[...] = normed
    arrive(groups[1])
    rows_times(normed, whole, MODEL_WIDTH, pre_ref, 256)
    act = gelu_parts(pre_ref[...])[0].astype(jnp.bfloat16)
    arrive(groups[2])
    rows_times(act, whole, 2 * MODEL_WIDTH, result_ref, 256)
    result_ref[...] += middle_ref[...]


def norm_back(rows, gain, grad):
    inverse = inverse_norm(rows)
    scaled = grad * gain
    mean = jnp.mean(rows * scaled, axis=-1, keepdims=True)
    sent = inverse * scaled - rows * (inverse * inverse * inverse * mean)
    return sent, jnp.sum(grad * rows * inverse, axis=0, keepdims=True)


def rest_backward_kernel(plan, me_ref, grad_ref, middle_ref, pre_ref, gain_ref, *refs):
    pieces = refs[: len(plan)]
    outs = refs[len(plan) : len(plan) + 7]
    grad_middle_ref, mixed_ref, attn_ref, grad_pre_ref, branch_ref, act_ref, gain_grad_ref = outs
    whole, wide, sems = refs[len(plan) + 7 :]
    groups = fetch(plan, me_ref[0], pieces, whole, sems)
    grad = grad_ref[...]
    branch = grad.astype(jnp.bfloat16)
    branch_ref[...] = branch
    arrive(groups[2])
    rows_times_turned(branch, whole, 2 * MODEL_WIDTH, MODEL_WIDTH, wide, 256)
    act, slope = gelu_parts(pre_ref[...])
    act_ref[...] = act.astype(jnp.bfloat16)
    grad_pre = (wide[...] * slope).astype(jnp.bfloat16)
    grad_pre_ref[...] = grad_pre
    arrive(groups[1])
    rows_times_turned(grad_pre, whole, MODEL_WIDTH, MODEL_WIDTH, wide, 256)
    sent, gain_grad_ref[...] = norm_back(middle_ref[...], gain_ref[...], wide[...])
    grad_middle = grad + sent
    grad_middle_ref[...] = grad_middle
    attn = grad_middle.astype(jnp.bfloat16)
    attn_ref[...] = attn
    arrive(groups[0])
    rows_times_turned(attn, whole, 0, MODEL_WIDTH, wide, 256)
    mixed_ref[...] = wide[...].astype(jnp.bfloat16)


def entry_backward_kernel(
    plan,
    me_ref,
    grad_middle_ref,
    grad_mixed_ref,
    resid_ref,
    query_ref,
    key_ref,
    value_ref,
    total_ref,
    gain_ref,
    cosine_ref,
    sine_ref,
    allowed_ref,
    *refs,
):
    pieces = refs[: len(plan)]
    grad_resid_ref, projected_ref, gain_grad_ref = refs[len(plan) : len(plan) + 3]
    whole, grad_query, grad_key, grad_value, sems = refs[len(plan) + 3 :]
    groups = fetch(plan, me_ref[0], pieces, whole, sems)
    scale = 1.0 / math.sqrt(HEAD_DIM)
    allowed = allowed_ref[...] > 0.0
    totals = total_ref[...]
    grad_query[...] = jnp.zeros_like(grad_query)
    grad_key[...] = jnp.zeros_like(grad_key)
    grad_value[...] = jnp.zeros_like(grad_value)
    for head in range(HEADS):
        window, inside = head_window(head, MODEL_WIDTH)
        query = jnp.where(inside, query_ref[:, window], 0)
        keys = key_ref[:, window]
        grad_mixed = jnp.where(inside, grad_mixed_ref[:, window], 0)
        scores = reverse_matmul_answer(query, keys) * scale
        probs = jnp.where(allowed, jnp.exp(scores - totals[:, head : head + 1]), 0.0)
        grad_probs = reverse_matmul_answer(grad_mixed, value_ref[:, window])
        grad_value[:, window] += dyadic_accumulation(probs.astype(jnp.bfloat16), grad_mixed)
        center = jnp.sum(grad_probs * probs, axis=-1, keepdims=True)
        grad_scores = (probs * (grad_probs - center)).astype(jnp.bfloat16)
        along = jnp.dot(grad_scores, keys, preferred_element_type=jnp.float32)
        grad_query[:, window] += jnp.where(inside, along * scale, 0.0)
        grad_key[:, window] += dyadic_accumulation(grad_scores, query) * scale
    for group, part in enumerate((grad_query, grad_key, grad_value)):
        rows = part[...]
        if group < 2:
            rows = rows * cosine_ref[...] - other_half(rows) * sine_ref[...]
        projected_ref[:, group * MODEL_WIDTH : (group + 1) * MODEL_WIDTH] = rows.astype(jnp.bfloat16)
    for copies in groups:
        arrive(copies)
    rows_times_turned(projected_ref[...], whole, 0, 3 * MODEL_WIDTH, grad_query, 256)
    sent, gain_grad_ref[...] = norm_back(resid_ref[...], gain_ref[...], grad_query[...])
    grad_resid_ref[...] = grad_middle_ref[...] + sent


def whole_call(kernel, me, pieces, inputs, outs, wides):
    rows = inputs[0].shape[0]
    plan = [(rel, row, array.shape[1]) for rel, row, array in pieces]
    blocks = 8 * pieces[0][2].shape[1]
    columns = 3 * MODEL_WIDTH
    vmem = pl.BlockSpec(memory_space=pltpu.VMEM)
    return pl.pallas_call(
        partial(kernel, plan),
        out_shape=[jax.ShapeDtypeStruct(shape, kind) for shape, kind in outs],
        in_specs=[pl.BlockSpec(memory_space=pltpu.SMEM)]
        + [vmem] * len(inputs)
        + [pl.BlockSpec(memory_space=pl.ANY)] * len(pieces),
        out_specs=[vmem] * len(outs),
        scratch_shapes=[pltpu.VMEM((blocks, columns), jnp.bfloat16)]
        + [pltpu.VMEM((rows, MODEL_WIDTH), jnp.float32)] * wides
        + [pltpu.SemaphoreType.DMA((3 * len(pieces),))],
        compiler_params=pltpu.CompilerParams(vmem_limit_bytes=44 << 20),
        cost_estimate=SMALL_COST,
    )(me, *inputs, *[array for _, _, array in pieces])


def in_kernel(pieces):
    lead, rows, _ = pieces[0][2].shape
    return lead == 1 and rows % 32 == 0


LOW, FULL = jnp.bfloat16, jnp.float32


class Layer:
    def __init__(self, places, entry_pieces, gains, tables, allowed):
        self.places, self.entry_pieces, self.gains = places, entry_pieces, gains
        self.tables, self.allowed = tables, allowed
        self.fetched = in_kernel(entry_pieces)
        if not self.fetched:
            self.entry_whole = place(places, entry_pieces, [3 * MODEL_WIDTH])[0][0]

    def add_rest(self, rest_pieces):
        self.rest_pieces = rest_pieces
        if not self.fetched:
            self.rest_whole = [part[0] for part in place(self.places, rest_pieces, [MODEL_WIDTH] * 3)]

    def shapes(self, *kinds):
        rows = self.allowed.shape[0]
        return [((rows, width), kind) for width, kind in kinds]

    def entry_forward(self, resid):
        if not self.fetched:
            self.saved = entry_forward(
                resid, self.entry_whole, self.gains, *self.tables[:2], self.allowed
            )
            return self.saved[6]
        wide = (MODEL_WIDTH, LOW)
        self.resid = resid
        outs = whole_call(
            entry_forward_kernel,
            self.places,
            self.entry_pieces,
            (resid, self.gains[:1].astype(FULL), *self.tables[2:], self.allowed.astype(FULL)),
            self.shapes(wide, wide, wide, wide, (128, FULL), wide),
            1,
        )
        self.normed_first, self.heads = outs[0], outs[1:5]
        return outs[5]

    def rest_forward(self, mixed):
        if not self.fetched:
            result, self.saved = rest_forward(
                (*self.saved[:6], mixed), *self.rest_whole, self.gains
            )
            return result
        self.mixed = mixed
        result, self.middle, self.normed_second, self.hidden_pre = whole_call(
            rest_forward_kernel,
            self.places,
            self.rest_pieces,
            (self.resid, mixed, self.gains[1:].astype(FULL)),
            self.shapes(
                (MODEL_WIDTH, FULL), (MODEL_WIDTH, FULL), (MODEL_WIDTH, LOW), (MODEL_WIDTH, FULL)
            ),
            0,
        )
        return result

    def rest_backward(self, grad):
        if not self.fetched:
            weights = (self.entry_whole, *self.rest_whole, self.gains)
            return rest_backward(self.saved, weights, grad)
        wide = (MODEL_WIDTH, LOW)
        grad_middle, grad_mixed, grad_attn, grad_pre, branch, act, gain_grad = whole_call(
            rest_backward_kernel,
            self.places,
            self.rest_pieces,
            (grad, self.middle, self.hidden_pre, self.gains[1:].astype(FULL)),
            self.shapes((MODEL_WIDTH, FULL), wide, wide, wide, wide, wide)
            + [((1, MODEL_WIDTH), FULL)],
            1,
        )
        lefts = (self.mixed, self.normed_second, act)
        return grad_middle, grad_mixed, lefts, (grad_attn, grad_pre, branch), gain_grad[0]

    def entry_backward(self, grad_middle, grad_mixed):
        if not self.fetched:
            weights = (self.entry_whole, *self.rest_whole, self.gains)
            return entry_backward(
                self.saved, weights, *self.tables[:2], self.allowed, grad_middle, grad_mixed
            )
        grad_resid, projected, gain_grad = whole_call(
            entry_backward_kernel,
            self.places,
            self.entry_pieces,
            (
                grad_middle,
                grad_mixed,
                self.resid,
                *self.heads,
                self.gains[:1].astype(FULL),
                *self.tables[2:],
                self.allowed.astype(FULL),
            ),
            self.shapes((MODEL_WIDTH, FULL), (3 * MODEL_WIDTH, LOW)) + [((1, MODEL_WIDTH), FULL)],
            3,
        )
        return grad_resid, self.normed_first, projected, gain_grad[0]


def entry_forward(resid, qkv_full, gain_pair, cosine, sine, allowed):
    gains = gain_pair.astype(jnp.float32)
    rows = resid.shape[0]
    normed_first = norm_apply(resid, gains[0]).astype(jnp.bfloat16)
    projected = jnp.dot(normed_first, qkv_full, preferred_element_type=jnp.float32)
    query_rows = rotate(
        projected[:, :MODEL_WIDTH].reshape(rows, HEADS, HEAD_DIM), cosine, sine
    ).astype(jnp.bfloat16)
    key_rows = rotate(
        projected[:, MODEL_WIDTH : 2 * MODEL_WIDTH].reshape(rows, HEADS, HEAD_DIM), cosine, sine
    ).astype(jnp.bfloat16)
    value_rows = projected[:, 2 * MODEL_WIDTH :].reshape(rows, HEADS, HEAD_DIM).astype(jnp.bfloat16)

    mixed, log_total = attend_forward(query_rows, key_rows, value_rows, allowed)
    mixed_low = mixed.reshape(rows, MODEL_WIDTH).astype(jnp.bfloat16)
    return (resid, normed_first, query_rows, key_rows, value_rows, log_total, mixed_low)


def rest_forward(saved, out_full, up_full, down_full, gain_pair):
    gains = gain_pair.astype(jnp.float32)
    resid, mixed_low = saved[0], saved[6]
    middle = resid + jnp.dot(mixed_low, out_full, preferred_element_type=jnp.float32)
    normed_second = norm_apply(middle, gains[1]).astype(jnp.bfloat16)
    hidden_pre = jnp.dot(normed_second, up_full, preferred_element_type=jnp.float32)
    hidden_act = jax.nn.gelu(hidden_pre, approximate=True).astype(jnp.bfloat16)
    result = middle + jnp.dot(hidden_act, down_full, preferred_element_type=jnp.float32)
    return (result, (*saved, middle, normed_second, hidden_pre))


def rest_backward(saved, weights, grad_result):
    mixed_low, middle, normed_second, hidden_pre = saved[6:]
    _, out_full, up_full, down_full, gain_pair = weights
    gains = gain_pair.astype(jnp.float32)
    grad_branch = grad_result.astype(jnp.bfloat16)
    hidden_act, gelu_pull = jax.vjp(partial(jax.nn.gelu, approximate=True), hidden_pre)
    hidden_low = hidden_act.astype(jnp.bfloat16)
    grad_act = reverse_matmul_answer(grad_branch, down_full)
    grad_pre = gelu_pull(grad_act)[0].astype(jnp.bfloat16)
    grad_normed_second = reverse_matmul_answer(grad_pre, up_full)
    unused_second, second_pull = jax.vjp(norm_apply, middle, gains[1])
    grad_middle_norm, grad_gain_second = second_pull(grad_normed_second)
    grad_middle = grad_result + grad_middle_norm
    grad_attn = grad_middle.astype(jnp.bfloat16)
    grad_mixed = reverse_matmul_answer(grad_attn, out_full).astype(jnp.bfloat16)
    left_rows = (mixed_low, normed_second, hidden_low)
    right_rows = (grad_attn, grad_pre, grad_branch)
    return (grad_middle, grad_mixed, left_rows, right_rows, grad_gain_second)


def entry_backward(saved, weights, cosine, sine, allowed, grad_middle, grad_mixed):
    resid, normed_first, query_rows, key_rows, value_rows, log_total = saved[:6]
    qkv_full = weights[0]
    gains = weights[4].astype(jnp.float32)
    rows = resid.shape[0]
    grad_query, grad_keys, grad_values = attend_backward(
        query_rows,
        key_rows,
        value_rows,
        allowed,
        log_total,
        grad_mixed.reshape(rows, HEADS, HEAD_DIM),
    )
    grad_query = unrotate(grad_query, cosine, sine).reshape(rows, MODEL_WIDTH)
    grad_keys = unrotate(grad_keys, cosine, sine).reshape(rows, MODEL_WIDTH)
    grad_values = grad_values.reshape(rows, MODEL_WIDTH)
    grad_projected = jnp.concatenate([grad_query, grad_keys, grad_values], axis=1).astype(
        jnp.bfloat16
    )
    grad_normed_first = reverse_matmul_answer(grad_projected, qkv_full)
    unused_first, first_pull = jax.vjp(norm_apply, resid, gains[0])
    grad_resid_norm, grad_gain_first = first_pull(grad_normed_first)
    return (grad_middle + grad_resid_norm, normed_first, grad_projected, grad_gain_first)


def body(
    patch_observations,
    sequence_labels,
    leading_filler_count,
    intake_latent_matrix,
    intake_latent_offset,
    intake_emit_matrix,
    intake_emit_offset,
    intake_shortcut_matrix,
    attention_entry_matrices,
    attention_merge_matrix,
    feedforward_widen_matrix,
    feedforward_shrink_matrix,
    layer_scale_factors,
    readout_latent_matrix,
    readout_latent_offset,
    readout_emit_matrix,
    readout_emit_offset,
    readout_shortcut_matrix,
    loss_sensitivity,
):
    patch_len = patch_observations.shape[1]
    position, pad_count, allowed, keep_rows = layout_rows(
        sequence_labels[0], leading_filler_count[0], patch_len
    )
    cosine, sine = rotary_tables(position, HEAD_DIM)
    columns = jnp.arange(patch_len, dtype=jnp.int32)
    pad_mask = columns[None, :] < pad_count[:, None]
    features = jnp.concatenate(
        [
            jnp.where(pad_mask, jnp.zeros_like(patch_observations), patch_observations),
            pad_mask.astype(jnp.bfloat16),
        ],
        axis=1,
    )
    entry_pre = (
        jnp.dot(features, intake_latent_matrix, preferred_element_type=jnp.float32)
        + intake_latent_offset
    )
    entry_hidden = jax.nn.silu(entry_pre).astype(jnp.bfloat16)
    resid = (
        jnp.dot(entry_hidden, intake_emit_matrix, preferred_element_type=jnp.float32)
        + intake_emit_offset
        + jnp.dot(features, intake_shortcut_matrix, preferred_element_type=jnp.float32)
    )
    layer_count = attention_entry_matrices.shape[0]
    group = lax.axis_size("head")
    group_place = lax.axis_index("head")
    outer = lax.axis_size("dp") // 8
    me = lax.axis_index("dp").astype(jnp.int32)
    places = (me & 7).reshape(1)
    own_count = layer_scale_factors.shape[2]
    rows = patch_observations.shape[0]

    group_width = readout_latent_offset.shape[0]
    offsets = jnp.stack([readout_latent_offset, readout_emit_offset])
    coarse = lax.reduce_precision(offsets, 8, 7)
    offset_rows = jnp.concatenate([coarse, offsets - coarse], axis=0).astype(jnp.bfloat16)
    offset_rows = jnp.pad(offset_rows, ((0, 12), (0, 0)))
    sent = jnp.concatenate(
        [
            loss_sensitivity.reshape(group, rows, group_width),
            jnp.broadcast_to(offset_rows[None], (group, 16, group_width)),
        ],
        axis=1,
    )
    gain_columns = layer_scale_factors.reshape(2 * layer_count, own_count).T
    gain_columns = jnp.pad(gain_columns, ((0, 0), (0, 128 - 2 * layer_count)))
    chunks = []
    for layer_index in range(layer_count):
        entry_own = attention_entry_matrices[layer_index]
        if layer_index == 0:
            entry_own = jnp.concatenate([entry_own, gain_columns], axis=1)
        chunks.append(entry_own)
        rest_own = jnp.concatenate(
            [
                attention_merge_matrix[layer_index],
                feedforward_widen_matrix[layer_index],
                feedforward_shrink_matrix[layer_index],
            ],
            axis=1,
        )
        chunks.append(rest_own)
    head_own = jnp.concatenate(
        [
            lax.dynamic_index_in_dim(
                matrix.reshape(outer, 8, -1, group_width), me % 8, 1, keepdims=False
            )
            for matrix in (readout_latent_matrix, readout_shortcut_matrix, readout_emit_matrix)
        ],
        axis=2,
    )
    chunks.append(head_own)
    count = len(chunks)

    def gather_chunk(number, own):
        if number < count - 1:
            return gather_head(own)
        return lax.all_gather(own, "head", axis=0, tiled=True)

    held = gather_chunk(0, chunks[0])
    cosine_wide = jnp.tile(jnp.concatenate([cosine[:, 0], cosine[:, 0]], axis=1), (1, HEADS))
    sine_wide = jnp.tile(jnp.concatenate([-sine[:, 0], sine[:, 0]], axis=1), (1, HEADS))
    tables = (cosine, sine, cosine_wide, sine_wide)
    nears, fars, near_mets = [], [], []
    layers = []
    onward = None
    for number in range(count + 1):
        step = {}
        if number < count:
            step["x"], step["y"] = swap(held, 1), swap(held, 2)
        if number + 1 < count:
            step["next"] = gather_chunk(number + 1, chunks[number + 1])
        if number == count - 1:
            step["met"] = lax.all_to_all(
                after(sent, held), "head", split_axis=0, concat_axis=0, tiled=True
            )
        if number == 0:
            step["resid"] = resid
        else:
            step["far"] = (swap(onward[0], 1), swap(onward[1], 2))
            near_mets.append([swap(part, 0) for part in after(nears[number - 1], onward)])
        if number > 1:
            chunk = number - 2
            far_met = [swap(part, 0) for part in after(fars[chunk], onward)]
            pieces = all_pieces(nears[chunk], fars[chunk], near_mets[chunk], far_met)
            if chunk == 0:
                gain_rows = place(places, pieces, [128], 3 * MODEL_WIDTH)[0][0]
                gain_rows = gain_rows[:, : 2 * layer_count].T.reshape(layer_count, 2, -1)
            if chunk % 2 == 0:
                layers.append(Layer(places, pieces, gain_rows[chunk // 2], tables, allowed))
                step["mixed"] = layers[-1].entry_forward(resid)
            else:
                layers[-1].add_rest(pieces)
                step["resid"] = layers[-1].rest_forward(mixed)
        step["own"] = chunks[number + 2 :]
        step = lax.optimization_barrier(step)
        chunks[number + 2 :] = step["own"]
        if number < count:
            nears.append((held, step["x"], step["y"]))
            onward = second_step(*nears[-1])
        held = step.get("next")
        if number > 0:
            fars.append(step["far"])
        resid = step.get("resid", resid)
        mixed = step.get("mixed")
        if "met" in step:
            met = step["met"]
    head_far_met = [swap(part, 0) for part in fars[-1]]
    head_pieces = all_pieces(nears[-1], fars[-1], near_mets[-1], head_far_met)
    sensitivity = met[:, :rows]
    head_offsets = met[:, rows : rows + 4].astype(jnp.float32)
    latent_offsets = head_offsets[:, 0] + head_offsets[:, 2]
    emit_offsets = head_offsets[:, 1] + head_offsets[:, 3]

    top = resid.astype(jnp.bfloat16)
    keep_column = keep_rows[:, None]
    grad_forecast = (sensitivity.astype(jnp.float32) * keep_column).astype(jnp.bfloat16)
    grad_forecast_rows = jnp.concatenate([grad_forecast[part] for part in range(group)], axis=1)
    head_inputs = (top, keep_column, latent_offsets, emit_offsets, grad_forecast)
    if layers[0].fetched:
        outs = output_block(places, head_pieces, *head_inputs)
    else:
        head_whole = place(places, head_pieces, [3 * group_width])[0]
        outs = output_plain(head_whole, *head_inputs)
    head_hidden, forecast, grad_head_pre, grad_resid, pre_sums = outs
    token_predictions = lax.all_to_all(
        forecast, "head", split_axis=0, concat_axis=0, tiled=True
    ).reshape(group * rows, group_width)
    head_bias_rows = (pre_sums[0], jnp.sum(grad_forecast_rows.astype(jnp.float32), axis=0))
    head_both = exchange(
        [
            (top, grad_head_pre),
            (top, grad_forecast_rows),
            (head_hidden, grad_forecast_rows),
        ]
    )
    gain_sums = [[None, None] for _ in range(layer_count)]

    def rest_stage(layer_index, carry):
        outs = layers[layer_index].rest_backward(carry["grad"])
        gain_sums[layer_index][1] = outs[4]
        both = exchange(list(zip(outs[2], outs[3], strict=True)))
        return {"middle": outs[0], "mixed": outs[1]}, both

    def entry_stage(layer_index, carry):
        outs = layers[layer_index].entry_backward(carry["middle"], carry["mixed"])
        gain_sums[layer_index][0] = outs[3]
        return {"grad": outs[0]}, exchange([(outs[1], outs[2])])

    def input_stage(carry):
        head_rows = [row[None] for row in head_bias_rows]
        gain_rows = [row[None] for pair in gain_sums for row in pair]
        if layers[0].fetched and 2 + len(head_rows) + len(gain_rows) == EXTRA_ROWS:
            low, pre_low, grad_features, bias_rows = input_back(
                carry["grad"],
                entry_pre,
                intake_emit_matrix,
                intake_latent_matrix,
                intake_shortcut_matrix,
            )
            values_grad = jnp.where(pad_mask, 0.0, grad_features[:, :patch_len])
            vectors = jnp.concatenate([bias_rows, *head_rows, *gain_rows], axis=0)
            operands = []
            for part in (entry_hidden, low, pre_low, features, vectors):
                operands += [part, swap(part, 0)]
            return values_grad, 4 * patch_len + EXTRA_ROWS, operands
        grad_entry = carry["grad"].astype(jnp.bfloat16)
        grad_entry_outer = dyadic_accumulation(entry_hidden, grad_entry)
        grad_entry_outer_bias = jnp.sum(grad_entry.astype(jnp.float32), axis=0)
        grad_entry_skip = dyadic_accumulation(features, grad_entry)
        unused_entry, entry_pull = jax.vjp(jax.nn.silu, entry_pre)
        grad_entry_pre = entry_pull(reverse_matmul_answer(grad_entry, intake_emit_matrix))[0].astype(
            jnp.bfloat16
        )
        grad_entry_inner = dyadic_accumulation(features, grad_entry_pre)
        grad_entry_inner_bias = jnp.sum(grad_entry_pre.astype(jnp.float32), axis=0)
        grad_features = reverse_matmul_answer(
            grad_entry_pre, intake_latent_matrix
        ) + reverse_matmul_answer(grad_entry, intake_shortcut_matrix)
        values_grad = jnp.where(pad_mask, 0.0, grad_features[:, :patch_len])
        extra_rows = jnp.concatenate(
            [
                grad_entry_inner,
                grad_entry_skip,
                grad_entry_inner_bias[None],
                grad_entry_outer_bias[None],
            ]
            + head_rows
            + [row[None] for pair in gain_sums for row in pair],
            axis=0,
        )
        plain = entry_products(me, grad_entry_outer, extra_rows)
        return values_grad, extra_rows.shape[0], (plain.sent, plain.later, plain.own)

    stages = []
    for layer_index in reversed(range(layer_count)):
        stages += [(rest_stage, layer_index), (entry_stage, layer_index)]
    stage_count = len(stages)
    carry = {"grad": grad_resid}
    boths = {0: head_both}
    sums = {0: RowSums(*pair_products(me, head_both))}
    finished = {}
    entry_chunk = None
    done = 0

    def close(**step):
        step["sent"] = {n: (sums[n].sent, sums[n].later, sums[n].own) for n in sums}
        step["boths"] = boths
        step["carry"] = carry
        step = lax.optimization_barrier(step)
        for n, parts in step.pop("sent").items():
            sums[n].sent, sums[n].later, sums[n].own = parts
        return step

    step = close()
    for number in range(stage_count + 1):
        carry, boths = step["carry"], step["boths"]
        parts = {"first": sums[number].first()}
        if number >= 2:
            finished[number - 1] = sum_group(sums.pop(number - 1).total())
        if number >= 2:
            parts["finished"] = finished[number - 2]
        until = number + 1 if number == 0 else number + 2
        while done < min(until, stage_count):
            stage, layer_index = stages[done]
            carry, boths[done + 1] = stage(layer_index, carry)
            done += 1
        if number == stage_count - 2:
            values_grad, extra_count, parts["entry"] = input_stage(carry)
        if number == stage_count - 1:
            entry_chunk.met = entry_chunk.first()
        if number == stage_count:
            entry_summed = entry_sums_of_group(entry_chunk.total())
        step = close(**parts)
        sums[number].met = step["first"]
        if number >= 2:
            finished[number - 2] = step["finished"]
        carry, boths = step["carry"], step["boths"]
        parts = {"last": sums[number].last()}
        if number == 1:
            finished[0] = sum_columns(sums.pop(0).total())
        if number == stage_count - 2:
            if layers[0].fetched:
                entry_chunk = input_products(me, step["entry"])
            else:
                (to_x, to_y), later, own = step["entry"]
                entry_chunk = RowSums(to_x, to_y, later, own)
            parts["entry"] = (entry_chunk.sent, entry_chunk.later, entry_chunk.own)
        if number == stage_count - 1:
            parts["entry"] = entry_chunk.last()
        if number < stage_count:
            sums[number + 1] = RowSums(*pair_products(me, boths.pop(number + 1)))
            step = close(**parts)
        else:
            step = parts
        sums[number].last_met = step["last"]
        if number == stage_count - 2:
            entry_chunk.sent, entry_chunk.later, entry_chunk.own = step["entry"]
        if number == stage_count - 1:
            entry_chunk.last_met = step["entry"]
    finished[stage_count] = sum_group_at_once(sums[stage_count].total())
    entry_main, entry_extra = entry_everywhere(me, entry_summed, own_count, extra_count)
    head_rows = gather_blocks(me, finished[0])
    head_sums = [after(head_rows[n], entry_summed).astype(jnp.float32) for n in range(3)]
    layer_sums = [None] * layer_count
    for member, layer_index in enumerate(reversed(range(layer_count))):
        rest = finished[1 + 2 * member].astype(jnp.float32)
        entry = finished[2 + 2 * member].astype(jnp.float32)
        layer_sums[layer_index] = (entry[0], rest[0], rest[1], rest[2])
    inner_rows = 2 * patch_len
    last = 2 * inner_rows
    entry_sums = (
        entry_extra[:inner_rows],
        entry_extra[last],
        entry_main,
        entry_extra[last + 1],
        entry_extra[inner_rows:last],
    )
    head_bias_sums = lax.dynamic_slice_in_dim(
        entry_extra[last + 2 : last + 4], group_place * group_width, group_width, 1
    )
    own_place = (me * group + group_place) * own_count
    gains_grad = lax.dynamic_slice_in_dim(
        entry_extra[last + 4 : last + 4 + 2 * layer_count], own_place, own_count, 1
    ).reshape(layer_count, 2, own_count)
    qkv_grad = jnp.stack([layer_sums[member][0] for member in range(layer_count)])
    out_grad = jnp.stack([layer_sums[member][1] for member in range(layer_count)])
    up_grad = jnp.stack([layer_sums[member][2] for member in range(layer_count)])
    down_grad = jnp.stack([layer_sums[member][3] for member in range(layer_count)])
    return (
        token_predictions,
        values_grad,
        entry_sums[0],
        entry_sums[1],
        entry_sums[2],
        entry_sums[3],
        entry_sums[4],
        qkv_grad,
        out_grad,
        up_grad,
        down_grad,
        gains_grad,
        head_sums[0],
        head_bias_sums[0],
        head_sums[2],
        head_bias_sums[1],
        head_sums[1],
    )


def solution(mesh):
    return jax.shard_map(
        body,
        mesh=mesh,
        in_specs=(
            P(("dp", "head"), None),
            P(("dp", "head"), None),
            P(("dp", "head"), None),
            P(),
            P(),
            P(),
            P(),
            P(),
            P(None, ("dp", "head"), None),
            P(None, ("dp", "head"), None),
            P(None, ("dp", "head"), None),
            P(None, ("dp", "head"), None),
            P(None, None, ("dp", "head")),
            P(None, "head"),
            P("head"),
            P(None, "head"),
            P("head"),
            P(None, "head"),
            P("dp", "head"),
        ),
        out_specs=(
            P("dp", "head"),
            P(("dp", "head"), None),
            P(),
            P(),
            P(),
            P(),
            P(),
            P(None, ("dp", "head"), None),
            P(None, ("dp", "head"), None),
            P(None, ("dp", "head"), None),
            P(None, ("dp", "head"), None),
            P(None, None, ("dp", "head")),
            P(None, "head"),
            P("head"),
            P(None, "head"),
            P("head"),
            P(None, "head"),
        ),
        check_vma=False,
    )
```

```python
from functools import partial
import math

import jax
import jax.numpy as jnp
from jax import lax
from jax.experimental import pallas as pl
from jax.experimental.pallas import tpu as pltpu
from jax.sharding import PartitionSpec as P

MODEL_WIDTH = 1280
HEADS = 16
HEAD_DIM = 80


EPS = 1e-06
SMALL_COST = pl.CostEstimate(flops=1, bytes_accessed=1, transcendentals=0)
ROPE_BASE = 10000.0


def layout_rows(series_row, pad_row, patch_len):
    count = series_row.shape[0]
    order = jnp.arange(count, dtype=jnp.int32)
    same_series = series_row[:, None] == series_row[None, :]
    earlier = order[None, :] < order[:, None]
    position = jnp.sum(jnp.logical_and(same_series, earlier).astype(jnp.int32), axis=1)
    numbers = jnp.arange(pad_row.shape[0], dtype=jnp.int32)
    series_pad = jnp.sum(
        jnp.where(series_row[:, None] == numbers[None, :], pad_row[None, :], 0), axis=1
    )
    pad_count = jnp.where(position == 0, series_pad, 0)
    padded = pad_count == patch_len
    diagonal = order[:, None] == order[None, :]
    reach = jnp.logical_or(jnp.logical_and(earlier, jnp.logical_not(padded)[None, :]), diagonal)
    allowed = jnp.logical_and(same_series, reach)
    keep_rows = jnp.where(padded, 0.0, 1.0).astype(jnp.float32)
    return (position, pad_count, allowed, keep_rows)


def rotary_tables(position, head_dim):
    half = head_dim // 2
    steps = jnp.arange(half, dtype=jnp.float32) / half
    inverse = jnp.exp(-math.log(ROPE_BASE) * steps)
    angles = position.astype(jnp.float32)[:, None] * inverse[None, :]
    return (jnp.cos(angles)[:, None, :], jnp.sin(angles)[:, None, :])


def rotate(heads_rows, cosine, sine):
    half = heads_rows.shape[-1] // 2
    first = heads_rows[..., :half]
    second = heads_rows[..., half:]
    return jnp.concatenate(
        [first * cosine - second * sine, second * cosine + first * sine], axis=-1
    )


def unrotate(grad_rows, cosine, sine):
    half = grad_rows.shape[-1] // 2
    first = grad_rows[..., :half]
    second = grad_rows[..., half:]
    return jnp.concatenate(
        [first * cosine + second * sine, second * cosine - first * sine], axis=-1
    )


def norm_apply(resid, gain):
    return resid * lax.rsqrt(jnp.mean(resid * resid, axis=-1, keepdims=True) + EPS) * gain


def dyadic_accumulation(left, right):
    return lax.dot_general(
        left, right, (((0,), (0,)), ((), ())), preferred_element_type=jnp.float32
    )


def reverse_matmul_answer(grad_rows, weight):
    return lax.dot_general(
        grad_rows, weight, (((1,), (1,)), ((), ())), preferred_element_type=jnp.float32
    )


def masked_scores(query_rows, key_rows, allowed):
    scale = 1.0 / math.sqrt(query_rows.shape[-1])
    scores = (
        jnp.einsum("qhd,khd->hqk", query_rows, key_rows, preferred_element_type=jnp.float32) * scale
    )
    return jnp.where(allowed[None], scores, -1e30)


def attend_forward(query_rows, key_rows, value_rows, allowed):
    scores = masked_scores(query_rows, key_rows, allowed)
    peak = jnp.max(scores, axis=-1, keepdims=True)
    weights = jnp.exp(scores - peak)
    total = jnp.sum(weights, axis=-1, keepdims=True)
    probs = (weights / total).astype(jnp.bfloat16)
    mixed = jnp.einsum("hqk,khd->qhd", probs, value_rows, preferred_element_type=jnp.float32)
    return (mixed, peak + jnp.log(total))


def attend_backward(query_rows, key_rows, value_rows, allowed, log_total, grad_mixed):
    scale = 1.0 / math.sqrt(query_rows.shape[-1])
    scores = masked_scores(query_rows, key_rows, allowed)
    probs = jnp.where(allowed[None], jnp.exp(scores - log_total), 0.0)
    grad_probs = jnp.einsum(
        "qhd,khd->hqk", grad_mixed, value_rows, preferred_element_type=jnp.float32
    )
    grad_values = jnp.einsum(
        "hqk,qhd->khd", probs.astype(jnp.bfloat16), grad_mixed, preferred_element_type=jnp.float32
    )
    center = jnp.sum(grad_probs * probs, axis=-1, keepdims=True)
    grad_scores = (probs * (grad_probs - center)).astype(jnp.bfloat16)
    grad_query = (
        jnp.einsum("hqk,khd->qhd", grad_scores, key_rows, preferred_element_type=jnp.float32)
        * scale
    )
    grad_keys = (
        jnp.einsum("hqk,qhd->khd", grad_scores, query_rows, preferred_element_type=jnp.float32)
        * scale
    )
    return (grad_query, grad_keys, grad_values)


def after(value, *earlier):
    return lax.optimization_barrier((value, *earlier))[0]


def swap(v, bit):
    size = lax.axis_size("dp")
    return lax.ppermute(v, "dp", [(i, i ^ (1 << bit)) for i in range(size)])


def outer_groups():
    size = lax.axis_size("dp")
    return [[j + 8 * o for o in range(size // 8)] for j in range(8)]


def place_kernel(plan, piece_count, out_count, me_ref, *refs):
    pieces = refs[:piece_count]
    outs = refs[piece_count : piece_count + out_count]
    held = refs[piece_count + out_count : piece_count + 2 * out_count]
    in_sems, out_sems = refs[piece_count + 2 * out_count :]
    inward, outward = [], []
    for n, (piece, rel, row, out, column) in enumerate(plan):
        source = pieces[piece]
        width = held[out].shape[-1]
        if width != source.shape[-1]:
            source = source.at[:, :, pl.ds(column, width)]
        spot = (slice(None), me_ref[0] ^ rel, pl.ds(row, source.shape[1]), slice(None))
        inward.append(pltpu.make_async_copy(source, held[out].at[spot], in_sems.at[n]))
        outward.append(
            pltpu.make_async_copy(held[out].at[spot], outs[out].at[spot], out_sems.at[n])
        )
    for copy in inward:
        copy.start()
    for copy, onward in zip(inward, outward):
        copy.wait()
        onward.start()
    for onward in outward:
        onward.wait()


def place(me, pieces, widths, first=0):
    plan = []
    for n, (rel, row, _) in enumerate(pieces):
        column = first
        for out, width in enumerate(widths):
            plan.append((n, rel, row, out, column))
            column += width
    arrays = [array for _, _, array in pieces]
    lead, rows, _ = arrays[0].shape
    kind = arrays[0].dtype
    total = sum(8 * lead * rows * -(-w // 128) * 128 for w in widths) * 2
    outs = pl.pallas_call(
        partial(place_kernel, plan, len(arrays), len(widths)),
        out_shape=[jax.ShapeDtypeStruct((lead, 8, rows, w), kind) for w in widths],
        in_specs=[pl.BlockSpec(memory_space=pltpu.SMEM)]
        + [pl.BlockSpec(memory_space=pl.ANY)] * len(arrays),
        out_specs=[pl.BlockSpec(memory_space=pl.ANY)] * len(widths),
        scratch_shapes=[pltpu.VMEM((lead, 8, rows, w), kind) for w in widths]
        + [pltpu.SemaphoreType.DMA((len(plan),))] * 2,
        compiler_params=pltpu.CompilerParams(vmem_limit_bytes=total + (4 << 20)),
        cost_estimate=SMALL_COST,
    )(me, *arrays)
    outer = lax.axis_size("dp") // 8
    return [o.reshape(-1, outer * 8 * rows, o.shape[-1]) for o in outs]


def row_half(rows):
    return rows // 32 * 16 if rows >= 32 else rows // 2


def second_step(held, from_x, from_y):
    half = row_half(held.shape[1])
    return from_y[:, :half], from_x[:, half:]


def all_pieces(near, far, near_met, far_met):
    half = far[0].shape[1]
    places = ((0, 0), (2, 0), (4, 0), (6, 0), (6, half))
    pieces = []
    for (rel, row), array, met in zip(places, (*near, *far), (*near_met, *far_met), strict=True):
        pieces += [(rel, row, array), (rel | 1, row, met)]
    return pieces


def spread_rows(held):
    near = (held, swap(held, 1), swap(held, 2))
    onward_x, onward_y = second_step(*near)
    far = (swap(onward_x, 1), swap(onward_y, 2))
    return all_pieces(near, far, [swap(part, 0) for part in near], [swap(part, 0) for part in far])


def gather_head(own):
    held = lax.all_gather(own, "head", axis=0, tiled=True)[None]
    if lax.axis_size("dp") > 8:
        held = lax.all_gather(
            held, "dp", axis=0, tiled=True, axis_index_groups=outer_groups()
        )
    return held


def product_kernel(count, outer, me_ref, *refs):
    lefts, rights, met_lefts, met_rights = (refs[n * count : (n + 1) * count] for n in range(4))
    to_x, to_y, later, own, right_pair, turned = refs[4 * count :]
    rows, width = own.shape[1] // outer, own.shape[-1]
    tokens = lefts[0].shape[0]
    half = width // 2
    tile = half if half <= 640 else 640
    odd = me_ref[0] & 1 == 1
    chip = me_ref[0] >> 1

    def store(rel, n, span, side, columns, total):
        if rel == 0:
            own[n, span, slice(side * half + columns.start, side * half + columns.stop)] = total
        elif rel == 1 and side == 0:
            to_x[1, n, span, columns] = total
        elif rel == 1:
            later[1, n, span, columns] = total
        elif rel == 2 and side == 0:
            later[0, n, span, columns] = total
        elif rel == 2:
            to_y[1, n, span, columns] = total
        elif side == 0:
            to_x[0, n, span, columns] = total
        else:
            to_y[0, n, span, columns] = total

    for n in range(count):
        right_pair[:tokens] = rights[n][...]
        right_pair[tokens:] = met_rights[n][...]
        for part in range(outer):
            span = slice(part * rows, (part + 1) * rows)
            for place in range(4):
                first = (part * 8 + 2 * place) * rows
                near, far = slice(first, first + rows), slice(first + rows, first + 2 * rows)
                left_pair = jnp.concatenate(
                    [
                        jnp.where(odd, side[n][:, far], side[n][:, near]).astype(jnp.float32)
                        for side in (lefts, met_lefts)
                    ],
                    axis=0,
                )
                turned[place] = left_pair.T.astype(own.dtype)
            every = turned[...].reshape(4 * rows, 2 * tokens)
            for side in range(2):
                for at in range(0, half, tile):
                    total = jnp.dot(
                        every,
                        right_pair[:, side * half + at : side * half + at + tile],
                        preferred_element_type=jnp.float32,
                    ).astype(own.dtype)
                    for place in range(4):
                        for rel in range(4):
                            pl.when(chip ^ place == rel)(
                                partial(
                                    store,
                                    rel,
                                    n,
                                    span,
                                    side,
                                    slice(at, at + tile),
                                    total[place * rows : (place + 1) * rows],
                                )
                            )


def exchange(pairs):
    met = {}
    for pair in pairs:
        for rows in pair:
            if id(rows) not in met:
                met[id(rows)] = swap(rows, 0)
    return [(left, right, met[id(left)], met[id(right)]) for left, right in pairs]


def pair_products(me, both):
    outer = lax.axis_size("dp") // 8
    count = len(both)
    left, right = both[0][:2]
    block, width = left.shape[1] // 8, right.shape[1]
    low = jnp.bfloat16
    return pl.pallas_call(
        partial(product_kernel, count, outer),
        out_shape=[
            jax.ShapeDtypeStruct((2, count, block, width // 2), low),
            jax.ShapeDtypeStruct((2, count, block, width // 2), low),
            jax.ShapeDtypeStruct((2, count, block, width // 2), low),
            jax.ShapeDtypeStruct((count, block, width), low),
        ],
        in_specs=[pl.BlockSpec(memory_space=pltpu.SMEM)]
        + [pl.BlockSpec(memory_space=pltpu.VMEM)] * (4 * count),
        out_specs=[pl.BlockSpec(memory_space=pltpu.VMEM)] * 4,
        scratch_shapes=[
            pltpu.VMEM((2 * left.shape[0], width), low),
            pltpu.VMEM((4, block // outer, 2 * left.shape[0]), low),
        ],
        compiler_params=pltpu.CompilerParams(vmem_limit_bytes=44 << 20),
        cost_estimate=SMALL_COST,
    )((me & 7).reshape(1), *[part for parts in zip(*both, strict=True) for part in parts])


def low_sum(*parts):
    total = parts[0].astype(jnp.float32)
    for part in parts[1:]:
        total = total + part.astype(jnp.float32)
    return total.astype(jnp.bfloat16)


class RowSums:
    def __init__(self, to_x, to_y, later, own):
        self.sent, self.later, self.own = (to_x, to_y), later, own

    def first(self):
        return swap(self.sent[0], 1), swap(self.sent[1], 2)

    def last(self):
        return (
            swap(low_sum(self.later[0], self.met[0][0]), 2),
            swap(low_sum(self.later[1], self.met[1][0]), 1),
        )

    def total(self):
        half = self.own.shape[-1] // 2
        return jnp.concatenate(
            [
                low_sum(self.own[..., :half], self.met[0][1], self.last_met[0]),
                low_sum(self.own[..., half:], self.met[1][1], self.last_met[1]),
            ],
            axis=-1,
        )


def sum_group(total):
    outer = lax.axis_size("dp") // 8
    group = lax.axis_size("head")
    lead = total.shape[:-2]
    rows, columns = total.shape[-2:]
    if outer > 1:
        total = lax.psum_scatter(
            total.reshape(*lead, outer, rows // outer, columns),
            "dp",
            scatter_dimension=len(lead),
            tiled=True,
            axis_index_groups=outer_groups(),
        )
    total = total.reshape(*lead, rows // outer, columns)
    return lax.psum_scatter(total, "head", scatter_dimension=len(lead), tiled=True)


def sum_group_at_once(total):
    outer = lax.axis_size("dp") // 8
    group = lax.axis_size("head")
    if outer > 1:
        return sum_group(total).astype(jnp.float32)
    lead = total.shape[:-2]
    rows, columns = total.shape[-2:]
    total = total.reshape(*lead, group, rows // group, columns)
    axis = len(lead)
    met = lax.all_to_all(total, "head", split_axis=axis, concat_axis=axis, tiled=True)
    return jnp.sum(met.astype(jnp.float32), axis=axis)


def sum_columns(total):
    group = lax.axis_size("head")
    if lax.axis_size("dp") > 8:
        total = lax.psum(total, "dp", axis_index_groups=outer_groups())
    count, rows, columns = total.shape
    total = jnp.moveaxis(total.reshape(count, rows, group, columns // group), 2, 0)
    return lax.psum_scatter(total, "head", scatter_dimension=0, tiled=True)[0]


def gather_blocks(me, summed):
    outer = lax.axis_size("dp") // 8
    count, rows, columns = summed.shape
    if outer == 1:
        whole = lax.all_gather(summed, "dp", axis=0)
        return [whole[:, n].reshape(8 * rows, columns) for n in range(count)]
    held = summed.reshape(count * outer, rows // outer, columns)
    return place((me & 7).reshape(1), spread_rows(held), [columns])[0]


EXTRA_ROWS = 8


def entry_products(me, main, extra):
    group = lax.axis_size("head")
    outer = lax.axis_size("dp") // 8
    devices = 8 * outer * group
    columns = main.shape[1]
    own = main.shape[0] // devices
    extra = jnp.pad(extra, ((0, EXTRA_ROWS * devices - extra.shape[0]), (0, 0)))
    rows = jnp.concatenate(
        [main.reshape(devices, own, columns), extra.reshape(devices, EXTRA_ROWS, columns)], axis=1
    ).astype(jnp.bfloat16)
    view = rows.reshape(outer, 4, 2, group * (own + EXTRA_ROWS), columns)
    core = me & 1
    other = lax.dynamic_index_in_dim(view, 1 - core, 2, keepdims=False)
    pair = low_sum(lax.dynamic_index_in_dim(view, core, 2, keepdims=False), swap(other, 0))
    chip = (me & 7) >> 1
    half = columns // 2

    def picked(rel):
        return lax.dynamic_index_in_dim(pair, chip ^ rel, 1, keepdims=False).reshape(-1, columns)

    own_rows, at_x, at_y, far = (picked(rel) for rel in range(4))
    return RowSums(
        jnp.stack([far[:, :half], at_x[:, :half]]),
        jnp.stack([far[:, half:], at_y[:, half:]]),
        (at_y[:, :half], at_x[:, half:]),
        own_rows,
    )


def silu_parts(x):
    gate = 1.0 / (1.0 + jnp.exp(-x))
    return x * gate, gate * (1.0 + x * (1.0 - gate))


def output_kernel(
    plan, me_ref, top_ref, keep_ref, latent_offset, emit_offset, sensitivity, *refs
):
    pieces = refs[: len(plan)]
    hidden_ref, forecast_ref, pre_low_ref, grad_ref, bias_ref = refs[len(plan) : len(plan) + 5]
    whole, pre, skips, sent, both, sems = refs[len(plan) + 5 :]
    group, width, _ = whole.shape
    each = sensitivity.shape[2]
    two = 2 * each
    rows = width // 8
    copies = []
    for part in range(group):
        copies.append([])
        for n, (rel, row, count) in enumerate(plan):
            first = pl.multiple_of((me_ref[0] ^ rel) * rows + row, 16)
            spot = whole.at[part, pl.ds(first, count), :]
            sem = sems.at[part * len(plan) + n]
            copies[part].append(pltpu.make_async_copy(pieces[n].at[part], spot, sem))
            copies[part][n].start()
    top = top_ref[...]
    keep = keep_ref[...]
    for part in range(group):
        arrive(copies[part])
        both[...] = jnp.dot(top, whole[part, :, :two], preferred_element_type=jnp.float32)
        pre[:, part * each : (part + 1) * each] = both[:, :each] + latent_offset[part : part + 1]
        skips[part] = both[:, each:two] + emit_offset[part : part + 1]
    hidden, slope = silu_parts(pre[...])
    hidden = hidden.astype(jnp.bfloat16)
    hidden_ref[...] = hidden
    for part in range(group):
        emitted = jnp.dot(hidden, whole[part, :, two:], preferred_element_type=jnp.float32)
        forecast_ref[part] = ((emitted + skips[part]) * keep).astype(jnp.bfloat16)

    def back_hidden(n, _):
        at = pl.multiple_of(n * 256, 256)
        total = reverse_matmul_answer(whole[0, pl.ds(at, 256), two:], sensitivity[0])
        for part in range(1, group):
            total += reverse_matmul_answer(whole[part, pl.ds(at, 256), two:], sensitivity[part])
        grad_ref[:, pl.ds(at, 256)] = total.T
        return 0

    lax.fori_loop(0, width // 256, back_hidden, 0)
    pre[...] = grad_ref[...] * slope
    pre_low_ref[...] = pre[...].astype(jnp.bfloat16)
    bias_ref[...] = jnp.sum(pre_low_ref[...].astype(jnp.float32), axis=0, keepdims=True)
    for part in range(group):
        both[:, :each] = pre[:, part * each : (part + 1) * each]
        both[:, each:] = sensitivity[part].astype(jnp.float32)
        sent[part] = both[...].astype(jnp.bfloat16)

    def back_top(n, _):
        at = pl.multiple_of(n * 256, 256)
        total = reverse_matmul_answer(whole[0, pl.ds(at, 256), :two], sent[0])
        for part in range(1, group):
            total += reverse_matmul_answer(whole[part, pl.ds(at, 256), :two], sent[part])
        grad_ref[:, pl.ds(at, 256)] = total.T
        return 0

    lax.fori_loop(0, width // 256, back_top, 0)


def output_block(me, pieces, top, keep, latent_offsets, emit_offsets, grad_forecast):
    plan = [(rel, row, array.shape[1]) for rel, row, array in pieces]
    group, rows, each = grad_forecast.shape
    width = top.shape[1]
    vmem = pl.BlockSpec(memory_space=pltpu.VMEM)
    return pl.pallas_call(
        partial(output_kernel, plan),
        out_shape=[
            jax.ShapeDtypeStruct((rows, width), LOW),
            jax.ShapeDtypeStruct((group, rows, each), LOW),
            jax.ShapeDtypeStruct((rows, width), LOW),
            jax.ShapeDtypeStruct((rows, width), FULL),
            jax.ShapeDtypeStruct((1, width), FULL),
        ],
        in_specs=[pl.BlockSpec(memory_space=pltpu.SMEM)]
        + [vmem] * 5
        + [pl.BlockSpec(memory_space=pl.ANY)] * len(pieces),
        out_specs=[vmem] * 5,
        scratch_shapes=[
            pltpu.VMEM((group, width, 3 * each), LOW),
            pltpu.VMEM((rows, width), FULL),
            pltpu.VMEM((group, rows, each), FULL),
            pltpu.VMEM((group, rows, 2 * each), LOW),
            pltpu.VMEM((rows, 2 * each), FULL),
            pltpu.SemaphoreType.DMA((group * len(pieces),)),
        ],
        compiler_params=pltpu.CompilerParams(vmem_limit_bytes=44 << 20),
        cost_estimate=SMALL_COST,
    )(
        me,
        top,
        keep,
        latent_offsets,
        emit_offsets,
        grad_forecast,
        *[array for _, _, array in pieces],
    )


def output_plain(head_whole, top, keep, latent_offsets, emit_offsets, grad_forecast):
    group, _, each = grad_forecast.shape
    two = 2 * each
    inner_parts = [
        jnp.dot(top, head_whole[part][:, :two], preferred_element_type=jnp.float32)
        for part in range(group)
    ]
    head_pre = jnp.concatenate(
        [inner_parts[part][:, :each] + latent_offsets[part] for part in range(group)], axis=1
    )
    hidden, slope = silu_parts(head_pre)
    hidden = hidden.astype(jnp.bfloat16)
    forecast = jnp.stack(
        [
            (
                jnp.dot(hidden, head_whole[part][:, two:], preferred_element_type=jnp.float32)
                + emit_offsets[part]
                + inner_parts[part][:, each:]
            )
            * keep
            for part in range(group)
        ]
    ).astype(jnp.bfloat16)
    grad_hidden = sum(
        reverse_matmul_answer(grad_forecast[part], head_whole[part][:, two:])
        for part in range(group)
    )
    pre_low = (grad_hidden * slope).astype(jnp.bfloat16)
    grad_top = sum(
        reverse_matmul_answer(
            jnp.concatenate(
                [pre_low[:, part * each : (part + 1) * each], grad_forecast[part]], axis=1
            ),
            head_whole[part][:, :two],
        )
        for part in range(group)
    )
    return hidden, forecast, pre_low, grad_top, jnp.sum(pre_low.astype(FULL), axis=0, keepdims=True)


def input_back_kernel(
    grad_ref, pre_ref, emit_ref, latent_ref, shortcut_ref, low_ref, pre_low_ref, sent_ref, bias_ref, wide
):
    low = grad_ref[...].astype(jnp.bfloat16)
    low_ref[...] = low
    rows_times_turned(low, emit_ref, 0, emit_ref.shape[1], wide, 256)
    pre = pre_ref[...]
    gate = 1.0 / (1.0 + jnp.exp(-pre))
    pre_low = (wide[...] * (gate * (1.0 + pre * (1.0 - gate)))).astype(jnp.bfloat16)
    pre_low_ref[...] = pre_low
    sent_ref[...] = reverse_matmul_answer(pre_low, latent_ref[...]) + reverse_matmul_answer(
        low, shortcut_ref[...]
    )
    bias_ref[0:1] = jnp.sum(pre_low.astype(jnp.float32), axis=0, keepdims=True)
    bias_ref[1:2] = jnp.sum(low.astype(jnp.float32), axis=0, keepdims=True)


def input_products_kernel(group, me_ref, *refs):
    hidden, met_hidden, low, met_low, pre_low, met_pre_low, features, met_features = refs[:8]
    vectors, met_vectors, to_x, to_y, later, own = refs[8:14]
    turned, low_pair, extras, block = refs[14:]
    tokens = hidden.shape[0]
    columns = low.shape[1]
    half = columns // 2
    core, chip = me_ref[0] & 1, me_ref[0] >> 1
    turned[:, :tokens] = hidden[...].astype(jnp.float32).T.astype(jnp.bfloat16)
    turned[:, tokens:] = met_hidden[...].astype(jnp.float32).T.astype(jnp.bfloat16)
    low_pair[:tokens] = low[...]
    low_pair[tokens:] = met_low[...]
    wide = features.shape[1]
    extras[...] = jnp.zeros_like(extras)
    extras[:wide] = dyadic_accumulation(features[...], pre_low[...]) + dyadic_accumulation(
        met_features[...], met_pre_low[...]
    )
    extras[wide : 2 * wide] = dyadic_accumulation(features[...], low[...]) + dyadic_accumulation(
        met_features[...], met_low[...]
    )
    extras[2 * wide : 2 * wide + vectors.shape[0]] = vectors[...] + met_vectors[...]
    rows = hidden.shape[1] // 8
    each = rows // group
    span = each + EXTRA_ROWS

    def store(rel, total):
        if rel == 0:
            own[0] = total
        elif rel == 1:
            to_x[1, 0] = total[:, :half]
            later[1, 0] = total[:, half:]
        elif rel == 2:
            later[0, 0] = total[:, :half]
            to_y[1, 0] = total[:, half:]
        else:
            to_x[0, 0] = total[:, :half]
            to_y[0, 0] = total[:, half:]

    for place in range(4):
        number = 2 * place + core
        first = pl.multiple_of(number * rows, rows)
        outer = jnp.dot(
            turned[pl.ds(first, rows), :], low_pair[...], preferred_element_type=jnp.float32
        )
        first = pl.multiple_of(number * group * EXTRA_ROWS, group * EXTRA_ROWS)
        extra = extras[pl.ds(first, group * EXTRA_ROWS), :]
        for member in range(group):
            block[member * span : member * span + each] = outer[member * each : (member + 1) * each]
            block[member * span + each : (member + 1) * span] = extra[
                member * EXTRA_ROWS : (member + 1) * EXTRA_ROWS
            ]
        total = block[...].astype(own.dtype)
        for rel in range(4):
            pl.when(chip ^ place == rel)(partial(store, rel, total))


def input_back(grad, pre, emit, latent, shortcut):
    rows, columns = grad.shape
    vmem = pl.BlockSpec(memory_space=pltpu.VMEM)
    return pl.pallas_call(
        input_back_kernel,
        out_shape=[
            jax.ShapeDtypeStruct((rows, columns), LOW),
            jax.ShapeDtypeStruct((rows, columns), LOW),
            jax.ShapeDtypeStruct((rows, latent.shape[0]), FULL),
            jax.ShapeDtypeStruct((2, columns), FULL),
        ],
        in_specs=[vmem] * 5,
        out_specs=[vmem] * 4,
        scratch_shapes=[pltpu.VMEM((rows, columns), FULL)],
        compiler_params=pltpu.CompilerParams(vmem_limit_bytes=32 << 20),
        cost_estimate=SMALL_COST,
    )(grad, pre, emit, latent, shortcut)


def input_products(me, operands):
    group = lax.axis_size("head")
    tokens, columns = operands[2].shape
    width = operands[0].shape[1]
    block = width // 8 + group * EXTRA_ROWS
    pair = jax.ShapeDtypeStruct((2, 1, block, columns // 2), LOW)
    return RowSums(
        *pl.pallas_call(
            partial(input_products_kernel, group),
            out_shape=[pair, pair, pair, jax.ShapeDtypeStruct((1, block, columns), LOW)],
            in_specs=[pl.BlockSpec(memory_space=pltpu.SMEM)]
            + [pl.BlockSpec(memory_space=pltpu.VMEM)] * len(operands),
            out_specs=[pl.BlockSpec(memory_space=pltpu.VMEM)] * 4,
            scratch_shapes=[
                pltpu.VMEM((width, 2 * tokens), LOW),
                pltpu.VMEM((2 * tokens, columns), LOW),
                pltpu.VMEM((8 * group * EXTRA_ROWS, columns), FULL),
                pltpu.VMEM((block, columns), FULL),
            ],
            compiler_params=pltpu.CompilerParams(vmem_limit_bytes=32 << 20),
            cost_estimate=SMALL_COST,
        )((me & 7).reshape(1), *operands)
    )


def entry_kernel(plan, own, me_ref, *refs):
    pieces = refs[: len(plan)]
    main_ref, extra_ref, held, sems = refs[len(plan) :]
    copies = []
    for n, (rel, row, rows) in enumerate(plan):
        spot = held.at[me_ref[0] ^ rel, pl.ds(row, rows)]
        copies.append(pltpu.make_async_copy(pieces[n].at[0], spot, sems.at[n]))
    for copy in copies:
        copy.start()
    for copy in copies:
        copy.wait()
    span = own + EXTRA_ROWS
    group = held.shape[1] // span
    for block in range(8):
        rows = held[block].astype(jnp.float32)
        for member in range(group):
            main_ref[block * group + member] = rows[member * span : member * span + own]
            extra_ref[block * group + member] = rows[member * span + own : (member + 1) * span]


def entry_sums_of_group(total):
    total = total.reshape(-1, total.shape[-1])
    return sum_group_at_once(total).astype(total.dtype)


def entry_everywhere(me, summed, own, count):
    columns = summed.shape[-1]
    group = lax.axis_size("head")
    if lax.axis_size("dp") > 8:
        held = gather_head(summed)
    else:
        every = jnp.broadcast_to(summed[None], (group, *summed.shape))
        held = lax.all_to_all(every, "head", split_axis=0, concat_axis=0, tiled=True)
        held = held.reshape(1, -1, columns)
    pieces = spread_rows(held)
    places = (me & 7).reshape(1)
    span = own + EXTRA_ROWS
    if held.shape[0] > 1 or own % 8 or not in_kernel(pieces):
        (whole,) = place(places, pieces, [columns])
        whole = whole.reshape(-1, span, columns).astype(jnp.float32)
        return whole[:, :own].reshape(-1, columns), whole[:, own:].reshape(-1, columns)[:count]
    rows = held.shape[1]
    blocks = 8 * rows // span
    plan = [(rel, row, array.shape[1]) for rel, row, array in pieces]
    vmem = pl.BlockSpec(memory_space=pltpu.VMEM)
    main, extra = pl.pallas_call(
        partial(entry_kernel, plan, own),
        out_shape=[
            jax.ShapeDtypeStruct((blocks, own, columns), jnp.float32),
            jax.ShapeDtypeStruct((blocks, EXTRA_ROWS, columns), jnp.float32),
        ],
        in_specs=[pl.BlockSpec(memory_space=pltpu.SMEM)]
        + [pl.BlockSpec(memory_space=pl.ANY)] * len(pieces),
        out_specs=[vmem, vmem],
        scratch_shapes=[
            pltpu.VMEM((8, rows, columns), held.dtype),
            pltpu.SemaphoreType.DMA((len(pieces),)),
        ],
        compiler_params=pltpu.CompilerParams(vmem_limit_bytes=44 << 20),
        cost_estimate=SMALL_COST,
    )(places, *[array for _, _, array in pieces])
    return main.reshape(-1, columns), extra.reshape(-1, columns)[:count]


def fetch(plan, me, pieces, whole, sems):
    groups = []
    for group in range(whole.shape[1] // MODEL_WIDTH):
        columns = pl.ds(group * MODEL_WIDTH, MODEL_WIDTH)
        copies = []
        for n, (rel, row, rows) in enumerate(plan):
            first = pl.multiple_of((me ^ rel) * (whole.shape[0] // 8) + row, 16)
            copies.append(
                pltpu.make_async_copy(
                    pieces[n].at[0, :, columns],
                    whole.at[pl.ds(first, rows), columns],
                    sems.at[group * len(plan) + n],
                )
            )
        for copy in copies:
            copy.start()
        groups.append(copies)
    return groups


def arrive(copies):
    for copy in copies:
        copy.wait()


def rows_times(left, whole, first, out, tile):
    def step(n, _):
        at = pl.multiple_of(n * tile, 128)
        out[:, pl.ds(at, tile)] = jnp.dot(
            left, whole[:, pl.ds(first + at, tile)], preferred_element_type=jnp.float32
        )
        return 0

    lax.fori_loop(0, out.shape[1] // tile, step, 0)


def rows_times_turned(left, whole, first, width, out, tile):
    def step(n, _):
        at = pl.multiple_of(n * tile, 128)
        part = reverse_matmul_answer(whole[pl.ds(at, tile), pl.ds(first, width)], left)
        out[:, pl.ds(at, tile)] = part.T
        return 0

    lax.fori_loop(0, out.shape[1] // tile, step, 0)


def inverse_norm(rows):
    return lax.rsqrt(jnp.mean(rows * rows, axis=-1, keepdims=True) + EPS)


def other_half(rows):
    half = HEAD_DIM // 2
    lane = lax.broadcasted_iota(jnp.int32, rows.shape, 1) % HEAD_DIM
    ahead = pltpu.roll(rows, rows.shape[1] - half, 1)
    behind = pltpu.roll(rows, half, 1)
    return jnp.where(lane < half, ahead, behind)


def head_window(head, width):
    first = head * HEAD_DIM // 128 * 128
    last = min(-(-(head + 1) * HEAD_DIM // 128) * 128, width)
    start = head * HEAD_DIM - first
    lane = lax.broadcasted_iota(jnp.int32, (1, last - first), 1)
    return slice(first, last), jnp.logical_and(lane >= start, lane < start + HEAD_DIM)


def entry_forward_kernel(plan, me_ref, resid_ref, gain_ref, cosine_ref, sine_ref, allowed_ref, *refs):
    pieces = refs[: len(plan)]
    normed_ref, query_ref, key_ref, value_ref, total_ref, mixed_ref = refs[len(plan) : len(plan) + 6]
    whole, wide, sems = refs[len(plan) + 6 :]
    groups = fetch(plan, me_ref[0], pieces, whole, sems)
    resid = resid_ref[...]
    normed = (resid * inverse_norm(resid) * gain_ref[...]).astype(jnp.bfloat16)
    normed_ref[...] = normed
    for group, out in enumerate((query_ref, key_ref, value_ref)):
        arrive(groups[group])
        rows_times(normed, whole, group * MODEL_WIDTH, wide, 256)
        rows = wide[...]
        if group < 2:
            rows = rows * cosine_ref[...] + other_half(rows) * sine_ref[...]
        out[...] = rows.astype(jnp.bfloat16)
    scale = 1.0 / math.sqrt(HEAD_DIM)
    allowed = allowed_ref[...] > 0.0
    wide[...] = jnp.zeros_like(wide)
    totals = jnp.zeros(total_ref.shape, jnp.float32)
    head_lane = lax.broadcasted_iota(jnp.int32, total_ref.shape, 1)
    for head in range(HEADS):
        window, inside = head_window(head, MODEL_WIDTH)
        query = jnp.where(inside, query_ref[:, window], 0)
        scores = reverse_matmul_answer(query, key_ref[:, window]) * scale
        scores = jnp.where(allowed, scores, -1e30)
        peak = jnp.max(scores, axis=-1, keepdims=True)
        weights = jnp.exp(scores - peak)
        total = jnp.sum(weights, axis=-1, keepdims=True)
        probs = (weights / total).astype(jnp.bfloat16)
        mixed = jnp.dot(probs, value_ref[:, window], preferred_element_type=jnp.float32)
        wide[:, window] += jnp.where(inside, mixed, 0.0)
        totals = jnp.where(head_lane == head, peak + jnp.log(total), totals)
    total_ref[...] = totals
    mixed_ref[...] = wide[...].astype(jnp.bfloat16)


def gelu_parts(x):
    root = math.sqrt(2.0 / math.pi)
    bend = jnp.tanh(root * (x + 0.044715 * (x * x * x)))
    slope = 0.5 * (1.0 + bend) + 0.5 * x * (1.0 - bend * bend) * root * (
        1.0 + 3.0 * 0.044715 * (x * x)
    )
    return 0.5 * x * (1.0 + bend), slope


def rest_forward_kernel(plan, me_ref, resid_ref, mixed_ref, gain_ref, *refs):
    pieces = refs[: len(plan)]
    result_ref, middle_ref, normed_ref, pre_ref = refs[len(plan) : len(plan) + 4]
    whole, sems = refs[len(plan) + 4 :]
    groups = fetch(plan, me_ref[0], pieces, whole, sems)
    arrive(groups[0])
    rows_times(mixed_ref[...], whole, 0, middle_ref, 256)
    middle = resid_ref[...] + middle_ref[...]
    middle_ref[...] = middle
    normed = (middle * inverse_norm(middle) * gain_ref[...]).astype(jnp.bfloat16)
    normed_ref[...] = normed
    arrive(groups[1])
    rows_times(normed, whole, MODEL_WIDTH, pre_ref, 256)
    act = gelu_parts(pre_ref[...])[0].astype(jnp.bfloat16)
    arrive(groups[2])
    rows_times(act, whole, 2 * MODEL_WIDTH, result_ref, 256)
    result_ref[...] += middle_ref[...]


def norm_back(rows, gain, grad):
    inverse = inverse_norm(rows)
    scaled = grad * gain
    mean = jnp.mean(rows * scaled, axis=-1, keepdims=True)
    sent = inverse * scaled - rows * (inverse * inverse * inverse * mean)
    return sent, jnp.sum(grad * rows * inverse, axis=0, keepdims=True)


def rest_backward_kernel(plan, me_ref, grad_ref, middle_ref, pre_ref, gain_ref, *refs):
    pieces = refs[: len(plan)]
    outs = refs[len(plan) : len(plan) + 7]
    grad_middle_ref, mixed_ref, attn_ref, grad_pre_ref, branch_ref, act_ref, gain_grad_ref = outs
    whole, wide, sems = refs[len(plan) + 7 :]
    groups = fetch(plan, me_ref[0], pieces, whole, sems)
    grad = grad_ref[...]
    branch = grad.astype(jnp.bfloat16)
    branch_ref[...] = branch
    arrive(groups[2])
    rows_times_turned(branch, whole, 2 * MODEL_WIDTH, MODEL_WIDTH, wide, 256)
    act, slope = gelu_parts(pre_ref[...])
    act_ref[...] = act.astype(jnp.bfloat16)
    grad_pre = (wide[...] * slope).astype(jnp.bfloat16)
    grad_pre_ref[...] = grad_pre
    arrive(groups[1])
    rows_times_turned(grad_pre, whole, MODEL_WIDTH, MODEL_WIDTH, wide, 256)
    sent, gain_grad_ref[...] = norm_back(middle_ref[...], gain_ref[...], wide[...])
    grad_middle = grad + sent
    grad_middle_ref[...] = grad_middle
    attn = grad_middle.astype(jnp.bfloat16)
    attn_ref[...] = attn
    arrive(groups[0])
    rows_times_turned(attn, whole, 0, MODEL_WIDTH, wide, 256)
    mixed_ref[...] = wide[...].astype(jnp.bfloat16)


def entry_backward_kernel(
    plan,
    me_ref,
    grad_middle_ref,
    grad_mixed_ref,
    resid_ref,
    query_ref,
    key_ref,
    value_ref,
    total_ref,
    gain_ref,
    cosine_ref,
    sine_ref,
    allowed_ref,
    *refs,
):
    pieces = refs[: len(plan)]
    grad_resid_ref, projected_ref, gain_grad_ref = refs[len(plan) : len(plan) + 3]
    whole, grad_query, grad_key, grad_value, sems = refs[len(plan) + 3 :]
    groups = fetch(plan, me_ref[0], pieces, whole, sems)
    scale = 1.0 / math.sqrt(HEAD_DIM)
    allowed = allowed_ref[...] > 0.0
    totals = total_ref[...]
    grad_query[...] = jnp.zeros_like(grad_query)
    grad_key[...] = jnp.zeros_like(grad_key)
    grad_value[...] = jnp.zeros_like(grad_value)
    for head in range(HEADS):
        window, inside = head_window(head, MODEL_WIDTH)
        query = jnp.where(inside, query_ref[:, window], 0)
        keys = key_ref[:, window]
        grad_mixed = jnp.where(inside, grad_mixed_ref[:, window], 0)
        scores = reverse_matmul_answer(query, keys) * scale
        probs = jnp.where(allowed, jnp.exp(scores - totals[:, head : head + 1]), 0.0)
        grad_probs = reverse_matmul_answer(grad_mixed, value_ref[:, window])
        grad_value[:, window] += dyadic_accumulation(probs.astype(jnp.bfloat16), grad_mixed)
        center = jnp.sum(grad_probs * probs, axis=-1, keepdims=True)
        grad_scores = (probs * (grad_probs - center)).astype(jnp.bfloat16)
        along = jnp.dot(grad_scores, keys, preferred_element_type=jnp.float32)
        grad_query[:, window] += jnp.where(inside, along * scale, 0.0)
        grad_key[:, window] += dyadic_accumulation(grad_scores, query) * scale
    for group, part in enumerate((grad_query, grad_key, grad_value)):
        rows = part[...]
        if group < 2:
            rows = rows * cosine_ref[...] - other_half(rows) * sine_ref[...]
        projected_ref[:, group * MODEL_WIDTH : (group + 1) * MODEL_WIDTH] = rows.astype(jnp.bfloat16)
    for copies in groups:
        arrive(copies)
    rows_times_turned(projected_ref[...], whole, 0, 3 * MODEL_WIDTH, grad_query, 256)
    sent, gain_grad_ref[...] = norm_back(resid_ref[...], gain_ref[...], grad_query[...])
    grad_resid_ref[...] = grad_middle_ref[...] + sent


def whole_call(kernel, me, pieces, inputs, outs, wides):
    rows = inputs[0].shape[0]
    plan = [(rel, row, array.shape[1]) for rel, row, array in pieces]
    blocks = 8 * pieces[0][2].shape[1]
    columns = 3 * MODEL_WIDTH
    vmem = pl.BlockSpec(memory_space=pltpu.VMEM)
    return pl.pallas_call(
        partial(kernel, plan),
        out_shape=[jax.ShapeDtypeStruct(shape, kind) for shape, kind in outs],
        in_specs=[pl.BlockSpec(memory_space=pltpu.SMEM)]
        + [vmem] * len(inputs)
        + [pl.BlockSpec(memory_space=pl.ANY)] * len(pieces),
        out_specs=[vmem] * len(outs),
        scratch_shapes=[pltpu.VMEM((blocks, columns), jnp.bfloat16)]
        + [pltpu.VMEM((rows, MODEL_WIDTH), jnp.float32)] * wides
        + [pltpu.SemaphoreType.DMA((3 * len(pieces),))],
        compiler_params=pltpu.CompilerParams(vmem_limit_bytes=44 << 20),
        cost_estimate=SMALL_COST,
    )(me, *inputs, *[array for _, _, array in pieces])


def in_kernel(pieces):
    lead, rows, _ = pieces[0][2].shape
    return lead == 1 and rows % 32 == 0


LOW, FULL = jnp.bfloat16, jnp.float32


class Layer:
    def __init__(self, places, entry_pieces, gains, tables, allowed):
        self.places, self.entry_pieces, self.gains = places, entry_pieces, gains
        self.tables, self.allowed = tables, allowed
        self.fetched = in_kernel(entry_pieces)
        if not self.fetched:
            self.entry_whole = place(places, entry_pieces, [3 * MODEL_WIDTH])[0][0]

    def add_rest(self, rest_pieces):
        self.rest_pieces = rest_pieces
        if not self.fetched:
            self.rest_whole = [part[0] for part in place(self.places, rest_pieces, [MODEL_WIDTH] * 3)]

    def shapes(self, *kinds):
        rows = self.allowed.shape[0]
        return [((rows, width), kind) for width, kind in kinds]

    def entry_forward(self, resid):
        if not self.fetched:
            self.saved = entry_forward(
                resid, self.entry_whole, self.gains, *self.tables[:2], self.allowed
            )
            return self.saved[6]
        wide = (MODEL_WIDTH, LOW)
        self.resid = resid
        outs = whole_call(
            entry_forward_kernel,
            self.places,
            self.entry_pieces,
            (resid, self.gains[:1].astype(FULL), *self.tables[2:], self.allowed.astype(FULL)),
            self.shapes(wide, wide, wide, wide, (128, FULL), wide),
            1,
        )
        self.normed_first, self.heads = outs[0], outs[1:5]
        return outs[5]

    def rest_forward(self, mixed):
        if not self.fetched:
            result, self.saved = rest_forward(
                (*self.saved[:6], mixed), *self.rest_whole, self.gains
            )
            return result
        self.mixed = mixed
        result, self.middle, self.normed_second, self.hidden_pre = whole_call(
            rest_forward_kernel,
            self.places,
            self.rest_pieces,
            (self.resid, mixed, self.gains[1:].astype(FULL)),
            self.shapes(
                (MODEL_WIDTH, FULL), (MODEL_WIDTH, FULL), (MODEL_WIDTH, LOW), (MODEL_WIDTH, FULL)
            ),
            0,
        )
        return result

    def rest_backward(self, grad):
        if not self.fetched:
            weights = (self.entry_whole, *self.rest_whole, self.gains)
            return rest_backward(self.saved, weights, grad)
        wide = (MODEL_WIDTH, LOW)
        grad_middle, grad_mixed, grad_attn, grad_pre, branch, act, gain_grad = whole_call(
            rest_backward_kernel,
            self.places,
            self.rest_pieces,
            (grad, self.middle, self.hidden_pre, self.gains[1:].astype(FULL)),
            self.shapes((MODEL_WIDTH, FULL), wide, wide, wide, wide, wide)
            + [((1, MODEL_WIDTH), FULL)],
            1,
        )
        lefts = (self.mixed, self.normed_second, act)
        return grad_middle, grad_mixed, lefts, (grad_attn, grad_pre, branch), gain_grad[0]

    def entry_backward(self, grad_middle, grad_mixed):
        if not self.fetched:
            weights = (self.entry_whole, *self.rest_whole, self.gains)
            return entry_backward(
                self.saved, weights, *self.tables[:2], self.allowed, grad_middle, grad_mixed
            )
        grad_resid, projected, gain_grad = whole_call(
            entry_backward_kernel,
            self.places,
            self.entry_pieces,
            (
                grad_middle,
                grad_mixed,
                self.resid,
                *self.heads,
                self.gains[:1].astype(FULL),
                *self.tables[2:],
                self.allowed.astype(FULL),
            ),
            self.shapes((MODEL_WIDTH, FULL), (3 * MODEL_WIDTH, LOW)) + [((1, MODEL_WIDTH), FULL)],
            3,
        )
        return grad_resid, self.normed_first, projected, gain_grad[0]


def entry_forward(resid, qkv_full, gain_pair, cosine, sine, allowed):
    gains = gain_pair.astype(jnp.float32)
    rows = resid.shape[0]
    normed_first = norm_apply(resid, gains[0]).astype(jnp.bfloat16)
    projected = jnp.dot(normed_first, qkv_full, preferred_element_type=jnp.float32)
    query_rows = rotate(
        projected[:, :MODEL_WIDTH].reshape(rows, HEADS, HEAD_DIM), cosine, sine
    ).astype(jnp.bfloat16)
    key_rows = rotate(
        projected[:, MODEL_WIDTH : 2 * MODEL_WIDTH].reshape(rows, HEADS, HEAD_DIM), cosine, sine
    ).astype(jnp.bfloat16)
    value_rows = projected[:, 2 * MODEL_WIDTH :].reshape(rows, HEADS, HEAD_DIM).astype(jnp.bfloat16)

    mixed, log_total = attend_forward(query_rows, key_rows, value_rows, allowed)
    mixed_low = mixed.reshape(rows, MODEL_WIDTH).astype(jnp.bfloat16)
    return (resid, normed_first, query_rows, key_rows, value_rows, log_total, mixed_low)


def rest_forward(saved, out_full, up_full, down_full, gain_pair):
    gains = gain_pair.astype(jnp.float32)
    resid, mixed_low = saved[0], saved[6]
    middle = resid + jnp.dot(mixed_low, out_full, preferred_element_type=jnp.float32)
    normed_second = norm_apply(middle, gains[1]).astype(jnp.bfloat16)
    hidden_pre = jnp.dot(normed_second, up_full, preferred_element_type=jnp.float32)
    hidden_act = jax.nn.gelu(hidden_pre, approximate=True).astype(jnp.bfloat16)
    result = middle + jnp.dot(hidden_act, down_full, preferred_element_type=jnp.float32)
    return (result, (*saved, middle, normed_second, hidden_pre))


def rest_backward(saved, weights, grad_result):
    mixed_low, middle, normed_second, hidden_pre = saved[6:]
    _, out_full, up_full, down_full, gain_pair = weights
    gains = gain_pair.astype(jnp.float32)
    grad_branch = grad_result.astype(jnp.bfloat16)
    hidden_act, gelu_pull = jax.vjp(partial(jax.nn.gelu, approximate=True), hidden_pre)
    hidden_low = hidden_act.astype(jnp.bfloat16)
    grad_act = reverse_matmul_answer(grad_branch, down_full)
    grad_pre = gelu_pull(grad_act)[0].astype(jnp.bfloat16)
    grad_normed_second = reverse_matmul_answer(grad_pre, up_full)
    unused_second, second_pull = jax.vjp(norm_apply, middle, gains[1])
    grad_middle_norm, grad_gain_second = second_pull(grad_normed_second)
    grad_middle = grad_result + grad_middle_norm
    grad_attn = grad_middle.astype(jnp.bfloat16)
    grad_mixed = reverse_matmul_answer(grad_attn, out_full).astype(jnp.bfloat16)
    left_rows = (mixed_low, normed_second, hidden_low)
    right_rows = (grad_attn, grad_pre, grad_branch)
    return (grad_middle, grad_mixed, left_rows, right_rows, grad_gain_second)


def entry_backward(saved, weights, cosine, sine, allowed, grad_middle, grad_mixed):
    resid, normed_first, query_rows, key_rows, value_rows, log_total = saved[:6]
    qkv_full = weights[0]
    gains = weights[4].astype(jnp.float32)
    rows = resid.shape[0]
    grad_query, grad_keys, grad_values = attend_backward(
        query_rows,
        key_rows,
        value_rows,
        allowed,
        log_total,
        grad_mixed.reshape(rows, HEADS, HEAD_DIM),
    )
    grad_query = unrotate(grad_query, cosine, sine).reshape(rows, MODEL_WIDTH)
    grad_keys = unrotate(grad_keys, cosine, sine).reshape(rows, MODEL_WIDTH)
    grad_values = grad_values.reshape(rows, MODEL_WIDTH)
    grad_projected = jnp.concatenate([grad_query, grad_keys, grad_values], axis=1).astype(
        jnp.bfloat16
    )
    grad_normed_first = reverse_matmul_answer(grad_projected, qkv_full)
    unused_first, first_pull = jax.vjp(norm_apply, resid, gains[0])
    grad_resid_norm, grad_gain_first = first_pull(grad_normed_first)
    return (grad_middle + grad_resid_norm, normed_first, grad_projected, grad_gain_first)


def body(
    patch_observations,
    sequence_labels,
    leading_filler_count,
    intake_latent_matrix,
    intake_latent_offset,
    intake_emit_matrix,
    intake_emit_offset,
    intake_shortcut_matrix,
    attention_entry_matrices,
    attention_merge_matrix,
    feedforward_widen_matrix,
    feedforward_shrink_matrix,
    layer_scale_factors,
    readout_latent_matrix,
    readout_latent_offset,
    readout_emit_matrix,
    readout_emit_offset,
    readout_shortcut_matrix,
    loss_sensitivity,
):
    patch_len = patch_observations.shape[1]
    position, pad_count, allowed, keep_rows = layout_rows(
        sequence_labels[0], leading_filler_count[0], patch_len
    )
    cosine, sine = rotary_tables(position, HEAD_DIM)
    columns = jnp.arange(patch_len, dtype=jnp.int32)
    pad_mask = columns[None, :] < pad_count[:, None]
    features = jnp.concatenate(
        [
            jnp.where(pad_mask, jnp.zeros_like(patch_observations), patch_observations),
            pad_mask.astype(jnp.bfloat16),
        ],
        axis=1,
    )
    entry_pre = (
        jnp.dot(features, intake_latent_matrix, preferred_element_type=jnp.float32)
        + intake_latent_offset
    )
    entry_hidden = jax.nn.silu(entry_pre).astype(jnp.bfloat16)
    resid = (
        jnp.dot(entry_hidden, intake_emit_matrix, preferred_element_type=jnp.float32)
        + intake_emit_offset
        + jnp.dot(features, intake_shortcut_matrix, preferred_element_type=jnp.float32)
    )
    layer_count = attention_entry_matrices.shape[0]
    group = lax.axis_size("head")
    group_place = lax.axis_index("head")
    outer = lax.axis_size("dp") // 8
    me = lax.axis_index("dp").astype(jnp.int32)
    places = (me & 7).reshape(1)
    own_count = layer_scale_factors.shape[2]
    rows = patch_observations.shape[0]

    group_width = readout_latent_offset.shape[0]
    offsets = jnp.stack([readout_latent_offset, readout_emit_offset])
    coarse = lax.reduce_precision(offsets, 8, 7)
    offset_rows = jnp.concatenate([coarse, offsets - coarse], axis=0).astype(jnp.bfloat16)
    offset_rows = jnp.pad(offset_rows, ((0, 12), (0, 0)))
    sent = jnp.concatenate(
        [
            loss_sensitivity.reshape(group, rows, group_width),
            jnp.broadcast_to(offset_rows[None], (group, 16, group_width)),
        ],
        axis=1,
    )
    gain_columns = layer_scale_factors.reshape(2 * layer_count, own_count).T
    gain_columns = jnp.pad(gain_columns, ((0, 0), (0, 128 - 2 * layer_count)))
    chunks = []
    for layer_index in range(layer_count):
        entry_own = attention_entry_matrices[layer_index]
        if layer_index == 0:
            entry_own = jnp.concatenate([entry_own, gain_columns], axis=1)
        chunks.append(entry_own)
        rest_own = jnp.concatenate(
            [
                attention_merge_matrix[layer_index],
                feedforward_widen_matrix[layer_index],
                feedforward_shrink_matrix[layer_index],
            ],
            axis=1,
        )
        chunks.append(rest_own)
    head_own = jnp.concatenate(
        [
            lax.dynamic_index_in_dim(
                matrix.reshape(outer, 8, -1, group_width), me % 8, 1, keepdims=False
            )
            for matrix in (readout_latent_matrix, readout_shortcut_matrix, readout_emit_matrix)
        ],
        axis=2,
    )
    chunks.append(head_own)
    count = len(chunks)

    def gather_chunk(number, own):
        if number < count - 1:
            return gather_head(own)
        return lax.all_gather(own, "head", axis=0, tiled=True)

    held = gather_chunk(0, chunks[0])
    cosine_wide = jnp.tile(jnp.concatenate([cosine[:, 0], cosine[:, 0]], axis=1), (1, HEADS))
    sine_wide = jnp.tile(jnp.concatenate([-sine[:, 0], sine[:, 0]], axis=1), (1, HEADS))
    tables = (cosine, sine, cosine_wide, sine_wide)
    nears, fars, near_mets = [], [], []
    layers = []
    onward = None
    for number in range(count + 1):
        step = {}
        if number < count:
            step["x"], step["y"] = swap(held, 1), swap(held, 2)
        if number + 1 < count:
            step["next"] = gather_chunk(number + 1, chunks[number + 1])
        if number == count - 1:
            step["met"] = lax.all_to_all(
                after(sent, held), "head", split_axis=0, concat_axis=0, tiled=True
            )
        if number == 0:
            step["resid"] = resid
        else:
            step["far"] = (swap(onward[0], 1), swap(onward[1], 2))
            near_mets.append([swap(part, 0) for part in after(nears[number - 1], onward)])
        if number > 1:
            chunk = number - 2
            far_met = [swap(part, 0) for part in after(fars[chunk], onward)]
            pieces = all_pieces(nears[chunk], fars[chunk], near_mets[chunk], far_met)
            if chunk == 0:
                gain_rows = place(places, pieces, [128], 3 * MODEL_WIDTH)[0][0]
                gain_rows = gain_rows[:, : 2 * layer_count].T.reshape(layer_count, 2, -1)
            if chunk % 2 == 0:
                layers.append(Layer(places, pieces, gain_rows[chunk // 2], tables, allowed))
                step["mixed"] = layers[-1].entry_forward(resid)
            else:
                layers[-1].add_rest(pieces)
                step["resid"] = layers[-1].rest_forward(mixed)
        step["own"] = chunks[number + 2 :]
        step = lax.optimization_barrier(step)
        chunks[number + 2 :] = step["own"]
        if number < count:
            nears.append((held, step["x"], step["y"]))
            onward = second_step(*nears[-1])
        held = step.get("next")
        if number > 0:
            fars.append(step["far"])
        resid = step.get("resid", resid)
        mixed = step.get("mixed")
        if "met" in step:
            met = step["met"]
    head_far_met = [swap(part, 0) for part in fars[-1]]
    head_pieces = all_pieces(nears[-1], fars[-1], near_mets[-1], head_far_met)
    sensitivity = met[:, :rows]
    head_offsets = met[:, rows : rows + 4].astype(jnp.float32)
    latent_offsets = head_offsets[:, 0] + head_offsets[:, 2]
    emit_offsets = head_offsets[:, 1] + head_offsets[:, 3]

    top = resid.astype(jnp.bfloat16)
    keep_column = keep_rows[:, None]
    grad_forecast = (sensitivity.astype(jnp.float32) * keep_column).astype(jnp.bfloat16)
    grad_forecast_rows = jnp.concatenate([grad_forecast[part] for part in range(group)], axis=1)
    head_inputs = (top, keep_column, latent_offsets, emit_offsets, grad_forecast)
    if layers[0].fetched:
        outs = output_block(places, head_pieces, *head_inputs)
    else:
        head_whole = place(places, head_pieces, [3 * group_width])[0]
        outs = output_plain(head_whole, *head_inputs)
    head_hidden, forecast, grad_head_pre, grad_resid, pre_sums = outs
    token_predictions = lax.all_to_all(
        forecast, "head", split_axis=0, concat_axis=0, tiled=True
    ).reshape(group * rows, group_width)
    head_bias_rows = (pre_sums[0], jnp.sum(grad_forecast_rows.astype(jnp.float32), axis=0))
    head_both = exchange(
        [
            (top, grad_head_pre),
            (top, grad_forecast_rows),
            (head_hidden, grad_forecast_rows),
        ]
    )
    gain_sums = [[None, None] for _ in range(layer_count)]

    def rest_stage(layer_index, carry):
        outs = layers[layer_index].rest_backward(carry["grad"])
        gain_sums[layer_index][1] = outs[4]
        both = exchange(list(zip(outs[2], outs[3], strict=True)))
        return {"middle": outs[0], "mixed": outs[1]}, both

    def entry_stage(layer_index, carry):
        outs = layers[layer_index].entry_backward(carry["middle"], carry["mixed"])
        gain_sums[layer_index][0] = outs[3]
        return {"grad": outs[0]}, exchange([(outs[1], outs[2])])

    def input_stage(carry):
        head_rows = [row[None] for row in head_bias_rows]
        gain_rows = [row[None] for pair in gain_sums for row in pair]
        if layers[0].fetched and 2 + len(head_rows) + len(gain_rows) == EXTRA_ROWS:
            low, pre_low, grad_features, bias_rows = input_back(
                carry["grad"],
                entry_pre,
                intake_emit_matrix,
                intake_latent_matrix,
                intake_shortcut_matrix,
            )
            values_grad = jnp.where(pad_mask, 0.0, grad_features[:, :patch_len])
            vectors = jnp.concatenate([bias_rows, *head_rows, *gain_rows], axis=0)
            operands = []
            for part in (entry_hidden, low, pre_low, features, vectors):
                operands += [part, swap(part, 0)]
            return values_grad, 4 * patch_len + EXTRA_ROWS, operands
        grad_entry = carry["grad"].astype(jnp.bfloat16)
        grad_entry_outer = dyadic_accumulation(entry_hidden, grad_entry)
        grad_entry_outer_bias = jnp.sum(grad_entry.astype(jnp.float32), axis=0)
        grad_entry_skip = dyadic_accumulation(features, grad_entry)
        unused_entry, entry_pull = jax.vjp(jax.nn.silu, entry_pre)
        grad_entry_pre = entry_pull(reverse_matmul_answer(grad_entry, intake_emit_matrix))[0].astype(
            jnp.bfloat16
        )
        grad_entry_inner = dyadic_accumulation(features, grad_entry_pre)
        grad_entry_inner_bias = jnp.sum(grad_entry_pre.astype(jnp.float32), axis=0)
        grad_features = reverse_matmul_answer(
            grad_entry_pre, intake_latent_matrix
        ) + reverse_matmul_answer(grad_entry, intake_shortcut_matrix)
        values_grad = jnp.where(pad_mask, 0.0, grad_features[:, :patch_len])
        extra_rows = jnp.concatenate(
            [
                grad_entry_inner,
                grad_entry_skip,
                grad_entry_inner_bias[None],
                grad_entry_outer_bias[None],
            ]
            + head_rows
            + [row[None] for pair in gain_sums for row in pair],
            axis=0,
        )
        plain = entry_products(me, grad_entry_outer, extra_rows)
        return values_grad, extra_rows.shape[0], (plain.sent, plain.later, plain.own)

    stages = []
    for layer_index in reversed(range(layer_count)):
        stages += [(rest_stage, layer_index), (entry_stage, layer_index)]
    stage_count = len(stages)
    carry = {"grad": grad_resid}
    boths = {0: head_both}
    sums = {0: RowSums(*pair_products(me, head_both))}
    finished = {}
    entry_chunk = None
    done = 0

    def close(**step):
        step["sent"] = {n: (sums[n].sent, sums[n].later, sums[n].own) for n in sums}
        step["boths"] = boths
        step["carry"] = carry
        step = lax.optimization_barrier(step)
        for n, parts in step.pop("sent").items():
            sums[n].sent, sums[n].later, sums[n].own = parts
        return step

    step = close()
    for number in range(stage_count + 1):
        carry, boths = step["carry"], step["boths"]
        parts = {"first": sums[number].first()}
        if number == 2:
            finished[0] = sum_columns(sums.pop(0).total())
        if number >= 2:
            finished[number - 1] = sum_group(sums.pop(number - 1).total())
        if number >= 3:
            parts["finished"] = {n: finished[n] for n in (number - 2, 0)}
        until = number + 1 if number == 0 else number + 2
        while done < min(until, stage_count):
            stage, layer_index = stages[done]
            carry, boths[done + 1] = stage(layer_index, carry)
            done += 1
        if number == stage_count - 2:
            values_grad, extra_count, parts["entry"] = input_stage(carry)
        if number == stage_count - 1:
            entry_chunk.met = entry_chunk.first()
        if number == stage_count:
            entry_summed = entry_sums_of_group(entry_chunk.total())
        step = close(**parts)
        sums[number].met = step["first"]
        finished.update(step.get("finished", {}))
        carry, boths = step["carry"], step["boths"]
        parts = {"last": sums[number].last()}
        if number == stage_count - 2:
            if layers[0].fetched:
                entry_chunk = input_products(me, step["entry"])
            else:
                (to_x, to_y), later, own = step["entry"]
                entry_chunk = RowSums(to_x, to_y, later, own)
            parts["entry"] = (entry_chunk.sent, entry_chunk.later, entry_chunk.own)
        if number == stage_count - 1:
            parts["entry"] = entry_chunk.last()
        if number < stage_count:
            sums[number + 1] = RowSums(*pair_products(me, boths.pop(number + 1)))
            step = close(**parts)
        else:
            step = parts
        sums[number].last_met = step["last"]
        if number == stage_count - 2:
            entry_chunk.sent, entry_chunk.later, entry_chunk.own = step["entry"]
        if number == stage_count - 1:
            entry_chunk.last_met = step["entry"]
    finished[stage_count] = sum_group_at_once(sums[stage_count].total())
    entry_main, entry_extra = entry_everywhere(me, entry_summed, own_count, extra_count)
    head_rows = gather_blocks(me, finished[0])
    head_sums = [after(head_rows[n], entry_summed).astype(jnp.float32) for n in range(3)]
    layer_sums = [None] * layer_count
    for member, layer_index in enumerate(reversed(range(layer_count))):
        rest = finished[1 + 2 * member].astype(jnp.float32)
        entry = finished[2 + 2 * member].astype(jnp.float32)
        layer_sums[layer_index] = (entry[0], rest[0], rest[1], rest[2])
    inner_rows = 2 * patch_len
    last = 2 * inner_rows
    entry_sums = (
        entry_extra[:inner_rows],
        entry_extra[last],
        entry_main,
        entry_extra[last + 1],
        entry_extra[inner_rows:last],
    )
    head_bias_sums = lax.dynamic_slice_in_dim(
        entry_extra[last + 2 : last + 4], group_place * group_width, group_width, 1
    )
    own_place = (me * group + group_place) * own_count
    gains_grad = lax.dynamic_slice_in_dim(
        entry_extra[last + 4 : last + 4 + 2 * layer_count], own_place, own_count, 1
    ).reshape(layer_count, 2, own_count)
    qkv_grad = jnp.stack([layer_sums[member][0] for member in range(layer_count)])
    out_grad = jnp.stack([layer_sums[member][1] for member in range(layer_count)])
    up_grad = jnp.stack([layer_sums[member][2] for member in range(layer_count)])
    down_grad = jnp.stack([layer_sums[member][3] for member in range(layer_count)])
    return (
        token_predictions,
        values_grad,
        entry_sums[0],
        entry_sums[1],
        entry_sums[2],
        entry_sums[3],
        entry_sums[4],
        qkv_grad,
        out_grad,
        up_grad,
        down_grad,
        gains_grad,
        head_sums[0],
        head_bias_sums[0],
        head_sums[2],
        head_bias_sums[1],
        head_sums[1],
    )


def solution(mesh):
    return jax.shard_map(
        body,
        mesh=mesh,
        in_specs=(
            P(("dp", "head"), None),
            P(("dp", "head"), None),
            P(("dp", "head"), None),
            P(),
            P(),
            P(),
            P(),
            P(),
            P(None, ("dp", "head"), None),
            P(None, ("dp", "head"), None),
            P(None, ("dp", "head"), None),
            P(None, ("dp", "head"), None),
            P(None, None, ("dp", "head")),
            P(None, "head"),
            P("head"),
            P(None, "head"),
            P("head"),
            P(None, "head"),
            P("dp", "head"),
        ),
        out_specs=(
            P("dp", "head"),
            P(("dp", "head"), None),
            P(),
            P(),
            P(),
            P(),
            P(),
            P(None, ("dp", "head"), None),
            P(None, ("dp", "head"), None),
            P(None, ("dp", "head"), None),
            P(None, ("dp", "head"), None),
            P(None, None, ("dp", "head")),
            P(None, "head"),
            P("head"),
            P(None, "head"),
            P("head"),
            P(None, "head"),
        ),
        check_vma=False,
    )
```
